32 devices in a mesh: blk: 4 (over y, x), dp: 8 (over z, core).
Axes of the slice: x: 2, y: 2, z: 4, core: 2. Of those that a mesh axis runs over, the one named last changes fastest.
Arguments:
- tokens: bfloat16 [16, 1024, 768], P('dp', 'blk'), may hold values from -6 to 6
- boxes: int32 [4, 16, 1024], P(None, 'dp', 'blk'), may hold values from 0 to 1000
- w_query: bfloat16 [768, 768], replicated, may hold values from -0.21875 to 0.21875
- w_key: bfloat16 [768, 768], replicated, may hold values from -0.21875 to 0.21875
- w_value: bfloat16 [768, 768], replicated, may hold values from -0.21875 to 0.21875
- w_output: bfloat16 [768, 768], replicated, may hold values from -2 to 2
- box_weight: bfloat16 [768, 768], replicated, may hold values from -0.3125 to 0.3125
- first_gain: float32 [768], replicated, may hold values from 0.5 to 1.5
- first_shift: float32 [768], replicated, may hold values from -1.8 to 1.8
- w_expand: bfloat16 [768, 3072], replicated, may hold values from -0.21875 to 0.21875
- w_reduce: bfloat16 [3072, 768], replicated, may hold values from -0.109375 to 0.109375
- second_gain: float32 [768], replicated, may hold values from 0.5 to 1.5
- second_shift: float32 [768], replicated, may hold values from -1.8 to 1.8
- cotangent: bfloat16 [16, 1024, 768], P('dp', 'blk'), may hold values from -6 to 6
Outputs:
- layer_out: bfloat16 [16, 1024, 768], P('dp', 'blk')
- input_grad: bfloat16 [16, 1024, 768], P('dp', 'blk')
- query_grad: float32 [768, 768], replicated
- key_grad: float32 [768, 768], replicated
- value_grad: float32 [768, 768], replicated
- project_grad: float32 [768, 768], replicated
- box_grad: float32 [768, 768], replicated
- first_gain_grad: float32 [768], replicated
- first_shift_grad: float32 [768], replicated
- expand_grad: float32 [768, 3072], replicated
- reduce_grad: float32 [3072, 768], replicated
- second_gain_grad: float32 [768], replicated
- second_shift_grad: float32 [768], replicated
The draws below stay inside these ranges and needn't reach their ends.
All inputs are finite; a program needn't handle non-finite values.
Results may differ from the reference program's by a relative error of at most 0.018.
Values may be sent and summed in bfloat16 or wider, within the bound.
No kernel may reach another device: no remote copies, remote signals or barrier semaphores. Data moves between devices by JAX's collectives and lax.ppermute only.
A program may use at most 256 MiB of HBM per device.

```python
import jax
import jax.numpy as jnp
from jax import lax

D = 768
HEADS = 12
HEAD_DIM = 64
FF = 3072
BOX_ENC = 384
FREQS = 192
PAGE_LEN = 1024
PAGE_DEV = 2
PAGES = 16


def set_ends(drawn, key, least, top_value):
    extent = drawn.shape
    spot = [jax.random.randint(jax.random.fold_in(key, axis), (), 0, extent[axis]) for axis in range(len(extent))]
    drawn = drawn.at[tuple(spot)].set(least)
    longest = extent.index(max(extent))
    spot[longest] = (spot[longest] + 1) % extent[longest]
    return drawn.at[tuple(spot)].set(top_value)


def shard_levels(stream_key, extent, split, low, largest):
    loudness = 1.0
    for axis_at, shards_of in split:
        heights = jax.random.uniform(jax.random.fold_in(jax.random.fold_in(stream_key, 6), axis_at), (shards_of,), jnp.float32, low / len(split), largest / len(split))
        loudness = loudness * jnp.repeat(jnp.exp(heights), extent[axis_at] // shards_of).reshape((-1,) + (1,) * (len(extent) - 1 - axis_at))
    return loudness


def centred(rng, dims, deviation, bound, cuts=(), kind=jnp.bfloat16):
    drawn = jax.random.normal(rng, dims, jnp.float32) * deviation
    if len(cuts) > 0:
        drawn = shard_levels(rng, dims, cuts, -0.22, 0.18) * drawn
    return jnp.clip(drawn, min=-bound, max=bound).astype(kind)


def setup_inputs(seed: int = 0) -> dict:
    arg_keys = jax.random.split(jax.random.key(seed), 15)
    return {
        "tokens": centred(arg_keys[0], (PAGES, PAGE_LEN, D), 1.0, 6.0, ((0, 8), (1, 4))),
        "boxes": set_ends(jax.random.randint(arg_keys[1], (4, PAGES, PAGE_LEN), 0, 1001), jax.random.fold_in(arg_keys[1], 1), 0, 1000).astype(jnp.int32),
        "w_query": centred(arg_keys[2], (D, D), D ** -0.5, 0.21875),
        "w_key": centred(arg_keys[3], (D, D), D ** -0.5, 0.21875),
        "w_value": centred(arg_keys[4], (D, D), D ** -0.5, 0.21875),
        "w_output": centred(arg_keys[5], (D, D), 8 ** -0.5, 2.0),
        "box_weight": centred(arg_keys[6], (2 * BOX_ENC, D), (2 * BOX_ENC * HEAD_DIM // 128) ** -0.5, 0.3125),
        "first_gain": jnp.clip(1.0 + 0.1 * jax.random.normal(arg_keys[7], (D,), jnp.float32), 0.5, 1.5),
        "first_shift": centred(arg_keys[8], (D,), 0.3, 1.8, (), jnp.float32),
        "w_expand": centred(arg_keys[9], (D, FF), D ** -0.5, 0.21875),
        "w_reduce": centred(arg_keys[10], (FF, D), FF ** -0.5, 0.109375),
        "second_gain": jnp.clip(1.0 + 0.1 * jax.random.normal(arg_keys[11], (D,), jnp.float32), 0.5, 1.5),
        "second_shift": centred(arg_keys[12], (D,), 0.3, 1.8, (), jnp.float32),
        "cotangent": centred(arg_keys[13], (PAGES, PAGE_LEN, D), 1.0, 6.0, ((0, 8), (1, 4))),
    }


@jax.custom_vjp
def low(v):
    return lax.optimization_barrier(v.astype(jnp.bfloat16)).astype(jnp.float32)

@jax.custom_vjp
def low_back(v):
    return v

def low_keep(v):
    return (low(v), None)

def low_pass(kept, grad):
    return (grad,)

def back_keep(v):
    return (v, None)

def back_low(kept, grad):
    return (low(grad),)
low.defvjp(low_keep, low_pass)
low_back.defvjp(back_keep, back_low)

def rounded_both(value):
    return low(low_back(value))

def product(left, right):
    return jnp.dot(left, right, precision=lax.Precision.HIGHEST)

def rotary(values, place, sign):
    half = values.shape[-1] // 2
    rates = 10000.0 ** (-jnp.arange(half, dtype=jnp.float32) / half)
    angles = place.astype(jnp.float32)[:, None] * rates[None, :]
    sines = sign * jnp.sin(angles)[:, None, :]
    cosines = jnp.cos(angles)[:, None, :]
    first = values[..., :half]
    second = values[..., half:]
    return jnp.concatenate([first * cosines - second * sines, second * cosines + first * sines], axis=-1)

def box_angles(boxes):
    middle = jnp.stack([boxes[0] + boxes[2], boxes[1] + boxes[3]], axis=-1).astype(jnp.float32) * 0.5
    rates = 10000.0 ** (-jnp.arange(FREQS, dtype=jnp.float32) / FREQS)
    angles = middle[..., None] * rates
    return (jnp.sin(angles), jnp.cos(angles))

def box_code(sines, cosines):
    return jnp.stack([sines, cosines], axis=-2).reshape(sines.shape[:-2] + (4 * FREQS,))

def box_turn(projected, sines, cosines, sign):
    parts = projected.reshape(projected.shape[:-1] + (2, 2, FREQS))
    upper = parts[..., 0, :]
    lower = parts[..., 1, :]
    sines = sign * sines[:, :, None]
    cosines = cosines[:, :, None]
    turned = jnp.stack([upper * cosines + lower * sines, lower * cosines - upper * sines], axis=-2)
    return turned.reshape(projected.shape)

def layer_norm(value, gain, shift):
    centered = value - lax.optimization_barrier(jnp.mean(value, axis=-1, keepdims=True))
    spread = lax.optimization_barrier(jnp.mean(centered * centered, axis=-1, keepdims=True))
    return centered * lax.rsqrt(spread + 1e-05) * gain + shift

def page_attention(item):
    queries, keys, values, rel_query, codes = item
    logits = jnp.einsum('qhd,khd->qhk', queries, keys, precision=lax.Precision.HIGHEST)
    logits = logits + jnp.einsum('qhe,ke->qhk', rel_query, codes, precision=lax.Precision.HIGHEST)
    logits = low_back(logits * 0.125)
    probs = jax.nn.softmax(logits, axis=-1)
    return jnp.einsum('qhk,khd->qhd', low(probs), values, precision=lax.Precision.HIGHEST)

def forward(tokens, boxes, w_query, w_key, w_value, w_output, box_weight, first_gain, first_shift, w_expand, w_reduce, second_gain, second_shift):
    pages, length, width = tokens.shape
    place = jnp.arange(length, dtype=jnp.int32)
    query_pre = rounded_both(product(tokens, w_query)).reshape(pages, length, HEADS, HEAD_DIM)
    key_pre = low_back(product(tokens, w_key)).reshape(pages, length, HEADS, HEAD_DIM)
    values = rounded_both(product(tokens, w_value)).reshape(pages, length, HEADS, HEAD_DIM)
    queries = low(rotary(query_pre, place, 1.0))
    keys = low(rotary(key_pre, place, 1.0))
    sines, cosines = box_angles(boxes)
    box_table = box_weight.reshape(2 * BOX_ENC, HEADS, HEAD_DIM)
    projected = low_back(jnp.einsum('pbhd,ehd->pbhe', query_pre, box_table, precision=lax.Precision.HIGHEST))
    rel_query = low(box_turn(projected, sines, cosines, 1.0))
    codes = low(box_code(sines, cosines))
    attended = lax.map(jax.checkpoint(page_attention), (queries, keys, values, rel_query, codes))
    attended = rounded_both(attended).reshape(pages, length, width)
    branch = low_back(product(attended, w_output))
    first_out = layer_norm(tokens + branch, first_gain, first_shift)
    expanded = low_back(product(low(first_out), w_expand))
    activated = low(jax.nn.gelu(expanded, approximate=False))
    reduced = low_back(product(activated, w_reduce))
    return layer_norm(first_out + reduced, second_gain, second_shift)

def reference(tokens, boxes, w_query, w_key, w_value, w_output, box_weight, first_gain, first_shift, w_expand, w_reduce, second_gain, second_shift, cotangent):
    weights = tuple((item.astype(jnp.float32) for item in (w_query, w_key, w_value, w_output, box_weight, first_gain, first_shift, w_expand, w_reduce, second_gain, second_shift)))
    groups = tokens.shape[0] // PAGE_DEV
    group_tokens = tokens.reshape(groups, PAGE_DEV, PAGE_LEN, D)
    group_boxes = boxes.reshape(4, groups, PAGE_DEV, PAGE_LEN).transpose(1, 0, 2, 3)
    group_grads = cotangent.reshape(groups, PAGE_DEV, PAGE_LEN, D)

    def one_group(totals, item):
        part_tokens, part_boxes, part_grads = item

        def runner(inputs, *params):
            return forward(inputs, part_boxes, *params)
        result, pull = jax.vjp(runner, part_tokens.astype(jnp.float32), *weights)
        grads = pull(part_grads.astype(jnp.float32))
        totals = tuple((total + grad for total, grad in zip(totals, grads[1:])))
        return (totals, (result.astype(jnp.bfloat16), grads[0].astype(jnp.bfloat16)))
    start = tuple((jnp.zeros_like(item) for item in weights))
    totals, (results, input_grads) = lax.scan(one_group, start, (group_tokens, group_boxes, group_grads))
    return (results.reshape(tokens.shape), input_grads.reshape(tokens.shape), totals[0], totals[1], totals[2], totals[3], totals[4], totals[5], totals[6], totals[7], totals[8], totals[9], totals[10])
```

```python
import jax
import jax.numpy as jnp
from jax import lax
from jax.sharding import PartitionSpec as P

HEADS = 12
HEAD_DIM = 64
BOX_ENC = 384
FREQS = 192


def passed_along(block, axis, distance):
    devices = range(lax.axis_size(axis))
    route = [((i - distance) % len(devices), i) for i in devices]
    return lax.ppermute(block, axis, route)


def rotary(values, place, sign):
    half = values.shape[-1] // 2
    rates = 10000.0 ** (-jnp.arange(half, dtype=jnp.float32) / half)
    angles = place.astype(jnp.float32)[:, None] * rates[None, :]
    sines = sign * jnp.sin(angles)[:, None, :]
    cosines = jnp.cos(angles)[:, None, :]
    first = values[..., :half]
    second = values[..., half:]
    return jnp.concatenate(
        [first * cosines - second * sines, second * cosines + first * sines], axis=-1
    )


def box_angles(boxes):
    middle = (
        jnp.stack([boxes[0] + boxes[2], boxes[1] + boxes[3]], axis=-1).astype(jnp.float32) * 0.5
    )
    rates = 10000.0 ** (-jnp.arange(FREQS, dtype=jnp.float32) / FREQS)
    angles = middle[..., None] * rates
    return (jnp.sin(angles), jnp.cos(angles))


def box_code(sines, cosines):
    return jnp.stack([sines, cosines], axis=-2).reshape(sines.shape[:-2] + (4 * FREQS,))


def box_turn(projected, sines, cosines, sign):
    parts = projected.reshape(projected.shape[:-1] + (2, 2, FREQS))
    upper = parts[..., 0, :]
    lower = parts[..., 1, :]
    sines = sign * sines[:, :, None]
    cosines = cosines[:, :, None]
    turned = jnp.stack([upper * cosines + lower * sines, lower * cosines - upper * sines], axis=-2)
    return turned.reshape(projected.shape)


def layer_norm(value, gain, shift):
    centered = value - jnp.mean(value, axis=-1, keepdims=True)
    spread = jnp.mean(centered * centered, axis=-1, keepdims=True)
    return centered * lax.rsqrt(spread + 1e-05) * gain + shift


def smooth_gate(value):
    return jax.nn.gelu(value, approximate=False)


def per_device(
    tokens,
    boxes,
    w_query,
    w_key,
    w_value,
    w_output,
    box_weight,
    first_gain,
    first_shift,
    w_expand,
    w_reduce,
    second_gain,
    second_shift,
    cotangent,
):
    pages, block, width = tokens.shape
    count = lax.axis_size("blk")
    rank = lax.axis_index("blk")
    place = rank * block + jnp.arange(block, dtype=jnp.int32)
    head_shape = (pages, block, HEADS, HEAD_DIM)
    query_pre = (
        jnp.dot(tokens, w_query, preferred_element_type=jnp.float32)
        .astype(jnp.bfloat16)
        .reshape(head_shape)
    )
    key_pre = jnp.dot(tokens, w_key, preferred_element_type=jnp.float32).reshape(head_shape)
    values_flat = jnp.dot(tokens, w_value, preferred_element_type=jnp.float32).astype(jnp.bfloat16)
    queries = rotary(query_pre.astype(jnp.float32), place, 1.0).astype(jnp.bfloat16)
    keys_flat = rotary(key_pre, place, 1.0).astype(jnp.bfloat16).reshape(pages, block, width)
    box_table = box_weight.reshape(2 * BOX_ENC, HEADS, HEAD_DIM)
    own_sines, own_cosines = box_angles(boxes)
    projected = jnp.einsum(
        "pbhd,ehd->pbhe", query_pre, box_table, preferred_element_type=jnp.float32
    )
    rel_query = box_turn(projected, own_sines, own_cosines, 1.0).astype(jnp.bfloat16)

    def scores(key_block, code_block):
        logits = jnp.einsum(
            "pqhd,pkhd->pqhk", queries, key_block, preferred_element_type=jnp.float32
        )
        logits = logits + jnp.einsum(
            "pqhe,pke->pqhk", rel_query, code_block, preferred_element_type=jnp.float32
        )
        return logits * 0.125

    own_code = box_code(own_sines, own_cosines).astype(jnp.bfloat16)
    key_flat = lax.all_gather(keys_flat, "blk", axis=1, tiled=True)
    rows = key_flat.shape[1]
    key_block = key_flat.reshape(pages, rows, HEADS, HEAD_DIM)
    value_block = lax.all_gather(values_flat, "blk", axis=1, tiled=True).reshape(
        pages, rows, HEADS, HEAD_DIM
    )
    peak = jnp.full((pages, block, HEADS), -1e30, jnp.float32)
    logits = scores(key_block, lax.all_gather(own_code, "blk", axis=1, tiled=True))
    newest = jnp.maximum(peak, jnp.max(logits, axis=-1))
    weights = jnp.exp(logits - newest[..., None])
    total = jnp.sum(weights, axis=-1)
    summed = jnp.einsum(
        "pqhk,pkhd->pqhd",
        weights.astype(jnp.bfloat16),
        value_block,
        preferred_element_type=jnp.float32,
    )
    peak, total, summed = (newest, total, summed)
    travel = jnp.concatenate([keys_flat, values_flat, own_code], axis=-1)
    attended = summed / total[..., None]
    attended_low = attended.astype(jnp.bfloat16).reshape(pages, block, width)
    log_total = peak + jnp.log(total)
    branch = jnp.dot(attended_low, w_output, preferred_element_type=jnp.float32)
    first_out, first_pull = jax.vjp(
        layer_norm, tokens.astype(jnp.float32) + branch, first_gain, first_shift
    )
    first_low = first_out.astype(jnp.bfloat16)
    expanded = jnp.dot(first_low, w_expand, preferred_element_type=jnp.float32)
    activated, gate_pull = jax.vjp(smooth_gate, expanded)
    activated_low = activated.astype(jnp.bfloat16)
    reduced = jnp.dot(activated_low, w_reduce, preferred_element_type=jnp.float32)
    layer_out, second_pull = jax.vjp(layer_norm, first_out + reduced, second_gain, second_shift)
    grad_second_in, grad_second_gain, grad_second_shift = second_pull(cotangent.astype(jnp.float32))
    grad_reduced = grad_second_in.astype(jnp.bfloat16)
    grad_w_reduce = jnp.einsum(
        "pbf,pbd->fd", activated_low, grad_reduced, preferred_element_type=jnp.float32
    )
    grad_activated = jnp.einsum(
        "pbd,fd->pbf", grad_reduced, w_reduce, preferred_element_type=jnp.float32
    )
    grad_expanded = gate_pull(grad_activated)[0].astype(jnp.bfloat16)
    grad_w_expand = jnp.einsum(
        "pbd,pbf->df", first_low, grad_expanded, preferred_element_type=jnp.float32
    )
    grad_first_out = grad_second_in + jnp.einsum(
        "pbf,df->pbd", grad_expanded, w_expand, preferred_element_type=jnp.float32
    )
    grad_first_in, grad_first_gain, grad_first_shift = first_pull(grad_first_out)
    grad_branch = grad_first_in.astype(jnp.bfloat16)
    grad_w_output = jnp.einsum(
        "pbd,pbe->de", attended_low, grad_branch, preferred_element_type=jnp.float32
    )
    grad_attended = (
        jnp.einsum("pbe,de->pbd", grad_branch, w_output, preferred_element_type=jnp.float32)
        .astype(jnp.bfloat16)
        .reshape(head_shape)
    )
    offsets = jnp.sum(grad_attended.astype(jnp.float32) * attended, axis=-1)
    grad_w_expand, grad_w_reduce = lax.psum(
        (grad_w_expand.astype(jnp.bfloat16), grad_w_reduce.astype(jnp.bfloat16)), ("blk", "dp")
    )

    def reverse(key_block, value_block, code_block):
        logits = scores(key_block, code_block)
        probs = jnp.exp(logits - log_total[..., None])
        grad_probs = jnp.einsum(
            "pqhd,pkhd->pqhk", grad_attended, value_block, preferred_element_type=jnp.float32
        )
        grad_logits = (probs * (grad_probs - offsets[..., None])).astype(jnp.bfloat16)
        grad_q = (
            jnp.einsum(
                "pqhk,pkhd->pqhd", grad_logits, key_block, preferred_element_type=jnp.float32
            )
            * 0.125
        )
        grad_r = (
            jnp.einsum(
                "pqhk,pke->pqhe", grad_logits, code_block, preferred_element_type=jnp.float32
            )
            * 0.125
        )
        grad_k = (
            jnp.einsum("pqhk,pqhd->pkhd", grad_logits, queries, preferred_element_type=jnp.float32)
            * 0.125
        )
        grad_v = jnp.einsum(
            "pqhk,pqhd->pkhd",
            probs.astype(jnp.bfloat16),
            grad_attended,
            preferred_element_type=jnp.float32,
        )
        return (
            grad_q,
            grad_r,
            grad_k.reshape(pages, block, width),
            grad_v.reshape(pages, block, width),
        )

    def split_travel(moving):
        key_block = moving[..., :width].reshape(head_shape)
        value_block = moving[..., width : 2 * width].reshape(head_shape)
        code_block = moving[..., 2 * width :]
        return (key_block, value_block, code_block)

    def pass_grads(grads):
        return passed_along(grads.astype(jnp.bfloat16), "blk", 1).astype(grads.dtype)

    def contribute(state):
        moving, grads, grad_query, grad_rel = state
        key_block, value_block, code_block = split_travel(moving)
        grad_q, grad_r, grad_k, grad_v = reverse(key_block, value_block, code_block)
        grads = grads + jnp.stack([grad_k, grad_v])
        return (moving, grads, grad_query + grad_q, grad_rel + grad_r)

    def rotate(turn, state):
        moving, grads, grad_query, grad_rel = contribute(state)
        moving = passed_along(moving, "blk", 1)
        return (moving, pass_grads(grads), grad_query, grad_rel)

    initial = (
        travel,
        jnp.zeros((2, pages, block, width), jnp.float32),
        jnp.zeros(head_shape, jnp.float32),
        jnp.zeros(rel_query.shape, jnp.float32),
    )
    state = lax.fori_loop(0, count - 1, rotate, initial)
    moving, grads, grad_query, grad_rel = contribute(state)
    grads = pass_grads(grads)
    grad_key_pre = (
        rotary(grads[0].reshape(head_shape), place, -1.0)
        .astype(jnp.bfloat16)
        .reshape(pages, block, width)
    )
    grad_values = grads[1].astype(jnp.bfloat16)
    grad_projected = box_turn(grad_rel, own_sines, own_cosines, -1.0).astype(jnp.bfloat16)
    grad_query_pre = rotary(grad_query, place, -1.0) + jnp.einsum(
        "pbhe,ehd->pbhd", grad_projected, box_table, preferred_element_type=jnp.float32
    )
    grad_query_pre = grad_query_pre.astype(jnp.bfloat16).reshape(pages, block, width)
    grad_box = jnp.einsum(
        "pbhd,pbhe->ehd", query_pre, grad_projected, preferred_element_type=jnp.float32
    ).reshape(2 * BOX_ENC, width)
    grad_w_query = jnp.einsum(
        "pbd,pbe->de", tokens, grad_query_pre, preferred_element_type=jnp.float32
    )
    grad_w_key = jnp.einsum("pbd,pbe->de", tokens, grad_key_pre, preferred_element_type=jnp.float32)
    grad_w_value = jnp.einsum(
        "pbd,pbe->de", tokens, grad_values, preferred_element_type=jnp.float32
    )
    input_grad = grad_first_in + jnp.einsum(
        "pbe,de->pbd", grad_query_pre, w_query, preferred_element_type=jnp.float32
    )
    input_grad = input_grad + jnp.einsum(
        "pbe,de->pbd", grad_key_pre, w_key, preferred_element_type=jnp.float32
    )
    input_grad = input_grad + jnp.einsum(
        "pbe,de->pbd", grad_values, w_value, preferred_element_type=jnp.float32
    )
    late = tuple(
        item.astype(jnp.bfloat16)
        for item in (grad_w_query, grad_w_key, grad_w_value, grad_w_output, grad_box)
    )
    late, grad_w_expand, grad_w_reduce = lax.optimization_barrier(
        (late, grad_w_expand, grad_w_reduce)
    )
    grad_w_query, grad_w_key, grad_w_value, grad_w_output, grad_box = (
        item.astype(jnp.float32) for item in lax.psum(late, ("blk", "dp"))
    )
    grad_w_expand = grad_w_expand.astype(jnp.float32)
    grad_w_reduce = grad_w_reduce.astype(jnp.float32)
    small = jnp.stack([grad_first_gain, grad_first_shift, grad_second_gain, grad_second_shift])
    grad_first_gain, grad_first_shift, grad_second_gain, grad_second_shift = lax.psum(
        small, ("blk", "dp")
    )
    return (
        layer_out.astype(jnp.bfloat16),
        input_grad.astype(jnp.bfloat16),
        grad_w_query,
        grad_w_key,
        grad_w_value,
        grad_w_output,
        grad_box,
        grad_first_gain,
        grad_first_shift,
        grad_w_expand,
        grad_w_reduce,
        grad_second_gain,
        grad_second_shift,
    )


def solution(mesh):
    return jax.shard_map(
        per_device,
        mesh=mesh,
        in_specs=(
            P("dp", "blk", None),
            P(None, "dp", "blk"),
            P(),
            P(),
            P(),
            P(),
            P(),
            P(),
            P(),
            P(),
            P(),
            P(),
            P(),
            P("dp", "blk", None),
        ),
        out_specs=(
            P("dp", "blk", None),
            P("dp", "blk", None),
            P(),
            P(),
            P(),
            P(),
            P(),
            P(),
            P(),
            P(),
            P(),
            P(),
            P(),
        ),
        check_vma=False,
    )
```

```python
import functools

import jax
import jax.numpy as jnp
import numpy as np
from jax import lax
from jax.experimental import pallas as pl
from jax.experimental.pallas import tpu as pltpu
from jax.sharding import PartitionSpec as P

HEADS = 12
HEAD_DIM = 64
HALF = 32
FREQS = 192
CODES = 4 * FREQS
VMEM_LIMIT = 60 * 1024 * 1024
F32 = jnp.float32
BF16 = jnp.bfloat16


def dot(left, right):
    return lax.dot_general(left, right, (((1,), (0,)), ((), ())), preferred_element_type=F32)


def dot_nt(left, right):
    return lax.dot_general(left, right, (((1,), (1,)), ((), ())), preferred_element_type=F32)


def dot_tn(left, right):
    return lax.dot_general(left, right, (((0,), (0,)), ((), ())), preferred_element_type=F32)


def swapped(block, distance):
    count = lax.axis_size("blk")
    return lax.ppermute(block, "blk", [(i, i ^ distance) for i in range(count)])


def turned(upper, lower, cosines, sines):
    return upper * cosines - lower * sines, lower * cosines + upper * sines


def forward_kernel(
    tok_ref,
    w_ref,
    box_ref,
    codes_ref,
    sin_ref,
    cos_ref,
    rot_cos_ref,
    rot_sin_ref,
    probs_ref,
    att_ref,
    att_low_ref,
    heads_ref,
    kc_ref,
    qr_ref,
):
    rows = tok_ref.shape[0]

    @pl.when(pl.program_id(0) == 0)
    def _():
        kc_ref[:, :CODES] = codes_ref[...].astype(F32).T.astype(BF16)

    weights = w_ref[...].reshape(3 * HEAD_DIM, w_ref.shape[-1])
    pre = dot_nt(weights, tok_ref[...])
    rot_cos = rot_cos_ref[...]
    rot_sin = rot_sin_ref[...]
    query_pre = pre[:HEAD_DIM].astype(BF16)
    wide = query_pre.astype(F32)
    query = jnp.concatenate(turned(wide[:HALF], wide[HALF:], rot_cos, rot_sin), axis=0)
    key_pre = pre[HEAD_DIM : 2 * HEAD_DIM]
    key = jnp.concatenate(turned(key_pre[:HALF], key_pre[HALF:], rot_cos, rot_sin), axis=0)
    value = pre[2 * HEAD_DIM :].astype(BF16)
    heads_ref[0, :HEAD_DIM] = query_pre
    heads_ref[0, HEAD_DIM : 2 * HEAD_DIM] = query.astype(BF16)
    heads_ref[0, 2 * HEAD_DIM : 3 * HEAD_DIM] = key.astype(BF16)
    heads_ref[0, 3 * HEAD_DIM :] = value
    kc_ref[:, CODES:] = key.T.astype(BF16)
    projected = dot_tn(box_ref[0], query_pre)
    sines = sin_ref[...]
    cosines = cos_ref[...]
    upper = projected[: 2 * FREQS]
    lower = projected[2 * FREQS :]
    qr_ref[: 2 * FREQS] = ((upper * cosines + lower * sines) * 0.125).astype(BF16)
    qr_ref[2 * FREQS : CODES] = ((lower * cosines - upper * sines) * 0.125).astype(BF16)
    qr_ref[CODES:] = (query * 0.125).astype(BF16)
    step = min(256, rows)
    for at in range(0, rows, step):
        logits = dot(kc_ref[...], qr_ref[:, at : at + step])
        weight = jnp.exp(logits - jnp.max(logits, axis=0, keepdims=True))
        total = jnp.sum(weight, axis=0, keepdims=True)
        probs = (weight * (1.0 / total)).astype(BF16)
        probs_ref[0, :, at : at + step] = probs
        attended = dot(value, probs)
        att_ref[0, :, at : at + step] = attended
        att_low_ref[:, at : at + step] = attended.astype(BF16)


def attention_forward(tok, w_own, box_own, codes, sines, cosines, rot_cos, rot_sin):
    rows, width = tok.shape
    heads = w_own.shape[1]

    def whole(array):
        return pl.BlockSpec(array.shape, lambda h: (0,) * array.ndim)

    return pl.pallas_call(
        forward_kernel,
        grid=(heads,),
        in_specs=[
            whole(tok),
            pl.BlockSpec((3, 1, HEAD_DIM, width), lambda h: (0, h, 0, 0)),
            pl.BlockSpec((1, HEAD_DIM, CODES), lambda h: (h, 0, 0)),
            whole(codes),
            whole(sines),
            whole(cosines),
            whole(rot_cos),
            whole(rot_sin),
        ],
        out_specs=[
            pl.BlockSpec((1, rows, rows), lambda h: (h, 0, 0)),
            pl.BlockSpec((1, HEAD_DIM, rows), lambda h: (h, 0, 0)),
            pl.BlockSpec((HEAD_DIM, rows), lambda h: (h, 0)),
            pl.BlockSpec((1, 4 * HEAD_DIM, rows), lambda h: (h, 0, 0)),
        ],
        out_shape=[
            jax.ShapeDtypeStruct((heads, rows, rows), BF16),
            jax.ShapeDtypeStruct((heads, HEAD_DIM, rows), F32),
            jax.ShapeDtypeStruct((heads * HEAD_DIM, rows), BF16),
            jax.ShapeDtypeStruct((heads, 4 * HEAD_DIM, rows), BF16),
        ],
        scratch_shapes=[
            pltpu.VMEM((rows, CODES + HEAD_DIM), BF16),
            pltpu.VMEM((CODES + HEAD_DIM, rows), BF16),
        ],
        compiler_params=pltpu.CompilerParams(vmem_limit_bytes=VMEM_LIMIT),
        cost_estimate=pl.CostEstimate(
            flops=2 * heads * rows * (rows * 1100 + 200 * width + 64 * CODES),
            bytes_accessed=2 * heads * rows * rows + 12 * rows * width,
            transcendentals=heads * rows * rows,
        ),
        name="attention_forward",
    )(tok, w_own, box_own, codes, sines, cosines, rot_cos, rot_sin)


def backward_kernel(
    grad_ref,
    probs_ref,
    att_ref,
    heads_ref,
    tok_ref,
    box_ref,
    codes_ref,
    sin_ref,
    cos_ref,
    rot_cos_ref,
    rot_sin_ref,
    pre_grad_ref,
    weight_grad_ref,
    kc_ref,
    query_grad_ref,
):
    rows = tok_ref.shape[0]
    head = pl.program_id(0)
    span = pl.num_programs(0) * HEAD_DIM

    @pl.when(head == 0)
    def _():
        kc_ref[:CODES] = codes_ref[...]

    kc_ref[CODES:] = heads_ref[0, 2 * HEAD_DIM : 3 * HEAD_DIM]
    packed = heads_ref[0].astype(F32).T.astype(BF16)
    query_pre = packed[:, :HEAD_DIM]
    query = packed[:, HEAD_DIM : 2 * HEAD_DIM]
    value = packed[:, 3 * HEAD_DIM :] * jnp.asarray(0.125, BF16)
    rot_cos = rot_cos_ref[...]
    rot_sin = rot_sin_ref[...]
    grad = grad_ref[...]
    grad_tall = grad.astype(F32).T.astype(BF16)
    offsets = jnp.sum(grad.astype(F32) * att_ref[0], axis=0, keepdims=True) * 0.125
    step = min(256, rows)
    key_grad = jnp.zeros((rows, HEAD_DIM), F32)
    value_grad = jnp.zeros((rows, HEAD_DIM), F32)
    box_grad = jnp.zeros((CODES, HEAD_DIM), F32)
    for at in range(0, rows, step):
        part = slice(at, at + step)
        probs = probs_ref[0, :, part]
        grad_probs = dot(value, grad[:, part])
        grad_logits = (probs.astype(F32) * (grad_probs - offsets[:, part])).astype(BF16)
        back = dot(kc_ref[...], grad_logits)
        sines = sin_ref[:, part]
        cosines = cos_ref[:, part]
        upper = back[: 2 * FREQS]
        lower = back[2 * FREQS : CODES]
        projected_grad = jnp.concatenate(
            [
                (upper * cosines - lower * sines).astype(BF16),
                (lower * cosines + upper * sines).astype(BF16),
            ],
            axis=0,
        )
        first = back[CODES : CODES + HALF]
        second = back[CODES + HALF :]
        own = jnp.concatenate(
            turned(first, second, rot_cos[:, part], -rot_sin[:, part]), axis=0
        )
        query_grad_ref[:, part] = (own + dot(box_ref[0], projected_grad)).astype(BF16)
        key_grad = key_grad + dot(grad_logits, query[part])
        value_grad = value_grad + dot(probs, grad_tall[part])
        box_grad = box_grad + dot(projected_grad, query_pre[part])
    key_flat = key_grad.T
    key_low = jnp.concatenate(
        turned(key_flat[:HALF], key_flat[HALF:], rot_cos, -rot_sin), axis=0
    ).astype(BF16)
    place = pl.multiple_of(head * HEAD_DIM, HEAD_DIM)
    pre_grad_ref[pl.ds(place, HEAD_DIM)] = query_grad_ref[...]
    pre_grad_ref[pl.ds(span + place, HEAD_DIM)] = key_low
    pre_grad_ref[pl.ds(2 * span + place, HEAD_DIM)] = value_grad.T.astype(BF16)
    weight_grad_ref[pl.ds(3 * span + place, HEAD_DIM)] = box_grad.T

    @pl.when(head == pl.num_programs(0) - 1)
    def _():
        weight_grad_ref[: 3 * span] = dot(pre_grad_ref[...], tok_ref[...])


def attention_backward(
    grad, probs, att, heads_saved, tok, box_own, codes, sines, cosines, rot_cos, rot_sin
):
    rows, width = tok.shape
    heads = probs.shape[0]

    def whole(array):
        return pl.BlockSpec(array.shape, lambda h: (0,) * array.ndim)

    return pl.pallas_call(
        backward_kernel,
        grid=(heads,),
        in_specs=[
            pl.BlockSpec((HEAD_DIM, rows), lambda h: (h, 0)),
            pl.BlockSpec((1, rows, rows), lambda h: (h, 0, 0)),
            pl.BlockSpec((1, HEAD_DIM, rows), lambda h: (h, 0, 0)),
            pl.BlockSpec((1, 4 * HEAD_DIM, rows), lambda h: (h, 0, 0)),
            whole(tok),
            pl.BlockSpec((1, HEAD_DIM, CODES), lambda h: (h, 0, 0)),
            whole(codes),
            whole(sines),
            whole(cosines),
            whole(rot_cos),
            whole(rot_sin),
        ],
        out_specs=[
            pl.BlockSpec((3 * heads * HEAD_DIM, rows), lambda h: (0, 0)),
            pl.BlockSpec((4 * heads * HEAD_DIM, width), lambda h: (0, 0)),
        ],
        out_shape=[
            jax.ShapeDtypeStruct((3 * heads * HEAD_DIM, rows), BF16),
            jax.ShapeDtypeStruct((4 * heads * HEAD_DIM, width), F32),
        ],
        scratch_shapes=[
            pltpu.VMEM((CODES + HEAD_DIM, rows), BF16),
            pltpu.VMEM((HEAD_DIM, rows), BF16),
        ],
        compiler_params=pltpu.CompilerParams(vmem_limit_bytes=VMEM_LIMIT),
        cost_estimate=pl.CostEstimate(
            flops=2 * heads * rows * (rows * 1400 + 200 * width + 128 * CODES),
            bytes_accessed=2 * heads * rows * rows + 12 * rows * width,
            transcendentals=0,
        ),
        name="attention_backward",
    )(grad, probs, att, heads_saved, tok, box_own, codes, sines, cosines, rot_cos, rot_sin)


def normed(value):
    centered = value - jnp.mean(value, axis=-1, keepdims=True)
    scale = lax.rsqrt(jnp.mean(centered * centered, axis=-1, keepdims=True) + 1e-05)
    return centered * scale, scale


def norm_back(grad, gain, unit, scale):
    scaled = grad * gain
    return scale * (
        scaled
        - jnp.mean(scaled, axis=-1, keepdims=True)
        - unit * jnp.mean(scaled * unit, axis=-1, keepdims=True)
    )


def column_sum(value):
    return jnp.sum(value, axis=0, keepdims=True)


def middle_kernel(pages, count, span, chunks, *refs):
    total = pages * count
    rank_ref = refs[0]
    att_refs = refs[1 : 1 + total]
    (
        tok_ref,
        cot_ref,
        w_out_ref,
        vectors_ref,
        w_expand_ref,
        w_reduce_ref,
    ) = refs[1 + total : 7 + total]
    outs = refs[7 + total :]
    layer_ref, first_in_ref, expand_ref, reduce_ref, project_ref, sums_ref = outs[:6]
    grad_refs = outs[6 : 6 + total]
    (
        att_all,
        grad_all,
        unit_one,
        scale_one,
        first_wide,
        first_low,
        first_tall,
        active,
        slope,
        gathered,
        second_in,
        second_low,
    ) = outs[6 + total :]
    rank = rank_ref[0]
    block = tok_ref.shape[0] // pages
    step = pl.program_id(0)

    def rows_of(at):
        return pl.ds(pl.multiple_of((rank ^ at) * span, span), span)

    @pl.when(step == 0)
    def _():
        for page in range(pages):
            for at in range(count):
                att_all[rows_of(at), page * block : (page + 1) * block] = att_refs[
                    page * count + at
                ][...]
        branch = dot_tn(att_all[: w_out_ref.shape[0]], w_out_ref[...])
        unit, scale = normed(tok_ref[...].astype(F32) + branch)
        unit_one[...] = unit
        scale_one[...] = jnp.broadcast_to(scale, scale_one.shape)
        first_out = unit * vectors_ref[0:1] + vectors_ref[1:2]
        first_wide[...] = first_out
        first_low[...] = first_out.astype(BF16)
        first_tall[...] = first_out.T.astype(BF16)
        gathered[...] = jnp.zeros_like(gathered)
        sums_ref[...] = jnp.zeros_like(sums_ref)

    for chunk in range(chunks):

        @pl.when(step == chunk)
        def _(chunk=chunk):
            expanded = dot(first_low[...], w_expand_ref[...])
            gate = 0.5 + 0.5 * lax.erf(expanded * np.float32(np.sqrt(0.5)))
            bell = jnp.exp(expanded * expanded * -0.5) * np.float32(1.0 / np.sqrt(2.0 * np.pi))
            low = (expanded * gate).astype(BF16)
            active[chunk] = low
            slope[chunk] = gate + expanded * bell
            gathered[...] += dot(low, w_reduce_ref[...])

    @pl.when(step == chunks - 1)
    def _():
        unit, scale = normed(first_wide[...] + gathered[...])
        layer_ref[...] = (unit * vectors_ref[2:3] + vectors_ref[3:4]).astype(BF16)
        cot = cot_ref[...].astype(F32)
        sums_ref[2:3] = column_sum(cot * unit)
        sums_ref[3:4] = column_sum(cot)
        grad = norm_back(cot, vectors_ref[2:3], unit, scale)
        second_in[...] = grad
        second_low[...] = grad.astype(BF16)
        gathered[...] = grad

    for chunk in range(chunks):

        @pl.when(step == 2 * chunks - 1 - chunk)
        def _(chunk=chunk):
            grad_active = dot_nt(second_low[...], w_reduce_ref[...])
            grad_expanded = (grad_active * slope[chunk]).astype(BF16)
            reduce_ref[...] = dot_tn(active[chunk], second_low[...]).astype(BF16)
            expand_ref[...] = dot(first_tall[...], grad_expanded).astype(BF16)
            gathered[...] += dot_nt(grad_expanded, w_expand_ref[...])

    @pl.when(step == 2 * chunks - 1)
    def _():
        unit = unit_one[...]
        grad_out = gathered[...]
        sums_ref[0:1] = column_sum(grad_out * unit)
        sums_ref[1:2] = column_sum(grad_out)
        grad = norm_back(grad_out, vectors_ref[0:1], unit, scale_one[:, :1])
        first_in_ref[...] = grad
        low = grad.astype(BF16)
        real = w_out_ref.shape[0]
        project_ref[...] = dot(att_all[:real], low).astype(BF16)
        if grad_all.shape[0] > real:
            grad_all[real:] = jnp.zeros((grad_all.shape[0] - real, low.shape[0]), BF16)
        grad_all[:real] = dot_nt(w_out_ref[...], low).astype(BF16)
        for page in range(pages):
            for at in range(count):
                grad_refs[page * count + at][...] = grad_all[
                    rows_of(at), page * block : (page + 1) * block
                ]


def middle(rank, att_parts, tok, cot, w_out, vectors, w_expand, w_reduce, pages):
    rows, width = tok.shape
    count = len(att_parts) // pages
    span, block = att_parts[0].shape
    hidden = w_expand.shape[1]
    chunks = 4
    piece = hidden // chunks

    def whole(array):
        return pl.BlockSpec(array.shape, lambda s: (0,) * array.ndim)

    def there(s):
        return jnp.minimum(s, 2 * chunks - 1 - s)

    def back(s):
        return jnp.minimum(chunks - 1, 2 * chunks - 1 - s)

    shapes = [
        jax.ShapeDtypeStruct((rows, width), BF16),
        jax.ShapeDtypeStruct((rows, width), F32),
        jax.ShapeDtypeStruct((width, hidden), BF16),
        jax.ShapeDtypeStruct((hidden, width), BF16),
        jax.ShapeDtypeStruct(w_out.shape, BF16),
        jax.ShapeDtypeStruct((8, width), F32),
    ] + [jax.ShapeDtypeStruct((span, block), BF16)] * len(att_parts)
    specs = [whole(item) for item in shapes]
    specs[2] = pl.BlockSpec((width, piece), lambda s: (0, back(s)))
    specs[3] = pl.BlockSpec((piece, width), lambda s: (back(s), 0))
    return pl.pallas_call(
        functools.partial(middle_kernel, pages, count, span, chunks),
        grid=(2 * chunks,),
        in_specs=[pl.BlockSpec(memory_space=pltpu.SMEM)]
        + [whole(item) for item in att_parts]
        + [
            whole(tok),
            whole(cot),
            whole(w_out),
            whole(vectors),
            pl.BlockSpec((width, piece), lambda s: (0, there(s))),
            pl.BlockSpec((piece, width), lambda s: (there(s), 0)),
        ],
        out_specs=specs,
        out_shape=shapes,
        scratch_shapes=[
            pltpu.VMEM((count * span, rows), BF16),
            pltpu.VMEM((count * span, rows), BF16),
            pltpu.VMEM((rows, width), F32),
            pltpu.VMEM((rows, 128), F32),
            pltpu.VMEM((rows, width), F32),
            pltpu.VMEM((rows, width), BF16),
            pltpu.VMEM((width, rows), BF16),
            pltpu.VMEM((chunks, rows, piece), BF16),
            pltpu.VMEM((chunks, rows, piece), F32),
            pltpu.VMEM((rows, width), F32),
            pltpu.VMEM((rows, width), F32),
            pltpu.VMEM((rows, width), BF16),
        ],
        compiler_params=pltpu.CompilerParams(vmem_limit_bytes=VMEM_LIMIT),
        cost_estimate=pl.CostEstimate(
            flops=2 * rows * width * (6 * hidden + 3 * width),
            bytes_accessed=8 * width * hidden + 16 * rows * width,
            transcendentals=2 * rows * hidden,
        ),
        name="middle",
    )(rank, *att_parts, tok, cot, w_out, vectors, w_expand, w_reduce)


def input_kernel(pages, count, span, *refs):
    total = pages * count
    rank_ref = refs[0]
    part_refs = refs[1 : 1 + total]
    weight_ref, first_in_ref, out_ref, held = refs[1 + total :]
    rank = rank_ref[0]
    block = out_ref.shape[0] // pages
    for page in range(pages):
        for at in range(count):
            part = part_refs[page * count + at]
            for kind in range(3):
                place = pl.multiple_of(kind * count * span + (rank ^ at) * span, span)
                held[pl.ds(place, span), page * block : (page + 1) * block] = part[
                    kind * span : (kind + 1) * span
                ]
    out_ref[...] = (first_in_ref[...] + dot_tn(held[...], weight_ref[...])).astype(BF16)


def input_gradient(rank, parts, weights, first_in, pages):
    count = len(parts) // pages
    span = parts[0].shape[0] // 3
    rows, width = first_in.shape
    vmem = pl.BlockSpec(memory_space=pltpu.VMEM)
    return pl.pallas_call(
        functools.partial(input_kernel, pages, count, span),
        in_specs=[pl.BlockSpec(memory_space=pltpu.SMEM)] + [vmem] * (len(parts) + 2),
        out_specs=vmem,
        out_shape=jax.ShapeDtypeStruct((rows, width), BF16),
        scratch_shapes=[pltpu.VMEM((3 * count * span, rows), BF16)],
        compiler_params=pltpu.CompilerParams(vmem_limit_bytes=VMEM_LIMIT),
        cost_estimate=pl.CostEstimate(
            flops=6 * rows * width * count * span,
            bytes_accessed=2 * width * (5 * rows + 3 * count * span),
            transcendentals=0,
        ),
        name="input_gradient",
    )(rank, *parts, weights, first_in)


def entry_order(rows):
    return jnp.concatenate(
        [
            rows[:FREQS],
            rows[2 * FREQS : 3 * FREQS],
            rows[FREQS : 2 * FREQS],
            rows[3 * FREQS :],
        ],
        axis=0,
    )


def rotary_tables(length):
    rates = np.float32(10000.0) ** (-np.arange(HALF, dtype=np.float32) / np.float32(HALF))
    angles = np.arange(length, dtype=np.float32)[None, :] * rates[:, None].astype(np.float32)
    angles = angles.astype(np.float64)
    return np.cos(angles).astype(np.float32), np.sin(angles).astype(np.float32)


def per_device(
    tokens,
    boxes,
    w_query,
    w_key,
    w_value,
    w_output,
    box_weight,
    first_gain,
    first_shift,
    w_expand,
    w_reduce,
    second_gain,
    second_shift,
    cotangent,
):
    pages, block, width = tokens.shape
    count = lax.axis_size("blk")
    rank = lax.axis_index("blk")
    own_heads = -(-HEADS // count)
    span = own_heads * HEAD_DIM
    spare = count * span - width
    rank_word = rank.astype(jnp.int32).reshape(1)

    middle_places = (
        jnp.stack([boxes[0] + boxes[2], boxes[1] + boxes[3]]).astype(F32) * 0.5
    )
    places = jnp.concatenate(
        [middle_places] + [swapped(middle_places, i) for i in range(1, count)], axis=-1
    )
    toks = []
    for page in range(pages):
        own = tokens[page]
        toks.append(
            jnp.concatenate([own] + [swapped(own, i) for i in range(1, count)], axis=0)
        )

    def tall(weight):
        return jnp.pad(weight.T, ((0, spare), (0, 0))) if spare else weight.T

    tall_weights = jnp.stack([tall(w_query), tall(w_key), tall(w_value)])
    w_own = lax.dynamic_slice_in_dim(tall_weights, rank * span, span, axis=1).reshape(
        3, own_heads, HEAD_DIM, width
    )
    box_own = lax.dynamic_slice_in_dim(
        tall(entry_order(box_weight)), rank * span, span, axis=0
    ).reshape(own_heads, HEAD_DIM, CODES)

    rot_cos, rot_sin = (jnp.asarray(item) for item in rotary_tables(count * block))

    def relative(table):
        return jnp.concatenate(
            [
                lax.dynamic_slice_in_dim(table, (rank ^ i) * block, block, axis=1)
                for i in range(count)
            ],
            axis=1,
        )

    rot_cos, rot_sin = relative(rot_cos), relative(rot_sin)
    rates = 10000.0 ** (-jnp.arange(FREQS, dtype=F32) / FREQS)
    angles = (places[:, :, None, :] * rates[:, None]).transpose(1, 0, 2, 3)
    angles = angles.reshape(pages, 2 * FREQS, count * block)
    sines = jnp.sin(angles)
    cosines = jnp.cos(angles)
    codes = jnp.concatenate([sines, cosines], axis=1).astype(BF16)

    saved = []
    att_parts = []
    for page in range(pages):
        probs, att, att_low, heads_saved = attention_forward(
            toks[page],
            w_own,
            box_own,
            codes[page],
            sines[page],
            cosines[page],
            rot_cos,
            rot_sin,
        )
        saved.append((probs, att, heads_saved))
        for i in range(count):
            part = att_low[:, i * block : (i + 1) * block]
            att_parts.append(swapped(part, i) if i else part)

    vectors = jnp.stack([first_gain, first_shift, second_gain, second_shift])
    vectors = jnp.concatenate([vectors, jnp.zeros_like(vectors)])
    results = middle(
        rank_word,
        att_parts,
        tokens.reshape(pages * block, width),
        cotangent.reshape(pages * block, width),
        w_output,
        vectors,
        w_expand,
        w_reduce,
        pages,
    )
    layer_out, first_in, grad_expand, grad_reduce, grad_project, sums = results[:6]
    grad_parts = results[6:]
    grad_expand, grad_reduce, grad_project, sums = lax.psum(
        (grad_expand, grad_reduce, grad_project, sums.astype(BF16)), ("blk", "dp")
    )

    pre_parts = []
    weight_grads = None
    for page in range(pages):
        pieces = grad_parts[page * count : (page + 1) * count]
        grad = jnp.concatenate(
            [pieces[0]] + [swapped(pieces[i], i) for i in range(1, count)], axis=1
        )
        probs, att, heads_saved = saved[page]
        pre_grad, weight_grad = attention_backward(
            grad,
            probs,
            att,
            heads_saved,
            toks[page],
            box_own,
            codes[page],
            sines[page],
            cosines[page],
            rot_cos,
            rot_sin,
        )
        weight_grads = weight_grad if weight_grads is None else weight_grads + weight_grad
        for i in range(count):
            part = pre_grad[:, i * block : (i + 1) * block]
            pre_parts.append(swapped(part, i) if i else part)

    input_grad = input_gradient(
        rank_word,
        pre_parts,
        tall_weights.reshape(3 * count * span, width),
        first_in,
        pages,
    )
    weight_grads = lax.psum(weight_grads.astype(BF16), "dp")
    weight_grads = lax.all_gather(weight_grads.reshape(4, span, width), "blk", axis=1, tiled=True)
    weight_grads = weight_grads[:, :width].astype(F32)
    return (
        layer_out.reshape(tokens.shape),
        input_grad.reshape(tokens.shape),
        weight_grads[0].T,
        weight_grads[1].T,
        weight_grads[2].T,
        grad_project.astype(F32),
        entry_order(weight_grads[3].T),
        sums[0].astype(F32),
        sums[1].astype(F32),
        grad_expand.astype(F32),
        grad_reduce.astype(F32),
        sums[2].astype(F32),
        sums[3].astype(F32),
    )


def solution(mesh):
    split = P("dp", "blk", None)
    return jax.shard_map(
        per_device,
        mesh=mesh,
        in_specs=(split, P(None, "dp", "blk")) + (P(),) * 11 + (split,),
        out_specs=(split, split) + (P(),) * 11,
        check_vma=False,
    )
```

```python
import functools

import jax
import jax.numpy as jnp
import numpy as np
from jax import lax
from jax.experimental import pallas as pl
from jax.experimental.pallas import tpu as pltpu
from jax.sharding import PartitionSpec as P

HEADS = 12
HEAD_DIM = 64
HALF = 32
FREQS = 192
CODES = 4 * FREQS
VMEM_LIMIT = 60 * 1024 * 1024
F32 = jnp.float32
BF16 = jnp.bfloat16


def dot(left, right):
    return lax.dot_general(left, right, (((1,), (0,)), ((), ())), preferred_element_type=F32)


def dot_nt(left, right):
    return lax.dot_general(left, right, (((1,), (1,)), ((), ())), preferred_element_type=F32)


def dot_tn(left, right):
    return lax.dot_general(left, right, (((0,), (0,)), ((), ())), preferred_element_type=F32)


def swapped(block, distance, axis="blk"):
    count = lax.axis_size(axis)
    return lax.ppermute(block, axis, [(i, i ^ distance) for i in range(count)])


def from_blk(block, distance):
    return swapped(block, distance) if distance else block


def from_depth(block, distance):
    return swapped(block, 2 * distance, "dp") if distance else block


def from_core(block):
    return swapped(block, 1, "dp")


def turned(upper, lower, cosines, sines):
    return upper * cosines - lower * sines, lower * cosines + upper * sines


def forward_kernel(
    tok_ref,
    w_ref,
    box_ref,
    codes_ref,
    sin_ref,
    cos_ref,
    rot_cos_ref,
    rot_sin_ref,
    probs_ref,
    att_ref,
    att_low_ref,
    heads_ref,
    kc_ref,
    qr_ref,
):
    rows = tok_ref.shape[0]

    @pl.when(pl.program_id(0) == 0)
    def _():
        kc_ref[:, :CODES] = codes_ref[...].astype(F32).T.astype(BF16)

    weights = w_ref[...].reshape(3 * HEAD_DIM, w_ref.shape[-1])
    pre = dot_nt(weights, tok_ref[...])
    rot_cos = rot_cos_ref[...]
    rot_sin = rot_sin_ref[...]
    query_pre = pre[:HEAD_DIM].astype(BF16)
    wide = query_pre.astype(F32)
    query = jnp.concatenate(turned(wide[:HALF], wide[HALF:], rot_cos, rot_sin), axis=0)
    key_pre = pre[HEAD_DIM : 2 * HEAD_DIM]
    key = jnp.concatenate(turned(key_pre[:HALF], key_pre[HALF:], rot_cos, rot_sin), axis=0)
    value = pre[2 * HEAD_DIM :].astype(BF16)
    heads_ref[0, :HEAD_DIM] = query_pre
    heads_ref[0, HEAD_DIM : 2 * HEAD_DIM] = query.astype(BF16)
    heads_ref[0, 2 * HEAD_DIM : 3 * HEAD_DIM] = key.astype(BF16)
    heads_ref[0, 3 * HEAD_DIM :] = value
    kc_ref[:, CODES:] = key.T.astype(BF16)
    projected = dot_tn(box_ref[0], query_pre)
    sines = sin_ref[...]
    cosines = cos_ref[...]
    upper = projected[: 2 * FREQS]
    lower = projected[2 * FREQS :]
    qr_ref[: 2 * FREQS] = ((upper * cosines + lower * sines) * 0.125).astype(BF16)
    qr_ref[2 * FREQS : CODES] = ((lower * cosines - upper * sines) * 0.125).astype(BF16)
    qr_ref[CODES:] = (query * 0.125).astype(BF16)
    step = min(256, rows)
    for at in range(0, rows, step):
        logits = dot(kc_ref[...], qr_ref[:, at : at + step])
        weight = jnp.exp(logits - jnp.max(logits, axis=0, keepdims=True))
        total = jnp.sum(weight, axis=0, keepdims=True)
        probs = (weight * (1.0 / total)).astype(BF16)
        probs_ref[0, :, at : at + step] = probs
        attended = dot(value, probs)
        att_ref[0, :, at : at + step] = attended
        att_low_ref[:, at : at + step] = attended.astype(BF16)


def attention_forward(tok, w_own, box_own, codes, sines, cosines, rot_cos, rot_sin):
    rows, width = tok.shape
    heads = w_own.shape[1]

    def whole(array):
        return pl.BlockSpec(array.shape, lambda h: (0,) * array.ndim)

    return pl.pallas_call(
        forward_kernel,
        grid=(heads,),
        in_specs=[
            whole(tok),
            pl.BlockSpec((3, 1, HEAD_DIM, width), lambda h: (0, h, 0, 0)),
            pl.BlockSpec((1, HEAD_DIM, CODES), lambda h: (h, 0, 0)),
            whole(codes),
            whole(sines),
            whole(cosines),
            whole(rot_cos),
            whole(rot_sin),
        ],
        out_specs=[
            pl.BlockSpec((1, rows, rows), lambda h: (h, 0, 0)),
            pl.BlockSpec((1, HEAD_DIM, rows), lambda h: (h, 0, 0)),
            pl.BlockSpec((HEAD_DIM, rows), lambda h: (h, 0)),
            pl.BlockSpec((1, 4 * HEAD_DIM, rows), lambda h: (h, 0, 0)),
        ],
        out_shape=[
            jax.ShapeDtypeStruct((heads, rows, rows), BF16),
            jax.ShapeDtypeStruct((heads, HEAD_DIM, rows), F32),
            jax.ShapeDtypeStruct((heads * HEAD_DIM, rows), BF16),
            jax.ShapeDtypeStruct((heads, 4 * HEAD_DIM, rows), BF16),
        ],
        scratch_shapes=[
            pltpu.VMEM((rows, CODES + HEAD_DIM), BF16),
            pltpu.VMEM((CODES + HEAD_DIM, rows), BF16),
        ],
        compiler_params=pltpu.CompilerParams(vmem_limit_bytes=VMEM_LIMIT),
        cost_estimate=pl.CostEstimate(
            flops=2 * heads * rows * (rows * 1100 + 200 * width + 64 * CODES),
            bytes_accessed=2 * heads * rows * rows + 12 * rows * width,
            transcendentals=heads * rows * rows,
        ),
        name="attention_forward",
    )(tok, w_own, box_own, codes, sines, cosines, rot_cos, rot_sin)


def backward_kernel(last, words_ref, *refs):
    (
        grad_ref,
        probs_ref,
        att_ref,
        heads_ref,
        tok_ref,
        box_ref,
        codes_ref,
        sin_ref,
        cos_ref,
        rot_cos_ref,
        rot_sin_ref,
    ) = refs[:11]
    if last:
        before_ref, pre_grad_ref, mine_ref, theirs_ref = refs[11:15]
        weight_grad_ref, kc_ref, query_grad_ref = refs[15:]
    else:
        pre_grad_ref, weight_grad_ref, kc_ref, query_grad_ref = refs[11:]
    rows = tok_ref.shape[0]
    head = pl.program_id(0)
    span = pl.num_programs(0) * HEAD_DIM

    @pl.when(head == 0)
    def _():
        kc_ref[:CODES] = codes_ref[...]

    kc_ref[CODES:] = heads_ref[0, 2 * HEAD_DIM : 3 * HEAD_DIM]
    packed = heads_ref[0].astype(F32).T.astype(BF16)
    query_pre = packed[:, :HEAD_DIM]
    query = packed[:, HEAD_DIM : 2 * HEAD_DIM]
    value = packed[:, 3 * HEAD_DIM :] * jnp.asarray(0.125, BF16)
    rot_cos = rot_cos_ref[...]
    rot_sin = rot_sin_ref[...]
    grad = grad_ref[...]
    grad_tall = grad.astype(F32).T.astype(BF16)
    offsets = jnp.sum(grad.astype(F32) * att_ref[0], axis=0, keepdims=True) * 0.125
    step = min(256, rows)
    key_grad = jnp.zeros((rows, HEAD_DIM), F32)
    value_grad = jnp.zeros((rows, HEAD_DIM), F32)
    box_grad = jnp.zeros((CODES, HEAD_DIM), F32)
    for at in range(0, rows, step):
        part = slice(at, at + step)
        probs = probs_ref[0, :, part]
        grad_probs = dot(value, grad[:, part])
        grad_logits = (probs.astype(F32) * (grad_probs - offsets[:, part])).astype(BF16)
        back = dot(kc_ref[...], grad_logits)
        sines = sin_ref[:, part]
        cosines = cos_ref[:, part]
        upper = back[: 2 * FREQS]
        lower = back[2 * FREQS : CODES]
        projected_grad = jnp.concatenate(
            [
                (upper * cosines - lower * sines).astype(BF16),
                (lower * cosines + upper * sines).astype(BF16),
            ],
            axis=0,
        )
        first = back[CODES : CODES + HALF]
        second = back[CODES + HALF :]
        own = jnp.concatenate(
            turned(first, second, rot_cos[:, part], -rot_sin[:, part]), axis=0
        )
        query_grad_ref[:, part] = (own + dot(box_ref[0], projected_grad)).astype(BF16)
        key_grad = key_grad + dot(grad_logits, query[part])
        value_grad = value_grad + dot(probs, grad_tall[part])
        box_grad = box_grad + dot(projected_grad, query_pre[part])
    key_flat = key_grad.T
    key_low = jnp.concatenate(
        turned(key_flat[:HALF], key_flat[HALF:], rot_cos, -rot_sin), axis=0
    ).astype(BF16)
    place = pl.multiple_of(head * HEAD_DIM, HEAD_DIM)
    pre_grad_ref[pl.ds(place, HEAD_DIM)] = query_grad_ref[...]
    pre_grad_ref[pl.ds(span + place, HEAD_DIM)] = key_low
    pre_grad_ref[pl.ds(2 * span + place, HEAD_DIM)] = value_grad.T.astype(BF16)
    weight_grad_ref[pl.ds(3 * span + place, HEAD_DIM)] = box_grad.T

    @pl.when(head == pl.num_programs(0) - 1)
    def _():
        weight_grad_ref[: 3 * span] = dot(pre_grad_ref[...], tok_ref[...])
        if last:
            half = 2 * span
            core = words_ref[2]
            here = pl.ds(pl.multiple_of(core * half, half), half)
            there = pl.ds(pl.multiple_of((1 - core) * half, half), half)
            mine_ref[...] = weight_grad_ref[here] + before_ref[here]
            theirs_ref[...] = (weight_grad_ref[there] + before_ref[there]).astype(BF16)


def attention_backward(
    words,
    grad,
    probs,
    att,
    heads_saved,
    tok,
    box_own,
    codes,
    sines,
    cosines,
    rot_cos,
    rot_sin,
    before=None,
):
    rows, width = tok.shape
    heads = probs.shape[0]
    last = before is not None
    grads_shape = (4 * heads * HEAD_DIM, width)
    half_shape = (2 * heads * HEAD_DIM, width)
    extra = (before,) if last else ()

    def whole(array):
        return pl.BlockSpec(array.shape, lambda h: (0,) * array.ndim)

    out_shape = [jax.ShapeDtypeStruct((3 * heads * HEAD_DIM, rows), BF16)]
    if last:
        out_shape += [
            jax.ShapeDtypeStruct(half_shape, F32),
            jax.ShapeDtypeStruct(half_shape, BF16),
        ]
    else:
        out_shape.append(jax.ShapeDtypeStruct(grads_shape, F32))
    return pl.pallas_call(
        functools.partial(backward_kernel, last),
        grid=(heads,),
        in_specs=[
            pl.BlockSpec(memory_space=pltpu.SMEM),
            pl.BlockSpec((HEAD_DIM, rows), lambda h: (h, 0)),
            pl.BlockSpec((1, rows, rows), lambda h: (h, 0, 0)),
            pl.BlockSpec((1, HEAD_DIM, rows), lambda h: (h, 0, 0)),
            pl.BlockSpec((1, 4 * HEAD_DIM, rows), lambda h: (h, 0, 0)),
            whole(tok),
            pl.BlockSpec((1, HEAD_DIM, CODES), lambda h: (h, 0, 0)),
            whole(codes),
            whole(sines),
            whole(cosines),
            whole(rot_cos),
            whole(rot_sin),
        ]
        + [whole(item) for item in extra],
        out_specs=[whole(item) for item in out_shape],
        out_shape=out_shape,
        scratch_shapes=([pltpu.VMEM(grads_shape, F32)] if last else [])
        + [
            pltpu.VMEM((CODES + HEAD_DIM, rows), BF16),
            pltpu.VMEM((HEAD_DIM, rows), BF16),
        ],
        compiler_params=pltpu.CompilerParams(vmem_limit_bytes=VMEM_LIMIT),
        cost_estimate=pl.CostEstimate(
            flops=2 * heads * rows * (rows * 1400 + 200 * width + 128 * CODES),
            bytes_accessed=2 * heads * rows * rows + 12 * rows * width,
            transcendentals=0,
        ),
        name="attention_backward",
    )(
        words,
        grad,
        probs,
        att,
        heads_saved,
        tok,
        box_own,
        codes,
        sines,
        cosines,
        rot_cos,
        rot_sin,
        *extra,
    )


def normed(value):
    centered = value - jnp.mean(value, axis=-1, keepdims=True)
    scale = lax.rsqrt(jnp.mean(centered * centered, axis=-1, keepdims=True) + 1e-05)
    return centered * scale, scale


def norm_back(grad, gain, unit, scale):
    scaled = grad * gain
    return scale * (
        scaled
        - jnp.mean(scaled, axis=-1, keepdims=True)
        - unit * jnp.mean(scaled * unit, axis=-1, keepdims=True)
    )


def column_sum(value):
    return jnp.sum(value, axis=0, keepdims=True)


def middle_kernel(pages, count, span, chunks, *refs):
    total = pages * count
    words_ref = refs[0]
    att_refs = refs[1 : 1 + total]
    (
        tok_ref,
        cot_ref,
        w_out_ref,
        vectors_ref,
        w_expand_ref,
        w_reduce_ref,
    ) = refs[1 + total : 7 + total]
    outs = refs[7 + total :]
    layer_ref, first_in_ref, theirs_ref, mine_ref, project_ref, sums_ref = outs[:6]
    grad_refs = outs[6 : 6 + total]
    (
        att_all,
        grad_all,
        unit_one,
        scale_one,
        first_wide,
        first_low,
        first_tall,
        active,
        slope,
        gathered,
        second_in,
        second_low,
    ) = outs[6 + total :]
    rank = words_ref[0]
    width = tok_ref.shape[1]
    block = tok_ref.shape[0] // pages
    step = pl.program_id(0)

    def rows_of(at):
        return pl.ds(pl.multiple_of((rank ^ at) * span, span), span)

    @pl.when(step == 0)
    def _():
        for page in range(pages):
            for at in range(count):
                att_all[rows_of(at), page * block : (page + 1) * block] = att_refs[
                    page * count + at
                ][...]
        branch = dot_tn(att_all[: w_out_ref.shape[0]], w_out_ref[...])
        unit, scale = normed(tok_ref[...].astype(F32) + branch)
        unit_one[...] = unit
        scale_one[...] = jnp.broadcast_to(scale, scale_one.shape)
        first_out = unit * vectors_ref[0:1] + vectors_ref[1:2]
        first_wide[...] = first_out
        first_low[...] = first_out.astype(BF16)
        first_tall[...] = first_out.T.astype(BF16)
        gathered[...] = jnp.zeros_like(gathered)
        sums_ref[...] = jnp.zeros_like(sums_ref)

    for chunk in range(chunks):

        @pl.when(step == chunk)
        def _(chunk=chunk):
            expanded = dot(first_low[...], w_expand_ref[...])
            gate = 0.5 + 0.5 * lax.erf(expanded * np.float32(np.sqrt(0.5)))
            bell = jnp.exp(expanded * expanded * -0.5) * np.float32(1.0 / np.sqrt(2.0 * np.pi))
            low = (expanded * gate).astype(BF16)
            active[chunk] = low
            slope[chunk] = gate + expanded * bell
            gathered[...] += dot(low, w_reduce_ref[...])

    @pl.when(step == chunks - 1)
    def _():
        unit, scale = normed(first_wide[...] + gathered[...])
        layer_ref[...] = (unit * vectors_ref[2:3] + vectors_ref[3:4]).astype(BF16)
        cot = cot_ref[...].astype(F32)
        sums_ref[2:3] = column_sum(cot * unit)
        sums_ref[3:4] = column_sum(cot)
        grad = norm_back(cot, vectors_ref[2:3], unit, scale)
        second_in[...] = grad
        second_low[...] = grad.astype(BF16)
        gathered[...] = grad

    for chunk in range(chunks):

        @pl.when(step == 2 * chunks - 1 - chunk)
        def _(chunk=chunk):
            grad_active = dot_nt(second_low[...], w_reduce_ref[...])
            grad_expanded = (grad_active * slope[chunk]).astype(BF16)
            grads_ref = mine_ref if chunk < chunks // 2 else theirs_ref
            grads_ref[:width] = dot(first_tall[...], grad_expanded).astype(BF16)
            grads_ref[width:] = dot_tn(active[chunk], second_low[...]).astype(BF16)
            gathered[...] += dot_nt(grad_expanded, w_expand_ref[...])

    @pl.when(step == 2 * chunks - 1)
    def _():
        unit = unit_one[...]
        grad_out = gathered[...]
        sums_ref[0:1] = column_sum(grad_out * unit)
        sums_ref[1:2] = column_sum(grad_out)
        grad = norm_back(grad_out, vectors_ref[0:1], unit, scale_one[:, :1])
        first_in_ref[...] = grad
        low = grad.astype(BF16)
        real = w_out_ref.shape[0]
        project_ref[...] = dot(att_all[:real], low).astype(BF16)
        if grad_all.shape[0] > real:
            grad_all[real:] = jnp.zeros((grad_all.shape[0] - real, low.shape[0]), BF16)
        grad_all[:real] = dot_nt(w_out_ref[...], low).astype(BF16)
        for page in range(pages):
            for at in range(count):
                grad_refs[page * count + at][...] = grad_all[
                    rows_of(at), page * block : (page + 1) * block
                ]


def middle(words, att_parts, tok, cot, w_out, vectors, w_expand, w_reduce, pages):
    rows, width = tok.shape
    count = len(att_parts) // pages
    span, block = att_parts[0].shape
    hidden = w_expand.shape[1]
    chunks = hidden // width
    pairs = chunks // 2

    def whole(array):
        return pl.BlockSpec(array.shape, lambda s, words: (0,) * len(array.shape))

    def chunk_at(s, words):
        at = jnp.minimum(s, 2 * chunks - 1 - s)
        return (at + words[2] * pairs) % chunks

    def theirs_at(s, words):
        return jnp.clip(2 * chunks - 1 - s - pairs, 0, pairs - 1), 0

    def mine_at(s, words):
        return jnp.clip(2 * chunks - 1 - s, 0, pairs - 1), 0

    shapes = [
        jax.ShapeDtypeStruct((rows, width), BF16),
        jax.ShapeDtypeStruct((rows, width), F32),
        jax.ShapeDtypeStruct((hidden, width), BF16),
        jax.ShapeDtypeStruct((hidden, width), BF16),
        jax.ShapeDtypeStruct(w_out.shape, BF16),
        jax.ShapeDtypeStruct((8, width), F32),
    ] + [jax.ShapeDtypeStruct((span, block), BF16)] * len(att_parts)
    specs = [whole(item) for item in shapes]
    specs[2] = pl.BlockSpec((2 * width, width), theirs_at)
    specs[3] = pl.BlockSpec((2 * width, width), mine_at)
    return pl.pallas_call(
        functools.partial(middle_kernel, pages, count, span, chunks),
        grid_spec=pltpu.PrefetchScalarGridSpec(
            num_scalar_prefetch=1,
            grid=(2 * chunks,),
            in_specs=[whole(item) for item in att_parts]
            + [
                whole(tok),
                whole(cot),
                whole(w_out),
                whole(vectors),
                pl.BlockSpec((width, width), lambda s, words: (0, chunk_at(s, words))),
                pl.BlockSpec((width, width), lambda s, words: (chunk_at(s, words), 0)),
            ],
            out_specs=specs,
            scratch_shapes=[
                pltpu.VMEM((count * span, rows), BF16),
                pltpu.VMEM((count * span, rows), BF16),
                pltpu.VMEM((rows, width), F32),
                pltpu.VMEM((rows, 128), F32),
                pltpu.VMEM((rows, width), F32),
                pltpu.VMEM((rows, width), BF16),
                pltpu.VMEM((width, rows), BF16),
                pltpu.VMEM((chunks, rows, width), BF16),
                pltpu.VMEM((chunks, rows, width), F32),
                pltpu.VMEM((rows, width), F32),
                pltpu.VMEM((rows, width), F32),
                pltpu.VMEM((rows, width), BF16),
            ],
        ),
        out_shape=shapes,
        compiler_params=pltpu.CompilerParams(vmem_limit_bytes=VMEM_LIMIT),
        cost_estimate=pl.CostEstimate(
            flops=2 * rows * width * (6 * hidden + 3 * width),
            bytes_accessed=8 * width * hidden + 16 * rows * width,
            transcendentals=2 * rows * hidden,
        ),
        name="middle",
    )(words, *att_parts, tok, cot, w_out, vectors, w_expand, w_reduce)


def input_kernel(pages, count, span, *refs):
    total = pages * count
    words_ref = refs[0]
    part_refs = refs[1 : 1 + total]
    weight_ref, first_in_ref, out_ref, held = refs[1 + total :]
    rank = words_ref[0]
    block = out_ref.shape[0] // pages
    for page in range(pages):
        for at in range(count):
            part = part_refs[page * count + at]
            for kind in range(3):
                place = pl.multiple_of(kind * count * span + (rank ^ at) * span, span)
                held[pl.ds(place, span), page * block : (page + 1) * block] = part[
                    kind * span : (kind + 1) * span
                ]
    out_ref[...] = (first_in_ref[...] + dot_tn(held[...], weight_ref[...])).astype(BF16)


def input_gradient(words, parts, weights, first_in, pages):
    count = len(parts) // pages
    span = parts[0].shape[0] // 3
    rows, width = first_in.shape
    vmem = pl.BlockSpec(memory_space=pltpu.VMEM)
    return pl.pallas_call(
        functools.partial(input_kernel, pages, count, span),
        in_specs=[pl.BlockSpec(memory_space=pltpu.SMEM)] + [vmem] * (len(parts) + 2),
        out_specs=vmem,
        out_shape=jax.ShapeDtypeStruct((rows, width), BF16),
        scratch_shapes=[pltpu.VMEM((3 * count * span, rows), BF16)],
        compiler_params=pltpu.CompilerParams(vmem_limit_bytes=VMEM_LIMIT),
        cost_estimate=pl.CostEstimate(
            flops=6 * rows * width * count * span,
            bytes_accessed=2 * width * (5 * rows + 3 * count * span),
            transcendentals=0,
        ),
        name="input_gradient",
    )(words, *parts, weights, first_in)


def local(body, name, words, arrays, shapes):
    def kernel(words_ref, *refs):
        body(words_ref, refs[: len(arrays)], refs[len(arrays) :])

    vmem = pl.BlockSpec(memory_space=pltpu.VMEM)
    shapes = [jax.ShapeDtypeStruct(shape, kind) for shape, kind in shapes]
    moved = sum(item.size * item.dtype.itemsize for item in list(arrays) + shapes)
    return pl.pallas_call(
        kernel,
        in_specs=[pl.BlockSpec(memory_space=pltpu.SMEM)] + [vmem] * len(arrays),
        out_specs=[vmem] * len(shapes),
        out_shape=shapes,
        compiler_params=pltpu.CompilerParams(vmem_limit_bytes=VMEM_LIMIT),
        cost_estimate=pl.CostEstimate(flops=moved, bytes_accessed=moved, transcendentals=0),
        name=name,
    )(words, *arrays)


def shard(index, rows, base=0):
    return pl.ds(pl.multiple_of(base + index * rows, 16), rows)


def total_of(refs, rows=slice(None)):
    total = refs[0][rows].astype(F32)
    for ref in refs[1:]:
        total = total + ref[rows].astype(F32)
    return total


class Plan:
    def __init__(self, words, rows, rows_a, width):
        self.words = words
        self.count = lax.axis_size("blk")
        self.depth = lax.axis_size("dp") // 2
        self.rows = rows
        self.rows_a = rows_a
        self.width = width
        self.a_one = rows_a // self.count
        self.a_two = self.a_one // self.depth
        self.b_one = (rows - rows_a) // self.depth
        self.b_two = self.b_one // self.count

    def shapes(self, rows_a, a, rows_b, b):
        return [((rows_a, self.width), BF16)] * a + [((rows_b, self.width), BF16)] * b

    def scatter_one(self, mine, theirs):
        def body(words, ins, outs):
            for i in range(self.count):
                rows = shard(words[0] ^ i, self.a_one)
                outs[i][...] = total_of(ins, rows).astype(BF16)
            for k in range(self.depth):
                rows = shard(words[1] ^ k, self.b_one, self.rows_a)
                outs[self.count + k][...] = total_of(ins, rows).astype(BF16)

        shapes = self.shapes(self.a_one, self.count, self.b_one, self.depth)
        return local(body, "scatter_one", self.words, [mine, theirs], shapes)

    def send_one(self, parts):
        return [from_blk(parts[i], i) for i in range(self.count)] + [
            from_depth(parts[self.count + k], k) for k in range(self.depth)
        ]

    def scatter_two(self, parts):
        def body(words, ins, outs):
            for k in range(self.depth):
                rows = shard(words[1] ^ k, self.a_two)
                outs[k][...] = total_of(ins[: self.count], rows).astype(BF16)
            for i in range(self.count):
                rows = shard(words[0] ^ i, self.b_two)
                outs[self.depth + i][...] = total_of(ins[self.count :], rows).astype(BF16)

        shapes = self.shapes(self.a_two, self.depth, self.b_two, self.count)
        return local(body, "scatter_two", self.words, parts, shapes)

    def send_two(self, parts):
        return [from_depth(parts[k], k) for k in range(self.depth)] + [
            from_blk(parts[self.depth + i], i) for i in range(self.count)
        ]

    def finish(self, parts):
        def body(words, ins, outs):
            outs[0][...] = total_of(ins[: self.depth]).astype(BF16)
            outs[1][...] = total_of(ins[self.depth :]).astype(BF16)

        shapes = self.shapes(self.a_two, 1, self.b_two, 1)
        return local(body, "scatter_sum", self.words, parts, shapes)

    def gather_one(self, a, b):
        parts = self.send_two([a] * self.depth + [b] * self.count)

        def body(words, ins, outs):
            for k in range(self.depth):
                outs[0][shard(words[1] ^ k, self.a_two)] = ins[k][...]
            for i in range(self.count):
                outs[1][shard(words[0] ^ i, self.b_two)] = ins[self.depth + i][...]

        shapes = self.shapes(self.a_one, 1, self.b_one, 1)
        return local(body, "gather_one", self.words, parts, shapes)

    def gather_two(self, a, b):
        parts = self.send_one([a] * self.count + [b] * self.depth)

        def body(words, ins, outs):
            for i in range(self.count):
                outs[0][shard(words[0] ^ i, self.a_one)] = ins[i][...]
            for k in range(self.depth):
                rows = shard(words[1] ^ k, self.b_one, self.rows_a)
                outs[0][rows] = ins[self.count + k][...]

        return local(body, "gather_two", self.words, parts, self.shapes(self.rows, 1, 0, 0))[0]


def widened(words, mine, theirs, hidden):
    width = mine.shape[1]
    chunks = hidden // width
    pairs = chunks // 2

    def kernel(words_ref, mine_ref, theirs_ref, expand_ref, reduce_ref):
        @pl.when(pl.program_id(0) < pairs)
        def _():
            expand_ref[...] = mine_ref[:width].astype(F32)
            reduce_ref[...] = mine_ref[width:].astype(F32)

        @pl.when(pl.program_id(0) >= pairs)
        def _():
            expand_ref[...] = theirs_ref[:width].astype(F32)
            reduce_ref[...] = theirs_ref[width:].astype(F32)

    def place(s, words):
        return (s + words[2] * pairs) % chunks

    block = (2 * width, width)
    return pl.pallas_call(
        kernel,
        grid_spec=pltpu.PrefetchScalarGridSpec(
            num_scalar_prefetch=1,
            grid=(chunks,),
            in_specs=[
                pl.BlockSpec(block, lambda s, words: (jnp.minimum(s, pairs - 1), 0)),
                pl.BlockSpec(block, lambda s, words: (jnp.maximum(s - pairs, 0), 0)),
            ],
            out_specs=[
                pl.BlockSpec((width, width), lambda s, words: (0, place(s, words))),
                pl.BlockSpec((width, width), lambda s, words: (place(s, words), 0)),
            ],
        ),
        out_shape=[
            jax.ShapeDtypeStruct((width, hidden), F32),
            jax.ShapeDtypeStruct((hidden, width), F32),
        ],
        compiler_params=pltpu.CompilerParams(vmem_limit_bytes=VMEM_LIMIT),
        cost_estimate=pl.CostEstimate(
            flops=0, bytes_accessed=12 * hidden * width, transcendentals=0
        ),
        name="widen",
    )(words, mine, theirs)


def gather_heads(words, mine, theirs):
    count = lax.axis_size("blk")
    depth = lax.axis_size("dp") // 2
    half, width = mine.shape
    piece = half // depth
    other = from_core(theirs)

    def split(words, ins, outs):
        for k in range(depth):
            outs[k][...] = total_of(ins, shard(words[1] ^ k, piece)).astype(BF16)

    parts = local(split, "heads_scatter", words, [mine, other], [((piece, width), BF16)] * depth)
    parts = [from_depth(parts[k], k) for k in range(depth)]

    def add(words, ins, outs):
        outs[0][...] = total_of(ins).astype(BF16)

    own = local(add, "heads_sum", words, parts, [((piece, width), BF16)])[0]
    parts = [from_depth(own, k) for k in range(depth)]

    def join(words, ins, outs):
        for k in range(depth):
            outs[0][shard(words[1] ^ k, piece)] = ins[k][...]

    own = local(join, "heads_gather_one", words, parts, [((half, width), BF16)])[0]
    parts = [from_blk(own, i) for i in range(count)]

    def join_blk(words, ins, outs):
        for i in range(count):
            outs[0][shard(words[0] ^ i, half)] = ins[i][...]

    own = local(join_blk, "heads_gather_two", words, parts, [((count * half, width), BF16)])[0]
    return own, from_core(own)


def entry_order(rows):
    return jnp.concatenate(
        [
            rows[:FREQS],
            rows[2 * FREQS : 3 * FREQS],
            rows[FREQS : 2 * FREQS],
            rows[3 * FREQS :],
        ],
        axis=0,
    )


def rotary_tables(length):
    rates = np.float32(10000.0) ** (-np.arange(HALF, dtype=np.float32) / np.float32(HALF))
    angles = np.arange(length, dtype=np.float32)[None, :] * rates[:, None].astype(np.float32)
    angles = angles.astype(np.float64)
    return np.cos(angles).astype(np.float32), np.sin(angles).astype(np.float32)


def per_device(
    tokens,
    boxes,
    w_query,
    w_key,
    w_value,
    w_output,
    box_weight,
    first_gain,
    first_shift,
    w_expand,
    w_reduce,
    second_gain,
    second_shift,
    cotangent,
):
    pages, block, width = tokens.shape
    count = lax.axis_size("blk")
    rank = lax.axis_index("blk")
    own_heads = -(-HEADS // count)
    span = own_heads * HEAD_DIM
    spare = count * span - width
    dp_rank = lax.axis_index("dp")
    words = jnp.stack([rank, dp_rank // 2, dp_rank % 2]).astype(jnp.int32)
    hidden = w_expand.shape[1]

    middle_places = (
        jnp.stack([boxes[0] + boxes[2], boxes[1] + boxes[3]]).astype(F32) * 0.5
    )
    places = jnp.concatenate(
        [middle_places] + [swapped(middle_places, i) for i in range(1, count)], axis=-1
    )
    toks = []
    for page in range(pages):
        own = tokens[page]
        toks.append(
            jnp.concatenate([own] + [swapped(own, i) for i in range(1, count)], axis=0)
        )

    def tall(weight):
        return jnp.pad(weight.T, ((0, spare), (0, 0))) if spare else weight.T

    tall_weights = jnp.stack([tall(w_query), tall(w_key), tall(w_value)])
    w_own = lax.dynamic_slice_in_dim(tall_weights, rank * span, span, axis=1).reshape(
        3, own_heads, HEAD_DIM, width
    )
    box_own = lax.dynamic_slice_in_dim(
        tall(entry_order(box_weight)), rank * span, span, axis=0
    ).reshape(own_heads, HEAD_DIM, CODES)

    rot_cos, rot_sin = (jnp.asarray(item) for item in rotary_tables(count * block))

    def relative(table):
        return jnp.concatenate(
            [
                lax.dynamic_slice_in_dim(table, (rank ^ i) * block, block, axis=1)
                for i in range(count)
            ],
            axis=1,
        )

    rot_cos, rot_sin = relative(rot_cos), relative(rot_sin)
    rates = 10000.0 ** (-jnp.arange(FREQS, dtype=F32) / FREQS)
    angles = (places[:, :, None, :] * rates[:, None]).transpose(1, 0, 2, 3)
    angles = angles.reshape(pages, 2 * FREQS, count * block)
    sines = jnp.sin(angles)
    cosines = jnp.cos(angles)
    codes = jnp.concatenate([sines, cosines], axis=1).astype(BF16)

    saved = []
    att_parts = []
    for page in range(pages):
        probs, att, att_low, heads_saved = attention_forward(
            toks[page],
            w_own,
            box_own,
            codes[page],
            sines[page],
            cosines[page],
            rot_cos,
            rot_sin,
        )
        saved.append((probs, att, heads_saved))
        for i in range(count):
            part = att_low[:, i * block : (i + 1) * block]
            att_parts.append(swapped(part, i) if i else part)

    vectors = jnp.stack([first_gain, first_shift, second_gain, second_shift])
    vectors = jnp.concatenate([vectors, jnp.zeros_like(vectors)])
    results = middle(
        words,
        att_parts,
        tokens.reshape(pages * block, width),
        cotangent.reshape(pages * block, width),
        w_output,
        vectors,
        w_expand,
        w_reduce,
        pages,
    )
    layer_out, first_in, ff_theirs, ff_mine, grad_project, sums = results[:6]
    grad_parts = results[6:]
    grads = []
    for page in range(pages):
        pieces = grad_parts[page * count : (page + 1) * count]
        grads.append(
            jnp.concatenate([from_blk(pieces[i], i) for i in range(count)], axis=1)
        )
    plan = Plan(words, hidden, 2 * hidden // 3, width)
    parts = plan.scatter_one(ff_mine, from_core(ff_theirs))
    grad_project, sums = lax.psum((grad_project, sums.astype(BF16)), ("blk", "dp"))

    pre_parts = []
    before = None
    for page in range(pages):
        (grads[page], parts) = lax.optimization_barrier((grads[page], parts))
        parts = plan.send_one(parts) if page == 0 else parts
        if page == pages - 1:
            parts = plan.send_two(parts)
        probs, att, heads_saved = saved[page]
        pre_grad, *weight_grads = attention_backward(
            words,
            grads[page],
            probs,
            att,
            heads_saved,
            toks[page],
            box_own,
            codes[page],
            sines[page],
            cosines[page],
            rot_cos,
            rot_sin,
            before,
        )
        before = weight_grads[0]
        (pre_grad, parts) = lax.optimization_barrier((pre_grad, parts))
        parts = plan.scatter_two(parts) if page == 0 else parts
        for i in range(count):
            part = pre_grad[:, i * block : (i + 1) * block]
            pre_parts.append(from_blk(part, i))
    ff_a, ff_b = plan.finish(parts)
    ff_own = plan.gather_two(*plan.gather_one(ff_a, ff_b))
    grad_expand, grad_reduce = widened(words, ff_own, from_core(ff_own), hidden)
    heads_own, heads_other = gather_heads(words, *weight_grads)
    input_grad = input_gradient(
        words,
        pre_parts,
        tall_weights.reshape(3 * count * span, width),
        first_in,
        pages,
    )
    core = dp_rank % 2
    lower = jnp.where(core == 0, heads_own, heads_other).reshape(count, 2, span, width)
    upper = jnp.where(core == 0, heads_other, heads_own).reshape(count, 2, span, width)

    def weight_grad(part):
        return part.reshape(count * span, width)[:width].astype(F32).T

    return (
        layer_out.reshape(tokens.shape),
        input_grad.reshape(tokens.shape),
        weight_grad(lower[:, 0]),
        weight_grad(lower[:, 1]),
        weight_grad(upper[:, 0]),
        grad_project.astype(F32),
        entry_order(weight_grad(upper[:, 1])),
        sums[0].astype(F32),
        sums[1].astype(F32),
        grad_expand,
        grad_reduce,
        sums[2].astype(F32),
        sums[3].astype(F32),
    )


def solution(mesh):
    split = P("dp", "blk", None)
    return jax.shard_map(
        per_device,
        mesh=mesh,
        in_specs=(split, P(None, "dp", "blk")) + (P(),) * 11 + (split,),
        out_specs=(split, split) + (P(),) * 11,
        check_vma=False,
    )
```

```python
import functools

import jax
import jax.numpy as jnp
import numpy as np
from jax import lax
from jax.experimental import pallas as pl
from jax.experimental.pallas import tpu as pltpu
from jax.sharding import PartitionSpec as P

HEADS = 12
HEAD_DIM = 64
HALF = 32
FREQS = 192
CODES = 4 * FREQS
VMEM_LIMIT = 60 * 1024 * 1024
F32 = jnp.float32
BF16 = jnp.bfloat16


def dot(left, right):
    return lax.dot_general(left, right, (((1,), (0,)), ((), ())), preferred_element_type=F32)


def dot_nt(left, right):
    return lax.dot_general(left, right, (((1,), (1,)), ((), ())), preferred_element_type=F32)


def dot_tn(left, right):
    return lax.dot_general(left, right, (((0,), (0,)), ((), ())), preferred_element_type=F32)


def swapped(block, distance, axis="blk"):
    count = lax.axis_size(axis)
    return lax.ppermute(block, axis, [(i, i ^ distance) for i in range(count)])


def from_blk(block, distance):
    return swapped(block, distance) if distance else block


def from_depth(block, distance):
    return swapped(block, 2 * distance, "dp") if distance else block


def from_core(block):
    return swapped(block, 1, "dp")


def after(done, value):
    return lax.optimization_barrier((value, done))[0]


def turned(upper, lower, cosines, sines):
    return upper * cosines - lower * sines, lower * cosines + upper * sines


def entry_order(rows):
    return jnp.concatenate(
        [
            rows[:FREQS],
            rows[2 * FREQS : 3 * FREQS],
            rows[FREQS : 2 * FREQS],
            rows[3 * FREQS :],
        ],
        axis=0,
    )


def angle_tables():
    rates = np.float32(10000.0) ** (-np.arange(FREQS, dtype=np.float32) / np.float32(FREQS))
    tables = []
    for places in (32.0 * np.arange(32), 0.5 * np.arange(64)):
        angles = rates.astype(np.float64)[:, None] * places[None, :]
        left = np.concatenate([np.sin(angles), np.cos(angles)])
        parts = []
        for _ in range(3):
            parts.append(left.astype(jnp.bfloat16))
            left = left - parts[-1].astype(np.float64)
        tables.append(np.concatenate(parts, axis=1))
    return tables


def rotary_tables(length):
    rates = np.float32(10000.0) ** (-np.arange(HALF, dtype=np.float32) / np.float32(HALF))
    angles = np.arange(length, dtype=np.float32)[None, :] * rates[:, None]
    angles = angles.astype(np.float64)
    return np.cos(angles).astype(np.float32), np.sin(angles).astype(np.float32)


def prepare_kernel(
    words_ref,
    query_ref,
    key_ref,
    value_ref,
    box_ref,
    cos_ref,
    sin_ref,
    own_ref,
    own_box_ref,
    own_cos_ref,
    own_sin_ref,
):
    rank = words_ref[0]
    span = own_box_ref.shape[0]
    width = query_ref.shape[1]
    count = cos_ref.shape[1] // (own_cos_ref.shape[1] // lax.axis_size("blk"))
    block = cos_ref.shape[1] // count
    row = lax.broadcasted_iota(jnp.int32, (span, width), 0) + rank * span
    column = lax.broadcasted_iota(jnp.int32, (span, width), 1)
    pick = jnp.where(row == column, 1.0, 0.0).astype(BF16)
    for kind, ref in enumerate((query_ref, key_ref, value_ref)):
        own_ref[kind] = dot_nt(pick, ref[...]).astype(BF16)
    own_box_ref[...] = dot_nt(pick, entry_order(box_ref[...])).astype(BF16)
    for i in range(count):
        from_cols = pl.ds(pl.multiple_of((rank ^ i) * block, block), block)
        own_cos_ref[:, i * block : (i + 1) * block] = cos_ref[:, from_cols]
        own_sin_ref[:, i * block : (i + 1) * block] = sin_ref[:, from_cols]


def prepare(words, w_query, w_key, w_value, box_weight, span, length):
    width = w_query.shape[0]
    vmem = pl.BlockSpec(memory_space=pltpu.VMEM)
    return pl.pallas_call(
        prepare_kernel,
        in_specs=[pl.BlockSpec(memory_space=pltpu.SMEM)] + [vmem] * 6,
        out_specs=[vmem] * 4,
        out_shape=[
            jax.ShapeDtypeStruct((3, span, width), BF16),
            jax.ShapeDtypeStruct((span, CODES), BF16),
            jax.ShapeDtypeStruct((HALF, length), F32),
            jax.ShapeDtypeStruct((HALF, length), F32),
        ],
        compiler_params=pltpu.CompilerParams(vmem_limit_bytes=VMEM_LIMIT),
        cost_estimate=pl.CostEstimate(
            flops=8 * span * width * width, bytes_accessed=10 * width * width, transcendentals=0
        ),
        name="prepare",
    )(words, w_query, w_key, w_value, box_weight, *map(jnp.asarray, rotary_tables(length)))


def write_codes(page, place_refs, high_ref, low_ref, sin_ref, cos_ref, codes_ref):
    block = place_refs[0].shape[1]

    def looked_up(table_ref, index):
        spots = table_ref.shape[1] // 3
        rows = lax.broadcasted_iota(jnp.int32, (spots, block), 0)
        once = jnp.where(rows == index, 1.0, 0.0)
        found = dot(table_ref[...], jnp.concatenate([once] * 3, axis=0).astype(BF16))
        return found[:FREQS], found[FREQS:]

    for i, place_ref in enumerate(place_refs):
        columns = slice(i * block, (i + 1) * block)
        for axis in range(2):
            place = place_ref[2 * page + axis : 2 * page + axis + 1]
            high_sin, high_cos = looked_up(high_ref, lax.shift_right_logical(place, 6))
            low_sin, low_cos = looked_up(low_ref, place & 63)
            sines = high_sin * low_cos + high_cos * low_sin
            cosines = high_cos * low_cos - high_sin * low_sin
            rows = slice(axis * FREQS, (axis + 1) * FREQS)
            later = slice((2 + axis) * FREQS, (3 + axis) * FREQS)
            sin_ref[rows, columns] = sines
            cos_ref[rows, columns] = cosines
            codes_ref[rows, columns] = sines.astype(BF16)
            codes_ref[later, columns] = cosines.astype(BF16)


def forward_kernel(page, count, *refs):
    place_refs, refs = refs[:count], refs[count:]
    piece_refs, refs = refs[:count], refs[count:]
    high_ref, low_ref, w_ref, box_ref, rot_cos_ref, rot_sin_ref = refs[:6]
    probs_ref, att_ref, heads_ref, sin_ref, cos_ref, codes_ref = refs[6:12]
    low_refs = refs[12 : 12 + count]
    tok_ref, kc_ref, qr_ref = refs[12 + count :]
    rows = tok_ref.shape[0]
    block = rows // count

    @pl.when(pl.program_id(0) == 0)
    def _():
        for i in range(count):
            tok_ref[i * block : (i + 1) * block] = piece_refs[i][...]
        write_codes(page, place_refs, high_ref, low_ref, sin_ref, cos_ref, codes_ref)
        kc_ref[:, :CODES] = codes_ref[...].astype(F32).T.astype(BF16)

    weights = w_ref[...].reshape(3 * HEAD_DIM, w_ref.shape[-1])
    pre = dot_nt(weights, tok_ref[...])
    rot_cos = rot_cos_ref[...]
    rot_sin = rot_sin_ref[...]
    query_pre = pre[:HEAD_DIM].astype(BF16)
    wide = query_pre.astype(F32)
    query = jnp.concatenate(turned(wide[:HALF], wide[HALF:], rot_cos, rot_sin), axis=0)
    key_pre = pre[HEAD_DIM : 2 * HEAD_DIM]
    key = jnp.concatenate(turned(key_pre[:HALF], key_pre[HALF:], rot_cos, rot_sin), axis=0)
    value = pre[2 * HEAD_DIM :].astype(BF16)
    heads_ref[0, :HEAD_DIM] = query_pre
    heads_ref[0, HEAD_DIM : 2 * HEAD_DIM] = query.astype(BF16)
    heads_ref[0, 2 * HEAD_DIM : 3 * HEAD_DIM] = key.astype(BF16)
    heads_ref[0, 3 * HEAD_DIM :] = value
    kc_ref[:, CODES:] = key.T.astype(BF16)
    projected = dot_tn(box_ref[...], query_pre)
    sines = sin_ref[...]
    cosines = cos_ref[...]
    upper = projected[: 2 * FREQS]
    lower = projected[2 * FREQS :]
    qr_ref[: 2 * FREQS] = ((upper * cosines + lower * sines) * 0.125).astype(BF16)
    qr_ref[2 * FREQS : CODES] = ((lower * cosines - upper * sines) * 0.125).astype(BF16)
    qr_ref[CODES:] = (query * 0.125).astype(BF16)
    step = min(256, block)
    for at in range(0, rows, step):
        logits = dot(kc_ref[...], qr_ref[:, at : at + step])
        weight = jnp.exp(logits - jnp.max(logits, axis=0, keepdims=True))
        total = jnp.sum(weight, axis=0, keepdims=True)
        probs = (weight * (1.0 / total)).astype(BF16)
        probs_ref[0, :, at : at + step] = probs
        attended = dot(value, probs)
        att_ref[0, :, at : at + step] = attended
        inner = at % block
        low_refs[at // block][:, inner : inner + step] = attended.astype(BF16)


def fixed(array):
    return pl.BlockSpec(array.shape, lambda *at: (0,) * len(array.shape))


def attention_forward(page, places, pieces, w_own, box_own, rot_cos, rot_sin):
    count = len(pieces)
    block, width = pieces[0].shape
    rows = count * block
    span = box_own.shape[0]
    heads = span // HEAD_DIM
    tables = [jnp.asarray(item) for item in angle_tables()]
    out_shape = [
        jax.ShapeDtypeStruct((heads, rows, rows), BF16),
        jax.ShapeDtypeStruct((heads, HEAD_DIM, rows), F32),
        jax.ShapeDtypeStruct((heads, 4 * HEAD_DIM, rows), BF16),
        jax.ShapeDtypeStruct((2 * FREQS, rows), F32),
        jax.ShapeDtypeStruct((2 * FREQS, rows), F32),
        jax.ShapeDtypeStruct((CODES, rows), BF16),
    ] + [jax.ShapeDtypeStruct((span, block), BF16)] * count
    return pl.pallas_call(
        functools.partial(forward_kernel, page, count),
        grid=(heads,),
        in_specs=[fixed(item) for item in (*places, *pieces, *tables)]
        + [
            pl.BlockSpec((3, HEAD_DIM, width), lambda h: (0, h, 0)),
            pl.BlockSpec((HEAD_DIM, CODES), lambda h: (h, 0)),
            fixed(rot_cos),
            fixed(rot_sin),
        ],
        out_specs=[
            pl.BlockSpec((1, rows, rows), lambda h: (h, 0, 0)),
            pl.BlockSpec((1, HEAD_DIM, rows), lambda h: (h, 0, 0)),
            pl.BlockSpec((1, 4 * HEAD_DIM, rows), lambda h: (h, 0, 0)),
        ]
        + [fixed(item) for item in out_shape[3:6]]
        + [pl.BlockSpec((HEAD_DIM, block), lambda h: (h, 0))] * count,
        out_shape=out_shape,
        scratch_shapes=[
            pltpu.VMEM((rows, width), BF16),
            pltpu.VMEM((rows, CODES + HEAD_DIM), BF16),
            pltpu.VMEM((CODES + HEAD_DIM, rows), BF16),
        ],
        compiler_params=pltpu.CompilerParams(vmem_limit_bytes=VMEM_LIMIT),
        cost_estimate=pl.CostEstimate(
            flops=2 * heads * rows * (rows * 1100 + 200 * width + 64 * CODES),
            bytes_accessed=2 * heads * rows * rows + 12 * rows * width,
            transcendentals=heads * rows * rows,
        ),
        name="attention_forward",
    )(*places, *pieces, *tables, w_own, box_own, rot_cos, rot_sin)


def backward_kernel(count, last, words_ref, *refs):
    grad_refs, refs = refs[:count], refs[count:]
    piece_refs, refs = refs[:count], refs[count:]
    probs_ref, att_ref, heads_ref, box_ref, codes_ref, sin_ref, cos_ref = refs[:7]
    rot_cos_ref, rot_sin_ref = refs[7:9]
    refs = refs[9:]
    if last:
        before_ref, refs = refs[0], refs[1:]
    pre_refs, refs = refs[:count], refs[count:]
    if last:
        mine_ref, theirs_ref, *refs = refs
    weight_grad_ref, kc_ref = refs
    block, width = piece_refs[0].shape
    rows = count * block
    head = pl.program_id(0)
    span = pl.num_programs(0) * HEAD_DIM

    @pl.when(head == 0)
    def _():
        kc_ref[:CODES] = codes_ref[...]

    kc_ref[CODES:] = heads_ref[0, 2 * HEAD_DIM : 3 * HEAD_DIM]
    packed = heads_ref[0].astype(F32).T.astype(BF16)
    query_pre = packed[:, :HEAD_DIM]
    query = packed[:, HEAD_DIM : 2 * HEAD_DIM]
    value = packed[:, 3 * HEAD_DIM :] * jnp.asarray(0.125, BF16)
    rot_cos = rot_cos_ref[...]
    rot_sin = rot_sin_ref[...]
    grad = jnp.concatenate([ref[...] for ref in grad_refs], axis=1)
    grad_tall = grad.astype(F32).T.astype(BF16)
    offsets = jnp.sum(grad.astype(F32) * att_ref[0], axis=0, keepdims=True) * 0.125
    step = min(256, block)
    place = pl.multiple_of(head * HEAD_DIM, HEAD_DIM)
    key_grad = jnp.zeros((rows, HEAD_DIM), F32)
    value_grad = jnp.zeros((rows, HEAD_DIM), F32)
    box_grad = jnp.zeros((CODES, HEAD_DIM), F32)
    for at in range(0, rows, step):
        part = slice(at, at + step)
        probs = probs_ref[0, :, part]
        grad_probs = dot(value, grad[:, part])
        grad_logits = (probs.astype(F32) * (grad_probs - offsets[:, part])).astype(BF16)
        back = dot(kc_ref[...], grad_logits)
        sines = sin_ref[:, part]
        cosines = cos_ref[:, part]
        upper = back[: 2 * FREQS]
        lower = back[2 * FREQS : CODES]
        projected_grad = jnp.concatenate(
            [
                (upper * cosines - lower * sines).astype(BF16),
                (lower * cosines + upper * sines).astype(BF16),
            ],
            axis=0,
        )
        first = back[CODES : CODES + HALF]
        second = back[CODES + HALF :]
        own = jnp.concatenate(
            turned(first, second, rot_cos[:, part], -rot_sin[:, part]), axis=0
        )
        inner = at % block
        pre_refs[at // block][pl.ds(place, HEAD_DIM), inner : inner + step] = (
            own + dot(box_ref[...], projected_grad)
        ).astype(BF16)
        key_grad = key_grad + dot(grad_logits, query[part])
        value_grad = value_grad + dot(probs, grad_tall[part])
        box_grad = box_grad + dot(projected_grad, query_pre[part])
    key_flat = key_grad.T
    key_low = jnp.concatenate(
        turned(key_flat[:HALF], key_flat[HALF:], rot_cos, -rot_sin), axis=0
    ).astype(BF16)
    value_low = value_grad.T.astype(BF16)
    for i in range(count):
        columns = slice(i * block, (i + 1) * block)
        pre_refs[i][pl.ds(span + place, HEAD_DIM)] = key_low[:, columns]
        pre_refs[i][pl.ds(2 * span + place, HEAD_DIM)] = value_low[:, columns]
    weight_grad_ref[pl.ds(3 * span + place, HEAD_DIM)] = box_grad.T

    @pl.when(head == pl.num_programs(0) - 1)
    def _():
        total = dot(pre_refs[0][...], piece_refs[0][...])
        for i in range(1, count):
            total = total + dot(pre_refs[i][...], piece_refs[i][...])
        weight_grad_ref[: 3 * span] = total
        if last:
            half = 2 * span
            core = words_ref[2]
            here = pl.ds(pl.multiple_of(core * half, half), half)
            there = pl.ds(pl.multiple_of((1 - core) * half, half), half)
            mine_ref[...] = weight_grad_ref[here] + before_ref[here]
            theirs_ref[...] = (weight_grad_ref[there] + before_ref[there]).astype(BF16)


def attention_backward(words, page, grads, pieces, saved, box_own, rot_cos, rot_sin, before=None):
    probs, att, heads_saved, sines, cosines, codes = saved
    count = len(pieces)
    block, width = pieces[0].shape
    rows = count * block
    span = box_own.shape[0]
    heads = span // HEAD_DIM
    last = before is not None
    extra = (before,) if last else ()
    full_shape = (4 * span, width)
    out_shape = [jax.ShapeDtypeStruct((3 * span, block), BF16)] * count
    if last:
        out_shape += [
            jax.ShapeDtypeStruct((2 * span, width), F32),
            jax.ShapeDtypeStruct((2 * span, width), BF16),
        ]
    else:
        out_shape.append(jax.ShapeDtypeStruct(full_shape, F32))
    return pl.pallas_call(
        functools.partial(backward_kernel, count, last),
        grid=(heads,),
        in_specs=[pl.BlockSpec(memory_space=pltpu.SMEM)]
        + [pl.BlockSpec((HEAD_DIM, block), lambda h: (h, page))] * count
        + [fixed(item) for item in pieces]
        + [
            pl.BlockSpec((1, rows, rows), lambda h: (h, 0, 0)),
            pl.BlockSpec((1, HEAD_DIM, rows), lambda h: (h, 0, 0)),
            pl.BlockSpec((1, 4 * HEAD_DIM, rows), lambda h: (h, 0, 0)),
            pl.BlockSpec((HEAD_DIM, CODES), lambda h: (h, 0)),
        ]
        + [fixed(item) for item in (codes, sines, cosines, rot_cos, rot_sin, *extra)],
        out_specs=[fixed(item) for item in out_shape],
        out_shape=out_shape,
        scratch_shapes=([pltpu.VMEM(full_shape, F32)] if last else [])
        + [pltpu.VMEM((CODES + HEAD_DIM, rows), BF16)],
        compiler_params=pltpu.CompilerParams(vmem_limit_bytes=VMEM_LIMIT),
        cost_estimate=pl.CostEstimate(
            flops=2 * heads * rows * (rows * 1400 + 200 * width + 128 * CODES),
            bytes_accessed=2 * heads * rows * rows + 12 * rows * width,
            transcendentals=0,
        ),
        name="attention_backward",
    )(
        words,
        *grads,
        *pieces,
        probs,
        att,
        heads_saved,
        box_own,
        codes,
        sines,
        cosines,
        rot_cos,
        rot_sin,
        *extra,
    )


def normed(value):
    centered = value - jnp.mean(value, axis=-1, keepdims=True)
    scale = lax.rsqrt(jnp.mean(centered * centered, axis=-1, keepdims=True) + 1e-05)
    return centered * scale, scale


def norm_back(grad, gain, unit, scale):
    scaled = grad * gain
    return scale * (
        scaled
        - jnp.mean(scaled, axis=-1, keepdims=True)
        - unit * jnp.mean(scaled * unit, axis=-1, keepdims=True)
    )


def column_sum(value):
    return jnp.sum(value, axis=0, keepdims=True)


def middle_kernel(pages, count, span, chunks, *refs):
    total = pages * count
    words_ref = refs[0]
    att_refs = refs[1 : 1 + total]
    (
        tok_ref,
        cot_ref,
        w_out_ref,
        vectors_ref,
        w_expand_ref,
        w_reduce_ref,
    ) = refs[1 + total : 7 + total]
    outs = refs[7 + total :]
    layer_ref, first_in_ref, theirs_ref, mine_ref, more_theirs_ref, more_mine_ref = outs[:6]
    grad_refs = outs[6 : 6 + count]
    (
        sums_ref,
        att_all,
        grad_all,
        unit_one,
        scale_one,
        first_wide,
        first_low,
        first_tall,
        active,
        slope,
        gathered,
        second_in,
        second_low,
    ) = outs[6 + count :]
    rank = words_ref[0]
    width = tok_ref.shape[1]
    block = tok_ref.shape[0] // pages
    step = pl.program_id(0)

    def rows_of(at):
        return pl.ds(pl.multiple_of((rank ^ at) * span, span), span)

    @pl.when(step == 0)
    def _():
        for page in range(pages):
            for at in range(count):
                att_all[rows_of(at), page * block : (page + 1) * block] = att_refs[
                    page * count + at
                ][...]
        branch = dot_tn(att_all[: w_out_ref.shape[0]], w_out_ref[...])
        unit, scale = normed(tok_ref[...].astype(F32) + branch)
        unit_one[...] = unit
        scale_one[...] = jnp.broadcast_to(scale, scale_one.shape)
        first_out = unit * vectors_ref[0:1] + vectors_ref[1:2]
        first_wide[...] = first_out
        first_low[...] = first_out.astype(BF16)
        first_tall[...] = first_out.T.astype(BF16)
        gathered[...] = jnp.zeros_like(gathered)
        sums_ref[...] = jnp.zeros_like(sums_ref)

    for chunk in range(chunks):

        @pl.when(step == chunk)
        def _(chunk=chunk):
            expanded = dot(first_low[...], w_expand_ref[...])
            gate = 0.5 + 0.5 * lax.erf(expanded * np.float32(np.sqrt(0.5)))
            bell = jnp.exp(expanded * expanded * -0.5) * np.float32(1.0 / np.sqrt(2.0 * np.pi))
            low = (expanded * gate).astype(BF16)
            active[chunk] = low
            slope[chunk] = gate + expanded * bell
            gathered[...] += dot(low, w_reduce_ref[...])

    @pl.when(step == chunks - 1)
    def _():
        unit, scale = normed(first_wide[...] + gathered[...])
        layer_ref[...] = (unit * vectors_ref[2:3] + vectors_ref[3:4]).astype(BF16)
        cot = cot_ref[...].astype(F32)
        sums_ref[2:3] = column_sum(cot * unit)
        sums_ref[3:4] = column_sum(cot)
        grad = norm_back(cot, vectors_ref[2:3], unit, scale)
        second_in[...] = grad
        second_low[...] = grad.astype(BF16)
        gathered[...] = grad

    for chunk in range(chunks):

        @pl.when(step == 2 * chunks - 1 - chunk)
        def _(chunk=chunk):
            grad_active = dot_nt(second_low[...], w_reduce_ref[...])
            grad_expanded = (grad_active * slope[chunk]).astype(BF16)
            grads_ref = mine_ref if chunk < chunks // 2 else theirs_ref
            grads_ref[:width] = dot(first_tall[...], grad_expanded).astype(BF16)
            grads_ref[width:] = dot_tn(active[chunk], second_low[...]).astype(BF16)
            gathered[...] += dot_nt(grad_expanded, w_expand_ref[...])

    @pl.when(step == 2 * chunks - 1)
    def _():
        unit = unit_one[...]
        grad_out = gathered[...]
        sums_ref[0:1] = column_sum(grad_out * unit)
        sums_ref[1:2] = column_sum(grad_out)
        grad = norm_back(grad_out, vectors_ref[0:1], unit, scale_one[:, :1])
        first_in_ref[...] = grad
        low = grad.astype(BF16)
        real = w_out_ref.shape[0]
        half = real // 2
        core = words_ref[2]
        for ref, side in ((more_mine_ref, core), (more_theirs_ref, 1 - core)):
            rows = pl.ds(pl.multiple_of(side * half, half), half)
            ref[:half] = dot(att_all[rows], low).astype(BF16)
            ref[half:] = jnp.zeros((ref.shape[0] - half, width), BF16)
            ref[half : half + 16] = sums_ref[...].astype(BF16)
        if grad_all.shape[0] > real:
            grad_all[real:] = jnp.zeros((grad_all.shape[0] - real, low.shape[0]), BF16)
        grad_all[:real] = dot_nt(w_out_ref[...], low).astype(BF16)
        for at in range(count):
            grad_refs[at][...] = grad_all[rows_of(at)]


def middle(words, att_parts, tok, cot, w_out, vectors, w_expand, w_reduce, pages, more):
    rows, width = tok.shape
    count = len(att_parts) // pages
    span, block = att_parts[0].shape
    hidden = w_expand.shape[1]
    chunks = hidden // width
    pairs = chunks // 2

    def whole(array):
        return pl.BlockSpec(array.shape, lambda s, words: (0,) * len(array.shape))

    def chunk_at(s, words):
        at = jnp.minimum(s, 2 * chunks - 1 - s)
        return (at + words[2] * pairs) % chunks

    def theirs_at(s, words):
        return jnp.clip(2 * chunks - 1 - s - pairs, 0, pairs - 1), 0

    def mine_at(s, words):
        return jnp.clip(2 * chunks - 1 - s, 0, pairs - 1), 0

    shapes = [
        jax.ShapeDtypeStruct((rows, width), BF16),
        jax.ShapeDtypeStruct((rows, width), F32),
        jax.ShapeDtypeStruct((hidden, width), BF16),
        jax.ShapeDtypeStruct((hidden, width), BF16),
        jax.ShapeDtypeStruct((more, width), BF16),
        jax.ShapeDtypeStruct((more, width), BF16),
    ] + [jax.ShapeDtypeStruct((span, pages * block), BF16)] * count
    specs = [whole(item) for item in shapes]
    specs[2] = pl.BlockSpec((2 * width, width), theirs_at)
    specs[3] = pl.BlockSpec((2 * width, width), mine_at)
    return pl.pallas_call(
        functools.partial(middle_kernel, pages, count, span, chunks),
        grid_spec=pltpu.PrefetchScalarGridSpec(
            num_scalar_prefetch=1,
            grid=(2 * chunks,),
            in_specs=[whole(item) for item in att_parts]
            + [
                whole(tok),
                whole(cot),
                whole(w_out),
                whole(vectors),
                pl.BlockSpec((width, width), lambda s, words: (0, chunk_at(s, words))),
                pl.BlockSpec((width, width), lambda s, words: (chunk_at(s, words), 0)),
            ],
            out_specs=specs,
            scratch_shapes=[
                pltpu.VMEM((16, width), F32),
                pltpu.VMEM((count * span, rows), BF16),
                pltpu.VMEM((count * span, rows), BF16),
                pltpu.VMEM((rows, width), F32),
                pltpu.VMEM((rows, 128), F32),
                pltpu.VMEM((rows, width), F32),
                pltpu.VMEM((rows, width), BF16),
                pltpu.VMEM((width, rows), BF16),
                pltpu.VMEM((chunks, rows, width), BF16),
                pltpu.VMEM((chunks, rows, width), F32),
                pltpu.VMEM((rows, width), F32),
                pltpu.VMEM((rows, width), F32),
                pltpu.VMEM((rows, width), BF16),
            ],
        ),
        out_shape=shapes,
        compiler_params=pltpu.CompilerParams(vmem_limit_bytes=VMEM_LIMIT),
        cost_estimate=pl.CostEstimate(
            flops=2 * rows * width * (6 * hidden + 3 * width),
            bytes_accessed=8 * width * hidden + 16 * rows * width,
            transcendentals=2 * rows * hidden,
        ),
        name="middle",
    )(words, *att_parts, tok, cot, w_out, vectors, w_expand, w_reduce)


def input_kernel(pages, count, span, *refs):
    total = pages * count
    words_ref = refs[0]
    part_refs = refs[1 : 1 + total]
    weight_refs = refs[1 + total : 4 + total]
    first_in_ref, out_ref, held = refs[4 + total :]
    rank = words_ref[0]
    width = out_ref.shape[1]
    block = out_ref.shape[0] // pages
    for page in range(pages):
        for at in range(count):
            part = part_refs[page * count + at]
            for kind in range(3):
                place = pl.multiple_of((rank ^ at) * span, span)
                held[kind, pl.ds(place, span), page * block : (page + 1) * block] = part[
                    kind * span : (kind + 1) * span
                ]
    total = dot(weight_refs[0][...], held[0, :width])
    for kind in range(1, 3):
        total = total + dot(weight_refs[kind][...], held[kind, :width])
    out_ref[...] = (first_in_ref[...] + total.T).astype(BF16)


def input_gradient(words, parts, weights, first_in, pages):
    count = len(parts) // pages
    span = parts[0].shape[0] // 3
    rows, width = first_in.shape
    vmem = pl.BlockSpec(memory_space=pltpu.VMEM)
    return pl.pallas_call(
        functools.partial(input_kernel, pages, count, span),
        in_specs=[pl.BlockSpec(memory_space=pltpu.SMEM)] + [vmem] * (len(parts) + 4),
        out_specs=vmem,
        out_shape=jax.ShapeDtypeStruct((rows, width), BF16),
        scratch_shapes=[pltpu.VMEM((3, count * span, rows), BF16)],
        compiler_params=pltpu.CompilerParams(vmem_limit_bytes=VMEM_LIMIT),
        cost_estimate=pl.CostEstimate(
            flops=6 * rows * width * count * span,
            bytes_accessed=2 * width * (5 * rows + 3 * count * span),
            transcendentals=0,
        ),
        name="input_gradient",
    )(words, *parts, *weights, first_in)


def local(body, name, words, arrays, shapes):
    def kernel(words_ref, *refs):
        body(words_ref, refs[: len(arrays)], refs[len(arrays) :])

    vmem = pl.BlockSpec(memory_space=pltpu.VMEM)
    shapes = [jax.ShapeDtypeStruct(shape, kind) for shape, kind in shapes]
    moved = sum(item.size * item.dtype.itemsize for item in list(arrays) + shapes)
    return pl.pallas_call(
        kernel,
        in_specs=[pl.BlockSpec(memory_space=pltpu.SMEM)] + [vmem] * len(arrays),
        out_specs=[vmem] * len(shapes),
        out_shape=shapes,
        compiler_params=pltpu.CompilerParams(vmem_limit_bytes=VMEM_LIMIT),
        cost_estimate=pl.CostEstimate(flops=moved, bytes_accessed=moved, transcendentals=0),
        name=name,
    )(words, *arrays)


def shard(index, rows, base=0):
    return pl.ds(pl.multiple_of(base + index * rows, 16), rows)


def total_of(refs, rows=slice(None)):
    total = refs[0][rows].astype(F32)
    for ref in refs[1:]:
        total = total + ref[rows].astype(F32)
    return total


class Plan:
    def __init__(self, rows, rows_a, more, width):
        self.count = lax.axis_size("blk")
        self.depth = lax.axis_size("dp") // 2
        self.rows = rows
        self.rows_a = rows_a
        self.more = more
        self.width = width
        self.a_ff = rows_a // self.count
        self.a_more = more // self.count
        self.a_one = self.a_ff + self.a_more
        self.a_two = self.a_one // self.depth
        self.b_one = (rows - rows_a) // self.depth
        self.b_two = self.b_one // self.count

    def shapes(self, *sizes):
        return [((rows, self.width), BF16) for rows in sizes]

    def scatter_one(self, words, halves):
        def body(words, ins, outs):
            for i in range(self.count):
                rows = shard(words[0] ^ i, self.a_ff)
                outs[i][: self.a_ff] = total_of(ins[:2], rows).astype(BF16)
                rows = shard(words[0] ^ i, self.a_more)
                outs[i][self.a_ff :] = total_of(ins[2:], rows).astype(BF16)
            for k in range(self.depth):
                rows = shard(words[1] ^ k, self.b_one, self.rows_a)
                outs[self.count + k][...] = total_of(ins[:2], rows).astype(BF16)

        shapes = self.shapes(*[self.a_one] * self.count, *[self.b_one] * self.depth)
        return local(body, "scatter_one", words, halves, shapes)

    def send_one(self, parts):
        return [from_blk(parts[i], i) for i in range(self.count)] + [
            from_depth(parts[self.count + k], k) for k in range(self.depth)
        ]

    def scatter_two(self, words, parts):
        def body(words, ins, outs):
            for k in range(self.depth):
                rows = shard(words[1] ^ k, self.a_two)
                outs[k][...] = total_of(ins[: self.count], rows).astype(BF16)
            for i in range(self.count):
                rows = shard(words[0] ^ i, self.b_two)
                outs[self.depth + i][...] = total_of(ins[self.count :], rows).astype(BF16)

        shapes = self.shapes(*[self.a_two] * self.depth, *[self.b_two] * self.count)
        return local(body, "scatter_two", words, parts, shapes)

    def send_two(self, parts):
        return [from_depth(parts[k], k) for k in range(self.depth)] + [
            from_blk(parts[self.depth + i], i) for i in range(self.count)
        ]

    def finish(self, words, parts):
        def body(words, ins, outs):
            outs[0][...] = total_of(ins[: self.depth]).astype(BF16)
            outs[1][...] = total_of(ins[self.depth :]).astype(BF16)

        return local(body, "scatter_sum", words, parts, self.shapes(self.a_two, self.b_two))

    def gather_one(self, words, parts):
        def body(words, ins, outs):
            for k in range(self.depth):
                outs[0][shard(words[1] ^ k, self.a_two)] = ins[k][...]
            for i in range(self.count):
                outs[1][shard(words[0] ^ i, self.b_two)] = ins[self.depth + i][...]

        return local(body, "gather_one", words, parts, self.shapes(self.a_one, self.b_one))

    def gather_two(self, words, parts):
        def body(words, ins, outs):
            for i in range(self.count):
                outs[0][shard(words[0] ^ i, self.a_ff)] = ins[i][: self.a_ff]
                outs[1][shard(words[0] ^ i, self.a_more)] = ins[i][self.a_ff :]
            for k in range(self.depth):
                rows = shard(words[1] ^ k, self.b_one, self.rows_a)
                outs[0][rows] = ins[self.count + k][...]

        return local(body, "gather_two", words, parts, self.shapes(self.rows, self.more))


def widened(words, half, side, hidden, before=()):
    width = half.shape[1]
    chunks = hidden // width
    pairs = chunks // 2

    def kernel(words_ref, half_ref, *refs):
        expand_ref, reduce_ref = refs[len(before) :]
        expand_ref[...] = half_ref[:width].astype(F32)
        reduce_ref[...] = half_ref[width:].astype(F32)

    def place(s, words):
        return (s + (words[2] + side) * pairs) % chunks

    return pl.pallas_call(
        kernel,
        grid_spec=pltpu.PrefetchScalarGridSpec(
            num_scalar_prefetch=1,
            grid=(pairs,),
            in_specs=[pl.BlockSpec((2 * width, width), lambda s, words: (s, 0))]
            + [pl.BlockSpec(memory_space=pl.ANY)] * len(before),
            out_specs=[
                pl.BlockSpec((width, width), lambda s, words: (0, place(s, words))),
                pl.BlockSpec((width, width), lambda s, words: (place(s, words), 0)),
            ],
        ),
        out_shape=[
            jax.ShapeDtypeStruct((width, hidden), F32),
            jax.ShapeDtypeStruct((hidden, width), F32),
        ],
        input_output_aliases={2: 0, 3: 1} if before else {},
        compiler_params=pltpu.CompilerParams(vmem_limit_bytes=VMEM_LIMIT),
        cost_estimate=pl.CostEstimate(
            flops=0, bytes_accessed=6 * hidden * width, transcendentals=0
        ),
        name="widen",
    )(words, half, *before)


class Heads:
    def __init__(self, half, width):
        self.count = lax.axis_size("blk")
        self.depth = lax.axis_size("dp") // 2
        self.half = half
        self.width = width
        self.piece = half // self.depth

    def scatter(self, words, mine, other):
        def body(words, ins, outs):
            for k in range(self.depth):
                outs[k][...] = total_of(ins, shard(words[1] ^ k, self.piece)).astype(BF16)

        shapes = [((self.piece, self.width), BF16)] * self.depth
        parts = local(body, "heads_scatter", words, [mine, other], shapes)
        return [from_depth(parts[k], k) for k in range(self.depth)]

    def add(self, words, parts):
        def body(words, ins, outs):
            outs[0][...] = total_of(ins).astype(BF16)

        own = local(body, "heads_sum", words, parts, [((self.piece, self.width), BF16)])[0]
        return [from_depth(own, k) for k in range(self.depth)]

    def join_depth(self, words, parts):
        def body(words, ins, outs):
            for k in range(self.depth):
                outs[0][shard(words[1] ^ k, self.piece)] = ins[k][...]

        own = local(body, "heads_join_depth", words, parts, [((self.half, self.width), BF16)])[0]
        return [from_blk(own, i) for i in range(self.count)]

    def join_blk(self, words, parts):
        def body(words, ins, outs):
            for i in range(self.count):
                outs[0][shard(words[0] ^ i, self.half)] = ins[i][...]

        shapes = [((self.count * self.half, self.width), BF16)]
        return local(body, "heads_join_blk", words, parts, shapes)[0]


def finish_kernel(count, span, half, words_ref, *refs):
    own_ref, other_ref, more_ref, more_other_ref = refs[:4]
    query_ref, key_ref, value_ref, project_ref, box_ref, sums_ref = refs[4:]
    width = query_ref.shape[0]

    def write(lower_ref, upper_ref, more_lower_ref, more_upper_ref):
        def grad(ref, part):
            rows = [
                ref[(2 * i + part) * span : (2 * i + part + 1) * span].astype(F32)
                for i in range(count)
            ]
            return jnp.concatenate(rows, axis=0)[:width].T

        query_ref[...] = grad(lower_ref, 0)
        key_ref[...] = grad(lower_ref, 1)
        value_ref[...] = grad(upper_ref, 0)
        box_ref[...] = entry_order(grad(upper_ref, 1))
        project_ref[:half] = more_lower_ref[:half].astype(F32)
        project_ref[half:] = more_upper_ref[:half].astype(F32)
        sums_ref[...] = more_lower_ref[half : half + 16].astype(F32)[:8]

    @pl.when(words_ref[2] == 0)
    def _():
        write(own_ref, other_ref, more_ref, more_other_ref)

    @pl.when(words_ref[2] == 1)
    def _():
        write(other_ref, own_ref, more_other_ref, more_ref)


def finished(words, own, other, more, more_other, span, width):
    count = lax.axis_size("blk")
    vmem = pl.BlockSpec(memory_space=pltpu.VMEM)
    shapes = [jax.ShapeDtypeStruct((width, width), F32)] * 5
    shapes.append(jax.ShapeDtypeStruct((8, width), F32))
    return pl.pallas_call(
        functools.partial(finish_kernel, count, span, width // 2),
        in_specs=[pl.BlockSpec(memory_space=pltpu.SMEM)] + [vmem] * 4,
        out_specs=[vmem] * 6,
        out_shape=shapes,
        compiler_params=pltpu.CompilerParams(vmem_limit_bytes=VMEM_LIMIT),
        cost_estimate=pl.CostEstimate(
            flops=0, bytes_accessed=32 * width * width, transcendentals=0
        ),
        name="finish",
    )(words, own, other, more, more_other)


def per_device(
    tokens,
    boxes,
    w_query,
    w_key,
    w_value,
    w_output,
    box_weight,
    first_gain,
    first_shift,
    w_expand,
    w_reduce,
    second_gain,
    second_shift,
    cotangent,
):
    pages, block, width = tokens.shape
    count = lax.axis_size("blk")
    depth = lax.axis_size("dp") // 2
    rank = lax.axis_index("blk")
    dp_rank = lax.axis_index("dp")
    words = jnp.stack(
        [rank, lax.shift_right_logical(dp_rank, 1), dp_rank & 1]
    ).astype(jnp.int32)
    hidden = w_expand.shape[1]
    span = -(-HEADS // count) * HEAD_DIM
    unit = 16 * count * depth
    more = -(-(width // 2 + 16) // unit) * unit

    own_places = jnp.stack([boxes[0] + boxes[2], boxes[1] + boxes[3]], axis=1)
    own_places = own_places.reshape(2 * pages, block)
    places = [from_blk(own_places, i) for i in range(count)]
    pieces = [[from_blk(tokens[0], i) for i in range(count)]]
    w_own, box_own, rot_cos, rot_sin = prepare(
        words, w_query, w_key, w_value, box_weight, span, count * block
    )
    for page in range(1, pages):
        own = after(w_own, tokens[page])
        pieces.append([from_blk(own, i) for i in range(count)])

    saved = []
    att_parts = []
    for page in range(pages):
        results = attention_forward(
            page, places, pieces[page], w_own, box_own, rot_cos, rot_sin
        )
        saved.append(results[:6])
        att_parts += [from_blk(results[6 + i], i) for i in range(count)]

    vectors = jnp.stack([first_gain, first_shift, second_gain, second_shift])
    results = middle(
        words,
        att_parts,
        tokens.reshape(pages * block, width),
        cotangent.reshape(pages * block, width),
        w_output,
        vectors,
        w_expand,
        w_reduce,
        pages,
        more,
    )
    layer_out, first_in, theirs, mine, more_theirs, more_mine = results[:6]
    grads = [from_blk(results[6 + i], i) for i in range(count)]
    plan = Plan(hidden, 2 * hidden // 3, more, width)
    parts = plan.scatter_one(
        words, [mine, from_core(theirs), more_mine, from_core(more_theirs)]
    )
    grads, parts = lax.optimization_barrier((grads, parts))
    parts = plan.send_one(parts)

    def backward(page, words, before=None):
        return attention_backward(
            words,
            page,
            grads,
            pieces[page],
            saved[page],
            box_own,
            rot_cos,
            rot_sin,
            before,
        )

    before = None
    pre_parts = []
    for page in range(pages - 1):
        results = backward(page, words, before)
        before = results[count] if before is None else before + results[count]
        pre_parts += [from_blk(results[i], i) for i in range(count)]
    parts = plan.scatter_two(after(before, words), parts)
    before, parts = lax.optimization_barrier((before, parts))
    parts = plan.send_two(parts)
    *last_parts, heads_mine, heads_theirs = backward(pages - 1, words, before)

    parts = plan.finish(after(heads_mine, words), parts)
    last_parts, heads_theirs, parts = lax.optimization_barrier((last_parts, heads_theirs, parts))
    parts = plan.send_two([parts[0]] * depth + [parts[1]] * count)
    heads = Heads(2 * span, width)
    heads_parts = heads.scatter(words, heads_mine, from_core(heads_theirs))
    pre_parts += [from_blk(last_parts[i], i) for i in range(count)]
    parts = plan.gather_one(after(heads_parts[0], words), parts)
    parts_a, parts_b = parts
    parts = plan.send_one([parts_a] * count + [parts_b] * depth)
    heads_parts = heads.add(after(parts_a, words), heads_parts)
    input_grad = input_gradient(
        after(heads_parts[0], words), pre_parts, (w_query, w_key, w_value), first_in, pages
    )
    heads_parts = heads.join_depth(after(input_grad, words), heads_parts)
    ff, extra = plan.gather_two(after(heads_parts[0], words), parts)
    ff_other, extra_other = from_core(ff), from_core(extra)
    wide = widened(words, ff, 0, hidden)
    heads_own = heads.join_blk(after(wide[0], words), heads_parts)
    heads_other = from_core(heads_own)
    grad_expand, grad_reduce = widened(after(heads_own, words), ff_other, 1, hidden, wide)
    grad_query, grad_key, grad_value, grad_project, grad_box, sums = finished(
        words, heads_own, heads_other, extra, extra_other, span, width
    )
    return (
        layer_out.reshape(tokens.shape),
        input_grad.reshape(tokens.shape),
        grad_query,
        grad_key,
        grad_value,
        grad_project,
        grad_box,
        sums[0],
        sums[1],
        grad_expand,
        grad_reduce,
        sums[2],
        sums[3],
    )


def solution(mesh):
    split = P("dp", "blk", None)
    return jax.shard_map(
        per_device,
        mesh=mesh,
        in_specs=(split, P(None, "dp", "blk")) + (P(),) * 11 + (split,),
        out_specs=(split, split) + (P(),) * 11,
        check_vma=False,
    )
```

```python
import functools

import jax
import jax.numpy as jnp
import numpy as np
from jax import lax
from jax.experimental import pallas as pl
from jax.experimental.pallas import tpu as pltpu
from jax.sharding import PartitionSpec as P

HEADS = 12
HEAD_DIM = 64
HALF = 32
FREQS = 192
CODES = 4 * FREQS
VMEM_LIMIT = 60 * 1024 * 1024
F32 = jnp.float32
BF16 = jnp.bfloat16


def dot(left, right):
    return lax.dot_general(left, right, (((1,), (0,)), ((), ())), preferred_element_type=F32)


def dot_nt(left, right):
    return lax.dot_general(left, right, (((1,), (1,)), ((), ())), preferred_element_type=F32)


def dot_tn(left, right):
    return lax.dot_general(left, right, (((0,), (0,)), ((), ())), preferred_element_type=F32)


def swapped(block, distance, axis="blk"):
    count = lax.axis_size(axis)
    return lax.ppermute(block, axis, [(i, i ^ distance) for i in range(count)])


def from_blk(block, distance):
    return swapped(block, distance) if distance else block


def from_core(block):
    return swapped(block, 1, "core")


def after(done, value):
    return lax.optimization_barrier((value, done))[0]


def turned(upper, lower, cosines, sines):
    return upper * cosines - lower * sines, lower * cosines + upper * sines


def entry_order(rows):
    return jnp.concatenate(
        [
            rows[:FREQS],
            rows[2 * FREQS : 3 * FREQS],
            rows[FREQS : 2 * FREQS],
            rows[3 * FREQS :],
        ],
        axis=0,
    )


def angle_tables():
    rates = np.float32(10000.0) ** (-np.arange(FREQS, dtype=np.float32) / np.float32(FREQS))
    tables = []
    for places in (32.0 * np.arange(32), 0.5 * np.arange(64)):
        angles = rates.astype(np.float64)[:, None] * places[None, :]
        left = np.concatenate([np.sin(angles), np.cos(angles)])
        parts = []
        for _ in range(3):
            parts.append(left.astype(jnp.bfloat16))
            left = left - parts[-1].astype(np.float64)
        tables.append(np.concatenate(parts, axis=1))
    return tables


def rotary_tables(length):
    rates = np.float32(10000.0) ** (-np.arange(HALF, dtype=np.float32) / np.float32(HALF))
    angles = np.arange(length, dtype=np.float32)[None, :] * rates[:, None]
    angles = angles.astype(np.float64)
    return np.cos(angles).astype(np.float32), np.sin(angles).astype(np.float32)


def prepare_kernel(
    words_ref,
    query_ref,
    key_ref,
    value_ref,
    box_ref,
    cos_ref,
    sin_ref,
    own_ref,
    own_box_ref,
    own_cos_ref,
    own_sin_ref,
):
    rank = words_ref[0]
    span = own_box_ref.shape[0]
    width = query_ref.shape[1]
    count = cos_ref.shape[1] // (own_cos_ref.shape[1] // lax.axis_size("blk"))
    block = cos_ref.shape[1] // count
    row = lax.broadcasted_iota(jnp.int32, (span, width), 0) + rank * span
    column = lax.broadcasted_iota(jnp.int32, (span, width), 1)
    pick = jnp.where(row == column, 1.0, 0.0).astype(BF16)
    for kind, ref in enumerate((query_ref, key_ref, value_ref)):
        own_ref[kind] = dot_nt(pick, ref[...]).astype(BF16)
    own_box_ref[...] = dot_nt(pick, entry_order(box_ref[...])).astype(BF16)
    for i in range(count):
        from_cols = pl.ds(pl.multiple_of((rank ^ i) * block, block), block)
        own_cos_ref[:, i * block : (i + 1) * block] = cos_ref[:, from_cols]
        own_sin_ref[:, i * block : (i + 1) * block] = sin_ref[:, from_cols]


def prepare(words, w_query, w_key, w_value, box_weight, span, length):
    width = w_query.shape[0]
    vmem = pl.BlockSpec(memory_space=pltpu.VMEM)
    return pl.pallas_call(
        prepare_kernel,
        in_specs=[pl.BlockSpec(memory_space=pltpu.SMEM)] + [vmem] * 6,
        out_specs=[vmem] * 4,
        out_shape=[
            jax.ShapeDtypeStruct((3, span, width), BF16),
            jax.ShapeDtypeStruct((span, CODES), BF16),
            jax.ShapeDtypeStruct((HALF, length), F32),
            jax.ShapeDtypeStruct((HALF, length), F32),
        ],
        compiler_params=pltpu.CompilerParams(vmem_limit_bytes=VMEM_LIMIT),
        cost_estimate=pl.CostEstimate(
            flops=8 * span * width * width, bytes_accessed=10 * width * width, transcendentals=0
        ),
        name="prepare",
    )(words, w_query, w_key, w_value, box_weight, *map(jnp.asarray, rotary_tables(length)))


def write_codes(page, place_refs, high_ref, low_ref, sin_ref, cos_ref, codes_ref):
    block = place_refs[0].shape[1]

    def looked_up(table_ref, index):
        spots = table_ref.shape[1] // 3
        rows = lax.broadcasted_iota(jnp.int32, (spots, block), 0)
        once = jnp.where(rows == index, 1.0, 0.0)
        found = dot(table_ref[...], jnp.concatenate([once] * 3, axis=0).astype(BF16))
        return found[:FREQS], found[FREQS:]

    for i, place_ref in enumerate(place_refs):
        columns = slice(i * block, (i + 1) * block)
        for axis in range(2):
            place = place_ref[2 * page + axis : 2 * page + axis + 1]
            high_sin, high_cos = looked_up(high_ref, lax.shift_right_logical(place, 6))
            low_sin, low_cos = looked_up(low_ref, place & 63)
            sines = high_sin * low_cos + high_cos * low_sin
            cosines = high_cos * low_cos - high_sin * low_sin
            rows = slice(axis * FREQS, (axis + 1) * FREQS)
            later = slice((2 + axis) * FREQS, (3 + axis) * FREQS)
            sin_ref[rows, columns] = sines
            cos_ref[rows, columns] = cosines
            codes_ref[rows, columns] = sines.astype(BF16)
            codes_ref[later, columns] = cosines.astype(BF16)


def forward_kernel(page, count, *refs):
    place_refs, refs = refs[:count], refs[count:]
    piece_refs, refs = refs[:count], refs[count:]
    high_ref, low_ref, w_ref, box_ref, rot_cos_ref, rot_sin_ref = refs[:6]
    probs_ref, att_ref, heads_ref, sin_ref, cos_ref, codes_ref = refs[6:12]
    low_refs = refs[12 : 12 + count]
    tok_ref, kc_ref, qr_ref = refs[12 + count :]
    rows = tok_ref.shape[0]
    block = rows // count

    @pl.when(pl.program_id(0) == 0)
    def _():
        for i in range(count):
            tok_ref[i * block : (i + 1) * block] = piece_refs[i][...]
        write_codes(page, place_refs, high_ref, low_ref, sin_ref, cos_ref, codes_ref)
        kc_ref[:, :CODES] = codes_ref[...].astype(F32).T.astype(BF16)

    weights = w_ref[...].reshape(3 * HEAD_DIM, w_ref.shape[-1])
    pre = dot_nt(weights, tok_ref[...])
    rot_cos = rot_cos_ref[...]
    rot_sin = rot_sin_ref[...]
    query_pre = pre[:HEAD_DIM].astype(BF16)
    wide = query_pre.astype(F32)
    query = jnp.concatenate(turned(wide[:HALF], wide[HALF:], rot_cos, rot_sin), axis=0)
    key_pre = pre[HEAD_DIM : 2 * HEAD_DIM]
    key = jnp.concatenate(turned(key_pre[:HALF], key_pre[HALF:], rot_cos, rot_sin), axis=0)
    value = pre[2 * HEAD_DIM :].astype(BF16)
    heads_ref[0, :HEAD_DIM] = query_pre
    heads_ref[0, HEAD_DIM : 2 * HEAD_DIM] = query.astype(BF16)
    heads_ref[0, 2 * HEAD_DIM : 3 * HEAD_DIM] = key.astype(BF16)
    heads_ref[0, 3 * HEAD_DIM :] = value
    kc_ref[:, CODES:] = key.T.astype(BF16)
    projected = dot_tn(box_ref[...], query_pre)
    sines = sin_ref[...]
    cosines = cos_ref[...]
    upper = projected[: 2 * FREQS]
    lower = projected[2 * FREQS :]
    qr_ref[: 2 * FREQS] = ((upper * cosines + lower * sines) * 0.125).astype(BF16)
    qr_ref[2 * FREQS : CODES] = ((lower * cosines - upper * sines) * 0.125).astype(BF16)
    qr_ref[CODES:] = (query * 0.125).astype(BF16)
    step = min(256, block)
    for at in range(0, rows, step):
        logits = dot(kc_ref[...], qr_ref[:, at : at + step])
        weight = jnp.exp(logits - jnp.max(logits, axis=0, keepdims=True))
        total = jnp.sum(weight, axis=0, keepdims=True)
        probs = (weight * (1.0 / total)).astype(BF16)
        probs_ref[0, :, at : at + step] = probs
        attended = dot(value, probs)
        att_ref[0, :, at : at + step] = attended
        inner = at % block
        low_refs[at // block][:, inner : inner + step] = attended.astype(BF16)


def fixed(array):
    return pl.BlockSpec(array.shape, lambda *at: (0,) * len(array.shape))


def attention_forward(page, places, pieces, w_own, box_own, rot_cos, rot_sin):
    count = len(pieces)
    block, width = pieces[0].shape
    rows = count * block
    span = box_own.shape[0]
    heads = span // HEAD_DIM
    tables = [jnp.asarray(item) for item in angle_tables()]
    out_shape = [
        jax.ShapeDtypeStruct((heads, rows, rows), BF16),
        jax.ShapeDtypeStruct((heads, HEAD_DIM, rows), F32),
        jax.ShapeDtypeStruct((heads, 4 * HEAD_DIM, rows), BF16),
        jax.ShapeDtypeStruct((2 * FREQS, rows), F32),
        jax.ShapeDtypeStruct((2 * FREQS, rows), F32),
        jax.ShapeDtypeStruct((CODES, rows), BF16),
    ] + [jax.ShapeDtypeStruct((span, block), BF16)] * count
    return pl.pallas_call(
        functools.partial(forward_kernel, page, count),
        grid=(heads,),
        in_specs=[fixed(item) for item in (*places, *pieces, *tables)]
        + [
            pl.BlockSpec((3, HEAD_DIM, width), lambda h: (0, h, 0)),
            pl.BlockSpec((HEAD_DIM, CODES), lambda h: (h, 0)),
            fixed(rot_cos),
            fixed(rot_sin),
        ],
        out_specs=[
            pl.BlockSpec((1, rows, rows), lambda h: (h, 0, 0)),
            pl.BlockSpec((1, HEAD_DIM, rows), lambda h: (h, 0, 0)),
            pl.BlockSpec((1, 4 * HEAD_DIM, rows), lambda h: (h, 0, 0)),
        ]
        + [fixed(item) for item in out_shape[3:6]]
        + [pl.BlockSpec((HEAD_DIM, block), lambda h: (h, 0))] * count,
        out_shape=out_shape,
        scratch_shapes=[
            pltpu.VMEM((rows, width), BF16),
            pltpu.VMEM((rows, CODES + HEAD_DIM), BF16),
            pltpu.VMEM((CODES + HEAD_DIM, rows), BF16),
        ],
        compiler_params=pltpu.CompilerParams(vmem_limit_bytes=VMEM_LIMIT),
        cost_estimate=pl.CostEstimate(
            flops=2 * heads * rows * (rows * 1100 + 200 * width + 64 * CODES),
            bytes_accessed=2 * heads * rows * rows + 12 * rows * width,
            transcendentals=heads * rows * rows,
        ),
        name="attention_forward",
    )(*places, *pieces, *tables, w_own, box_own, rot_cos, rot_sin)


def backward_kernel(count, last, words_ref, *refs):
    grad_refs, refs = refs[:count], refs[count:]
    piece_refs, refs = refs[:count], refs[count:]
    probs_ref, att_ref, heads_ref, box_ref, codes_ref, sin_ref, cos_ref = refs[:7]
    rot_cos_ref, rot_sin_ref = refs[7:9]
    refs = refs[9:]
    if last:
        before_ref, refs = refs[0], refs[1:]
    pre_refs, refs = refs[:count], refs[count:]
    if last:
        mine_ref, theirs_ref, *refs = refs
    weight_grad_ref, kc_ref = refs
    block, width = piece_refs[0].shape
    rows = count * block
    head = pl.program_id(0)
    span = pl.num_programs(0) * HEAD_DIM

    @pl.when(head == 0)
    def _():
        kc_ref[:CODES] = codes_ref[...]

    kc_ref[CODES:] = heads_ref[0, 2 * HEAD_DIM : 3 * HEAD_DIM]
    packed = heads_ref[0].astype(F32).T.astype(BF16)
    query_pre = packed[:, :HEAD_DIM]
    query = packed[:, HEAD_DIM : 2 * HEAD_DIM]
    value = packed[:, 3 * HEAD_DIM :] * jnp.asarray(0.125, BF16)
    rot_cos = rot_cos_ref[...]
    rot_sin = rot_sin_ref[...]
    grad = jnp.concatenate([ref[...] for ref in grad_refs], axis=1)
    grad_tall = grad.astype(F32).T.astype(BF16)
    offsets = jnp.sum(grad.astype(F32) * att_ref[0], axis=0, keepdims=True) * 0.125
    step = min(256, block)
    place = pl.multiple_of(head * HEAD_DIM, HEAD_DIM)
    here = pl.ds(place, HEAD_DIM)
    key_grad = jnp.zeros((rows, HEAD_DIM), F32)
    value_grad = jnp.zeros((rows, HEAD_DIM), F32)
    box_grad = jnp.zeros((CODES, HEAD_DIM), F32)
    for at in range(0, rows, step):
        part = slice(at, at + step)
        probs = probs_ref[0, :, part]
        grad_probs = dot(value, grad[:, part])
        grad_logits = (probs.astype(F32) * (grad_probs - offsets[:, part])).astype(BF16)
        back = dot(kc_ref[...], grad_logits)
        sines = sin_ref[:, part]
        cosines = cos_ref[:, part]
        upper = back[: 2 * FREQS]
        lower = back[2 * FREQS : CODES]
        projected_grad = jnp.concatenate(
            [
                (upper * cosines - lower * sines).astype(BF16),
                (lower * cosines + upper * sines).astype(BF16),
            ],
            axis=0,
        )
        first = back[CODES : CODES + HALF]
        second = back[CODES + HALF :]
        own = jnp.concatenate(
            turned(first, second, rot_cos[:, part], -rot_sin[:, part]), axis=0
        )
        inner = at % block
        pre_refs[at // block][here, inner : inner + step] = (
            own + dot(box_ref[...], projected_grad)
        ).astype(BF16)
        key_grad = key_grad + dot(grad_logits, query[part])
        value_grad = value_grad + dot(probs, grad_tall[part])
        box_grad = box_grad + dot(projected_grad, query_pre[part])
    key_flat = key_grad.T
    key_low = jnp.concatenate(
        turned(key_flat[:HALF], key_flat[HALF:], rot_cos, -rot_sin), axis=0
    ).astype(BF16)
    value_low = value_grad.T.astype(BF16)
    for i in range(count):
        columns = slice(i * block, (i + 1) * block)
        pre_refs[i][here, block : 2 * block] = key_low[:, columns]
        pre_refs[i][here, 2 * block :] = value_low[:, columns]
    weight_grad_ref[pl.ds(3 * span + place, HEAD_DIM)] = box_grad.T

    @pl.when(head == pl.num_programs(0) - 1)
    def _():
        for kind in range(3):
            columns = slice(kind * block, (kind + 1) * block)
            total = dot(pre_refs[0][:, columns], piece_refs[0][...])
            for i in range(1, count):
                total = total + dot(pre_refs[i][:, columns], piece_refs[i][...])
            weight_grad_ref[kind * span : (kind + 1) * span] = total
        if last:
            half = 2 * span
            core = words_ref[2]
            ours = pl.ds(pl.multiple_of(core * half, half), half)
            there = pl.ds(pl.multiple_of((1 - core) * half, half), half)
            mine_ref[...] = weight_grad_ref[ours] + before_ref[ours]
            theirs_ref[...] = (weight_grad_ref[there] + before_ref[there]).astype(BF16)


def attention_backward(words, page, grads, pieces, saved, box_own, rot_cos, rot_sin, before=None):
    probs, att, heads_saved, sines, cosines, codes = saved
    count = len(pieces)
    block, width = pieces[0].shape
    rows = count * block
    span = box_own.shape[0]
    heads = span // HEAD_DIM
    last = before is not None
    extra = (before,) if last else ()
    full_shape = (4 * span, width)
    out_shape = [jax.ShapeDtypeStruct((span, 3 * block), BF16)] * count
    if last:
        out_shape += [
            jax.ShapeDtypeStruct((2 * span, width), F32),
            jax.ShapeDtypeStruct((2 * span, width), BF16),
        ]
    else:
        out_shape.append(jax.ShapeDtypeStruct(full_shape, F32))
    return pl.pallas_call(
        functools.partial(backward_kernel, count, last),
        grid=(heads,),
        in_specs=[pl.BlockSpec(memory_space=pltpu.SMEM)]
        + [pl.BlockSpec((HEAD_DIM, block), lambda h: (h, page))] * count
        + [fixed(item) for item in pieces]
        + [
            pl.BlockSpec((1, rows, rows), lambda h: (h, 0, 0)),
            pl.BlockSpec((1, HEAD_DIM, rows), lambda h: (h, 0, 0)),
            pl.BlockSpec((1, 4 * HEAD_DIM, rows), lambda h: (h, 0, 0)),
            pl.BlockSpec((HEAD_DIM, CODES), lambda h: (h, 0)),
        ]
        + [fixed(item) for item in (codes, sines, cosines, rot_cos, rot_sin, *extra)],
        out_specs=[fixed(item) for item in out_shape],
        out_shape=out_shape,
        scratch_shapes=([pltpu.VMEM(full_shape, F32)] if last else [])
        + [pltpu.VMEM((CODES + HEAD_DIM, rows), BF16)],
        compiler_params=pltpu.CompilerParams(vmem_limit_bytes=VMEM_LIMIT),
        cost_estimate=pl.CostEstimate(
            flops=2 * heads * rows * (rows * 1400 + 200 * width + 128 * CODES),
            bytes_accessed=2 * heads * rows * rows + 12 * rows * width,
            transcendentals=0,
        ),
        name="attention_backward",
    )(
        words,
        *grads,
        *pieces,
        probs,
        att,
        heads_saved,
        box_own,
        codes,
        sines,
        cosines,
        rot_cos,
        rot_sin,
        *extra,
    )


def normed(value):
    centered = value - jnp.mean(value, axis=-1, keepdims=True)
    scale = lax.rsqrt(jnp.mean(centered * centered, axis=-1, keepdims=True) + 1e-05)
    return centered * scale, scale


def norm_back(grad, gain, unit, scale):
    scaled = grad * gain
    return scale * (
        scaled
        - jnp.mean(scaled, axis=-1, keepdims=True)
        - unit * jnp.mean(scaled * unit, axis=-1, keepdims=True)
    )


def column_sum(value):
    return jnp.sum(value, axis=0, keepdims=True)


def middle_kernel(pages, count, span, chunks, *refs):
    total = pages * count
    words_ref = refs[0]
    att_refs = refs[1 : 1 + total]
    (
        tok_ref,
        cot_ref,
        w_out_ref,
        vectors_ref,
        w_expand_ref,
        w_reduce_ref,
    ) = refs[1 + total : 7 + total]
    outs = refs[7 + total :]
    layer_ref, first_in_ref, theirs_ref, mine_ref, more_theirs_ref, more_mine_ref = outs[:6]
    grad_refs = outs[6 : 6 + count]
    (
        sums_ref,
        att_all,
        grad_all,
        unit_one,
        scale_one,
        first_wide,
        first_low,
        first_tall,
        active,
        slope,
        gathered,
        second_in,
        second_low,
    ) = outs[6 + count :]
    rank = words_ref[0]
    width = tok_ref.shape[1]
    block = tok_ref.shape[0] // pages
    step = pl.program_id(0)

    def rows_of(at):
        return pl.ds(pl.multiple_of((rank ^ at) * span, span), span)

    @pl.when(step == 0)
    def _():
        for page in range(pages):
            for at in range(count):
                att_all[rows_of(at), page * block : (page + 1) * block] = att_refs[
                    page * count + at
                ][...]
        branch = dot_tn(att_all[: w_out_ref.shape[0]], w_out_ref[...])
        unit, scale = normed(tok_ref[...].astype(F32) + branch)
        unit_one[...] = unit
        scale_one[...] = jnp.broadcast_to(scale, scale_one.shape)
        first_out = unit * vectors_ref[0:1] + vectors_ref[1:2]
        first_wide[...] = first_out
        first_low[...] = first_out.astype(BF16)
        first_tall[...] = first_out.T.astype(BF16)
        gathered[...] = jnp.zeros_like(gathered)
        sums_ref[...] = jnp.zeros_like(sums_ref)

    for chunk in range(chunks):

        @pl.when(step == chunk)
        def _(chunk=chunk):
            expanded = dot(first_low[...], w_expand_ref[...])
            gate = 0.5 + 0.5 * lax.erf(expanded * np.float32(np.sqrt(0.5)))
            bell = jnp.exp(expanded * expanded * -0.5) * np.float32(1.0 / np.sqrt(2.0 * np.pi))
            low = (expanded * gate).astype(BF16)
            active[chunk] = low
            slope[chunk] = gate + expanded * bell
            gathered[...] += dot(low, w_reduce_ref[...])

    @pl.when(step == chunks - 1)
    def _():
        unit, scale = normed(first_wide[...] + gathered[...])
        layer_ref[...] = (unit * vectors_ref[2:3] + vectors_ref[3:4]).astype(BF16)
        cot = cot_ref[...].astype(F32)
        sums_ref[2:3] = column_sum(cot * unit)
        sums_ref[3:4] = column_sum(cot)
        grad = norm_back(cot, vectors_ref[2:3], unit, scale)
        second_in[...] = grad
        second_low[...] = grad.astype(BF16)
        gathered[...] = grad

    for chunk in range(chunks):

        @pl.when(step == 2 * chunks - 1 - chunk)
        def _(chunk=chunk):
            grad_active = dot_nt(second_low[...], w_reduce_ref[...])
            grad_expanded = (grad_active * slope[chunk]).astype(BF16)
            grads_ref = mine_ref if chunk < chunks // 2 else theirs_ref
            grads_ref[:width] = dot(first_tall[...], grad_expanded).astype(BF16)
            grads_ref[width:] = dot_tn(active[chunk], second_low[...]).astype(BF16)
            gathered[...] += dot_nt(grad_expanded, w_expand_ref[...])

    @pl.when(step == 2 * chunks - 1)
    def _():
        unit = unit_one[...]
        grad_out = gathered[...]
        sums_ref[0:1] = column_sum(grad_out * unit)
        sums_ref[1:2] = column_sum(grad_out)
        grad = norm_back(grad_out, vectors_ref[0:1], unit, scale_one[:, :1])
        first_in_ref[...] = grad
        low = grad.astype(BF16)
        real = w_out_ref.shape[0]
        half = real // 2
        core = words_ref[2]
        for ref, side in ((more_mine_ref, core), (more_theirs_ref, 1 - core)):
            rows = pl.ds(pl.multiple_of(side * half, half), half)
            ref[:half] = dot(att_all[rows], low).astype(BF16)
            ref[half:] = jnp.zeros((ref.shape[0] - half, width), BF16)
            ref[half : half + 16] = sums_ref[...].astype(BF16)
        if grad_all.shape[0] > real:
            grad_all[real:] = jnp.zeros((grad_all.shape[0] - real, low.shape[0]), BF16)
        grad_all[:real] = dot_nt(w_out_ref[...], low).astype(BF16)
        for at in range(count):
            grad_refs[at][...] = grad_all[rows_of(at)]


def middle(words, att_parts, tok, cot, w_out, vectors, w_expand, w_reduce, pages, more):
    rows, width = tok.shape
    count = len(att_parts) // pages
    span, block = att_parts[0].shape
    hidden = w_expand.shape[1]
    chunks = hidden // width
    pairs = chunks // 2

    def whole(array):
        return pl.BlockSpec(array.shape, lambda s, words: (0,) * len(array.shape))

    def chunk_at(s, words):
        at = jnp.minimum(s, 2 * chunks - 1 - s)
        return (at + words[2] * pairs) % chunks

    def theirs_at(s, words):
        return jnp.clip(2 * chunks - 1 - s - pairs, 0, pairs - 1), 0

    def mine_at(s, words):
        return jnp.clip(2 * chunks - 1 - s, 0, pairs - 1), 0

    shapes = [
        jax.ShapeDtypeStruct((rows, width), BF16),
        jax.ShapeDtypeStruct((rows, width), F32),
        jax.ShapeDtypeStruct((hidden, width), BF16),
        jax.ShapeDtypeStruct((hidden, width), BF16),
        jax.ShapeDtypeStruct((more, width), BF16),
        jax.ShapeDtypeStruct((more, width), BF16),
    ] + [jax.ShapeDtypeStruct((span, pages * block), BF16)] * count
    specs = [whole(item) for item in shapes]
    specs[2] = pl.BlockSpec((2 * width, width), theirs_at)
    specs[3] = pl.BlockSpec((2 * width, width), mine_at)
    return pl.pallas_call(
        functools.partial(middle_kernel, pages, count, span, chunks),
        grid_spec=pltpu.PrefetchScalarGridSpec(
            num_scalar_prefetch=1,
            grid=(2 * chunks,),
            in_specs=[whole(item) for item in att_parts]
            + [
                whole(tok),
                whole(cot),
                whole(w_out),
                whole(vectors),
                pl.BlockSpec((width, width), lambda s, words: (0, chunk_at(s, words))),
                pl.BlockSpec((width, width), lambda s, words: (chunk_at(s, words), 0)),
            ],
            out_specs=specs,
            scratch_shapes=[
                pltpu.VMEM((16, width), F32),
                pltpu.VMEM((count * span, rows), BF16),
                pltpu.VMEM((count * span, rows), BF16),
                pltpu.VMEM((rows, width), F32),
                pltpu.VMEM((rows, 128), F32),
                pltpu.VMEM((rows, width), F32),
                pltpu.VMEM((rows, width), BF16),
                pltpu.VMEM((width, rows), BF16),
                pltpu.VMEM((chunks, rows, width), BF16),
                pltpu.VMEM((chunks, rows, width), F32),
                pltpu.VMEM((rows, width), F32),
                pltpu.VMEM((rows, width), F32),
                pltpu.VMEM((rows, width), BF16),
            ],
        ),
        out_shape=shapes,
        compiler_params=pltpu.CompilerParams(vmem_limit_bytes=VMEM_LIMIT),
        cost_estimate=pl.CostEstimate(
            flops=2 * rows * width * (6 * hidden + 3 * width),
            bytes_accessed=8 * width * hidden + 16 * rows * width,
            transcendentals=2 * rows * hidden,
        ),
        name="middle",
    )(words, *att_parts, tok, cot, w_out, vectors, w_expand, w_reduce)


def input_kernel(pages, count, span, bases, *refs):
    total = pages * count
    words_ref = refs[0]
    part_refs = refs[1 : 1 + total]
    weight_refs = refs[1 + total : 4 + total]
    first_in_ref, out_ref, held = refs[4 + total :]
    rank = words_ref[0]
    width = out_ref.shape[1]
    block = out_ref.shape[0] // pages
    for page in range(pages):
        for at in range(count):
            base = bases[page] if at else 0
            part = part_refs[page * count + at]
            place = pl.multiple_of((rank ^ at) * span, span)
            for kind in range(3):
                held[kind, pl.ds(place, span), page * block : (page + 1) * block] = part[
                    base : base + span, kind * block : (kind + 1) * block
                ]
    total = dot(weight_refs[0][...], held[0, :width])
    for kind in range(1, 3):
        total = total + dot(weight_refs[kind][...], held[kind, :width])
    out_ref[...] = (first_in_ref[...] + total.T).astype(BF16)


def input_gradient(words, parts, bases, span, weights, first_in, pages):
    count = len(parts) // pages
    rows, width = first_in.shape
    vmem = pl.BlockSpec(memory_space=pltpu.VMEM)
    return pl.pallas_call(
        functools.partial(input_kernel, pages, count, span, bases),
        in_specs=[pl.BlockSpec(memory_space=pltpu.SMEM)] + [vmem] * (len(parts) + 4),
        out_specs=vmem,
        out_shape=jax.ShapeDtypeStruct((rows, width), BF16),
        scratch_shapes=[pltpu.VMEM((3, count * span, rows), BF16)],
        compiler_params=pltpu.CompilerParams(vmem_limit_bytes=VMEM_LIMIT),
        cost_estimate=pl.CostEstimate(
            flops=6 * rows * width * count * span,
            bytes_accessed=2 * width * (5 * rows + 3 * count * span),
            transcendentals=0,
        ),
        name="input_gradient",
    )(words, *parts, *weights, first_in)


def local(body, name, words, arrays, shapes):
    def kernel(words_ref, *refs):
        body(words_ref, refs[: len(arrays)], refs[len(arrays) :])

    vmem = pl.BlockSpec(memory_space=pltpu.VMEM)
    shapes = [jax.ShapeDtypeStruct(shape, kind) for shape, kind in shapes]
    moved = sum(item.size * item.dtype.itemsize for item in list(arrays) + shapes)
    return pl.pallas_call(
        kernel,
        in_specs=[pl.BlockSpec(memory_space=pltpu.SMEM)] + [vmem] * len(arrays),
        out_specs=[vmem] * len(shapes),
        out_shape=shapes,
        compiler_params=pltpu.CompilerParams(vmem_limit_bytes=VMEM_LIMIT),
        cost_estimate=pl.CostEstimate(flops=moved, bytes_accessed=moved, transcendentals=0),
        name=name,
    )(words, *arrays)


def shard(index, rows, base=0):
    return pl.ds(pl.multiple_of(base + index * rows, 16), rows)


def total_of(refs, rows=slice(None)):
    total = refs[0][rows].astype(F32)
    for ref in refs[1:]:
        total = total + ref[rows].astype(F32)
    return total


def tree_sum(terms):
    while len(terms) > 1:
        terms = [terms[i] + terms[i + 1] for i in range(0, len(terms), 2)]
    return terms[0]


class Plan:
    def __init__(self, rows, rows_a, more, span, width):
        self.count = lax.axis_size("blk")
        self.rows = rows
        self.rows_a = rows_a
        self.more = more
        self.span = span
        self.width = width
        self.a_ff = rows_a // self.count
        self.a_more = more // self.count
        self.a = self.a_ff + self.a_more
        self.b = (rows - rows_a) // lax.axis_size("depth")

    def shapes(self, *sizes):
        return [((rows, self.width), BF16) for rows in sizes]

    def scatter_one(self, words, halves):
        def body(words, ins, outs):
            for i in range(self.count):
                rows = shard(words[0] ^ i, self.a_ff)
                outs[i][: self.a_ff] = total_of(ins[:2], rows).astype(BF16)
                rows = shard(words[0] ^ i, self.a_more)
                outs[i][self.a_ff :] = total_of(ins[2:], rows).astype(BF16)
            outs[self.count][...] = total_of(ins[:2], slice(self.rows_a, None)).astype(BF16)

        shapes = self.shapes(*[self.a] * self.count, self.rows - self.rows_a)
        *parts_a, part_b = local(body, "scatter_one", words, halves, shapes)
        return [from_blk(part, i) for i, part in enumerate(parts_a)], part_b

    def scatter_two(self, words, parts_a, part_b, pieces):
        def body(words, ins, outs):
            outs[0][...] = total_of(ins[: self.count]).astype(BF16)
            for out, piece in zip(outs[1:], ins[self.count + 1 :]):
                out[: self.b] = ins[self.count][...]
                out[self.b :, : piece.shape[1]] = piece[...]

        shapes = self.shapes(self.a, *[self.b + self.span] * (self.count - 1))
        part_a, *messages = local(
            body, "scatter_two", words, [*parts_a, part_b, *pieces[1:]], shapes
        )
        return part_a, [from_blk(item, i + 1) for i, item in enumerate(messages)]

    def gather_a(self, words, part_a, pieces):
        def body(words, ins, outs):
            for out, piece in zip(outs, ins[1:]):
                out[: self.a] = ins[0][...]
                out[self.a :, : piece.shape[1]] = piece[...]

        shapes = self.shapes(*[self.a + self.span] * (self.count - 1))
        messages = local(body, "gather_a", words, [part_a, *pieces[1:]], shapes)
        return [from_blk(item, i + 1) for i, item in enumerate(messages)]

    def sum_b(self, words, part_b, messages):
        def body(words, ins, outs):
            terms = [ref[: self.b].astype(F32) for ref in ins]
            outs[0][...] = tree_sum(terms).astype(BF16)

        return local(body, "sum_b", words, [part_b, *messages], self.shapes(self.b))[0]

    def join(self, words, part_a, messages, gathered_b):
        def body(words, ins, outs):
            for i in range(self.count):
                outs[0][shard(words[0] ^ i, self.a_ff)] = ins[i][: self.a_ff]
                outs[1][shard(words[0] ^ i, self.a_more)] = ins[i][self.a_ff : self.a]
            outs[0][self.rows_a :] = ins[self.count][...]

        shapes = self.shapes(self.rows, self.more)
        return local(body, "join", words, [part_a, *messages, gathered_b], shapes)


def widened(words, half, side, hidden, before=()):
    width = half.shape[1]
    chunks = hidden // width
    pairs = chunks // 2

    def kernel(words_ref, half_ref, *refs):
        expand_ref, reduce_ref = refs[len(before) :]
        expand_ref[...] = half_ref[:width].astype(F32)
        reduce_ref[...] = half_ref[width:].astype(F32)

    def place(s, words):
        return (s + (words[2] + side) * pairs) % chunks

    return pl.pallas_call(
        kernel,
        grid_spec=pltpu.PrefetchScalarGridSpec(
            num_scalar_prefetch=1,
            grid=(pairs,),
            in_specs=[pl.BlockSpec((2 * width, width), lambda s, words: (s, 0))]
            + [pl.BlockSpec(memory_space=pl.ANY)] * len(before),
            out_specs=[
                pl.BlockSpec((width, width), lambda s, words: (0, place(s, words))),
                pl.BlockSpec((width, width), lambda s, words: (place(s, words), 0)),
            ],
        ),
        out_shape=[
            jax.ShapeDtypeStruct((width, hidden), F32),
            jax.ShapeDtypeStruct((hidden, width), F32),
        ],
        input_output_aliases={2: 0, 3: 1} if before else {},
        compiler_params=pltpu.CompilerParams(vmem_limit_bytes=VMEM_LIMIT),
        cost_estimate=pl.CostEstimate(
            flops=0, bytes_accessed=6 * hidden * width, transcendentals=0
        ),
        name="widen",
    )(words, half, *before)


def core_sum(words, mine, other):
    def body(words, ins, outs):
        outs[0][...] = total_of(ins).astype(BF16)

    return local(body, "heads_sum", words, [mine, other], [(mine.shape, BF16)])[0]


def join_blk(words, own):
    count = lax.axis_size("blk")
    half, width = own.shape
    parts = [from_blk(own, i) for i in range(count)]

    def body(words, ins, outs):
        for i in range(count):
            outs[0][shard(words[0] ^ i, half)] = ins[i][...]

    return local(body, "heads_join", words, parts, [((count * half, width), BF16)])[0]


def finish_kernel(count, span, half, words_ref, *refs):
    own_ref, other_ref, more_ref, more_other_ref = refs[:4]
    query_ref, key_ref, value_ref, project_ref, box_ref, sums_ref = refs[4:]
    width = query_ref.shape[0]

    def write(lower_ref, upper_ref, more_lower_ref, more_upper_ref):
        def grad(ref, part):
            rows = [
                ref[(2 * i + part) * span : (2 * i + part + 1) * span].astype(F32)
                for i in range(count)
            ]
            return jnp.concatenate(rows, axis=0)[:width].T

        query_ref[...] = grad(lower_ref, 0)
        key_ref[...] = grad(lower_ref, 1)
        value_ref[...] = grad(upper_ref, 0)
        box_ref[...] = entry_order(grad(upper_ref, 1))
        project_ref[:half] = more_lower_ref[:half].astype(F32)
        project_ref[half:] = more_upper_ref[:half].astype(F32)
        sums_ref[...] = more_lower_ref[half : half + 16].astype(F32)[:8]

    @pl.when(words_ref[2] == 0)
    def _():
        write(own_ref, other_ref, more_ref, more_other_ref)

    @pl.when(words_ref[2] == 1)
    def _():
        write(other_ref, own_ref, more_other_ref, more_ref)


def finished(words, own, other, more, more_other, span, width):
    count = lax.axis_size("blk")
    vmem = pl.BlockSpec(memory_space=pltpu.VMEM)
    shapes = [jax.ShapeDtypeStruct((width, width), F32)] * 5
    shapes.append(jax.ShapeDtypeStruct((8, width), F32))
    return pl.pallas_call(
        functools.partial(finish_kernel, count, span, width // 2),
        in_specs=[pl.BlockSpec(memory_space=pltpu.SMEM)] + [vmem] * 4,
        out_specs=[vmem] * 6,
        out_shape=shapes,
        compiler_params=pltpu.CompilerParams(vmem_limit_bytes=VMEM_LIMIT),
        cost_estimate=pl.CostEstimate(
            flops=0, bytes_accessed=32 * width * width, transcendentals=0
        ),
        name="finish",
    )(words, own, other, more, more_other)


def per_device(
    tokens,
    boxes,
    w_query,
    w_key,
    w_value,
    w_output,
    box_weight,
    first_gain,
    first_shift,
    w_expand,
    w_reduce,
    second_gain,
    second_shift,
    cotangent,
):
    pages, block, width = tokens.shape
    count = lax.axis_size("blk")
    depth = lax.axis_size("depth")
    words = jnp.stack(
        [lax.axis_index("blk"), lax.axis_index("depth"), lax.axis_index("core")]
    ).astype(jnp.int32)
    hidden = w_expand.shape[1]
    span = -(-HEADS // count) * HEAD_DIM
    unit = 16 * count * depth
    more = -(-(width // 2 + 16) // unit) * unit

    own_places = jnp.stack([boxes[0] + boxes[2], boxes[1] + boxes[3]], axis=1)
    own_places = own_places.reshape(2 * pages, block)
    places = [from_blk(own_places, i) for i in range(count)]
    pieces = [[from_blk(tokens[0], i) for i in range(count)]]
    w_own, box_own, rot_cos, rot_sin = prepare(
        words, w_query, w_key, w_value, box_weight, span, count * block
    )
    for page in range(1, pages):
        own = after(w_own, tokens[page])
        pieces.append([from_blk(own, i) for i in range(count)])

    saved = []
    att_parts = []
    for page in range(pages):
        results = attention_forward(
            page, places, pieces[page], w_own, box_own, rot_cos, rot_sin
        )
        saved.append(results[:6])
        att_parts += [from_blk(results[6 + i], i) for i in range(count)]

    vectors = jnp.stack([first_gain, first_shift, second_gain, second_shift])
    results = middle(
        words,
        att_parts,
        tokens.reshape(pages * block, width),
        cotangent.reshape(pages * block, width),
        w_output,
        vectors,
        w_expand,
        w_reduce,
        pages,
        more,
    )
    layer_out, first_in, theirs, mine, more_theirs, more_mine = results[:6]
    grads = [from_blk(results[6 + i], i) for i in range(count)]
    plan = Plan(hidden, hidden // 2, more, span, width)
    parts_a, part_b = plan.scatter_one(
        words, [mine, from_core(theirs), more_mine, from_core(more_theirs)]
    )
    part_b = lax.psum_scatter(part_b, "depth", scatter_dimension=0, tiled=True)

    def backward(page, words, before=None):
        return attention_backward(
            words,
            page,
            grads,
            pieces[page],
            saved[page],
            box_own,
            rot_cos,
            rot_sin,
            before,
        )

    *pre_one, before = backward(0, after(parts_a[0], words))
    part_a, messages_b = plan.scatter_two(after(before, words), parts_a, part_b, pre_one)
    before = after(part_a, before)
    part_a = lax.psum(part_a, "depth")
    *pre_two, heads_mine, heads_theirs = backward(1, words, before)

    messages_a = plan.gather_a(after(heads_mine, words), part_a, pre_two)
    heads_own = core_sum(after(messages_a[0], words), heads_mine, from_core(heads_theirs))
    part_b = plan.sum_b(after(heads_own, words), part_b, messages_b)
    heads_own = lax.psum(heads_own, "depth")
    gathered_b = lax.all_gather(part_b, "depth", axis=0, tiled=True)
    input_grad = input_gradient(
        after(part_b, words),
        [pre_one[0], *messages_b, pre_two[0], *messages_a],
        (plan.b, plan.a),
        span,
        (w_query, w_key, w_value),
        first_in,
        pages,
    )
    ff, extra = plan.join(after(input_grad, words), part_a, messages_a, gathered_b)
    ff_other, extra_other = from_core(ff), from_core(extra)
    wide = widened(words, ff, 0, hidden)
    heads_own = join_blk(after(wide[0], words), heads_own)
    heads_other = from_core(heads_own)
    grad_expand, grad_reduce = widened(after(heads_own, words), ff_other, 1, hidden, wide)
    grad_query, grad_key, grad_value, grad_project, grad_box, sums = finished(
        words, heads_own, heads_other, extra, extra_other, span, width
    )
    return (
        layer_out.reshape(tokens.shape),
        input_grad.reshape(tokens.shape),
        grad_query,
        grad_key,
        grad_value,
        grad_project,
        grad_box,
        sums[0],
        sums[1],
        grad_expand,
        grad_reduce,
        sums[2],
        sums[3],
    )


def solution(mesh):
    blocks, rest = mesh.devices.shape
    parts = jax.sharding.Mesh(
        mesh.devices.reshape(blocks, rest // 2, 2), ("blk", "depth", "core")
    )
    split = P(("depth", "core"), "blk", None)
    return jax.shard_map(
        per_device,
        mesh=parts,
        in_specs=(split, P(None, ("depth", "core"), "blk")) + (P(),) * 11 + (split,),
        out_specs=(split, split) + (P(),) * 11,
        check_vma=False,
    )
```

```python
import functools

import jax
import jax.numpy as jnp
import numpy as np
from jax import lax
from jax.experimental import pallas as pl
from jax.experimental.pallas import tpu as pltpu
from jax.sharding import PartitionSpec as P

HEADS = 12
HEAD_DIM = 64
HALF = 32
FREQS = 192
CODES = 4 * FREQS
VMEM_LIMIT = 60 * 1024 * 1024
F32 = jnp.float32
BF16 = jnp.bfloat16


def dot(left, right):
    return lax.dot_general(left, right, (((1,), (0,)), ((), ())), preferred_element_type=F32)


def dot_nt(left, right):
    return lax.dot_general(left, right, (((1,), (1,)), ((), ())), preferred_element_type=F32)


def dot_tn(left, right):
    return lax.dot_general(left, right, (((0,), (0,)), ((), ())), preferred_element_type=F32)


def swapped(block, distance, axis="blk"):
    count = lax.axis_size(axis)
    return lax.ppermute(block, axis, [(i, i ^ distance) for i in range(count)])


def from_blk(block, distance):
    return swapped(block, distance) if distance else block


def from_core(block):
    return swapped(block, 1, "core")


def after(done, value):
    return lax.optimization_barrier((value, done))[0]


def turned(upper, lower, cosines, sines):
    return upper * cosines - lower * sines, lower * cosines + upper * sines


def entry_order(rows):
    return jnp.concatenate(
        [
            rows[:FREQS],
            rows[2 * FREQS : 3 * FREQS],
            rows[FREQS : 2 * FREQS],
            rows[3 * FREQS :],
        ],
        axis=0,
    )


def angle_tables():
    rates = np.float32(10000.0) ** (-np.arange(FREQS, dtype=np.float32) / np.float32(FREQS))
    tables = []
    for places in (32.0 * np.arange(32), 0.5 * np.arange(64)):
        angles = rates.astype(np.float64)[:, None] * places[None, :]
        left = np.concatenate([np.sin(angles), np.cos(angles)])
        parts = []
        for _ in range(3):
            parts.append(left.astype(jnp.bfloat16))
            left = left - parts[-1].astype(np.float64)
        tables.append(np.concatenate(parts, axis=1))
    return tables


def rotary_tables(length):
    rates = np.float32(10000.0) ** (-np.arange(HALF, dtype=np.float32) / np.float32(HALF))
    angles = np.arange(length, dtype=np.float32)[None, :] * rates[:, None]
    angles = angles.astype(np.float64)
    return np.cos(angles).astype(np.float32), np.sin(angles).astype(np.float32)


def prepare_kernel(
    words_ref,
    query_ref,
    key_ref,
    value_ref,
    box_ref,
    cos_ref,
    sin_ref,
    own_ref,
    own_box_ref,
    own_cos_ref,
    own_sin_ref,
):
    rank = words_ref[0]
    span = own_box_ref.shape[0]
    width = query_ref.shape[1]
    count = lax.axis_size("blk")
    block = cos_ref.shape[1] // count
    row = lax.broadcasted_iota(jnp.int32, (span, width), 0) + rank * span
    column = lax.broadcasted_iota(jnp.int32, (span, width), 1)
    pick = jnp.where(row == column, 1.0, 0.0).astype(BF16)
    for kind, ref in enumerate((query_ref, key_ref, value_ref)):
        own_ref[kind * span : (kind + 1) * span] = dot_nt(pick, ref[...]).astype(BF16)
    own_box_ref[...] = dot_nt(pick, entry_order(box_ref[...])).astype(BF16)
    for i in range(count):
        from_cols = pl.ds(pl.multiple_of((rank ^ i) * block, block), block)
        own_cos_ref[:, i * block : (i + 1) * block] = cos_ref[:, from_cols]
        own_sin_ref[:, i * block : (i + 1) * block] = sin_ref[:, from_cols]


def prepare(words, w_query, w_key, w_value, box_weight, span, length):
    width = w_query.shape[0]
    vmem = pl.BlockSpec(memory_space=pltpu.VMEM)
    return pl.pallas_call(
        prepare_kernel,
        in_specs=[pl.BlockSpec(memory_space=pltpu.SMEM)] + [vmem] * 6,
        out_specs=[vmem] * 4,
        out_shape=[
            jax.ShapeDtypeStruct((3 * span, width), BF16),
            jax.ShapeDtypeStruct((span, CODES), BF16),
            jax.ShapeDtypeStruct((HALF, length), F32),
            jax.ShapeDtypeStruct((HALF, length), F32),
        ],
        compiler_params=pltpu.CompilerParams(vmem_limit_bytes=VMEM_LIMIT),
        cost_estimate=pl.CostEstimate(
            flops=8 * span * width * width, bytes_accessed=10 * width * width, transcendentals=0
        ),
        name="prepare",
    )(words, w_query, w_key, w_value, box_weight, *map(jnp.asarray, rotary_tables(length)))


def fold(value, combine):
    while value.shape[0] > 8:
        half = value.shape[0] // 2
        value = combine(value[:half], value[half:])
    return value


def write_codes(page, place_refs, high_ref, low_ref, sin_ref, cos_ref, codes_ref):
    block = sin_ref.shape[1] // len(place_refs)

    def looked_up(table_ref, index):
        spots = table_ref.shape[1] // 3
        rows = lax.broadcasted_iota(jnp.int32, (spots, block), 0).astype(F32)
        once = jnp.where(rows == index, 1.0, 0.0)
        found = dot(table_ref[...], jnp.concatenate([once] * 3, axis=0).astype(BF16))
        return found[:FREQS], found[FREQS:]

    for i, place_ref in enumerate(place_refs):
        columns = slice(i * block, (i + 1) * block)
        places = place_ref[:, :block].astype(F32)
        for axis in range(2):
            at = 4 * page + 2 * axis
            high_sin, high_cos = looked_up(high_ref, places[at : at + 1])
            low_sin, low_cos = looked_up(low_ref, places[at + 1 : at + 2])
            sines = high_sin * low_cos + high_cos * low_sin
            cosines = high_cos * low_cos - high_sin * low_sin
            rows = slice(axis * FREQS, (axis + 1) * FREQS)
            later = slice((2 + axis) * FREQS, (3 + axis) * FREQS)
            sin_ref[rows, columns] = sines
            cos_ref[rows, columns] = cosines
            codes_ref[rows, columns] = sines.astype(BF16)
            codes_ref[later, columns] = cosines.astype(BF16)


def forward_kernel(page, count, words_ref, *refs):
    place_refs, refs = refs[:count], refs[count:]
    piece_refs, refs = refs[:count], refs[count:]
    high_ref, low_ref, w_ref, box_ref, rot_cos_ref, rot_sin_ref = refs[:6]
    probs_ref, att_ref, heads_ref, sin_ref, cos_ref, codes_ref = refs[6:12]
    low_refs = refs[12 : 12 + count]
    tok_ref, pre_ref, kc_ref, qr_ref = refs[12 + count :]
    rows = tok_ref.shape[0]
    block = rows // count
    head = pl.program_id(0)
    span = pl.num_programs(0) * HEAD_DIM

    @pl.when(head == 0)
    def _():
        for i in range(count):
            tok_ref[i * block : (i + 1) * block] = piece_refs[i][...]
        pre_ref[...] = dot_nt(w_ref[...], tok_ref[...])
        write_codes(page, place_refs, high_ref, low_ref, sin_ref, cos_ref, codes_ref)
        kc_ref[:, :CODES] = codes_ref[...].astype(F32).T.astype(BF16)

    def pre(kind):
        at = kind * span + head * HEAD_DIM
        return pre_ref[pl.ds(pl.multiple_of(at, HEAD_DIM), HEAD_DIM)]

    rot_cos = rot_cos_ref[...]
    rot_sin = rot_sin_ref[...]
    query_pre = pre(0).astype(BF16)
    wide = query_pre.astype(F32)
    query = jnp.concatenate(turned(wide[:HALF], wide[HALF:], rot_cos, rot_sin), axis=0)
    key_pre = pre(1)
    key = jnp.concatenate(turned(key_pre[:HALF], key_pre[HALF:], rot_cos, rot_sin), axis=0)
    value = pre(2).astype(BF16)
    heads_ref[0, :HEAD_DIM] = query_pre
    heads_ref[0, HEAD_DIM : 2 * HEAD_DIM] = query.astype(BF16)
    heads_ref[0, 2 * HEAD_DIM : 3 * HEAD_DIM] = key.astype(BF16)
    heads_ref[0, 3 * HEAD_DIM :] = value
    kc_ref[:, CODES:] = key.T.astype(BF16)
    qr_ref[CODES:] = (query * 0.125).astype(BF16)
    step = min(256, block)

    def logits_at(at):
        part = slice(at, at + step)
        projected = dot_tn(box_ref[...], query_pre[:, part])
        sines = sin_ref[:, part]
        cosines = cos_ref[:, part]
        upper = projected[: 2 * FREQS]
        lower = projected[2 * FREQS :]
        qr_ref[: 2 * FREQS, part] = ((upper * cosines + lower * sines) * 0.125).astype(BF16)
        qr_ref[2 * FREQS : CODES, part] = ((lower * cosines - upper * sines) * 0.125).astype(BF16)
        return dot(kc_ref[...], qr_ref[:, part])

    following = logits_at(0)
    for at in range(0, rows, step):
        logits = following
        if at + step < rows:
            following = logits_at(at + step)
        peak = jnp.max(fold(logits, jnp.maximum), axis=0, keepdims=True)
        weight = jnp.exp(logits - peak)
        total = jnp.sum(fold(weight, jnp.add), axis=0, keepdims=True)
        probs = (weight * (1.0 / total)).astype(BF16)
        probs_ref[0, :, at : at + step] = probs
        attended = dot(value, probs)
        att_ref[0, :, at : at + step] = attended
        inner = at % block
        low_refs[at // block][:, inner : inner + step] = attended.astype(BF16)


def fixed(array):
    return pl.BlockSpec(array.shape, lambda *at: (0,) * len(array.shape))


def piece_specs(page, messages, gathered):
    block, width = gathered.shape[0] // len(messages), gathered.shape[1]
    if page == 0:
        return list(messages), [pl.BlockSpec((block, width), lambda h, words: (0, 0))] * len(
            messages
        )

    def spec(i):
        return pl.BlockSpec((block, width), lambda h, words: (words[0] ^ i, 0))

    return [gathered] * len(messages), [spec(i) for i in range(len(messages))]


def attention_forward(words, page, messages, gathered, w_own, box_own, rot_cos, rot_sin):
    count = len(messages)
    rows, width = gathered.shape
    block = rows // count
    span = box_own.shape[0]
    heads = span // HEAD_DIM
    tables = [jnp.asarray(item) for item in angle_tables()]
    pieces, specs = piece_specs(page, messages, gathered)
    places = pl.BlockSpec((16, width), lambda h, words: (block // 16, 0))
    out_shape = [
        jax.ShapeDtypeStruct((heads, rows, rows), BF16),
        jax.ShapeDtypeStruct((heads, HEAD_DIM, rows), F32),
        jax.ShapeDtypeStruct((heads, 4 * HEAD_DIM, rows), BF16),
        jax.ShapeDtypeStruct((2 * FREQS, rows), F32),
        jax.ShapeDtypeStruct((2 * FREQS, rows), F32),
        jax.ShapeDtypeStruct((CODES, rows), BF16),
    ] + [jax.ShapeDtypeStruct((span, block), BF16)] * count
    return pl.pallas_call(
        functools.partial(forward_kernel, page, count),
        grid_spec=pltpu.PrefetchScalarGridSpec(
            num_scalar_prefetch=1,
            grid=(heads,),
            in_specs=[places] * count
            + specs
            + [fixed(item) for item in (*tables, w_own)]
            + [
                pl.BlockSpec((HEAD_DIM, CODES), lambda h, words: (h, 0)),
                fixed(rot_cos),
                fixed(rot_sin),
            ],
            out_specs=[
                pl.BlockSpec((1, rows, rows), lambda h, words: (h, 0, 0)),
                pl.BlockSpec((1, HEAD_DIM, rows), lambda h, words: (h, 0, 0)),
                pl.BlockSpec((1, 4 * HEAD_DIM, rows), lambda h, words: (h, 0, 0)),
            ]
            + [fixed(item) for item in out_shape[3:6]]
            + [pl.BlockSpec((HEAD_DIM, block), lambda h, words: (h, 0))] * count,
            scratch_shapes=[
                pltpu.VMEM((rows, width), BF16),
                pltpu.VMEM((3 * span, rows), F32),
                pltpu.VMEM((rows, CODES + HEAD_DIM), BF16),
                pltpu.VMEM((CODES + HEAD_DIM, rows), BF16),
            ],
        ),
        out_shape=out_shape,
        compiler_params=pltpu.CompilerParams(vmem_limit_bytes=VMEM_LIMIT),
        cost_estimate=pl.CostEstimate(
            flops=2 * heads * rows * (rows * 1100 + 200 * width + 64 * CODES),
            bytes_accessed=2 * heads * rows * rows + 12 * rows * width,
            transcendentals=heads * rows * rows,
        ),
        name="attention_forward",
    )(words, *messages, *pieces, *tables, w_own, box_own, rot_cos, rot_sin)


def backward_kernel(count, last, words_ref, *refs):
    grad_refs, refs = refs[:count], refs[count:]
    piece_refs, refs = refs[:count], refs[count:]
    probs_ref, att_ref, heads_ref, box_ref, codes_ref, sin_ref, cos_ref = refs[:7]
    rot_cos_ref, rot_sin_ref = refs[7:9]
    refs = refs[9:]
    if last:
        before_ref, refs = refs[0], refs[1:]
    pre_refs, refs = refs[:count], refs[count:]
    if last:
        mine_ref, theirs_ref, *refs = refs
    weight_grad_ref, kc_ref, logit_grad_ref, entry_grad_ref, turned_ref = refs
    block, width = piece_refs[0].shape
    rows = count * block
    head = pl.program_id(0)
    span = pl.num_programs(0) * HEAD_DIM

    @pl.when(head == 0)
    def _():
        kc_ref[:CODES] = codes_ref[...]

    kc_ref[CODES:] = heads_ref[0, 2 * HEAD_DIM : 3 * HEAD_DIM]
    packed = heads_ref[0].astype(F32).T.astype(BF16)
    query_pre = packed[:, :HEAD_DIM]
    query = packed[:, HEAD_DIM : 2 * HEAD_DIM]
    value = packed[:, 3 * HEAD_DIM :] * jnp.asarray(0.125, BF16)
    rot_cos = rot_cos_ref[...]
    rot_sin = rot_sin_ref[...]
    grad = jnp.concatenate([ref[...] for ref in grad_refs], axis=1)
    grad_tall = grad.astype(F32).T.astype(BF16)
    offsets = jnp.sum(grad.astype(F32) * att_ref[0], axis=0, keepdims=True) * 0.125
    step = min(256, block)
    place = pl.multiple_of(head * HEAD_DIM, HEAD_DIM)
    here = pl.ds(place, HEAD_DIM)

    def logits_back(at):
        part = slice(at, at + step)
        grad_probs = dot(value, grad[:, part])
        logit_grad_ref[:, part] = (
            probs_ref[0, :, part].astype(F32) * (grad_probs - offsets[:, part])
        ).astype(BF16)

    logits_back(0)
    for at in range(0, rows, step):
        if at + step < rows:
            logits_back(at + step)
        part = slice(at, at + step)
        back = dot(kc_ref[...], logit_grad_ref[:, part])
        sines = sin_ref[:, part]
        cosines = cos_ref[:, part]
        upper = back[: 2 * FREQS]
        lower = back[2 * FREQS : CODES]
        entry_grad_ref[: 2 * FREQS, part] = (upper * cosines - lower * sines).astype(BF16)
        entry_grad_ref[2 * FREQS :, part] = (lower * cosines + upper * sines).astype(BF16)
        first = back[CODES : CODES + HALF]
        second = back[CODES + HALF :]
        turned_ref[:HALF, part], turned_ref[HALF:, part] = turned(
            first, second, rot_cos[:, part], -rot_sin[:, part]
        )
    key_flat = dot(logit_grad_ref[...], query).T
    value_low = dot(probs_ref[0], grad_tall).T.astype(BF16)
    query_low = (turned_ref[...] + dot(box_ref[...], entry_grad_ref[...])).astype(BF16)
    key_low = jnp.concatenate(
        turned(key_flat[:HALF], key_flat[HALF:], rot_cos, -rot_sin), axis=0
    ).astype(BF16)
    for i in range(count):
        columns = slice(i * block, (i + 1) * block)
        pre_refs[i][here, :block] = query_low[:, columns]
        pre_refs[i][here, block : 2 * block] = key_low[:, columns]
        pre_refs[i][here, 2 * block :] = value_low[:, columns]
    weight_grad_ref[pl.ds(3 * span + place, HEAD_DIM)] = dot(entry_grad_ref[...], query_pre).T

    @pl.when(head == pl.num_programs(0) - 1)
    def _():
        for kind in range(3):
            columns = slice(kind * block, (kind + 1) * block)
            total = dot(pre_refs[0][:, columns], piece_refs[0][...])
            for i in range(1, count):
                total = total + dot(pre_refs[i][:, columns], piece_refs[i][...])
            weight_grad_ref[kind * span : (kind + 1) * span] = total
        if last:
            half = 2 * span
            core = words_ref[2]
            ours = pl.ds(pl.multiple_of(core * half, half), half)
            there = pl.ds(pl.multiple_of((1 - core) * half, half), half)
            mine_ref[...] = weight_grad_ref[ours] + before_ref[ours]
            theirs_ref[...] = (weight_grad_ref[there] + before_ref[there]).astype(BF16)


def attention_backward(
    words, page, grads, messages, gathered, saved, box_own, rot_cos, rot_sin, before=None
):
    probs, att, heads_saved, sines, cosines, codes = saved
    count = len(messages)
    rows, width = gathered.shape
    block = rows // count
    span = box_own.shape[0]
    heads = span // HEAD_DIM
    last = before is not None
    extra = (before,) if last else ()
    full_shape = (4 * span, width)
    pieces, specs = piece_specs(page, messages, gathered)
    out_shape = [jax.ShapeDtypeStruct((span, 3 * block), BF16)] * count
    if last:
        out_shape += [
            jax.ShapeDtypeStruct((2 * span, width), F32),
            jax.ShapeDtypeStruct((2 * span, width), BF16),
        ]
    else:
        out_shape.append(jax.ShapeDtypeStruct(full_shape, F32))
    return pl.pallas_call(
        functools.partial(backward_kernel, count, last),
        grid_spec=pltpu.PrefetchScalarGridSpec(
            num_scalar_prefetch=1,
            grid=(heads,),
            in_specs=[pl.BlockSpec((HEAD_DIM, block), lambda h, words: (h, page))] * count
            + specs
            + [
                pl.BlockSpec((1, rows, rows), lambda h, words: (h, 0, 0)),
                pl.BlockSpec((1, HEAD_DIM, rows), lambda h, words: (h, 0, 0)),
                pl.BlockSpec((1, 4 * HEAD_DIM, rows), lambda h, words: (h, 0, 0)),
                pl.BlockSpec((HEAD_DIM, CODES), lambda h, words: (h, 0)),
            ]
            + [fixed(item) for item in (codes, sines, cosines, rot_cos, rot_sin, *extra)],
            out_specs=[fixed(item) for item in out_shape],
            scratch_shapes=([pltpu.VMEM(full_shape, F32)] if last else [])
            + [
                pltpu.VMEM((CODES + HEAD_DIM, rows), BF16),
                pltpu.VMEM((rows, rows), BF16),
                pltpu.VMEM((CODES, rows), BF16),
                pltpu.VMEM((HEAD_DIM, rows), F32),
            ],
        ),
        out_shape=out_shape,
        compiler_params=pltpu.CompilerParams(vmem_limit_bytes=VMEM_LIMIT),
        cost_estimate=pl.CostEstimate(
            flops=2 * heads * rows * (rows * 1400 + 200 * width + 128 * CODES),
            bytes_accessed=2 * heads * rows * rows + 12 * rows * width,
            transcendentals=0,
        ),
        name="attention_backward",
    )(
        words,
        *grads,
        *pieces,
        probs,
        att,
        heads_saved,
        box_own,
        codes,
        sines,
        cosines,
        rot_cos,
        rot_sin,
        *extra,
    )


def normed(value):
    centered = value - jnp.mean(value, axis=-1, keepdims=True)
    scale = lax.rsqrt(jnp.mean(centered * centered, axis=-1, keepdims=True) + 1e-05)
    return centered * scale, scale


def norm_back(grad, gain, unit, scale):
    scaled = grad * gain
    return scale * (
        scaled
        - jnp.mean(scaled, axis=-1, keepdims=True)
        - unit * jnp.mean(scaled * unit, axis=-1, keepdims=True)
    )


def column_sum(value):
    return jnp.sum(value, axis=0, keepdims=True)


def middle_kernel(pages, count, span, chunks, *refs):
    total = pages * count
    words_ref = refs[0]
    att_refs = refs[1 : 1 + total]
    (
        tok_ref,
        cot_ref,
        w_out_ref,
        vectors_ref,
        w_expand_ref,
        w_reduce_ref,
    ) = refs[1 + total : 7 + total]
    outs = refs[7 + total :]
    layer_ref, first_in_ref, theirs_ref, mine_ref, more_theirs_ref, more_mine_ref = outs[:6]
    grad_refs = outs[6 : 6 + count]
    (
        sums_ref,
        att_all,
        grad_all,
        unit_one,
        scale_one,
        first_wide,
        first_low,
        first_tall,
        active,
        slope,
        gathered,
        second_in,
        second_low,
    ) = outs[6 + count :]
    rank = words_ref[0]
    width = tok_ref.shape[1]
    block = tok_ref.shape[0] // pages
    step = pl.program_id(0)

    def rows_of(at):
        return pl.ds(pl.multiple_of((rank ^ at) * span, span), span)

    @pl.when(step == 0)
    def _():
        for page in range(pages):
            for at in range(count):
                att_all[rows_of(at), page * block : (page + 1) * block] = att_refs[
                    page * count + at
                ][...]
        branch = dot_tn(att_all[: w_out_ref.shape[0]], w_out_ref[...])
        unit, scale = normed(tok_ref[...].astype(F32) + branch)
        unit_one[...] = unit
        scale_one[...] = jnp.broadcast_to(scale, scale_one.shape)
        first_out = unit * vectors_ref[0:1] + vectors_ref[1:2]
        first_wide[...] = first_out
        first_low[...] = first_out.astype(BF16)
        first_tall[...] = first_out.T.astype(BF16)
        gathered[...] = jnp.zeros_like(gathered)
        sums_ref[...] = jnp.zeros_like(sums_ref)

    for chunk in range(chunks):

        @pl.when(step == chunk)
        def _(chunk=chunk):
            expanded = dot(first_low[...], w_expand_ref[...])
            gate = 0.5 + 0.5 * lax.erf(expanded * np.float32(np.sqrt(0.5)))
            bell = jnp.exp(expanded * expanded * -0.5) * np.float32(1.0 / np.sqrt(2.0 * np.pi))
            low = (expanded * gate).astype(BF16)
            active[chunk] = low
            slope[chunk] = gate + expanded * bell
            gathered[...] += dot(low, w_reduce_ref[...])

    @pl.when(step == chunks - 1)
    def _():
        unit, scale = normed(first_wide[...] + gathered[...])
        layer_ref[...] = (unit * vectors_ref[2:3] + vectors_ref[3:4]).astype(BF16)
        cot = cot_ref[...].astype(F32)
        sums_ref[2:3] = column_sum(cot * unit)
        sums_ref[3:4] = column_sum(cot)
        grad = norm_back(cot, vectors_ref[2:3], unit, scale)
        second_in[...] = grad
        second_low[...] = grad.astype(BF16)
        gathered[...] = grad

    for chunk in range(chunks):

        @pl.when(step == 2 * chunks - 1 - chunk)
        def _(chunk=chunk):
            grad_active = dot_nt(second_low[...], w_reduce_ref[...])
            grad_expanded = (grad_active * slope[chunk]).astype(BF16)
            grads_ref = mine_ref if chunk < chunks // 2 else theirs_ref
            grads_ref[:width] = dot(first_tall[...], grad_expanded).astype(BF16)
            grads_ref[width:] = dot_tn(active[chunk], second_low[...]).astype(BF16)
            gathered[...] += dot_nt(grad_expanded, w_expand_ref[...])

    @pl.when(step == 2 * chunks - 1)
    def _():
        unit = unit_one[...]
        grad_out = gathered[...]
        sums_ref[0:1] = column_sum(grad_out * unit)
        sums_ref[1:2] = column_sum(grad_out)
        grad = norm_back(grad_out, vectors_ref[0:1], unit, scale_one[:, :1])
        first_in_ref[...] = grad
        low = grad.astype(BF16)
        real = w_out_ref.shape[0]
        half = real // 2
        core = words_ref[2]
        for ref, side in ((more_mine_ref, core), (more_theirs_ref, 1 - core)):
            rows = pl.ds(pl.multiple_of(side * half, half), half)
            ref[:half] = dot(att_all[rows], low).astype(BF16)
            ref[half:] = jnp.zeros((ref.shape[0] - half, width), BF16)
            ref[half : half + 16] = sums_ref[...].astype(BF16)
        if grad_all.shape[0] > real:
            grad_all[real:] = jnp.zeros((grad_all.shape[0] - real, low.shape[0]), BF16)
        grad_all[:real] = dot_nt(w_out_ref[...], low).astype(BF16)
        for at in range(count):
            grad_refs[at][...] = grad_all[rows_of(at)]


def middle(words, att_parts, tok, cot, w_out, vectors, w_expand, w_reduce, pages, more):
    rows, width = tok.shape
    count = len(att_parts) // pages
    span, block = att_parts[0].shape
    hidden = w_expand.shape[1]
    chunks = hidden // width
    pairs = chunks // 2

    def whole(array):
        return pl.BlockSpec(array.shape, lambda s, words: (0,) * len(array.shape))

    def chunk_at(s, words):
        at = jnp.minimum(s, 2 * chunks - 1 - s)
        return (at + words[2] * pairs) % chunks

    def theirs_at(s, words):
        return jnp.clip(2 * chunks - 1 - s - pairs, 0, pairs - 1), 0

    def mine_at(s, words):
        return jnp.clip(2 * chunks - 1 - s, 0, pairs - 1), 0

    shapes = [
        jax.ShapeDtypeStruct((rows, width), BF16),
        jax.ShapeDtypeStruct((rows, width), F32),
        jax.ShapeDtypeStruct((hidden, width), BF16),
        jax.ShapeDtypeStruct((hidden, width), BF16),
        jax.ShapeDtypeStruct((more, width), BF16),
        jax.ShapeDtypeStruct((more, width), BF16),
    ] + [jax.ShapeDtypeStruct((span, pages * block), BF16)] * count
    specs = [whole(item) for item in shapes]
    specs[2] = pl.BlockSpec((2 * width, width), theirs_at)
    specs[3] = pl.BlockSpec((2 * width, width), mine_at)
    return pl.pallas_call(
        functools.partial(middle_kernel, pages, count, span, chunks),
        grid_spec=pltpu.PrefetchScalarGridSpec(
            num_scalar_prefetch=1,
            grid=(2 * chunks,),
            in_specs=[whole(item) for item in att_parts]
            + [
                whole(tok),
                whole(cot),
                whole(w_out),
                whole(vectors),
                pl.BlockSpec((width, width), lambda s, words: (0, chunk_at(s, words))),
                pl.BlockSpec((width, width), lambda s, words: (chunk_at(s, words), 0)),
            ],
            out_specs=specs,
            scratch_shapes=[
                pltpu.VMEM((16, width), F32),
                pltpu.VMEM((count * span, rows), BF16),
                pltpu.VMEM((count * span, rows), BF16),
                pltpu.VMEM((rows, width), F32),
                pltpu.VMEM((rows, 128), F32),
                pltpu.VMEM((rows, width), F32),
                pltpu.VMEM((rows, width), BF16),
                pltpu.VMEM((width, rows), BF16),
                pltpu.VMEM((chunks, rows, width), BF16),
                pltpu.VMEM((chunks, rows, width), F32),
                pltpu.VMEM((rows, width), F32),
                pltpu.VMEM((rows, width), F32),
                pltpu.VMEM((rows, width), BF16),
            ],
        ),
        out_shape=shapes,
        compiler_params=pltpu.CompilerParams(vmem_limit_bytes=VMEM_LIMIT),
        cost_estimate=pl.CostEstimate(
            flops=2 * rows * width * (6 * hidden + 3 * width),
            bytes_accessed=8 * width * hidden + 16 * rows * width,
            transcendentals=2 * rows * hidden,
        ),
        name="middle",
    )(words, *att_parts, tok, cot, w_out, vectors, w_expand, w_reduce)


def input_kernel(pages, count, span, bases, *refs):
    total = pages * count
    words_ref = refs[0]
    part_refs = refs[1 : 1 + total]
    weight_refs = refs[1 + total : 4 + total]
    first_in_ref, out_ref, held = refs[4 + total :]
    rank = words_ref[0]
    width = out_ref.shape[1]
    block = out_ref.shape[0] // pages
    for page in range(pages):
        for at in range(count):
            base = bases[page] if at else 0
            part = part_refs[page * count + at]
            place = pl.multiple_of((rank ^ at) * span, span)
            for kind in range(3):
                held[kind, pl.ds(place, span), page * block : (page + 1) * block] = part[
                    base : base + span, kind * block : (kind + 1) * block
                ]
    total = dot(weight_refs[0][...], held[0, :width])
    for kind in range(1, 3):
        total = total + dot(weight_refs[kind][...], held[kind, :width])
    out_ref[...] = (first_in_ref[...] + total.T).astype(BF16)


def input_gradient(words, parts, bases, span, weights, first_in, pages):
    count = len(parts) // pages
    rows, width = first_in.shape
    vmem = pl.BlockSpec(memory_space=pltpu.VMEM)
    return pl.pallas_call(
        functools.partial(input_kernel, pages, count, span, bases),
        in_specs=[pl.BlockSpec(memory_space=pltpu.SMEM)] + [vmem] * (len(parts) + 4),
        out_specs=vmem,
        out_shape=jax.ShapeDtypeStruct((rows, width), BF16),
        scratch_shapes=[pltpu.VMEM((3, count * span, rows), BF16)],
        compiler_params=pltpu.CompilerParams(vmem_limit_bytes=VMEM_LIMIT),
        cost_estimate=pl.CostEstimate(
            flops=6 * rows * width * count * span,
            bytes_accessed=2 * width * (5 * rows + 3 * count * span),
            transcendentals=0,
        ),
        name="input_gradient",
    )(words, *parts, *weights, first_in)


def local(body, name, words, arrays, shapes):
    def kernel(words_ref, *refs):
        body(words_ref, refs[: len(arrays)], refs[len(arrays) :])

    vmem = pl.BlockSpec(memory_space=pltpu.VMEM)
    shapes = [jax.ShapeDtypeStruct(shape, kind) for shape, kind in shapes]
    moved = sum(item.size * item.dtype.itemsize for item in list(arrays) + shapes)
    return pl.pallas_call(
        kernel,
        in_specs=[pl.BlockSpec(memory_space=pltpu.SMEM)] + [vmem] * len(arrays),
        out_specs=[vmem] * len(shapes),
        out_shape=shapes,
        compiler_params=pltpu.CompilerParams(vmem_limit_bytes=VMEM_LIMIT),
        cost_estimate=pl.CostEstimate(flops=moved, bytes_accessed=moved, transcendentals=0),
        name=name,
    )(words, *arrays)


def shard(index, rows, base=0):
    return pl.ds(pl.multiple_of(base + index * rows, 16), rows)


def total_of(refs, rows=slice(None)):
    total = refs[0][rows].astype(F32)
    for ref in refs[1:]:
        total = total + ref[rows].astype(F32)
    return total


def tree_sum(terms):
    while len(terms) > 1:
        terms = [terms[i] + terms[i + 1] for i in range(0, len(terms), 2)]
    return terms[0]


class Plan:
    def __init__(self, rows, rows_a, more, span, width):
        self.count = lax.axis_size("blk")
        self.rows = rows
        self.rows_a = rows_a
        self.more = more
        self.span = span
        self.width = width
        self.a_ff = rows_a // self.count
        self.a_more = more // self.count
        self.a = self.a_ff + self.a_more
        self.b = (rows - rows_a) // lax.axis_size("depth")

    def shapes(self, *sizes):
        return [((rows, self.width), BF16) for rows in sizes]

    def scatter_one(self, words, halves):
        count, width = self.count, self.width
        a_ff, a_more = self.a_ff, self.a_more
        b_rows = (self.rows - self.rows_a) // count

        def kernel(words_ref, *refs):
            parts = refs[6 : 6 + count]
            for i in range(count):

                @pl.when(pl.program_id(0) == i)
                def _(i=i):
                    parts[i][:a_ff] = total_of(refs[:2]).astype(BF16)
                    parts[i][a_ff:] = total_of(refs[2:4]).astype(BF16)

            refs[6 + count][...] = total_of(refs[4:6]).astype(BF16)

        def there(rows):
            return pl.BlockSpec((rows, width), lambda i, words: (words[0] ^ i, 0))

        own_b = pl.BlockSpec((b_rows, width), lambda i, words: (self.rows_a // b_rows + i, 0))
        shapes = [jax.ShapeDtypeStruct((self.a, width), BF16)] * count
        shapes.append(jax.ShapeDtypeStruct((self.rows - self.rows_a, width), BF16))
        *parts_a, part_b = pl.pallas_call(
            kernel,
            grid_spec=pltpu.PrefetchScalarGridSpec(
                num_scalar_prefetch=1,
                grid=(count,),
                in_specs=[there(a_ff)] * 2 + [there(a_more)] * 2 + [own_b] * 2,
                out_specs=[fixed(item) for item in shapes[:count]]
                + [pl.BlockSpec((b_rows, width), lambda i, words: (i, 0))],
            ),
            out_shape=shapes,
            compiler_params=pltpu.CompilerParams(vmem_limit_bytes=VMEM_LIMIT),
            cost_estimate=pl.CostEstimate(
                flops=0, bytes_accessed=6 * self.rows * width, transcendentals=0
            ),
            name="scatter_one",
        )(words, *halves, *halves[:2])
        return [from_blk(part, i) for i, part in enumerate(parts_a)], part_b

    def scatter_two(self, words, parts_a, part_b, pieces):
        def body(words, ins, outs):
            outs[0][...] = total_of(ins[: self.count]).astype(BF16)
            for out, piece in zip(outs[1:], ins[self.count + 1 :]):
                out[: self.b] = ins[self.count][...]
                out[self.b :, : piece.shape[1]] = piece[...]

        shapes = self.shapes(self.a, *[self.b + self.span] * (self.count - 1))
        part_a, *messages = local(
            body, "scatter_two", words, [*parts_a, part_b, *pieces[1:]], shapes
        )
        return part_a, [from_blk(item, i + 1) for i, item in enumerate(messages)]

    def gather_a(self, words, part_a, pieces):
        def body(words, ins, outs):
            for out, piece in zip(outs, ins[1:]):
                out[: self.a] = ins[0][...]
                out[self.a :, : piece.shape[1]] = piece[...]

        shapes = self.shapes(*[self.a + self.span] * (self.count - 1))
        messages = local(body, "gather_a", words, [part_a, *pieces[1:]], shapes)
        return [from_blk(item, i + 1) for i, item in enumerate(messages)]

    def sum_b(self, words, part_b, messages):
        def body(words, ins, outs):
            terms = [ref[: self.b].astype(F32) for ref in ins]
            outs[0][...] = tree_sum(terms).astype(BF16)

        return local(body, "sum_b", words, [part_b, *messages], self.shapes(self.b))[0]

    def gather_b(self, words, part_b):
        depth = lax.axis_size("depth")
        distance = depth // 2
        held = part_b
        while distance:
            other = swapped(held, distance, "depth")
            distance //= 2
            if distance:

                def body(words, ins, outs):
                    rows = ins[0].shape[0]
                    outs[0][:rows] = ins[0][...]
                    outs[0][rows:] = ins[1][...]

                shapes = self.shapes(2 * held.shape[0])
                held = local(body, "gather_b", words, [held, other], shapes)[0]
        return held, other

    def join(self, words, part_a, messages, parts_b):
        depth = lax.axis_size("depth")
        order = [0]
        distance = depth // 2
        while distance:
            order = order + [item ^ distance for item in order]
            distance //= 2

        def body(words, ins, outs):
            for i in range(self.count):
                outs[0][shard(words[0] ^ i, self.a_ff)] = ins[i][: self.a_ff]
                outs[1][shard(words[0] ^ i, self.a_more)] = ins[i][self.a_ff : self.a]
            for at, k in enumerate(order):
                ref = ins[self.count + at // (depth // 2)]
                base = at % (depth // 2) * self.b
                rows = shard(words[1] ^ k, self.b, self.rows_a)
                outs[0][rows] = ref[base : base + self.b]

        shapes = self.shapes(self.rows, self.more)
        return local(body, "join", words, [part_a, *messages, *parts_b], shapes)


def widened(words, half, side, hidden, before=()):
    width = half.shape[1]
    chunks = hidden // width
    pairs = chunks // 2

    def kernel(words_ref, half_ref, *refs):
        expand_ref, reduce_ref = refs[len(before) :]
        expand_ref[...] = half_ref[:width].astype(F32)
        reduce_ref[...] = half_ref[width:].astype(F32)

    def place(s, words):
        return (s + (words[2] + side) * pairs) % chunks

    return pl.pallas_call(
        kernel,
        grid_spec=pltpu.PrefetchScalarGridSpec(
            num_scalar_prefetch=1,
            grid=(pairs,),
            in_specs=[pl.BlockSpec((2 * width, width), lambda s, words: (s, 0))]
            + [pl.BlockSpec(memory_space=pl.ANY)] * len(before),
            out_specs=[
                pl.BlockSpec((width, width), lambda s, words: (0, place(s, words))),
                pl.BlockSpec((width, width), lambda s, words: (place(s, words), 0)),
            ],
        ),
        out_shape=[
            jax.ShapeDtypeStruct((width, hidden), F32),
            jax.ShapeDtypeStruct((hidden, width), F32),
        ],
        input_output_aliases={2: 0, 3: 1} if before else {},
        compiler_params=pltpu.CompilerParams(vmem_limit_bytes=VMEM_LIMIT),
        cost_estimate=pl.CostEstimate(
            flops=0, bytes_accessed=6 * hidden * width, transcendentals=0
        ),
        name="widen",
    )(words, half, *before)


def core_sum(words, mine, other):
    def body(words, ins, outs):
        outs[0][...] = total_of(ins).astype(BF16)

    return local(body, "heads_sum", words, [mine, other], [(mine.shape, BF16)])[0]


def join_blk(words, own):
    count = lax.axis_size("blk")
    half, width = own.shape
    parts = [from_blk(own, i) for i in range(count)]

    def body(words, ins, outs):
        for i in range(count):
            outs[0][shard(words[0] ^ i, half)] = ins[i][...]

    return local(body, "heads_join", words, parts, [((count * half, width), BF16)])[0]


def finish_kernel(count, span, half, words_ref, *refs):
    own_ref, other_ref, more_ref, more_other_ref = refs[:4]
    query_ref, key_ref, value_ref, project_ref, box_ref, sums_ref = refs[4:]
    width = query_ref.shape[0]

    def write(lower_ref, upper_ref, more_lower_ref, more_upper_ref):
        def grad(ref, part):
            rows = [
                ref[(2 * i + part) * span : (2 * i + part + 1) * span].astype(F32)
                for i in range(count)
            ]
            return jnp.concatenate(rows, axis=0)[:width].T

        query_ref[...] = grad(lower_ref, 0)
        key_ref[...] = grad(lower_ref, 1)
        value_ref[...] = grad(upper_ref, 0)
        box_ref[...] = entry_order(grad(upper_ref, 1))
        project_ref[:half] = more_lower_ref[:half].astype(F32)
        project_ref[half:] = more_upper_ref[:half].astype(F32)
        sums_ref[...] = more_lower_ref[half : half + 16].astype(F32)[:8]

    @pl.when(words_ref[2] == 0)
    def _():
        write(own_ref, other_ref, more_ref, more_other_ref)

    @pl.when(words_ref[2] == 1)
    def _():
        write(other_ref, own_ref, more_other_ref, more_ref)


def finished(words, own, other, more, more_other, span, width):
    count = lax.axis_size("blk")
    vmem = pl.BlockSpec(memory_space=pltpu.VMEM)
    shapes = [jax.ShapeDtypeStruct((width, width), F32)] * 5
    shapes.append(jax.ShapeDtypeStruct((8, width), F32))
    return pl.pallas_call(
        functools.partial(finish_kernel, count, span, width // 2),
        in_specs=[pl.BlockSpec(memory_space=pltpu.SMEM)] + [vmem] * 4,
        out_specs=[vmem] * 6,
        out_shape=shapes,
        compiler_params=pltpu.CompilerParams(vmem_limit_bytes=VMEM_LIMIT),
        cost_estimate=pl.CostEstimate(
            flops=0, bytes_accessed=32 * width * width, transcendentals=0
        ),
        name="finish",
    )(words, own, other, more, more_other)


def per_device(
    tokens,
    boxes,
    w_query,
    w_key,
    w_value,
    w_output,
    box_weight,
    first_gain,
    first_shift,
    w_expand,
    w_reduce,
    second_gain,
    second_shift,
    cotangent,
):
    pages, block, width = tokens.shape
    count = lax.axis_size("blk")
    depth = lax.axis_size("depth")
    words = jnp.stack(
        [lax.axis_index("blk"), lax.axis_index("depth"), lax.axis_index("core")]
    ).astype(jnp.int32)
    hidden = w_expand.shape[1]
    span = -(-HEADS // count) * HEAD_DIM
    unit = 16 * count * depth
    more = -(-(width // 2 + 16) // unit) * unit

    own_places = jnp.stack([boxes[0] + boxes[2], boxes[1] + boxes[3]], axis=1)
    own_places = jnp.stack([lax.shift_right_logical(own_places, 6), own_places & 63], axis=2)
    own_places = own_places.reshape(4 * pages, block).astype(BF16)
    own_places = jnp.pad(own_places, ((0, 16 - 4 * pages), (0, width - block)))
    message = jnp.concatenate([tokens[0], own_places])
    messages = [from_blk(message, i) for i in range(count)]
    w_own, box_own, rot_cos, rot_sin = prepare(
        words, w_query, w_key, w_value, box_weight, span, count * block
    )
    messages, rot_cos = lax.optimization_barrier((messages, rot_cos))
    gathered = lax.all_gather(after(messages, tokens[1]), "blk", axis=0, tiled=True)

    saved = []
    att_parts = []
    for page in range(pages):
        source = gathered if page else message
        if page == 0:
            source = jax.ShapeDtypeStruct((count * block, width), BF16)
        results = attention_forward(
            words, page, messages, source, w_own, box_own, rot_cos, rot_sin
        )
        saved.append(results[:6])
        att_parts += [from_blk(results[6 + i], i) for i in range(count)]

    vectors = jnp.stack([first_gain, first_shift, second_gain, second_shift])
    results = middle(
        words,
        att_parts,
        tokens.reshape(pages * block, width),
        cotangent.reshape(pages * block, width),
        w_output,
        vectors,
        w_expand,
        w_reduce,
        pages,
        more,
    )
    layer_out, first_in, theirs, mine, more_theirs, more_mine = results[:6]
    grads = [from_blk(results[6 + i], i) for i in range(count)]
    plan = Plan(hidden, 2 * hidden // 3, more, span, width)
    parts_a, part_b = plan.scatter_one(
        after(grads, words), [mine, from_core(theirs), more_mine, from_core(more_theirs)]
    )
    part_b = lax.psum_scatter(part_b, "depth", scatter_dimension=0, tiled=True)

    def backward(page, words, before=None):
        return attention_backward(
            words,
            page,
            grads,
            messages,
            gathered,
            saved[page],
            box_own,
            rot_cos,
            rot_sin,
            before,
        )

    *pre_one, before = backward(0, after(parts_a[0], words))
    part_a, messages_b = plan.scatter_two(after(before, words), parts_a, part_b, pre_one)
    before = after(part_a, before)
    part_a = lax.psum(part_a, "depth")
    *pre_two, heads_mine, heads_theirs = backward(1, words, before)

    part_b = plan.sum_b(after(heads_mine, words), part_b, messages_b)
    heads_own = core_sum(after(part_b, words), heads_mine, from_core(heads_theirs))
    heads_sum = lax.psum(after(part_a, heads_own), "depth")
    parts_b = plan.gather_b(after(heads_own, words), part_b)
    messages_a = plan.gather_a(after(heads_own, words), part_a, pre_two)
    input_grad = input_gradient(
        after(messages_a, words),
        [pre_one[0], *messages_b, pre_two[0], *messages_a],
        (plan.b, plan.a),
        span,
        (w_query, w_key, w_value),
        first_in,
        pages,
    )
    ff, extra = plan.join(words, part_a, messages_a, parts_b)
    ff_other, extra_other = from_core(ff), from_core(extra)
    wide = widened(words, ff, 0, hidden)
    heads_own = join_blk(after(wide[0], words), heads_sum)
    heads_other = from_core(heads_own)
    grad_expand, grad_reduce = widened(after(heads_own, words), ff_other, 1, hidden, wide)
    grad_query, grad_key, grad_value, grad_project, grad_box, sums = finished(
        words, heads_own, heads_other, extra, extra_other, span, width
    )
    return (
        layer_out.reshape(tokens.shape),
        input_grad.reshape(tokens.shape),
        grad_query,
        grad_key,
        grad_value,
        grad_project,
        grad_box,
        sums[0],
        sums[1],
        grad_expand,
        grad_reduce,
        sums[2],
        sums[3],
    )


def solution(mesh):
    blocks, rest = mesh.devices.shape
    parts = jax.sharding.Mesh(
        mesh.devices.reshape(blocks, rest // 2, 2), ("blk", "depth", "core")
    )
    split = P(("depth", "core"), "blk", None)
    return jax.shard_map(
        per_device,
        mesh=parts,
        in_specs=(split, P(None, ("depth", "core"), "blk")) + (P(),) * 11 + (split,),
        out_specs=(split, split) + (P(),) * 11,
        check_vma=False,
    )
```

```python
import functools

import jax
import jax.numpy as jnp
import numpy as np
from jax import lax
from jax.experimental import pallas as pl
from jax.experimental.pallas import tpu as pltpu
from jax.sharding import PartitionSpec as P

HEADS = 12
HEAD_DIM = 64
HALF = 32
FREQS = 192
CODES = 4 * FREQS
VMEM_LIMIT = 60 * 1024 * 1024
NO_COST = pl.CostEstimate(flops=0, bytes_accessed=0, transcendentals=0)
F32 = jnp.float32
BF16 = jnp.bfloat16


def dot(left, right):
    return lax.dot_general(left, right, (((1,), (0,)), ((), ())), preferred_element_type=F32)


def dot_nt(left, right):
    return lax.dot_general(left, right, (((1,), (1,)), ((), ())), preferred_element_type=F32)


def dot_tn(left, right):
    return lax.dot_general(left, right, (((0,), (0,)), ((), ())), preferred_element_type=F32)


def swapped(block, distance, axis="blk"):
    count = lax.axis_size(axis)
    return lax.ppermute(block, axis, [(i, i ^ distance) for i in range(count)])


def from_blk(block, distance):
    return swapped(block, distance) if distance else block


def from_core(block):
    return swapped(block, 1, "core")


def after(done, value):
    return lax.optimization_barrier((value, done))[0]


def turned(upper, lower, cosines, sines):
    return upper * cosines - lower * sines, lower * cosines + upper * sines


def entry_order(rows):
    return jnp.concatenate(
        [
            rows[:FREQS],
            rows[2 * FREQS : 3 * FREQS],
            rows[FREQS : 2 * FREQS],
            rows[3 * FREQS :],
        ],
        axis=0,
    )


def angle_tables():
    rates = np.float32(10000.0) ** (-np.arange(FREQS, dtype=np.float32) / np.float32(FREQS))
    tables = []
    for places in (32.0 * np.arange(32), 0.5 * np.arange(64)):
        angles = rates.astype(np.float64)[:, None] * places[None, :]
        left = np.concatenate([np.sin(angles), np.cos(angles)])
        parts = []
        for _ in range(3):
            parts.append(left.astype(jnp.bfloat16))
            left = left - parts[-1].astype(np.float64)
        tables.append(np.concatenate(parts, axis=1))
    return tables


def rotary_tables(length):
    rates = np.float32(10000.0) ** (-np.arange(HALF, dtype=np.float32) / np.float32(HALF))
    angles = np.arange(length, dtype=np.float32)[None, :] * rates[:, None]
    angles = angles.astype(np.float64)
    return np.cos(angles).astype(np.float32), np.sin(angles).astype(np.float32)


def prepare_kernel(
    words_ref,
    query_ref,
    key_ref,
    value_ref,
    box_ref,
    cos_ref,
    sin_ref,
    own_ref,
    own_box_ref,
    own_cos_ref,
    own_sin_ref,
):
    rank = words_ref[0]
    span = own_box_ref.shape[0]
    width = query_ref.shape[1]
    count = lax.axis_size("blk")
    block = cos_ref.shape[1] // count
    row = lax.broadcasted_iota(jnp.int32, (span, width), 0) + rank * span
    column = lax.broadcasted_iota(jnp.int32, (span, width), 1)
    pick = jnp.where(row == column, 1.0, 0.0).astype(BF16)
    for kind, ref in enumerate((query_ref, key_ref, value_ref)):
        own_ref[kind * span : (kind + 1) * span] = dot_nt(pick, ref[...]).astype(BF16)
    own_box_ref[...] = dot_nt(pick, entry_order(box_ref[...])).astype(BF16)
    for i in range(count):
        from_cols = pl.ds(pl.multiple_of((rank ^ i) * block, block), block)
        own_cos_ref[:, i * block : (i + 1) * block] = cos_ref[:, from_cols]
        own_sin_ref[:, i * block : (i + 1) * block] = sin_ref[:, from_cols]


def prepare(words, w_query, w_key, w_value, box_weight, span, length):
    width = w_query.shape[0]
    vmem = pl.BlockSpec(memory_space=pltpu.VMEM)
    return pl.pallas_call(
        prepare_kernel,
        in_specs=[pl.BlockSpec(memory_space=pltpu.SMEM)] + [vmem] * 6,
        out_specs=[vmem] * 4,
        out_shape=[
            jax.ShapeDtypeStruct((3 * span, width), BF16),
            jax.ShapeDtypeStruct((span, CODES), BF16),
            jax.ShapeDtypeStruct((HALF, length), F32),
            jax.ShapeDtypeStruct((HALF, length), F32),
        ],
        compiler_params=pltpu.CompilerParams(vmem_limit_bytes=VMEM_LIMIT),
        cost_estimate=pl.CostEstimate(
            flops=8 * span * width * width, bytes_accessed=10 * width * width, transcendentals=0
        ),
        name="prepare",
    )(words, w_query, w_key, w_value, box_weight, *map(jnp.asarray, rotary_tables(length)))


def fold(value, combine):
    while value.shape[0] > 8:
        half = value.shape[0] // 2
        value = combine(value[:half], value[half:])
    return value


def write_codes(page, place_refs, high_ref, low_ref, sin_ref, cos_ref, codes_ref):
    block = sin_ref.shape[1] // len(place_refs)

    def looked_up(table_ref, index):
        spots = table_ref.shape[1] // 3
        rows = lax.broadcasted_iota(jnp.int32, (spots, block), 0).astype(F32)
        once = jnp.where(rows == index, 1.0, 0.0)
        found = dot(table_ref[...], jnp.concatenate([once] * 3, axis=0).astype(BF16))
        return found[:FREQS], found[FREQS:]

    for i, place_ref in enumerate(place_refs):
        columns = slice(i * block, (i + 1) * block)
        places = place_ref[:, :block].astype(F32)
        for axis in range(2):
            at = 4 * page + 2 * axis
            high_sin, high_cos = looked_up(high_ref, places[at : at + 1])
            low_sin, low_cos = looked_up(low_ref, places[at + 1 : at + 2])
            sines = high_sin * low_cos + high_cos * low_sin
            cosines = high_cos * low_cos - high_sin * low_sin
            rows = slice(axis * FREQS, (axis + 1) * FREQS)
            later = slice((2 + axis) * FREQS, (3 + axis) * FREQS)
            sin_ref[rows, columns] = sines
            cos_ref[rows, columns] = cosines
            codes_ref[rows, columns] = sines.astype(BF16)
            codes_ref[later, columns] = cosines.astype(BF16)


def forward_kernel(page, count, words_ref, *refs):
    place_refs, refs = refs[:count], refs[count:]
    piece_refs, refs = refs[:count], refs[count:]
    high_ref, low_ref, w_ref, box_ref, rot_cos_ref, rot_sin_ref = refs[:6]
    probs_ref, att_ref, heads_ref, sin_ref, cos_ref, codes_ref = refs[6:12]
    low_refs = refs[12 : 12 + count]
    tok_ref, pre_ref, kc_ref, qr_ref = refs[12 + count :]
    rows = tok_ref.shape[0]
    block = rows // count
    head = pl.program_id(0)
    span = pl.num_programs(0) * HEAD_DIM

    @pl.when(head == 0)
    def _():
        for i in range(count):
            tok_ref[i * block : (i + 1) * block] = piece_refs[i][...]
        pre_ref[...] = dot_nt(w_ref[...], tok_ref[...])
        write_codes(page, place_refs, high_ref, low_ref, sin_ref, cos_ref, codes_ref)
        kc_ref[:, :CODES] = codes_ref[...].astype(F32).T.astype(BF16)

    def pre(kind):
        at = kind * span + head * HEAD_DIM
        return pre_ref[pl.ds(pl.multiple_of(at, HEAD_DIM), HEAD_DIM)]

    rot_cos = rot_cos_ref[...]
    rot_sin = rot_sin_ref[...]
    query_pre = pre(0).astype(BF16)
    wide = query_pre.astype(F32)
    query = jnp.concatenate(turned(wide[:HALF], wide[HALF:], rot_cos, rot_sin), axis=0)
    key_pre = pre(1)
    key = jnp.concatenate(turned(key_pre[:HALF], key_pre[HALF:], rot_cos, rot_sin), axis=0)
    value = pre(2).astype(BF16)
    heads_ref[0, :HEAD_DIM] = query_pre
    heads_ref[0, HEAD_DIM : 2 * HEAD_DIM] = query.astype(BF16)
    heads_ref[0, 2 * HEAD_DIM : 3 * HEAD_DIM] = key.astype(BF16)
    heads_ref[0, 3 * HEAD_DIM :] = value
    kc_ref[:, CODES:] = key.T.astype(BF16)
    qr_ref[CODES:] = (query * 0.125).astype(BF16)
    step = min(256, block)

    def logits_at(at):
        part = slice(at, at + step)
        projected = dot_tn(box_ref[...], query_pre[:, part])
        sines = sin_ref[:, part]
        cosines = cos_ref[:, part]
        upper = projected[: 2 * FREQS]
        lower = projected[2 * FREQS :]
        qr_ref[: 2 * FREQS, part] = ((upper * cosines + lower * sines) * 0.125).astype(BF16)
        qr_ref[2 * FREQS : CODES, part] = ((lower * cosines - upper * sines) * 0.125).astype(BF16)
        return dot(kc_ref[...], qr_ref[:, part])

    following = logits_at(0)
    for at in range(0, rows, step):
        logits = following
        if at + step < rows:
            following = logits_at(at + step)
        peak = jnp.max(fold(logits, jnp.maximum), axis=0, keepdims=True)
        weight = jnp.exp(logits - peak)
        total = jnp.sum(fold(weight, jnp.add), axis=0, keepdims=True)
        probs = (weight * (1.0 / total)).astype(BF16)
        probs_ref[0, :, at : at + step] = probs
        attended = dot(value, probs)
        att_ref[0, :, at : at + step] = attended
        inner = at % block
        low_refs[at // block][:, inner : inner + step] = attended.astype(BF16)


def fixed(array):
    return pl.BlockSpec(array.shape, lambda *at: (0,) * len(array.shape))


def attention_forward(words, page, messages, pieces, w_own, box_own, rot_cos, rot_sin):
    count = len(messages)
    block, width = messages[0].shape[0] - 16, messages[0].shape[1]
    rows = count * block
    span = box_own.shape[0]
    heads = span // HEAD_DIM
    tables = [jnp.asarray(item) for item in angle_tables()]
    specs = [pl.BlockSpec((block, width), lambda h, words: (0, 0))] * count
    places = pl.BlockSpec((16, width), lambda h, words: (block // 16, 0))
    out_shape = [
        jax.ShapeDtypeStruct((heads, rows, rows), BF16),
        jax.ShapeDtypeStruct((heads, HEAD_DIM, rows), F32),
        jax.ShapeDtypeStruct((heads, 4 * HEAD_DIM, rows), BF16),
        jax.ShapeDtypeStruct((2 * FREQS, rows), F32),
        jax.ShapeDtypeStruct((2 * FREQS, rows), F32),
        jax.ShapeDtypeStruct((CODES, rows), BF16),
    ] + [jax.ShapeDtypeStruct((span, block), BF16)] * count
    return pl.pallas_call(
        functools.partial(forward_kernel, page, count),
        grid_spec=pltpu.PrefetchScalarGridSpec(
            num_scalar_prefetch=1,
            grid=(heads,),
            in_specs=[places] * count
            + specs
            + [fixed(item) for item in (*tables, w_own)]
            + [
                pl.BlockSpec((HEAD_DIM, CODES), lambda h, words: (h, 0)),
                fixed(rot_cos),
                fixed(rot_sin),
            ],
            out_specs=[
                pl.BlockSpec((1, rows, rows), lambda h, words: (h, 0, 0)),
                pl.BlockSpec((1, HEAD_DIM, rows), lambda h, words: (h, 0, 0)),
                pl.BlockSpec((1, 4 * HEAD_DIM, rows), lambda h, words: (h, 0, 0)),
            ]
            + [fixed(item) for item in out_shape[3:6]]
            + [pl.BlockSpec((HEAD_DIM, block), lambda h, words: (h, 0))] * count,
            scratch_shapes=[
                pltpu.VMEM((rows, width), BF16),
                pltpu.VMEM((3 * span, rows), F32),
                pltpu.VMEM((rows, CODES + HEAD_DIM), BF16),
                pltpu.VMEM((CODES + HEAD_DIM, rows), BF16),
            ],
        ),
        out_shape=out_shape,
        compiler_params=pltpu.CompilerParams(vmem_limit_bytes=VMEM_LIMIT),
        cost_estimate=pl.CostEstimate(
            flops=2 * heads * rows * (rows * 1100 + 200 * width + 64 * CODES),
            bytes_accessed=2 * heads * rows * rows + 12 * rows * width,
            transcendentals=heads * rows * rows,
        ),
        name="attention_forward",
    )(words, *messages, *pieces, *tables, w_own, box_own, rot_cos, rot_sin)


def backward_kernel(count, last, words_ref, *refs):
    grad_refs, refs = refs[:count], refs[count:]
    piece_refs, refs = refs[:count], refs[count:]
    probs_ref, att_ref, heads_ref, box_ref, codes_ref, sin_ref, cos_ref = refs[:7]
    rot_cos_ref, rot_sin_ref = refs[7:9]
    refs = refs[9:]
    if last:
        before_ref, refs = refs[0], refs[1:]
    pre_refs, refs = refs[:count], refs[count:]
    if last:
        mine_ref, theirs_ref, *refs = refs
    weight_grad_ref, kc_ref, logit_grad_ref, entry_grad_ref, turned_ref = refs
    block, width = piece_refs[0].shape
    rows = count * block
    head = pl.program_id(0)
    span = pl.num_programs(0) * HEAD_DIM

    @pl.when(head == 0)
    def _():
        kc_ref[:CODES] = codes_ref[...]

    kc_ref[CODES:] = heads_ref[0, 2 * HEAD_DIM : 3 * HEAD_DIM]
    packed = heads_ref[0].astype(F32).T.astype(BF16)
    query_pre = packed[:, :HEAD_DIM]
    query = packed[:, HEAD_DIM : 2 * HEAD_DIM]
    value = packed[:, 3 * HEAD_DIM :] * jnp.asarray(0.125, BF16)
    rot_cos = rot_cos_ref[...]
    rot_sin = rot_sin_ref[...]
    grad = jnp.concatenate([ref[...] for ref in grad_refs], axis=1)
    grad_tall = grad.astype(F32).T.astype(BF16)
    offsets = jnp.sum(grad.astype(F32) * att_ref[0], axis=0, keepdims=True) * 0.125
    step = min(256, block)
    place = pl.multiple_of(head * HEAD_DIM, HEAD_DIM)
    here = pl.ds(place, HEAD_DIM)

    def logits_back(at):
        part = slice(at, at + step)
        grad_probs = dot(value, grad[:, part])
        logit_grad_ref[:, part] = (
            probs_ref[0, :, part].astype(F32) * (grad_probs - offsets[:, part])
        ).astype(BF16)

    logits_back(0)
    for at in range(0, rows, step):
        if at + step < rows:
            logits_back(at + step)
        part = slice(at, at + step)
        back = dot(kc_ref[...], logit_grad_ref[:, part])
        sines = sin_ref[:, part]
        cosines = cos_ref[:, part]
        upper = back[: 2 * FREQS]
        lower = back[2 * FREQS : CODES]
        entry_grad_ref[: 2 * FREQS, part] = (upper * cosines - lower * sines).astype(BF16)
        entry_grad_ref[2 * FREQS :, part] = (lower * cosines + upper * sines).astype(BF16)
        first = back[CODES : CODES + HALF]
        second = back[CODES + HALF :]
        turned_ref[:HALF, part], turned_ref[HALF:, part] = turned(
            first, second, rot_cos[:, part], -rot_sin[:, part]
        )
    key_flat = dot(logit_grad_ref[...], query).T
    value_low = dot(probs_ref[0], grad_tall).T.astype(BF16)
    query_low = (turned_ref[...] + dot(box_ref[...], entry_grad_ref[...])).astype(BF16)
    key_low = jnp.concatenate(
        turned(key_flat[:HALF], key_flat[HALF:], rot_cos, -rot_sin), axis=0
    ).astype(BF16)
    for i in range(count):
        columns = slice(i * block, (i + 1) * block)
        pre_refs[i][here, :block] = query_low[:, columns]
        pre_refs[i][here, block : 2 * block] = key_low[:, columns]
        pre_refs[i][here, 2 * block :] = value_low[:, columns]
    weight_grad_ref[pl.ds(3 * span + place, HEAD_DIM)] = dot(entry_grad_ref[...], query_pre).T

    @pl.when(head == pl.num_programs(0) - 1)
    def _():
        for kind in range(3):
            columns = slice(kind * block, (kind + 1) * block)
            total = dot(pre_refs[0][:, columns], piece_refs[0][...])
            for i in range(1, count):
                total = total + dot(pre_refs[i][:, columns], piece_refs[i][...])
            weight_grad_ref[kind * span : (kind + 1) * span] = total
        if last:
            half = 2 * span
            core = words_ref[2]
            ours = pl.ds(pl.multiple_of(core * half, half), half)
            there = pl.ds(pl.multiple_of((1 - core) * half, half), half)
            mine_ref[...] = weight_grad_ref[ours] + before_ref[ours]
            theirs_ref[...] = (weight_grad_ref[there] + before_ref[there]).astype(BF16)


def attention_backward(
    words, page, grads, pieces, saved, box_own, rot_cos, rot_sin, before=None
):
    probs, att, heads_saved, sines, cosines, codes = saved
    count = len(pieces)
    rows, width = probs.shape[1], pieces[0].shape[1]
    block = rows // count
    span = box_own.shape[0]
    heads = span // HEAD_DIM
    last = before is not None
    extra = (before,) if last else ()
    full_shape = (4 * span, width)
    specs = [pl.BlockSpec((block, width), lambda h, words: (0, 0))] * count
    out_shape = [jax.ShapeDtypeStruct((span, 3 * block), BF16)] * count
    if last:
        out_shape += [
            jax.ShapeDtypeStruct((2 * span, width), F32),
            jax.ShapeDtypeStruct((2 * span, width), BF16),
        ]
    else:
        out_shape.append(jax.ShapeDtypeStruct(full_shape, F32))
    return pl.pallas_call(
        functools.partial(backward_kernel, count, last),
        grid_spec=pltpu.PrefetchScalarGridSpec(
            num_scalar_prefetch=1,
            grid=(heads,),
            in_specs=[pl.BlockSpec((HEAD_DIM, block), lambda h, words: (h, page))] * count
            + specs
            + [
                pl.BlockSpec((1, rows, rows), lambda h, words: (h, 0, 0)),
                pl.BlockSpec((1, HEAD_DIM, rows), lambda h, words: (h, 0, 0)),
                pl.BlockSpec((1, 4 * HEAD_DIM, rows), lambda h, words: (h, 0, 0)),
                pl.BlockSpec((HEAD_DIM, CODES), lambda h, words: (h, 0)),
            ]
            + [fixed(item) for item in (codes, sines, cosines, rot_cos, rot_sin, *extra)],
            out_specs=[fixed(item) for item in out_shape],
            scratch_shapes=([pltpu.VMEM(full_shape, F32)] if last else [])
            + [
                pltpu.VMEM((CODES + HEAD_DIM, rows), BF16),
                pltpu.VMEM((rows, rows), BF16),
                pltpu.VMEM((CODES, rows), BF16),
                pltpu.VMEM((HEAD_DIM, rows), F32),
            ],
        ),
        out_shape=out_shape,
        compiler_params=pltpu.CompilerParams(vmem_limit_bytes=VMEM_LIMIT),
        cost_estimate=pl.CostEstimate(
            flops=2 * heads * rows * (rows * 1400 + 200 * width + 128 * CODES),
            bytes_accessed=2 * heads * rows * rows + 12 * rows * width,
            transcendentals=0,
        ),
        name="attention_backward",
    )(
        words,
        *grads,
        *pieces,
        probs,
        att,
        heads_saved,
        box_own,
        codes,
        sines,
        cosines,
        rot_cos,
        rot_sin,
        *extra,
    )


def normed(value):
    centered = value - jnp.mean(value, axis=-1, keepdims=True)
    scale = lax.rsqrt(jnp.mean(centered * centered, axis=-1, keepdims=True) + 1e-05)
    return centered * scale, scale


def norm_back(grad, gain, unit, scale):
    scaled = grad * gain
    return scale * (
        scaled
        - jnp.mean(scaled, axis=-1, keepdims=True)
        - unit * jnp.mean(scaled * unit, axis=-1, keepdims=True)
    )


def column_sum(value):
    return jnp.sum(value, axis=0, keepdims=True)


def middle_kernel(pages, count, span, chunks, *refs):
    total = pages * count
    words_ref = refs[0]
    att_refs = refs[1 : 1 + total]
    (
        tok_ref,
        cot_ref,
        w_out_ref,
        vectors_ref,
        w_expand_ref,
        w_reduce_ref,
    ) = refs[1 + total : 7 + total]
    outs = refs[7 + total :]
    layer_ref, first_in_ref, theirs_ref, mine_ref, more_theirs_ref, more_mine_ref = outs[:6]
    grad_refs = outs[6 : 6 + count]
    (
        sums_ref,
        att_all,
        grad_all,
        unit_one,
        scale_one,
        first_wide,
        first_low,
        first_tall,
        active,
        slope,
        gathered,
        second_in,
        second_low,
    ) = outs[6 + count :]
    rank = words_ref[0]
    width = tok_ref.shape[1]
    block = tok_ref.shape[0] // pages
    step = pl.program_id(0)

    def rows_of(at):
        return pl.ds(pl.multiple_of((rank ^ at) * span, span), span)

    @pl.when(step == 0)
    def _():
        for page in range(pages):
            for at in range(count):
                att_all[rows_of(at), page * block : (page + 1) * block] = att_refs[
                    page * count + at
                ][...]
        branch = dot_tn(att_all[: w_out_ref.shape[0]], w_out_ref[...])
        unit, scale = normed(tok_ref[...].astype(F32) + branch)
        unit_one[...] = unit
        scale_one[...] = jnp.broadcast_to(scale, scale_one.shape)
        first_out = unit * vectors_ref[0:1] + vectors_ref[1:2]
        first_wide[...] = first_out
        first_low[...] = first_out.astype(BF16)
        first_tall[...] = first_out.T.astype(BF16)
        gathered[...] = jnp.zeros_like(gathered)
        sums_ref[...] = jnp.zeros_like(sums_ref)

    for chunk in range(chunks):

        @pl.when(step == chunk)
        def _(chunk=chunk):
            expanded = dot(first_low[...], w_expand_ref[...])
            gate = 0.5 + 0.5 * lax.erf(expanded * np.float32(np.sqrt(0.5)))
            bell = jnp.exp(expanded * expanded * -0.5) * np.float32(1.0 / np.sqrt(2.0 * np.pi))
            low = (expanded * gate).astype(BF16)
            active[chunk] = low
            slope[chunk] = gate + expanded * bell
            gathered[...] += dot(low, w_reduce_ref[...])

    @pl.when(step == chunks - 1)
    def _():
        unit, scale = normed(first_wide[...] + gathered[...])
        layer_ref[...] = (unit * vectors_ref[2:3] + vectors_ref[3:4]).astype(BF16)
        cot = cot_ref[...].astype(F32)
        sums_ref[2:3] = column_sum(cot * unit)
        sums_ref[3:4] = column_sum(cot)
        grad = norm_back(cot, vectors_ref[2:3], unit, scale)
        second_in[...] = grad
        second_low[...] = grad.astype(BF16)
        gathered[...] = grad

    for chunk in range(chunks):

        @pl.when(step == 2 * chunks - 1 - chunk)
        def _(chunk=chunk):
            grad_active = dot_nt(second_low[...], w_reduce_ref[...])
            grad_expanded = (grad_active * slope[chunk]).astype(BF16)
            grads_ref = mine_ref if chunk < chunks // 2 else theirs_ref
            grads_ref[:width] = dot(first_tall[...], grad_expanded).astype(BF16)
            grads_ref[width:] = dot_tn(active[chunk], second_low[...]).astype(BF16)
            gathered[...] += dot_nt(grad_expanded, w_expand_ref[...])

    @pl.when(step == 2 * chunks - 1)
    def _():
        unit = unit_one[...]
        grad_out = gathered[...]
        sums_ref[0:1] = column_sum(grad_out * unit)
        sums_ref[1:2] = column_sum(grad_out)
        grad = norm_back(grad_out, vectors_ref[0:1], unit, scale_one[:, :1])
        first_in_ref[...] = grad
        low = grad.astype(BF16)
        real = w_out_ref.shape[0]
        half = real // 2
        core = words_ref[2]
        for ref, side in ((more_mine_ref, core), (more_theirs_ref, 1 - core)):
            rows = pl.ds(pl.multiple_of(side * half, half), half)
            ref[:half] = dot(att_all[rows], low).astype(BF16)
            ref[half:] = jnp.zeros((ref.shape[0] - half, width), BF16)
            ref[half : half + 16] = sums_ref[...].astype(BF16)
        if grad_all.shape[0] > real:
            grad_all[real:] = jnp.zeros((grad_all.shape[0] - real, low.shape[0]), BF16)
        grad_all[:real] = dot_nt(w_out_ref[...], low).astype(BF16)
        for at in range(count):
            grad_refs[at][...] = grad_all[rows_of(at)]


def middle(words, att_parts, tok, cot, w_out, vectors, w_expand, w_reduce, pages, more):
    rows, width = tok.shape
    count = len(att_parts) // pages
    span, block = att_parts[0].shape
    hidden = w_expand.shape[1]
    chunks = hidden // width
    pairs = chunks // 2

    def whole(array):
        return pl.BlockSpec(array.shape, lambda s, words: (0,) * len(array.shape))

    def chunk_at(s, words):
        at = jnp.minimum(s, 2 * chunks - 1 - s)
        return (at + words[2] * pairs) % chunks

    def theirs_at(s, words):
        return jnp.clip(2 * chunks - 1 - s - pairs, 0, pairs - 1), 0

    def mine_at(s, words):
        return jnp.clip(2 * chunks - 1 - s, 0, pairs - 1), 0

    shapes = [
        jax.ShapeDtypeStruct((rows, width), BF16),
        jax.ShapeDtypeStruct((rows, width), F32),
        jax.ShapeDtypeStruct((hidden, width), BF16),
        jax.ShapeDtypeStruct((hidden, width), BF16),
        jax.ShapeDtypeStruct((more, width), BF16),
        jax.ShapeDtypeStruct((more, width), BF16),
    ] + [jax.ShapeDtypeStruct((span, pages * block), BF16)] * count
    specs = [whole(item) for item in shapes]
    specs[2] = pl.BlockSpec((2 * width, width), theirs_at)
    specs[3] = pl.BlockSpec((2 * width, width), mine_at)
    return pl.pallas_call(
        functools.partial(middle_kernel, pages, count, span, chunks),
        grid_spec=pltpu.PrefetchScalarGridSpec(
            num_scalar_prefetch=1,
            grid=(2 * chunks,),
            in_specs=[whole(item) for item in att_parts]
            + [
                whole(tok),
                whole(cot),
                whole(w_out),
                whole(vectors),
                pl.BlockSpec((width, width), lambda s, words: (0, chunk_at(s, words))),
                pl.BlockSpec((width, width), lambda s, words: (chunk_at(s, words), 0)),
            ],
            out_specs=specs,
            scratch_shapes=[
                pltpu.VMEM((16, width), F32),
                pltpu.VMEM((count * span, rows), BF16),
                pltpu.VMEM((count * span, rows), BF16),
                pltpu.VMEM((rows, width), F32),
                pltpu.VMEM((rows, 128), F32),
                pltpu.VMEM((rows, width), F32),
                pltpu.VMEM((rows, width), BF16),
                pltpu.VMEM((width, rows), BF16),
                pltpu.VMEM((chunks, rows, width), BF16),
                pltpu.VMEM((chunks, rows, width), F32),
                pltpu.VMEM((rows, width), F32),
                pltpu.VMEM((rows, width), F32),
                pltpu.VMEM((rows, width), BF16),
            ],
        ),
        out_shape=shapes,
        compiler_params=pltpu.CompilerParams(vmem_limit_bytes=VMEM_LIMIT),
        cost_estimate=pl.CostEstimate(
            flops=2 * rows * width * (6 * hidden + 3 * width),
            bytes_accessed=8 * width * hidden + 16 * rows * width,
            transcendentals=2 * rows * hidden,
        ),
        name="middle",
    )(words, *att_parts, tok, cot, w_out, vectors, w_expand, w_reduce)


def input_kernel(pages, count, span, base, *refs):
    words_ref = refs[0]
    own_refs = refs[1 : 1 + pages]
    message_refs = refs[1 + pages : pages + count]
    weight_refs = refs[pages + count : 3 + pages + count]
    first_in_ref, out_ref, held = refs[3 + pages + count :]
    rank = words_ref[0]
    width = out_ref.shape[1]
    block = out_ref.shape[0] // pages
    for page in range(pages):
        for at in range(count):
            part = message_refs[at - 1] if at else own_refs[page]
            top = base + page * span if at else 0
            place = pl.multiple_of((rank ^ at) * span, span)
            for kind in range(3):
                held[kind, pl.ds(place, span), page * block : (page + 1) * block] = part[
                    top : top + span, kind * block : (kind + 1) * block
                ]
    total = dot(weight_refs[0][...], held[0, :width])
    for kind in range(1, 3):
        total = total + dot(weight_refs[kind][...], held[kind, :width])
    out_ref[...] = (first_in_ref[...] + total.T).astype(BF16)


def input_gradient(words, own, messages, base, span, weights, first_in):
    pages = len(own)
    count = 1 + len(messages)
    rows, width = first_in.shape
    vmem = pl.BlockSpec(memory_space=pltpu.VMEM)
    return pl.pallas_call(
        functools.partial(input_kernel, pages, count, span, base),
        in_specs=[pl.BlockSpec(memory_space=pltpu.SMEM)] + [vmem] * (pages + count + 3),
        out_specs=vmem,
        out_shape=jax.ShapeDtypeStruct((rows, width), BF16),
        scratch_shapes=[pltpu.VMEM((3, count * span, rows), BF16)],
        compiler_params=pltpu.CompilerParams(vmem_limit_bytes=VMEM_LIMIT),
        cost_estimate=NO_COST,
        name="input_gradient",
    )(words, *own, *messages, *weights, first_in)


def local(body, name, words, arrays, shapes):
    def kernel(words_ref, *refs):
        body(words_ref, refs[: len(arrays)], refs[len(arrays) :])

    vmem = pl.BlockSpec(memory_space=pltpu.VMEM)
    shapes = [jax.ShapeDtypeStruct(shape, kind) for shape, kind in shapes]
    return pl.pallas_call(
        kernel,
        in_specs=[pl.BlockSpec(memory_space=pltpu.SMEM)] + [vmem] * len(arrays),
        out_specs=[vmem] * len(shapes),
        out_shape=shapes,
        compiler_params=pltpu.CompilerParams(vmem_limit_bytes=VMEM_LIMIT),
        cost_estimate=NO_COST,
        name=name,
    )(words, *arrays)


def shard(index, rows, base=0):
    return pl.ds(pl.multiple_of(base + index * rows, 16), rows)


def total_of(refs, rows=slice(None)):
    total = refs[0][rows].astype(F32)
    for ref in refs[1:]:
        total = total + ref[rows].astype(F32)
    return total


def tree_sum(terms):
    while len(terms) > 1:
        terms = [terms[i] + terms[i + 1] for i in range(0, len(terms), 2)]
    return terms[0]


class Plan:
    def __init__(self, rows, rows_a, more, span, width):
        self.count = lax.axis_size("blk")
        self.rows = rows
        self.rows_a = rows_a
        self.more = more
        self.span = span
        self.width = width
        self.a_ff = rows_a // self.count
        self.a_more = more // self.count
        self.a = self.a_ff + self.a_more
        self.b = (rows - rows_a) // lax.axis_size("depth")

    def shapes(self, *sizes):
        return [((rows, self.width), BF16) for rows in sizes]

    def scatter_one(self, words, halves):
        count, width = self.count, self.width
        a_ff, a_more = self.a_ff, self.a_more
        b_rows = (self.rows - self.rows_a) // count

        def kernel(words_ref, *refs):
            parts = refs[6 : 6 + count]
            for i in range(count):

                @pl.when(pl.program_id(0) == i)
                def _(i=i):
                    parts[i][:a_ff] = total_of(refs[:2]).astype(BF16)
                    parts[i][a_ff:] = total_of(refs[2:4]).astype(BF16)

            refs[6 + count][...] = total_of(refs[4:6]).astype(BF16)

        def there(rows):
            return pl.BlockSpec((rows, width), lambda i, words: (words[0] ^ i, 0))

        own_b = pl.BlockSpec((b_rows, width), lambda i, words: (self.rows_a // b_rows + i, 0))
        shapes = [jax.ShapeDtypeStruct((self.a, width), BF16)] * count
        shapes.append(jax.ShapeDtypeStruct((self.rows - self.rows_a, width), BF16))
        *parts_a, part_b = pl.pallas_call(
            kernel,
            grid_spec=pltpu.PrefetchScalarGridSpec(
                num_scalar_prefetch=1,
                grid=(count,),
                in_specs=[there(a_ff)] * 2 + [there(a_more)] * 2 + [own_b] * 2,
                out_specs=[fixed(item) for item in shapes[:count]]
                + [pl.BlockSpec((b_rows, width), lambda i, words: (i, 0))],
            ),
            out_shape=shapes,
            compiler_params=pltpu.CompilerParams(vmem_limit_bytes=VMEM_LIMIT),
            cost_estimate=NO_COST,
            name="scatter_one",
        )(words, *halves, *halves[:2])
        return [from_blk(part, i) for i, part in enumerate(parts_a)], part_b

    def scatter_two(self, words, parts_a, part_b, pages):
        count = self.count

        def body(words, ins, outs):
            outs[0][...] = total_of(ins[:count]).astype(BF16)
            for i, out in enumerate(outs[1:]):
                out[: self.b] = ins[count][...]
                for page in range(len(pages)):
                    piece = ins[count + 1 + page * (count - 1) + i]
                    base = self.b + page * self.span
                    out[base : base + self.span, : piece.shape[1]] = piece[...]

        shapes = self.shapes(self.a, *[self.b + len(pages) * self.span] * (count - 1))
        pieces = [piece for page in pages for piece in page[1:]]
        part_a, *messages = local(body, "scatter_two", words, [*parts_a, part_b, *pieces], shapes)
        return part_a, [from_blk(item, i + 1) for i, item in enumerate(messages)]

    def sum_b(self, words, part_b, messages):
        def body(words, ins, outs):
            terms = [ref[: self.b].astype(F32) for ref in ins]
            outs[0][...] = tree_sum(terms).astype(BF16)

        return local(body, "sum_b", words, [part_b, *messages], self.shapes(self.b))[0]

    def gather_b(self, words, part_b):
        depth = lax.axis_size("depth")
        distance = depth // 2
        held = part_b
        while distance:
            other = swapped(held, distance, "depth")
            distance //= 2
            if distance:

                def body(words, ins, outs):
                    rows = ins[0].shape[0]
                    outs[0][:rows] = ins[0][...]
                    outs[0][rows:] = ins[1][...]

                shapes = self.shapes(2 * held.shape[0])
                held = local(body, "gather_b", words, [held, other], shapes)[0]
        return held, other

    def join(self, words, parts_a, parts_b):
        depth = lax.axis_size("depth")
        order = [0]
        distance = depth // 2
        while distance:
            order = order + [item ^ distance for item in order]
            distance //= 2

        def body(words, ins, outs):
            for i in range(self.count):
                outs[0][shard(words[0] ^ i, self.a_ff)] = ins[i][: self.a_ff]
                outs[1][shard(words[0] ^ i, self.a_more)] = ins[i][self.a_ff : self.a]
            for at, k in enumerate(order):
                ref = ins[self.count + at // (depth // 2)]
                base = at % (depth // 2) * self.b
                rows = shard(words[1] ^ k, self.b, self.rows_a)
                outs[0][rows] = ref[base : base + self.b]

        shapes = self.shapes(self.rows, self.more)
        return local(body, "join", words, [*parts_a, *parts_b], shapes)


def widened(words, half, side, hidden, before=()):
    width = half.shape[1]
    chunks = hidden // width
    pairs = chunks // 2

    def kernel(words_ref, half_ref, *refs):
        expand_ref, reduce_ref = refs[len(before) :]
        expand_ref[...] = half_ref[:width].astype(F32)
        reduce_ref[...] = half_ref[width:].astype(F32)

    def place(s, words):
        return (s + (words[2] + side) * pairs) % chunks

    return pl.pallas_call(
        kernel,
        grid_spec=pltpu.PrefetchScalarGridSpec(
            num_scalar_prefetch=1,
            grid=(pairs,),
            in_specs=[pl.BlockSpec((2 * width, width), lambda s, words: (s, 0))]
            + [pl.BlockSpec(memory_space=pl.ANY)] * len(before),
            out_specs=[
                pl.BlockSpec((width, width), lambda s, words: (0, place(s, words))),
                pl.BlockSpec((width, width), lambda s, words: (place(s, words), 0)),
            ],
        ),
        out_shape=[
            jax.ShapeDtypeStruct((width, hidden), F32),
            jax.ShapeDtypeStruct((hidden, width), F32),
        ],
        input_output_aliases={2: 0, 3: 1} if before else {},
        compiler_params=pltpu.CompilerParams(vmem_limit_bytes=VMEM_LIMIT),
        cost_estimate=NO_COST,
        name="widen",
    )(words, half, *before)


def pair_sum(words, mine, other):
    def body(words, ins, outs):
        outs[0][...] = total_of(ins).astype(BF16)

    return local(body, "pair_sum", words, [mine, other], [(mine.shape, BF16)])[0]


def join_blk(words, parts):
    half, width = parts[0].shape

    def body(words, ins, outs):
        for i in range(len(parts)):
            outs[0][shard(words[0] ^ i, half)] = ins[i][...]

    return local(body, "heads_join", words, parts, [((len(parts) * half, width), BF16)])[0]


def finish_kernel(count, span, half, words_ref, *refs):
    own_ref, other_ref, more_ref, more_other_ref = refs[:4]
    query_ref, key_ref, value_ref, project_ref, box_ref, sums_ref = refs[4:]
    width = query_ref.shape[0]

    def write(lower_ref, upper_ref, more_lower_ref, more_upper_ref):
        def grad(ref, part):
            rows = [
                ref[(2 * i + part) * span : (2 * i + part + 1) * span].astype(F32)
                for i in range(count)
            ]
            return jnp.concatenate(rows, axis=0)[:width].T

        query_ref[...] = grad(lower_ref, 0)
        key_ref[...] = grad(lower_ref, 1)
        value_ref[...] = grad(upper_ref, 0)
        box_ref[...] = entry_order(grad(upper_ref, 1))
        project_ref[:half] = more_lower_ref[:half].astype(F32)
        project_ref[half:] = more_upper_ref[:half].astype(F32)
        sums_ref[...] = more_lower_ref[half : half + 16].astype(F32)[:8]

    @pl.when(words_ref[2] == 0)
    def _():
        write(own_ref, other_ref, more_ref, more_other_ref)

    @pl.when(words_ref[2] == 1)
    def _():
        write(other_ref, own_ref, more_other_ref, more_ref)


def finished(words, own, other, more, more_other, span, width):
    count = lax.axis_size("blk")
    vmem = pl.BlockSpec(memory_space=pltpu.VMEM)
    shapes = [jax.ShapeDtypeStruct((width, width), F32)] * 5
    shapes.append(jax.ShapeDtypeStruct((8, width), F32))
    return pl.pallas_call(
        functools.partial(finish_kernel, count, span, width // 2),
        in_specs=[pl.BlockSpec(memory_space=pltpu.SMEM)] + [vmem] * 4,
        out_specs=[vmem] * 6,
        out_shape=shapes,
        compiler_params=pltpu.CompilerParams(vmem_limit_bytes=VMEM_LIMIT),
        cost_estimate=NO_COST,
        name="finish",
    )(words, own, other, more, more_other)


def per_device(
    tokens,
    boxes,
    w_query,
    w_key,
    w_value,
    w_output,
    box_weight,
    first_gain,
    first_shift,
    w_expand,
    w_reduce,
    second_gain,
    second_shift,
    cotangent,
):
    pages, block, width = tokens.shape
    count = lax.axis_size("blk")
    depth = lax.axis_size("depth")
    words = jnp.stack(
        [lax.axis_index("blk"), lax.axis_index("depth"), lax.axis_index("core")]
    ).astype(jnp.int32)
    hidden = w_expand.shape[1]
    span = -(-HEADS // count) * HEAD_DIM
    unit = 16 * count * depth
    more = -(-(width // 2 + 16) // unit) * unit

    own_places = jnp.stack([boxes[0] + boxes[2], boxes[1] + boxes[3]], axis=1)
    own_places = jnp.stack([lax.shift_right_logical(own_places, 6), own_places & 63], axis=2)
    own_places = own_places.reshape(4 * pages, block).astype(BF16)
    own_places = jnp.pad(own_places, ((0, 16 - 4 * pages), (0, width - block)))
    message = jnp.concatenate([tokens[0], own_places])
    messages = [from_blk(message, i) for i in range(count)]
    w_own, box_own, rot_cos, rot_sin = prepare(
        words, w_query, w_key, w_value, box_weight, span, count * block
    )
    messages, rot_cos = lax.optimization_barrier((messages, rot_cos))
    own = after(messages, tokens[1])
    pieces = [messages, [from_blk(own, i) for i in range(count)]]

    saved = []
    att_parts = []
    for page in range(pages):
        results = attention_forward(
            words, page, messages, pieces[page], w_own, box_own, rot_cos, rot_sin
        )
        saved.append(results[:6])
        att_parts += [from_blk(results[6 + i], i) for i in range(count)]

    vectors = jnp.stack([first_gain, first_shift, second_gain, second_shift])
    results = middle(
        words,
        att_parts,
        tokens.reshape(pages * block, width),
        cotangent.reshape(pages * block, width),
        w_output,
        vectors,
        w_expand,
        w_reduce,
        pages,
        more,
    )
    layer_out, first_in, theirs, mine, more_theirs, more_mine = results[:6]
    grads = [from_blk(results[6 + i], i) for i in range(count)]
    plan = Plan(hidden, 2 * hidden // 3, more, span, width)
    parts_a, part_b = plan.scatter_one(
        after(grads, words), [mine, from_core(theirs), more_mine, from_core(more_theirs)]
    )
    part_b = lax.psum_scatter(part_b, "depth", scatter_dimension=0, tiled=True)

    def backward(page, words, before=None):
        return attention_backward(
            words,
            page,
            grads,
            pieces[page],
            saved[page],
            box_own,
            rot_cos,
            rot_sin,
            before,
        )

    *pre_one, before = backward(0, after(parts_a[0], words))
    *pre_two, heads_mine, heads_theirs = backward(1, words, before)
    own = [pre_one[0], pre_two[0]]
    part_a, messages_b = plan.scatter_two(
        after(heads_mine, words), parts_a, part_b, [pre_one, pre_two]
    )
    heads_theirs = after(part_a, heads_theirs)
    done = part_a
    part_a = lax.psum(part_a, "depth")
    heads = pair_sum(after(done, words), heads_mine, from_core(heads_theirs))
    heads = pair_sum(after(heads, words), heads, swapped(heads, 1, "depth"))
    part_b = plan.sum_b(after(heads, words), part_b, messages_b)
    parts_a = [from_blk(after(part_b, part_a), i) for i in range(count)]
    distance = 2
    done = part_b
    while distance < depth:
        heads = pair_sum(after(done, words), heads, swapped(heads, distance, "depth"))
        done = heads
        distance *= 2
    parts_b = plan.gather_b(after(heads, words), part_b)
    parts_a, heads = lax.optimization_barrier((parts_a, heads))
    heads = [from_blk(heads, i) for i in range(count)]
    ff, extra = plan.join(words, parts_a, parts_b)
    ff_other, extra_other = from_core(ff), from_core(extra)
    wide = widened(words, ff, 0, hidden)
    input_grad = input_gradient(
        after(wide[0], words),
        own,
        messages_b,
        plan.b,
        span,
        (w_query, w_key, w_value),
        first_in,
    )
    grad_expand, grad_reduce = widened(after(input_grad, words), ff_other, 1, hidden, wide)
    heads_own = join_blk(after(grad_expand, words), heads)
    heads_other = from_core(heads_own)
    grad_query, grad_key, grad_value, grad_project, grad_box, sums = finished(
        words, heads_own, heads_other, extra, extra_other, span, width
    )
    return (
        layer_out.reshape(tokens.shape),
        input_grad.reshape(tokens.shape),
        grad_query,
        grad_key,
        grad_value,
        grad_project,
        grad_box,
        sums[0],
        sums[1],
        grad_expand,
        grad_reduce,
        sums[2],
        sums[3],
    )


def solution(mesh):
    blocks, rest = mesh.devices.shape
    parts = jax.sharding.Mesh(
        mesh.devices.reshape(blocks, rest // 2, 2), ("blk", "depth", "core")
    )
    split = P(("depth", "core"), "blk", None)
    return jax.shard_map(
        per_device,
        mesh=parts,
        in_specs=(split, P(None, ("depth", "core"), "blk")) + (P(),) * 11 + (split,),
        out_specs=(split, split) + (P(),) * 11,
        check_vma=False,
    )
```

```python
import functools

import jax
import jax.numpy as jnp
import numpy as np
from jax import lax
from jax.experimental import pallas as pl
from jax.experimental.pallas import tpu as pltpu
from jax.sharding import PartitionSpec as P

HEADS = 12
HEAD_DIM = 64
HALF = 32
FREQS = 192
CODES = 4 * FREQS
VMEM_LIMIT = 60 * 1024 * 1024
NO_COST = pl.CostEstimate(flops=0, bytes_accessed=0, transcendentals=0)
F32 = jnp.float32
BF16 = jnp.bfloat16


def dot(left, right):
    return lax.dot_general(left, right, (((1,), (0,)), ((), ())), preferred_element_type=F32)


def dot_nt(left, right):
    return lax.dot_general(left, right, (((1,), (1,)), ((), ())), preferred_element_type=F32)


def dot_tn(left, right):
    return lax.dot_general(left, right, (((0,), (0,)), ((), ())), preferred_element_type=F32)


def swapped(block, distance, axis="blk"):
    count = lax.axis_size(axis)
    return lax.ppermute(block, axis, [(i, i ^ distance) for i in range(count)])


def from_blk(block, distance):
    return swapped(block, distance) if distance else block


def from_core(block):
    return swapped(block, 1, "core")


def after(done, value):
    return lax.optimization_barrier((value, done))[0]


def turned(upper, lower, cosines, sines):
    return upper * cosines - lower * sines, lower * cosines + upper * sines


def entry_order(rows):
    return jnp.concatenate(
        [
            rows[:FREQS],
            rows[2 * FREQS : 3 * FREQS],
            rows[FREQS : 2 * FREQS],
            rows[3 * FREQS :],
        ],
        axis=0,
    )


def angle_tables():
    rates = np.float32(10000.0) ** (-np.arange(FREQS, dtype=np.float32) / np.float32(FREQS))
    tables = []
    for places in (32.0 * np.arange(32), 0.5 * np.arange(64)):
        angles = rates.astype(np.float64)[:, None] * places[None, :]
        left = np.concatenate([np.sin(angles), np.cos(angles)])
        parts = []
        for _ in range(3):
            parts.append(left.astype(jnp.bfloat16))
            left = left - parts[-1].astype(np.float64)
        tables.append(np.concatenate(parts, axis=1))
    return tables


def rotary_tables(length):
    rates = np.float32(10000.0) ** (-np.arange(HALF, dtype=np.float32) / np.float32(HALF))
    angles = np.arange(length, dtype=np.float32)[None, :] * rates[:, None]
    angles = angles.astype(np.float64)
    return np.cos(angles).astype(np.float32), np.sin(angles).astype(np.float32)


def prepare_kernel(
    words_ref,
    query_ref,
    key_ref,
    value_ref,
    box_ref,
    cos_ref,
    sin_ref,
    own_ref,
    own_box_ref,
    own_cos_ref,
    own_sin_ref,
):
    rank = words_ref[0]
    span = own_box_ref.shape[0]
    width = query_ref.shape[1]
    count = lax.axis_size("blk")
    block = cos_ref.shape[1] // count
    row = lax.broadcasted_iota(jnp.int32, (span, width), 0) + rank * span
    column = lax.broadcasted_iota(jnp.int32, (span, width), 1)
    pick = jnp.where(row == column, 1.0, 0.0).astype(BF16)
    for kind, ref in enumerate((query_ref, key_ref, value_ref)):
        own_ref[kind * span : (kind + 1) * span] = dot_nt(pick, ref[...]).astype(BF16)
    own_box_ref[...] = dot_nt(pick, entry_order(box_ref[...])).astype(BF16)
    for i in range(count):
        from_cols = pl.ds(pl.multiple_of((rank ^ i) * block, block), block)
        own_cos_ref[:, i * block : (i + 1) * block] = cos_ref[:, from_cols]
        own_sin_ref[:, i * block : (i + 1) * block] = sin_ref[:, from_cols]


def prepare(words, w_query, w_key, w_value, box_weight, span, length):
    width = w_query.shape[0]
    vmem = pl.BlockSpec(memory_space=pltpu.VMEM)
    return pl.pallas_call(
        prepare_kernel,
        in_specs=[pl.BlockSpec(memory_space=pltpu.SMEM)] + [vmem] * 6,
        out_specs=[vmem] * 4,
        out_shape=[
            jax.ShapeDtypeStruct((3 * span, width), BF16),
            jax.ShapeDtypeStruct((span, CODES), BF16),
            jax.ShapeDtypeStruct((HALF, length), F32),
            jax.ShapeDtypeStruct((HALF, length), F32),
        ],
        compiler_params=pltpu.CompilerParams(vmem_limit_bytes=VMEM_LIMIT),
        cost_estimate=pl.CostEstimate(
            flops=8 * span * width * width, bytes_accessed=10 * width * width, transcendentals=0
        ),
        name="prepare",
    )(words, w_query, w_key, w_value, box_weight, *map(jnp.asarray, rotary_tables(length)))


def fold(value, combine):
    while value.shape[0] > 8:
        half = value.shape[0] // 2
        value = combine(value[:half], value[half:])
    return value


def write_codes(page, place_refs, high_ref, low_ref, sin_ref, cos_ref, codes_ref):
    block = sin_ref.shape[1] // len(place_refs)

    def looked_up(table_ref, index):
        spots = table_ref.shape[1] // 3
        rows = lax.broadcasted_iota(jnp.int32, (spots, block), 0).astype(F32)
        once = jnp.where(rows == index, 1.0, 0.0)
        found = dot(table_ref[...], jnp.concatenate([once] * 3, axis=0).astype(BF16))
        return found[:FREQS], found[FREQS:]

    for i, place_ref in enumerate(place_refs):
        columns = slice(i * block, (i + 1) * block)
        places = place_ref[:, :block].astype(F32)
        for axis in range(2):
            at = 4 * page + 2 * axis
            high_sin, high_cos = looked_up(high_ref, places[at : at + 1])
            low_sin, low_cos = looked_up(low_ref, places[at + 1 : at + 2])
            sines = high_sin * low_cos + high_cos * low_sin
            cosines = high_cos * low_cos - high_sin * low_sin
            rows = slice(axis * FREQS, (axis + 1) * FREQS)
            later = slice((2 + axis) * FREQS, (3 + axis) * FREQS)
            sin_ref[rows, columns] = sines
            cos_ref[rows, columns] = cosines
            codes_ref[rows, columns] = sines.astype(BF16)
            codes_ref[later, columns] = cosines.astype(BF16)


def forward_kernel(page, count, words_ref, *refs):
    place_refs, refs = refs[:count], refs[count:]
    piece_refs, refs = refs[:count], refs[count:]
    high_ref, low_ref, w_ref, box_ref, rot_cos_ref, rot_sin_ref = refs[:6]
    probs_ref, att_ref, heads_ref, sin_ref, cos_ref, codes_ref = refs[6:12]
    low_refs = refs[12 : 12 + count]
    tok_ref, pre_ref, kc_ref, qr_ref = refs[12 + count :]
    rows = tok_ref.shape[0]
    block = rows // count
    head = pl.program_id(0)
    span = pl.num_programs(0) * HEAD_DIM

    @pl.when(head == 0)
    def _():
        for i in range(count):
            tok_ref[i * block : (i + 1) * block] = piece_refs[i][...]
        pre_ref[...] = dot_nt(w_ref[...], tok_ref[...])
        write_codes(page, place_refs, high_ref, low_ref, sin_ref, cos_ref, codes_ref)
        kc_ref[:, :CODES] = codes_ref[...].astype(F32).T.astype(BF16)

    def pre(kind):
        at = kind * span + head * HEAD_DIM
        return pre_ref[pl.ds(pl.multiple_of(at, HEAD_DIM), HEAD_DIM)]

    rot_cos = rot_cos_ref[...]
    rot_sin = rot_sin_ref[...]
    query_pre = pre(0).astype(BF16)
    wide = query_pre.astype(F32)
    query = jnp.concatenate(turned(wide[:HALF], wide[HALF:], rot_cos, rot_sin), axis=0)
    key_pre = pre(1)
    key = jnp.concatenate(turned(key_pre[:HALF], key_pre[HALF:], rot_cos, rot_sin), axis=0)
    value = pre(2).astype(BF16)
    heads_ref[0, :HEAD_DIM] = query_pre
    heads_ref[0, HEAD_DIM : 2 * HEAD_DIM] = query.astype(BF16)
    heads_ref[0, 2 * HEAD_DIM : 3 * HEAD_DIM] = key.astype(BF16)
    heads_ref[0, 3 * HEAD_DIM :] = value
    kc_ref[:, CODES:] = key.T.astype(BF16)
    qr_ref[CODES:] = (query * 0.125).astype(BF16)
    step = min(256, block)

    def logits_at(at):
        part = slice(at, at + step)
        projected = dot_tn(box_ref[...], query_pre[:, part])
        sines = sin_ref[:, part]
        cosines = cos_ref[:, part]
        upper = projected[: 2 * FREQS]
        lower = projected[2 * FREQS :]
        qr_ref[: 2 * FREQS, part] = ((upper * cosines + lower * sines) * 0.125).astype(BF16)
        qr_ref[2 * FREQS : CODES, part] = ((lower * cosines - upper * sines) * 0.125).astype(BF16)
        return dot(kc_ref[...], qr_ref[:, part])

    following = logits_at(0)
    for at in range(0, rows, step):
        logits = following
        if at + step < rows:
            following = logits_at(at + step)
        peak = jnp.max(fold(logits, jnp.maximum), axis=0, keepdims=True)
        weight = jnp.exp(logits - peak)
        total = jnp.sum(fold(weight, jnp.add), axis=0, keepdims=True)
        probs = (weight * (1.0 / total)).astype(BF16)
        probs_ref[0, :, at : at + step] = probs
        attended = dot(value, probs)
        att_ref[0, :, at : at + step] = attended
        inner = at % block
        low_refs[at // block][:, inner : inner + step] = attended.astype(BF16)


def fixed(array):
    return pl.BlockSpec(array.shape, lambda *at: (0,) * len(array.shape))


def attention_forward(words, page, messages, pieces, w_own, box_own, rot_cos, rot_sin):
    count = len(messages)
    block, width = messages[0].shape[0] - 16, messages[0].shape[1]
    rows = count * block
    span = box_own.shape[0]
    heads = span // HEAD_DIM
    tables = [jnp.asarray(item) for item in angle_tables()]
    specs = [pl.BlockSpec((block, width), lambda h, words: (0, 0))] * count
    places = pl.BlockSpec((16, width), lambda h, words: (block // 16, 0))
    out_shape = [
        jax.ShapeDtypeStruct((heads, rows, rows), BF16),
        jax.ShapeDtypeStruct((heads, HEAD_DIM, rows), F32),
        jax.ShapeDtypeStruct((heads, 4 * HEAD_DIM, rows), BF16),
        jax.ShapeDtypeStruct((2 * FREQS, rows), F32),
        jax.ShapeDtypeStruct((2 * FREQS, rows), F32),
        jax.ShapeDtypeStruct((CODES, rows), BF16),
    ] + [jax.ShapeDtypeStruct((span, block), BF16)] * count
    return pl.pallas_call(
        functools.partial(forward_kernel, page, count),
        grid_spec=pltpu.PrefetchScalarGridSpec(
            num_scalar_prefetch=1,
            grid=(heads,),
            in_specs=[places] * count
            + specs
            + [fixed(item) for item in (*tables, w_own)]
            + [
                pl.BlockSpec((HEAD_DIM, CODES), lambda h, words: (h, 0)),
                fixed(rot_cos),
                fixed(rot_sin),
            ],
            out_specs=[
                pl.BlockSpec((1, rows, rows), lambda h, words: (h, 0, 0)),
                pl.BlockSpec((1, HEAD_DIM, rows), lambda h, words: (h, 0, 0)),
                pl.BlockSpec((1, 4 * HEAD_DIM, rows), lambda h, words: (h, 0, 0)),
            ]
            + [fixed(item) for item in out_shape[3:6]]
            + [pl.BlockSpec((HEAD_DIM, block), lambda h, words: (h, 0))] * count,
            scratch_shapes=[
                pltpu.VMEM((rows, width), BF16),
                pltpu.VMEM((3 * span, rows), F32),
                pltpu.VMEM((rows, CODES + HEAD_DIM), BF16),
                pltpu.VMEM((CODES + HEAD_DIM, rows), BF16),
            ],
        ),
        out_shape=out_shape,
        compiler_params=pltpu.CompilerParams(vmem_limit_bytes=VMEM_LIMIT),
        cost_estimate=pl.CostEstimate(
            flops=2 * heads * rows * (rows * 1100 + 200 * width + 64 * CODES),
            bytes_accessed=2 * heads * rows * rows + 12 * rows * width,
            transcendentals=heads * rows * rows,
        ),
        name="attention_forward",
    )(words, *messages, *pieces, *tables, w_own, box_own, rot_cos, rot_sin)


def backward_kernel(count, last, words_ref, *refs):
    grad_refs, refs = refs[:count], refs[count:]
    piece_refs, refs = refs[:count], refs[count:]
    probs_ref, att_ref, heads_ref, box_ref, codes_ref, sin_ref, cos_ref = refs[:7]
    rot_cos_ref, rot_sin_ref = refs[7:9]
    refs = refs[9:]
    if last:
        before_ref, refs = refs[0], refs[1:]
    pre_refs, refs = refs[:count], refs[count:]
    if last:
        mine_ref, theirs_ref, *refs = refs
    weight_grad_ref, kc_ref, logit_grad_ref, entry_grad_ref, turned_ref = refs
    block, width = piece_refs[0].shape
    rows = count * block
    head = pl.program_id(0)
    span = pl.num_programs(0) * HEAD_DIM

    @pl.when(head == 0)
    def _():
        kc_ref[:CODES] = codes_ref[...]

    kc_ref[CODES:] = heads_ref[0, 2 * HEAD_DIM : 3 * HEAD_DIM]
    packed = heads_ref[0].astype(F32).T.astype(BF16)
    query_pre = packed[:, :HEAD_DIM]
    query = packed[:, HEAD_DIM : 2 * HEAD_DIM]
    value = packed[:, 3 * HEAD_DIM :] * jnp.asarray(0.125, BF16)
    rot_cos = rot_cos_ref[...]
    rot_sin = rot_sin_ref[...]
    grad = jnp.concatenate([ref[...] for ref in grad_refs], axis=1)
    grad_tall = grad.astype(F32).T.astype(BF16)
    offsets = jnp.sum(grad.astype(F32) * att_ref[0], axis=0, keepdims=True) * 0.125
    step = min(256, block)
    place = pl.multiple_of(head * HEAD_DIM, HEAD_DIM)
    here = pl.ds(place, HEAD_DIM)

    def logits_back(at):
        part = slice(at, at + step)
        grad_probs = dot(value, grad[:, part])
        logit_grad_ref[:, part] = (
            probs_ref[0, :, part].astype(F32) * (grad_probs - offsets[:, part])
        ).astype(BF16)

    logits_back(0)
    for at in range(0, rows, step):
        if at + step < rows:
            logits_back(at + step)
        part = slice(at, at + step)
        back = dot(kc_ref[...], logit_grad_ref[:, part])
        sines = sin_ref[:, part]
        cosines = cos_ref[:, part]
        upper = back[: 2 * FREQS]
        lower = back[2 * FREQS : CODES]
        entry_grad_ref[: 2 * FREQS, part] = (upper * cosines - lower * sines).astype(BF16)
        entry_grad_ref[2 * FREQS :, part] = (lower * cosines + upper * sines).astype(BF16)
        first = back[CODES : CODES + HALF]
        second = back[CODES + HALF :]
        turned_ref[:HALF, part], turned_ref[HALF:, part] = turned(
            first, second, rot_cos[:, part], -rot_sin[:, part]
        )
    key_flat = dot(logit_grad_ref[...], query).T
    value_low = dot(probs_ref[0], grad_tall).T.astype(BF16)
    query_low = (turned_ref[...] + dot(box_ref[...], entry_grad_ref[...])).astype(BF16)
    key_low = jnp.concatenate(
        turned(key_flat[:HALF], key_flat[HALF:], rot_cos, -rot_sin), axis=0
    ).astype(BF16)
    for i in range(count):
        columns = slice(i * block, (i + 1) * block)
        pre_refs[i][here, :block] = query_low[:, columns]
        pre_refs[i][here, block : 2 * block] = key_low[:, columns]
        pre_refs[i][here, 2 * block :] = value_low[:, columns]
    weight_grad_ref[pl.ds(3 * span + place, HEAD_DIM)] = dot(entry_grad_ref[...], query_pre).T

    @pl.when(head == pl.num_programs(0) - 1)
    def _():
        for kind in range(3):
            columns = slice(kind * block, (kind + 1) * block)
            total = dot(pre_refs[0][:, columns], piece_refs[0][...])
            for i in range(1, count):
                total = total + dot(pre_refs[i][:, columns], piece_refs[i][...])
            weight_grad_ref[kind * span : (kind + 1) * span] = total
        if last:
            half = 2 * span
            core = words_ref[2]
            ours = pl.ds(pl.multiple_of(core * half, half), half)
            there = pl.ds(pl.multiple_of((1 - core) * half, half), half)
            mine_ref[...] = weight_grad_ref[ours] + before_ref[ours]
            theirs_ref[...] = (weight_grad_ref[there] + before_ref[there]).astype(BF16)


def attention_backward(
    words, page, grads, pieces, saved, box_own, rot_cos, rot_sin, before=None
):
    probs, att, heads_saved, sines, cosines, codes = saved
    count = len(pieces)
    rows, width = probs.shape[1], pieces[0].shape[1]
    block = rows // count
    span = box_own.shape[0]
    heads = span // HEAD_DIM
    last = before is not None
    extra = (before,) if last else ()
    full_shape = (4 * span, width)
    specs = [pl.BlockSpec((block, width), lambda h, words: (0, 0))] * count
    out_shape = [jax.ShapeDtypeStruct((span, 3 * block), BF16)] * count
    if last:
        out_shape += [
            jax.ShapeDtypeStruct((2 * span, width), F32),
            jax.ShapeDtypeStruct((2 * span, width), BF16),
        ]
    else:
        out_shape.append(jax.ShapeDtypeStruct(full_shape, F32))
    return pl.pallas_call(
        functools.partial(backward_kernel, count, last),
        grid_spec=pltpu.PrefetchScalarGridSpec(
            num_scalar_prefetch=1,
            grid=(heads,),
            in_specs=[pl.BlockSpec((HEAD_DIM, block), lambda h, words: (h, page))] * count
            + specs
            + [
                pl.BlockSpec((1, rows, rows), lambda h, words: (h, 0, 0)),
                pl.BlockSpec((1, HEAD_DIM, rows), lambda h, words: (h, 0, 0)),
                pl.BlockSpec((1, 4 * HEAD_DIM, rows), lambda h, words: (h, 0, 0)),
                pl.BlockSpec((HEAD_DIM, CODES), lambda h, words: (h, 0)),
            ]
            + [fixed(item) for item in (codes, sines, cosines, rot_cos, rot_sin, *extra)],
            out_specs=[fixed(item) for item in out_shape],
            scratch_shapes=([pltpu.VMEM(full_shape, F32)] if last else [])
            + [
                pltpu.VMEM((CODES + HEAD_DIM, rows), BF16),
                pltpu.VMEM((rows, rows), BF16),
                pltpu.VMEM((CODES, rows), BF16),
                pltpu.VMEM((HEAD_DIM, rows), F32),
            ],
        ),
        out_shape=out_shape,
        compiler_params=pltpu.CompilerParams(vmem_limit_bytes=VMEM_LIMIT),
        cost_estimate=pl.CostEstimate(
            flops=2 * heads * rows * (rows * 1400 + 200 * width + 128 * CODES),
            bytes_accessed=2 * heads * rows * rows + 12 * rows * width,
            transcendentals=0,
        ),
        name="attention_backward",
    )(
        words,
        *grads,
        *pieces,
        probs,
        att,
        heads_saved,
        box_own,
        codes,
        sines,
        cosines,
        rot_cos,
        rot_sin,
        *extra,
    )


def normed(value):
    centered = value - jnp.mean(value, axis=-1, keepdims=True)
    scale = lax.rsqrt(jnp.mean(centered * centered, axis=-1, keepdims=True) + 1e-05)
    return centered * scale, scale


def norm_back(grad, gain, unit, scale):
    scaled = grad * gain
    return scale * (
        scaled
        - jnp.mean(scaled, axis=-1, keepdims=True)
        - unit * jnp.mean(scaled * unit, axis=-1, keepdims=True)
    )


def column_sum(value):
    return jnp.sum(value, axis=0, keepdims=True)


def middle_kernel(pages, count, span, chunks, *refs):
    total = pages * count
    words_ref = refs[0]
    att_refs = refs[1 : 1 + total]
    (
        tok_ref,
        cot_ref,
        w_out_ref,
        vectors_ref,
        w_expand_ref,
        w_reduce_ref,
    ) = refs[1 + total : 7 + total]
    outs = refs[7 + total :]
    layer_ref, first_in_ref, theirs_ref, mine_ref, more_theirs_ref, more_mine_ref = outs[:6]
    grad_refs = outs[6 : 6 + count]
    (
        sums_ref,
        att_all,
        grad_all,
        unit_one,
        scale_one,
        first_wide,
        first_low,
        first_tall,
        active,
        slope,
        gathered,
        second_in,
        second_low,
    ) = outs[6 + count :]
    rank = words_ref[0]
    width = tok_ref.shape[1]
    block = tok_ref.shape[0] // pages
    step = pl.program_id(0)

    def rows_of(at):
        return pl.ds(pl.multiple_of((rank ^ at) * span, span), span)

    @pl.when(step == 0)
    def _():
        for page in range(pages):
            for at in range(count):
                att_all[rows_of(at), page * block : (page + 1) * block] = att_refs[
                    page * count + at
                ][...]
        branch = dot_tn(att_all[: w_out_ref.shape[0]], w_out_ref[...])
        unit, scale = normed(tok_ref[...].astype(F32) + branch)
        unit_one[...] = unit
        scale_one[...] = jnp.broadcast_to(scale, scale_one.shape)
        first_out = unit * vectors_ref[0:1] + vectors_ref[1:2]
        first_wide[...] = first_out
        first_low[...] = first_out.astype(BF16)
        first_tall[...] = first_out.T.astype(BF16)
        gathered[...] = jnp.zeros_like(gathered)
        sums_ref[...] = jnp.zeros_like(sums_ref)

    for chunk in range(chunks):

        @pl.when(step == chunk)
        def _(chunk=chunk):
            expanded = dot(first_low[...], w_expand_ref[...])
            gate = 0.5 + 0.5 * lax.erf(expanded * np.float32(np.sqrt(0.5)))
            bell = jnp.exp(expanded * expanded * -0.5) * np.float32(1.0 / np.sqrt(2.0 * np.pi))
            low = (expanded * gate).astype(BF16)
            active[chunk] = low
            slope[chunk] = gate + expanded * bell
            gathered[...] += dot(low, w_reduce_ref[...])

    @pl.when(step == chunks - 1)
    def _():
        unit, scale = normed(first_wide[...] + gathered[...])
        layer_ref[...] = (unit * vectors_ref[2:3] + vectors_ref[3:4]).astype(BF16)
        cot = cot_ref[...].astype(F32)
        sums_ref[2:3] = column_sum(cot * unit)
        sums_ref[3:4] = column_sum(cot)
        grad = norm_back(cot, vectors_ref[2:3], unit, scale)
        second_in[...] = grad
        second_low[...] = grad.astype(BF16)
        gathered[...] = grad

    for chunk in range(chunks):

        @pl.when(step == 2 * chunks - 1 - chunk)
        def _(chunk=chunk):
            grad_active = dot_nt(second_low[...], w_reduce_ref[...])
            grad_expanded = (grad_active * slope[chunk]).astype(BF16)
            grads_ref = mine_ref if chunk < chunks // 2 else theirs_ref
            grads_ref[:width] = dot(first_tall[...], grad_expanded).astype(BF16)
            grads_ref[width:] = dot_tn(active[chunk], second_low[...]).astype(BF16)
            gathered[...] += dot_nt(grad_expanded, w_expand_ref[...])

    @pl.when(step == 2 * chunks - 1)
    def _():
        unit = unit_one[...]
        grad_out = gathered[...]
        sums_ref[0:1] = column_sum(grad_out * unit)
        sums_ref[1:2] = column_sum(grad_out)
        grad = norm_back(grad_out, vectors_ref[0:1], unit, scale_one[:, :1])
        first_in_ref[...] = grad
        low = grad.astype(BF16)
        real = w_out_ref.shape[0]
        half = real // 2
        core = words_ref[2]
        for ref, side in ((more_mine_ref, core), (more_theirs_ref, 1 - core)):
            rows = pl.ds(pl.multiple_of(side * half, half), half)
            ref[:half] = dot(att_all[rows], low).astype(BF16)
            ref[half:] = jnp.zeros((ref.shape[0] - half, width), BF16)
            ref[half : half + 16] = sums_ref[...].astype(BF16)
        if grad_all.shape[0] > real:
            grad_all[real:] = jnp.zeros((grad_all.shape[0] - real, low.shape[0]), BF16)
        grad_all[:real] = dot_nt(w_out_ref[...], low).astype(BF16)
        for at in range(count):
            grad_refs[at][...] = grad_all[rows_of(at)]


def middle(words, att_parts, tok, cot, w_out, vectors, w_expand, w_reduce, pages, more):
    rows, width = tok.shape
    count = len(att_parts) // pages
    span, block = att_parts[0].shape
    hidden = w_expand.shape[1]
    chunks = hidden // width
    pairs = chunks // 2

    def whole(array):
        return pl.BlockSpec(array.shape, lambda s, words: (0,) * len(array.shape))

    def chunk_at(s, words):
        at = jnp.minimum(s, 2 * chunks - 1 - s)
        return (at + words[2] * pairs) % chunks

    def theirs_at(s, words):
        return jnp.clip(2 * chunks - 1 - s - pairs, 0, pairs - 1), 0

    def mine_at(s, words):
        return jnp.clip(2 * chunks - 1 - s, 0, pairs - 1), 0

    shapes = [
        jax.ShapeDtypeStruct((rows, width), BF16),
        jax.ShapeDtypeStruct((rows, width), F32),
        jax.ShapeDtypeStruct((hidden, width), BF16),
        jax.ShapeDtypeStruct((hidden, width), BF16),
        jax.ShapeDtypeStruct((more, width), BF16),
        jax.ShapeDtypeStruct((more, width), BF16),
    ] + [jax.ShapeDtypeStruct((span, pages * block), BF16)] * count
    specs = [whole(item) for item in shapes]
    specs[2] = pl.BlockSpec((2 * width, width), theirs_at)
    specs[3] = pl.BlockSpec((2 * width, width), mine_at)
    return pl.pallas_call(
        functools.partial(middle_kernel, pages, count, span, chunks),
        grid_spec=pltpu.PrefetchScalarGridSpec(
            num_scalar_prefetch=1,
            grid=(2 * chunks,),
            in_specs=[whole(item) for item in att_parts]
            + [
                whole(tok),
                whole(cot),
                whole(w_out),
                whole(vectors),
                pl.BlockSpec((width, width), lambda s, words: (0, chunk_at(s, words))),
                pl.BlockSpec((width, width), lambda s, words: (chunk_at(s, words), 0)),
            ],
            out_specs=specs,
            scratch_shapes=[
                pltpu.VMEM((16, width), F32),
                pltpu.VMEM((count * span, rows), BF16),
                pltpu.VMEM((count * span, rows), BF16),
                pltpu.VMEM((rows, width), F32),
                pltpu.VMEM((rows, 128), F32),
                pltpu.VMEM((rows, width), F32),
                pltpu.VMEM((rows, width), BF16),
                pltpu.VMEM((width, rows), BF16),
                pltpu.VMEM((chunks, rows, width), BF16),
                pltpu.VMEM((chunks, rows, width), F32),
                pltpu.VMEM((rows, width), F32),
                pltpu.VMEM((rows, width), F32),
                pltpu.VMEM((rows, width), BF16),
            ],
        ),
        out_shape=shapes,
        compiler_params=pltpu.CompilerParams(vmem_limit_bytes=VMEM_LIMIT),
        cost_estimate=pl.CostEstimate(
            flops=2 * rows * width * (6 * hidden + 3 * width),
            bytes_accessed=8 * width * hidden + 16 * rows * width,
            transcendentals=2 * rows * hidden,
        ),
        name="middle",
    )(words, *att_parts, tok, cot, w_out, vectors, w_expand, w_reduce)


def input_kernel(pages, count, span, base, *refs):
    words_ref = refs[0]
    own_refs = refs[1 : 1 + pages]
    message_refs = refs[1 + pages : pages + count]
    weight_refs = refs[pages + count : 3 + pages + count]
    first_in_ref, out_ref, held = refs[3 + pages + count :]
    rank = words_ref[0]
    width = out_ref.shape[1]
    block = out_ref.shape[0] // pages
    for page in range(pages):
        for at in range(count):
            part = message_refs[at - 1] if at else own_refs[page]
            top = base + page * span if at else 0
            place = pl.multiple_of((rank ^ at) * span, span)
            for kind in range(3):
                held[kind, pl.ds(place, span), page * block : (page + 1) * block] = part[
                    top : top + span, kind * block : (kind + 1) * block
                ]
    total = dot(weight_refs[0][...], held[0, :width])
    for kind in range(1, 3):
        total = total + dot(weight_refs[kind][...], held[kind, :width])
    out_ref[...] = (first_in_ref[...] + total.T).astype(BF16)


def input_gradient(words, own, messages, base, span, weights, first_in):
    pages = len(own)
    count = 1 + len(messages)
    rows, width = first_in.shape
    vmem = pl.BlockSpec(memory_space=pltpu.VMEM)
    return pl.pallas_call(
        functools.partial(input_kernel, pages, count, span, base),
        in_specs=[pl.BlockSpec(memory_space=pltpu.SMEM)] + [vmem] * (pages + count + 3),
        out_specs=vmem,
        out_shape=jax.ShapeDtypeStruct((rows, width), BF16),
        scratch_shapes=[pltpu.VMEM((3, count * span, rows), BF16)],
        compiler_params=pltpu.CompilerParams(vmem_limit_bytes=VMEM_LIMIT),
        cost_estimate=pl.CostEstimate(
            flops=6 * rows * width * count * span,
            bytes_accessed=2 * width * (5 * rows + 3 * count * span),
            transcendentals=0,
        ),
        name="input_gradient",
    )(words, *own, *messages, *weights, first_in)


def local(body, name, words, arrays, shapes, costly=False):
    def kernel(words_ref, *refs):
        body(words_ref, refs[: len(arrays)], refs[len(arrays) :])

    vmem = pl.BlockSpec(memory_space=pltpu.VMEM)
    shapes = [jax.ShapeDtypeStruct(shape, kind) for shape, kind in shapes]
    moved = sum(item.size * item.dtype.itemsize for item in list(arrays) + shapes)
    cost = pl.CostEstimate(flops=0, bytes_accessed=moved, transcendentals=0)
    return pl.pallas_call(
        kernel,
        in_specs=[pl.BlockSpec(memory_space=pltpu.SMEM)] + [vmem] * len(arrays),
        out_specs=[vmem] * len(shapes),
        out_shape=shapes,
        compiler_params=pltpu.CompilerParams(vmem_limit_bytes=VMEM_LIMIT),
        cost_estimate=cost if costly else NO_COST,
        name=name,
    )(words, *arrays)


def shard(index, rows, base=0):
    return pl.ds(pl.multiple_of(base + index * rows, 16), rows)


def total_of(refs, rows=slice(None)):
    total = refs[0][rows].astype(F32)
    for ref in refs[1:]:
        total = total + ref[rows].astype(F32)
    return total


def tree_sum(terms):
    while len(terms) > 1:
        terms = [terms[i] + terms[i + 1] for i in range(0, len(terms), 2)]
    return terms[0]


def bit_of(words, level):
    return lax.shift_right_logical(words[1], level) & 1


def pair_sum(words, mine, other):
    def body(words, ins, outs):
        outs[0][...] = total_of(ins).astype(BF16)

    return local(body, "pair_sum", words, [mine, other], [(mine.shape, BF16)])[0]


def halve(words, level, mine, other):
    rows, width = mine.shape
    half = rows // 2

    def body(words, ins, outs):
        bit = bit_of(words, level)
        outs[0][...] = total_of(ins, shard(bit, half)).astype(BF16)
        outs[1][...] = total_of(ins, shard(1 - bit, half)).astype(BF16)

    return local(body, "halve", words, [mine, other], [((half, width), BF16)] * 2)


def join_halves(words, level, mine, other):
    rows, width = mine.shape

    def body(words, ins, outs):
        bit = bit_of(words, level)
        outs[0][shard(bit, rows)] = ins[0][...]
        outs[0][shard(1 - bit, rows)] = ins[1][...]

    return local(body, "join_halves", words, [mine, other], [((2 * rows, width), BF16)])[0]


def across(block, level):
    return swapped(block, 1 << level, "depth")


class Plan:
    def __init__(self, rows, rows_a, more, span, width):
        self.count = lax.axis_size("blk")
        self.levels = lax.axis_size("depth").bit_length() - 1
        self.rows = rows
        self.rows_a = rows_a
        self.more = more
        self.span = span
        self.width = width
        self.a_ff = rows_a // self.count
        self.a_more = more // self.count
        self.a = self.a_ff + self.a_more
        self.b = (rows - rows_a) >> self.levels

    def shapes(self, *sizes):
        return [((rows, self.width), BF16) for rows in sizes]

    def scatter_one(self, words, halves):
        count, width = self.count, self.width
        a_ff, a_more = self.a_ff, self.a_more
        b_rows = (self.rows - self.rows_a) // count
        steps = count // 2

        def kernel(words_ref, *refs):
            parts = refs[6 : 6 + count]
            keep_ref, send_ref = refs[6 + count :]
            for i in range(count):

                @pl.when(pl.program_id(0) == i)
                def _(i=i):
                    parts[i][:a_ff] = total_of(refs[:2]).astype(BF16)
                    parts[i][a_ff:] = total_of(refs[2:4]).astype(BF16)
                    side = send_ref if i < steps else keep_ref
                    side[...] = total_of(refs[4:6]).astype(BF16)

        def there(rows):
            return pl.BlockSpec((rows, width), lambda i, words: (words[0] ^ i, 0))

        def b_at(i, words):
            bit = bit_of(words, 0)
            side = jnp.where(i < steps, 1 - bit, bit)
            return self.rows_a // b_rows + side * steps + i % steps, 0

        own_b = pl.BlockSpec((b_rows, width), b_at)
        shapes = [jax.ShapeDtypeStruct((self.a, width), BF16)] * count
        shapes += [jax.ShapeDtypeStruct((b_rows * steps, width), BF16)] * 2
        *parts_a, keep, send = pl.pallas_call(
            kernel,
            grid_spec=pltpu.PrefetchScalarGridSpec(
                num_scalar_prefetch=1,
                grid=(count,),
                in_specs=[there(a_ff)] * 2 + [there(a_more)] * 2 + [own_b] * 2,
                out_specs=[fixed(item) for item in shapes[:count]]
                + [
                    pl.BlockSpec((b_rows, width), lambda i, words: (jnp.maximum(i - steps, 0), 0)),
                    pl.BlockSpec((b_rows, width), lambda i, words: (jnp.minimum(i, steps - 1), 0)),
                ],
            ),
            out_shape=shapes,
            compiler_params=pltpu.CompilerParams(vmem_limit_bytes=VMEM_LIMIT),
            cost_estimate=NO_COST,
            name="scatter_one",
        )(words, *halves, *halves[:2])
        return [from_blk(part, i) for i, part in enumerate(parts_a)], keep, across(send, 0)

    def scatter_two(self, words, parts_a, keep_b, other_b, pages):
        count = self.count
        half = self.a // 2

        def body(words, ins, outs):
            bit = bit_of(words, 0)
            outs[0][...] = total_of(ins[:count], shard(bit, half)).astype(BF16)
            outs[1][...] = total_of(ins[:count], shard(1 - bit, half)).astype(BF16)
            part_b = total_of(ins[count : count + 2]).astype(BF16)
            outs[2][...] = part_b
            for i, out in enumerate(outs[3:]):
                out[: self.b] = part_b
                for page in range(len(pages)):
                    piece = ins[count + 2 + page * (count - 1) + i]
                    base = self.b + page * self.span
                    out[base : base + self.span, : piece.shape[1]] = piece[...]

        message = self.b + len(pages) * self.span
        shapes = self.shapes(half, half, self.b, *[message] * (count - 1))
        pieces = [piece for page in pages for piece in page[1:]]
        keep, send, part_b, *messages = local(
            body, "scatter_two", words, [*parts_a, keep_b, other_b, *pieces], shapes
        )
        return (
            keep,
            across(send, 0),
            part_b,
            [from_blk(item, i + 1) for i, item in enumerate(messages)],
        )

    def sum_b(self, words, part_b, messages):
        def body(words, ins, outs):
            terms = [ref[: self.b].astype(F32) for ref in ins]
            outs[0][...] = tree_sum(terms).astype(BF16)

        return local(body, "sum_b", words, [part_b, *messages], self.shapes(self.b))[0]

    def gather_b(self, words, part_b):
        for level in range(self.levels - 1, 0, -1):
            part_b = join_halves(words, level, part_b, across(part_b, level))
        return part_b, across(part_b, 0)

    def join(self, words, parts_a, parts_b):
        def body(words, ins, outs):
            for i in range(self.count):
                outs[0][shard(words[0] ^ i, self.a_ff)] = ins[i][: self.a_ff]
                outs[1][shard(words[0] ^ i, self.a_more)] = ins[i][self.a_ff : self.a]
            bit = bit_of(words, 0)
            half = ins[self.count].shape[0]
            outs[0][shard(bit, half, self.rows_a)] = ins[self.count][...]
            outs[0][shard(1 - bit, half, self.rows_a)] = ins[self.count + 1][...]

        shapes = self.shapes(self.rows, self.more)
        return local(body, "join", words, [*parts_a, *parts_b], shapes, True)


def widened(words, half, side, hidden, before=()):
    width = half.shape[1]
    chunks = hidden // width
    pairs = chunks // 2

    def kernel(words_ref, half_ref, *refs):
        expand_ref, reduce_ref = refs[len(before) :]
        expand_ref[...] = half_ref[:width].astype(F32)
        reduce_ref[...] = half_ref[width:].astype(F32)

    def place(s, words):
        return (s + (words[2] + side) * pairs) % chunks

    return pl.pallas_call(
        kernel,
        grid_spec=pltpu.PrefetchScalarGridSpec(
            num_scalar_prefetch=1,
            grid=(pairs,),
            in_specs=[pl.BlockSpec((2 * width, width), lambda s, words: (s, 0))]
            + [pl.BlockSpec(memory_space=pl.ANY)] * len(before),
            out_specs=[
                pl.BlockSpec((width, width), lambda s, words: (0, place(s, words))),
                pl.BlockSpec((width, width), lambda s, words: (place(s, words), 0)),
            ],
        ),
        out_shape=[
            jax.ShapeDtypeStruct((width, hidden), F32),
            jax.ShapeDtypeStruct((hidden, width), F32),
        ],
        input_output_aliases={2: 0, 3: 1} if before else {},
        compiler_params=pltpu.CompilerParams(vmem_limit_bytes=VMEM_LIMIT),
        cost_estimate=pl.CostEstimate(
            flops=0, bytes_accessed=6 * hidden * width, transcendentals=0
        ),
        name="widen",
    )(words, half, *before)


def join_blk(words, parts):
    half, width = parts[0].shape

    def body(words, ins, outs):
        for i in range(len(parts)):
            outs[0][shard(words[0] ^ i, half)] = ins[i][...]

    return local(body, "heads_join", words, parts, [((len(parts) * half, width), BF16)])[0]


def finish_kernel(count, span, half, words_ref, *refs):
    own_ref, other_ref, more_ref, more_other_ref = refs[:4]
    query_ref, key_ref, value_ref, project_ref, box_ref, sums_ref = refs[4:]
    width = query_ref.shape[0]

    def write(lower_ref, upper_ref, more_lower_ref, more_upper_ref):
        def grad(ref, part):
            rows = [
                ref[(2 * i + part) * span : (2 * i + part + 1) * span].astype(F32)
                for i in range(count)
            ]
            return jnp.concatenate(rows, axis=0)[:width].T

        query_ref[...] = grad(lower_ref, 0)
        key_ref[...] = grad(lower_ref, 1)
        value_ref[...] = grad(upper_ref, 0)
        box_ref[...] = entry_order(grad(upper_ref, 1))
        project_ref[:half] = more_lower_ref[:half].astype(F32)
        project_ref[half:] = more_upper_ref[:half].astype(F32)
        sums_ref[...] = more_lower_ref[half : half + 16].astype(F32)[:8]

    @pl.when(words_ref[2] == 0)
    def _():
        write(own_ref, other_ref, more_ref, more_other_ref)

    @pl.when(words_ref[2] == 1)
    def _():
        write(other_ref, own_ref, more_other_ref, more_ref)


def finished(words, own, other, more, more_other, span, width):
    count = lax.axis_size("blk")
    vmem = pl.BlockSpec(memory_space=pltpu.VMEM)
    shapes = [jax.ShapeDtypeStruct((width, width), F32)] * 5
    shapes.append(jax.ShapeDtypeStruct((8, width), F32))
    return pl.pallas_call(
        functools.partial(finish_kernel, count, span, width // 2),
        in_specs=[pl.BlockSpec(memory_space=pltpu.SMEM)] + [vmem] * 4,
        out_specs=[vmem] * 6,
        out_shape=shapes,
        compiler_params=pltpu.CompilerParams(vmem_limit_bytes=VMEM_LIMIT),
        cost_estimate=NO_COST,
        name="finish",
    )(words, own, other, more, more_other)


def per_device(
    tokens,
    boxes,
    w_query,
    w_key,
    w_value,
    w_output,
    box_weight,
    first_gain,
    first_shift,
    w_expand,
    w_reduce,
    second_gain,
    second_shift,
    cotangent,
):
    pages, block, width = tokens.shape
    count = lax.axis_size("blk")
    depth = lax.axis_size("depth")
    words = jnp.stack(
        [lax.axis_index("blk"), lax.axis_index("depth"), lax.axis_index("core")]
    ).astype(jnp.int32)
    hidden = w_expand.shape[1]
    span = -(-HEADS // count) * HEAD_DIM
    unit = 16 * count * depth
    more = -(-(width // 2 + 16) // unit) * unit

    own_places = jnp.stack([boxes[0] + boxes[2], boxes[1] + boxes[3]], axis=1)
    own_places = jnp.stack([lax.shift_right_logical(own_places, 6), own_places & 63], axis=2)
    own_places = own_places.reshape(4 * pages, block).astype(BF16)
    own_places = jnp.pad(own_places, ((0, 16 - 4 * pages), (0, width - block)))
    message = jnp.concatenate([tokens[0], own_places])
    messages = [from_blk(message, i) for i in range(count)]
    w_own, box_own, rot_cos, rot_sin = prepare(
        words, w_query, w_key, w_value, box_weight, span, count * block
    )
    messages, rot_cos = lax.optimization_barrier((messages, rot_cos))
    own = after(messages, tokens[1])
    pieces = [messages, [from_blk(own, i) for i in range(count)]]

    saved = []
    att_parts = []
    for page in range(pages):
        results = attention_forward(
            words, page, messages, pieces[page], w_own, box_own, rot_cos, rot_sin
        )
        saved.append(results[:6])
        att_parts += [from_blk(results[6 + i], i) for i in range(count)]

    vectors = jnp.stack([first_gain, first_shift, second_gain, second_shift])
    results = middle(
        words,
        att_parts,
        tokens.reshape(pages * block, width),
        cotangent.reshape(pages * block, width),
        w_output,
        vectors,
        w_expand,
        w_reduce,
        pages,
        more,
    )
    layer_out, first_in, theirs, mine, more_theirs, more_mine = results[:6]
    grads = [from_blk(results[6 + i], i) for i in range(count)]
    plan = Plan(hidden, 2 * hidden // 3, more, span, width)
    parts_a, keep_b, other_b = plan.scatter_one(
        after(grads[:2], words), [mine, from_core(theirs), more_mine, from_core(more_theirs)]
    )

    def backward(page, words, before=None):
        return attention_backward(
            words,
            page,
            grads,
            pieces[page],
            saved[page],
            box_own,
            rot_cos,
            rot_sin,
            before,
        )

    *pre_one, before = backward(0, after(parts_a[0], words))
    done = before
    for level in range(1, plan.levels):
        keep_b, send_b = halve(after(done, words), level, keep_b, other_b)
        other_b = across(send_b, level)
        done = keep_b
    *pre_two, heads_mine, heads_theirs = backward(1, after(done, words), before)
    own = [pre_one[0], pre_two[0]]
    part_a, other_a, part_b, messages_b = plan.scatter_two(
        after(heads_mine, words), parts_a, keep_b, other_b, [pre_one, pre_two]
    )
    heads = pair_sum(
        after(part_a, words), heads_mine, from_core(after(part_a, heads_theirs))
    )
    other = across(heads, 0)
    part_a = pair_sum(after(heads, words), part_a, other_a)
    done = part_a
    for level in range(1, plan.levels):
        part_a = pair_sum(after(done, words), part_a, across(part_a, level))
        done = part_a
    other_a = across(part_a, 0)
    heads = pair_sum(after(done, words), heads, other)
    done = heads
    other = across(heads, 1)
    part_b = plan.sum_b(after(done, words), part_b, messages_b)
    part_a = join_halves(after(part_b, words), 0, part_a, other_a)
    parts_a = [from_blk(part_a, i) for i in range(count)]
    heads = pair_sum(after(part_a, words), heads, other)
    for level in range(2, plan.levels):
        heads = pair_sum(words, heads, across(heads, level))
    parts_b = plan.gather_b(after(heads, words), part_b)
    parts_a, heads = lax.optimization_barrier((parts_a, heads))
    heads = [from_blk(heads, i) for i in range(count)]
    ff, extra = plan.join(words, parts_a, parts_b)
    ff_other, extra_other = from_core(ff), from_core(extra)
    wide = widened(words, ff, 0, hidden)
    input_grad = input_gradient(
        after(wide[0], words),
        own,
        messages_b,
        plan.b,
        span,
        (w_query, w_key, w_value),
        first_in,
    )
    grad_expand, grad_reduce = widened(after(input_grad, words), ff_other, 1, hidden, wide)
    heads_own = join_blk(after(grad_expand, words), heads)
    heads_other = from_core(heads_own)
    grad_query, grad_key, grad_value, grad_project, grad_box, sums = finished(
        words, heads_own, heads_other, extra, extra_other, span, width
    )
    return (
        layer_out.reshape(tokens.shape),
        input_grad.reshape(tokens.shape),
        grad_query,
        grad_key,
        grad_value,
        grad_project,
        grad_box,
        sums[0],
        sums[1],
        grad_expand,
        grad_reduce,
        sums[2],
        sums[3],
    )


def solution(mesh):
    blocks, rest = mesh.devices.shape
    parts = jax.sharding.Mesh(
        mesh.devices.reshape(blocks, rest // 2, 2), ("blk", "depth", "core")
    )
    split = P(("depth", "core"), "blk", None)
    return jax.shard_map(
        per_device,
        mesh=parts,
        in_specs=(split, P(None, ("depth", "core"), "blk")) + (P(),) * 11 + (split,),
        out_specs=(split, split) + (P(),) * 11,
        check_vma=False,
    )
```

```python
import functools

import jax
import jax.numpy as jnp
import numpy as np
from jax import lax
from jax.experimental import pallas as pl
from jax.experimental.pallas import tpu as pltpu
from jax.sharding import PartitionSpec as P

HEADS = 12
HEAD_DIM = 64
HALF = 32
FREQS = 192
CODES = 4 * FREQS
VMEM_LIMIT = 60 * 1024 * 1024
NO_COST = pl.CostEstimate(flops=0, bytes_accessed=0, transcendentals=0)
F32 = jnp.float32
BF16 = jnp.bfloat16


def dot(left, right):
    return lax.dot_general(left, right, (((1,), (0,)), ((), ())), preferred_element_type=F32)


def dot_nt(left, right):
    return lax.dot_general(left, right, (((1,), (1,)), ((), ())), preferred_element_type=F32)


def dot_tn(left, right):
    return lax.dot_general(left, right, (((0,), (0,)), ((), ())), preferred_element_type=F32)


def swapped(block, distance, axis="blk"):
    count = lax.axis_size(axis)
    return lax.ppermute(block, axis, [(i, i ^ distance) for i in range(count)])


def from_blk(block, distance):
    return swapped(block, distance) if distance else block


def from_core(block):
    return swapped(block, 1, "core")


def after(done, value):
    return lax.optimization_barrier((value, done))[0]


def turned(upper, lower, cosines, sines):
    return upper * cosines - lower * sines, lower * cosines + upper * sines


def entry_order(rows):
    return jnp.concatenate(
        [
            rows[:FREQS],
            rows[2 * FREQS : 3 * FREQS],
            rows[FREQS : 2 * FREQS],
            rows[3 * FREQS :],
        ],
        axis=0,
    )


def angle_tables():
    rates = np.float32(10000.0) ** (-np.arange(FREQS, dtype=np.float32) / np.float32(FREQS))
    tables = []
    for places in (32.0 * np.arange(32), 0.5 * np.arange(64)):
        angles = rates.astype(np.float64)[:, None] * places[None, :]
        left = np.concatenate([np.sin(angles), np.cos(angles)])
        parts = []
        for _ in range(3):
            parts.append(left.astype(jnp.bfloat16))
            left = left - parts[-1].astype(np.float64)
        tables.append(np.concatenate(parts, axis=1))
    return tables


def rotary_tables(length):
    rates = np.float32(10000.0) ** (-np.arange(HALF, dtype=np.float32) / np.float32(HALF))
    angles = np.arange(length, dtype=np.float32)[None, :] * rates[:, None]
    angles = angles.astype(np.float64)
    return np.cos(angles).astype(np.float32), np.sin(angles).astype(np.float32)


def prepare_kernel(
    words_ref,
    query_ref,
    key_ref,
    value_ref,
    box_ref,
    cos_ref,
    sin_ref,
    own_ref,
    own_box_ref,
    own_cos_ref,
    own_sin_ref,
):
    rank = words_ref[0]
    span = own_box_ref.shape[0]
    width = query_ref.shape[1]
    count = lax.axis_size("blk")
    block = cos_ref.shape[1] // count
    row = lax.broadcasted_iota(jnp.int32, (span, width), 0) + rank * span
    column = lax.broadcasted_iota(jnp.int32, (span, width), 1)
    pick = jnp.where(row == column, 1.0, 0.0).astype(BF16)
    for kind, ref in enumerate((query_ref, key_ref, value_ref)):
        own_ref[kind * span : (kind + 1) * span] = dot_nt(pick, ref[...]).astype(BF16)
    own_box_ref[...] = dot_nt(pick, entry_order(box_ref[...])).astype(BF16)
    for i in range(count):
        from_cols = pl.ds(pl.multiple_of((rank ^ i) * block, block), block)
        own_cos_ref[:, i * block : (i + 1) * block] = cos_ref[:, from_cols]
        own_sin_ref[:, i * block : (i + 1) * block] = sin_ref[:, from_cols]


def prepare(words, w_query, w_key, w_value, box_weight, span, length):
    width = w_query.shape[0]
    vmem = pl.BlockSpec(memory_space=pltpu.VMEM)
    return pl.pallas_call(
        prepare_kernel,
        in_specs=[pl.BlockSpec(memory_space=pltpu.SMEM)] + [vmem] * 6,
        out_specs=[vmem] * 4,
        out_shape=[
            jax.ShapeDtypeStruct((3 * span, width), BF16),
            jax.ShapeDtypeStruct((span, CODES), BF16),
            jax.ShapeDtypeStruct((HALF, length), F32),
            jax.ShapeDtypeStruct((HALF, length), F32),
        ],
        compiler_params=pltpu.CompilerParams(vmem_limit_bytes=VMEM_LIMIT),
        cost_estimate=pl.CostEstimate(
            flops=8 * span * width * width, bytes_accessed=10 * width * width, transcendentals=0
        ),
        name="prepare",
    )(words, w_query, w_key, w_value, box_weight, *map(jnp.asarray, rotary_tables(length)))


def fold(value, combine):
    while value.shape[0] > 8:
        half = value.shape[0] // 2
        value = combine(value[:half], value[half:])
    return value


def write_codes(page, place_refs, high_ref, low_ref, sin_ref, cos_ref, codes_ref):
    block = sin_ref.shape[1] // len(place_refs)

    def looked_up(table_ref, index):
        spots = table_ref.shape[1] // 3
        rows = lax.broadcasted_iota(jnp.int32, (spots, block), 0).astype(F32)
        once = jnp.where(rows == index, 1.0, 0.0)
        found = dot(table_ref[...], jnp.concatenate([once] * 3, axis=0).astype(BF16))
        return found[:FREQS], found[FREQS:]

    for i, place_ref in enumerate(place_refs):
        columns = slice(i * block, (i + 1) * block)
        places = place_ref[:, :block].astype(F32)
        for axis in range(2):
            at = 4 * page + 2 * axis
            high_sin, high_cos = looked_up(high_ref, places[at : at + 1])
            low_sin, low_cos = looked_up(low_ref, places[at + 1 : at + 2])
            sines = high_sin * low_cos + high_cos * low_sin
            cosines = high_cos * low_cos - high_sin * low_sin
            rows = slice(axis * FREQS, (axis + 1) * FREQS)
            later = slice((2 + axis) * FREQS, (3 + axis) * FREQS)
            sin_ref[rows, columns] = sines
            cos_ref[rows, columns] = cosines
            codes_ref[rows, columns] = sines.astype(BF16)
            codes_ref[later, columns] = cosines.astype(BF16)


def forward_kernel(page, count, words_ref, *refs):
    place_refs, refs = refs[:count], refs[count:]
    piece_refs, refs = refs[:count], refs[count:]
    high_ref, low_ref, w_ref, box_ref, rot_cos_ref, rot_sin_ref = refs[:6]
    probs_ref, att_ref, heads_ref, sin_ref, cos_ref, codes_ref = refs[6:12]
    low_refs = refs[12 : 12 + count]
    tok_ref, pre_ref, kc_ref, qr_ref = refs[12 + count :]
    rows = tok_ref.shape[0]
    block = rows // count
    head = pl.program_id(0)
    span = pl.num_programs(0) * HEAD_DIM

    @pl.when(head == 0)
    def _():
        for i in range(count):
            tok_ref[i * block : (i + 1) * block] = piece_refs[i][...]
        pre_ref[...] = dot_nt(w_ref[...], tok_ref[...])
        write_codes(page, place_refs, high_ref, low_ref, sin_ref, cos_ref, codes_ref)
        kc_ref[:, :CODES] = codes_ref[...].astype(F32).T.astype(BF16)

    def pre(kind):
        at = kind * span + head * HEAD_DIM
        return pre_ref[pl.ds(pl.multiple_of(at, HEAD_DIM), HEAD_DIM)]

    rot_cos = rot_cos_ref[...]
    rot_sin = rot_sin_ref[...]
    query_pre = pre(0).astype(BF16)
    wide = query_pre.astype(F32)
    query = jnp.concatenate(turned(wide[:HALF], wide[HALF:], rot_cos, rot_sin), axis=0)
    key_pre = pre(1)
    key = jnp.concatenate(turned(key_pre[:HALF], key_pre[HALF:], rot_cos, rot_sin), axis=0)
    value = pre(2).astype(BF16)
    heads_ref[0, :HEAD_DIM] = query_pre
    heads_ref[0, HEAD_DIM : 2 * HEAD_DIM] = query.astype(BF16)
    heads_ref[0, 2 * HEAD_DIM : 3 * HEAD_DIM] = key.astype(BF16)
    heads_ref[0, 3 * HEAD_DIM :] = value
    kc_ref[:, CODES:] = key.T.astype(BF16)
    qr_ref[CODES:] = (query * 0.125).astype(BF16)
    step = min(256, block)

    def logits_at(at):
        part = slice(at, at + step)
        projected = dot_tn(box_ref[...], query_pre[:, part])
        sines = sin_ref[:, part]
        cosines = cos_ref[:, part]
        upper = projected[: 2 * FREQS]
        lower = projected[2 * FREQS :]
        qr_ref[: 2 * FREQS, part] = ((upper * cosines + lower * sines) * 0.125).astype(BF16)
        qr_ref[2 * FREQS : CODES, part] = ((lower * cosines - upper * sines) * 0.125).astype(BF16)
        return dot(kc_ref[...], qr_ref[:, part])

    following = logits_at(0)
    for at in range(0, rows, step):
        logits = following
        if at + step < rows:
            following = logits_at(at + step)
        peak = jnp.max(fold(logits, jnp.maximum), axis=0, keepdims=True)
        weight = jnp.exp(logits - peak)
        total = jnp.sum(fold(weight, jnp.add), axis=0, keepdims=True)
        probs = (weight * (1.0 / total)).astype(BF16)
        probs_ref[0, :, at : at + step] = probs
        attended = dot(value, probs)
        att_ref[0, :, at : at + step] = attended
        inner = at % block
        low_refs[at // block][:, inner : inner + step] = attended.astype(BF16)


def fixed(array):
    return pl.BlockSpec(array.shape, lambda *at: (0,) * len(array.shape))


def attention_forward(words, page, messages, pieces, w_own, box_own, rot_cos, rot_sin):
    count = len(messages)
    block, width = messages[0].shape[0] - 16, messages[0].shape[1]
    rows = count * block
    span = box_own.shape[0]
    heads = span // HEAD_DIM
    tables = [jnp.asarray(item) for item in angle_tables()]
    specs = [pl.BlockSpec((block, width), lambda h, words: (0, 0))] * count
    places = pl.BlockSpec((16, width), lambda h, words: (block // 16, 0))
    out_shape = [
        jax.ShapeDtypeStruct((heads, rows, rows), BF16),
        jax.ShapeDtypeStruct((heads, HEAD_DIM, rows), F32),
        jax.ShapeDtypeStruct((heads, 4 * HEAD_DIM, rows), BF16),
        jax.ShapeDtypeStruct((2 * FREQS, rows), F32),
        jax.ShapeDtypeStruct((2 * FREQS, rows), F32),
        jax.ShapeDtypeStruct((CODES, rows), BF16),
    ] + [jax.ShapeDtypeStruct((span, block), BF16)] * count
    return pl.pallas_call(
        functools.partial(forward_kernel, page, count),
        grid_spec=pltpu.PrefetchScalarGridSpec(
            num_scalar_prefetch=1,
            grid=(heads,),
            in_specs=[places] * count
            + specs
            + [fixed(item) for item in (*tables, w_own)]
            + [
                pl.BlockSpec((HEAD_DIM, CODES), lambda h, words: (h, 0)),
                fixed(rot_cos),
                fixed(rot_sin),
            ],
            out_specs=[
                pl.BlockSpec((1, rows, rows), lambda h, words: (h, 0, 0)),
                pl.BlockSpec((1, HEAD_DIM, rows), lambda h, words: (h, 0, 0)),
                pl.BlockSpec((1, 4 * HEAD_DIM, rows), lambda h, words: (h, 0, 0)),
            ]
            + [fixed(item) for item in out_shape[3:6]]
            + [pl.BlockSpec((HEAD_DIM, block), lambda h, words: (h, 0))] * count,
            scratch_shapes=[
                pltpu.VMEM((rows, width), BF16),
                pltpu.VMEM((3 * span, rows), F32),
                pltpu.VMEM((rows, CODES + HEAD_DIM), BF16),
                pltpu.VMEM((CODES + HEAD_DIM, rows), BF16),
            ],
        ),
        out_shape=out_shape,
        compiler_params=pltpu.CompilerParams(vmem_limit_bytes=VMEM_LIMIT),
        cost_estimate=pl.CostEstimate(
            flops=2 * heads * rows * (rows * 1100 + 200 * width + 64 * CODES),
            bytes_accessed=2 * heads * rows * rows + 12 * rows * width,
            transcendentals=heads * rows * rows,
        ),
        name="attention_forward",
    )(words, *messages, *pieces, *tables, w_own, box_own, rot_cos, rot_sin)


def backward_kernel(count, last, words_ref, *refs):
    grad_refs, refs = refs[:count], refs[count:]
    piece_refs, refs = refs[:count], refs[count:]
    probs_ref, att_ref, heads_ref, box_ref, codes_ref, sin_ref, cos_ref = refs[:7]
    rot_cos_ref, rot_sin_ref = refs[7:9]
    refs = refs[9:]
    if last:
        before_ref, refs = refs[0], refs[1:]
    pre_refs, refs = refs[:count], refs[count:]
    if last:
        mine_ref, theirs_ref, *refs = refs
    weight_grad_ref, kc_ref, logit_grad_ref, entry_grad_ref, turned_ref = refs
    block, width = piece_refs[0].shape
    rows = count * block
    head = pl.program_id(0)
    span = pl.num_programs(0) * HEAD_DIM

    @pl.when(head == 0)
    def _():
        kc_ref[:CODES] = codes_ref[...]

    kc_ref[CODES:] = heads_ref[0, 2 * HEAD_DIM : 3 * HEAD_DIM]
    packed = heads_ref[0].astype(F32).T.astype(BF16)
    query_pre = packed[:, :HEAD_DIM]
    query = packed[:, HEAD_DIM : 2 * HEAD_DIM]
    value = packed[:, 3 * HEAD_DIM :] * jnp.asarray(0.125, BF16)
    rot_cos = rot_cos_ref[...]
    rot_sin = rot_sin_ref[...]
    grad = jnp.concatenate([ref[...] for ref in grad_refs], axis=1)
    grad_tall = grad.astype(F32).T.astype(BF16)
    offsets = jnp.sum(grad.astype(F32) * att_ref[0], axis=0, keepdims=True) * 0.125
    step = min(256, block)
    place = pl.multiple_of(head * HEAD_DIM, HEAD_DIM)
    here = pl.ds(place, HEAD_DIM)

    def logits_back(at):
        part = slice(at, at + step)
        grad_probs = dot(value, grad[:, part])
        logit_grad_ref[:, part] = (
            probs_ref[0, :, part].astype(F32) * (grad_probs - offsets[:, part])
        ).astype(BF16)

    logits_back(0)
    for at in range(0, rows, step):
        if at + step < rows:
            logits_back(at + step)
        part = slice(at, at + step)
        back = dot(kc_ref[...], logit_grad_ref[:, part])
        sines = sin_ref[:, part]
        cosines = cos_ref[:, part]
        upper = back[: 2 * FREQS]
        lower = back[2 * FREQS : CODES]
        entry_grad_ref[: 2 * FREQS, part] = (upper * cosines - lower * sines).astype(BF16)
        entry_grad_ref[2 * FREQS :, part] = (lower * cosines + upper * sines).astype(BF16)
        first = back[CODES : CODES + HALF]
        second = back[CODES + HALF :]
        turned_ref[:HALF, part], turned_ref[HALF:, part] = turned(
            first, second, rot_cos[:, part], -rot_sin[:, part]
        )
    key_flat = dot(logit_grad_ref[...], query).T
    value_low = dot(probs_ref[0], grad_tall).T.astype(BF16)
    query_low = (turned_ref[...] + dot(box_ref[...], entry_grad_ref[...])).astype(BF16)
    key_low = jnp.concatenate(
        turned(key_flat[:HALF], key_flat[HALF:], rot_cos, -rot_sin), axis=0
    ).astype(BF16)
    for i in range(count):
        columns = slice(i * block, (i + 1) * block)
        pre_refs[i][here, :block] = query_low[:, columns]
        pre_refs[i][here, block : 2 * block] = key_low[:, columns]
        pre_refs[i][here, 2 * block :] = value_low[:, columns]
    weight_grad_ref[pl.ds(3 * span + place, HEAD_DIM)] = dot(entry_grad_ref[...], query_pre).T

    @pl.when(head == pl.num_programs(0) - 1)
    def _():
        for kind in range(3):
            columns = slice(kind * block, (kind + 1) * block)
            total = dot(pre_refs[0][:, columns], piece_refs[0][...])
            for i in range(1, count):
                total = total + dot(pre_refs[i][:, columns], piece_refs[i][...])
            weight_grad_ref[kind * span : (kind + 1) * span] = total
        if last:
            half = 2 * span
            core = words_ref[2]
            ours = pl.ds(pl.multiple_of(core * half, half), half)
            there = pl.ds(pl.multiple_of((1 - core) * half, half), half)
            mine_ref[...] = weight_grad_ref[ours] + before_ref[ours]
            theirs_ref[...] = (weight_grad_ref[there] + before_ref[there]).astype(BF16)


def attention_backward(
    words, page, grads, pieces, saved, box_own, rot_cos, rot_sin, before=None
):
    probs, att, heads_saved, sines, cosines, codes = saved
    count = len(pieces)
    rows, width = probs.shape[1], pieces[0].shape[1]
    block = rows // count
    span = box_own.shape[0]
    heads = span // HEAD_DIM
    last = before is not None
    extra = (before,) if last else ()
    full_shape = (4 * span, width)
    specs = [pl.BlockSpec((block, width), lambda h, words: (0, 0))] * count
    out_shape = [jax.ShapeDtypeStruct((span, 3 * block), BF16)] * count
    if last:
        out_shape += [
            jax.ShapeDtypeStruct((2 * span, width), F32),
            jax.ShapeDtypeStruct((2 * span, width), BF16),
        ]
    else:
        out_shape.append(jax.ShapeDtypeStruct(full_shape, F32))
    return pl.pallas_call(
        functools.partial(backward_kernel, count, last),
        grid_spec=pltpu.PrefetchScalarGridSpec(
            num_scalar_prefetch=1,
            grid=(heads,),
            in_specs=[pl.BlockSpec((HEAD_DIM, block), lambda h, words: (h, page))] * count
            + specs
            + [
                pl.BlockSpec((1, rows, rows), lambda h, words: (h, 0, 0)),
                pl.BlockSpec((1, HEAD_DIM, rows), lambda h, words: (h, 0, 0)),
                pl.BlockSpec((1, 4 * HEAD_DIM, rows), lambda h, words: (h, 0, 0)),
                pl.BlockSpec((HEAD_DIM, CODES), lambda h, words: (h, 0)),
            ]
            + [fixed(item) for item in (codes, sines, cosines, rot_cos, rot_sin, *extra)],
            out_specs=[fixed(item) for item in out_shape],
            scratch_shapes=([pltpu.VMEM(full_shape, F32)] if last else [])
            + [
                pltpu.VMEM((CODES + HEAD_DIM, rows), BF16),
                pltpu.VMEM((rows, rows), BF16),
                pltpu.VMEM((CODES, rows), BF16),
                pltpu.VMEM((HEAD_DIM, rows), F32),
            ],
        ),
        out_shape=out_shape,
        compiler_params=pltpu.CompilerParams(vmem_limit_bytes=VMEM_LIMIT),
        cost_estimate=pl.CostEstimate(
            flops=2 * heads * rows * (rows * 1400 + 200 * width + 128 * CODES),
            bytes_accessed=2 * heads * rows * rows + 12 * rows * width,
            transcendentals=0,
        ),
        name="attention_backward",
    )(
        words,
        *grads,
        *pieces,
        probs,
        att,
        heads_saved,
        box_own,
        codes,
        sines,
        cosines,
        rot_cos,
        rot_sin,
        *extra,
    )


def normed(value):
    centered = value - jnp.mean(value, axis=-1, keepdims=True)
    scale = lax.rsqrt(jnp.mean(centered * centered, axis=-1, keepdims=True) + 1e-05)
    return centered * scale, scale


def norm_back(grad, gain, unit, scale):
    scaled = grad * gain
    return scale * (
        scaled
        - jnp.mean(scaled, axis=-1, keepdims=True)
        - unit * jnp.mean(scaled * unit, axis=-1, keepdims=True)
    )


def column_sum(value):
    return jnp.sum(value, axis=0, keepdims=True)


def middle_kernel(pages, count, span, chunks, *refs):
    total = pages * count
    words_ref = refs[0]
    att_refs = refs[1 : 1 + total]
    (
        tok_ref,
        cot_ref,
        w_out_ref,
        vectors_ref,
        w_expand_ref,
        w_reduce_ref,
    ) = refs[1 + total : 7 + total]
    outs = refs[7 + total :]
    layer_ref, first_in_ref, theirs_ref, mine_ref, more_theirs_ref, more_mine_ref = outs[:6]
    grad_refs = outs[6 : 6 + count]
    (
        sums_ref,
        att_all,
        grad_all,
        unit_one,
        scale_one,
        first_wide,
        first_low,
        first_tall,
        active,
        slope,
        gathered,
        second_in,
        second_low,
    ) = outs[6 + count :]
    rank = words_ref[0]
    width = tok_ref.shape[1]
    block = tok_ref.shape[0] // pages
    step = pl.program_id(0)

    def rows_of(at):
        return pl.ds(pl.multiple_of((rank ^ at) * span, span), span)

    @pl.when(step == 0)
    def _():
        for page in range(pages):
            for at in range(count):
                att_all[rows_of(at), page * block : (page + 1) * block] = att_refs[
                    page * count + at
                ][...]
        branch = dot_tn(att_all[: w_out_ref.shape[0]], w_out_ref[...])
        unit, scale = normed(tok_ref[...].astype(F32) + branch)
        unit_one[...] = unit
        scale_one[...] = jnp.broadcast_to(scale, scale_one.shape)
        first_out = unit * vectors_ref[0:1] + vectors_ref[1:2]
        first_wide[...] = first_out
        first_low[...] = first_out.astype(BF16)
        first_tall[...] = first_out.T.astype(BF16)
        gathered[...] = jnp.zeros_like(gathered)
        sums_ref[...] = jnp.zeros_like(sums_ref)

    for chunk in range(chunks):

        @pl.when(step == chunk)
        def _(chunk=chunk):
            expanded = dot(first_low[...], w_expand_ref[...])
            gate = 0.5 + 0.5 * lax.erf(expanded * np.float32(np.sqrt(0.5)))
            bell = jnp.exp(expanded * expanded * -0.5) * np.float32(1.0 / np.sqrt(2.0 * np.pi))
            low = (expanded * gate).astype(BF16)
            active[chunk] = low
            slope[chunk] = gate + expanded * bell
            gathered[...] += dot(low, w_reduce_ref[...])

    @pl.when(step == chunks - 1)
    def _():
        unit, scale = normed(first_wide[...] + gathered[...])
        layer_ref[...] = (unit * vectors_ref[2:3] + vectors_ref[3:4]).astype(BF16)
        cot = cot_ref[...].astype(F32)
        sums_ref[2:3] = column_sum(cot * unit)
        sums_ref[3:4] = column_sum(cot)
        grad = norm_back(cot, vectors_ref[2:3], unit, scale)
        second_in[...] = grad
        second_low[...] = grad.astype(BF16)
        gathered[...] = grad

    for chunk in range(chunks):

        @pl.when(step == 2 * chunks - 1 - chunk)
        def _(chunk=chunk):
            grad_active = dot_nt(second_low[...], w_reduce_ref[...])
            grad_expanded = (grad_active * slope[chunk]).astype(BF16)
            grads_ref = mine_ref if chunk < chunks // 2 else theirs_ref
            grads_ref[:width] = dot(first_tall[...], grad_expanded).astype(BF16)
            grads_ref[width:] = dot_tn(active[chunk], second_low[...]).astype(BF16)
            gathered[...] += dot_nt(grad_expanded, w_expand_ref[...])

    @pl.when(step == 2 * chunks - 1)
    def _():
        unit = unit_one[...]
        grad_out = gathered[...]
        sums_ref[0:1] = column_sum(grad_out * unit)
        sums_ref[1:2] = column_sum(grad_out)
        grad = norm_back(grad_out, vectors_ref[0:1], unit, scale_one[:, :1])
        first_in_ref[...] = grad
        low = grad.astype(BF16)
        real = w_out_ref.shape[0]
        half = real // 2
        core = words_ref[2]
        for ref, side in ((more_mine_ref, core), (more_theirs_ref, 1 - core)):
            rows = pl.ds(pl.multiple_of(side * half, half), half)
            ref[:half] = dot(att_all[rows], low).astype(BF16)
            ref[half:] = jnp.zeros((ref.shape[0] - half, width), BF16)
            ref[half : half + 16] = sums_ref[...].astype(BF16)
        if grad_all.shape[0] > real:
            grad_all[real:] = jnp.zeros((grad_all.shape[0] - real, low.shape[0]), BF16)
        grad_all[:real] = dot_nt(w_out_ref[...], low).astype(BF16)
        for at in range(count):
            grad_refs[at][...] = grad_all[rows_of(at)]


def middle(words, att_parts, tok, cot, w_out, vectors, w_expand, w_reduce, pages, more):
    rows, width = tok.shape
    count = len(att_parts) // pages
    span, block = att_parts[0].shape
    hidden = w_expand.shape[1]
    chunks = hidden // width
    pairs = chunks // 2

    def whole(array):
        return pl.BlockSpec(array.shape, lambda s, words: (0,) * len(array.shape))

    def chunk_at(s, words):
        at = jnp.minimum(s, 2 * chunks - 1 - s)
        return (at + words[2] * pairs) % chunks

    def theirs_at(s, words):
        return jnp.clip(2 * chunks - 1 - s - pairs, 0, pairs - 1), 0

    def mine_at(s, words):
        return jnp.clip(2 * chunks - 1 - s, 0, pairs - 1), 0

    shapes = [
        jax.ShapeDtypeStruct((rows, width), BF16),
        jax.ShapeDtypeStruct((rows, width), F32),
        jax.ShapeDtypeStruct((hidden, width), BF16),
        jax.ShapeDtypeStruct((hidden, width), BF16),
        jax.ShapeDtypeStruct((more, width), BF16),
        jax.ShapeDtypeStruct((more, width), BF16),
    ] + [jax.ShapeDtypeStruct((span, pages * block), BF16)] * count
    specs = [whole(item) for item in shapes]
    specs[2] = pl.BlockSpec((2 * width, width), theirs_at)
    specs[3] = pl.BlockSpec((2 * width, width), mine_at)
    return pl.pallas_call(
        functools.partial(middle_kernel, pages, count, span, chunks),
        grid_spec=pltpu.PrefetchScalarGridSpec(
            num_scalar_prefetch=1,
            grid=(2 * chunks,),
            in_specs=[whole(item) for item in att_parts]
            + [
                whole(tok),
                whole(cot),
                whole(w_out),
                whole(vectors),
                pl.BlockSpec((width, width), lambda s, words: (0, chunk_at(s, words))),
                pl.BlockSpec((width, width), lambda s, words: (chunk_at(s, words), 0)),
            ],
            out_specs=specs,
            scratch_shapes=[
                pltpu.VMEM((16, width), F32),
                pltpu.VMEM((count * span, rows), BF16),
                pltpu.VMEM((count * span, rows), BF16),
                pltpu.VMEM((rows, width), F32),
                pltpu.VMEM((rows, 128), F32),
                pltpu.VMEM((rows, width), F32),
                pltpu.VMEM((rows, width), BF16),
                pltpu.VMEM((width, rows), BF16),
                pltpu.VMEM((chunks, rows, width), BF16),
                pltpu.VMEM((chunks, rows, width), F32),
                pltpu.VMEM((rows, width), F32),
                pltpu.VMEM((rows, width), F32),
                pltpu.VMEM((rows, width), BF16),
            ],
        ),
        out_shape=shapes,
        compiler_params=pltpu.CompilerParams(vmem_limit_bytes=VMEM_LIMIT),
        cost_estimate=pl.CostEstimate(
            flops=2 * rows * width * (6 * hidden + 3 * width),
            bytes_accessed=8 * width * hidden + 16 * rows * width,
            transcendentals=2 * rows * hidden,
        ),
        name="middle",
    )(words, *att_parts, tok, cot, w_out, vectors, w_expand, w_reduce)


def input_kernel(pages, count, span, base, *refs):
    words_ref = refs[0]
    own_refs = refs[1 : 1 + pages]
    message_refs = refs[1 + pages : pages + count]
    weight_refs = refs[pages + count : 3 + pages + count]
    first_in_ref, out_ref, held = refs[3 + pages + count :]
    rank = words_ref[0]
    width = out_ref.shape[1]
    block = out_ref.shape[0] // pages
    for page in range(pages):
        for at in range(count):
            part = message_refs[at - 1] if at else own_refs[page]
            top = base + page * span if at else 0
            place = pl.multiple_of((rank ^ at) * span, span)
            for kind in range(3):
                held[kind, pl.ds(place, span), page * block : (page + 1) * block] = part[
                    top : top + span, kind * block : (kind + 1) * block
                ]
    total = dot(weight_refs[0][...], held[0, :width])
    for kind in range(1, 3):
        total = total + dot(weight_refs[kind][...], held[kind, :width])
    out_ref[...] = (first_in_ref[...] + total.T).astype(BF16)


def input_gradient(words, own, messages, base, span, weights, first_in):
    pages = len(own)
    count = 1 + len(messages)
    rows, width = first_in.shape
    vmem = pl.BlockSpec(memory_space=pltpu.VMEM)
    return pl.pallas_call(
        functools.partial(input_kernel, pages, count, span, base),
        in_specs=[pl.BlockSpec(memory_space=pltpu.SMEM)] + [vmem] * (pages + count + 3),
        out_specs=vmem,
        out_shape=jax.ShapeDtypeStruct((rows, width), BF16),
        scratch_shapes=[pltpu.VMEM((3, count * span, rows), BF16)],
        compiler_params=pltpu.CompilerParams(vmem_limit_bytes=VMEM_LIMIT),
        cost_estimate=pl.CostEstimate(
            flops=6 * rows * width * count * span,
            bytes_accessed=2 * width * (5 * rows + 3 * count * span),
            transcendentals=0,
        ),
        name="input_gradient",
    )(words, *own, *messages, *weights, first_in)


def local(body, name, words, arrays, shapes, costly=False):
    def kernel(words_ref, *refs):
        body(words_ref, refs[: len(arrays)], refs[len(arrays) :])

    vmem = pl.BlockSpec(memory_space=pltpu.VMEM)
    shapes = [jax.ShapeDtypeStruct(shape, kind) for shape, kind in shapes]
    moved = sum(item.size * item.dtype.itemsize for item in list(arrays) + shapes)
    cost = pl.CostEstimate(flops=0, bytes_accessed=moved, transcendentals=0)
    return pl.pallas_call(
        kernel,
        in_specs=[pl.BlockSpec(memory_space=pltpu.SMEM)] + [vmem] * len(arrays),
        out_specs=[vmem] * len(shapes),
        out_shape=shapes,
        compiler_params=pltpu.CompilerParams(vmem_limit_bytes=VMEM_LIMIT),
        cost_estimate=cost if costly else NO_COST,
        name=name,
    )(words, *arrays)


def shard(index, rows, base=0):
    return pl.ds(pl.multiple_of(base + index * rows, 16), rows)


def total_of(refs, rows=slice(None)):
    total = refs[0][rows].astype(F32)
    for ref in refs[1:]:
        total = total + ref[rows].astype(F32)
    return total


def tree_sum(terms):
    while len(terms) > 1:
        terms = [terms[i] + terms[i + 1] for i in range(0, len(terms), 2)]
    return terms[0]


def bit_of(words, level):
    return lax.shift_right_logical(words[1], level) & 1


def pair_sum(words, mine, other):
    def body(words, ins, outs):
        outs[0][...] = total_of(ins).astype(BF16)

    return local(body, "pair_sum", words, [mine, other], [(mine.shape, BF16)])[0]


def halve(words, level, mine, other):
    rows, width = mine.shape
    half = rows // 2

    def body(words, ins, outs):
        bit = bit_of(words, level)
        outs[0][...] = total_of(ins, shard(bit, half)).astype(BF16)
        outs[1][...] = total_of(ins, shard(1 - bit, half)).astype(BF16)

    return local(body, "halve", words, [mine, other], [((half, width), BF16)] * 2)


def join_halves(words, level, mine, other):
    rows, width = mine.shape

    def body(words, ins, outs):
        bit = bit_of(words, level)
        outs[0][shard(bit, rows)] = ins[0][...]
        outs[0][shard(1 - bit, rows)] = ins[1][...]

    return local(body, "join_halves", words, [mine, other], [((2 * rows, width), BF16)])[0]


def across(block, level):
    return swapped(block, 1 << level, "depth")


class Plan:
    def __init__(self, rows, rows_a, more, span, width):
        self.count = lax.axis_size("blk")
        self.levels = lax.axis_size("depth").bit_length() - 1
        self.rows = rows
        self.rows_a = rows_a
        self.more = more
        self.span = span
        self.width = width
        self.a_ff = rows_a // self.count
        self.a_more = more // self.count
        self.a = self.a_ff + self.a_more
        self.b = (rows - rows_a) >> self.levels

    def shapes(self, *sizes):
        return [((rows, self.width), BF16) for rows in sizes]

    def scatter_one(self, words, halves):
        count, width = self.count, self.width
        a_ff, a_more = self.a_ff, self.a_more
        b_rows = (self.rows - self.rows_a) // count
        steps = count // 2

        def kernel(words_ref, *refs):
            parts = refs[6 : 6 + count]
            keep_ref, send_ref = refs[6 + count :]
            for i in range(count):

                @pl.when(pl.program_id(0) == i)
                def _(i=i):
                    parts[i][:a_ff] = total_of(refs[:2]).astype(BF16)
                    parts[i][a_ff:] = total_of(refs[2:4]).astype(BF16)
                    side = send_ref if i < steps else keep_ref
                    side[...] = total_of(refs[4:6]).astype(BF16)

        def there(rows):
            return pl.BlockSpec((rows, width), lambda i, words: (words[0] ^ i, 0))

        def b_at(i, words):
            bit = bit_of(words, 0)
            side = jnp.where(i < steps, 1 - bit, bit)
            return self.rows_a // b_rows + side * steps + i % steps, 0

        own_b = pl.BlockSpec((b_rows, width), b_at)
        shapes = [jax.ShapeDtypeStruct((self.a, width), BF16)] * count
        shapes += [jax.ShapeDtypeStruct((b_rows * steps, width), BF16)] * 2
        *parts_a, keep, send = pl.pallas_call(
            kernel,
            grid_spec=pltpu.PrefetchScalarGridSpec(
                num_scalar_prefetch=1,
                grid=(count,),
                in_specs=[there(a_ff)] * 2 + [there(a_more)] * 2 + [own_b] * 2,
                out_specs=[fixed(item) for item in shapes[:count]]
                + [
                    pl.BlockSpec((b_rows, width), lambda i, words: (jnp.maximum(i - steps, 0), 0)),
                    pl.BlockSpec((b_rows, width), lambda i, words: (jnp.minimum(i, steps - 1), 0)),
                ],
            ),
            out_shape=shapes,
            compiler_params=pltpu.CompilerParams(vmem_limit_bytes=VMEM_LIMIT),
            cost_estimate=NO_COST,
            name="scatter_one",
        )(words, *halves, *halves[:2])
        return [from_blk(part, i) for i, part in enumerate(parts_a)], keep, across(send, 0)

    def scatter_two(self, words, parts_a, keep_b, other_b, pages):
        count = self.count
        half = self.a // 2

        def body(words, ins, outs):
            bit = bit_of(words, 0)
            outs[0][...] = total_of(ins[:count], shard(bit, half)).astype(BF16)
            outs[1][...] = total_of(ins[:count], shard(1 - bit, half)).astype(BF16)
            part_b = total_of(ins[count : count + 2]).astype(BF16)
            outs[2][...] = part_b
            for i, out in enumerate(outs[3:]):
                out[: self.b] = part_b
                for page in range(len(pages)):
                    piece = ins[count + 2 + page * (count - 1) + i]
                    base = self.b + page * self.span
                    out[base : base + self.span, : piece.shape[1]] = piece[...]

        message = self.b + len(pages) * self.span
        shapes = self.shapes(half, half, self.b, *[message] * (count - 1))
        pieces = [piece for page in pages for piece in page[1:]]
        keep, send, part_b, *messages = local(
            body, "scatter_two", words, [*parts_a, keep_b, other_b, *pieces], shapes
        )
        return (
            keep,
            across(send, 0),
            part_b,
            [from_blk(item, i + 1) for i, item in enumerate(messages)],
        )

    def sum_b(self, words, part_b, messages):
        def body(words, ins, outs):
            terms = [ref[: self.b].astype(F32) for ref in ins]
            outs[0][...] = tree_sum(terms).astype(BF16)

        return local(body, "sum_b", words, [part_b, *messages], self.shapes(self.b))[0]

    def gather_b(self, words, part_b):
        for level in range(self.levels - 1, 0, -1):
            part_b = join_halves(words, level, part_b, across(part_b, level))
        return part_b, across(part_b, 0)


def gather_blk(part, cut, late=None):
    count = lax.axis_size("blk")
    if count != 4:
        return [(i, 0, from_blk(part, i)) for i in range(count)]
    one, two = swapped(part, 1), swapped(part, 2)
    if late is not None:
        one, two = after(late, (one, two))
    first, second = swapped(one[:cut], 2), swapped(two[cut:], 1)
    return [(0, 0, part), (1, 0, one), (2, 0, two), (3, 0, first), (3, cut, second)]


def with_core(pieces):
    return [(distance, base, from_core(item)) for distance, base, item in pieces]


SEGMENT = 256
SLOTS = 4


def widen_own(words, plan, pieces, halves_b, hidden):
    width = plan.width
    chunks = hidden // width
    pairs = chunks // 2
    per_matrix = width // SEGMENT
    arrays = [item for _, _, item in pieces] + list(halves_b)
    segments = []
    extras = []
    for at, (distance, base, item) in enumerate(pieces):
        stop = min(item.shape[0], plan.a_ff - base)
        for top in range(0, stop, SEGMENT):
            segments.append((at, top, min(SEGMENT, stop - top), distance, base + top))
        if base + item.shape[0] == plan.a:
            extras.append((at, distance))
    for at, item in enumerate(halves_b):
        for top in range(0, item.shape[0], SEGMENT):
            segments.append((len(pieces) + at, top, SEGMENT, None, top))

    def kernel(words_ref, *refs):
        ins = refs[: len(arrays)]
        joined_ref, expand_ref, reduce_ref, held, sems = refs[len(arrays) :]
        copies = []
        for index, (at, top, rows, distance, base) in enumerate(segments):
            slot = index % SLOTS
            if index >= SLOTS:
                copies[index - SLOTS].wait()
            part = ins[at][top : top + rows]
            held[slot, :rows] = part.astype(F32)
            if distance is None:
                half = ins[len(pieces)].shape[0]
                bit = bit_of(words_ref, 0)
                place = plan.rows_a + half * (bit if at == len(pieces) else 1 - bit) + base
            else:
                place = (words_ref[0] ^ distance) * plan.a_ff + base
            joined_ref[pl.ds(pl.multiple_of(place, SEGMENT), rows)] = part
            block = lax.div(place, SEGMENT)
            matrix = lax.div(block, per_matrix)
            row = (block - matrix * per_matrix) * SEGMENT
            chunk = (lax.div(matrix, 2) + words_ref[2] * pairs) % chunks
            column = pl.multiple_of(chunk * width, width)
            source = held.at[slot, :rows]
            to_expand = pltpu.make_async_copy(
                source,
                expand_ref.at[pl.ds(pl.multiple_of(row, SEGMENT), rows), pl.ds(column, width)],
                sems.at[slot],
            )
            to_reduce = pltpu.make_async_copy(
                source,
                reduce_ref.at[pl.ds(pl.multiple_of(column + row, SEGMENT), rows)],
                sems.at[slot],
            )
            is_expand = lax.rem(matrix, 2) == 0
            pl.when(is_expand)(to_expand.start)
            pl.when(jnp.logical_not(is_expand))(to_reduce.start)
            copies.append(to_reduce)
        for at, distance in extras:
            rows = shard(words_ref[0] ^ distance, plan.a_more, plan.rows)
            joined_ref[rows] = ins[at][ins[at].shape[0] - plan.a_more :]
        for copy in copies[-SLOTS:]:
            copy.wait()

    assert all(base % SEGMENT == 0 for *_, base in segments)
    vmem = pl.BlockSpec(memory_space=pltpu.VMEM)
    anywhere = pl.BlockSpec(memory_space=pl.ANY)
    return pl.pallas_call(
        kernel,
        in_specs=[pl.BlockSpec(memory_space=pltpu.SMEM)] + [vmem] * len(arrays),
        out_specs=[vmem, anywhere, anywhere],
        out_shape=[
            jax.ShapeDtypeStruct((plan.rows + plan.more, width), BF16),
            jax.ShapeDtypeStruct((width, hidden), F32),
            jax.ShapeDtypeStruct((hidden, width), F32),
        ],
        scratch_shapes=[
            pltpu.VMEM((SLOTS, SEGMENT, width), F32),
            pltpu.SemaphoreType.DMA((SLOTS,)),
        ],
        compiler_params=pltpu.CompilerParams(vmem_limit_bytes=VMEM_LIMIT),
        cost_estimate=pl.CostEstimate(
            flops=0, bytes_accessed=6 * hidden * width, transcendentals=0
        ),
        name="widen_own",
    )(words, *arrays)


def widen_other(words, joined, expand, reduce):
    width, hidden = expand.shape
    chunks = hidden // width
    pairs = chunks // 2

    def kernel(words_ref, half_ref, before_ref, before_too_ref, expand_ref, reduce_ref):
        expand_ref[...] = half_ref[:width].astype(F32)
        reduce_ref[...] = half_ref[width:].astype(F32)

    def place(s, words):
        return (s + (words[2] + 1) * pairs) % chunks

    anywhere = pl.BlockSpec(memory_space=pl.ANY)
    return pl.pallas_call(
        kernel,
        grid_spec=pltpu.PrefetchScalarGridSpec(
            num_scalar_prefetch=1,
            grid=(pairs,),
            in_specs=[
                pl.BlockSpec((2 * width, width), lambda s, words: (s, 0)),
                anywhere,
                anywhere,
            ],
            out_specs=[
                pl.BlockSpec((width, width), lambda s, words: (0, place(s, words))),
                pl.BlockSpec((width, width), lambda s, words: (place(s, words), 0)),
            ],
        ),
        out_shape=[
            jax.ShapeDtypeStruct((width, hidden), F32),
            jax.ShapeDtypeStruct((hidden, width), F32),
        ],
        input_output_aliases={2: 0, 3: 1},
        compiler_params=pltpu.CompilerParams(vmem_limit_bytes=VMEM_LIMIT),
        cost_estimate=pl.CostEstimate(
            flops=0, bytes_accessed=6 * hidden * width, transcendentals=0
        ),
        name="widen_other",
    )(words, joined, expand, reduce)


def finished(words, plan, heads, joined, side, before=()):
    count = plan.count
    span = plan.span
    width = plan.width
    half_rows = width // 2
    arrays = [item for _, _, item in heads]

    def kernel(words_ref, *refs):
        heads_refs, refs = refs[: len(heads)], refs[len(heads) :]
        extras, refs = refs[: len(joined)], refs[len(joined) :]
        refs = refs[len(before) :]
        outs, sum_refs, refs = refs[:5], refs[5 : 5 + 4 * side], refs[5 + 4 * side :]
        gathered, wide, project, sems = refs
        rank = words_ref[0]
        half = words_ref[2] ^ side
        for ref, (distance, base, _) in zip(heads_refs, heads):
            rows = ref.shape[0]
            place = pl.multiple_of((rank ^ distance) * span, HEAD_DIM)
            for part in range(2):
                low, high = max(base, part * span), min(base + rows, (part + 1) * span)
                if low < high:
                    gathered[part, pl.ds(place + (low - part * span), high - low)] = ref[
                        low - base : high - base
                    ]
        for part in range(2):
            wide[part] = gathered[part, :width].astype(F32).T
        project[...] = extras[side][:half_rows].astype(F32)

        @pl.when(half == 1)
        def _():
            wide[1] = entry_order(wide[1])

        def copy(source, target, at):
            return pltpu.make_async_copy(source, target, sems.at[at])

        for part in range(2):
            pl.when(half == 0)(copy(wide.at[part], outs[part], part).start)
            pl.when(half == 1)(copy(wide.at[part], outs[2 + part], part).start)
        rows = pl.ds(pl.multiple_of(half * half_rows, half_rows), half_rows)
        last = copy(project, outs[4].at[rows], 2)
        last.start()
        if side:
            rows = slice(half_rows, half_rows + 16)
            sums = jnp.where(half == 0, extras[1][rows].astype(F32), extras[0][rows].astype(F32))
            for at, ref in enumerate(sum_refs):
                ref[...] = sums[at : at + 1]
        for part in range(2):
            copy(wide.at[part], outs[part], part).wait()
        last.wait()

    def whole(item):
        return pl.BlockSpec(item.shape, lambda s: (0, 0))

    more = pl.BlockSpec((plan.more, width), lambda s: (plan.rows // plan.more, 0))
    anywhere = pl.BlockSpec(memory_space=pl.ANY)
    first = 1 + len(heads) + len(joined)
    shapes = [jax.ShapeDtypeStruct((width, width), F32)] * 5
    sums_shapes = [jax.ShapeDtypeStruct((1, width), F32)] * (4 * side)
    return pl.pallas_call(
        kernel,
        grid=(1,),
        in_specs=[pl.BlockSpec(memory_space=pltpu.SMEM)]
        + [whole(item) for item in arrays]
        + [more] * len(joined)
        + [anywhere] * len(before),
        out_specs=[anywhere] * 5 + [whole(item) for item in sums_shapes],
        out_shape=shapes + sums_shapes,
        scratch_shapes=[
            pltpu.VMEM((2, count * span, width), BF16),
            pltpu.VMEM((2, width, width), F32),
            pltpu.VMEM((half_rows, width), F32),
            pltpu.SemaphoreType.DMA((3,)),
        ],
        input_output_aliases={first + at: at for at in range(len(before))},
        compiler_params=pltpu.CompilerParams(vmem_limit_bytes=VMEM_LIMIT),
        cost_estimate=pl.CostEstimate(
            flops=0, bytes_accessed=16 * width * width, transcendentals=0
        ),
        name="finish",
    )(words, *arrays, *joined, *before)


def per_device(
    tokens,
    boxes,
    w_query,
    w_key,
    w_value,
    w_output,
    box_weight,
    first_gain,
    first_shift,
    w_expand,
    w_reduce,
    second_gain,
    second_shift,
    cotangent,
):
    pages, block, width = tokens.shape
    count = lax.axis_size("blk")
    depth = lax.axis_size("depth")
    words = jnp.stack(
        [lax.axis_index("blk"), lax.axis_index("depth"), lax.axis_index("core")]
    ).astype(jnp.int32)
    hidden = w_expand.shape[1]
    span = -(-HEADS // count) * HEAD_DIM
    unit = 16 * count * depth
    more = -(-(width // 2 + 16) // unit) * unit

    own_places = jnp.stack([boxes[0] + boxes[2], boxes[1] + boxes[3]], axis=1)
    own_places = jnp.stack([lax.shift_right_logical(own_places, 6), own_places & 63], axis=2)
    own_places = own_places.reshape(4 * pages, block).astype(BF16)
    own_places = jnp.pad(own_places, ((0, 16 - 4 * pages), (0, width - block)))
    message = jnp.concatenate([tokens[0], own_places])
    messages = [from_blk(message, i) for i in range(count)]
    w_own, box_own, rot_cos, rot_sin = prepare(
        words, w_query, w_key, w_value, box_weight, span, count * block
    )
    messages, rot_cos = lax.optimization_barrier((messages, rot_cos))
    own = after(messages, tokens[1])
    pieces = [messages, [from_blk(own, i) for i in range(count)]]

    saved = []
    att_parts = []
    for page in range(pages):
        results = attention_forward(
            words, page, messages, pieces[page], w_own, box_own, rot_cos, rot_sin
        )
        saved.append(results[:6])
        att_parts += [from_blk(results[6 + i], i) for i in range(count)]

    vectors = jnp.stack([first_gain, first_shift, second_gain, second_shift])
    results = middle(
        words,
        att_parts,
        tokens.reshape(pages * block, width),
        cotangent.reshape(pages * block, width),
        w_output,
        vectors,
        w_expand,
        w_reduce,
        pages,
        more,
    )
    layer_out, first_in, theirs, mine, more_theirs, more_mine = results[:6]
    grads = [from_blk(results[6 + i], i) for i in range(count)]
    plan = Plan(hidden, 2 * hidden // 3, more, span, width)
    parts_a, keep_b, other_b = plan.scatter_one(
        after(grads[:2], words), [mine, from_core(theirs), more_mine, from_core(more_theirs)]
    )

    def backward(page, words, before=None):
        return attention_backward(
            words,
            page,
            grads,
            pieces[page],
            saved[page],
            box_own,
            rot_cos,
            rot_sin,
            before,
        )

    *pre_one, before = backward(0, after(parts_a[0], words))
    done = before
    for level in range(1, plan.levels):
        keep_b, send_b = halve(after(done, words), level, keep_b, other_b)
        other_b = across(send_b, level)
        done = keep_b
    *pre_two, heads_mine, heads_theirs = backward(1, after(done, words), before)
    own = [pre_one[0], pre_two[0]]
    part_a, other_a, part_b, messages_b = plan.scatter_two(
        after(heads_mine, words), parts_a, keep_b, other_b, [pre_one, pre_two]
    )
    heads = pair_sum(
        after(part_a, words), heads_mine, from_core(after(part_a, heads_theirs))
    )
    part_a = pair_sum(after(heads, words), part_a, other_a)
    other = across(after(part_a, heads), 0)
    done = part_a
    for level in range(1, plan.levels):
        part_a = pair_sum(after(done, words), part_a, across(part_a, level))
        done = part_a
    other_a = across(part_a, 0)
    heads = pair_sum(after(done, words), heads, other)
    part_b = plan.sum_b(after(heads, words), part_b, messages_b)
    part_a = join_halves(after(part_b, words), 0, part_a, other_a)
    heads, part_b = after(part_a, (heads, part_b))
    other = across(heads, 1)
    input_grad = input_gradient(
        after(part_a, words),
        own,
        messages_b,
        plan.b,
        span,
        (w_query, w_key, w_value),
        first_in,
    )
    parts_b = plan.gather_b(after(input_grad, words), part_b)
    pieces_a = gather_blk(part_a, plan.a_ff // 2, input_grad)
    heads = pair_sum(after(pieces_a[1][2], words), heads, other)
    for level in range(2, plan.levels):
        heads = pair_sum(words, heads, across(heads, level))
    heads = after([item for _, _, item in pieces_a], heads)
    joined, *wide = widen_own(after(heads, words), plan, pieces_a, parts_b, hidden)
    pieces_heads = gather_blk(heads, span, joined)
    joined_other = from_core(after(pieces_heads[1][2], joined))
    grads = finished(words, plan, pieces_heads, [joined], 0)
    grad_expand, grad_reduce = widen_other(after(grads, words), joined_other, *wide)
    grad_query, grad_key, grad_value, grad_box, grad_project, *sums = finished(
        after(grad_expand, words),
        plan,
        with_core(pieces_heads),
        [joined, joined_other],
        1,
        grads,
    )
    sums = [item.reshape(width) for item in sums]
    return (
        layer_out.reshape(tokens.shape),
        input_grad.reshape(tokens.shape),
        grad_query,
        grad_key,
        grad_value,
        grad_project,
        grad_box,
        sums[0],
        sums[1],
        grad_expand,
        grad_reduce,
        sums[2],
        sums[3],
    )


def solution(mesh):
    blocks, rest = mesh.devices.shape
    parts = jax.sharding.Mesh(
        mesh.devices.reshape(blocks, rest // 2, 2), ("blk", "depth", "core")
    )
    split = P(("depth", "core"), "blk", None)
    return jax.shard_map(
        per_device,
        mesh=parts,
        in_specs=(split, P(None, ("depth", "core"), "blk")) + (P(),) * 11 + (split,),
        out_specs=(split, split) + (P(),) * 11,
        check_vma=False,
    )
```

```python
import functools

import jax
import jax.numpy as jnp
import numpy as np
from jax import lax
from jax.experimental import pallas as pl
from jax.experimental.pallas import tpu as pltpu
from jax.sharding import PartitionSpec as P

HEADS = 12
HEAD_DIM = 64
HALF = 32
FREQS = 192
CODES = 4 * FREQS
VMEM_LIMIT = 60 * 1024 * 1024
NO_COST = pl.CostEstimate(flops=0, bytes_accessed=0, transcendentals=0)
F32 = jnp.float32
BF16 = jnp.bfloat16


def dot(left, right):
    return lax.dot_general(left, right, (((1,), (0,)), ((), ())), preferred_element_type=F32)


def dot_nt(left, right):
    return lax.dot_general(left, right, (((1,), (1,)), ((), ())), preferred_element_type=F32)


def dot_tn(left, right):
    return lax.dot_general(left, right, (((0,), (0,)), ((), ())), preferred_element_type=F32)


def swapped(block, distance, axis="blk"):
    count = lax.axis_size(axis)
    return lax.ppermute(block, axis, [(i, i ^ distance) for i in range(count)])


def from_blk(block, distance):
    return swapped(block, distance) if distance else block


def from_core(block):
    return swapped(block, 1, "core")


def after(done, value):
    return lax.optimization_barrier((value, done))[0]


def turned(upper, lower, cosines, sines):
    return upper * cosines - lower * sines, lower * cosines + upper * sines


def entry_order(rows):
    return jnp.concatenate(
        [
            rows[:FREQS],
            rows[2 * FREQS : 3 * FREQS],
            rows[FREQS : 2 * FREQS],
            rows[3 * FREQS :],
        ],
        axis=0,
    )


def angle_tables():
    rates = np.float32(10000.0) ** (-np.arange(FREQS, dtype=np.float32) / np.float32(FREQS))
    tables = []
    for places in (32.0 * np.arange(32), 0.5 * np.arange(64)):
        angles = rates.astype(np.float64)[:, None] * places[None, :]
        left = np.concatenate([np.sin(angles), np.cos(angles)])
        parts = []
        for _ in range(3):
            parts.append(left.astype(jnp.bfloat16))
            left = left - parts[-1].astype(np.float64)
        tables.append(np.concatenate(parts, axis=1))
    return tables


def rotary_tables(length):
    rates = np.float32(10000.0) ** (-np.arange(HALF, dtype=np.float32) / np.float32(HALF))
    angles = np.arange(length, dtype=np.float32)[None, :] * rates[:, None]
    angles = angles.astype(np.float64)
    return np.cos(angles).astype(np.float32), np.sin(angles).astype(np.float32)


def prepare_kernel(
    words_ref,
    query_ref,
    key_ref,
    value_ref,
    box_ref,
    cos_ref,
    sin_ref,
    own_ref,
    own_box_ref,
    own_cos_ref,
    own_sin_ref,
):
    rank = words_ref[0]
    span = own_box_ref.shape[0]
    width = query_ref.shape[1]
    count = lax.axis_size("blk")
    block = cos_ref.shape[1] // count
    row = lax.broadcasted_iota(jnp.int32, (span, width), 0) + rank * span
    column = lax.broadcasted_iota(jnp.int32, (span, width), 1)
    pick = jnp.where(row == column, 1.0, 0.0).astype(BF16)
    for kind, ref in enumerate((query_ref, key_ref, value_ref)):
        own_ref[kind * span : (kind + 1) * span] = dot_nt(pick, ref[...]).astype(BF16)
    own_box_ref[...] = dot_nt(pick, entry_order(box_ref[...])).astype(BF16)
    for i in range(count):
        from_cols = pl.ds(pl.multiple_of((rank ^ i) * block, block), block)
        own_cos_ref[:, i * block : (i + 1) * block] = cos_ref[:, from_cols]
        own_sin_ref[:, i * block : (i + 1) * block] = sin_ref[:, from_cols]


def prepare(words, w_query, w_key, w_value, box_weight, span, length):
    width = w_query.shape[0]
    vmem = pl.BlockSpec(memory_space=pltpu.VMEM)
    return pl.pallas_call(
        prepare_kernel,
        in_specs=[pl.BlockSpec(memory_space=pltpu.SMEM)] + [vmem] * 6,
        out_specs=[vmem] * 4,
        out_shape=[
            jax.ShapeDtypeStruct((3 * span, width), BF16),
            jax.ShapeDtypeStruct((span, CODES), BF16),
            jax.ShapeDtypeStruct((HALF, length), F32),
            jax.ShapeDtypeStruct((HALF, length), F32),
        ],
        compiler_params=pltpu.CompilerParams(vmem_limit_bytes=VMEM_LIMIT),
        cost_estimate=pl.CostEstimate(
            flops=8 * span * width * width, bytes_accessed=10 * width * width, transcendentals=0
        ),
        name="prepare",
    )(words, w_query, w_key, w_value, box_weight, *map(jnp.asarray, rotary_tables(length)))


def fold(value, combine):
    while value.shape[0] > 8:
        half = value.shape[0] // 2
        value = combine(value[:half], value[half:])
    return value


def write_codes(page, place_refs, high_ref, low_ref, sin_ref, cos_ref, codes_ref):
    block = sin_ref.shape[1] // len(place_refs)

    def looked_up(table_ref, index):
        spots = table_ref.shape[1] // 3
        rows = lax.broadcasted_iota(jnp.int32, (spots, block), 0).astype(F32)
        once = jnp.where(rows == index, 1.0, 0.0)
        found = dot(table_ref[...], jnp.concatenate([once] * 3, axis=0).astype(BF16))
        return found[:FREQS], found[FREQS:]

    for i, place_ref in enumerate(place_refs):
        columns = slice(i * block, (i + 1) * block)
        places = place_ref[:, :block].astype(F32)
        for axis in range(2):
            at = 4 * page + 2 * axis
            high_sin, high_cos = looked_up(high_ref, places[at : at + 1])
            low_sin, low_cos = looked_up(low_ref, places[at + 1 : at + 2])
            sines = high_sin * low_cos + high_cos * low_sin
            cosines = high_cos * low_cos - high_sin * low_sin
            rows = slice(axis * FREQS, (axis + 1) * FREQS)
            later = slice((2 + axis) * FREQS, (3 + axis) * FREQS)
            sin_ref[rows, columns] = sines
            cos_ref[rows, columns] = cosines
            codes_ref[rows, columns] = sines.astype(BF16)
            codes_ref[later, columns] = cosines.astype(BF16)


def forward_kernel(page, count, words_ref, *refs):
    place_refs, refs = refs[:count], refs[count:]
    piece_refs, refs = refs[:count], refs[count:]
    high_ref, low_ref, w_ref, box_ref, rot_cos_ref, rot_sin_ref = refs[:6]
    probs_ref, att_ref, heads_ref, sin_ref, cos_ref, codes_ref = refs[6:12]
    low_refs = refs[12 : 12 + count]
    tok_ref, pre_ref, kc_ref, qr_ref = refs[12 + count :]
    rows = tok_ref.shape[0]
    block = rows // count
    head = pl.program_id(0)
    span = pl.num_programs(0) * HEAD_DIM

    @pl.when(head == 0)
    def _():
        for i in range(count):
            tok_ref[i * block : (i + 1) * block] = piece_refs[i][...]
        pre_ref[...] = dot_nt(w_ref[...], tok_ref[...])
        write_codes(page, place_refs, high_ref, low_ref, sin_ref, cos_ref, codes_ref)
        kc_ref[:, :CODES] = codes_ref[...].astype(F32).T.astype(BF16)

    def pre(kind):
        at = kind * span + head * HEAD_DIM
        return pre_ref[pl.ds(pl.multiple_of(at, HEAD_DIM), HEAD_DIM)]

    rot_cos = rot_cos_ref[...]
    rot_sin = rot_sin_ref[...]
    query_pre = pre(0).astype(BF16)
    wide = query_pre.astype(F32)
    query = jnp.concatenate(turned(wide[:HALF], wide[HALF:], rot_cos, rot_sin), axis=0)
    key_pre = pre(1)
    key = jnp.concatenate(turned(key_pre[:HALF], key_pre[HALF:], rot_cos, rot_sin), axis=0)
    value = pre(2).astype(BF16)
    heads_ref[0, :HEAD_DIM] = query_pre
    heads_ref[0, HEAD_DIM : 2 * HEAD_DIM] = query.astype(BF16)
    heads_ref[0, 2 * HEAD_DIM : 3 * HEAD_DIM] = key.astype(BF16)
    heads_ref[0, 3 * HEAD_DIM :] = value
    kc_ref[:, CODES:] = key.T.astype(BF16)
    qr_ref[CODES:] = (query * 0.125).astype(BF16)
    step = min(256, block)

    def logits_at(at):
        part = slice(at, at + step)
        projected = dot_tn(box_ref[...], query_pre[:, part])
        sines = sin_ref[:, part]
        cosines = cos_ref[:, part]
        upper = projected[: 2 * FREQS]
        lower = projected[2 * FREQS :]
        qr_ref[: 2 * FREQS, part] = ((upper * cosines + lower * sines) * 0.125).astype(BF16)
        qr_ref[2 * FREQS : CODES, part] = ((lower * cosines - upper * sines) * 0.125).astype(BF16)
        return dot(kc_ref[...], qr_ref[:, part])

    following = logits_at(0)
    for at in range(0, rows, step):
        logits = following
        if at + step < rows:
            following = logits_at(at + step)
        peak = jnp.max(fold(logits, jnp.maximum), axis=0, keepdims=True)
        weight = jnp.exp(logits - peak)
        total = jnp.sum(fold(weight, jnp.add), axis=0, keepdims=True)
        probs = (weight * (1.0 / total)).astype(BF16)
        probs_ref[0, :, at : at + step] = probs
        attended = dot(value, probs)
        att_ref[0, :, at : at + step] = attended
        inner = at % block
        low_refs[at // block][:, inner : inner + step] = attended.astype(BF16)


def fixed(array):
    return pl.BlockSpec(array.shape, lambda *at: (0,) * len(array.shape))


def attention_forward(words, page, messages, pieces, w_own, box_own, rot_cos, rot_sin):
    count = len(messages)
    block, width = messages[0].shape[0] - 16, messages[0].shape[1]
    rows = count * block
    span = box_own.shape[0]
    heads = span // HEAD_DIM
    tables = [jnp.asarray(item) for item in angle_tables()]
    specs = [pl.BlockSpec((block, width), lambda h, words: (0, 0))] * count
    places = pl.BlockSpec((16, width), lambda h, words: (block // 16, 0))
    out_shape = [
        jax.ShapeDtypeStruct((heads, rows, rows), BF16),
        jax.ShapeDtypeStruct((heads, HEAD_DIM, rows), F32),
        jax.ShapeDtypeStruct((heads, 4 * HEAD_DIM, rows), BF16),
        jax.ShapeDtypeStruct((2 * FREQS, rows), F32),
        jax.ShapeDtypeStruct((2 * FREQS, rows), F32),
        jax.ShapeDtypeStruct((CODES, rows), BF16),
    ] + [jax.ShapeDtypeStruct((span, block), BF16)] * count
    return pl.pallas_call(
        functools.partial(forward_kernel, page, count),
        grid_spec=pltpu.PrefetchScalarGridSpec(
            num_scalar_prefetch=1,
            grid=(heads,),
            in_specs=[places] * count
            + specs
            + [fixed(item) for item in (*tables, w_own)]
            + [
                pl.BlockSpec((HEAD_DIM, CODES), lambda h, words: (h, 0)),
                fixed(rot_cos),
                fixed(rot_sin),
            ],
            out_specs=[
                pl.BlockSpec((1, rows, rows), lambda h, words: (h, 0, 0)),
                pl.BlockSpec((1, HEAD_DIM, rows), lambda h, words: (h, 0, 0)),
                pl.BlockSpec((1, 4 * HEAD_DIM, rows), lambda h, words: (h, 0, 0)),
            ]
            + [fixed(item) for item in out_shape[3:6]]
            + [pl.BlockSpec((HEAD_DIM, block), lambda h, words: (h, 0))] * count,
            scratch_shapes=[
                pltpu.VMEM((rows, width), BF16),
                pltpu.VMEM((3 * span, rows), F32),
                pltpu.VMEM((rows, CODES + HEAD_DIM), BF16),
                pltpu.VMEM((CODES + HEAD_DIM, rows), BF16),
            ],
        ),
        out_shape=out_shape,
        compiler_params=pltpu.CompilerParams(vmem_limit_bytes=VMEM_LIMIT),
        cost_estimate=pl.CostEstimate(
            flops=2 * heads * rows * (rows * 1100 + 200 * width + 64 * CODES),
            bytes_accessed=2 * heads * rows * rows + 12 * rows * width,
            transcendentals=heads * rows * rows,
        ),
        name="attention_forward",
    )(words, *messages, *pieces, *tables, w_own, box_own, rot_cos, rot_sin)


def backward_kernel(count, last, words_ref, *refs):
    grad_refs, refs = refs[:count], refs[count:]
    piece_refs, refs = refs[:count], refs[count:]
    probs_ref, att_ref, heads_ref, box_ref, codes_ref, sin_ref, cos_ref = refs[:7]
    rot_cos_ref, rot_sin_ref = refs[7:9]
    refs = refs[9:]
    if last:
        before_ref, refs = refs[0], refs[1:]
    pre_refs, refs = refs[:count], refs[count:]
    if last:
        mine_ref, theirs_ref, *refs = refs
    weight_grad_ref, kc_ref, logit_grad_ref, entry_grad_ref, turned_ref = refs
    block, width = piece_refs[0].shape
    rows = count * block
    head = pl.program_id(0)
    span = pl.num_programs(0) * HEAD_DIM

    @pl.when(head == 0)
    def _():
        kc_ref[:CODES] = codes_ref[...]

    kc_ref[CODES:] = heads_ref[0, 2 * HEAD_DIM : 3 * HEAD_DIM]
    packed = heads_ref[0].astype(F32).T.astype(BF16)
    query_pre = packed[:, :HEAD_DIM]
    query = packed[:, HEAD_DIM : 2 * HEAD_DIM]
    value = packed[:, 3 * HEAD_DIM :] * jnp.asarray(0.125, BF16)
    rot_cos = rot_cos_ref[...]
    rot_sin = rot_sin_ref[...]
    grad = jnp.concatenate([ref[...] for ref in grad_refs], axis=1)
    grad_tall = grad.astype(F32).T.astype(BF16)
    offsets = jnp.sum(grad.astype(F32) * att_ref[0], axis=0, keepdims=True) * 0.125
    step = min(256, block)
    place = pl.multiple_of(head * HEAD_DIM, HEAD_DIM)
    here = pl.ds(place, HEAD_DIM)

    def logits_back(at):
        part = slice(at, at + step)
        grad_probs = dot(value, grad[:, part])
        logit_grad_ref[:, part] = (
            probs_ref[0, :, part].astype(F32) * (grad_probs - offsets[:, part])
        ).astype(BF16)

    logits_back(0)
    for at in range(0, rows, step):
        if at + step < rows:
            logits_back(at + step)
        part = slice(at, at + step)
        back = dot(kc_ref[...], logit_grad_ref[:, part])
        sines = sin_ref[:, part]
        cosines = cos_ref[:, part]
        upper = back[: 2 * FREQS]
        lower = back[2 * FREQS : CODES]
        entry_grad_ref[: 2 * FREQS, part] = (upper * cosines - lower * sines).astype(BF16)
        entry_grad_ref[2 * FREQS :, part] = (lower * cosines + upper * sines).astype(BF16)
        first = back[CODES : CODES + HALF]
        second = back[CODES + HALF :]
        turned_ref[:HALF, part], turned_ref[HALF:, part] = turned(
            first, second, rot_cos[:, part], -rot_sin[:, part]
        )
    key_flat = dot(logit_grad_ref[...], query).T
    value_low = dot(probs_ref[0], grad_tall).T.astype(BF16)
    query_low = (turned_ref[...] + dot(box_ref[...], entry_grad_ref[...])).astype(BF16)
    key_low = jnp.concatenate(
        turned(key_flat[:HALF], key_flat[HALF:], rot_cos, -rot_sin), axis=0
    ).astype(BF16)
    for i in range(count):
        columns = slice(i * block, (i + 1) * block)
        pre_refs[i][here, :block] = query_low[:, columns]
        pre_refs[i][here, block : 2 * block] = key_low[:, columns]
        pre_refs[i][here, 2 * block :] = value_low[:, columns]
    weight_grad_ref[pl.ds(3 * span + place, HEAD_DIM)] = dot(entry_grad_ref[...], query_pre).T

    @pl.when(head == pl.num_programs(0) - 1)
    def _():
        for kind in range(3):
            columns = slice(kind * block, (kind + 1) * block)
            total = dot(pre_refs[0][:, columns], piece_refs[0][...])
            for i in range(1, count):
                total = total + dot(pre_refs[i][:, columns], piece_refs[i][...])
            weight_grad_ref[kind * span : (kind + 1) * span] = total
        if last:
            half = 2 * span
            core = words_ref[2]
            ours = pl.ds(pl.multiple_of(core * half, half), half)
            there = pl.ds(pl.multiple_of((1 - core) * half, half), half)
            mine_ref[...] = weight_grad_ref[ours] + before_ref[ours]
            theirs_ref[...] = (weight_grad_ref[there] + before_ref[there]).astype(BF16)


def attention_backward(
    words, page, grads, pieces, saved, box_own, rot_cos, rot_sin, before=None
):
    probs, att, heads_saved, sines, cosines, codes = saved
    count = len(pieces)
    rows, width = probs.shape[1], pieces[0].shape[1]
    block = rows // count
    span = box_own.shape[0]
    heads = span // HEAD_DIM
    last = before is not None
    extra = (before,) if last else ()
    full_shape = (4 * span, width)
    specs = [pl.BlockSpec((block, width), lambda h, words: (0, 0))] * count
    out_shape = [jax.ShapeDtypeStruct((span, 3 * block), BF16)] * count
    if last:
        out_shape += [
            jax.ShapeDtypeStruct((2 * span, width), F32),
            jax.ShapeDtypeStruct((2 * span, width), BF16),
        ]
    else:
        out_shape.append(jax.ShapeDtypeStruct(full_shape, F32))
    return pl.pallas_call(
        functools.partial(backward_kernel, count, last),
        grid_spec=pltpu.PrefetchScalarGridSpec(
            num_scalar_prefetch=1,
            grid=(heads,),
            in_specs=[pl.BlockSpec((HEAD_DIM, block), lambda h, words: (h, page))] * count
            + specs
            + [
                pl.BlockSpec((1, rows, rows), lambda h, words: (h, 0, 0)),
                pl.BlockSpec((1, HEAD_DIM, rows), lambda h, words: (h, 0, 0)),
                pl.BlockSpec((1, 4 * HEAD_DIM, rows), lambda h, words: (h, 0, 0)),
                pl.BlockSpec((HEAD_DIM, CODES), lambda h, words: (h, 0)),
            ]
            + [fixed(item) for item in (codes, sines, cosines, rot_cos, rot_sin, *extra)],
            out_specs=[fixed(item) for item in out_shape],
            scratch_shapes=([pltpu.VMEM(full_shape, F32)] if last else [])
            + [
                pltpu.VMEM((CODES + HEAD_DIM, rows), BF16),
                pltpu.VMEM((rows, rows), BF16),
                pltpu.VMEM((CODES, rows), BF16),
                pltpu.VMEM((HEAD_DIM, rows), F32),
            ],
        ),
        out_shape=out_shape,
        compiler_params=pltpu.CompilerParams(vmem_limit_bytes=VMEM_LIMIT),
        cost_estimate=pl.CostEstimate(
            flops=2 * heads * rows * (rows * 1400 + 200 * width + 128 * CODES),
            bytes_accessed=2 * heads * rows * rows + 12 * rows * width,
            transcendentals=0,
        ),
        name="attention_backward",
    )(
        words,
        *grads,
        *pieces,
        probs,
        att,
        heads_saved,
        box_own,
        codes,
        sines,
        cosines,
        rot_cos,
        rot_sin,
        *extra,
    )


def normed(value):
    centered = value - jnp.mean(value, axis=-1, keepdims=True)
    scale = lax.rsqrt(jnp.mean(centered * centered, axis=-1, keepdims=True) + 1e-05)
    return centered * scale, scale


def norm_back(grad, gain, unit, scale):
    scaled = grad * gain
    return scale * (
        scaled
        - jnp.mean(scaled, axis=-1, keepdims=True)
        - unit * jnp.mean(scaled * unit, axis=-1, keepdims=True)
    )


def column_sum(value):
    return jnp.sum(value, axis=0, keepdims=True)


def middle_kernel(pages, count, span, chunks, *refs):
    total = pages * count
    words_ref = refs[0]
    att_refs = refs[1 : 1 + total]
    (
        tok_ref,
        cot_ref,
        w_out_ref,
        vectors_ref,
        w_expand_ref,
        w_reduce_ref,
    ) = refs[1 + total : 7 + total]
    outs = refs[7 + total :]
    layer_ref, first_in_ref, theirs_ref, mine_ref, more_theirs_ref, more_mine_ref = outs[:6]
    grad_refs = outs[6 : 6 + count]
    (
        sums_ref,
        att_all,
        grad_all,
        unit_one,
        scale_one,
        first_wide,
        first_low,
        first_tall,
        active,
        slope,
        gathered,
        second_in,
        second_low,
    ) = outs[6 + count :]
    rank = words_ref[0]
    width = tok_ref.shape[1]
    block = tok_ref.shape[0] // pages
    step = pl.program_id(0)

    def rows_of(at):
        return pl.ds(pl.multiple_of((rank ^ at) * span, span), span)

    @pl.when(step == 0)
    def _():
        for page in range(pages):
            for at in range(count):
                att_all[rows_of(at), page * block : (page + 1) * block] = att_refs[
                    page * count + at
                ][...]
        branch = dot_tn(att_all[: w_out_ref.shape[0]], w_out_ref[...])
        unit, scale = normed(tok_ref[...].astype(F32) + branch)
        unit_one[...] = unit
        scale_one[...] = jnp.broadcast_to(scale, scale_one.shape)
        first_out = unit * vectors_ref[0:1] + vectors_ref[1:2]
        first_wide[...] = first_out
        first_low[...] = first_out.astype(BF16)
        first_tall[...] = first_out.T.astype(BF16)
        gathered[...] = jnp.zeros_like(gathered)
        sums_ref[...] = jnp.zeros_like(sums_ref)

    for chunk in range(chunks):

        @pl.when(step == chunk)
        def _(chunk=chunk):
            expanded = dot(first_low[...], w_expand_ref[...])
            gate = 0.5 + 0.5 * lax.erf(expanded * np.float32(np.sqrt(0.5)))
            bell = jnp.exp(expanded * expanded * -0.5) * np.float32(1.0 / np.sqrt(2.0 * np.pi))
            low = (expanded * gate).astype(BF16)
            active[chunk] = low
            slope[chunk] = gate + expanded * bell
            gathered[...] += dot(low, w_reduce_ref[...])

    @pl.when(step == chunks - 1)
    def _():
        unit, scale = normed(first_wide[...] + gathered[...])
        layer_ref[...] = (unit * vectors_ref[2:3] + vectors_ref[3:4]).astype(BF16)
        cot = cot_ref[...].astype(F32)
        sums_ref[2:3] = column_sum(cot * unit)
        sums_ref[3:4] = column_sum(cot)
        grad = norm_back(cot, vectors_ref[2:3], unit, scale)
        second_in[...] = grad
        second_low[...] = grad.astype(BF16)
        gathered[...] = grad

    for chunk in range(chunks):

        @pl.when(step == 2 * chunks - 1 - chunk)
        def _(chunk=chunk):
            grad_active = dot_nt(second_low[...], w_reduce_ref[...])
            grad_expanded = (grad_active * slope[chunk]).astype(BF16)
            grads_ref = mine_ref if chunk < chunks // 2 else theirs_ref
            grads_ref[:width] = dot(first_tall[...], grad_expanded).astype(BF16)
            grads_ref[width:] = dot_tn(active[chunk], second_low[...]).astype(BF16)
            gathered[...] += dot_nt(grad_expanded, w_expand_ref[...])

    @pl.when(step == 2 * chunks - 1)
    def _():
        unit = unit_one[...]
        grad_out = gathered[...]
        sums_ref[0:1] = column_sum(grad_out * unit)
        sums_ref[1:2] = column_sum(grad_out)
        grad = norm_back(grad_out, vectors_ref[0:1], unit, scale_one[:, :1])
        first_in_ref[...] = grad
        low = grad.astype(BF16)
        real = w_out_ref.shape[0]
        half = real // 2
        core = words_ref[2]
        for ref, side in ((more_mine_ref, core), (more_theirs_ref, 1 - core)):
            rows = pl.ds(pl.multiple_of(side * half, half), half)
            ref[:half] = dot(att_all[rows], low).astype(BF16)
            ref[half:] = jnp.zeros((ref.shape[0] - half, width), BF16)
            ref[half : half + 16] = sums_ref[...].astype(BF16)
        if grad_all.shape[0] > real:
            grad_all[real:] = jnp.zeros((grad_all.shape[0] - real, low.shape[0]), BF16)
        grad_all[:real] = dot_nt(w_out_ref[...], low).astype(BF16)
        for at in range(count):
            grad_refs[at][...] = grad_all[rows_of(at)]


def middle(words, att_parts, tok, cot, w_out, vectors, w_expand, w_reduce, pages, more):
    rows, width = tok.shape
    count = len(att_parts) // pages
    span, block = att_parts[0].shape
    hidden = w_expand.shape[1]
    chunks = hidden // width
    pairs = chunks // 2

    def whole(array):
        return pl.BlockSpec(array.shape, lambda s, words: (0,) * len(array.shape))

    def chunk_at(s, words):
        at = jnp.minimum(s, 2 * chunks - 1 - s)
        return (at + words[2] * pairs) % chunks

    def theirs_at(s, words):
        return jnp.clip(2 * chunks - 1 - s - pairs, 0, pairs - 1), 0

    def mine_at(s, words):
        return jnp.clip(2 * chunks - 1 - s, 0, pairs - 1), 0

    shapes = [
        jax.ShapeDtypeStruct((rows, width), BF16),
        jax.ShapeDtypeStruct((rows, width), F32),
        jax.ShapeDtypeStruct((hidden, width), BF16),
        jax.ShapeDtypeStruct((hidden, width), BF16),
        jax.ShapeDtypeStruct((more, width), BF16),
        jax.ShapeDtypeStruct((more, width), BF16),
    ] + [jax.ShapeDtypeStruct((span, pages * block), BF16)] * count
    specs = [whole(item) for item in shapes]
    specs[2] = pl.BlockSpec((2 * width, width), theirs_at)
    specs[3] = pl.BlockSpec((2 * width, width), mine_at)
    return pl.pallas_call(
        functools.partial(middle_kernel, pages, count, span, chunks),
        grid_spec=pltpu.PrefetchScalarGridSpec(
            num_scalar_prefetch=1,
            grid=(2 * chunks,),
            in_specs=[whole(item) for item in att_parts]
            + [
                whole(tok),
                whole(cot),
                whole(w_out),
                whole(vectors),
                pl.BlockSpec((width, width), lambda s, words: (0, chunk_at(s, words))),
                pl.BlockSpec((width, width), lambda s, words: (chunk_at(s, words), 0)),
            ],
            out_specs=specs,
            scratch_shapes=[
                pltpu.VMEM((16, width), F32),
                pltpu.VMEM((count * span, rows), BF16),
                pltpu.VMEM((count * span, rows), BF16),
                pltpu.VMEM((rows, width), F32),
                pltpu.VMEM((rows, 128), F32),
                pltpu.VMEM((rows, width), F32),
                pltpu.VMEM((rows, width), BF16),
                pltpu.VMEM((width, rows), BF16),
                pltpu.VMEM((chunks, rows, width), BF16),
                pltpu.VMEM((chunks, rows, width), F32),
                pltpu.VMEM((rows, width), F32),
                pltpu.VMEM((rows, width), F32),
                pltpu.VMEM((rows, width), BF16),
            ],
        ),
        out_shape=shapes,
        compiler_params=pltpu.CompilerParams(vmem_limit_bytes=VMEM_LIMIT),
        cost_estimate=pl.CostEstimate(
            flops=2 * rows * width * (6 * hidden + 3 * width),
            bytes_accessed=8 * width * hidden + 16 * rows * width,
            transcendentals=2 * rows * hidden,
        ),
        name="middle",
    )(words, *att_parts, tok, cot, w_out, vectors, w_expand, w_reduce)


def input_kernel(pages, count, span, base, *refs):
    words_ref = refs[0]
    own_refs = refs[1 : 1 + pages]
    message_refs = refs[1 + pages : pages + count]
    weight_refs = refs[pages + count : 3 + pages + count]
    first_in_ref, out_ref, held = refs[3 + pages + count :]
    rank = words_ref[0]
    width = out_ref.shape[1]
    block = out_ref.shape[0] // pages
    for page in range(pages):
        for at in range(count):
            part = message_refs[at - 1] if at else own_refs[page]
            top = base + page * span if at else 0
            place = pl.multiple_of((rank ^ at) * span, span)
            for kind in range(3):
                held[kind, pl.ds(place, span), page * block : (page + 1) * block] = part[
                    top : top + span, kind * block : (kind + 1) * block
                ]
    total = dot(weight_refs[0][...], held[0, :width])
    for kind in range(1, 3):
        total = total + dot(weight_refs[kind][...], held[kind, :width])
    out_ref[...] = (first_in_ref[...] + total.T).astype(BF16)


def input_gradient(words, own, messages, base, span, weights, first_in):
    pages = len(own)
    count = 1 + len(messages)
    rows, width = first_in.shape
    vmem = pl.BlockSpec(memory_space=pltpu.VMEM)
    return pl.pallas_call(
        functools.partial(input_kernel, pages, count, span, base),
        in_specs=[pl.BlockSpec(memory_space=pltpu.SMEM)] + [vmem] * (pages + count + 3),
        out_specs=vmem,
        out_shape=jax.ShapeDtypeStruct((rows, width), BF16),
        scratch_shapes=[pltpu.VMEM((3, count * span, rows), BF16)],
        compiler_params=pltpu.CompilerParams(vmem_limit_bytes=VMEM_LIMIT),
        cost_estimate=pl.CostEstimate(
            flops=6 * rows * width * count * span,
            bytes_accessed=2 * width * (5 * rows + 3 * count * span),
            transcendentals=0,
        ),
        name="input_gradient",
    )(words, *own, *messages, *weights, first_in)


def local(body, name, words, arrays, shapes, costly=False):
    def kernel(words_ref, *refs):
        body(words_ref, refs[: len(arrays)], refs[len(arrays) :])

    vmem = pl.BlockSpec(memory_space=pltpu.VMEM)
    shapes = [jax.ShapeDtypeStruct(shape, kind) for shape, kind in shapes]
    moved = sum(item.size * item.dtype.itemsize for item in list(arrays) + shapes)
    cost = pl.CostEstimate(flops=0, bytes_accessed=moved, transcendentals=0)
    return pl.pallas_call(
        kernel,
        in_specs=[pl.BlockSpec(memory_space=pltpu.SMEM)] + [vmem] * len(arrays),
        out_specs=[vmem] * len(shapes),
        out_shape=shapes,
        compiler_params=pltpu.CompilerParams(vmem_limit_bytes=VMEM_LIMIT),
        cost_estimate=cost if costly else NO_COST,
        name=name,
    )(words, *arrays)


def shard(index, rows, base=0):
    return pl.ds(pl.multiple_of(base + index * rows, 16), rows)


def total_of(refs, rows=slice(None)):
    total = refs[0][rows].astype(F32)
    for ref in refs[1:]:
        total = total + ref[rows].astype(F32)
    return total


def tree_sum(terms):
    while len(terms) > 1:
        terms = [terms[i] + terms[i + 1] for i in range(0, len(terms), 2)]
    return terms[0]


def bit_of(words, level):
    return lax.shift_right_logical(words[1], level) & 1


def pair_sum(words, mine, other):
    def body(words, ins, outs):
        outs[0][...] = total_of(ins).astype(BF16)

    return local(body, "pair_sum", words, [mine, other], [(mine.shape, BF16)])[0]


def halve(words, level, mine, other):
    *lead, rows, width = mine.shape
    half = rows // 2

    def body(words, ins, outs):
        bit = bit_of(words, level)
        for out, side in zip(outs, (bit, 1 - bit)):
            at = shard(side, half)
            out[...] = total_of(ins, (slice(None), at) if lead else at).astype(BF16)

    return local(body, "halve", words, [mine, other], [((*lead, half, width), BF16)] * 2)


def join_halves(words, level, mine, other):
    rows, width = mine.shape

    def body(words, ins, outs):
        bit = bit_of(words, level)
        outs[0][shard(bit, rows)] = ins[0][...]
        outs[0][shard(1 - bit, rows)] = ins[1][...]

    return local(body, "join_halves", words, [mine, other], [((2 * rows, width), BF16)])[0]


def across(block, level):
    return swapped(block, 1 << level, "depth")


class Plan:
    def __init__(self, rows, rows_a, more, span, width):
        self.count = lax.axis_size("blk")
        self.levels = lax.axis_size("depth").bit_length() - 1
        self.rows = rows
        self.rows_a = rows_a
        self.more = more
        self.span = span
        self.width = width
        self.a_ff = rows_a // self.count
        self.a_more = more // self.count
        self.a = self.a_ff + self.a_more
        self.b = (rows - rows_a) // self.count
        self.share = self.a + self.b
        assert width % self.a_ff == 0 and width % self.b == 0 and rows_a % self.b == 0

    def shapes(self, *sizes):
        return [((rows, self.width), BF16) for rows in sizes]

    def scatter_one(self, words, halves):
        count, width = self.count, self.width
        a_ff, half = self.a_ff, self.b // 2

        def kernel(words_ref, *refs):
            parts = refs[6 : 6 + count]
            keep_ref, send_ref = refs[6 + count :]
            for i in range(count):

                @pl.when(pl.program_id(0) == i)
                def _(i=i):
                    parts[i][:a_ff] = total_of(refs[:2]).astype(BF16)
                    parts[i][a_ff:] = total_of(refs[2:4]).astype(BF16)

            bit = bit_of(words_ref, 0)
            keep_ref[0] = total_of(refs[4:6], shard(bit, half)).astype(BF16)
            send_ref[0] = total_of(refs[4:6], shard(1 - bit, half)).astype(BF16)

        def there(rows):
            return pl.BlockSpec((rows, width), lambda i, words: (words[0] ^ i, 0))

        part_b = pl.BlockSpec((self.b, width), lambda i, words: (self.rows_a // self.b + i, 0))
        half_b = pl.BlockSpec((1, half, width), lambda i, words: (i, 0, 0))
        shapes = [jax.ShapeDtypeStruct((self.a, width), BF16)] * count
        shapes += [jax.ShapeDtypeStruct((count, half, width), BF16)] * 2
        *parts_a, keep, send = pl.pallas_call(
            kernel,
            grid_spec=pltpu.PrefetchScalarGridSpec(
                num_scalar_prefetch=1,
                grid=(count,),
                in_specs=[there(a_ff)] * 2 + [there(self.a_more)] * 2 + [part_b] * 2,
                out_specs=[fixed(item) for item in shapes[:count]] + [half_b] * 2,
            ),
            out_shape=shapes,
            compiler_params=pltpu.CompilerParams(vmem_limit_bytes=VMEM_LIMIT),
            cost_estimate=NO_COST,
            name="scatter_one",
        )(words, *halves, *halves[:2])
        return [from_blk(part, i) for i, part in enumerate(parts_a)], keep, across(send, 0)

    def scatter_two(self, words, parts_a, keep_b, other_b, pages):
        count = self.count
        half = self.a // 2
        b_rows = keep_b.shape[1]

        def body(words, ins, outs):
            bit = bit_of(words, 0)
            outs[0][...] = total_of(ins[:count], shard(bit, half)).astype(BF16)
            outs[1][...] = total_of(ins[:count], shard(1 - bit, half)).astype(BF16)
            for i in range(count):
                outs[2 + i][...] = total_of(ins[count : count + 2], words[0] ^ i).astype(BF16)
            for i, out in enumerate(outs[2 + count :]):
                for page in range(len(pages)):
                    piece = ins[count + 2 + page * (count - 1) + i]
                    base = page * self.span
                    out[base : base + self.span, : piece.shape[1]] = piece[...]

        shapes = self.shapes(
            half, half, *[b_rows] * count, *[len(pages) * self.span] * (count - 1)
        )
        pieces = [piece for page in pages for piece in page[1:]]
        keep, send, *rest = local(
            body, "scatter_two", words, [*parts_a, keep_b, other_b, *pieces], shapes
        )
        parts_b = [from_blk(item, i) for i, item in enumerate(rest[:count])]
        return keep, across(send, 0), parts_b, rest[count:]

    def sum_b(self, words, parts_b):
        def body(words, ins, outs):
            outs[0][...] = total_of(ins).astype(BF16)

        return local(body, "sum_b", words, parts_b, self.shapes(parts_b[0].shape[0]))[0]

    def merge(self, words, halves_a, halves_b):
        a, b = self.a // 2, self.b // 2

        def body(words, ins, outs):
            bit = bit_of(words, 0)

            def write(ref, start, rows, to):
                if rows > 0:
                    outs[0][to : to + rows] = ref[start : start + rows]

            for side in range(2):

                @pl.when(bit == side)
                def _(side=side):
                    for at, ref in ((side, ins[0]), (1 - side, ins[1])):
                        cut = max(0, min(a, self.a_ff - at * a))
                        write(ref, 0, cut, at * a)
                        write(ref, cut, a - cut, max(0, at * a - self.a_ff) + self.a_ff + self.b)
                    for at, ref in ((side, ins[2]), (1 - side, ins[3])):
                        write(ref, 0, b, self.a_ff + at * b)

        arrays = [*halves_a, *halves_b]
        return local(body, "merge", words, arrays, self.shapes(self.share))[0]


def gather_blk(part, cut, late=None):
    count = lax.axis_size("blk")
    if count != 4:
        return [(i, 0, from_blk(part, i)) for i in range(count)]
    one, two = swapped(part, 1), swapped(part, 2)
    if late is not None:
        one, two = after(late, (one, two))
    first, second = swapped(one[:cut], 2), swapped(two[cut:], 1)
    return [(0, 0, part), (1, 0, one), (2, 0, two), (3, 0, first), (3, cut, second)]


def with_core(pieces):
    return [(distance, base, from_core(item)) for distance, base, item in pieces]


SLOTS = 4


def widen_own(words, plan, pieces, hidden):
    width = plan.width
    chunks = hidden // width
    pairs = chunks // 2
    arrays = [item for _, _, item in pieces]
    segments = []
    extras = []
    for at, (distance, base, item) in enumerate(pieces):
        stop = base + item.shape[0]
        for start, rows, first in ((0, plan.a_ff, 0), (plan.a_ff, plan.b, plan.rows_a)):
            if base <= start and start + rows <= stop:
                segments.append((at, start - base, rows, distance, first))
        if stop == plan.share:
            extras.append((at, distance))
    assert len(segments) == 2 * plan.count and len(extras) == plan.count

    def kernel(words_ref, *refs):
        ins = refs[: len(arrays)]
        joined_ref, expand_ref, reduce_ref, held, sems = refs[len(arrays) :]
        copies = []
        for index, (at, top, rows, distance, first) in enumerate(segments):
            slot = index % SLOTS
            if index >= SLOTS:
                copies[index - SLOTS].wait()
            part = ins[at][top : top + rows]
            held[slot, :rows] = part.astype(F32)
            place = pl.multiple_of(first + (words_ref[0] ^ distance) * rows, 64)
            joined_ref[pl.ds(place, rows)] = part
            matrix = lax.div(place, width)
            row = place - matrix * width
            chunk = (lax.div(matrix, 2) + words_ref[2] * pairs) % chunks
            column = pl.multiple_of(chunk * width, width)
            source = held.at[slot, :rows]
            to_expand = pltpu.make_async_copy(
                source,
                expand_ref.at[pl.ds(pl.multiple_of(row, 64), rows), pl.ds(column, width)],
                sems.at[slot],
            )
            to_reduce = pltpu.make_async_copy(
                source,
                reduce_ref.at[pl.ds(pl.multiple_of(column + row, 64), rows)],
                sems.at[slot],
            )
            is_expand = lax.rem(matrix, 2) == 0
            pl.when(is_expand)(to_expand.start)
            pl.when(jnp.logical_not(is_expand))(to_reduce.start)
            copies.append(to_reduce)
        for at, distance in extras:
            rows = shard(words_ref[0] ^ distance, plan.a_more, plan.rows)
            joined_ref[rows] = ins[at][ins[at].shape[0] - plan.a_more :]
        for copy in copies[-SLOTS:]:
            copy.wait()

    vmem = pl.BlockSpec(memory_space=pltpu.VMEM)
    anywhere = pl.BlockSpec(memory_space=pl.ANY)
    return pl.pallas_call(
        kernel,
        in_specs=[pl.BlockSpec(memory_space=pltpu.SMEM)] + [vmem] * len(arrays),
        out_specs=[vmem, anywhere, anywhere],
        out_shape=[
            jax.ShapeDtypeStruct((plan.rows + plan.more, width), BF16),
            jax.ShapeDtypeStruct((width, hidden), F32),
            jax.ShapeDtypeStruct((hidden, width), F32),
        ],
        scratch_shapes=[
            pltpu.VMEM((SLOTS, max(plan.a_ff, plan.b), width), F32),
            pltpu.SemaphoreType.DMA((SLOTS,)),
        ],
        compiler_params=pltpu.CompilerParams(vmem_limit_bytes=VMEM_LIMIT),
        cost_estimate=pl.CostEstimate(
            flops=0, bytes_accessed=6 * hidden * width, transcendentals=0
        ),
        name="widen_own",
    )(words, *arrays)


def widen_other(words, joined, expand, reduce):
    width, hidden = expand.shape
    chunks = hidden // width
    pairs = chunks // 2

    def kernel(words_ref, half_ref, before_ref, before_too_ref, expand_ref, reduce_ref):
        expand_ref[...] = half_ref[:width].astype(F32)
        reduce_ref[...] = half_ref[width:].astype(F32)

    def place(s, words):
        return (s + (words[2] + 1) * pairs) % chunks

    anywhere = pl.BlockSpec(memory_space=pl.ANY)
    return pl.pallas_call(
        kernel,
        grid_spec=pltpu.PrefetchScalarGridSpec(
            num_scalar_prefetch=1,
            grid=(pairs,),
            in_specs=[
                pl.BlockSpec((2 * width, width), lambda s, words: (s, 0)),
                anywhere,
                anywhere,
            ],
            out_specs=[
                pl.BlockSpec((width, width), lambda s, words: (0, place(s, words))),
                pl.BlockSpec((width, width), lambda s, words: (place(s, words), 0)),
            ],
        ),
        out_shape=[
            jax.ShapeDtypeStruct((width, hidden), F32),
            jax.ShapeDtypeStruct((hidden, width), F32),
        ],
        input_output_aliases={2: 0, 3: 1},
        compiler_params=pltpu.CompilerParams(vmem_limit_bytes=VMEM_LIMIT),
        cost_estimate=pl.CostEstimate(
            flops=0, bytes_accessed=6 * hidden * width, transcendentals=0
        ),
        name="widen_other",
    )(words, joined, expand, reduce)


def finished(words, plan, heads, joined, side, before=()):
    count = plan.count
    span = plan.span
    width = plan.width
    half_rows = width // 2
    arrays = [item for _, _, item in heads]

    def kernel(words_ref, *refs):
        heads_refs, refs = refs[: len(heads)], refs[len(heads) :]
        extra_ref, refs = refs[0], refs[1 + len(before) :]
        outs, refs = refs[:5], refs[5:]
        gathered, wide, project, sems = refs
        rank = words_ref[0]
        half = words_ref[2] ^ side
        for ref, (distance, base, _) in zip(heads_refs, heads):
            rows = ref.shape[0]
            place = pl.multiple_of((rank ^ distance) * span, HEAD_DIM)
            for part in range(2):
                low, high = max(base, part * span), min(base + rows, (part + 1) * span)
                if low < high:
                    gathered[part, pl.ds(place + (low - part * span), high - low)] = ref[
                        low - base : high - base
                    ]
        for part in range(2):
            wide[part] = gathered[part, :width].astype(F32).T
        project[...] = extra_ref[:half_rows].astype(F32)

        @pl.when(half == 1)
        def _():
            wide[1] = entry_order(wide[1])

        def copy(source, target, at):
            return pltpu.make_async_copy(source, target, sems.at[at])

        for part in range(2):
            pl.when(half == 0)(copy(wide.at[part], outs[part], part).start)
            pl.when(half == 1)(copy(wide.at[part], outs[2 + part], part).start)
        rows = pl.ds(pl.multiple_of(half * half_rows, half_rows), half_rows)
        last = copy(project, outs[4].at[rows], 2)
        last.start()
        for part in range(2):
            copy(wide.at[part], outs[part], part).wait()
        last.wait()

    def whole(item):
        return pl.BlockSpec(item.shape, lambda s: (0, 0))

    more = pl.BlockSpec((plan.more, width), lambda s: (plan.rows // plan.more, 0))
    anywhere = pl.BlockSpec(memory_space=pl.ANY)
    first = 2 + len(heads)
    shapes = [jax.ShapeDtypeStruct((width, width), F32)] * 5
    return pl.pallas_call(
        kernel,
        grid=(1,),
        in_specs=[pl.BlockSpec(memory_space=pltpu.SMEM)]
        + [whole(item) for item in arrays]
        + [more]
        + [anywhere] * len(before),
        out_specs=[anywhere] * 5,
        out_shape=shapes,
        scratch_shapes=[
            pltpu.VMEM((2, count * span, width), BF16),
            pltpu.VMEM((2, width, width), F32),
            pltpu.VMEM((half_rows, width), F32),
            pltpu.SemaphoreType.DMA((3,)),
        ],
        input_output_aliases={first + at: at for at in range(len(before))},
        compiler_params=pltpu.CompilerParams(vmem_limit_bytes=VMEM_LIMIT),
        cost_estimate=pl.CostEstimate(
            flops=0, bytes_accessed=16 * width * width, transcendentals=0
        ),
        name="finish",
    )(words, *arrays, joined, *before)


def per_device(
    tokens,
    boxes,
    w_query,
    w_key,
    w_value,
    w_output,
    box_weight,
    first_gain,
    first_shift,
    w_expand,
    w_reduce,
    second_gain,
    second_shift,
    cotangent,
):
    pages, block, width = tokens.shape
    count = lax.axis_size("blk")
    depth = lax.axis_size("depth")
    words = jnp.stack(
        [lax.axis_index("blk"), lax.axis_index("depth"), lax.axis_index("core")]
    ).astype(jnp.int32)
    hidden = w_expand.shape[1]
    span = -(-HEADS // count) * HEAD_DIM
    unit = 16 * count * depth
    more = -(-(width // 2 + 16) // unit) * unit

    own_places = jnp.stack([boxes[0] + boxes[2], boxes[1] + boxes[3]], axis=1)
    own_places = jnp.stack([lax.shift_right_logical(own_places, 6), own_places & 63], axis=2)
    own_places = own_places.reshape(4 * pages, block).astype(BF16)
    own_places = jnp.pad(own_places, ((0, 16 - 4 * pages), (0, width - block)))
    message = jnp.concatenate([tokens[0], own_places])
    messages = [from_blk(message, i) for i in range(count)]
    w_own, box_own, rot_cos, rot_sin = prepare(
        words, w_query, w_key, w_value, box_weight, span, count * block
    )
    messages, rot_cos = lax.optimization_barrier((messages, rot_cos))
    own = after(messages, tokens[1])
    pieces = [messages, [from_blk(own, i) for i in range(count)]]

    saved = []
    att_parts = []
    for page in range(pages):
        results = attention_forward(
            words, page, messages, pieces[page], w_own, box_own, rot_cos, rot_sin
        )
        saved.append(results[:6])
        att_parts += [from_blk(results[6 + i], i) for i in range(count)]

    vectors = jnp.stack([first_gain, first_shift, second_gain, second_shift])
    results = middle(
        words,
        att_parts,
        tokens.reshape(pages * block, width),
        cotangent.reshape(pages * block, width),
        w_output,
        vectors,
        w_expand,
        w_reduce,
        pages,
        more,
    )
    layer_out, first_in, theirs, mine, more_theirs, more_mine = results[:6]
    grads = [from_blk(results[6 + i], i) for i in range(count)]
    plan = Plan(hidden, hidden - hidden // 2 // unit * unit, more, span, width)
    parts_a, keep_b, other_b = plan.scatter_one(
        after(grads[:2], words), [mine, from_core(theirs), more_mine, from_core(more_theirs)]
    )

    def backward(page, words, before=None):
        return attention_backward(
            words,
            page,
            grads,
            pieces[page],
            saved[page],
            box_own,
            rot_cos,
            rot_sin,
            before,
        )

    *pre_one, before = backward(0, after(parts_a[0], words))
    done = before
    for level in range(1, plan.levels):
        keep_b, send_b = halve(after(done, words), level, keep_b, other_b)
        other_b = across(send_b, level)
        done = keep_b
    *pre_two, heads_mine, heads_theirs = backward(1, after(done, words), before)
    own = [pre_one[0], pre_two[0]]
    part_a, other_a, parts_b, messages = plan.scatter_two(
        after(heads_mine, words), parts_a, keep_b, other_b, [pre_one, pre_two]
    )
    heads, other = halve(
        after(part_a, words), 0, heads_mine, from_core(after(part_a, heads_theirs))
    )
    part_b = plan.sum_b(after(heads, words), parts_b)
    messages = [from_blk(item, i + 1) for i, item in enumerate(after(part_b, messages))]
    part_a = pair_sum(after(part_b, words), part_a, other_a)
    other = after(part_a, other)
    done = part_a
    for level in range(plan.levels - 1, 0, -1):
        part_b = join_halves(after(done, words), level, part_b, across(part_b, level))
        done = part_b
    halves_b = [part_b, across(part_b, 0)]
    for level in range(1, plan.levels):
        part_a = pair_sum(after(done, words), part_a, across(part_a, level))
        done = part_a
    other = across(after((part_a, halves_b), other), 0)
    input_grad = input_gradient(
        after(done, words),
        own,
        messages,
        0,
        span,
        (w_query, w_key, w_value),
        first_in,
    )
    share = plan.merge(after(input_grad, words), [part_a, across(part_a, 0)], halves_b)
    heads = pair_sum(after(share, words), heads, other)
    for level in range(1, plan.levels):
        heads = pair_sum(words, heads, across(heads, level))
    pieces = gather_blk(share, plan.a_ff, heads)
    heads = join_halves(after(pieces[1][2], words), 0, heads, across(heads, 0))
    heads = after([item for _, _, item in pieces], heads)
    joined, *wide = widen_own(after(heads, words), plan, pieces, hidden)
    pieces_heads = gather_blk(heads, span, joined)
    joined_other = from_core(after(pieces_heads[1][2], joined))
    grads = finished(words, plan, pieces_heads, joined, 0)
    at = plan.rows + width // 2
    sums = jnp.where(words[2] == 0, joined[at : at + 4], joined_other[at : at + 4])
    sums = [sums[i].astype(F32) for i in range(4)]
    grad_expand, grad_reduce = widen_other(after((grads, sums), words), joined_other, *wide)
    grad_query, grad_key, grad_value, grad_box, grad_project = finished(
        after(grad_expand, words), plan, with_core(pieces_heads), joined_other, 1, grads
    )
    return (
        layer_out.reshape(tokens.shape),
        input_grad.reshape(tokens.shape),
        grad_query,
        grad_key,
        grad_value,
        grad_project,
        grad_box,
        sums[0],
        sums[1],
        grad_expand,
        grad_reduce,
        sums[2],
        sums[3],
    )


def solution(mesh):
    blocks, rest = mesh.devices.shape
    parts = jax.sharding.Mesh(
        mesh.devices.reshape(blocks, rest // 2, 2), ("blk", "depth", "core")
    )
    split = P(("depth", "core"), "blk", None)
    return jax.shard_map(
        per_device,
        mesh=parts,
        in_specs=(split, P(None, ("depth", "core"), "blk")) + (P(),) * 11 + (split,),
        out_specs=(split, split) + (P(),) * 11,
        check_vma=False,
    )
```

```python
import functools

import jax
import jax.numpy as jnp
import numpy as np
from jax import lax
from jax.experimental import pallas as pl
from jax.experimental.pallas import tpu as pltpu
from jax.sharding import PartitionSpec as P

HEADS = 12
HEAD_DIM = 64
HALF = 32
FREQS = 192
CODES = 4 * FREQS
VMEM_LIMIT = 60 * 1024 * 1024
NO_COST = pl.CostEstimate(flops=0, bytes_accessed=0, transcendentals=0)
F32 = jnp.float32
BF16 = jnp.bfloat16


def dot(left, right):
    return lax.dot_general(left, right, (((1,), (0,)), ((), ())), preferred_element_type=F32)


def dot_nt(left, right):
    return lax.dot_general(left, right, (((1,), (1,)), ((), ())), preferred_element_type=F32)


def dot_tn(left, right):
    return lax.dot_general(left, right, (((0,), (0,)), ((), ())), preferred_element_type=F32)


def swapped(block, distance, axis="blk"):
    count = lax.axis_size(axis)
    return lax.ppermute(block, axis, [(i, i ^ distance) for i in range(count)])


def from_blk(block, distance):
    return swapped(block, distance) if distance else block


def from_core(block):
    return swapped(block, 1, "core")


def after(done, value):
    return lax.optimization_barrier((value, done))[0]


def turned(upper, lower, cosines, sines):
    return upper * cosines - lower * sines, lower * cosines + upper * sines


def entry_order(rows):
    return jnp.concatenate(
        [
            rows[:FREQS],
            rows[2 * FREQS : 3 * FREQS],
            rows[FREQS : 2 * FREQS],
            rows[3 * FREQS :],
        ],
        axis=0,
    )


def angle_tables():
    rates = np.float32(10000.0) ** (-np.arange(FREQS, dtype=np.float32) / np.float32(FREQS))
    tables = []
    for places in (32.0 * np.arange(32), 0.5 * np.arange(64)):
        angles = rates.astype(np.float64)[:, None] * places[None, :]
        left = np.concatenate([np.sin(angles), np.cos(angles)])
        parts = []
        for _ in range(3):
            parts.append(left.astype(jnp.bfloat16))
            left = left - parts[-1].astype(np.float64)
        tables.append(np.concatenate(parts, axis=1))
    return tables


def rotary_tables(length):
    rates = np.float32(10000.0) ** (-np.arange(HALF, dtype=np.float32) / np.float32(HALF))
    angles = np.arange(length, dtype=np.float32)[None, :] * rates[:, None]
    angles = angles.astype(np.float64)
    return np.cos(angles).astype(np.float32), np.sin(angles).astype(np.float32)


def prepare_kernel(
    words_ref,
    query_ref,
    key_ref,
    value_ref,
    box_ref,
    cos_ref,
    sin_ref,
    own_ref,
    own_box_ref,
    own_cos_ref,
    own_sin_ref,
):
    rank = words_ref[0]
    span = own_box_ref.shape[0]
    width = query_ref.shape[1]
    count = lax.axis_size("blk")
    block = cos_ref.shape[1] // count
    row = lax.broadcasted_iota(jnp.int32, (span, width), 0) + rank * span
    column = lax.broadcasted_iota(jnp.int32, (span, width), 1)
    pick = jnp.where(row == column, 1.0, 0.0).astype(BF16)
    for kind, ref in enumerate((query_ref, key_ref, value_ref)):
        own_ref[kind * span : (kind + 1) * span] = dot_nt(pick, ref[...]).astype(BF16)
    own_box_ref[...] = dot_nt(pick, entry_order(box_ref[...])).astype(BF16)
    for i in range(count):
        from_cols = pl.ds(pl.multiple_of((rank ^ i) * block, block), block)
        own_cos_ref[:, i * block : (i + 1) * block] = cos_ref[:, from_cols]
        own_sin_ref[:, i * block : (i + 1) * block] = sin_ref[:, from_cols]


def prepare(words, w_query, w_key, w_value, box_weight, span, length):
    width = w_query.shape[0]
    vmem = pl.BlockSpec(memory_space=pltpu.VMEM)
    return pl.pallas_call(
        prepare_kernel,
        in_specs=[pl.BlockSpec(memory_space=pltpu.SMEM)] + [vmem] * 6,
        out_specs=[vmem] * 4,
        out_shape=[
            jax.ShapeDtypeStruct((3 * span, width), BF16),
            jax.ShapeDtypeStruct((span, CODES), BF16),
            jax.ShapeDtypeStruct((HALF, length), F32),
            jax.ShapeDtypeStruct((HALF, length), F32),
        ],
        compiler_params=pltpu.CompilerParams(vmem_limit_bytes=VMEM_LIMIT),
        cost_estimate=pl.CostEstimate(
            flops=8 * span * width * width, bytes_accessed=10 * width * width, transcendentals=0
        ),
        name="prepare",
    )(words, w_query, w_key, w_value, box_weight, *map(jnp.asarray, rotary_tables(length)))


def fold(value, combine):
    while value.shape[0] > 8:
        half = value.shape[0] // 2
        value = combine(value[:half], value[half:])
    return value


def write_codes(page, place_refs, high_ref, low_ref, sin_ref, cos_ref, codes_ref):
    block = sin_ref.shape[1] // len(place_refs)

    def looked_up(table_ref, index):
        spots = table_ref.shape[1] // 3
        rows = lax.broadcasted_iota(jnp.int32, (spots, block), 0).astype(F32)
        once = jnp.where(rows == index, 1.0, 0.0)
        found = dot(table_ref[...], jnp.concatenate([once] * 3, axis=0).astype(BF16))
        return found[:FREQS], found[FREQS:]

    for i, place_ref in enumerate(place_refs):
        columns = slice(i * block, (i + 1) * block)
        places = place_ref[:, :block].astype(F32)
        for axis in range(2):
            at = 4 * page + 2 * axis
            high_sin, high_cos = looked_up(high_ref, places[at : at + 1])
            low_sin, low_cos = looked_up(low_ref, places[at + 1 : at + 2])
            sines = high_sin * low_cos + high_cos * low_sin
            cosines = high_cos * low_cos - high_sin * low_sin
            rows = slice(axis * FREQS, (axis + 1) * FREQS)
            later = slice((2 + axis) * FREQS, (3 + axis) * FREQS)
            sin_ref[rows, columns] = sines
            cos_ref[rows, columns] = cosines
            codes_ref[rows, columns] = sines.astype(BF16)
            codes_ref[later, columns] = cosines.astype(BF16)


def forward_kernel(page, count, words_ref, *refs):
    place_refs, refs = refs[:count], refs[count:]
    piece_refs, refs = refs[:count], refs[count:]
    high_ref, low_ref, w_ref, box_ref, rot_cos_ref, rot_sin_ref = refs[:6]
    probs_ref, att_ref, heads_ref, sin_ref, cos_ref, codes_ref = refs[6:12]
    low_refs = refs[12 : 12 + count]
    tok_ref, pre_ref, kc_ref, qr_ref = refs[12 + count :]
    rows = tok_ref.shape[0]
    block = rows // count
    head = pl.program_id(0)
    span = pl.num_programs(0) * HEAD_DIM

    @pl.when(head == 0)
    def _():
        for i in range(count):
            tok_ref[i * block : (i + 1) * block] = piece_refs[i][...]
        pre_ref[...] = dot_nt(w_ref[...], tok_ref[...])
        write_codes(page, place_refs, high_ref, low_ref, sin_ref, cos_ref, codes_ref)
        kc_ref[:, :CODES] = codes_ref[...].astype(F32).T.astype(BF16)

    def pre(kind):
        at = kind * span + head * HEAD_DIM
        return pre_ref[pl.ds(pl.multiple_of(at, HEAD_DIM), HEAD_DIM)]

    rot_cos = rot_cos_ref[...]
    rot_sin = rot_sin_ref[...]
    query_pre = pre(0).astype(BF16)
    wide = query_pre.astype(F32)
    query = jnp.concatenate(turned(wide[:HALF], wide[HALF:], rot_cos, rot_sin), axis=0)
    key_pre = pre(1)
    key = jnp.concatenate(turned(key_pre[:HALF], key_pre[HALF:], rot_cos, rot_sin), axis=0)
    value = pre(2).astype(BF16)
    heads_ref[0, :HEAD_DIM] = query_pre
    heads_ref[0, HEAD_DIM : 2 * HEAD_DIM] = query.astype(BF16)
    heads_ref[0, 2 * HEAD_DIM : 3 * HEAD_DIM] = key.astype(BF16)
    heads_ref[0, 3 * HEAD_DIM :] = value
    kc_ref[:, CODES:] = key.T.astype(BF16)
    qr_ref[CODES:] = (query * 0.125).astype(BF16)
    step = min(256, block)

    def logits_at(at):
        part = slice(at, at + step)
        projected = dot_tn(box_ref[...], query_pre[:, part])
        sines = sin_ref[:, part]
        cosines = cos_ref[:, part]
        upper = projected[: 2 * FREQS]
        lower = projected[2 * FREQS :]
        qr_ref[: 2 * FREQS, part] = ((upper * cosines + lower * sines) * 0.125).astype(BF16)
        qr_ref[2 * FREQS : CODES, part] = ((lower * cosines - upper * sines) * 0.125).astype(BF16)
        return dot(kc_ref[...], qr_ref[:, part])

    following = logits_at(0)
    for at in range(0, rows, step):
        logits = following
        if at + step < rows:
            following = logits_at(at + step)
        peak = jnp.max(fold(logits, jnp.maximum), axis=0, keepdims=True)
        weight = jnp.exp(logits - peak)
        total = jnp.sum(fold(weight, jnp.add), axis=0, keepdims=True)
        probs = (weight * (1.0 / total)).astype(BF16)
        probs_ref[0, :, at : at + step] = probs
        attended = dot(value, probs)
        att_ref[0, :, at : at + step] = attended
        inner = at % block
        low_refs[at // block][:, inner : inner + step] = attended.astype(BF16)


def fixed(array):
    return pl.BlockSpec(array.shape, lambda *at: (0,) * len(array.shape))


def attention_forward(words, page, messages, pieces, w_own, box_own, rot_cos, rot_sin):
    count = len(messages)
    block, width = messages[0].shape[0] - 16, messages[0].shape[1]
    rows = count * block
    span = box_own.shape[0]
    heads = span // HEAD_DIM
    tables = [jnp.asarray(item) for item in angle_tables()]
    specs = [pl.BlockSpec((block, width), lambda h, words: (0, 0))] * count
    places = pl.BlockSpec((16, width), lambda h, words: (block // 16, 0))
    out_shape = [
        jax.ShapeDtypeStruct((heads, rows, rows), BF16),
        jax.ShapeDtypeStruct((heads, HEAD_DIM, rows), F32),
        jax.ShapeDtypeStruct((heads, 4 * HEAD_DIM, rows), BF16),
        jax.ShapeDtypeStruct((2 * FREQS, rows), F32),
        jax.ShapeDtypeStruct((2 * FREQS, rows), F32),
        jax.ShapeDtypeStruct((CODES, rows), BF16),
    ] + [jax.ShapeDtypeStruct((span, block), BF16)] * count
    return pl.pallas_call(
        functools.partial(forward_kernel, page, count),
        grid_spec=pltpu.PrefetchScalarGridSpec(
            num_scalar_prefetch=1,
            grid=(heads,),
            in_specs=[places] * count
            + specs
            + [fixed(item) for item in (*tables, w_own)]
            + [
                pl.BlockSpec((HEAD_DIM, CODES), lambda h, words: (h, 0)),
                fixed(rot_cos),
                fixed(rot_sin),
            ],
            out_specs=[
                pl.BlockSpec((1, rows, rows), lambda h, words: (h, 0, 0)),
                pl.BlockSpec((1, HEAD_DIM, rows), lambda h, words: (h, 0, 0)),
                pl.BlockSpec((1, 4 * HEAD_DIM, rows), lambda h, words: (h, 0, 0)),
            ]
            + [fixed(item) for item in out_shape[3:6]]
            + [pl.BlockSpec((HEAD_DIM, block), lambda h, words: (h, 0))] * count,
            scratch_shapes=[
                pltpu.VMEM((rows, width), BF16),
                pltpu.VMEM((3 * span, rows), F32),
                pltpu.VMEM((rows, CODES + HEAD_DIM), BF16),
                pltpu.VMEM((CODES + HEAD_DIM, rows), BF16),
            ],
        ),
        out_shape=out_shape,
        compiler_params=pltpu.CompilerParams(vmem_limit_bytes=VMEM_LIMIT),
        cost_estimate=pl.CostEstimate(
            flops=2 * heads * rows * (rows * 1100 + 200 * width + 64 * CODES),
            bytes_accessed=2 * heads * rows * rows + 12 * rows * width,
            transcendentals=heads * rows * rows,
        ),
        name="attention_forward",
    )(words, *messages, *pieces, *tables, w_own, box_own, rot_cos, rot_sin)


def backward_kernel(count, last, words_ref, *refs):
    grad_refs, refs = refs[:count], refs[count:]
    piece_refs, refs = refs[:count], refs[count:]
    probs_ref, att_ref, heads_ref, box_ref, codes_ref, sin_ref, cos_ref = refs[:7]
    rot_cos_ref, rot_sin_ref = refs[7:9]
    refs = refs[9:]
    if last:
        before_ref, refs = refs[0], refs[1:]
    pre_refs, refs = refs[:count], refs[count:]
    if last:
        mine_ref, theirs_ref, *refs = refs
    weight_grad_ref, kc_ref, logit_grad_ref, entry_grad_ref, turned_ref = refs
    block, width = piece_refs[0].shape
    rows = count * block
    head = pl.program_id(0)
    span = pl.num_programs(0) * HEAD_DIM

    @pl.when(head == 0)
    def _():
        kc_ref[:CODES] = codes_ref[...]

    kc_ref[CODES:] = heads_ref[0, 2 * HEAD_DIM : 3 * HEAD_DIM]
    packed = heads_ref[0].astype(F32).T.astype(BF16)
    query_pre = packed[:, :HEAD_DIM]
    query = packed[:, HEAD_DIM : 2 * HEAD_DIM]
    value = packed[:, 3 * HEAD_DIM :] * jnp.asarray(0.125, BF16)
    rot_cos = rot_cos_ref[...]
    rot_sin = rot_sin_ref[...]
    grad = jnp.concatenate([ref[...] for ref in grad_refs], axis=1)
    grad_tall = grad.astype(F32).T.astype(BF16)
    offsets = jnp.sum(grad.astype(F32) * att_ref[0], axis=0, keepdims=True) * 0.125
    step = min(256, block)
    place = pl.multiple_of(head * HEAD_DIM, HEAD_DIM)
    here = pl.ds(place, HEAD_DIM)

    def logits_back(at):
        part = slice(at, at + step)
        grad_probs = dot(value, grad[:, part])
        logit_grad_ref[:, part] = (
            probs_ref[0, :, part].astype(F32) * (grad_probs - offsets[:, part])
        ).astype(BF16)

    logits_back(0)
    for at in range(0, rows, step):
        if at + step < rows:
            logits_back(at + step)
        part = slice(at, at + step)
        back = dot(kc_ref[...], logit_grad_ref[:, part])
        sines = sin_ref[:, part]
        cosines = cos_ref[:, part]
        upper = back[: 2 * FREQS]
        lower = back[2 * FREQS : CODES]
        entry_grad_ref[: 2 * FREQS, part] = (upper * cosines - lower * sines).astype(BF16)
        entry_grad_ref[2 * FREQS :, part] = (lower * cosines + upper * sines).astype(BF16)
        first = back[CODES : CODES + HALF]
        second = back[CODES + HALF :]
        turned_ref[:HALF, part], turned_ref[HALF:, part] = turned(
            first, second, rot_cos[:, part], -rot_sin[:, part]
        )
    key_flat = dot(logit_grad_ref[...], query).T
    value_low = dot(probs_ref[0], grad_tall).T.astype(BF16)
    query_low = (turned_ref[...] + dot(box_ref[...], entry_grad_ref[...])).astype(BF16)
    key_low = jnp.concatenate(
        turned(key_flat[:HALF], key_flat[HALF:], rot_cos, -rot_sin), axis=0
    ).astype(BF16)
    for i in range(count):
        columns = slice(i * block, (i + 1) * block)
        pre_refs[i][here, :block] = query_low[:, columns]
        pre_refs[i][here, block : 2 * block] = key_low[:, columns]
        pre_refs[i][here, 2 * block :] = value_low[:, columns]
    weight_grad_ref[pl.ds(3 * span + place, HEAD_DIM)] = dot(entry_grad_ref[...], query_pre).T

    @pl.when(head == pl.num_programs(0) - 1)
    def _():
        for kind in range(3):
            columns = slice(kind * block, (kind + 1) * block)
            total = dot(pre_refs[0][:, columns], piece_refs[0][...])
            for i in range(1, count):
                total = total + dot(pre_refs[i][:, columns], piece_refs[i][...])
            weight_grad_ref[kind * span : (kind + 1) * span] = total
        if last:
            half = 2 * span
            core = words_ref[2]
            ours = pl.ds(pl.multiple_of(core * half, half), half)
            there = pl.ds(pl.multiple_of((1 - core) * half, half), half)
            mine_ref[...] = weight_grad_ref[ours] + before_ref[ours]
            theirs_ref[...] = (weight_grad_ref[there] + before_ref[there]).astype(BF16)


def attention_backward(
    words, page, grads, pieces, saved, box_own, rot_cos, rot_sin, before=None
):
    probs, att, heads_saved, sines, cosines, codes = saved
    count = len(pieces)
    rows, width = probs.shape[1], pieces[0].shape[1]
    block = rows // count
    span = box_own.shape[0]
    heads = span // HEAD_DIM
    last = before is not None
    extra = (before,) if last else ()
    full_shape = (4 * span, width)
    specs = [pl.BlockSpec((block, width), lambda h, words: (0, 0))] * count
    out_shape = [jax.ShapeDtypeStruct((span, 3 * block), BF16)] * count
    if last:
        out_shape += [
            jax.ShapeDtypeStruct((2 * span, width), F32),
            jax.ShapeDtypeStruct((2 * span, width), BF16),
        ]
    else:
        out_shape.append(jax.ShapeDtypeStruct(full_shape, F32))
    return pl.pallas_call(
        functools.partial(backward_kernel, count, last),
        grid_spec=pltpu.PrefetchScalarGridSpec(
            num_scalar_prefetch=1,
            grid=(heads,),
            in_specs=[pl.BlockSpec((HEAD_DIM, block), lambda h, words: (h, page))] * count
            + specs
            + [
                pl.BlockSpec((1, rows, rows), lambda h, words: (h, 0, 0)),
                pl.BlockSpec((1, HEAD_DIM, rows), lambda h, words: (h, 0, 0)),
                pl.BlockSpec((1, 4 * HEAD_DIM, rows), lambda h, words: (h, 0, 0)),
                pl.BlockSpec((HEAD_DIM, CODES), lambda h, words: (h, 0)),
            ]
            + [fixed(item) for item in (codes, sines, cosines, rot_cos, rot_sin, *extra)],
            out_specs=[fixed(item) for item in out_shape],
            scratch_shapes=([pltpu.VMEM(full_shape, F32)] if last else [])
            + [
                pltpu.VMEM((CODES + HEAD_DIM, rows), BF16),
                pltpu.VMEM((rows, rows), BF16),
                pltpu.VMEM((CODES, rows), BF16),
                pltpu.VMEM((HEAD_DIM, rows), F32),
            ],
        ),
        out_shape=out_shape,
        compiler_params=pltpu.CompilerParams(vmem_limit_bytes=VMEM_LIMIT),
        cost_estimate=pl.CostEstimate(
            flops=2 * heads * rows * (rows * 1400 + 200 * width + 128 * CODES),
            bytes_accessed=2 * heads * rows * rows + 12 * rows * width,
            transcendentals=0,
        ),
        name="attention_backward",
    )(
        words,
        *grads,
        *pieces,
        probs,
        att,
        heads_saved,
        box_own,
        codes,
        sines,
        cosines,
        rot_cos,
        rot_sin,
        *extra,
    )


def normed(value):
    centered = value - jnp.mean(value, axis=-1, keepdims=True)
    scale = lax.rsqrt(jnp.mean(centered * centered, axis=-1, keepdims=True) + 1e-05)
    return centered * scale, scale


def norm_back(grad, gain, unit, scale):
    scaled = grad * gain
    return scale * (
        scaled
        - jnp.mean(scaled, axis=-1, keepdims=True)
        - unit * jnp.mean(scaled * unit, axis=-1, keepdims=True)
    )


def column_sum(value):
    return jnp.sum(value, axis=0, keepdims=True)


def middle_kernel(pages, count, span, chunks, *refs):
    total = pages * count
    words_ref = refs[0]
    att_refs = refs[1 : 1 + total]
    (
        tok_ref,
        cot_ref,
        w_out_ref,
        vectors_ref,
        w_expand_ref,
        w_reduce_ref,
    ) = refs[1 + total : 7 + total]
    outs = refs[7 + total :]
    layer_ref, first_in_ref, theirs_ref, mine_ref, more_theirs_ref, more_mine_ref = outs[:6]
    grad_refs = outs[6 : 6 + count]
    (
        sums_ref,
        att_all,
        grad_all,
        unit_one,
        scale_one,
        first_wide,
        first_low,
        first_tall,
        active,
        slope,
        gathered,
        second_in,
        second_low,
    ) = outs[6 + count :]
    rank = words_ref[0]
    width = tok_ref.shape[1]
    block = tok_ref.shape[0] // pages
    step = pl.program_id(0)

    def rows_of(at):
        return pl.ds(pl.multiple_of((rank ^ at) * span, span), span)

    @pl.when(step == 0)
    def _():
        for page in range(pages):
            for at in range(count):
                att_all[rows_of(at), page * block : (page + 1) * block] = att_refs[
                    page * count + at
                ][...]
        branch = dot_tn(att_all[: w_out_ref.shape[0]], w_out_ref[...])
        unit, scale = normed(tok_ref[...].astype(F32) + branch)
        unit_one[...] = unit
        scale_one[...] = jnp.broadcast_to(scale, scale_one.shape)
        first_out = unit * vectors_ref[0:1] + vectors_ref[1:2]
        first_wide[...] = first_out
        first_low[...] = first_out.astype(BF16)
        first_tall[...] = first_out.T.astype(BF16)
        gathered[...] = jnp.zeros_like(gathered)
        sums_ref[...] = jnp.zeros_like(sums_ref)

    for chunk in range(chunks):

        @pl.when(step == chunk)
        def _(chunk=chunk):
            expanded = dot(first_low[...], w_expand_ref[...])
            gate = 0.5 + 0.5 * lax.erf(expanded * np.float32(np.sqrt(0.5)))
            bell = jnp.exp(expanded * expanded * -0.5) * np.float32(1.0 / np.sqrt(2.0 * np.pi))
            low = (expanded * gate).astype(BF16)
            active[chunk] = low
            slope[chunk] = gate + expanded * bell
            gathered[...] += dot(low, w_reduce_ref[...])

    @pl.when(step == chunks - 1)
    def _():
        unit, scale = normed(first_wide[...] + gathered[...])
        layer_ref[...] = (unit * vectors_ref[2:3] + vectors_ref[3:4]).astype(BF16)
        cot = cot_ref[...].astype(F32)
        sums_ref[2:3] = column_sum(cot * unit)
        sums_ref[3:4] = column_sum(cot)
        grad = norm_back(cot, vectors_ref[2:3], unit, scale)
        second_in[...] = grad
        second_low[...] = grad.astype(BF16)
        gathered[...] = grad

    for chunk in range(chunks):

        @pl.when(step == 2 * chunks - 1 - chunk)
        def _(chunk=chunk):
            grad_active = dot_nt(second_low[...], w_reduce_ref[...])
            grad_expanded = (grad_active * slope[chunk]).astype(BF16)
            grads_ref = mine_ref if chunk < chunks // 2 else theirs_ref
            grads_ref[:width] = dot(first_tall[...], grad_expanded).astype(BF16)
            grads_ref[width:] = dot_tn(active[chunk], second_low[...]).astype(BF16)
            gathered[...] += dot_nt(grad_expanded, w_expand_ref[...])

    @pl.when(step == 2 * chunks - 1)
    def _():
        unit = unit_one[...]
        grad_out = gathered[...]
        sums_ref[0:1] = column_sum(grad_out * unit)
        sums_ref[1:2] = column_sum(grad_out)
        grad = norm_back(grad_out, vectors_ref[0:1], unit, scale_one[:, :1])
        first_in_ref[...] = grad
        low = grad.astype(BF16)
        real = w_out_ref.shape[0]
        half = real // 2
        core = words_ref[2]
        for ref, side in ((more_mine_ref, core), (more_theirs_ref, 1 - core)):
            rows = pl.ds(pl.multiple_of(side * half, half), half)
            ref[:half] = dot(att_all[rows], low).astype(BF16)
            ref[half:] = jnp.zeros((ref.shape[0] - half, width), BF16)
            ref[half : half + 16] = sums_ref[...].astype(BF16)
        if grad_all.shape[0] > real:
            grad_all[real:] = jnp.zeros((grad_all.shape[0] - real, low.shape[0]), BF16)
        grad_all[:real] = dot_nt(w_out_ref[...], low).astype(BF16)
        for at in range(count):
            grad_refs[at][...] = grad_all[rows_of(at)]


def middle(words, att_parts, tok, cot, w_out, vectors, w_expand, w_reduce, pages, more):
    rows, width = tok.shape
    count = len(att_parts) // pages
    span, block = att_parts[0].shape
    hidden = w_expand.shape[1]
    chunks = hidden // width
    pairs = chunks // 2

    def whole(array):
        return pl.BlockSpec(array.shape, lambda s, words: (0,) * len(array.shape))

    def chunk_at(s, words):
        at = jnp.minimum(s, 2 * chunks - 1 - s)
        return (at + words[2] * pairs) % chunks

    def theirs_at(s, words):
        return jnp.clip(2 * chunks - 1 - s - pairs, 0, pairs - 1), 0

    def mine_at(s, words):
        return jnp.clip(2 * chunks - 1 - s, 0, pairs - 1), 0

    shapes = [
        jax.ShapeDtypeStruct((rows, width), BF16),
        jax.ShapeDtypeStruct((rows, width), F32),
        jax.ShapeDtypeStruct((hidden, width), BF16),
        jax.ShapeDtypeStruct((hidden, width), BF16),
        jax.ShapeDtypeStruct((more, width), BF16),
        jax.ShapeDtypeStruct((more, width), BF16),
    ] + [jax.ShapeDtypeStruct((span, pages * block), BF16)] * count
    specs = [whole(item) for item in shapes]
    specs[2] = pl.BlockSpec((2 * width, width), theirs_at)
    specs[3] = pl.BlockSpec((2 * width, width), mine_at)
    return pl.pallas_call(
        functools.partial(middle_kernel, pages, count, span, chunks),
        grid_spec=pltpu.PrefetchScalarGridSpec(
            num_scalar_prefetch=1,
            grid=(2 * chunks,),
            in_specs=[whole(item) for item in att_parts]
            + [
                whole(tok),
                whole(cot),
                whole(w_out),
                whole(vectors),
                pl.BlockSpec((width, width), lambda s, words: (0, chunk_at(s, words))),
                pl.BlockSpec((width, width), lambda s, words: (chunk_at(s, words), 0)),
            ],
            out_specs=specs,
            scratch_shapes=[
                pltpu.VMEM((16, width), F32),
                pltpu.VMEM((count * span, rows), BF16),
                pltpu.VMEM((count * span, rows), BF16),
                pltpu.VMEM((rows, width), F32),
                pltpu.VMEM((rows, 128), F32),
                pltpu.VMEM((rows, width), F32),
                pltpu.VMEM((rows, width), BF16),
                pltpu.VMEM((width, rows), BF16),
                pltpu.VMEM((chunks, rows, width), BF16),
                pltpu.VMEM((chunks, rows, width), F32),
                pltpu.VMEM((rows, width), F32),
                pltpu.VMEM((rows, width), F32),
                pltpu.VMEM((rows, width), BF16),
            ],
        ),
        out_shape=shapes,
        compiler_params=pltpu.CompilerParams(vmem_limit_bytes=VMEM_LIMIT),
        cost_estimate=pl.CostEstimate(
            flops=2 * rows * width * (6 * hidden + 3 * width),
            bytes_accessed=8 * width * hidden + 16 * rows * width,
            transcendentals=2 * rows * hidden,
        ),
        name="middle",
    )(words, *att_parts, tok, cot, w_out, vectors, w_expand, w_reduce)


def input_kernel(pages, count, span, *refs):
    words_ref = refs[0]
    part_refs = refs[1 : 1 + pages * count]
    weight_refs = refs[1 + pages * count : 4 + pages * count]
    first_in_ref, out_ref, held = refs[4 + pages * count :]
    rank = words_ref[0]
    width = out_ref.shape[1]
    block = out_ref.shape[0] // pages
    for page in range(pages):
        for at in range(count):
            part = part_refs[page * count + at]
            place = pl.multiple_of((rank ^ at) * span, span)
            for kind in range(3):
                held[kind, pl.ds(place, span), page * block : (page + 1) * block] = part[
                    :, kind * block : (kind + 1) * block
                ]
    total = dot(weight_refs[0][...], held[0, :width])
    for kind in range(1, 3):
        total = total + dot(weight_refs[kind][...], held[kind, :width])
    out_ref[...] = (first_in_ref[...] + total.T).astype(BF16)


def input_gradient(words, parts, weights, first_in):
    pages, count = len(parts), len(parts[0])
    span = parts[0][0].shape[0]
    rows, width = first_in.shape
    vmem = pl.BlockSpec(memory_space=pltpu.VMEM)
    return pl.pallas_call(
        functools.partial(input_kernel, pages, count, span),
        in_specs=[pl.BlockSpec(memory_space=pltpu.SMEM)] + [vmem] * (pages * count + 4),
        out_specs=vmem,
        out_shape=jax.ShapeDtypeStruct((rows, width), BF16),
        scratch_shapes=[pltpu.VMEM((3, count * span, rows), BF16)],
        compiler_params=pltpu.CompilerParams(vmem_limit_bytes=VMEM_LIMIT),
        cost_estimate=pl.CostEstimate(
            flops=6 * rows * width * count * span,
            bytes_accessed=2 * width * (5 * rows + 3 * count * span),
            transcendentals=0,
        ),
        name="input_gradient",
    )(words, *[part for page in parts for part in page], *weights, first_in)


def local(body, name, words, arrays, shapes, costly=False):
    def kernel(words_ref, *refs):
        body(words_ref, refs[: len(arrays)], refs[len(arrays) :])

    vmem = pl.BlockSpec(memory_space=pltpu.VMEM)
    shapes = [jax.ShapeDtypeStruct(shape, kind) for shape, kind in shapes]
    moved = sum(item.size * item.dtype.itemsize for item in list(arrays) + shapes)
    cost = pl.CostEstimate(flops=0, bytes_accessed=moved, transcendentals=0)
    return pl.pallas_call(
        kernel,
        in_specs=[pl.BlockSpec(memory_space=pltpu.SMEM)] + [vmem] * len(arrays),
        out_specs=[vmem] * len(shapes),
        out_shape=shapes,
        compiler_params=pltpu.CompilerParams(vmem_limit_bytes=VMEM_LIMIT),
        cost_estimate=cost if costly else NO_COST,
        name=name,
    )(words, *arrays)


def shard(index, rows, base=0):
    return pl.ds(pl.multiple_of(base + index * rows, 16), rows)


def total_of(refs, rows=slice(None)):
    total = refs[0][rows].astype(F32)
    for ref in refs[1:]:
        total = total + ref[rows].astype(F32)
    return total


def tree_sum(terms):
    while len(terms) > 1:
        terms = [terms[i] + terms[i + 1] for i in range(0, len(terms), 2)]
    return terms[0]


def bit_of(words, level):
    return lax.shift_right_logical(words[1], level) & 1


def pair_sum(words, mine, other):
    def body(words, ins, outs):
        outs[0][...] = total_of(ins).astype(BF16)

    return local(body, "pair_sum", words, [mine, other], [(mine.shape, BF16)])[0]


def halve(words, level, mine, other):
    *lead, rows, width = mine.shape
    half = rows // 2

    def body(words, ins, outs):
        bit = bit_of(words, level)
        for out, side in zip(outs, (bit, 1 - bit)):
            at = shard(side, half)
            out[...] = total_of(ins, (slice(None), at) if lead else at).astype(BF16)

    return local(body, "halve", words, [mine, other], [((*lead, half, width), BF16)] * 2)


def join_halves(words, level, mine, other):
    rows, width = mine.shape

    def body(words, ins, outs):
        bit = bit_of(words, level)
        outs[0][shard(bit, rows)] = ins[0][...]
        outs[0][shard(1 - bit, rows)] = ins[1][...]

    return local(body, "join_halves", words, [mine, other], [((2 * rows, width), BF16)])[0]


def across(block, level):
    return swapped(block, 1 << level, "depth")


class Plan:
    def __init__(self, rows, rows_a, more, span, width):
        self.count = lax.axis_size("blk")
        self.levels = lax.axis_size("depth").bit_length() - 1
        self.rows = rows
        self.rows_a = rows_a
        self.more = more
        self.span = span
        self.width = width
        self.a_ff = rows_a // self.count
        self.a_more = more // self.count
        self.a = self.a_ff + self.a_more
        self.b = (rows - rows_a) // self.count
        self.share = self.a + self.b
        assert width % self.a_ff == 0 and width % self.b == 0 and rows_a % self.b == 0

    def shapes(self, *sizes):
        return [((rows, self.width), BF16) for rows in sizes]

    def scatter_one(self, words, halves):
        count, width = self.count, self.width
        a_ff, half = self.a_ff, self.b // 2

        def kernel(words_ref, *refs):
            parts = refs[6 : 6 + count]
            keep_ref, send_ref = refs[6 + count :]
            for i in range(count):

                @pl.when(pl.program_id(0) == i)
                def _(i=i):
                    parts[i][:a_ff] = total_of(refs[:2]).astype(BF16)
                    parts[i][a_ff:] = total_of(refs[2:4]).astype(BF16)

            bit = bit_of(words_ref, 0)
            keep_ref[0] = total_of(refs[4:6], shard(bit, half)).astype(BF16)
            send_ref[0] = total_of(refs[4:6], shard(1 - bit, half)).astype(BF16)

        def there(rows):
            return pl.BlockSpec((rows, width), lambda i, words: (words[0] ^ i, 0))

        part_b = pl.BlockSpec((self.b, width), lambda i, words: (self.rows_a // self.b + i, 0))
        half_b = pl.BlockSpec((1, half, width), lambda i, words: (i, 0, 0))
        shapes = [jax.ShapeDtypeStruct((self.a, width), BF16)] * count
        shapes += [jax.ShapeDtypeStruct((count, half, width), BF16)] * 2
        *parts_a, keep, send = pl.pallas_call(
            kernel,
            grid_spec=pltpu.PrefetchScalarGridSpec(
                num_scalar_prefetch=1,
                grid=(count,),
                in_specs=[there(a_ff)] * 2 + [there(self.a_more)] * 2 + [part_b] * 2,
                out_specs=[fixed(item) for item in shapes[:count]] + [half_b] * 2,
            ),
            out_shape=shapes,
            compiler_params=pltpu.CompilerParams(vmem_limit_bytes=VMEM_LIMIT),
            cost_estimate=NO_COST,
            name="scatter_one",
        )(words, *halves, *halves[:2])
        return [from_blk(part, i) for i, part in enumerate(parts_a)], keep, across(send, 0)

    def scatter_two(self, words, parts_a, keep_b, other_b):
        count = self.count
        half_a = self.a // 2
        last = self.levels == 1
        half_b = keep_b.shape[1] // 2

        def body(words, ins, outs):
            bit = bit_of(words, 0)
            outs[0][...] = total_of(ins[:count], shard(bit, half_a)).astype(BF16)
            outs[1][...] = total_of(ins[:count], shard(1 - bit, half_a)).astype(BF16)
            bit = bit_of(words, 1)
            for out, side in ((outs[2], bit), (outs[3], 1 - bit)):
                rows = (slice(None), shard(side, half_b))
                out[...] = total_of(ins[count:], rows).astype(BF16)

        assert not last
        shapes = self.shapes(half_a, half_a) + [((count, half_b, self.width), BF16)] * 2
        keep_a, send_a, keep_b, send_b = local(
            body, "scatter_two", words, [*parts_a, keep_b, other_b], shapes
        )
        return keep_a, across(send_a, 0), keep_b, across(send_b, 1)

    def scatter_three(self, words, keep_a, other_a, keep_b, other_b):
        count = self.count
        b_rows = keep_b.shape[1]

        def body(words, ins, outs):
            outs[0][...] = total_of(ins[:2]).astype(BF16)
            for i in range(count):
                outs[1 + i][...] = total_of(ins[2:], words[0] ^ i).astype(BF16)

        shapes = self.shapes(keep_a.shape[0], *[b_rows] * count)
        arrays = [keep_a, other_a, keep_b, other_b]
        part_a, *parts_b = local(body, "scatter_three", words, arrays, shapes)
        return part_a, [from_blk(item, i) for i, item in enumerate(parts_b)]

    def sum_b(self, words, parts_b):
        def body(words, ins, outs):
            outs[0][...] = total_of(ins).astype(BF16)

        return local(body, "sum_b", words, parts_b, self.shapes(parts_b[0].shape[0]))[0]

    def merge(self, words, halves_a, halves_b):
        a, b = self.a // 2, self.b // 2

        def body(words, ins, outs):
            bit = bit_of(words, 0)

            def write(ref, start, rows, to):
                if rows > 0:
                    outs[0][to : to + rows] = ref[start : start + rows]

            for side in range(2):

                @pl.when(bit == side)
                def _(side=side):
                    for at, ref in ((side, ins[0]), (1 - side, ins[1])):
                        cut = max(0, min(a, self.a_ff - at * a))
                        write(ref, 0, cut, at * a)
                        write(ref, cut, a - cut, max(0, at * a - self.a_ff) + self.a_ff + self.b)
                    for at, ref in ((side, ins[2]), (1 - side, ins[3])):
                        write(ref, 0, b, self.a_ff + at * b)

        arrays = [*halves_a, *halves_b]
        return local(body, "merge", words, arrays, self.shapes(self.share))[0]


def gather_blk(part, cut, late=None):
    count = lax.axis_size("blk")
    if count != 4:
        return [(i, 0, from_blk(part, i)) for i in range(count)]
    one, two = swapped(part, 1), swapped(part, 2)
    if late is not None:
        one, two = after(late, (one, two))
    first, second = swapped(one[:cut], 2), swapped(two[cut:], 1)
    return [(0, 0, part), (1, 0, one), (2, 0, two), (3, 0, first), (3, cut, second)]


def with_core(pieces):
    return [(distance, base, from_core(item)) for distance, base, item in pieces]


SLOTS = 4


def widen_own(words, plan, pieces, hidden):
    width = plan.width
    chunks = hidden // width
    pairs = chunks // 2
    arrays = [item for _, _, item in pieces]
    segments = []
    extras = []
    for at, (distance, base, item) in enumerate(pieces):
        stop = base + item.shape[0]
        for start, rows, first in ((0, plan.a_ff, 0), (plan.a_ff, plan.b, plan.rows_a)):
            if base <= start and start + rows <= stop:
                segments.append((at, start - base, rows, distance, first))
        if stop == plan.share:
            extras.append((at, distance))
    assert len(segments) == 2 * plan.count and len(extras) == plan.count

    def kernel(words_ref, *refs):
        ins = refs[: len(arrays)]
        joined_ref, expand_ref, reduce_ref, held, sems = refs[len(arrays) :]
        copies = []
        for index, (at, top, rows, distance, first) in enumerate(segments):
            slot = index % SLOTS
            if index >= SLOTS:
                copies[index - SLOTS].wait()
            part = ins[at][top : top + rows]
            held[slot, :rows] = part.astype(F32)
            place = pl.multiple_of(first + (words_ref[0] ^ distance) * rows, 64)
            joined_ref[pl.ds(place, rows)] = part
            matrix = lax.div(place, width)
            row = place - matrix * width
            chunk = (lax.div(matrix, 2) + words_ref[2] * pairs) % chunks
            column = pl.multiple_of(chunk * width, width)
            source = held.at[slot, :rows]
            to_expand = pltpu.make_async_copy(
                source,
                expand_ref.at[pl.ds(pl.multiple_of(row, 64), rows), pl.ds(column, width)],
                sems.at[slot],
            )
            to_reduce = pltpu.make_async_copy(
                source,
                reduce_ref.at[pl.ds(pl.multiple_of(column + row, 64), rows)],
                sems.at[slot],
            )
            is_expand = lax.rem(matrix, 2) == 0
            pl.when(is_expand)(to_expand.start)
            pl.when(jnp.logical_not(is_expand))(to_reduce.start)
            copies.append(to_reduce)
        for at, distance in extras:
            rows = shard(words_ref[0] ^ distance, plan.a_more, plan.rows)
            joined_ref[rows] = ins[at][ins[at].shape[0] - plan.a_more :]
        for copy in copies[-SLOTS:]:
            copy.wait()

    vmem = pl.BlockSpec(memory_space=pltpu.VMEM)
    anywhere = pl.BlockSpec(memory_space=pl.ANY)
    return pl.pallas_call(
        kernel,
        in_specs=[pl.BlockSpec(memory_space=pltpu.SMEM)] + [vmem] * len(arrays),
        out_specs=[vmem, anywhere, anywhere],
        out_shape=[
            jax.ShapeDtypeStruct((plan.rows + plan.more, width), BF16),
            jax.ShapeDtypeStruct((width, hidden), F32),
            jax.ShapeDtypeStruct((hidden, width), F32),
        ],
        scratch_shapes=[
            pltpu.VMEM((SLOTS, max(plan.a_ff, plan.b), width), F32),
            pltpu.SemaphoreType.DMA((SLOTS,)),
        ],
        compiler_params=pltpu.CompilerParams(vmem_limit_bytes=VMEM_LIMIT),
        cost_estimate=pl.CostEstimate(
            flops=0, bytes_accessed=6 * hidden * width, transcendentals=0
        ),
        name="widen_own",
    )(words, *arrays)


def widen_other(words, joined, expand, reduce):
    width, hidden = expand.shape
    chunks = hidden // width
    pairs = chunks // 2

    def kernel(words_ref, half_ref, before_ref, before_too_ref, expand_ref, reduce_ref):
        expand_ref[...] = half_ref[:width].astype(F32)
        reduce_ref[...] = half_ref[width:].astype(F32)

    def place(s, words):
        return (s + (words[2] + 1) * pairs) % chunks

    anywhere = pl.BlockSpec(memory_space=pl.ANY)
    return pl.pallas_call(
        kernel,
        grid_spec=pltpu.PrefetchScalarGridSpec(
            num_scalar_prefetch=1,
            grid=(pairs,),
            in_specs=[
                pl.BlockSpec((2 * width, width), lambda s, words: (s, 0)),
                anywhere,
                anywhere,
            ],
            out_specs=[
                pl.BlockSpec((width, width), lambda s, words: (0, place(s, words))),
                pl.BlockSpec((width, width), lambda s, words: (place(s, words), 0)),
            ],
        ),
        out_shape=[
            jax.ShapeDtypeStruct((width, hidden), F32),
            jax.ShapeDtypeStruct((hidden, width), F32),
        ],
        input_output_aliases={2: 0, 3: 1},
        compiler_params=pltpu.CompilerParams(vmem_limit_bytes=VMEM_LIMIT),
        cost_estimate=pl.CostEstimate(
            flops=0, bytes_accessed=6 * hidden * width, transcendentals=0
        ),
        name="widen_other",
    )(words, joined, expand, reduce)


def finished(words, plan, heads, joined, side, before=()):
    count = plan.count
    span = plan.span
    width = plan.width
    half_rows = width // 2
    arrays = [item for _, _, item in heads]

    def kernel(words_ref, *refs):
        heads_refs, refs = refs[: len(heads)], refs[len(heads) :]
        extra_ref, refs = refs[0], refs[1 + len(before) :]
        outs, refs = refs[:5], refs[5:]
        gathered, wide, project, sems = refs
        rank = words_ref[0]
        half = words_ref[2] ^ side
        for ref, (distance, base, _) in zip(heads_refs, heads):
            rows = ref.shape[0]
            place = pl.multiple_of((rank ^ distance) * span, HEAD_DIM)
            for part in range(2):
                low, high = max(base, part * span), min(base + rows, (part + 1) * span)
                if low < high:
                    gathered[part, pl.ds(place + (low - part * span), high - low)] = ref[
                        low - base : high - base
                    ]
        for part in range(2):
            wide[part] = gathered[part, :width].astype(F32).T
        project[...] = extra_ref[:half_rows].astype(F32)

        @pl.when(half == 1)
        def _():
            wide[1] = entry_order(wide[1])

        def copy(source, target, at):
            return pltpu.make_async_copy(source, target, sems.at[at])

        for part in range(2):
            pl.when(half == 0)(copy(wide.at[part], outs[part], part).start)
            pl.when(half == 1)(copy(wide.at[part], outs[2 + part], part).start)
        rows = pl.ds(pl.multiple_of(half * half_rows, half_rows), half_rows)
        last = copy(project, outs[4].at[rows], 2)
        last.start()
        for part in range(2):
            copy(wide.at[part], outs[part], part).wait()
        last.wait()

    def whole(item):
        return pl.BlockSpec(item.shape, lambda s: (0, 0))

    more = pl.BlockSpec((plan.more, width), lambda s: (plan.rows // plan.more, 0))
    anywhere = pl.BlockSpec(memory_space=pl.ANY)
    first = 2 + len(heads)
    shapes = [jax.ShapeDtypeStruct((width, width), F32)] * 5
    return pl.pallas_call(
        kernel,
        grid=(1,),
        in_specs=[pl.BlockSpec(memory_space=pltpu.SMEM)]
        + [whole(item) for item in arrays]
        + [more]
        + [anywhere] * len(before),
        out_specs=[anywhere] * 5,
        out_shape=shapes,
        scratch_shapes=[
            pltpu.VMEM((2, count * span, width), BF16),
            pltpu.VMEM((2, width, width), F32),
            pltpu.VMEM((half_rows, width), F32),
            pltpu.SemaphoreType.DMA((3,)),
        ],
        input_output_aliases={first + at: at for at in range(len(before))},
        compiler_params=pltpu.CompilerParams(vmem_limit_bytes=VMEM_LIMIT),
        cost_estimate=pl.CostEstimate(
            flops=0, bytes_accessed=16 * width * width, transcendentals=0
        ),
        name="finish",
    )(words, *arrays, joined, *before)


def per_device(
    tokens,
    boxes,
    w_query,
    w_key,
    w_value,
    w_output,
    box_weight,
    first_gain,
    first_shift,
    w_expand,
    w_reduce,
    second_gain,
    second_shift,
    cotangent,
):
    pages, block, width = tokens.shape
    count = lax.axis_size("blk")
    depth = lax.axis_size("depth")
    words = jnp.stack(
        [lax.axis_index("blk"), lax.axis_index("depth"), lax.axis_index("core")]
    ).astype(jnp.int32)
    hidden = w_expand.shape[1]
    span = -(-HEADS // count) * HEAD_DIM
    unit = 16 * count * depth
    more = -(-(width // 2 + 16) // unit) * unit

    own_places = jnp.stack([boxes[0] + boxes[2], boxes[1] + boxes[3]], axis=1)
    own_places = jnp.stack([lax.shift_right_logical(own_places, 6), own_places & 63], axis=2)
    own_places = own_places.reshape(4 * pages, block).astype(BF16)
    own_places = jnp.pad(own_places, ((0, 16 - 4 * pages), (0, width - block)))
    message = jnp.concatenate([tokens[0], own_places])
    messages = [from_blk(message, i) for i in range(count)]
    w_own, box_own, rot_cos, rot_sin = prepare(
        words, w_query, w_key, w_value, box_weight, span, count * block
    )
    messages, rot_cos = lax.optimization_barrier((messages, rot_cos))
    own = after(messages, tokens[1])
    pieces = [messages, [from_blk(own, i) for i in range(count)]]

    saved = []
    att_parts = []
    for page in range(pages):
        results = attention_forward(
            words, page, messages, pieces[page], w_own, box_own, rot_cos, rot_sin
        )
        saved.append(results[:6])
        att_parts += [from_blk(results[6 + i], i) for i in range(count)]

    vectors = jnp.stack([first_gain, first_shift, second_gain, second_shift])
    results = middle(
        words,
        att_parts,
        tokens.reshape(pages * block, width),
        cotangent.reshape(pages * block, width),
        w_output,
        vectors,
        w_expand,
        w_reduce,
        pages,
        more,
    )
    layer_out, first_in, theirs, mine, more_theirs, more_mine = results[:6]
    grads = [from_blk(results[6 + i], i) for i in range(count)]
    plan = Plan(hidden, hidden - hidden // 2 // unit * unit, more, span, width)
    parts_a, keep_b, other_b = plan.scatter_one(
        after(grads, words), [mine, from_core(theirs), more_mine, from_core(more_theirs)]
    )

    def backward(page, words, before=None):
        return attention_backward(
            words,
            page,
            grads,
            pieces[page],
            saved[page],
            box_own,
            rot_cos,
            rot_sin,
            before,
        )

    *pre_one, before = backward(0, after(parts_a[0], words))
    part_a, other_a, keep_b, other_b = plan.scatter_two(
        after(before, words), parts_a, keep_b, other_b
    )
    done = part_a
    for level in range(2, plan.levels):
        keep_b, send_b = halve(after(done, words), level, keep_b, other_b)
        other_b = across(send_b, level)
        done = keep_b
    pre_one = [from_blk(item, i) for i, item in enumerate(after(part_a, pre_one))]
    *pre_two, heads_mine, heads_theirs = backward(1, after(done, words), before)

    part_a, parts_b = plan.scatter_three(
        after((heads_mine, pre_one), words), part_a, other_a, keep_b, other_b
    )
    heads, other = halve(
        after(part_a, words), 0, heads_mine, from_core(after(part_a, heads_theirs))
    )
    done = heads
    part_b = plan.sum_b(after(done, words), parts_b)
    done = part_b
    pre_two = [from_blk(item, i) for i, item in enumerate(after(part_b, pre_two))]
    for level in range(plan.levels - 1, 0, -1):
        part_b = join_halves(after(done, words), level, part_b, across(part_b, level))
        done = part_b
    halves_b = [part_b, across(part_b, 0)]
    for level in range(1, plan.levels):
        part_a = pair_sum(after(done, words), part_a, across(part_a, level))
        done = part_a
    other = across(after((part_a, halves_b), other), 0)
    share = plan.merge(
        after((done, pre_two), words), [part_a, across(part_a, 0)], halves_b
    )
    heads = pair_sum(after(share, words), heads, other)
    input_grad = input_gradient(
        after(heads, words), [pre_one, pre_two], (w_query, w_key, w_value), first_in
    )
    for level in range(1, plan.levels):
        heads = pair_sum(after(input_grad, words), heads, across(heads, level))
    pieces = gather_blk(share, plan.a_ff, heads)
    heads = join_halves(after(pieces[1][2], words), 0, heads, across(heads, 0))
    heads = after([item for _, _, item in pieces], heads)
    joined, *wide = widen_own(after(heads, words), plan, pieces, hidden)
    pieces_heads = gather_blk(heads, span, joined)
    joined_other = from_core(after(pieces_heads[1][2], joined))
    at = plan.rows + width // 2
    sums = jnp.where(words[2] == 0, joined[at : at + 4], joined_other[at : at + 4])
    sums = [sums[i].astype(F32) for i in range(4)]
    grad_expand, grad_reduce = widen_other(after(sums, words), joined_other, *wide)
    grads = finished(after(grad_expand, words), plan, pieces_heads, joined, 0)
    grad_query, grad_key, grad_value, grad_box, grad_project = finished(
        after(grads, words), plan, with_core(pieces_heads), joined_other, 1, grads
    )
    return (
        layer_out.reshape(tokens.shape),
        input_grad.reshape(tokens.shape),
        grad_query,
        grad_key,
        grad_value,
        grad_project,
        grad_box,
        sums[0],
        sums[1],
        grad_expand,
        grad_reduce,
        sums[2],
        sums[3],
    )


def solution(mesh):
    blocks, rest = mesh.devices.shape
    parts = jax.sharding.Mesh(
        mesh.devices.reshape(blocks, rest // 2, 2), ("blk", "depth", "core")
    )
    split = P(("depth", "core"), "blk", None)
    return jax.shard_map(
        per_device,
        mesh=parts,
        in_specs=(split, P(None, ("depth", "core"), "blk")) + (P(),) * 11 + (split,),
        out_specs=(split, split) + (P(),) * 11,
        check_vma=False,
    )
```

```python
import functools

import jax
import jax.numpy as jnp
import numpy as np
from jax import lax
from jax.experimental import pallas as pl
from jax.experimental.pallas import tpu as pltpu
from jax.sharding import PartitionSpec as P

HEADS = 12
HEAD_DIM = 64
HALF = 32
FREQS = 192
CODES = 4 * FREQS
VMEM_LIMIT = 60 * 1024 * 1024
NO_COST = pl.CostEstimate(flops=0, bytes_accessed=0, transcendentals=0)
F32 = jnp.float32
BF16 = jnp.bfloat16


def dot(left, right):
    return lax.dot_general(left, right, (((1,), (0,)), ((), ())), preferred_element_type=F32)


def dot_nt(left, right):
    return lax.dot_general(left, right, (((1,), (1,)), ((), ())), preferred_element_type=F32)


def dot_tn(left, right):
    return lax.dot_general(left, right, (((0,), (0,)), ((), ())), preferred_element_type=F32)


def swapped(block, distance, axis="blk"):
    count = lax.axis_size(axis)
    return lax.ppermute(block, axis, [(i, i ^ distance) for i in range(count)])


def from_blk(block, distance):
    return swapped(block, distance) if distance else block


def from_core(block):
    return swapped(block, 1, "core")


def after(done, value):
    return lax.optimization_barrier((value, done))[0]


def turned(upper, lower, cosines, sines):
    return upper * cosines - lower * sines, lower * cosines + upper * sines


def entry_order(rows):
    return jnp.concatenate(
        [
            rows[:FREQS],
            rows[2 * FREQS : 3 * FREQS],
            rows[FREQS : 2 * FREQS],
            rows[3 * FREQS :],
        ],
        axis=0,
    )


def angle_tables():
    rates = np.float32(10000.0) ** (-np.arange(FREQS, dtype=np.float32) / np.float32(FREQS))
    tables = []
    for places in (32.0 * np.arange(32), 0.5 * np.arange(64)):
        angles = rates.astype(np.float64)[:, None] * places[None, :]
        left = np.concatenate([np.sin(angles), np.cos(angles)])
        parts = []
        for _ in range(3):
            parts.append(left.astype(jnp.bfloat16))
            left = left - parts[-1].astype(np.float64)
        tables.append(np.concatenate(parts, axis=1))
    return tables


def rotary_tables(length):
    rates = np.float32(10000.0) ** (-np.arange(HALF, dtype=np.float32) / np.float32(HALF))
    angles = np.arange(length, dtype=np.float32)[None, :] * rates[:, None]
    angles = angles.astype(np.float64)
    return np.cos(angles).astype(np.float32), np.sin(angles).astype(np.float32)


def prepare_kernel(
    words_ref,
    query_ref,
    key_ref,
    value_ref,
    box_ref,
    cos_ref,
    sin_ref,
    own_ref,
    own_box_ref,
    own_cos_ref,
    own_sin_ref,
):
    rank = words_ref[0]
    span = own_box_ref.shape[0]
    width = query_ref.shape[1]
    count = lax.axis_size("blk")
    block = cos_ref.shape[1] // count
    row = lax.broadcasted_iota(jnp.int32, (span, width), 0) + rank * span
    column = lax.broadcasted_iota(jnp.int32, (span, width), 1)
    pick = jnp.where(row == column, 1.0, 0.0).astype(BF16)
    for kind, ref in enumerate((query_ref, key_ref, value_ref)):
        own_ref[kind * span : (kind + 1) * span] = dot_nt(pick, ref[...]).astype(BF16)
    own_box_ref[...] = dot_nt(pick, entry_order(box_ref[...])).astype(BF16)
    for i in range(count):
        from_cols = pl.ds(pl.multiple_of((rank ^ i) * block, block), block)
        own_cos_ref[:, i * block : (i + 1) * block] = cos_ref[:, from_cols]
        own_sin_ref[:, i * block : (i + 1) * block] = sin_ref[:, from_cols]


def prepare(words, w_query, w_key, w_value, box_weight, span, length):
    width = w_query.shape[0]
    vmem = pl.BlockSpec(memory_space=pltpu.VMEM)
    return pl.pallas_call(
        prepare_kernel,
        in_specs=[pl.BlockSpec(memory_space=pltpu.SMEM)] + [vmem] * 6,
        out_specs=[vmem] * 4,
        out_shape=[
            jax.ShapeDtypeStruct((3 * span, width), BF16),
            jax.ShapeDtypeStruct((span, CODES), BF16),
            jax.ShapeDtypeStruct((HALF, length), F32),
            jax.ShapeDtypeStruct((HALF, length), F32),
        ],
        compiler_params=pltpu.CompilerParams(vmem_limit_bytes=VMEM_LIMIT),
        cost_estimate=pl.CostEstimate(
            flops=8 * span * width * width, bytes_accessed=10 * width * width, transcendentals=0
        ),
        name="prepare",
    )(words, w_query, w_key, w_value, box_weight, *map(jnp.asarray, rotary_tables(length)))


def fold(value, combine):
    while value.shape[0] > 8:
        half = value.shape[0] // 2
        value = combine(value[:half], value[half:])
    return value


def write_codes(page, place_refs, high_ref, low_ref, sin_ref, cos_ref, codes_ref):
    block = sin_ref.shape[1] // len(place_refs)

    def looked_up(table_ref, index):
        spots = table_ref.shape[1] // 3
        rows = lax.broadcasted_iota(jnp.int32, (spots, block), 0).astype(F32)
        once = jnp.where(rows == index, 1.0, 0.0)
        found = dot(table_ref[...], jnp.concatenate([once] * 3, axis=0).astype(BF16))
        return found[:FREQS], found[FREQS:]

    for i, place_ref in enumerate(place_refs):
        columns = slice(i * block, (i + 1) * block)
        places = place_ref[:, :block].astype(F32)
        for axis in range(2):
            at = 4 * page + 2 * axis
            high_sin, high_cos = looked_up(high_ref, places[at : at + 1])
            low_sin, low_cos = looked_up(low_ref, places[at + 1 : at + 2])
            sines = high_sin * low_cos + high_cos * low_sin
            cosines = high_cos * low_cos - high_sin * low_sin
            rows = slice(axis * FREQS, (axis + 1) * FREQS)
            later = slice((2 + axis) * FREQS, (3 + axis) * FREQS)
            sin_ref[rows, columns] = sines
            cos_ref[rows, columns] = cosines
            codes_ref[rows, columns] = sines.astype(BF16)
            codes_ref[later, columns] = cosines.astype(BF16)


def forward_kernel(page, count, words_ref, *refs):
    place_refs, refs = refs[:count], refs[count:]
    piece_refs, refs = refs[:count], refs[count:]
    high_ref, low_ref, w_ref, box_ref, rot_cos_ref, rot_sin_ref = refs[:6]
    probs_ref, att_ref, heads_ref, sin_ref, cos_ref, codes_ref = refs[6:12]
    low_refs = refs[12 : 12 + count]
    tok_ref, pre_ref, kc_ref, qr_ref = refs[12 + count :]
    rows = tok_ref.shape[0]
    block = rows // count
    head = pl.program_id(0)
    span = pl.num_programs(0) * HEAD_DIM

    @pl.when(head == 0)
    def _():
        for i in range(count):
            tok_ref[i * block : (i + 1) * block] = piece_refs[i][...]
        pre_ref[...] = dot_nt(w_ref[...], tok_ref[...])
        write_codes(page, place_refs, high_ref, low_ref, sin_ref, cos_ref, codes_ref)
        kc_ref[:, :CODES] = codes_ref[...].astype(F32).T.astype(BF16)

    def pre(kind):
        at = kind * span + head * HEAD_DIM
        return pre_ref[pl.ds(pl.multiple_of(at, HEAD_DIM), HEAD_DIM)]

    rot_cos = rot_cos_ref[...]
    rot_sin = rot_sin_ref[...]
    query_pre = pre(0).astype(BF16)
    wide = query_pre.astype(F32)
    query = jnp.concatenate(turned(wide[:HALF], wide[HALF:], rot_cos, rot_sin), axis=0)
    key_pre = pre(1)
    key = jnp.concatenate(turned(key_pre[:HALF], key_pre[HALF:], rot_cos, rot_sin), axis=0)
    value = pre(2).astype(BF16)
    heads_ref[0, :HEAD_DIM] = query_pre
    heads_ref[0, HEAD_DIM : 2 * HEAD_DIM] = query.astype(BF16)
    heads_ref[0, 2 * HEAD_DIM : 3 * HEAD_DIM] = key.astype(BF16)
    heads_ref[0, 3 * HEAD_DIM :] = value
    kc_ref[:, CODES:] = key.T.astype(BF16)
    qr_ref[CODES:] = (query * 0.125).astype(BF16)
    step = min(256, block)

    def logits_at(at):
        part = slice(at, at + step)
        projected = dot_tn(box_ref[...], query_pre[:, part])
        sines = sin_ref[:, part]
        cosines = cos_ref[:, part]
        upper = projected[: 2 * FREQS]
        lower = projected[2 * FREQS :]
        qr_ref[: 2 * FREQS, part] = ((upper * cosines + lower * sines) * 0.125).astype(BF16)
        qr_ref[2 * FREQS : CODES, part] = ((lower * cosines - upper * sines) * 0.125).astype(BF16)
        return dot(kc_ref[...], qr_ref[:, part])

    following = logits_at(0)
    for at in range(0, rows, step):
        logits = following
        if at + step < rows:
            following = logits_at(at + step)
        peak = jnp.max(fold(logits, jnp.maximum), axis=0, keepdims=True)
        weight = jnp.exp(logits - peak)
        total = jnp.sum(fold(weight, jnp.add), axis=0, keepdims=True)
        probs = (weight * (1.0 / total)).astype(BF16)
        probs_ref[0, :, at : at + step] = probs
        attended = dot(value, probs)
        att_ref[0, :, at : at + step] = attended
        inner = at % block
        low_refs[at // block][:, inner : inner + step] = attended.astype(BF16)


def fixed(array):
    return pl.BlockSpec(array.shape, lambda *at: (0,) * len(array.shape))


def attention_forward(words, page, messages, pieces, w_own, box_own, rot_cos, rot_sin):
    count = len(messages)
    block, width = messages[0].shape[0] - 16, messages[0].shape[1]
    rows = count * block
    span = box_own.shape[0]
    heads = span // HEAD_DIM
    tables = [jnp.asarray(item) for item in angle_tables()]
    specs = [pl.BlockSpec((block, width), lambda h, words: (0, 0))] * count
    places = pl.BlockSpec((16, width), lambda h, words: (block // 16, 0))
    out_shape = [
        jax.ShapeDtypeStruct((heads, rows, rows), BF16),
        jax.ShapeDtypeStruct((heads, HEAD_DIM, rows), F32),
        jax.ShapeDtypeStruct((heads, 4 * HEAD_DIM, rows), BF16),
        jax.ShapeDtypeStruct((2 * FREQS, rows), F32),
        jax.ShapeDtypeStruct((2 * FREQS, rows), F32),
        jax.ShapeDtypeStruct((CODES, rows), BF16),
    ] + [jax.ShapeDtypeStruct((span, block), BF16)] * count
    return pl.pallas_call(
        functools.partial(forward_kernel, page, count),
        grid_spec=pltpu.PrefetchScalarGridSpec(
            num_scalar_prefetch=1,
            grid=(heads,),
            in_specs=[places] * count
            + specs
            + [fixed(item) for item in (*tables, w_own)]
            + [
                pl.BlockSpec((HEAD_DIM, CODES), lambda h, words: (h, 0)),
                fixed(rot_cos),
                fixed(rot_sin),
            ],
            out_specs=[
                pl.BlockSpec((1, rows, rows), lambda h, words: (h, 0, 0)),
                pl.BlockSpec((1, HEAD_DIM, rows), lambda h, words: (h, 0, 0)),
                pl.BlockSpec((1, 4 * HEAD_DIM, rows), lambda h, words: (h, 0, 0)),
            ]
            + [fixed(item) for item in out_shape[3:6]]
            + [pl.BlockSpec((HEAD_DIM, block), lambda h, words: (h, 0))] * count,
            scratch_shapes=[
                pltpu.VMEM((rows, width), BF16),
                pltpu.VMEM((3 * span, rows), F32),
                pltpu.VMEM((rows, CODES + HEAD_DIM), BF16),
                pltpu.VMEM((CODES + HEAD_DIM, rows), BF16),
            ],
        ),
        out_shape=out_shape,
        compiler_params=pltpu.CompilerParams(vmem_limit_bytes=VMEM_LIMIT),
        cost_estimate=pl.CostEstimate(
            flops=2 * heads * rows * (rows * 1100 + 200 * width + 64 * CODES),
            bytes_accessed=2 * heads * rows * rows + 12 * rows * width,
            transcendentals=heads * rows * rows,
        ),
        name="attention_forward",
    )(words, *messages, *pieces, *tables, w_own, box_own, rot_cos, rot_sin)


def backward_kernel(count, last, words_ref, *refs):
    grad_refs, refs = refs[:count], refs[count:]
    piece_refs, refs = refs[:count], refs[count:]
    probs_ref, att_ref, heads_ref, box_ref, codes_ref, sin_ref, cos_ref = refs[:7]
    rot_cos_ref, rot_sin_ref = refs[7:9]
    refs = refs[9:]
    if last:
        before_ref, refs = refs[0], refs[1:]
    pre_refs, refs = refs[:count], refs[count:]
    if last:
        mine_ref, theirs_ref, *refs = refs
    weight_grad_ref, kc_ref, logit_grad_ref, entry_grad_ref, turned_ref = refs
    block, width = piece_refs[0].shape
    rows = count * block
    head = pl.program_id(0)
    span = pl.num_programs(0) * HEAD_DIM

    @pl.when(head == 0)
    def _():
        kc_ref[:CODES] = codes_ref[...]

    kc_ref[CODES:] = heads_ref[0, 2 * HEAD_DIM : 3 * HEAD_DIM]
    packed = heads_ref[0].astype(F32).T.astype(BF16)
    query_pre = packed[:, :HEAD_DIM]
    query = packed[:, HEAD_DIM : 2 * HEAD_DIM]
    value = packed[:, 3 * HEAD_DIM :] * jnp.asarray(0.125, BF16)
    rot_cos = rot_cos_ref[...]
    rot_sin = rot_sin_ref[...]
    grad = jnp.concatenate([ref[...] for ref in grad_refs], axis=1)
    grad_tall = grad.astype(F32).T.astype(BF16)
    offsets = jnp.sum(grad.astype(F32) * att_ref[0], axis=0, keepdims=True) * 0.125
    step = min(256, block)
    place = pl.multiple_of(head * HEAD_DIM, HEAD_DIM)
    here = pl.ds(place, HEAD_DIM)

    def logits_back(at):
        part = slice(at, at + step)
        grad_probs = dot(value, grad[:, part])
        logit_grad_ref[:, part] = (
            probs_ref[0, :, part].astype(F32) * (grad_probs - offsets[:, part])
        ).astype(BF16)

    logits_back(0)
    for at in range(0, rows, step):
        if at + step < rows:
            logits_back(at + step)
        part = slice(at, at + step)
        back = dot(kc_ref[...], logit_grad_ref[:, part])
        sines = sin_ref[:, part]
        cosines = cos_ref[:, part]
        upper = back[: 2 * FREQS]
        lower = back[2 * FREQS : CODES]
        entry_grad_ref[: 2 * FREQS, part] = (upper * cosines - lower * sines).astype(BF16)
        entry_grad_ref[2 * FREQS :, part] = (lower * cosines + upper * sines).astype(BF16)
        first = back[CODES : CODES + HALF]
        second = back[CODES + HALF :]
        turned_ref[:HALF, part], turned_ref[HALF:, part] = turned(
            first, second, rot_cos[:, part], -rot_sin[:, part]
        )
    key_flat = dot(logit_grad_ref[...], query).T
    value_low = dot(probs_ref[0], grad_tall).T.astype(BF16)
    query_low = (turned_ref[...] + dot(box_ref[...], entry_grad_ref[...])).astype(BF16)
    key_low = jnp.concatenate(
        turned(key_flat[:HALF], key_flat[HALF:], rot_cos, -rot_sin), axis=0
    ).astype(BF16)
    for i in range(count):
        columns = slice(i * block, (i + 1) * block)
        pre_refs[i][here, :block] = query_low[:, columns]
        pre_refs[i][here, block : 2 * block] = key_low[:, columns]
        pre_refs[i][here, 2 * block :] = value_low[:, columns]
    weight_grad_ref[pl.ds(3 * span + place, HEAD_DIM)] = dot(entry_grad_ref[...], query_pre).T

    @pl.when(head == pl.num_programs(0) - 1)
    def _():
        for kind in range(3):
            columns = slice(kind * block, (kind + 1) * block)
            total = dot(pre_refs[0][:, columns], piece_refs[0][...])
            for i in range(1, count):
                total = total + dot(pre_refs[i][:, columns], piece_refs[i][...])
            weight_grad_ref[kind * span : (kind + 1) * span] = total
        if last:
            half = 2 * span
            core = words_ref[2]
            ours = pl.ds(pl.multiple_of(core * half, half), half)
            there = pl.ds(pl.multiple_of((1 - core) * half, half), half)
            mine_ref[...] = weight_grad_ref[ours] + before_ref[ours]
            theirs_ref[...] = (weight_grad_ref[there] + before_ref[there]).astype(BF16)


def attention_backward(
    words, page, grads, pieces, saved, box_own, rot_cos, rot_sin, before=None
):
    probs, att, heads_saved, sines, cosines, codes = saved
    count = len(pieces)
    rows, width = probs.shape[1], pieces[0].shape[1]
    block = rows // count
    span = box_own.shape[0]
    heads = span // HEAD_DIM
    last = before is not None
    extra = (before,) if last else ()
    full_shape = (4 * span, width)
    specs = [pl.BlockSpec((block, width), lambda h, words: (0, 0))] * count
    out_shape = [jax.ShapeDtypeStruct((span, 3 * block), BF16)] * count
    if last:
        out_shape += [
            jax.ShapeDtypeStruct((2 * span, width), F32),
            jax.ShapeDtypeStruct((2 * span, width), BF16),
        ]
    else:
        out_shape.append(jax.ShapeDtypeStruct(full_shape, F32))
    return pl.pallas_call(
        functools.partial(backward_kernel, count, last),
        grid_spec=pltpu.PrefetchScalarGridSpec(
            num_scalar_prefetch=1,
            grid=(heads,),
            in_specs=[pl.BlockSpec((HEAD_DIM, block), lambda h, words: (h, page))] * count
            + specs
            + [
                pl.BlockSpec((1, rows, rows), lambda h, words: (h, 0, 0)),
                pl.BlockSpec((1, HEAD_DIM, rows), lambda h, words: (h, 0, 0)),
                pl.BlockSpec((1, 4 * HEAD_DIM, rows), lambda h, words: (h, 0, 0)),
                pl.BlockSpec((HEAD_DIM, CODES), lambda h, words: (h, 0)),
            ]
            + [fixed(item) for item in (codes, sines, cosines, rot_cos, rot_sin, *extra)],
            out_specs=[fixed(item) for item in out_shape],
            scratch_shapes=([pltpu.VMEM(full_shape, F32)] if last else [])
            + [
                pltpu.VMEM((CODES + HEAD_DIM, rows), BF16),
                pltpu.VMEM((rows, rows), BF16),
                pltpu.VMEM((CODES, rows), BF16),
                pltpu.VMEM((HEAD_DIM, rows), F32),
            ],
        ),
        out_shape=out_shape,
        compiler_params=pltpu.CompilerParams(vmem_limit_bytes=VMEM_LIMIT),
        cost_estimate=pl.CostEstimate(
            flops=2 * heads * rows * (rows * 1400 + 200 * width + 128 * CODES),
            bytes_accessed=2 * heads * rows * rows + 12 * rows * width,
            transcendentals=0,
        ),
        name="attention_backward",
    )(
        words,
        *grads,
        *pieces,
        probs,
        att,
        heads_saved,
        box_own,
        codes,
        sines,
        cosines,
        rot_cos,
        rot_sin,
        *extra,
    )


def normed(value):
    centered = value - jnp.mean(value, axis=-1, keepdims=True)
    scale = lax.rsqrt(jnp.mean(centered * centered, axis=-1, keepdims=True) + 1e-05)
    return centered * scale, scale


def norm_back(grad, gain, unit, scale):
    scaled = grad * gain
    return scale * (
        scaled
        - jnp.mean(scaled, axis=-1, keepdims=True)
        - unit * jnp.mean(scaled * unit, axis=-1, keepdims=True)
    )


def column_sum(value):
    return jnp.sum(value, axis=0, keepdims=True)


def middle_kernel(pages, count, span, chunks, *refs):
    total = pages * count
    words_ref = refs[0]
    att_refs = refs[1 : 1 + total]
    (
        tok_ref,
        cot_ref,
        w_out_ref,
        vectors_ref,
        w_expand_ref,
        w_reduce_ref,
    ) = refs[1 + total : 7 + total]
    outs = refs[7 + total :]
    layer_ref, first_in_ref, theirs_ref, mine_ref, more_theirs_ref, more_mine_ref = outs[:6]
    grad_refs = outs[6 : 6 + count]
    (
        sums_ref,
        att_all,
        grad_all,
        unit_one,
        scale_one,
        first_wide,
        first_low,
        first_tall,
        active,
        slope,
        gathered,
        second_in,
        second_low,
    ) = outs[6 + count :]
    rank = words_ref[0]
    width = tok_ref.shape[1]
    block = tok_ref.shape[0] // pages
    step = pl.program_id(0)

    def rows_of(at):
        return pl.ds(pl.multiple_of((rank ^ at) * span, span), span)

    @pl.when(step == 0)
    def _():
        for page in range(pages):
            for at in range(count):
                att_all[rows_of(at), page * block : (page + 1) * block] = att_refs[
                    page * count + at
                ][...]
        branch = dot_tn(att_all[: w_out_ref.shape[0]], w_out_ref[...])
        unit, scale = normed(tok_ref[...].astype(F32) + branch)
        unit_one[...] = unit
        scale_one[...] = jnp.broadcast_to(scale, scale_one.shape)
        first_out = unit * vectors_ref[0:1] + vectors_ref[1:2]
        first_wide[...] = first_out
        first_low[...] = first_out.astype(BF16)
        first_tall[...] = first_out.T.astype(BF16)
        gathered[...] = jnp.zeros_like(gathered)
        sums_ref[...] = jnp.zeros_like(sums_ref)

    for chunk in range(chunks):

        @pl.when(step == chunk)
        def _(chunk=chunk):
            expanded = dot(first_low[...], w_expand_ref[...])
            gate = 0.5 + 0.5 * lax.erf(expanded * np.float32(np.sqrt(0.5)))
            bell = jnp.exp(expanded * expanded * -0.5) * np.float32(1.0 / np.sqrt(2.0 * np.pi))
            low = (expanded * gate).astype(BF16)
            active[chunk] = low
            slope[chunk] = gate + expanded * bell
            gathered[...] += dot(low, w_reduce_ref[...])

    @pl.when(step == chunks - 1)
    def _():
        unit, scale = normed(first_wide[...] + gathered[...])
        layer_ref[...] = (unit * vectors_ref[2:3] + vectors_ref[3:4]).astype(BF16)
        cot = cot_ref[...].astype(F32)
        sums_ref[2:3] = column_sum(cot * unit)
        sums_ref[3:4] = column_sum(cot)
        grad = norm_back(cot, vectors_ref[2:3], unit, scale)
        second_in[...] = grad
        second_low[...] = grad.astype(BF16)
        gathered[...] = grad

    for chunk in range(chunks):

        @pl.when(step == 2 * chunks - 1 - chunk)
        def _(chunk=chunk):
            grad_active = dot_nt(second_low[...], w_reduce_ref[...])
            grad_expanded = (grad_active * slope[chunk]).astype(BF16)
            grads_ref = mine_ref if chunk < chunks // 2 else theirs_ref
            grads_ref[:width] = dot(first_tall[...], grad_expanded).astype(BF16)
            grads_ref[width:] = dot_tn(active[chunk], second_low[...]).astype(BF16)
            gathered[...] += dot_nt(grad_expanded, w_expand_ref[...])

    @pl.when(step == 2 * chunks - 1)
    def _():
        unit = unit_one[...]
        grad_out = gathered[...]
        sums_ref[0:1] = column_sum(grad_out * unit)
        sums_ref[1:2] = column_sum(grad_out)
        grad = norm_back(grad_out, vectors_ref[0:1], unit, scale_one[:, :1])
        first_in_ref[...] = grad
        low = grad.astype(BF16)
        real = w_out_ref.shape[0]
        half = real // 2
        core = words_ref[2]
        for ref, side in ((more_mine_ref, core), (more_theirs_ref, 1 - core)):
            rows = pl.ds(pl.multiple_of(side * half, half), half)
            ref[:half] = dot(att_all[rows], low).astype(BF16)
            ref[half:] = jnp.zeros((ref.shape[0] - half, width), BF16)
            ref[half : half + 16] = sums_ref[...].astype(BF16)
        if grad_all.shape[0] > real:
            grad_all[real:] = jnp.zeros((grad_all.shape[0] - real, low.shape[0]), BF16)
        grad_all[:real] = dot_nt(w_out_ref[...], low).astype(BF16)
        for at in range(count):
            grad_refs[at][...] = grad_all[rows_of(at)]


def middle(words, att_parts, tok, cot, w_out, vectors, w_expand, w_reduce, pages, more):
    rows, width = tok.shape
    count = len(att_parts) // pages
    span, block = att_parts[0].shape
    hidden = w_expand.shape[1]
    chunks = hidden // width
    pairs = chunks // 2

    def whole(array):
        return pl.BlockSpec(array.shape, lambda s, words: (0,) * len(array.shape))

    def chunk_at(s, words):
        at = jnp.minimum(s, 2 * chunks - 1 - s)
        return (at + words[2] * pairs) % chunks

    def theirs_at(s, words):
        return jnp.clip(2 * chunks - 1 - s - pairs, 0, pairs - 1), 0

    def mine_at(s, words):
        return jnp.clip(2 * chunks - 1 - s, 0, pairs - 1), 0

    shapes = [
        jax.ShapeDtypeStruct((rows, width), BF16),
        jax.ShapeDtypeStruct((rows, width), F32),
        jax.ShapeDtypeStruct((hidden, width), BF16),
        jax.ShapeDtypeStruct((hidden, width), BF16),
        jax.ShapeDtypeStruct((more, width), BF16),
        jax.ShapeDtypeStruct((more, width), BF16),
    ] + [jax.ShapeDtypeStruct((span, pages * block), BF16)] * count
    specs = [whole(item) for item in shapes]
    specs[2] = pl.BlockSpec((2 * width, width), theirs_at)
    specs[3] = pl.BlockSpec((2 * width, width), mine_at)
    return pl.pallas_call(
        functools.partial(middle_kernel, pages, count, span, chunks),
        grid_spec=pltpu.PrefetchScalarGridSpec(
            num_scalar_prefetch=1,
            grid=(2 * chunks,),
            in_specs=[whole(item) for item in att_parts]
            + [
                whole(tok),
                whole(cot),
                whole(w_out),
                whole(vectors),
                pl.BlockSpec((width, width), lambda s, words: (0, chunk_at(s, words))),
                pl.BlockSpec((width, width), lambda s, words: (chunk_at(s, words), 0)),
            ],
            out_specs=specs,
            scratch_shapes=[
                pltpu.VMEM((16, width), F32),
                pltpu.VMEM((count * span, rows), BF16),
                pltpu.VMEM((count * span, rows), BF16),
                pltpu.VMEM((rows, width), F32),
                pltpu.VMEM((rows, 128), F32),
                pltpu.VMEM((rows, width), F32),
                pltpu.VMEM((rows, width), BF16),
                pltpu.VMEM((width, rows), BF16),
                pltpu.VMEM((chunks, rows, width), BF16),
                pltpu.VMEM((chunks, rows, width), F32),
                pltpu.VMEM((rows, width), F32),
                pltpu.VMEM((rows, width), F32),
                pltpu.VMEM((rows, width), BF16),
            ],
        ),
        out_shape=shapes,
        compiler_params=pltpu.CompilerParams(vmem_limit_bytes=VMEM_LIMIT),
        cost_estimate=pl.CostEstimate(
            flops=2 * rows * width * (6 * hidden + 3 * width),
            bytes_accessed=8 * width * hidden + 16 * rows * width,
            transcendentals=2 * rows * hidden,
        ),
        name="middle",
    )(words, *att_parts, tok, cot, w_out, vectors, w_expand, w_reduce)


def input_kernel(pages, count, span, *refs):
    words_ref = refs[0]
    part_refs = refs[1 : 1 + pages * count]
    weight_refs = refs[1 + pages * count : 4 + pages * count]
    first_in_ref, out_ref, held = refs[4 + pages * count :]
    rank = words_ref[0]
    width = out_ref.shape[1]
    block = out_ref.shape[0] // pages
    for page in range(pages):
        for at in range(count):
            part = part_refs[page * count + at]
            place = pl.multiple_of((rank ^ at) * span, span)
            for kind in range(3):
                held[kind, pl.ds(place, span), page * block : (page + 1) * block] = part[
                    :, kind * block : (kind + 1) * block
                ]
    total = dot(weight_refs[0][...], held[0, :width])
    for kind in range(1, 3):
        total = total + dot(weight_refs[kind][...], held[kind, :width])
    out_ref[...] = (first_in_ref[...] + total.T).astype(BF16)


def input_gradient(words, parts, weights, first_in):
    pages, count = len(parts), len(parts[0])
    span = parts[0][0].shape[0]
    rows, width = first_in.shape
    vmem = pl.BlockSpec(memory_space=pltpu.VMEM)
    return pl.pallas_call(
        functools.partial(input_kernel, pages, count, span),
        in_specs=[pl.BlockSpec(memory_space=pltpu.SMEM)] + [vmem] * (pages * count + 4),
        out_specs=vmem,
        out_shape=jax.ShapeDtypeStruct((rows, width), BF16),
        scratch_shapes=[pltpu.VMEM((3, count * span, rows), BF16)],
        compiler_params=pltpu.CompilerParams(vmem_limit_bytes=VMEM_LIMIT),
        cost_estimate=pl.CostEstimate(
            flops=6 * rows * width * count * span,
            bytes_accessed=2 * width * (5 * rows + 3 * count * span),
            transcendentals=0,
        ),
        name="input_gradient",
    )(words, *[part for page in parts for part in page], *weights, first_in)


def local(body, name, words, arrays, shapes, costly=False):
    def kernel(words_ref, *refs):
        body(words_ref, refs[: len(arrays)], refs[len(arrays) :])

    vmem = pl.BlockSpec(memory_space=pltpu.VMEM)
    shapes = [jax.ShapeDtypeStruct(shape, kind) for shape, kind in shapes]
    moved = sum(item.size * item.dtype.itemsize for item in list(arrays) + shapes)
    cost = pl.CostEstimate(flops=0, bytes_accessed=moved, transcendentals=0)
    return pl.pallas_call(
        kernel,
        in_specs=[pl.BlockSpec(memory_space=pltpu.SMEM)] + [vmem] * len(arrays),
        out_specs=[vmem] * len(shapes),
        out_shape=shapes,
        compiler_params=pltpu.CompilerParams(vmem_limit_bytes=VMEM_LIMIT),
        cost_estimate=cost if costly else NO_COST,
        name=name,
    )(words, *arrays)


def shard(index, rows, base=0):
    return pl.ds(pl.multiple_of(base + index * rows, 16), rows)


def total_of(refs, rows=slice(None)):
    total = refs[0][rows].astype(F32)
    for ref in refs[1:]:
        total = total + ref[rows].astype(F32)
    return total


def tree_sum(terms):
    while len(terms) > 1:
        terms = [terms[i] + terms[i + 1] for i in range(0, len(terms), 2)]
    return terms[0]


def bit_of(words, level):
    return lax.shift_right_logical(words[1], level) & 1


def pair_sum(words, mine, other):
    def body(words, ins, outs):
        outs[0][...] = total_of(ins).astype(BF16)

    return local(body, "pair_sum", words, [mine, other], [(mine.shape, BF16)])[0]


def halve(words, level, mine, other):
    *lead, rows, width = mine.shape
    half = rows // 2

    def body(words, ins, outs):
        bit = bit_of(words, level)
        for out, side in zip(outs, (bit, 1 - bit)):
            at = shard(side, half)
            out[...] = total_of(ins, (slice(None), at) if lead else at).astype(BF16)

    return local(body, "halve", words, [mine, other], [((*lead, half, width), BF16)] * 2)


def join_halves(words, level, mine, other):
    rows, width = mine.shape

    def body(words, ins, outs):
        bit = bit_of(words, level)
        outs[0][shard(bit, rows)] = ins[0][...]
        outs[0][shard(1 - bit, rows)] = ins[1][...]

    return local(body, "join_halves", words, [mine, other], [((2 * rows, width), BF16)])[0]


def across(block, level):
    return swapped(block, 1 << level, "depth")


class Plan:
    def __init__(self, rows, rows_a, more, span, width):
        self.count = lax.axis_size("blk")
        self.levels = lax.axis_size("depth").bit_length() - 1
        self.rows = rows
        self.rows_a = rows_a
        self.more = more
        self.span = span
        self.width = width
        self.a_ff = rows_a // self.count
        self.a_more = more // self.count
        self.a = self.a_ff + self.a_more
        self.b = (rows - rows_a) // self.count
        assert width % self.a_ff == 0 and width % self.b == 0 and rows_a % self.b == 0

    def shapes(self, *sizes):
        return [((rows, self.width), BF16) for rows in sizes]

    def scatter_one(self, words, halves):
        count, width = self.count, self.width
        a_ff, half = self.a_ff, self.b // 2

        def kernel(words_ref, *refs):
            parts = refs[6 : 6 + count]
            keep_ref, send_ref = refs[6 + count :]
            for i in range(count):

                @pl.when(pl.program_id(0) == i)
                def _(i=i):
                    parts[i][:a_ff] = total_of(refs[:2]).astype(BF16)
                    parts[i][a_ff:] = total_of(refs[2:4]).astype(BF16)

            bit = bit_of(words_ref, 0)
            keep_ref[0] = total_of(refs[4:6], shard(bit, half)).astype(BF16)
            send_ref[0] = total_of(refs[4:6], shard(1 - bit, half)).astype(BF16)

        def there(rows):
            return pl.BlockSpec((rows, width), lambda i, words: (words[0] ^ i, 0))

        part_b = pl.BlockSpec((self.b, width), lambda i, words: (self.rows_a // self.b + i, 0))
        half_b = pl.BlockSpec((1, half, width), lambda i, words: (i, 0, 0))
        shapes = [jax.ShapeDtypeStruct((self.a, width), BF16)] * count
        shapes += [jax.ShapeDtypeStruct((count, half, width), BF16)] * 2
        *parts_a, keep, send = pl.pallas_call(
            kernel,
            grid_spec=pltpu.PrefetchScalarGridSpec(
                num_scalar_prefetch=1,
                grid=(count,),
                in_specs=[there(a_ff)] * 2 + [there(self.a_more)] * 2 + [part_b] * 2,
                out_specs=[fixed(item) for item in shapes[:count]] + [half_b] * 2,
            ),
            out_shape=shapes,
            compiler_params=pltpu.CompilerParams(vmem_limit_bytes=VMEM_LIMIT),
            cost_estimate=NO_COST,
            name="scatter_one",
        )(words, *halves, *halves[:2])
        return [from_blk(part, i) for i, part in enumerate(parts_a)], keep, across(send, 0)

    def scatter_two(self, words, parts_a, keep_b, other_b):
        count = self.count
        half_a = self.a // 2
        last = self.levels == 1
        half_b = keep_b.shape[1] // 2

        def body(words, ins, outs):
            bit = bit_of(words, 0)
            outs[0][...] = total_of(ins[:count], shard(bit, half_a)).astype(BF16)
            outs[1][...] = total_of(ins[:count], shard(1 - bit, half_a)).astype(BF16)
            bit = bit_of(words, 1)
            for out, side in ((outs[2], bit), (outs[3], 1 - bit)):
                rows = (slice(None), shard(side, half_b))
                out[...] = total_of(ins[count:], rows).astype(BF16)

        assert not last
        shapes = self.shapes(half_a, half_a) + [((count, half_b, self.width), BF16)] * 2
        keep_a, send_a, keep_b, send_b = local(
            body, "scatter_two", words, [*parts_a, keep_b, other_b], shapes
        )
        return keep_a, across(send_a, 0), keep_b, across(send_b, 1)

    def scatter_three(self, words, keep_a, other_a, keep_b, other_b):
        count = self.count
        b_rows = keep_b.shape[1]

        def body(words, ins, outs):
            outs[0][...] = total_of(ins[:2]).astype(BF16)
            for i in range(count):
                outs[1 + i][...] = total_of(ins[2:], words[0] ^ i).astype(BF16)

        shapes = self.shapes(keep_a.shape[0], *[b_rows] * count)
        arrays = [keep_a, other_a, keep_b, other_b]
        part_a, *parts_b = local(body, "scatter_three", words, arrays, shapes)
        return part_a, [from_blk(item, i) for i, item in enumerate(parts_b)]

    def sum_b(self, words, parts_b):
        def body(words, ins, outs):
            outs[0][...] = total_of(ins).astype(BF16)

        return local(body, "sum_b", words, parts_b, self.shapes(parts_b[0].shape[0]))[0]


def gather_blk(part, cut, late=None):
    count = lax.axis_size("blk")
    if count != 4:
        return [(i, 0, from_blk(part, i)) for i in range(count)]
    one, two = swapped(part, 1), swapped(part, 2)
    if late is not None:
        one, two = after(late, (one, two))
    first, second = swapped(one[:cut], 2), swapped(two[cut:], 1)
    return [(0, 0, part), (1, 0, one), (2, 0, two), (3, 0, first), (3, cut, second)]


def with_core(pieces):
    return [(distance, base, from_core(item)) for distance, base, item in pieces]


SLOTS = 4


def widen_own(words, plan, pieces_a, pieces_b, hidden):
    width = plan.width
    chunks = hidden // width
    pairs = chunks // 2
    arrays = [item for _, _, item in (*pieces_a, *pieces_b)]
    segments = []
    extras = []
    for at, (distance, base, item) in enumerate(pieces_a):
        rows = min(item.shape[0], plan.a_ff - base)
        if rows > 0:
            segments.append((at, rows, distance, plan.a_ff, base))
        if base + item.shape[0] == plan.a:
            extras.append((at, distance))
    for at, (distance, base, item) in enumerate(pieces_b, len(pieces_a)):
        segments.append((at, item.shape[0], distance, plan.b, plan.rows_a + base))

    def kernel(words_ref, *refs):
        ins = refs[: len(arrays)]
        joined_ref, expand_ref, reduce_ref, held, sems = refs[len(arrays) :]
        copies = []
        for index, (at, rows, distance, share, first) in enumerate(segments):
            slot = index % SLOTS
            if index >= SLOTS:
                copies[index - SLOTS].wait()
            part = ins[at][:rows]
            held[slot, :rows] = part.astype(F32)
            place = pl.multiple_of(first + (words_ref[0] ^ distance) * share, 64)
            joined_ref[pl.ds(place, rows)] = part
            matrix = lax.div(place, width)
            row = place - matrix * width
            chunk = (lax.div(matrix, 2) + words_ref[2] * pairs) % chunks
            column = pl.multiple_of(chunk * width, width)
            source = held.at[slot, :rows]
            to_expand = pltpu.make_async_copy(
                source,
                expand_ref.at[pl.ds(pl.multiple_of(row, 64), rows), pl.ds(column, width)],
                sems.at[slot],
            )
            to_reduce = pltpu.make_async_copy(
                source,
                reduce_ref.at[pl.ds(pl.multiple_of(column + row, 64), rows)],
                sems.at[slot],
            )
            is_expand = lax.rem(matrix, 2) == 0
            pl.when(is_expand)(to_expand.start)
            pl.when(jnp.logical_not(is_expand))(to_reduce.start)
            copies.append(to_reduce)
        for at, distance in extras:
            rows = shard(words_ref[0] ^ distance, plan.a_more, plan.rows)
            joined_ref[rows] = ins[at][ins[at].shape[0] - plan.a_more :]
        for copy in copies[-SLOTS:]:
            copy.wait()

    vmem = pl.BlockSpec(memory_space=pltpu.VMEM)
    anywhere = pl.BlockSpec(memory_space=pl.ANY)
    return pl.pallas_call(
        kernel,
        in_specs=[pl.BlockSpec(memory_space=pltpu.SMEM)] + [vmem] * len(arrays),
        out_specs=[vmem, anywhere, anywhere],
        out_shape=[
            jax.ShapeDtypeStruct((plan.rows + plan.more, width), BF16),
            jax.ShapeDtypeStruct((width, hidden), F32),
            jax.ShapeDtypeStruct((hidden, width), F32),
        ],
        scratch_shapes=[
            pltpu.VMEM((SLOTS, max(plan.a_ff, plan.b), width), F32),
            pltpu.SemaphoreType.DMA((SLOTS,)),
        ],
        compiler_params=pltpu.CompilerParams(vmem_limit_bytes=VMEM_LIMIT),
        cost_estimate=pl.CostEstimate(
            flops=0, bytes_accessed=6 * hidden * width, transcendentals=0
        ),
        name="widen_own",
    )(words, *arrays)


def widen_other(words, joined, expand, reduce):
    width, hidden = expand.shape
    chunks = hidden // width
    pairs = chunks // 2

    def kernel(words_ref, half_ref, before_ref, before_too_ref, expand_ref, reduce_ref):
        expand_ref[...] = half_ref[:width].astype(F32)
        reduce_ref[...] = half_ref[width:].astype(F32)

    def place(s, words):
        return (s + (words[2] + 1) * pairs) % chunks

    anywhere = pl.BlockSpec(memory_space=pl.ANY)
    return pl.pallas_call(
        kernel,
        grid_spec=pltpu.PrefetchScalarGridSpec(
            num_scalar_prefetch=1,
            grid=(pairs,),
            in_specs=[
                pl.BlockSpec((2 * width, width), lambda s, words: (s, 0)),
                anywhere,
                anywhere,
            ],
            out_specs=[
                pl.BlockSpec((width, width), lambda s, words: (0, place(s, words))),
                pl.BlockSpec((width, width), lambda s, words: (place(s, words), 0)),
            ],
        ),
        out_shape=[
            jax.ShapeDtypeStruct((width, hidden), F32),
            jax.ShapeDtypeStruct((hidden, width), F32),
        ],
        input_output_aliases={2: 0, 3: 1},
        compiler_params=pltpu.CompilerParams(vmem_limit_bytes=VMEM_LIMIT),
        cost_estimate=pl.CostEstimate(
            flops=0, bytes_accessed=6 * hidden * width, transcendentals=0
        ),
        name="widen_other",
    )(words, joined, expand, reduce)


def finished(words, plan, heads, joined, side, before=()):
    count = plan.count
    span = plan.span
    width = plan.width
    half_rows = width // 2
    arrays = [item for _, _, item in heads]

    def kernel(words_ref, *refs):
        heads_refs, refs = refs[: len(heads)], refs[len(heads) :]
        extra_ref, refs = refs[0], refs[1 + len(before) :]
        outs, refs = refs[:5], refs[5:]
        gathered, wide, project, sems = refs
        rank = words_ref[0]
        half = words_ref[2] ^ side
        for ref, (distance, base, _) in zip(heads_refs, heads):
            rows = ref.shape[0]
            place = pl.multiple_of((rank ^ distance) * span, HEAD_DIM)
            for part in range(2):
                low, high = max(base, part * span), min(base + rows, (part + 1) * span)
                if low < high:
                    gathered[part, pl.ds(place + (low - part * span), high - low)] = ref[
                        low - base : high - base
                    ]
        for part in range(2):
            wide[part] = gathered[part, :width].astype(F32).T
        project[...] = extra_ref[:half_rows].astype(F32)

        @pl.when(half == 1)
        def _():
            wide[1] = entry_order(wide[1])

        def copy(source, target, at):
            return pltpu.make_async_copy(source, target, sems.at[at])

        for part in range(2):
            pl.when(half == 0)(copy(wide.at[part], outs[part], part).start)
            pl.when(half == 1)(copy(wide.at[part], outs[2 + part], part).start)
        rows = pl.ds(pl.multiple_of(half * half_rows, half_rows), half_rows)
        last = copy(project, outs[4].at[rows], 2)
        last.start()
        for part in range(2):
            copy(wide.at[part], outs[part], part).wait()
        last.wait()

    def whole(item):
        return pl.BlockSpec(item.shape, lambda s: (0, 0))

    more = pl.BlockSpec((plan.more, width), lambda s: (plan.rows // plan.more, 0))
    anywhere = pl.BlockSpec(memory_space=pl.ANY)
    first = 2 + len(heads)
    shapes = [jax.ShapeDtypeStruct((width, width), F32)] * 5
    return pl.pallas_call(
        kernel,
        grid=(1,),
        in_specs=[pl.BlockSpec(memory_space=pltpu.SMEM)]
        + [whole(item) for item in arrays]
        + [more]
        + [anywhere] * len(before),
        out_specs=[anywhere] * 5,
        out_shape=shapes,
        scratch_shapes=[
            pltpu.VMEM((2, count * span, width), BF16),
            pltpu.VMEM((2, width, width), F32),
            pltpu.VMEM((half_rows, width), F32),
            pltpu.SemaphoreType.DMA((3,)),
        ],
        input_output_aliases={first + at: at for at in range(len(before))},
        compiler_params=pltpu.CompilerParams(vmem_limit_bytes=VMEM_LIMIT),
        cost_estimate=pl.CostEstimate(
            flops=0, bytes_accessed=16 * width * width, transcendentals=0
        ),
        name="finish",
    )(words, *arrays, joined, *before)


def per_device(
    tokens,
    boxes,
    w_query,
    w_key,
    w_value,
    w_output,
    box_weight,
    first_gain,
    first_shift,
    w_expand,
    w_reduce,
    second_gain,
    second_shift,
    cotangent,
):
    pages, block, width = tokens.shape
    count = lax.axis_size("blk")
    depth = lax.axis_size("depth")
    words = jnp.stack(
        [lax.axis_index("blk"), lax.axis_index("depth"), lax.axis_index("core")]
    ).astype(jnp.int32)
    hidden = w_expand.shape[1]
    span = -(-HEADS // count) * HEAD_DIM
    unit = 16 * count * depth
    more = -(-(width // 2 + 16) // unit) * unit

    own_places = jnp.stack([boxes[0] + boxes[2], boxes[1] + boxes[3]], axis=1)
    own_places = jnp.stack([lax.shift_right_logical(own_places, 6), own_places & 63], axis=2)
    own_places = own_places.reshape(4 * pages, block).astype(BF16)
    own_places = jnp.pad(own_places, ((0, 16 - 4 * pages), (0, width - block)))
    message = jnp.concatenate([tokens[0], own_places])
    messages = [from_blk(message, i) for i in range(count)]
    w_own, box_own, rot_cos, rot_sin = prepare(
        words, w_query, w_key, w_value, box_weight, span, count * block
    )
    messages, rot_cos = lax.optimization_barrier((messages, rot_cos))
    own = after(messages, tokens[1])
    pieces = [messages, [from_blk(own, i) for i in range(count)]]

    saved = []
    att_parts = []
    for page in range(pages):
        results = attention_forward(
            words, page, messages, pieces[page], w_own, box_own, rot_cos, rot_sin
        )
        saved.append(results[:6])
        att_parts += [from_blk(results[6 + i], i) for i in range(count)]

    vectors = jnp.stack([first_gain, first_shift, second_gain, second_shift])
    results = middle(
        words,
        att_parts,
        tokens.reshape(pages * block, width),
        cotangent.reshape(pages * block, width),
        w_output,
        vectors,
        w_expand,
        w_reduce,
        pages,
        more,
    )
    layer_out, first_in, theirs, mine, more_theirs, more_mine = results[:6]
    grads = [from_blk(results[6 + i], i) for i in range(count)]
    plan = Plan(hidden, hidden - hidden // 2 // unit * unit, more, span, width)
    parts_a, keep_b, other_b = plan.scatter_one(
        after(grads, words), [mine, from_core(theirs), more_mine, from_core(more_theirs)]
    )

    def backward(page, words, before=None):
        return attention_backward(
            words,
            page,
            grads,
            pieces[page],
            saved[page],
            box_own,
            rot_cos,
            rot_sin,
            before,
        )

    *pre_one, before = backward(0, after(parts_a[0], words))
    part_a, other_a, keep_b, other_b = plan.scatter_two(
        after(before, words), parts_a, keep_b, other_b
    )
    done = part_a
    for level in range(2, plan.levels):
        keep_b, send_b = halve(after(done, words), level, keep_b, other_b)
        other_b = across(send_b, level)
        done = keep_b
    pre_one = [from_blk(item, i) for i, item in enumerate(after(part_a, pre_one))]
    *pre_two, heads_mine, heads_theirs = backward(1, after(done, words), before)

    part_a, parts_b = plan.scatter_three(
        after((heads_mine, pre_one), words), part_a, other_a, keep_b, other_b
    )
    heads, other = halve(
        after(part_a, words), 0, heads_mine, from_core(after(part_a, heads_theirs))
    )
    done = heads
    part_b = plan.sum_b(after(done, words), parts_b)
    done = part_b
    pre_two = [from_blk(item, i) for i, item in enumerate(after(part_b, pre_two))]
    done = (part_b, pre_two[1:3])
    for level in range(1, plan.levels):
        part_a = pair_sum(after(done, words), part_a, across(part_a, level))
        done = part_a
    level = plan.levels - 1
    other_b = across(after(part_a, part_b), level)
    part_a = join_halves(words, 0, part_a, across(part_a, 0))
    other = across(after(part_a, other), 0)
    done = part_a
    while level:
        part_b = join_halves(after(done, words), level, part_b, other_b)
        level -= 1
        other_b = across(part_b, level)
        done = part_b
    heads = pair_sum(after(done, words), heads, other)
    input_grad = input_gradient(
        after(heads, words), [pre_one, pre_two], (w_query, w_key, w_value), first_in
    )
    part_b = join_halves(after(input_grad, words), 0, part_b, other_b)
    pieces_a = gather_blk(part_a, plan.a // 2, part_b)
    for level in range(1, plan.levels):
        heads = pair_sum(after(pieces_a[1][2], words), heads, across(heads, level))
    pieces_b = gather_blk(part_b, plan.b // 2, heads)
    done = [pieces_b[1][2], pieces_a[-2][2], pieces_a[-1][2]]
    heads = join_halves(after(done, words), 0, heads, across(heads, 0))
    joined, *wide = widen_own(after(heads, words), plan, pieces_a, pieces_b, hidden)
    pieces_heads = gather_blk(heads, span, joined)
    joined_other = from_core(after(pieces_heads[1][2], joined))
    at = plan.rows + width // 2
    sums = jnp.where(words[2] == 0, joined[at : at + 4], joined_other[at : at + 4])
    sums = [sums[i].astype(F32) for i in range(4)]
    grad_expand, grad_reduce = widen_other(after(sums, words), joined_other, *wide)
    grads = finished(after(grad_expand, words), plan, pieces_heads, joined, 0)
    grad_query, grad_key, grad_value, grad_box, grad_project = finished(
        after(grads, words), plan, with_core(pieces_heads), joined_other, 1, grads
    )
    return (
        layer_out.reshape(tokens.shape),
        input_grad.reshape(tokens.shape),
        grad_query,
        grad_key,
        grad_value,
        grad_project,
        grad_box,
        sums[0],
        sums[1],
        grad_expand,
        grad_reduce,
        sums[2],
        sums[3],
    )


def solution(mesh):
    blocks, rest = mesh.devices.shape
    parts = jax.sharding.Mesh(
        mesh.devices.reshape(blocks, rest // 2, 2), ("blk", "depth", "core")
    )
    split = P(("depth", "core"), "blk", None)
    return jax.shard_map(
        per_device,
        mesh=parts,
        in_specs=(split, P(None, ("depth", "core"), "blk")) + (P(),) * 11 + (split,),
        out_specs=(split, split) + (P(),) * 11,
        check_vma=False,
    )
```

```python
import functools

import jax
import jax.numpy as jnp
import numpy as np
from jax import lax
from jax.experimental import pallas as pl
from jax.experimental.pallas import tpu as pltpu
from jax.sharding import PartitionSpec as P

HEADS = 12
HEAD_DIM = 64
HALF = 32
FREQS = 192
CODES = 4 * FREQS
VMEM_LIMIT = 60 * 1024 * 1024
NO_COST = pl.CostEstimate(flops=0, bytes_accessed=0, transcendentals=0)
F32 = jnp.float32
BF16 = jnp.bfloat16


def dot(left, right):
    return lax.dot_general(left, right, (((1,), (0,)), ((), ())), preferred_element_type=F32)


def dot_nt(left, right):
    return lax.dot_general(left, right, (((1,), (1,)), ((), ())), preferred_element_type=F32)


def dot_tn(left, right):
    return lax.dot_general(left, right, (((0,), (0,)), ((), ())), preferred_element_type=F32)


def swapped(block, distance, axis="blk"):
    count = lax.axis_size(axis)
    return lax.ppermute(block, axis, [(i, i ^ distance) for i in range(count)])


def from_blk(block, distance):
    return swapped(block, distance) if distance else block


def from_core(block):
    return swapped(block, 1, "core")


def after(done, value):
    return lax.optimization_barrier((value, done))[0]


def turned(upper, lower, cosines, sines):
    return upper * cosines - lower * sines, lower * cosines + upper * sines


def entry_order(rows):
    return jnp.concatenate(
        [
            rows[:FREQS],
            rows[2 * FREQS : 3 * FREQS],
            rows[FREQS : 2 * FREQS],
            rows[3 * FREQS :],
        ],
        axis=0,
    )


def angle_tables():
    rates = np.float32(10000.0) ** (-np.arange(FREQS, dtype=np.float32) / np.float32(FREQS))
    tables = []
    for places in (32.0 * np.arange(32), 0.5 * np.arange(64)):
        angles = rates.astype(np.float64)[:, None] * places[None, :]
        left = np.concatenate([np.sin(angles), np.cos(angles)])
        parts = []
        for _ in range(3):
            parts.append(left.astype(jnp.bfloat16))
            left = left - parts[-1].astype(np.float64)
        tables.append(np.concatenate(parts, axis=1))
    return tables


def rotary_tables(length):
    rates = np.float32(10000.0) ** (-np.arange(HALF, dtype=np.float32) / np.float32(HALF))
    angles = np.arange(length, dtype=np.float32)[None, :] * rates[:, None]
    angles = angles.astype(np.float64)
    return np.cos(angles).astype(np.float32), np.sin(angles).astype(np.float32)


def prepare_kernel(
    words_ref,
    query_ref,
    key_ref,
    value_ref,
    box_ref,
    cos_ref,
    sin_ref,
    own_ref,
    own_box_ref,
    own_cos_ref,
    own_sin_ref,
):
    rank = words_ref[0]
    span = own_box_ref.shape[0]
    width = query_ref.shape[1]
    count = lax.axis_size("blk")
    block = cos_ref.shape[1] // count
    row = lax.broadcasted_iota(jnp.int32, (span, width), 0) + rank * span
    column = lax.broadcasted_iota(jnp.int32, (span, width), 1)
    pick = jnp.where(row == column, 1.0, 0.0).astype(BF16)
    for kind, ref in enumerate((query_ref, key_ref, value_ref)):
        own_ref[kind * span : (kind + 1) * span] = dot_nt(pick, ref[...]).astype(BF16)
    own_box_ref[...] = dot_nt(pick, entry_order(box_ref[...])).astype(BF16)
    for i in range(count):
        from_cols = pl.ds(pl.multiple_of((rank ^ i) * block, block), block)
        own_cos_ref[:, i * block : (i + 1) * block] = cos_ref[:, from_cols]
        own_sin_ref[:, i * block : (i + 1) * block] = sin_ref[:, from_cols]


def prepare(words, w_query, w_key, w_value, box_weight, span, length):
    width = w_query.shape[0]
    vmem = pl.BlockSpec(memory_space=pltpu.VMEM)
    return pl.pallas_call(
        prepare_kernel,
        in_specs=[pl.BlockSpec(memory_space=pltpu.SMEM)] + [vmem] * 6,
        out_specs=[vmem] * 4,
        out_shape=[
            jax.ShapeDtypeStruct((3 * span, width), BF16),
            jax.ShapeDtypeStruct((span, CODES), BF16),
            jax.ShapeDtypeStruct((HALF, length), F32),
            jax.ShapeDtypeStruct((HALF, length), F32),
        ],
        compiler_params=pltpu.CompilerParams(vmem_limit_bytes=VMEM_LIMIT),
        cost_estimate=pl.CostEstimate(
            flops=8 * span * width * width, bytes_accessed=10 * width * width, transcendentals=0
        ),
        name="prepare",
    )(words, w_query, w_key, w_value, box_weight, *map(jnp.asarray, rotary_tables(length)))


def fold(value, combine):
    while value.shape[0] > 8:
        half = value.shape[0] // 2
        value = combine(value[:half], value[half:])
    return value


def write_codes(page, place_refs, high_ref, low_ref, sin_ref, cos_ref, codes_ref):
    block = sin_ref.shape[1] // len(place_refs)

    def looked_up(table_ref, index):
        spots = table_ref.shape[1] // 3
        rows = lax.broadcasted_iota(jnp.int32, (spots, block), 0).astype(F32)
        once = jnp.where(rows == index, 1.0, 0.0)
        found = dot(table_ref[...], jnp.concatenate([once] * 3, axis=0).astype(BF16))
        return found[:FREQS], found[FREQS:]

    for i, place_ref in enumerate(place_refs):
        columns = slice(i * block, (i + 1) * block)
        places = place_ref[:, :block].astype(F32)
        for axis in range(2):
            at = 4 * page + 2 * axis
            high_sin, high_cos = looked_up(high_ref, places[at : at + 1])
            low_sin, low_cos = looked_up(low_ref, places[at + 1 : at + 2])
            sines = high_sin * low_cos + high_cos * low_sin
            cosines = high_cos * low_cos - high_sin * low_sin
            rows = slice(axis * FREQS, (axis + 1) * FREQS)
            later = slice((2 + axis) * FREQS, (3 + axis) * FREQS)
            sin_ref[rows, columns] = sines
            cos_ref[rows, columns] = cosines
            codes_ref[rows, columns] = sines.astype(BF16)
            codes_ref[later, columns] = cosines.astype(BF16)


def forward_kernel(page, count, words_ref, *refs):
    place_refs, refs = refs[:count], refs[count:]
    piece_refs, refs = refs[:count], refs[count:]
    high_ref, low_ref, w_ref, box_ref, rot_cos_ref, rot_sin_ref = refs[:6]
    probs_ref, att_ref, heads_ref, sin_ref, cos_ref, codes_ref = refs[6:12]
    low_refs = refs[12 : 12 + count]
    tok_ref, pre_ref, kc_ref, qr_ref = refs[12 + count :]
    rows = tok_ref.shape[0]
    block = rows // count
    head = pl.program_id(0)
    span = pl.num_programs(0) * HEAD_DIM

    @pl.when(head == 0)
    def _():
        for i in range(count):
            tok_ref[i * block : (i + 1) * block] = piece_refs[i][...]
        pre_ref[...] = dot_nt(w_ref[...], tok_ref[...])
        write_codes(page, place_refs, high_ref, low_ref, sin_ref, cos_ref, codes_ref)
        kc_ref[:, :CODES] = codes_ref[...].astype(F32).T.astype(BF16)

    def pre(kind):
        at = kind * span + head * HEAD_DIM
        return pre_ref[pl.ds(pl.multiple_of(at, HEAD_DIM), HEAD_DIM)]

    rot_cos = rot_cos_ref[...]
    rot_sin = rot_sin_ref[...]
    query_pre = pre(0).astype(BF16)
    wide = query_pre.astype(F32)
    query = jnp.concatenate(turned(wide[:HALF], wide[HALF:], rot_cos, rot_sin), axis=0)
    key_pre = pre(1)
    key = jnp.concatenate(turned(key_pre[:HALF], key_pre[HALF:], rot_cos, rot_sin), axis=0)
    value = pre(2).astype(BF16)
    heads_ref[0, :HEAD_DIM] = query_pre
    heads_ref[0, HEAD_DIM : 2 * HEAD_DIM] = query.astype(BF16)
    heads_ref[0, 2 * HEAD_DIM : 3 * HEAD_DIM] = key.astype(BF16)
    heads_ref[0, 3 * HEAD_DIM :] = value
    kc_ref[:, CODES:] = key.T.astype(BF16)
    qr_ref[CODES:] = (query * 0.125).astype(BF16)
    step = min(256, block)

    def logits_at(at):
        part = slice(at, at + step)
        projected = dot_tn(box_ref[...], query_pre[:, part])
        sines = sin_ref[:, part]
        cosines = cos_ref[:, part]
        upper = projected[: 2 * FREQS]
        lower = projected[2 * FREQS :]
        qr_ref[: 2 * FREQS, part] = ((upper * cosines + lower * sines) * 0.125).astype(BF16)
        qr_ref[2 * FREQS : CODES, part] = ((lower * cosines - upper * sines) * 0.125).astype(BF16)
        return dot(kc_ref[...], qr_ref[:, part])

    following = logits_at(0)
    for at in range(0, rows, step):
        logits = following
        if at + step < rows:
            following = logits_at(at + step)
        peak = jnp.max(fold(logits, jnp.maximum), axis=0, keepdims=True)
        weight = jnp.exp(logits - peak)
        total = jnp.sum(fold(weight, jnp.add), axis=0, keepdims=True)
        probs = (weight * (1.0 / total)).astype(BF16)
        probs_ref[0, :, at : at + step] = probs
        attended = dot(value, probs)
        att_ref[0, :, at : at + step] = attended
        inner = at % block
        low_refs[at // block][:, inner : inner + step] = attended.astype(BF16)


def fixed(array):
    return pl.BlockSpec(array.shape, lambda *at: (0,) * len(array.shape))


def attention_forward(words, page, messages, pieces, w_own, box_own, rot_cos, rot_sin):
    count = len(messages)
    block, width = messages[0].shape[0] - 16, messages[0].shape[1]
    rows = count * block
    span = box_own.shape[0]
    heads = span // HEAD_DIM
    tables = [jnp.asarray(item) for item in angle_tables()]
    specs = [pl.BlockSpec((block, width), lambda h, words: (0, 0))] * count
    places = pl.BlockSpec((16, width), lambda h, words: (block // 16, 0))
    out_shape = [
        jax.ShapeDtypeStruct((heads, rows, rows), BF16),
        jax.ShapeDtypeStruct((heads, HEAD_DIM, rows), F32),
        jax.ShapeDtypeStruct((heads, 4 * HEAD_DIM, rows), BF16),
        jax.ShapeDtypeStruct((2 * FREQS, rows), F32),
        jax.ShapeDtypeStruct((2 * FREQS, rows), F32),
        jax.ShapeDtypeStruct((CODES, rows), BF16),
    ] + [jax.ShapeDtypeStruct((span, block), BF16)] * count
    return pl.pallas_call(
        functools.partial(forward_kernel, page, count),
        grid_spec=pltpu.PrefetchScalarGridSpec(
            num_scalar_prefetch=1,
            grid=(heads,),
            in_specs=[places] * count
            + specs
            + [fixed(item) for item in (*tables, w_own)]
            + [
                pl.BlockSpec((HEAD_DIM, CODES), lambda h, words: (h, 0)),
                fixed(rot_cos),
                fixed(rot_sin),
            ],
            out_specs=[
                pl.BlockSpec((1, rows, rows), lambda h, words: (h, 0, 0)),
                pl.BlockSpec((1, HEAD_DIM, rows), lambda h, words: (h, 0, 0)),
                pl.BlockSpec((1, 4 * HEAD_DIM, rows), lambda h, words: (h, 0, 0)),
            ]
            + [fixed(item) for item in out_shape[3:6]]
            + [pl.BlockSpec((HEAD_DIM, block), lambda h, words: (h, 0))] * count,
            scratch_shapes=[
                pltpu.VMEM((rows, width), BF16),
                pltpu.VMEM((3 * span, rows), F32),
                pltpu.VMEM((rows, CODES + HEAD_DIM), BF16),
                pltpu.VMEM((CODES + HEAD_DIM, rows), BF16),
            ],
        ),
        out_shape=out_shape,
        compiler_params=pltpu.CompilerParams(vmem_limit_bytes=VMEM_LIMIT),
        cost_estimate=pl.CostEstimate(
            flops=2 * heads * rows * (rows * 1100 + 200 * width + 64 * CODES),
            bytes_accessed=2 * heads * rows * rows + 12 * rows * width,
            transcendentals=heads * rows * rows,
        ),
        name="attention_forward",
    )(words, *messages, *pieces, *tables, w_own, box_own, rot_cos, rot_sin)


def backward_kernel(count, last, words_ref, *refs):
    grad_refs, refs = refs[:count], refs[count:]
    piece_refs, refs = refs[:count], refs[count:]
    probs_ref, att_ref, heads_ref, box_ref, codes_ref, sin_ref, cos_ref = refs[:7]
    rot_cos_ref, rot_sin_ref = refs[7:9]
    refs = refs[9:]
    if last:
        before_ref, refs = refs[0], refs[1:]
    pre_refs, refs = refs[:count], refs[count:]
    if last:
        mine_ref, theirs_ref, *refs = refs
    weight_grad_ref, kc_ref, logit_grad_ref, entry_grad_ref, turned_ref = refs
    block, width = piece_refs[0].shape
    rows = count * block
    head = pl.program_id(0)
    span = pl.num_programs(0) * HEAD_DIM

    @pl.when(head == 0)
    def _():
        kc_ref[:CODES] = codes_ref[...]

    kc_ref[CODES:] = heads_ref[0, 2 * HEAD_DIM : 3 * HEAD_DIM]
    packed = heads_ref[0].astype(F32).T.astype(BF16)
    query_pre = packed[:, :HEAD_DIM]
    query = packed[:, HEAD_DIM : 2 * HEAD_DIM]
    value = packed[:, 3 * HEAD_DIM :] * jnp.asarray(0.125, BF16)
    rot_cos = rot_cos_ref[...]
    rot_sin = rot_sin_ref[...]
    grad = jnp.concatenate([ref[...] for ref in grad_refs], axis=1)
    grad_tall = grad.astype(F32).T.astype(BF16)
    offsets = jnp.sum(grad.astype(F32) * att_ref[0], axis=0, keepdims=True) * 0.125
    step = min(256, block)
    place = pl.multiple_of(head * HEAD_DIM, HEAD_DIM)
    here = pl.ds(place, HEAD_DIM)

    def logits_back(at):
        part = slice(at, at + step)
        grad_probs = dot(value, grad[:, part])
        logit_grad_ref[:, part] = (
            probs_ref[0, :, part].astype(F32) * (grad_probs - offsets[:, part])
        ).astype(BF16)

    logits_back(0)
    for at in range(0, rows, step):
        if at + step < rows:
            logits_back(at + step)
        part = slice(at, at + step)
        back = dot(kc_ref[...], logit_grad_ref[:, part])
        sines = sin_ref[:, part]
        cosines = cos_ref[:, part]
        upper = back[: 2 * FREQS]
        lower = back[2 * FREQS : CODES]
        entry_grad_ref[: 2 * FREQS, part] = (upper * cosines - lower * sines).astype(BF16)
        entry_grad_ref[2 * FREQS :, part] = (lower * cosines + upper * sines).astype(BF16)
        first = back[CODES : CODES + HALF]
        second = back[CODES + HALF :]
        turned_ref[:HALF, part], turned_ref[HALF:, part] = turned(
            first, second, rot_cos[:, part], -rot_sin[:, part]
        )
    key_flat = dot(logit_grad_ref[...], query).T
    value_low = dot(probs_ref[0], grad_tall).T.astype(BF16)
    query_low = (turned_ref[...] + dot(box_ref[...], entry_grad_ref[...])).astype(BF16)
    key_low = jnp.concatenate(
        turned(key_flat[:HALF], key_flat[HALF:], rot_cos, -rot_sin), axis=0
    ).astype(BF16)
    for i in range(count):
        columns = slice(i * block, (i + 1) * block)
        pre_refs[i][here, :block] = query_low[:, columns]
        pre_refs[i][here, block : 2 * block] = key_low[:, columns]
        pre_refs[i][here, 2 * block :] = value_low[:, columns]
    weight_grad_ref[pl.ds(3 * span + place, HEAD_DIM)] = dot(entry_grad_ref[...], query_pre).T

    @pl.when(head == pl.num_programs(0) - 1)
    def _():
        for kind in range(3):
            columns = slice(kind * block, (kind + 1) * block)
            total = dot(pre_refs[0][:, columns], piece_refs[0][...])
            for i in range(1, count):
                total = total + dot(pre_refs[i][:, columns], piece_refs[i][...])
            weight_grad_ref[kind * span : (kind + 1) * span] = total
        if last:
            half = 2 * span
            core = words_ref[2]
            ours = pl.ds(pl.multiple_of(core * half, half), half)
            there = pl.ds(pl.multiple_of((1 - core) * half, half), half)
            mine_ref[...] = weight_grad_ref[ours] + before_ref[ours]
            theirs_ref[...] = (weight_grad_ref[there] + before_ref[there]).astype(BF16)


def attention_backward(
    words, page, grads, pieces, saved, box_own, rot_cos, rot_sin, before=None
):
    probs, att, heads_saved, sines, cosines, codes = saved
    count = len(pieces)
    rows, width = probs.shape[1], pieces[0].shape[1]
    block = rows // count
    span = box_own.shape[0]
    heads = span // HEAD_DIM
    last = before is not None
    extra = (before,) if last else ()
    full_shape = (4 * span, width)
    specs = [pl.BlockSpec((block, width), lambda h, words: (0, 0))] * count
    out_shape = [jax.ShapeDtypeStruct((span, 3 * block), BF16)] * count
    if last:
        out_shape += [
            jax.ShapeDtypeStruct((2 * span, width), F32),
            jax.ShapeDtypeStruct((2 * span, width), BF16),
        ]
    else:
        out_shape.append(jax.ShapeDtypeStruct(full_shape, F32))
    return pl.pallas_call(
        functools.partial(backward_kernel, count, last),
        grid_spec=pltpu.PrefetchScalarGridSpec(
            num_scalar_prefetch=1,
            grid=(heads,),
            in_specs=[pl.BlockSpec((HEAD_DIM, block), lambda h, words: (h, page))] * count
            + specs
            + [
                pl.BlockSpec((1, rows, rows), lambda h, words: (h, 0, 0)),
                pl.BlockSpec((1, HEAD_DIM, rows), lambda h, words: (h, 0, 0)),
                pl.BlockSpec((1, 4 * HEAD_DIM, rows), lambda h, words: (h, 0, 0)),
                pl.BlockSpec((HEAD_DIM, CODES), lambda h, words: (h, 0)),
            ]
            + [fixed(item) for item in (codes, sines, cosines, rot_cos, rot_sin, *extra)],
            out_specs=[fixed(item) for item in out_shape],
            scratch_shapes=([pltpu.VMEM(full_shape, F32)] if last else [])
            + [
                pltpu.VMEM((CODES + HEAD_DIM, rows), BF16),
                pltpu.VMEM((rows, rows), BF16),
                pltpu.VMEM((CODES, rows), BF16),
                pltpu.VMEM((HEAD_DIM, rows), F32),
            ],
        ),
        out_shape=out_shape,
        compiler_params=pltpu.CompilerParams(vmem_limit_bytes=VMEM_LIMIT),
        cost_estimate=pl.CostEstimate(
            flops=2 * heads * rows * (rows * 1400 + 200 * width + 128 * CODES),
            bytes_accessed=2 * heads * rows * rows + 12 * rows * width,
            transcendentals=0,
        ),
        name="attention_backward",
    )(
        words,
        *grads,
        *pieces,
        probs,
        att,
        heads_saved,
        box_own,
        codes,
        sines,
        cosines,
        rot_cos,
        rot_sin,
        *extra,
    )


def normed(value):
    centered = value - jnp.mean(value, axis=-1, keepdims=True)
    scale = lax.rsqrt(jnp.mean(centered * centered, axis=-1, keepdims=True) + 1e-05)
    return centered * scale, scale


def norm_back(grad, gain, unit, scale):
    scaled = grad * gain
    return scale * (
        scaled
        - jnp.mean(scaled, axis=-1, keepdims=True)
        - unit * jnp.mean(scaled * unit, axis=-1, keepdims=True)
    )


def column_sum(value):
    return jnp.sum(value, axis=0, keepdims=True)


def middle_kernel(pages, count, span, chunks, *refs):
    total = pages * count
    words_ref = refs[0]
    att_refs = refs[1 : 1 + total]
    (
        tok_ref,
        cot_ref,
        w_out_ref,
        vectors_ref,
        w_expand_ref,
        w_reduce_ref,
    ) = refs[1 + total : 7 + total]
    outs = refs[7 + total :]
    layer_ref, first_in_ref, theirs_ref, mine_ref, more_theirs_ref, more_mine_ref = outs[:6]
    grad_refs = outs[6 : 6 + count]
    (
        sums_ref,
        att_all,
        grad_all,
        unit_one,
        scale_one,
        first_wide,
        first_low,
        first_tall,
        active,
        slope,
        gathered,
        second_in,
        second_low,
    ) = outs[6 + count :]
    rank = words_ref[0]
    width = tok_ref.shape[1]
    block = tok_ref.shape[0] // pages
    step = pl.program_id(0)

    def rows_of(at):
        return pl.ds(pl.multiple_of((rank ^ at) * span, span), span)

    @pl.when(step == 0)
    def _():
        for page in range(pages):
            for at in range(count):
                att_all[rows_of(at), page * block : (page + 1) * block] = att_refs[
                    page * count + at
                ][...]
        branch = dot_tn(att_all[: w_out_ref.shape[0]], w_out_ref[...])
        unit, scale = normed(tok_ref[...].astype(F32) + branch)
        unit_one[...] = unit
        scale_one[...] = jnp.broadcast_to(scale, scale_one.shape)
        first_out = unit * vectors_ref[0:1] + vectors_ref[1:2]
        first_wide[...] = first_out
        first_low[...] = first_out.astype(BF16)
        first_tall[...] = first_out.T.astype(BF16)
        gathered[...] = jnp.zeros_like(gathered)
        sums_ref[...] = jnp.zeros_like(sums_ref)

    for chunk in range(chunks):

        @pl.when(step == chunk)
        def _(chunk=chunk):
            expanded = dot(first_low[...], w_expand_ref[...])
            gate = 0.5 + 0.5 * lax.erf(expanded * np.float32(np.sqrt(0.5)))
            bell = jnp.exp(expanded * expanded * -0.5) * np.float32(1.0 / np.sqrt(2.0 * np.pi))
            low = (expanded * gate).astype(BF16)
            active[chunk] = low
            slope[chunk] = gate + expanded * bell
            gathered[...] += dot(low, w_reduce_ref[...])

    @pl.when(step == chunks - 1)
    def _():
        unit, scale = normed(first_wide[...] + gathered[...])
        layer_ref[...] = (unit * vectors_ref[2:3] + vectors_ref[3:4]).astype(BF16)
        cot = cot_ref[...].astype(F32)
        sums_ref[2:3] = column_sum(cot * unit)
        sums_ref[3:4] = column_sum(cot)
        grad = norm_back(cot, vectors_ref[2:3], unit, scale)
        second_in[...] = grad
        second_low[...] = grad.astype(BF16)
        gathered[...] = grad

    for chunk in range(chunks):

        @pl.when(step == 2 * chunks - 1 - chunk)
        def _(chunk=chunk):
            grad_active = dot_nt(second_low[...], w_reduce_ref[...])
            grad_expanded = (grad_active * slope[chunk]).astype(BF16)
            grads_ref = mine_ref if chunk < chunks // 2 else theirs_ref
            grads_ref[:width] = dot(first_tall[...], grad_expanded).astype(BF16)
            grads_ref[width:] = dot_tn(active[chunk], second_low[...]).astype(BF16)
            gathered[...] += dot_nt(grad_expanded, w_expand_ref[...])

    @pl.when(step == 2 * chunks - 1)
    def _():
        unit = unit_one[...]
        grad_out = gathered[...]
        sums_ref[0:1] = column_sum(grad_out * unit)
        sums_ref[1:2] = column_sum(grad_out)
        grad = norm_back(grad_out, vectors_ref[0:1], unit, scale_one[:, :1])
        first_in_ref[...] = grad
        low = grad.astype(BF16)
        real = w_out_ref.shape[0]
        half = real // 2
        core = words_ref[2]
        for ref, side in ((more_mine_ref, core), (more_theirs_ref, 1 - core)):
            rows = pl.ds(pl.multiple_of(side * half, half), half)
            ref[:half] = dot(att_all[rows], low).astype(BF16)
            ref[half:] = jnp.zeros((ref.shape[0] - half, width), BF16)
            ref[half : half + 16] = sums_ref[...].astype(BF16)
        if grad_all.shape[0] > real:
            grad_all[real:] = jnp.zeros((grad_all.shape[0] - real, low.shape[0]), BF16)
        grad_all[:real] = dot_nt(w_out_ref[...], low).astype(BF16)
        for at in range(count):
            grad_refs[at][...] = grad_all[rows_of(at)]


def middle(words, att_parts, tok, cot, w_out, vectors, w_expand, w_reduce, pages, more):
    rows, width = tok.shape
    count = len(att_parts) // pages
    span, block = att_parts[0].shape
    hidden = w_expand.shape[1]
    chunks = hidden // width
    pairs = chunks // 2

    def whole(array):
        return pl.BlockSpec(array.shape, lambda s, words: (0,) * len(array.shape))

    def chunk_at(s, words):
        at = jnp.minimum(s, 2 * chunks - 1 - s)
        return (at + words[2] * pairs) % chunks

    def theirs_at(s, words):
        return jnp.clip(2 * chunks - 1 - s - pairs, 0, pairs - 1), 0

    def mine_at(s, words):
        return jnp.clip(2 * chunks - 1 - s, 0, pairs - 1), 0

    shapes = [
        jax.ShapeDtypeStruct((rows, width), BF16),
        jax.ShapeDtypeStruct((rows, width), F32),
        jax.ShapeDtypeStruct((hidden, width), BF16),
        jax.ShapeDtypeStruct((hidden, width), BF16),
        jax.ShapeDtypeStruct((more, width), BF16),
        jax.ShapeDtypeStruct((more, width), BF16),
    ] + [jax.ShapeDtypeStruct((span, pages * block), BF16)] * count
    specs = [whole(item) for item in shapes]
    specs[2] = pl.BlockSpec((2 * width, width), theirs_at)
    specs[3] = pl.BlockSpec((2 * width, width), mine_at)
    return pl.pallas_call(
        functools.partial(middle_kernel, pages, count, span, chunks),
        grid_spec=pltpu.PrefetchScalarGridSpec(
            num_scalar_prefetch=1,
            grid=(2 * chunks,),
            in_specs=[whole(item) for item in att_parts]
            + [
                whole(tok),
                whole(cot),
                whole(w_out),
                whole(vectors),
                pl.BlockSpec((width, width), lambda s, words: (0, chunk_at(s, words))),
                pl.BlockSpec((width, width), lambda s, words: (chunk_at(s, words), 0)),
            ],
            out_specs=specs,
            scratch_shapes=[
                pltpu.VMEM((16, width), F32),
                pltpu.VMEM((count * span, rows), BF16),
                pltpu.VMEM((count * span, rows), BF16),
                pltpu.VMEM((rows, width), F32),
                pltpu.VMEM((rows, 128), F32),
                pltpu.VMEM((rows, width), F32),
                pltpu.VMEM((rows, width), BF16),
                pltpu.VMEM((width, rows), BF16),
                pltpu.VMEM((chunks, rows, width), BF16),
                pltpu.VMEM((chunks, rows, width), F32),
                pltpu.VMEM((rows, width), F32),
                pltpu.VMEM((rows, width), F32),
                pltpu.VMEM((rows, width), BF16),
            ],
        ),
        out_shape=shapes,
        compiler_params=pltpu.CompilerParams(vmem_limit_bytes=VMEM_LIMIT),
        cost_estimate=pl.CostEstimate(
            flops=2 * rows * width * (6 * hidden + 3 * width),
            bytes_accessed=8 * width * hidden + 16 * rows * width,
            transcendentals=2 * rows * hidden,
        ),
        name="middle",
    )(words, *att_parts, tok, cot, w_out, vectors, w_expand, w_reduce)


def input_kernel(pages, count, span, *refs):
    words_ref = refs[0]
    part_refs = refs[1 : 1 + pages * count]
    weight_refs = refs[1 + pages * count : 4 + pages * count]
    first_in_ref, out_ref, held = refs[4 + pages * count :]
    rank = words_ref[0]
    width = out_ref.shape[1]
    block = out_ref.shape[0] // pages
    for page in range(pages):
        for at in range(count):
            part = part_refs[page * count + at]
            place = pl.multiple_of((rank ^ at) * span, span)
            for kind in range(3):
                held[kind, pl.ds(place, span), page * block : (page + 1) * block] = part[
                    :, kind * block : (kind + 1) * block
                ]
    total = dot(weight_refs[0][...], held[0, :width])
    for kind in range(1, 3):
        total = total + dot(weight_refs[kind][...], held[kind, :width])
    out_ref[...] = (first_in_ref[...] + total.T).astype(BF16)


def input_gradient(words, parts, weights, first_in):
    pages, count = len(parts), len(parts[0])
    span = parts[0][0].shape[0]
    rows, width = first_in.shape
    vmem = pl.BlockSpec(memory_space=pltpu.VMEM)
    return pl.pallas_call(
        functools.partial(input_kernel, pages, count, span),
        in_specs=[pl.BlockSpec(memory_space=pltpu.SMEM)] + [vmem] * (pages * count + 4),
        out_specs=vmem,
        out_shape=jax.ShapeDtypeStruct((rows, width), BF16),
        scratch_shapes=[pltpu.VMEM((3, count * span, rows), BF16)],
        compiler_params=pltpu.CompilerParams(vmem_limit_bytes=VMEM_LIMIT),
        cost_estimate=pl.CostEstimate(
            flops=6 * rows * width * count * span,
            bytes_accessed=2 * width * (5 * rows + 3 * count * span),
            transcendentals=0,
        ),
        name="input_gradient",
    )(words, *[part for page in parts for part in page], *weights, first_in)


def local(body, name, words, arrays, shapes, costly=False):
    def kernel(words_ref, *refs):
        body(words_ref, refs[: len(arrays)], refs[len(arrays) :])

    vmem = pl.BlockSpec(memory_space=pltpu.VMEM)
    shapes = [jax.ShapeDtypeStruct(shape, kind) for shape, kind in shapes]
    moved = sum(item.size * item.dtype.itemsize for item in list(arrays) + shapes)
    cost = pl.CostEstimate(flops=0, bytes_accessed=moved, transcendentals=0)
    return pl.pallas_call(
        kernel,
        in_specs=[pl.BlockSpec(memory_space=pltpu.SMEM)] + [vmem] * len(arrays),
        out_specs=[vmem] * len(shapes),
        out_shape=shapes,
        compiler_params=pltpu.CompilerParams(vmem_limit_bytes=VMEM_LIMIT),
        cost_estimate=cost if costly else NO_COST,
        name=name,
    )(words, *arrays)


def shard(index, rows, base=0):
    return pl.ds(pl.multiple_of(base + index * rows, 16), rows)


def total_of(refs, rows=slice(None)):
    total = refs[0][rows].astype(F32)
    for ref in refs[1:]:
        total = total + ref[rows].astype(F32)
    return total


def tree_sum(terms):
    while len(terms) > 1:
        terms = [terms[i] + terms[i + 1] for i in range(0, len(terms), 2)]
    return terms[0]


def bit_of(words, level):
    return lax.shift_right_logical(words[1], level) & 1


def pair_sum(words, mine, other):
    def body(words, ins, outs):
        outs[0][...] = total_of(ins).astype(BF16)

    return local(body, "pair_sum", words, [mine, other], [(mine.shape, BF16)])[0]


def halve(words, level, mine, other):
    *lead, rows, width = mine.shape
    half = rows // 2

    def body(words, ins, outs):
        bit = bit_of(words, level)
        for out, side in zip(outs, (bit, 1 - bit)):
            at = shard(side, half)
            out[...] = total_of(ins, (slice(None), at) if lead else at).astype(BF16)

    return local(body, "halve", words, [mine, other], [((*lead, half, width), BF16)] * 2)


def join_halves(words, level, mine, other):
    rows, width = mine.shape

    def body(words, ins, outs):
        bit = bit_of(words, level)
        outs[0][shard(bit, rows)] = ins[0][...]
        outs[0][shard(1 - bit, rows)] = ins[1][...]

    return local(body, "join_halves", words, [mine, other], [((2 * rows, width), BF16)])[0]


def across(block, level):
    return swapped(block, 1 << level, "depth")


class Plan:
    def __init__(self, rows, rows_a, more, span, width):
        self.count = lax.axis_size("blk")
        self.levels = lax.axis_size("depth").bit_length() - 1
        self.rows = rows
        self.rows_a = rows_a
        self.more = more
        self.span = span
        self.width = width
        self.a_ff = rows_a // self.count
        self.a_more = more // self.count
        self.a = self.a_ff + self.a_more
        self.b = (rows - rows_a) // self.count
        assert width % self.a_ff == 0 and width % self.b == 0 and rows_a % self.b == 0

    def shapes(self, *sizes):
        return [((rows, self.width), BF16) for rows in sizes]

    def scatter_one(self, words, halves):
        count, width = self.count, self.width
        a_ff, half = self.a_ff, self.b // 2

        def kernel(words_ref, *refs):
            parts = refs[6 : 6 + count]
            keep_ref, send_ref = refs[6 + count :]
            for i in range(count):

                @pl.when(pl.program_id(0) == i)
                def _(i=i):
                    parts[i][:a_ff] = total_of(refs[:2]).astype(BF16)
                    parts[i][a_ff:] = total_of(refs[2:4]).astype(BF16)

            bit = bit_of(words_ref, 0)
            keep_ref[0] = total_of(refs[4:6], shard(bit, half)).astype(BF16)
            send_ref[0] = total_of(refs[4:6], shard(1 - bit, half)).astype(BF16)

        def there(rows):
            return pl.BlockSpec((rows, width), lambda i, words: (words[0] ^ i, 0))

        part_b = pl.BlockSpec((self.b, width), lambda i, words: (self.rows_a // self.b + i, 0))
        half_b = pl.BlockSpec((1, half, width), lambda i, words: (i, 0, 0))
        shapes = [jax.ShapeDtypeStruct((self.a, width), BF16)] * count
        shapes += [jax.ShapeDtypeStruct((count, half, width), BF16)] * 2
        *parts_a, keep, send = pl.pallas_call(
            kernel,
            grid_spec=pltpu.PrefetchScalarGridSpec(
                num_scalar_prefetch=1,
                grid=(count,),
                in_specs=[there(a_ff)] * 2 + [there(self.a_more)] * 2 + [part_b] * 2,
                out_specs=[fixed(item) for item in shapes[:count]] + [half_b] * 2,
            ),
            out_shape=shapes,
            compiler_params=pltpu.CompilerParams(vmem_limit_bytes=VMEM_LIMIT),
            cost_estimate=NO_COST,
            name="scatter_one",
        )(words, *halves, *halves[:2])
        return [from_blk(part, i) for i, part in enumerate(parts_a)], keep, across(send, 0)

    def scatter_two(self, words, parts_a, keep_b, other_b):
        count = self.count
        half_a = self.a // 2
        last = self.levels == 1
        half_b = keep_b.shape[1] // 2

        def body(words, ins, outs):
            bit = bit_of(words, 0)
            outs[0][...] = total_of(ins[:count], shard(bit, half_a)).astype(BF16)
            outs[1][...] = total_of(ins[:count], shard(1 - bit, half_a)).astype(BF16)
            bit = bit_of(words, 1)
            for out, side in ((outs[2], bit), (outs[3], 1 - bit)):
                rows = (slice(None), shard(side, half_b))
                out[...] = total_of(ins[count:], rows).astype(BF16)

        assert not last
        shapes = self.shapes(half_a, half_a) + [((count, half_b, self.width), BF16)] * 2
        keep_a, send_a, keep_b, send_b = local(
            body, "scatter_two", words, [*parts_a, keep_b, other_b], shapes
        )
        return keep_a, across(send_a, 0), keep_b, across(send_b, 1)

    def scatter_three(self, words, keep_a, other_a, keep_b, other_b):
        count = self.count
        b_rows = keep_b.shape[1]

        def body(words, ins, outs):
            outs[0][...] = total_of(ins[:2]).astype(BF16)
            for i in range(count):
                outs[1 + i][...] = total_of(ins[2:], words[0] ^ i).astype(BF16)

        shapes = self.shapes(keep_a.shape[0], *[b_rows] * count)
        arrays = [keep_a, other_a, keep_b, other_b]
        part_a, *parts_b = local(body, "scatter_three", words, arrays, shapes)
        return part_a, [from_blk(item, i) for i, item in enumerate(parts_b)]

    def pack(self, words, heads, other, parts_b):
        def body(words, ins, outs):
            rows = ins[0].shape[0]
            outs[0][:rows] = total_of(ins[:2]).astype(BF16)
            outs[0][rows:] = total_of(ins[2:]).astype(BF16)

        arrays = [heads, other, *parts_b]
        rows = heads.shape[0] + parts_b[0].shape[0]
        return local(body, "pack", words, arrays, self.shapes(rows))[0]

    def step(self, words, level, mine, other):
        heads = self.span
        rows = mine.shape[0] - heads
        to = 2 * heads if level == 0 else heads

        def body(words, ins, outs):
            bit = bit_of(words, level)
            if level:
                outs[0][:heads] = total_of(ins, slice(0, heads)).astype(BF16)
            else:
                outs[0][shard(bit, heads)] = ins[0][:heads]
                outs[0][shard(1 - bit, heads)] = ins[1][:heads]
            outs[0][shard(bit, rows, to)] = ins[0][heads:]
            outs[0][shard(1 - bit, rows, to)] = ins[1][heads:]

        return local(body, "step", words, [mine, other], self.shapes(to + 2 * rows))[0]


def gather_blk(part, cut, late=None):
    count = lax.axis_size("blk")
    if count != 4:
        return [(i, 0, from_blk(part, i)) for i in range(count)], []
    one, two = swapped(part, 1), swapped(part, 2)
    if late is not None:
        one, two = after(late, (one, two))
    sent = [one[:cut], two[cut:]]
    first, second = swapped(sent[0], 2), swapped(sent[1], 1)
    return [(0, 0, part), (1, 0, one), (2, 0, two), (3, 0, first), (3, cut, second)], sent


def with_core(pieces):
    return [(distance, base, from_core(item)) for distance, base, item in pieces]


def widened(words, plan, pieces, part, side, hidden, before=()):
    width = plan.width
    chunks = hidden // width
    pairs = chunks // 2
    share = plan.b if part else plan.a_ff
    skip = 2 * plan.span if part else 0
    arrays = []
    segments = []
    extras = []
    joins = not part and not side
    for distance, base, item in pieces:
        at = len(arrays)
        if distance is None:
            segments += [(at, top, share, None, top) for top in range(0, plan.rows_a, share)]
            arrays.append(item)
            continue
        stop = base + item.shape[0]
        low, high = max(base, skip), min(stop, skip + share)
        if low < high:
            segments.append((at, low - base, high - low, distance, low - skip))
        if joins and stop == plan.a:
            extras.append((at, distance))
        if low < high or joins and stop == plan.a:
            arrays.append(item)

    def kernel(words_ref, *refs):
        ins = refs[: len(arrays)]
        refs = refs[len(arrays) + len(before) :]
        expand_ref, reduce_ref, *joined_refs, held, sems = refs
        copies = []
        for slot, (at, top, rows, distance, inner) in enumerate(segments):
            value = ins[at][top : top + rows]
            held[slot, :rows] = value.astype(F32)
            place = part * plan.rows_a + inner
            if distance is not None:
                place = place + (words_ref[0] ^ distance) * share
            if joins:
                joined_refs[0][pl.ds(pl.multiple_of(place, 64), rows)] = value
            matrix = lax.div(jnp.asarray(place, jnp.int32), width)
            row = place - matrix * width
            chunk = (lax.div(matrix, 2) + (words_ref[2] + side) * pairs) % chunks
            column = pl.multiple_of(chunk * width, width)
            source = held.at[slot, :rows]
            to_expand = pltpu.make_async_copy(
                source,
                expand_ref.at[pl.ds(pl.multiple_of(row, 64), rows), pl.ds(column, width)],
                sems.at[slot],
            )
            to_reduce = pltpu.make_async_copy(
                source,
                reduce_ref.at[pl.ds(pl.multiple_of(column + row, 64), rows)],
                sems.at[slot],
            )
            is_expand = lax.rem(matrix, 2) == 0
            pl.when(is_expand)(to_expand.start)
            pl.when(jnp.logical_not(is_expand))(to_reduce.start)
            copies.append(to_reduce)
        for at, distance in extras:
            rows = shard(words_ref[0] ^ distance, plan.a_more, plan.rows_a)
            joined_refs[0][rows] = ins[at][ins[at].shape[0] - plan.a_more :]
        for copy in copies:
            copy.wait()

    vmem = pl.BlockSpec(memory_space=pltpu.VMEM)
    anywhere = pl.BlockSpec(memory_space=pl.ANY)
    first = 1 + len(arrays)
    shapes = [
        jax.ShapeDtypeStruct((width, hidden), F32),
        jax.ShapeDtypeStruct((hidden, width), F32),
    ]
    if joins:
        shapes.append(jax.ShapeDtypeStruct((plan.rows_a + plan.more, width), BF16))
    return pl.pallas_call(
        kernel,
        in_specs=[pl.BlockSpec(memory_space=pltpu.SMEM)]
        + [vmem] * len(arrays)
        + [anywhere] * len(before),
        out_specs=[anywhere] * 2 + [vmem] * joins,
        out_shape=shapes,
        scratch_shapes=[
            pltpu.VMEM((len(segments), share, width), F32),
            pltpu.SemaphoreType.DMA((len(segments),)),
        ],
        input_output_aliases={first: 0, first + 1: 1} if before else {},
        compiler_params=pltpu.CompilerParams(vmem_limit_bytes=VMEM_LIMIT),
        cost_estimate=pl.CostEstimate(
            flops=0, bytes_accessed=3 * hidden * width, transcendentals=0
        ),
        name="widen",
    )(words, *arrays, *before)


def finished(words, plan, pieces, more, side, before=()):
    count = plan.count
    span = plan.span
    width = plan.width
    half_rows = width // 2
    heads = [
        (distance, base, min(2 * span - base, item.shape[0]), item)
        for distance, base, item in pieces
        if base < 2 * span
    ]

    def kernel(words_ref, *refs):
        heads_refs, refs = refs[: len(heads)], refs[len(heads) :]
        extra_ref, refs = refs[0], refs[1 + len(before) :]
        outs, refs = refs[:5], refs[5:]
        gathered, wide, project, sems = refs
        rank = words_ref[0]
        half = words_ref[2] ^ side
        for ref, (distance, base, rows, _) in zip(heads_refs, heads):
            place = pl.multiple_of((rank ^ distance) * span, HEAD_DIM)
            for part in range(2):
                low, high = max(base, part * span), min(base + rows, (part + 1) * span)
                if low < high:
                    gathered[part, pl.ds(place + (low - part * span), high - low)] = ref[
                        low - base : high - base
                    ]
        for part in range(2):
            wide[part] = gathered[part, :width].astype(F32).T
        project[...] = extra_ref[:half_rows].astype(F32)

        @pl.when(half == 1)
        def _():
            wide[1] = entry_order(wide[1])

        def copy(source, target, at):
            return pltpu.make_async_copy(source, target, sems.at[at])

        for part in range(2):
            pl.when(half == 0)(copy(wide.at[part], outs[part], part).start)
            pl.when(half == 1)(copy(wide.at[part], outs[2 + part], part).start)
        rows = pl.ds(pl.multiple_of(half * half_rows, half_rows), half_rows)
        last = copy(project, outs[4].at[rows], 2)
        last.start()
        for part in range(2):
            copy(wide.at[part], outs[part], part).wait()
        last.wait()

    anywhere = pl.BlockSpec(memory_space=pl.ANY)
    first = 2 + len(heads)
    shapes = [jax.ShapeDtypeStruct((width, width), F32)] * 5
    return pl.pallas_call(
        kernel,
        grid=(1,),
        in_specs=[pl.BlockSpec(memory_space=pltpu.SMEM)]
        + [pl.BlockSpec((rows, width), lambda s: (0, 0)) for _, _, rows, _ in heads]
        + [pl.BlockSpec((plan.more, width), lambda s: (plan.rows_a // plan.more, 0))]
        + [anywhere] * len(before),
        out_specs=[anywhere] * 5,
        out_shape=shapes,
        scratch_shapes=[
            pltpu.VMEM((2, count * span, width), BF16),
            pltpu.VMEM((2, width, width), F32),
            pltpu.VMEM((half_rows, width), F32),
            pltpu.SemaphoreType.DMA((3,)),
        ],
        input_output_aliases={first + at: at for at in range(len(before))},
        compiler_params=pltpu.CompilerParams(vmem_limit_bytes=VMEM_LIMIT),
        cost_estimate=pl.CostEstimate(
            flops=0, bytes_accessed=16 * width * width, transcendentals=0
        ),
        name="finish",
    )(words, *[item for *_, item in heads], more, *before)


def per_device(
    tokens,
    boxes,
    w_query,
    w_key,
    w_value,
    w_output,
    box_weight,
    first_gain,
    first_shift,
    w_expand,
    w_reduce,
    second_gain,
    second_shift,
    cotangent,
):
    pages, block, width = tokens.shape
    count = lax.axis_size("blk")
    depth = lax.axis_size("depth")
    words = jnp.stack(
        [lax.axis_index("blk"), lax.axis_index("depth"), lax.axis_index("core")]
    ).astype(jnp.int32)
    hidden = w_expand.shape[1]
    span = -(-HEADS // count) * HEAD_DIM
    unit = 16 * count * depth
    more = -(-(width // 2 + 16) // unit) * unit

    own_places = jnp.stack([boxes[0] + boxes[2], boxes[1] + boxes[3]], axis=1)
    own_places = jnp.stack([lax.shift_right_logical(own_places, 6), own_places & 63], axis=2)
    own_places = own_places.reshape(4 * pages, block).astype(BF16)
    own_places = jnp.pad(own_places, ((0, 16 - 4 * pages), (0, width - block)))
    message = jnp.concatenate([tokens[0], own_places])
    messages = [from_blk(message, i) for i in range(count)]
    w_own, box_own, rot_cos, rot_sin = prepare(
        words, w_query, w_key, w_value, box_weight, span, count * block
    )
    messages, rot_cos = lax.optimization_barrier((messages, rot_cos))
    own = after(messages, tokens[1])
    pieces = [messages, [from_blk(own, i) for i in range(count)]]

    saved = []
    att_parts = []
    for page in range(pages):
        results = attention_forward(
            words, page, messages, pieces[page], w_own, box_own, rot_cos, rot_sin
        )
        saved.append(results[:6])
        att_parts += [from_blk(results[6 + i], i) for i in range(count)]

    vectors = jnp.stack([first_gain, first_shift, second_gain, second_shift])
    results = middle(
        words,
        att_parts,
        tokens.reshape(pages * block, width),
        cotangent.reshape(pages * block, width),
        w_output,
        vectors,
        w_expand,
        w_reduce,
        pages,
        more,
    )
    layer_out, first_in, theirs, mine, more_theirs, more_mine = results[:6]
    grads = [from_blk(results[6 + i], i) for i in range(count)]
    plan = Plan(hidden, hidden - hidden // 2 // unit * unit, more, span, width)
    parts_a, keep_b, other_b = plan.scatter_one(
        after(grads, words), [mine, from_core(theirs), more_mine, from_core(more_theirs)]
    )

    def backward(page, words, before=None):
        return attention_backward(
            words,
            page,
            grads,
            pieces[page],
            saved[page],
            box_own,
            rot_cos,
            rot_sin,
            before,
        )

    *pre_one, before = backward(0, after(parts_a[0], words))
    part_a, other_a, keep_b, other_b = plan.scatter_two(
        after(before, words), parts_a, keep_b, other_b
    )
    done = part_a
    for level in range(2, plan.levels):
        keep_b, send_b = halve(after(done, words), level, keep_b, other_b)
        other_b = across(send_b, level)
        done = keep_b
    pre_one = [from_blk(item, i) for i, item in enumerate(after(part_a, pre_one))]
    *pre_two, heads_mine, heads_theirs = backward(1, after(done, words), before)

    part_a, parts_b = plan.scatter_three(
        after((heads_mine, pre_one), words), part_a, other_a, keep_b, other_b
    )
    heads, other = halve(
        after(part_a, words), 0, heads_mine, from_core(after(part_a, heads_theirs))
    )
    other = across(other, 0)
    pre_two = [from_blk(item, i) for i, item in enumerate(after(heads, pre_two))]
    both = plan.pack(words, heads, other, parts_b)
    done = (both, pre_two)
    for level in range(1, plan.levels):
        part_a = pair_sum(after(done, words), part_a, across(part_a, level))
        done = part_a
    level = plan.levels - 1
    other = across(after(part_a, both), level)
    other_a = across(part_a, 0)
    while level:
        both = plan.step(words, level, both, other)
        level -= 1
        other = across(both, level)
    part_a = join_halves(after(both, words), 0, part_a, other_a)
    pieces_a, sent = gather_blk(part_a, plan.a // 2)
    both = plan.step(after((pieces_a[1][2], sent), words), 0, both, other)
    *wide, joined = widened(after(both, words), plan, pieces_a, 0, 0, hidden)
    input_grad = input_gradient(
        after(joined, words), [pre_one, pre_two], (w_query, w_key, w_value), first_in
    )
    pieces, sent = gather_blk(both, 2 * span, (joined, input_grad))
    joined_other = from_core(after(pieces[1][2], joined))
    wide = widened(
        after(sent, words), plan, [(None, 0, joined_other)], 0, 1, hidden, wide
    )
    at = plan.rows_a + width // 2
    sums = jnp.where(words[2] == 0, joined[at : at + 4], joined_other[at : at + 4])
    sums = [sums[i].astype(F32) for i in range(4)]
    arrays = after((wide, sums), [item for _, _, item in pieces])
    pieces = [(distance, base, item) for (distance, base, _), item in zip(pieces, arrays)]
    others = with_core(pieces)
    wide = widened(words, plan, pieces, 1, 0, hidden, wide)
    grads = finished(after(wide, words), plan, pieces, joined, 0)
    grad_expand, grad_reduce = widened(
        after(grads, words), plan, others, 1, 1, hidden, wide
    )
    grad_query, grad_key, grad_value, grad_box, grad_project = finished(
        after(grad_expand, words), plan, others, joined_other, 1, grads
    )
    return (
        layer_out.reshape(tokens.shape),
        input_grad.reshape(tokens.shape),
        grad_query,
        grad_key,
        grad_value,
        grad_project,
        grad_box,
        sums[0],
        sums[1],
        grad_expand,
        grad_reduce,
        sums[2],
        sums[3],
    )


def solution(mesh):
    blocks, rest = mesh.devices.shape
    parts = jax.sharding.Mesh(
        mesh.devices.reshape(blocks, rest // 2, 2), ("blk", "depth", "core")
    )
    split = P(("depth", "core"), "blk", None)
    return jax.shard_map(
        per_device,
        mesh=parts,
        in_specs=(split, P(None, ("depth", "core"), "blk")) + (P(),) * 11 + (split,),
        out_specs=(split, split) + (P(),) * 11,
        check_vma=False,
    )
```

```python
import functools

import jax
import jax.numpy as jnp
import numpy as np
from jax import lax
from jax.experimental import pallas as pl
from jax.experimental.pallas import tpu as pltpu
from jax.sharding import PartitionSpec as P

HEADS = 12
HEAD_DIM = 64
HALF = 32
FREQS = 192
CODES = 4 * FREQS
VMEM_LIMIT = 60 * 1024 * 1024
NO_COST = pl.CostEstimate(flops=0, bytes_accessed=0, transcendentals=0)
F32 = jnp.float32
BF16 = jnp.bfloat16


def dot(left, right):
    return lax.dot_general(left, right, (((1,), (0,)), ((), ())), preferred_element_type=F32)


def dot_nt(left, right):
    return lax.dot_general(left, right, (((1,), (1,)), ((), ())), preferred_element_type=F32)


def dot_tn(left, right):
    return lax.dot_general(left, right, (((0,), (0,)), ((), ())), preferred_element_type=F32)


def swapped(block, distance, axis="blk"):
    count = lax.axis_size(axis)
    return lax.ppermute(block, axis, [(i, i ^ distance) for i in range(count)])


def from_blk(block, distance):
    return swapped(block, distance) if distance else block


def from_core(block):
    return swapped(block, 1, "core")


def after(done, value):
    return lax.optimization_barrier((value, done))[0]


def turned(upper, lower, cosines, sines):
    return upper * cosines - lower * sines, lower * cosines + upper * sines


def entry_order(rows):
    return jnp.concatenate(
        [
            rows[:FREQS],
            rows[2 * FREQS : 3 * FREQS],
            rows[FREQS : 2 * FREQS],
            rows[3 * FREQS :],
        ],
        axis=0,
    )


def angle_tables():
    rates = np.float32(10000.0) ** (-np.arange(FREQS, dtype=np.float32) / np.float32(FREQS))
    tables = []
    for places in (32.0 * np.arange(32), 0.5 * np.arange(64)):
        angles = rates.astype(np.float64)[:, None] * places[None, :]
        left = np.concatenate([np.sin(angles), np.cos(angles)])
        parts = []
        for _ in range(3):
            parts.append(left.astype(jnp.bfloat16))
            left = left - parts[-1].astype(np.float64)
        tables.append(np.concatenate(parts, axis=1))
    return tables


def rotary_tables(length):
    rates = np.float32(10000.0) ** (-np.arange(HALF, dtype=np.float32) / np.float32(HALF))
    angles = np.arange(length, dtype=np.float32)[None, :] * rates[:, None]
    angles = angles.astype(np.float64)
    return np.cos(angles).astype(np.float32), np.sin(angles).astype(np.float32)


def prepare_kernel(
    words_ref,
    query_ref,
    key_ref,
    value_ref,
    box_ref,
    cos_ref,
    sin_ref,
    own_ref,
    own_box_ref,
    own_cos_ref,
    own_sin_ref,
):
    rank = words_ref[0]
    span = own_box_ref.shape[0]
    width = query_ref.shape[1]
    count = lax.axis_size("blk")
    block = cos_ref.shape[1] // count
    row = lax.broadcasted_iota(jnp.int32, (span, width), 0) + rank * span
    column = lax.broadcasted_iota(jnp.int32, (span, width), 1)
    pick = jnp.where(row == column, 1.0, 0.0).astype(BF16)
    for kind, ref in enumerate((query_ref, key_ref, value_ref)):
        own_ref[kind * span : (kind + 1) * span] = dot_nt(pick, ref[...]).astype(BF16)
    own_box_ref[...] = dot_nt(pick, entry_order(box_ref[...])).astype(BF16)
    for i in range(count):
        from_cols = pl.ds(pl.multiple_of((rank ^ i) * block, block), block)
        own_cos_ref[:, i * block : (i + 1) * block] = cos_ref[:, from_cols]
        own_sin_ref[:, i * block : (i + 1) * block] = sin_ref[:, from_cols]


def prepare(words, w_query, w_key, w_value, box_weight, span, length):
    width = w_query.shape[0]
    vmem = pl.BlockSpec(memory_space=pltpu.VMEM)
    return pl.pallas_call(
        prepare_kernel,
        in_specs=[pl.BlockSpec(memory_space=pltpu.SMEM)] + [vmem] * 6,
        out_specs=[vmem] * 4,
        out_shape=[
            jax.ShapeDtypeStruct((3 * span, width), BF16),
            jax.ShapeDtypeStruct((span, CODES), BF16),
            jax.ShapeDtypeStruct((HALF, length), F32),
            jax.ShapeDtypeStruct((HALF, length), F32),
        ],
        compiler_params=pltpu.CompilerParams(vmem_limit_bytes=VMEM_LIMIT),
        cost_estimate=pl.CostEstimate(
            flops=8 * span * width * width, bytes_accessed=10 * width * width, transcendentals=0
        ),
        name="prepare",
    )(words, w_query, w_key, w_value, box_weight, *map(jnp.asarray, rotary_tables(length)))


def fold(value, combine):
    while value.shape[0] > 8:
        half = value.shape[0] // 2
        value = combine(value[:half], value[half:])
    return value


def write_codes(page, place_refs, high_ref, low_ref, sin_ref, cos_ref, codes_ref):
    block = sin_ref.shape[1] // len(place_refs)

    def looked_up(table_ref, index):
        spots = table_ref.shape[1] // 3
        rows = lax.broadcasted_iota(jnp.int32, (spots, block), 0).astype(F32)
        once = jnp.where(rows == index, 1.0, 0.0)
        found = dot(table_ref[...], jnp.concatenate([once] * 3, axis=0).astype(BF16))
        return found[:FREQS], found[FREQS:]

    for i, place_ref in enumerate(place_refs):
        columns = slice(i * block, (i + 1) * block)
        places = place_ref[:, :block].astype(F32)
        for axis in range(2):
            at = 4 * page + 2 * axis
            high_sin, high_cos = looked_up(high_ref, places[at : at + 1])
            low_sin, low_cos = looked_up(low_ref, places[at + 1 : at + 2])
            sines = high_sin * low_cos + high_cos * low_sin
            cosines = high_cos * low_cos - high_sin * low_sin
            rows = slice(axis * FREQS, (axis + 1) * FREQS)
            later = slice((2 + axis) * FREQS, (3 + axis) * FREQS)
            sin_ref[rows, columns] = sines
            cos_ref[rows, columns] = cosines
            codes_ref[rows, columns] = sines.astype(BF16)
            codes_ref[later, columns] = cosines.astype(BF16)


def forward_kernel(page, count, words_ref, *refs):
    place_refs, refs = refs[:count], refs[count:]
    piece_refs, refs = refs[:count], refs[count:]
    high_ref, low_ref, w_ref, box_ref, rot_cos_ref, rot_sin_ref = refs[:6]
    probs_ref, att_ref, heads_ref, sin_ref, cos_ref, codes_ref = refs[6:12]
    low_refs = refs[12 : 12 + count]
    tok_ref, pre_ref, kc_ref, qr_ref = refs[12 + count :]
    rows = tok_ref.shape[0]
    block = rows // count
    head = pl.program_id(0)
    span = pl.num_programs(0) * HEAD_DIM

    @pl.when(head == 0)
    def _():
        for i in range(count):
            tok_ref[i * block : (i + 1) * block] = piece_refs[i][...]
        pre_ref[...] = dot_nt(w_ref[...], tok_ref[...])
        write_codes(page, place_refs, high_ref, low_ref, sin_ref, cos_ref, codes_ref)
        kc_ref[:, :CODES] = codes_ref[...].astype(F32).T.astype(BF16)

    def pre(kind):
        at = kind * span + head * HEAD_DIM
        return pre_ref[pl.ds(pl.multiple_of(at, HEAD_DIM), HEAD_DIM)]

    rot_cos = rot_cos_ref[...]
    rot_sin = rot_sin_ref[...]
    query_pre = pre(0).astype(BF16)
    wide = query_pre.astype(F32)
    query = jnp.concatenate(turned(wide[:HALF], wide[HALF:], rot_cos, rot_sin), axis=0)
    key_pre = pre(1)
    key = jnp.concatenate(turned(key_pre[:HALF], key_pre[HALF:], rot_cos, rot_sin), axis=0)
    value = pre(2).astype(BF16)
    heads_ref[0, :HEAD_DIM] = query_pre
    heads_ref[0, HEAD_DIM : 2 * HEAD_DIM] = query.astype(BF16)
    heads_ref[0, 2 * HEAD_DIM : 3 * HEAD_DIM] = key.astype(BF16)
    heads_ref[0, 3 * HEAD_DIM :] = value
    kc_ref[:, CODES:] = key.T.astype(BF16)
    qr_ref[CODES:] = (query * 0.125).astype(BF16)
    step = min(256, block)

    def logits_at(at):
        part = slice(at, at + step)
        projected = dot_tn(box_ref[...], query_pre[:, part])
        sines = sin_ref[:, part]
        cosines = cos_ref[:, part]
        upper = projected[: 2 * FREQS]
        lower = projected[2 * FREQS :]
        qr_ref[: 2 * FREQS, part] = ((upper * cosines + lower * sines) * 0.125).astype(BF16)
        qr_ref[2 * FREQS : CODES, part] = ((lower * cosines - upper * sines) * 0.125).astype(BF16)
        return dot(kc_ref[...], qr_ref[:, part])

    following = logits_at(0)
    for at in range(0, rows, step):
        logits = following
        if at + step < rows:
            following = logits_at(at + step)
        peak = jnp.max(fold(logits, jnp.maximum), axis=0, keepdims=True)
        weight = jnp.exp(logits - peak)
        total = jnp.sum(fold(weight, jnp.add), axis=0, keepdims=True)
        probs = (weight * (1.0 / total)).astype(BF16)
        probs_ref[0, :, at : at + step] = probs
        attended = dot(value, probs)
        att_ref[0, :, at : at + step] = attended
        inner = at % block
        low_refs[at // block][:, inner : inner + step] = attended.astype(BF16)


def fixed(array):
    return pl.BlockSpec(array.shape, lambda *at: (0,) * len(array.shape))


def attention_forward(words, page, messages, pieces, w_own, box_own, rot_cos, rot_sin):
    count = len(messages)
    block, width = messages[0].shape[0] - 16, messages[0].shape[1]
    rows = count * block
    span = box_own.shape[0]
    heads = span // HEAD_DIM
    tables = [jnp.asarray(item) for item in angle_tables()]
    specs = [pl.BlockSpec((block, width), lambda h, words: (0, 0))] * count
    places = pl.BlockSpec((16, width), lambda h, words: (block // 16, 0))
    out_shape = [
        jax.ShapeDtypeStruct((heads, rows, rows), BF16),
        jax.ShapeDtypeStruct((heads, HEAD_DIM, rows), F32),
        jax.ShapeDtypeStruct((heads, 4 * HEAD_DIM, rows), BF16),
        jax.ShapeDtypeStruct((2 * FREQS, rows), F32),
        jax.ShapeDtypeStruct((2 * FREQS, rows), F32),
        jax.ShapeDtypeStruct((CODES, rows), BF16),
    ] + [jax.ShapeDtypeStruct((span, block), BF16)] * count
    return pl.pallas_call(
        functools.partial(forward_kernel, page, count),
        grid_spec=pltpu.PrefetchScalarGridSpec(
            num_scalar_prefetch=1,
            grid=(heads,),
            in_specs=[places] * count
            + specs
            + [fixed(item) for item in (*tables, w_own)]
            + [
                pl.BlockSpec((HEAD_DIM, CODES), lambda h, words: (h, 0)),
                fixed(rot_cos),
                fixed(rot_sin),
            ],
            out_specs=[
                pl.BlockSpec((1, rows, rows), lambda h, words: (h, 0, 0)),
                pl.BlockSpec((1, HEAD_DIM, rows), lambda h, words: (h, 0, 0)),
                pl.BlockSpec((1, 4 * HEAD_DIM, rows), lambda h, words: (h, 0, 0)),
            ]
            + [fixed(item) for item in out_shape[3:6]]
            + [pl.BlockSpec((HEAD_DIM, block), lambda h, words: (h, 0))] * count,
            scratch_shapes=[
                pltpu.VMEM((rows, width), BF16),
                pltpu.VMEM((3 * span, rows), F32),
                pltpu.VMEM((rows, CODES + HEAD_DIM), BF16),
                pltpu.VMEM((CODES + HEAD_DIM, rows), BF16),
            ],
        ),
        out_shape=out_shape,
        compiler_params=pltpu.CompilerParams(vmem_limit_bytes=VMEM_LIMIT),
        cost_estimate=pl.CostEstimate(
            flops=2 * heads * rows * (rows * 1100 + 200 * width + 64 * CODES),
            bytes_accessed=2 * heads * rows * rows + 12 * rows * width,
            transcendentals=heads * rows * rows,
        ),
        name="attention_forward",
    )(words, *messages, *pieces, *tables, w_own, box_own, rot_cos, rot_sin)


def backward_kernel(count, last, words_ref, *refs):
    grad_refs, refs = refs[:count], refs[count:]
    piece_refs, refs = refs[:count], refs[count:]
    probs_ref, att_ref, heads_ref, box_ref, codes_ref, sin_ref, cos_ref = refs[:7]
    rot_cos_ref, rot_sin_ref = refs[7:9]
    refs = refs[9:]
    if last:
        before_ref, refs = refs[0], refs[1:]
    pre_refs, refs = refs[:count], refs[count:]
    if last:
        mine_ref, theirs_ref, *refs = refs
    weight_grad_ref, kc_ref, logit_grad_ref, entry_grad_ref, turned_ref = refs
    block, width = piece_refs[0].shape
    rows = count * block
    head = pl.program_id(0)
    span = pl.num_programs(0) * HEAD_DIM

    @pl.when(head == 0)
    def _():
        kc_ref[:CODES] = codes_ref[...]

    kc_ref[CODES:] = heads_ref[0, 2 * HEAD_DIM : 3 * HEAD_DIM]
    packed = heads_ref[0].astype(F32).T.astype(BF16)
    query_pre = packed[:, :HEAD_DIM]
    query = packed[:, HEAD_DIM : 2 * HEAD_DIM]
    value = packed[:, 3 * HEAD_DIM :] * jnp.asarray(0.125, BF16)
    rot_cos = rot_cos_ref[...]
    rot_sin = rot_sin_ref[...]
    grad = jnp.concatenate([ref[...] for ref in grad_refs], axis=1)
    grad_tall = grad.astype(F32).T.astype(BF16)
    offsets = jnp.sum(grad.astype(F32) * att_ref[0], axis=0, keepdims=True) * 0.125
    step = min(256, block)
    place = pl.multiple_of(head * HEAD_DIM, HEAD_DIM)
    here = pl.ds(place, HEAD_DIM)

    def logits_back(at):
        part = slice(at, at + step)
        grad_probs = dot(value, grad[:, part])
        logit_grad_ref[:, part] = (
            probs_ref[0, :, part].astype(F32) * (grad_probs - offsets[:, part])
        ).astype(BF16)

    logits_back(0)
    for at in range(0, rows, step):
        if at + step < rows:
            logits_back(at + step)
        part = slice(at, at + step)
        back = dot(kc_ref[...], logit_grad_ref[:, part])
        sines = sin_ref[:, part]
        cosines = cos_ref[:, part]
        upper = back[: 2 * FREQS]
        lower = back[2 * FREQS : CODES]
        entry_grad_ref[: 2 * FREQS, part] = (upper * cosines - lower * sines).astype(BF16)
        entry_grad_ref[2 * FREQS :, part] = (lower * cosines + upper * sines).astype(BF16)
        first = back[CODES : CODES + HALF]
        second = back[CODES + HALF :]
        turned_ref[:HALF, part], turned_ref[HALF:, part] = turned(
            first, second, rot_cos[:, part], -rot_sin[:, part]
        )
    key_flat = dot(logit_grad_ref[...], query).T
    value_low = dot(probs_ref[0], grad_tall).T.astype(BF16)
    query_low = (turned_ref[...] + dot(box_ref[...], entry_grad_ref[...])).astype(BF16)
    key_low = jnp.concatenate(
        turned(key_flat[:HALF], key_flat[HALF:], rot_cos, -rot_sin), axis=0
    ).astype(BF16)
    for i in range(count):
        columns = slice(i * block, (i + 1) * block)
        pre_refs[i][here, :block] = query_low[:, columns]
        pre_refs[i][here, block : 2 * block] = key_low[:, columns]
        pre_refs[i][here, 2 * block :] = value_low[:, columns]
    weight_grad_ref[pl.ds(3 * span + place, HEAD_DIM)] = dot(entry_grad_ref[...], query_pre).T

    @pl.when(head == pl.num_programs(0) - 1)
    def _():
        for kind in range(3):
            columns = slice(kind * block, (kind + 1) * block)
            total = dot(pre_refs[0][:, columns], piece_refs[0][...])
            for i in range(1, count):
                total = total + dot(pre_refs[i][:, columns], piece_refs[i][...])
            weight_grad_ref[kind * span : (kind + 1) * span] = total
        if last:
            half = 2 * span
            core = words_ref[2]
            ours = pl.ds(pl.multiple_of(core * half, half), half)
            there = pl.ds(pl.multiple_of((1 - core) * half, half), half)
            mine_ref[...] = weight_grad_ref[ours] + before_ref[ours]
            theirs_ref[...] = (weight_grad_ref[there] + before_ref[there]).astype(BF16)


def attention_backward(
    words, page, grads, pieces, saved, box_own, rot_cos, rot_sin, before=None
):
    probs, att, heads_saved, sines, cosines, codes = saved
    count = len(pieces)
    rows, width = probs.shape[1], pieces[0].shape[1]
    block = rows // count
    span = box_own.shape[0]
    heads = span // HEAD_DIM
    last = before is not None
    extra = (before,) if last else ()
    full_shape = (4 * span, width)
    specs = [pl.BlockSpec((block, width), lambda h, words: (0, 0))] * count
    out_shape = [jax.ShapeDtypeStruct((span, 3 * block), BF16)] * count
    if last:
        out_shape += [
            jax.ShapeDtypeStruct((2 * span, width), F32),
            jax.ShapeDtypeStruct((2 * span, width), BF16),
        ]
    else:
        out_shape.append(jax.ShapeDtypeStruct(full_shape, F32))
    return pl.pallas_call(
        functools.partial(backward_kernel, count, last),
        grid_spec=pltpu.PrefetchScalarGridSpec(
            num_scalar_prefetch=1,
            grid=(heads,),
            in_specs=[pl.BlockSpec((HEAD_DIM, block), lambda h, words: (h, page))] * count
            + specs
            + [
                pl.BlockSpec((1, rows, rows), lambda h, words: (h, 0, 0)),
                pl.BlockSpec((1, HEAD_DIM, rows), lambda h, words: (h, 0, 0)),
                pl.BlockSpec((1, 4 * HEAD_DIM, rows), lambda h, words: (h, 0, 0)),
                pl.BlockSpec((HEAD_DIM, CODES), lambda h, words: (h, 0)),
            ]
            + [fixed(item) for item in (codes, sines, cosines, rot_cos, rot_sin, *extra)],
            out_specs=[fixed(item) for item in out_shape],
            scratch_shapes=([pltpu.VMEM(full_shape, F32)] if last else [])
            + [
                pltpu.VMEM((CODES + HEAD_DIM, rows), BF16),
                pltpu.VMEM((rows, rows), BF16),
                pltpu.VMEM((CODES, rows), BF16),
                pltpu.VMEM((HEAD_DIM, rows), F32),
            ],
        ),
        out_shape=out_shape,
        compiler_params=pltpu.CompilerParams(vmem_limit_bytes=VMEM_LIMIT),
        cost_estimate=pl.CostEstimate(
            flops=2 * heads * rows * (rows * 1400 + 200 * width + 128 * CODES),
            bytes_accessed=2 * heads * rows * rows + 12 * rows * width,
            transcendentals=0,
        ),
        name="attention_backward",
    )(
        words,
        *grads,
        *pieces,
        probs,
        att,
        heads_saved,
        box_own,
        codes,
        sines,
        cosines,
        rot_cos,
        rot_sin,
        *extra,
    )


def normed(value):
    centered = value - jnp.mean(value, axis=-1, keepdims=True)
    scale = lax.rsqrt(jnp.mean(centered * centered, axis=-1, keepdims=True) + 1e-05)
    return centered * scale, scale


def norm_back(grad, gain, unit, scale):
    scaled = grad * gain
    return scale * (
        scaled
        - jnp.mean(scaled, axis=-1, keepdims=True)
        - unit * jnp.mean(scaled * unit, axis=-1, keepdims=True)
    )


def column_sum(value):
    return jnp.sum(value, axis=0, keepdims=True)


def middle_kernel(pages, count, span, chunks, *refs):
    total = pages * count
    words_ref = refs[0]
    att_refs = refs[1 : 1 + total]
    (
        tok_ref,
        cot_ref,
        w_out_ref,
        vectors_ref,
        w_expand_ref,
        w_reduce_ref,
    ) = refs[1 + total : 7 + total]
    outs = refs[7 + total :]
    layer_ref, first_in_ref, theirs_ref, mine_ref, more_theirs_ref, more_mine_ref = outs[:6]
    grad_refs = outs[6 : 6 + count]
    (
        sums_ref,
        att_all,
        grad_all,
        unit_one,
        scale_one,
        first_wide,
        first_low,
        first_tall,
        active,
        slope,
        gathered,
        second_low,
    ) = outs[6 + count :]
    rank = words_ref[0]
    width = tok_ref.shape[1]
    block = tok_ref.shape[0] // pages
    half = tok_ref.shape[0] // 2
    step = pl.program_id(0)

    def rows_of(at):
        return pl.ds(pl.multiple_of((rank ^ at) * span, span), span)

    @pl.when(step == 0)
    def _():
        for page in range(pages):
            for at in range(count):
                att_all[rows_of(at), page * block : (page + 1) * block] = att_refs[
                    page * count + at
                ][...]
        branch = dot_tn(att_all[: w_out_ref.shape[0]], w_out_ref[...])
        unit, scale = normed(tok_ref[...].astype(F32) + branch)
        unit_one[...] = unit
        scale_one[...] = jnp.broadcast_to(scale, scale_one.shape)
        first_out = unit * vectors_ref[0:1] + vectors_ref[1:2]
        first_wide[...] = first_out
        first_low[...] = first_out.astype(BF16)
        first_tall[...] = first_out.T.astype(BF16)
        gathered[...] = jnp.zeros_like(gathered)
        sums_ref[...] = jnp.zeros_like(sums_ref)

    for chunk in range(chunks):

        @pl.when(step == chunk)
        def _(chunk=chunk):
            halves = [slice(at, at + half) for at in range(0, 2 * half, half)]
            expanded = [dot(first_low[rows], w_expand_ref[...]) for rows in halves]
            for rows, value in zip(halves, expanded):
                gate = 0.5 + 0.5 * lax.erf(value * np.float32(np.sqrt(0.5)))
                bell = jnp.exp(value * value * -0.5) * np.float32(1.0 / np.sqrt(2.0 * np.pi))
                low = (value * gate).astype(BF16)
                active[chunk, rows] = low
                slope[chunk, rows] = gate + value * bell
                gathered[rows] += dot(low, w_reduce_ref[...])

    @pl.when(step == chunks - 1)
    def _():
        unit, scale = normed(first_wide[...] + gathered[...])
        layer_ref[...] = (unit * vectors_ref[2:3] + vectors_ref[3:4]).astype(BF16)
        cot = cot_ref[...].astype(F32)
        sums_ref[2:3] = column_sum(cot * unit)
        sums_ref[3:4] = column_sum(cot)
        grad = norm_back(cot, vectors_ref[2:3], unit, scale)
        second_low[...] = grad.astype(BF16)
        gathered[...] = grad

    for chunk in range(chunks):

        @pl.when(step == 2 * chunks - 1 - chunk)
        def _(chunk=chunk):
            grads_ref = mine_ref if chunk < chunks // 2 else theirs_ref
            halves = [slice(at, at + half) for at in range(0, 2 * half, half)]
            grad_active = [dot_nt(second_low[rows], w_reduce_ref[...]) for rows in halves]
            grads_ref[width:] = dot_tn(active[chunk], second_low[...]).astype(BF16)
            for rows, value in zip(halves, grad_active):
                low = (value * slope[chunk, rows]).astype(BF16)
                active[chunk, rows] = low
                gathered[rows] += dot_nt(low, w_expand_ref[...])
            grads_ref[:width] = dot(first_tall[...], active[chunk]).astype(BF16)

    @pl.when(step == 2 * chunks - 1)
    def _():
        unit = unit_one[...]
        grad_out = gathered[...]
        sums_ref[0:1] = column_sum(grad_out * unit)
        sums_ref[1:2] = column_sum(grad_out)
        grad = norm_back(grad_out, vectors_ref[0:1], unit, scale_one[:, :1])
        first_in_ref[...] = grad
        low = grad.astype(BF16)
        real = w_out_ref.shape[0]
        half = real // 2
        core = words_ref[2]
        for ref, side in ((more_mine_ref, core), (more_theirs_ref, 1 - core)):
            rows = pl.ds(pl.multiple_of(side * half, half), half)
            ref[:half] = dot(att_all[rows], low).astype(BF16)
            ref[half:] = jnp.zeros((ref.shape[0] - half, width), BF16)
            ref[half : half + 16] = sums_ref[...].astype(BF16)
        if grad_all.shape[0] > real:
            grad_all[real:] = jnp.zeros((grad_all.shape[0] - real, low.shape[0]), BF16)
        grad_all[:real] = dot_nt(w_out_ref[...], low).astype(BF16)
        for at in range(count):
            grad_refs[at][...] = grad_all[rows_of(at)]


def middle(words, att_parts, tok, cot, w_out, vectors, w_expand, w_reduce, pages, more):
    rows, width = tok.shape
    count = len(att_parts) // pages
    span, block = att_parts[0].shape
    hidden = w_expand.shape[1]
    chunks = hidden // width
    pairs = chunks // 2

    def whole(array):
        return pl.BlockSpec(array.shape, lambda s, words: (0,) * len(array.shape))

    def chunk_at(s, words):
        at = jnp.minimum(s, 2 * chunks - 1 - s)
        return (at + words[2] * pairs) % chunks

    def theirs_at(s, words):
        return jnp.clip(2 * chunks - 1 - s - pairs, 0, pairs - 1), 0

    def mine_at(s, words):
        return jnp.clip(2 * chunks - 1 - s, 0, pairs - 1), 0

    shapes = [
        jax.ShapeDtypeStruct((rows, width), BF16),
        jax.ShapeDtypeStruct((rows, width), F32),
        jax.ShapeDtypeStruct((hidden, width), BF16),
        jax.ShapeDtypeStruct((hidden, width), BF16),
        jax.ShapeDtypeStruct((more, width), BF16),
        jax.ShapeDtypeStruct((more, width), BF16),
    ] + [jax.ShapeDtypeStruct((span, pages * block), BF16)] * count
    specs = [whole(item) for item in shapes]
    specs[2] = pl.BlockSpec((2 * width, width), theirs_at)
    specs[3] = pl.BlockSpec((2 * width, width), mine_at)
    return pl.pallas_call(
        functools.partial(middle_kernel, pages, count, span, chunks),
        grid_spec=pltpu.PrefetchScalarGridSpec(
            num_scalar_prefetch=1,
            grid=(2 * chunks,),
            in_specs=[whole(item) for item in att_parts]
            + [
                whole(tok),
                whole(cot),
                whole(w_out),
                whole(vectors),
                pl.BlockSpec((width, width), lambda s, words: (0, chunk_at(s, words))),
                pl.BlockSpec((width, width), lambda s, words: (chunk_at(s, words), 0)),
            ],
            out_specs=specs,
            scratch_shapes=[
                pltpu.VMEM((16, width), F32),
                pltpu.VMEM((count * span, rows), BF16),
                pltpu.VMEM((count * span, rows), BF16),
                pltpu.VMEM((rows, width), F32),
                pltpu.VMEM((rows, 128), F32),
                pltpu.VMEM((rows, width), F32),
                pltpu.VMEM((rows, width), BF16),
                pltpu.VMEM((width, rows), BF16),
                pltpu.VMEM((chunks, rows, width), BF16),
                pltpu.VMEM((chunks, rows, width), F32),
                pltpu.VMEM((rows, width), F32),
                pltpu.VMEM((rows, width), BF16),
            ],
        ),
        out_shape=shapes,
        compiler_params=pltpu.CompilerParams(vmem_limit_bytes=VMEM_LIMIT),
        cost_estimate=pl.CostEstimate(
            flops=2 * rows * width * (6 * hidden + 3 * width),
            bytes_accessed=8 * width * hidden + 16 * rows * width,
            transcendentals=2 * rows * hidden,
        ),
        name="middle",
    )(words, *att_parts, tok, cot, w_out, vectors, w_expand, w_reduce)


def input_kernel(pages, count, span, *refs):
    words_ref = refs[0]
    part_refs = refs[1 : 1 + pages * count]
    weight_refs = refs[1 + pages * count : 4 + pages * count]
    first_in_ref, out_ref, held = refs[4 + pages * count :]
    rank = words_ref[0]
    width = out_ref.shape[1]
    block = out_ref.shape[0] // pages
    for page in range(pages):
        for at in range(count):
            part = part_refs[page * count + at]
            place = pl.multiple_of((rank ^ at) * span, span)
            for kind in range(3):
                held[kind, pl.ds(place, span), page * block : (page + 1) * block] = part[
                    :, kind * block : (kind + 1) * block
                ]
    total = dot(weight_refs[0][...], held[0, :width])
    for kind in range(1, 3):
        total = total + dot(weight_refs[kind][...], held[kind, :width])
    out_ref[...] = (first_in_ref[...] + total.T).astype(BF16)


def input_gradient(words, parts, weights, first_in):
    pages, count = len(parts), len(parts[0])
    span = parts[0][0].shape[0]
    rows, width = first_in.shape
    vmem = pl.BlockSpec(memory_space=pltpu.VMEM)
    return pl.pallas_call(
        functools.partial(input_kernel, pages, count, span),
        in_specs=[pl.BlockSpec(memory_space=pltpu.SMEM)] + [vmem] * (pages * count + 4),
        out_specs=vmem,
        out_shape=jax.ShapeDtypeStruct((rows, width), BF16),
        scratch_shapes=[pltpu.VMEM((3, count * span, rows), BF16)],
        compiler_params=pltpu.CompilerParams(vmem_limit_bytes=VMEM_LIMIT),
        cost_estimate=pl.CostEstimate(
            flops=6 * rows * width * count * span,
            bytes_accessed=2 * width * (5 * rows + 3 * count * span),
            transcendentals=0,
        ),
        name="input_gradient",
    )(words, *[part for page in parts for part in page], *weights, first_in)


def local(body, name, words, arrays, shapes, costly=False):
    def kernel(words_ref, *refs):
        body(words_ref, refs[: len(arrays)], refs[len(arrays) :])

    vmem = pl.BlockSpec(memory_space=pltpu.VMEM)
    shapes = [jax.ShapeDtypeStruct(shape, kind) for shape, kind in shapes]
    moved = sum(item.size * item.dtype.itemsize for item in list(arrays) + shapes)
    cost = pl.CostEstimate(flops=0, bytes_accessed=moved, transcendentals=0)
    return pl.pallas_call(
        kernel,
        in_specs=[pl.BlockSpec(memory_space=pltpu.SMEM)] + [vmem] * len(arrays),
        out_specs=[vmem] * len(shapes),
        out_shape=shapes,
        compiler_params=pltpu.CompilerParams(vmem_limit_bytes=VMEM_LIMIT),
        cost_estimate=cost if costly else NO_COST,
        name=name,
    )(words, *arrays)


def shard(index, rows, base=0):
    return pl.ds(pl.multiple_of(base + index * rows, 16), rows)


def total_of(refs, rows=slice(None)):
    if len(refs) == 2 and all(ref.dtype == BF16 for ref in refs):
        return refs[0][rows] + refs[1][rows]
    total = refs[0][rows].astype(F32)
    for ref in refs[1:]:
        total = total + ref[rows].astype(F32)
    return total


def tree_sum(terms):
    while len(terms) > 1:
        terms = [terms[i] + terms[i + 1] for i in range(0, len(terms), 2)]
    return terms[0]


def bit_of(words, level):
    return lax.shift_right_logical(words[1], level) & 1


def pair_sum(words, mine, other):
    def body(words, ins, outs):
        outs[0][...] = total_of(ins).astype(BF16)

    return local(body, "pair_sum", words, [mine, other], [(mine.shape, BF16)])[0]


def halve(words, level, mine, other):
    *lead, rows, width = mine.shape
    half = rows // 2

    def body(words, ins, outs):
        bit = bit_of(words, level)
        for out, side in zip(outs, (bit, 1 - bit)):
            at = shard(side, half)
            out[...] = total_of(ins, (slice(None), at) if lead else at).astype(BF16)

    return local(body, "halve", words, [mine, other], [((*lead, half, width), BF16)] * 2)


def join_halves(words, level, mine, other):
    rows, width = mine.shape

    def body(words, ins, outs):
        bit = bit_of(words, level)
        outs[0][shard(bit, rows)] = ins[0][...]
        outs[0][shard(1 - bit, rows)] = ins[1][...]

    return local(body, "join_halves", words, [mine, other], [((2 * rows, width), BF16)])[0]


def across(block, level):
    return swapped(block, 1 << level, "depth")


class Plan:
    def __init__(self, rows, rows_a, more, span, width):
        self.count = lax.axis_size("blk")
        self.levels = lax.axis_size("depth").bit_length() - 1
        self.rows = rows
        self.rows_a = rows_a
        self.more = more
        self.span = span
        self.width = width
        self.a_ff = rows_a // self.count
        self.a_more = more // self.count
        self.a = self.a_ff + self.a_more
        self.b = (rows - rows_a) // self.count
        self.share = self.a + self.b
        assert width % self.a_ff == 0 and width % self.b == 0 and rows_a % self.b == 0

    def shapes(self, *sizes):
        return [((rows, self.width), BF16) for rows in sizes]

    def scatter_one(self, words, halves):
        count, width = self.count, self.width
        a_ff, half = self.a_ff, self.b // 2

        def kernel(words_ref, *refs):
            parts = refs[6 : 6 + count]
            keep_ref, send_ref = refs[6 + count :]
            for i in range(count):

                @pl.when(pl.program_id(0) == i)
                def _(i=i):
                    parts[i][:a_ff] = total_of(refs[:2]).astype(BF16)
                    parts[i][a_ff:] = total_of(refs[2:4]).astype(BF16)

            bit = bit_of(words_ref, 0)
            keep_ref[0] = total_of(refs[4:6], shard(bit, half)).astype(BF16)
            send_ref[0] = total_of(refs[4:6], shard(1 - bit, half)).astype(BF16)

        def there(rows):
            return pl.BlockSpec((rows, width), lambda i, words: (words[0] ^ i, 0))

        part_b = pl.BlockSpec((self.b, width), lambda i, words: (self.rows_a // self.b + i, 0))
        half_b = pl.BlockSpec((1, half, width), lambda i, words: (i, 0, 0))
        shapes = [jax.ShapeDtypeStruct((self.a, width), BF16)] * count
        shapes += [jax.ShapeDtypeStruct((count, half, width), BF16)] * 2
        *parts_a, keep, send = pl.pallas_call(
            kernel,
            grid_spec=pltpu.PrefetchScalarGridSpec(
                num_scalar_prefetch=1,
                grid=(count,),
                in_specs=[there(a_ff)] * 2 + [there(self.a_more)] * 2 + [part_b] * 2,
                out_specs=[fixed(item) for item in shapes[:count]] + [half_b] * 2,
            ),
            out_shape=shapes,
            compiler_params=pltpu.CompilerParams(vmem_limit_bytes=VMEM_LIMIT),
            cost_estimate=NO_COST,
            name="scatter_one",
        )(words, *halves, *halves[:2])
        return [from_blk(part, i) for i, part in enumerate(parts_a)], keep, across(send, 0)

    def scatter_two(self, words, parts_a, keep_b, other_b):
        count = self.count
        half_a = self.a // 2
        last = self.levels == 1
        half_b = keep_b.shape[1] // 2

        def body(words, ins, outs):
            bit = bit_of(words, 0)
            outs[0][...] = total_of(ins[:count], shard(bit, half_a)).astype(BF16)
            outs[1][...] = total_of(ins[:count], shard(1 - bit, half_a)).astype(BF16)
            bit = bit_of(words, 1)
            for out, side in ((outs[2], bit), (outs[3], 1 - bit)):
                rows = (slice(None), shard(side, half_b))
                out[...] = total_of(ins[count:], rows).astype(BF16)

        assert not last
        shapes = self.shapes(half_a, half_a) + [((count, half_b, self.width), BF16)] * 2
        keep_a, send_a, keep_b, send_b = local(
            body, "scatter_two", words, [*parts_a, keep_b, other_b], shapes
        )
        return keep_a, across(send_a, 0), keep_b, across(send_b, 1)

    def scatter_three(self, words, keep_a, other_a, keep_b, other_b):
        count = self.count
        b_rows = keep_b.shape[1]

        def body(words, ins, outs):
            outs[0][...] = total_of(ins[:2]).astype(BF16)
            for i in range(count):
                outs[1 + i][...] = total_of(ins[2:], words[0] ^ i).astype(BF16)

        shapes = self.shapes(keep_a.shape[0], *[b_rows] * count)
        arrays = [keep_a, other_a, keep_b, other_b]
        part_a, *parts_b = local(body, "scatter_three", words, arrays, shapes)
        return part_a, [from_blk(item, i) for i, item in enumerate(parts_b)]

    def sum_b(self, words, parts_b):
        def body(words, ins, outs):
            outs[0][...] = total_of(ins).astype(BF16)

        return local(body, "sum_b", words, parts_b, self.shapes(parts_b[0].shape[0]))[0]

    def merge(self, words, halves_a, halves_b):
        a, b = self.a // 2, self.b // 2

        def body(words, ins, outs):
            bit = bit_of(words, 0)

            def write(ref, start, rows, to):
                if rows > 0:
                    outs[0][to : to + rows] = ref[start : start + rows]

            for side in range(2):

                @pl.when(bit == side)
                def _(side=side):
                    for at, ref in ((side, ins[0]), (1 - side, ins[1])):
                        cut = max(0, min(a, self.a_ff - at * a))
                        write(ref, 0, cut, at * a)
                        write(ref, cut, a - cut, max(0, at * a - self.a_ff) + self.a_ff + self.b)
                    for at, ref in ((side, ins[2]), (1 - side, ins[3])):
                        write(ref, 0, b, self.a_ff + at * b)

        arrays = [*halves_a, *halves_b]
        return local(body, "merge", words, arrays, self.shapes(self.share))[0]


def gather_blk(part, cut, late=None):
    count = lax.axis_size("blk")
    if count != 4:
        return [(i, 0, from_blk(part, i)) for i in range(count)]
    one, two = swapped(part, 1), swapped(part, 2)
    if late is not None:
        one, two = after(late, (one, two))
    first, second = swapped(one[:cut], 2), swapped(two[cut:], 1)
    return [(0, 0, part), (1, 0, one), (2, 0, two), (3, 0, first), (3, cut, second)]


def with_core(pieces):
    return [(distance, base, from_core(item)) for distance, base, item in pieces]


SLOTS = 4


def widen_own(words, plan, pieces, hidden):
    width = plan.width
    chunks = hidden // width
    pairs = chunks // 2
    arrays = [item for _, _, item in pieces]
    segments = []
    extras = []
    for at, (distance, base, item) in enumerate(pieces):
        stop = base + item.shape[0]
        for start, rows, first in ((0, plan.a_ff, 0), (plan.a_ff, plan.b, plan.rows_a)):
            if base <= start and start + rows <= stop:
                segments.append((at, start - base, rows, distance, first))
        if stop == plan.share:
            extras.append((at, distance))
    assert len(segments) == 2 * plan.count and len(extras) == plan.count

    def kernel(words_ref, *refs):
        ins = refs[: len(arrays)]
        joined_ref, expand_ref, reduce_ref, held, sems = refs[len(arrays) :]
        copies = []
        for index, (at, top, rows, distance, first) in enumerate(segments):
            slot = index % SLOTS
            if index >= SLOTS:
                copies[index - SLOTS].wait()
            part = ins[at][top : top + rows]
            held[slot, :rows] = part.astype(F32)
            place = pl.multiple_of(first + (words_ref[0] ^ distance) * rows, 64)
            joined_ref[pl.ds(place, rows)] = part
            matrix = lax.div(place, width)
            row = place - matrix * width
            chunk = (lax.div(matrix, 2) + words_ref[2] * pairs) % chunks
            column = pl.multiple_of(chunk * width, width)
            source = held.at[slot, :rows]
            to_expand = pltpu.make_async_copy(
                source,
                expand_ref.at[pl.ds(pl.multiple_of(row, 64), rows), pl.ds(column, width)],
                sems.at[slot],
            )
            to_reduce = pltpu.make_async_copy(
                source,
                reduce_ref.at[pl.ds(pl.multiple_of(column + row, 64), rows)],
                sems.at[slot],
            )
            is_expand = lax.rem(matrix, 2) == 0
            pl.when(is_expand)(to_expand.start)
            pl.when(jnp.logical_not(is_expand))(to_reduce.start)
            copies.append(to_reduce)
        for at, distance in extras:
            rows = shard(words_ref[0] ^ distance, plan.a_more, plan.rows)
            joined_ref[rows] = ins[at][ins[at].shape[0] - plan.a_more :]
        for copy in copies[-SLOTS:]:
            copy.wait()

    vmem = pl.BlockSpec(memory_space=pltpu.VMEM)
    anywhere = pl.BlockSpec(memory_space=pl.ANY)
    return pl.pallas_call(
        kernel,
        in_specs=[pl.BlockSpec(memory_space=pltpu.SMEM)] + [vmem] * len(arrays),
        out_specs=[vmem, anywhere, anywhere],
        out_shape=[
            jax.ShapeDtypeStruct((plan.rows + plan.more, width), BF16),
            jax.ShapeDtypeStruct((width, hidden), F32),
            jax.ShapeDtypeStruct((hidden, width), F32),
        ],
        scratch_shapes=[
            pltpu.VMEM((SLOTS, max(plan.a_ff, plan.b), width), F32),
            pltpu.SemaphoreType.DMA((SLOTS,)),
        ],
        compiler_params=pltpu.CompilerParams(vmem_limit_bytes=VMEM_LIMIT),
        cost_estimate=pl.CostEstimate(
            flops=0, bytes_accessed=6 * hidden * width, transcendentals=0
        ),
        name="widen_own",
    )(words, *arrays)


def widen_other(words, joined, expand, reduce):
    width, hidden = expand.shape
    chunks = hidden // width
    pairs = chunks // 2

    def kernel(words_ref, half_ref, before_ref, before_too_ref, expand_ref, reduce_ref):
        expand_ref[...] = half_ref[:width].astype(F32)
        reduce_ref[...] = half_ref[width:].astype(F32)

    def place(s, words):
        return (s + (words[2] + 1) * pairs) % chunks

    anywhere = pl.BlockSpec(memory_space=pl.ANY)
    return pl.pallas_call(
        kernel,
        grid_spec=pltpu.PrefetchScalarGridSpec(
            num_scalar_prefetch=1,
            grid=(pairs,),
            in_specs=[
                pl.BlockSpec((2 * width, width), lambda s, words: (s, 0)),
                anywhere,
                anywhere,
            ],
            out_specs=[
                pl.BlockSpec((width, width), lambda s, words: (0, place(s, words))),
                pl.BlockSpec((width, width), lambda s, words: (place(s, words), 0)),
            ],
        ),
        out_shape=[
            jax.ShapeDtypeStruct((width, hidden), F32),
            jax.ShapeDtypeStruct((hidden, width), F32),
        ],
        input_output_aliases={2: 0, 3: 1},
        compiler_params=pltpu.CompilerParams(vmem_limit_bytes=VMEM_LIMIT),
        cost_estimate=pl.CostEstimate(
            flops=0, bytes_accessed=6 * hidden * width, transcendentals=0
        ),
        name="widen_other",
    )(words, joined, expand, reduce)


def finished(words, plan, heads, joined, side, before=()):
    count = plan.count
    span = plan.span
    width = plan.width
    half_rows = width // 2
    arrays = [item for _, _, item in heads]

    def kernel(words_ref, *refs):
        heads_refs, refs = refs[: len(heads)], refs[len(heads) :]
        extra_ref, refs = refs[0], refs[1 + len(before) :]
        outs, refs = refs[:5], refs[5:]
        gathered, wide, project, sems = refs
        rank = words_ref[0]
        half = words_ref[2] ^ side
        for ref, (distance, base, _) in zip(heads_refs, heads):
            rows = ref.shape[0]
            place = pl.multiple_of((rank ^ distance) * span, HEAD_DIM)
            for part in range(2):
                low, high = max(base, part * span), min(base + rows, (part + 1) * span)
                if low < high:
                    gathered[part, pl.ds(place + (low - part * span), high - low)] = ref[
                        low - base : high - base
                    ]
        for part in range(2):
            wide[part] = gathered[part, :width].astype(F32).T
        project[...] = extra_ref[:half_rows].astype(F32)

        @pl.when(half == 1)
        def _():
            wide[1] = entry_order(wide[1])

        def copy(source, target, at):
            return pltpu.make_async_copy(source, target, sems.at[at])

        for part in range(2):
            pl.when(half == 0)(copy(wide.at[part], outs[part], part).start)
            pl.when(half == 1)(copy(wide.at[part], outs[2 + part], part).start)
        rows = pl.ds(pl.multiple_of(half * half_rows, half_rows), half_rows)
        last = copy(project, outs[4].at[rows], 2)
        last.start()
        for part in range(2):
            copy(wide.at[part], outs[part], part).wait()
        last.wait()

    def whole(item):
        return pl.BlockSpec(item.shape, lambda s: (0, 0))

    more = pl.BlockSpec((plan.more, width), lambda s: (plan.rows // plan.more, 0))
    anywhere = pl.BlockSpec(memory_space=pl.ANY)
    first = 2 + len(heads)
    shapes = [jax.ShapeDtypeStruct((width, width), F32)] * 5
    return pl.pallas_call(
        kernel,
        grid=(1,),
        in_specs=[pl.BlockSpec(memory_space=pltpu.SMEM)]
        + [whole(item) for item in arrays]
        + [more]
        + [anywhere] * len(before),
        out_specs=[anywhere] * 5,
        out_shape=shapes,
        scratch_shapes=[
            pltpu.VMEM((2, count * span, width), BF16),
            pltpu.VMEM((2, width, width), F32),
            pltpu.VMEM((half_rows, width), F32),
            pltpu.SemaphoreType.DMA((3,)),
        ],
        input_output_aliases={first + at: at for at in range(len(before))},
        compiler_params=pltpu.CompilerParams(vmem_limit_bytes=VMEM_LIMIT),
        cost_estimate=pl.CostEstimate(
            flops=0, bytes_accessed=16 * width * width, transcendentals=0
        ),
        name="finish",
    )(words, *arrays, joined, *before)


def per_device(
    tokens,
    boxes,
    w_query,
    w_key,
    w_value,
    w_output,
    box_weight,
    first_gain,
    first_shift,
    w_expand,
    w_reduce,
    second_gain,
    second_shift,
    cotangent,
):
    pages, block, width = tokens.shape
    count = lax.axis_size("blk")
    depth = lax.axis_size("depth")
    words = jnp.stack(
        [lax.axis_index("blk"), lax.axis_index("depth"), lax.axis_index("core")]
    ).astype(jnp.int32)
    hidden = w_expand.shape[1]
    span = -(-HEADS // count) * HEAD_DIM
    unit = 16 * count * depth
    more = -(-(width // 2 + 16) // unit) * unit

    own_places = jnp.stack([boxes[0] + boxes[2], boxes[1] + boxes[3]], axis=1)
    own_places = jnp.stack([lax.shift_right_logical(own_places, 6), own_places & 63], axis=2)
    own_places = own_places.reshape(4 * pages, block).astype(BF16)
    own_places = jnp.pad(own_places, ((0, 16 - 4 * pages), (0, width - block)))
    message = jnp.concatenate([tokens[0], own_places])
    messages = [from_blk(message, i) for i in range(count)]
    w_own, box_own, rot_cos, rot_sin = prepare(
        words, w_query, w_key, w_value, box_weight, span, count * block
    )
    messages, rot_cos = lax.optimization_barrier((messages, rot_cos))
    own = after(messages, tokens[1])
    pieces = [messages, [from_blk(own, i) for i in range(count)]]

    saved = []
    att_parts = []
    for page in range(pages):
        results = attention_forward(
            words, page, messages, pieces[page], w_own, box_own, rot_cos, rot_sin
        )
        saved.append(results[:6])
        att_parts += [from_blk(results[6 + i], i) for i in range(count)]

    vectors = jnp.stack([first_gain, first_shift, second_gain, second_shift])
    results = middle(
        words,
        att_parts,
        tokens.reshape(pages * block, width),
        cotangent.reshape(pages * block, width),
        w_output,
        vectors,
        w_expand,
        w_reduce,
        pages,
        more,
    )
    layer_out, first_in, theirs, mine, more_theirs, more_mine = results[:6]
    grads = [from_blk(results[6 + i], i) for i in range(count)]
    plan = Plan(hidden, hidden - hidden // 2 // unit * unit, more, span, width)
    parts_a, keep_b, other_b = plan.scatter_one(
        after(grads, words), [mine, from_core(theirs), more_mine, from_core(more_theirs)]
    )

    def backward(page, words, before=None):
        return attention_backward(
            words,
            page,
            grads,
            pieces[page],
            saved[page],
            box_own,
            rot_cos,
            rot_sin,
            before,
        )

    *pre_one, before = backward(0, after(parts_a[0], words))
    part_a, other_a, keep_b, other_b = plan.scatter_two(
        after(before, words), parts_a, keep_b, other_b
    )
    done = part_a
    for level in range(2, plan.levels):
        keep_b, send_b = halve(after(done, words), level, keep_b, other_b)
        other_b = across(send_b, level)
        done = keep_b
    pre_one = [from_blk(item, i) for i, item in enumerate(after(part_a, pre_one))]
    *pre_two, heads_mine, heads_theirs = backward(1, after(done, words), before)

    part_a, parts_b = plan.scatter_three(
        after((heads_mine, pre_one), words), part_a, other_a, keep_b, other_b
    )
    heads, other = halve(
        after(part_a, words), 0, heads_mine, from_core(after(part_a, heads_theirs))
    )
    done = heads
    part_b = plan.sum_b(after(done, words), parts_b)
    done = part_b
    pre_two = [from_blk(item, i) for i, item in enumerate(after(part_b, pre_two))]
    for level in range(plan.levels - 1, 0, -1):
        part_b = join_halves(after(done, words), level, part_b, across(part_b, level))
        done = part_b
    halves_b = [part_b, across(part_b, 0)]
    for level in range(1, plan.levels):
        part_a = pair_sum(after(done, words), part_a, across(part_a, level))
        done = part_a
    other = across(after((part_a, halves_b), other), 0)
    share = plan.merge(
        after((done, pre_two), words), [part_a, across(part_a, 0)], halves_b
    )
    heads = pair_sum(after(share, words), heads, other)
    input_grad = input_gradient(
        after(heads, words), [pre_one, pre_two], (w_query, w_key, w_value), first_in
    )
    for level in range(1, plan.levels):
        heads = pair_sum(after(input_grad, words), heads, across(heads, level))
    pieces = gather_blk(share, plan.a_ff, heads)
    heads = join_halves(after(pieces[1][2], words), 0, heads, across(heads, 0))
    heads = after([item for _, _, item in pieces], heads)
    joined, *wide = widen_own(after(heads, words), plan, pieces, hidden)
    pieces_heads = gather_blk(heads, span, joined)
    joined_other = from_core(after(pieces_heads[1][2], joined))
    at = plan.rows + width // 2
    sums = jnp.where(words[2] == 0, joined[at : at + 4], joined_other[at : at + 4])
    sums = [sums[i].astype(F32) for i in range(4)]
    grad_expand, grad_reduce = widen_other(after(sums, words), joined_other, *wide)
    grads = finished(after(grad_expand, words), plan, pieces_heads, joined, 0)
    grad_query, grad_key, grad_value, grad_box, grad_project = finished(
        after(grads, words), plan, with_core(pieces_heads), joined_other, 1, grads
    )
    return (
        layer_out.reshape(tokens.shape),
        input_grad.reshape(tokens.shape),
        grad_query,
        grad_key,
        grad_value,
        grad_project,
        grad_box,
        sums[0],
        sums[1],
        grad_expand,
        grad_reduce,
        sums[2],
        sums[3],
    )


def solution(mesh):
    blocks, rest = mesh.devices.shape
    parts = jax.sharding.Mesh(
        mesh.devices.reshape(blocks, rest // 2, 2), ("blk", "depth", "core")
    )
    split = P(("depth", "core"), "blk", None)
    return jax.shard_map(
        per_device,
        mesh=parts,
        in_specs=(split, P(None, ("depth", "core"), "blk")) + (P(),) * 11 + (split,),
        out_specs=(split, split) + (P(),) * 11,
        check_vma=False,
    )
```

```python
import functools

import jax
import jax.numpy as jnp
import numpy as np
from jax import lax
from jax.experimental import pallas as pl
from jax.experimental.pallas import tpu as pltpu
from jax.sharding import PartitionSpec as P

HEADS = 12
HEAD_DIM = 64
HALF = 32
FREQS = 192
CODES = 4 * FREQS
VMEM_LIMIT = 60 * 1024 * 1024
NO_COST = pl.CostEstimate(flops=0, bytes_accessed=0, transcendentals=0)
F32 = jnp.float32
BF16 = jnp.bfloat16


def dot(left, right):
    return lax.dot_general(left, right, (((1,), (0,)), ((), ())), preferred_element_type=F32)


def dot_nt(left, right):
    return lax.dot_general(left, right, (((1,), (1,)), ((), ())), preferred_element_type=F32)


def dot_tn(left, right):
    return lax.dot_general(left, right, (((0,), (0,)), ((), ())), preferred_element_type=F32)


def swapped(block, distance, axis="blk"):
    count = lax.axis_size(axis)
    return lax.ppermute(block, axis, [(i, i ^ distance) for i in range(count)])


def from_blk(block, distance):
    return swapped(block, distance) if distance else block


def from_core(block):
    return swapped(block, 1, "core")


def after(done, value):
    return lax.optimization_barrier((value, done))[0]


def turned(upper, lower, cosines, sines):
    return upper * cosines - lower * sines, lower * cosines + upper * sines


def entry_order(rows):
    return jnp.concatenate(
        [
            rows[:FREQS],
            rows[2 * FREQS : 3 * FREQS],
            rows[FREQS : 2 * FREQS],
            rows[3 * FREQS :],
        ],
        axis=0,
    )


def angle_tables():
    rates = np.float32(10000.0) ** (-np.arange(FREQS, dtype=np.float32) / np.float32(FREQS))
    tables = []
    for places in (32.0 * np.arange(32), 0.5 * np.arange(64)):
        angles = rates.astype(np.float64)[:, None] * places[None, :]
        left = np.concatenate([np.sin(angles), np.cos(angles)])
        parts = []
        for _ in range(3):
            parts.append(left.astype(jnp.bfloat16))
            left = left - parts[-1].astype(np.float64)
        tables.append(np.concatenate(parts, axis=1))
    return tables


def rotary_tables(length):
    rates = np.float32(10000.0) ** (-np.arange(HALF, dtype=np.float32) / np.float32(HALF))
    angles = np.arange(length, dtype=np.float32)[None, :] * rates[:, None]
    angles = angles.astype(np.float64)
    return np.cos(angles).astype(np.float32), np.sin(angles).astype(np.float32)


def prepare_kernel(
    words_ref,
    query_ref,
    key_ref,
    value_ref,
    box_ref,
    cos_ref,
    sin_ref,
    own_ref,
    own_box_ref,
    own_cos_ref,
    own_sin_ref,
):
    rank = words_ref[0]
    span = own_box_ref.shape[0]
    width = query_ref.shape[1]
    count = lax.axis_size("blk")
    block = cos_ref.shape[1] // count
    row = lax.broadcasted_iota(jnp.int32, (span, width), 0) + rank * span
    column = lax.broadcasted_iota(jnp.int32, (span, width), 1)
    pick = jnp.where(row == column, 1.0, 0.0).astype(BF16)
    for kind, ref in enumerate((query_ref, key_ref, value_ref)):
        own_ref[kind * span : (kind + 1) * span] = dot_nt(pick, ref[...]).astype(BF16)
    own_box_ref[...] = dot_nt(pick, entry_order(box_ref[...])).astype(BF16)
    for i in range(count):
        from_cols = pl.ds(pl.multiple_of((rank ^ i) * block, block), block)
        own_cos_ref[:, i * block : (i + 1) * block] = cos_ref[:, from_cols]
        own_sin_ref[:, i * block : (i + 1) * block] = sin_ref[:, from_cols]


def prepare(words, w_query, w_key, w_value, box_weight, span, length):
    width = w_query.shape[0]
    vmem = pl.BlockSpec(memory_space=pltpu.VMEM)
    return pl.pallas_call(
        prepare_kernel,
        in_specs=[pl.BlockSpec(memory_space=pltpu.SMEM)] + [vmem] * 6,
        out_specs=[vmem] * 4,
        out_shape=[
            jax.ShapeDtypeStruct((3 * span, width), BF16),
            jax.ShapeDtypeStruct((span, CODES), BF16),
            jax.ShapeDtypeStruct((HALF, length), F32),
            jax.ShapeDtypeStruct((HALF, length), F32),
        ],
        compiler_params=pltpu.CompilerParams(vmem_limit_bytes=VMEM_LIMIT),
        cost_estimate=pl.CostEstimate(
            flops=8 * span * width * width, bytes_accessed=10 * width * width, transcendentals=0
        ),
        name="prepare",
    )(words, w_query, w_key, w_value, box_weight, *map(jnp.asarray, rotary_tables(length)))


def fold(value, combine):
    while value.shape[0] > 8:
        half = value.shape[0] // 2
        value = combine(value[:half], value[half:])
    return value


def write_codes(page, place_refs, high_ref, low_ref, sin_ref, cos_ref, codes_ref):
    block = sin_ref.shape[1] // len(place_refs)

    def looked_up(table_ref, index):
        spots = table_ref.shape[1] // 3
        rows = lax.broadcasted_iota(jnp.int32, (spots, block), 0).astype(F32)
        once = jnp.where(rows == index, 1.0, 0.0)
        found = dot(table_ref[...], jnp.concatenate([once] * 3, axis=0).astype(BF16))
        return found[:FREQS], found[FREQS:]

    for i, place_ref in enumerate(place_refs):
        columns = slice(i * block, (i + 1) * block)
        places = place_ref[:, :block].astype(F32)
        for axis in range(2):
            at = 4 * page + 2 * axis
            high_sin, high_cos = looked_up(high_ref, places[at : at + 1])
            low_sin, low_cos = looked_up(low_ref, places[at + 1 : at + 2])
            sines = high_sin * low_cos + high_cos * low_sin
            cosines = high_cos * low_cos - high_sin * low_sin
            rows = slice(axis * FREQS, (axis + 1) * FREQS)
            later = slice((2 + axis) * FREQS, (3 + axis) * FREQS)
            sin_ref[rows, columns] = sines
            cos_ref[rows, columns] = cosines
            codes_ref[rows, columns] = sines.astype(BF16)
            codes_ref[later, columns] = cosines.astype(BF16)


def forward_kernel(page, count, words_ref, *refs):
    place_refs, refs = refs[:count], refs[count:]
    piece_refs, refs = refs[:count], refs[count:]
    high_ref, low_ref, w_ref, box_ref, rot_cos_ref, rot_sin_ref = refs[:6]
    probs_ref, att_ref, heads_ref, sin_ref, cos_ref, codes_ref = refs[6:12]
    low_refs = refs[12 : 12 + count]
    tok_ref, pre_ref, kc_ref, qr_ref = refs[12 + count :]
    rows = tok_ref.shape[0]
    block = rows // count
    head = pl.program_id(0)
    span = pl.num_programs(0) * HEAD_DIM

    @pl.when(head == 0)
    def _():
        for i in range(count):
            tok_ref[i * block : (i + 1) * block] = piece_refs[i][...]
        pre_ref[...] = dot_nt(w_ref[...], tok_ref[...])
        write_codes(page, place_refs, high_ref, low_ref, sin_ref, cos_ref, codes_ref)
        kc_ref[:, :CODES] = codes_ref[...].astype(F32).T.astype(BF16)

    def pre(kind):
        at = kind * span + head * HEAD_DIM
        return pre_ref[pl.ds(pl.multiple_of(at, HEAD_DIM), HEAD_DIM)]

    rot_cos = rot_cos_ref[...]
    rot_sin = rot_sin_ref[...]
    query_pre = pre(0).astype(BF16)
    wide = query_pre.astype(F32)
    query = jnp.concatenate(turned(wide[:HALF], wide[HALF:], rot_cos, rot_sin), axis=0)
    key_pre = pre(1)
    key = jnp.concatenate(turned(key_pre[:HALF], key_pre[HALF:], rot_cos, rot_sin), axis=0)
    value = pre(2).astype(BF16)
    heads_ref[0, :HEAD_DIM] = query_pre
    heads_ref[0, HEAD_DIM : 2 * HEAD_DIM] = query.astype(BF16)
    heads_ref[0, 2 * HEAD_DIM : 3 * HEAD_DIM] = key.astype(BF16)
    heads_ref[0, 3 * HEAD_DIM :] = value
    kc_ref[:, CODES:] = key.T.astype(BF16)
    qr_ref[CODES:] = (query * 0.125).astype(BF16)
    step = min(256, block)

    def logits_at(at):
        part = slice(at, at + step)
        projected = dot_tn(box_ref[...], query_pre[:, part])
        sines = sin_ref[:, part]
        cosines = cos_ref[:, part]
        upper = projected[: 2 * FREQS]
        lower = projected[2 * FREQS :]
        qr_ref[: 2 * FREQS, part] = ((upper * cosines + lower * sines) * 0.125).astype(BF16)
        qr_ref[2 * FREQS : CODES, part] = ((lower * cosines - upper * sines) * 0.125).astype(BF16)
        return dot(kc_ref[...], qr_ref[:, part])

    following = logits_at(0)
    for at in range(0, rows, step):
        logits = following
        if at + step < rows:
            following = logits_at(at + step)
        peak = jnp.max(fold(logits, jnp.maximum), axis=0, keepdims=True)
        weight = jnp.exp(logits - peak)
        total = jnp.sum(fold(weight, jnp.add), axis=0, keepdims=True)
        probs = (weight * (1.0 / total)).astype(BF16)
        probs_ref[0, :, at : at + step] = probs
        attended = dot(value, probs)
        att_ref[0, :, at : at + step] = attended
        inner = at % block
        low_refs[at // block][:, inner : inner + step] = attended.astype(BF16)


def fixed(array):
    return pl.BlockSpec(array.shape, lambda *at: (0,) * len(array.shape))


def attention_forward(words, page, messages, pieces, w_own, box_own, rot_cos, rot_sin):
    count = len(messages)
    block, width = messages[0].shape[0] - 16, messages[0].shape[1]
    rows = count * block
    span = box_own.shape[0]
    heads = span // HEAD_DIM
    tables = [jnp.asarray(item) for item in angle_tables()]
    specs = [pl.BlockSpec((block, width), lambda h, words: (0, 0))] * count
    places = pl.BlockSpec((16, width), lambda h, words: (block // 16, 0))
    out_shape = [
        jax.ShapeDtypeStruct((heads, rows, rows), BF16),
        jax.ShapeDtypeStruct((heads, HEAD_DIM, rows), F32),
        jax.ShapeDtypeStruct((heads, 4 * HEAD_DIM, rows), BF16),
        jax.ShapeDtypeStruct((2 * FREQS, rows), F32),
        jax.ShapeDtypeStruct((2 * FREQS, rows), F32),
        jax.ShapeDtypeStruct((CODES, rows), BF16),
    ] + [jax.ShapeDtypeStruct((span, block), BF16)] * count
    return pl.pallas_call(
        functools.partial(forward_kernel, page, count),
        grid_spec=pltpu.PrefetchScalarGridSpec(
            num_scalar_prefetch=1,
            grid=(heads,),
            in_specs=[places] * count
            + specs
            + [fixed(item) for item in (*tables, w_own)]
            + [
                pl.BlockSpec((HEAD_DIM, CODES), lambda h, words: (h, 0)),
                fixed(rot_cos),
                fixed(rot_sin),
            ],
            out_specs=[
                pl.BlockSpec((1, rows, rows), lambda h, words: (h, 0, 0)),
                pl.BlockSpec((1, HEAD_DIM, rows), lambda h, words: (h, 0, 0)),
                pl.BlockSpec((1, 4 * HEAD_DIM, rows), lambda h, words: (h, 0, 0)),
            ]
            + [fixed(item) for item in out_shape[3:6]]
            + [pl.BlockSpec((HEAD_DIM, block), lambda h, words: (h, 0))] * count,
            scratch_shapes=[
                pltpu.VMEM((rows, width), BF16),
                pltpu.VMEM((3 * span, rows), F32),
                pltpu.VMEM((rows, CODES + HEAD_DIM), BF16),
                pltpu.VMEM((CODES + HEAD_DIM, rows), BF16),
            ],
        ),
        out_shape=out_shape,
        compiler_params=pltpu.CompilerParams(vmem_limit_bytes=VMEM_LIMIT),
        cost_estimate=pl.CostEstimate(
            flops=2 * heads * rows * (rows * 1100 + 200 * width + 64 * CODES),
            bytes_accessed=2 * heads * rows * rows + 12 * rows * width,
            transcendentals=heads * rows * rows,
        ),
        name="attention_forward",
    )(words, *messages, *pieces, *tables, w_own, box_own, rot_cos, rot_sin)


def backward_kernel(count, last, words_ref, *refs):
    grad_refs, refs = refs[:count], refs[count:]
    piece_refs, refs = refs[:count], refs[count:]
    probs_ref, att_ref, heads_ref, box_ref, codes_ref, sin_ref, cos_ref = refs[:7]
    rot_cos_ref, rot_sin_ref = refs[7:9]
    refs = refs[9:]
    if last:
        before_ref, refs = refs[0], refs[1:]
    pre_refs, refs = refs[:count], refs[count:]
    if last:
        mine_ref, theirs_ref, *refs = refs
    weight_grad_ref, kc_ref, logit_grad_ref, entry_grad_ref, turned_ref = refs
    block, width = piece_refs[0].shape
    rows = count * block
    head = pl.program_id(0)
    span = pl.num_programs(0) * HEAD_DIM

    @pl.when(head == 0)
    def _():
        kc_ref[:CODES] = codes_ref[...]

    kc_ref[CODES:] = heads_ref[0, 2 * HEAD_DIM : 3 * HEAD_DIM]
    packed = heads_ref[0].astype(F32).T.astype(BF16)
    query_pre = packed[:, :HEAD_DIM]
    query = packed[:, HEAD_DIM : 2 * HEAD_DIM]
    value = packed[:, 3 * HEAD_DIM :] * jnp.asarray(0.125, BF16)
    rot_cos = rot_cos_ref[...]
    rot_sin = rot_sin_ref[...]
    grad = jnp.concatenate([ref[...] for ref in grad_refs], axis=1)
    grad_tall = grad.astype(F32).T.astype(BF16)
    offsets = jnp.sum(grad.astype(F32) * att_ref[0], axis=0, keepdims=True) * 0.125
    step = min(256, block)
    place = pl.multiple_of(head * HEAD_DIM, HEAD_DIM)
    here = pl.ds(place, HEAD_DIM)

    def logits_back(at):
        part = slice(at, at + step)
        grad_probs = dot(value, grad[:, part])
        logit_grad_ref[:, part] = (
            probs_ref[0, :, part].astype(F32) * (grad_probs - offsets[:, part])
        ).astype(BF16)

    logits_back(0)
    for at in range(0, rows, step):
        if at + step < rows:
            logits_back(at + step)
        part = slice(at, at + step)
        back = dot(kc_ref[...], logit_grad_ref[:, part])
        sines = sin_ref[:, part]
        cosines = cos_ref[:, part]
        upper = back[: 2 * FREQS]
        lower = back[2 * FREQS : CODES]
        entry_grad_ref[: 2 * FREQS, part] = (upper * cosines - lower * sines).astype(BF16)
        entry_grad_ref[2 * FREQS :, part] = (lower * cosines + upper * sines).astype(BF16)
        first = back[CODES : CODES + HALF]
        second = back[CODES + HALF :]
        turned_ref[:HALF, part], turned_ref[HALF:, part] = turned(
            first, second, rot_cos[:, part], -rot_sin[:, part]
        )
    key_flat = dot(logit_grad_ref[...], query).T
    value_low = dot(probs_ref[0], grad_tall).T.astype(BF16)
    query_low = (turned_ref[...] + dot(box_ref[...], entry_grad_ref[...])).astype(BF16)
    key_low = jnp.concatenate(
        turned(key_flat[:HALF], key_flat[HALF:], rot_cos, -rot_sin), axis=0
    ).astype(BF16)
    for i in range(count):
        columns = slice(i * block, (i + 1) * block)
        pre_refs[i][here, :block] = query_low[:, columns]
        pre_refs[i][here, block : 2 * block] = key_low[:, columns]
        pre_refs[i][here, 2 * block :] = value_low[:, columns]
    weight_grad_ref[pl.ds(3 * span + place, HEAD_DIM)] = dot(entry_grad_ref[...], query_pre).T

    @pl.when(head == pl.num_programs(0) - 1)
    def _():
        for kind in range(3):
            columns = slice(kind * block, (kind + 1) * block)
            total = dot(pre_refs[0][:, columns], piece_refs[0][...])
            for i in range(1, count):
                total = total + dot(pre_refs[i][:, columns], piece_refs[i][...])
            weight_grad_ref[kind * span : (kind + 1) * span] = total
        if last:
            half = 2 * span
            core = words_ref[2]
            ours = pl.ds(pl.multiple_of(core * half, half), half)
            there = pl.ds(pl.multiple_of((1 - core) * half, half), half)
            mine_ref[...] = weight_grad_ref[ours] + before_ref[ours]
            theirs_ref[...] = (weight_grad_ref[there] + before_ref[there]).astype(BF16)


def attention_backward(
    words, page, grads, pieces, saved, box_own, rot_cos, rot_sin, before=None
):
    probs, att, heads_saved, sines, cosines, codes = saved
    count = len(pieces)
    rows, width = probs.shape[1], pieces[0].shape[1]
    block = rows // count
    span = box_own.shape[0]
    heads = span // HEAD_DIM
    last = before is not None
    extra = (before,) if last else ()
    full_shape = (4 * span, width)
    specs = [pl.BlockSpec((block, width), lambda h, words: (0, 0))] * count
    out_shape = [jax.ShapeDtypeStruct((span, 3 * block), BF16)] * count
    if last:
        out_shape += [
            jax.ShapeDtypeStruct((2 * span, width), F32),
            jax.ShapeDtypeStruct((2 * span, width), BF16),
        ]
    else:
        out_shape.append(jax.ShapeDtypeStruct(full_shape, F32))
    return pl.pallas_call(
        functools.partial(backward_kernel, count, last),
        grid_spec=pltpu.PrefetchScalarGridSpec(
            num_scalar_prefetch=1,
            grid=(heads,),
            in_specs=[pl.BlockSpec((HEAD_DIM, block), lambda h, words: (h, page))] * count
            + specs
            + [
                pl.BlockSpec((1, rows, rows), lambda h, words: (h, 0, 0)),
                pl.BlockSpec((1, HEAD_DIM, rows), lambda h, words: (h, 0, 0)),
                pl.BlockSpec((1, 4 * HEAD_DIM, rows), lambda h, words: (h, 0, 0)),
                pl.BlockSpec((HEAD_DIM, CODES), lambda h, words: (h, 0)),
            ]
            + [fixed(item) for item in (codes, sines, cosines, rot_cos, rot_sin, *extra)],
            out_specs=[fixed(item) for item in out_shape],
            scratch_shapes=([pltpu.VMEM(full_shape, F32)] if last else [])
            + [
                pltpu.VMEM((CODES + HEAD_DIM, rows), BF16),
                pltpu.VMEM((rows, rows), BF16),
                pltpu.VMEM((CODES, rows), BF16),
                pltpu.VMEM((HEAD_DIM, rows), F32),
            ],
        ),
        out_shape=out_shape,
        compiler_params=pltpu.CompilerParams(vmem_limit_bytes=VMEM_LIMIT),
        cost_estimate=pl.CostEstimate(
            flops=2 * heads * rows * (rows * 1400 + 200 * width + 128 * CODES),
            bytes_accessed=2 * heads * rows * rows + 12 * rows * width,
            transcendentals=0,
        ),
        name="attention_backward",
    )(
        words,
        *grads,
        *pieces,
        probs,
        att,
        heads_saved,
        box_own,
        codes,
        sines,
        cosines,
        rot_cos,
        rot_sin,
        *extra,
    )


def normed(value):
    centered = value - jnp.mean(value, axis=-1, keepdims=True)
    scale = lax.rsqrt(jnp.mean(centered * centered, axis=-1, keepdims=True) + 1e-05)
    return centered * scale, scale


def norm_back(grad, gain, unit, scale):
    scaled = grad * gain
    return scale * (
        scaled
        - jnp.mean(scaled, axis=-1, keepdims=True)
        - unit * jnp.mean(scaled * unit, axis=-1, keepdims=True)
    )


def column_sum(value):
    return jnp.sum(value, axis=0, keepdims=True)


def middle_kernel(pages, count, span, chunks, *refs):
    total = pages * count
    words_ref = refs[0]
    att_refs = refs[1 : 1 + total]
    (
        tok_ref,
        cot_ref,
        w_out_ref,
        vectors_ref,
        w_expand_ref,
        w_reduce_ref,
    ) = refs[1 + total : 7 + total]
    outs = refs[7 + total :]
    layer_ref, first_in_ref, theirs_ref, mine_ref, more_theirs_ref, more_mine_ref = outs[:6]
    grad_refs = outs[6 : 6 + count]
    (
        sums_ref,
        att_all,
        grad_all,
        unit_one,
        scale_one,
        first_wide,
        first_low,
        first_tall,
        active,
        slope,
        gathered,
        second_in,
        second_low,
    ) = outs[6 + count :]
    rank = words_ref[0]
    width = tok_ref.shape[1]
    block = tok_ref.shape[0] // pages
    step = pl.program_id(0)

    def rows_of(at):
        return pl.ds(pl.multiple_of((rank ^ at) * span, span), span)

    @pl.when(step == 0)
    def _():
        for page in range(pages):
            for at in range(count):
                att_all[rows_of(at), page * block : (page + 1) * block] = att_refs[
                    page * count + at
                ][...]
        branch = dot_tn(att_all[: w_out_ref.shape[0]], w_out_ref[...])
        unit, scale = normed(tok_ref[...].astype(F32) + branch)
        unit_one[...] = unit
        scale_one[...] = jnp.broadcast_to(scale, scale_one.shape)
        first_out = unit * vectors_ref[0:1] + vectors_ref[1:2]
        first_wide[...] = first_out
        first_low[...] = first_out.astype(BF16)
        first_tall[...] = first_out.T.astype(BF16)
        gathered[...] = jnp.zeros_like(gathered)
        sums_ref[...] = jnp.zeros_like(sums_ref)

    for chunk in range(chunks):

        @pl.when(step == chunk)
        def _(chunk=chunk):
            expanded = dot(first_low[...], w_expand_ref[...])
            gate = 0.5 + 0.5 * lax.erf(expanded * np.float32(np.sqrt(0.5)))
            bell = jnp.exp(expanded * expanded * -0.5) * np.float32(1.0 / np.sqrt(2.0 * np.pi))
            low = (expanded * gate).astype(BF16)
            active[chunk] = low
            slope[chunk] = gate + expanded * bell
            gathered[...] += dot(low, w_reduce_ref[...])

    @pl.when(step == chunks - 1)
    def _():
        unit, scale = normed(first_wide[...] + gathered[...])
        layer_ref[...] = (unit * vectors_ref[2:3] + vectors_ref[3:4]).astype(BF16)
        cot = cot_ref[...].astype(F32)
        sums_ref[2:3] = column_sum(cot * unit)
        sums_ref[3:4] = column_sum(cot)
        grad = norm_back(cot, vectors_ref[2:3], unit, scale)
        second_in[...] = grad
        second_low[...] = grad.astype(BF16)
        gathered[...] = grad

    for chunk in range(chunks):

        @pl.when(step == 2 * chunks - 1 - chunk)
        def _(chunk=chunk):
            grad_active = dot_nt(second_low[...], w_reduce_ref[...])
            grad_expanded = (grad_active * slope[chunk]).astype(BF16)
            grads_ref = mine_ref if chunk < chunks // 2 else theirs_ref
            grads_ref[:width] = dot(first_tall[...], grad_expanded).astype(BF16)
            grads_ref[width:] = dot_tn(active[chunk], second_low[...]).astype(BF16)
            gathered[...] += dot_nt(grad_expanded, w_expand_ref[...])

    @pl.when(step == 2 * chunks - 1)
    def _():
        unit = unit_one[...]
        grad_out = gathered[...]
        sums_ref[0:1] = column_sum(grad_out * unit)
        sums_ref[1:2] = column_sum(grad_out)
        grad = norm_back(grad_out, vectors_ref[0:1], unit, scale_one[:, :1])
        first_in_ref[...] = grad
        low = grad.astype(BF16)
        real = w_out_ref.shape[0]
        half = real // 2
        core = words_ref[2]
        for ref, side in ((more_mine_ref, core), (more_theirs_ref, 1 - core)):
            rows = pl.ds(pl.multiple_of(side * half, half), half)
            ref[:half] = dot(att_all[rows], low).astype(BF16)
            ref[half:] = jnp.zeros((ref.shape[0] - half, width), BF16)
            ref[half : half + 16] = sums_ref[...].astype(BF16)
        if grad_all.shape[0] > real:
            grad_all[real:] = jnp.zeros((grad_all.shape[0] - real, low.shape[0]), BF16)
        grad_all[:real] = dot_nt(w_out_ref[...], low).astype(BF16)
        for at in range(count):
            grad_refs[at][...] = grad_all[rows_of(at)]


def middle(words, att_parts, tok, cot, w_out, vectors, w_expand, w_reduce, pages, more):
    rows, width = tok.shape
    count = len(att_parts) // pages
    span, block = att_parts[0].shape
    hidden = w_expand.shape[1]
    chunks = hidden // width
    pairs = chunks // 2

    def whole(array):
        return pl.BlockSpec(array.shape, lambda s, words: (0,) * len(array.shape))

    def chunk_at(s, words):
        at = jnp.minimum(s, 2 * chunks - 1 - s)
        return (at + words[2] * pairs) % chunks

    def theirs_at(s, words):
        return jnp.clip(2 * chunks - 1 - s - pairs, 0, pairs - 1), 0

    def mine_at(s, words):
        return jnp.clip(2 * chunks - 1 - s, 0, pairs - 1), 0

    shapes = [
        jax.ShapeDtypeStruct((rows, width), BF16),
        jax.ShapeDtypeStruct((rows, width), F32),
        jax.ShapeDtypeStruct((hidden, width), BF16),
        jax.ShapeDtypeStruct((hidden, width), BF16),
        jax.ShapeDtypeStruct((more, width), BF16),
        jax.ShapeDtypeStruct((more, width), BF16),
    ] + [jax.ShapeDtypeStruct((span, pages * block), BF16)] * count
    specs = [whole(item) for item in shapes]
    specs[2] = pl.BlockSpec((2 * width, width), theirs_at)
    specs[3] = pl.BlockSpec((2 * width, width), mine_at)
    return pl.pallas_call(
        functools.partial(middle_kernel, pages, count, span, chunks),
        grid_spec=pltpu.PrefetchScalarGridSpec(
            num_scalar_prefetch=1,
            grid=(2 * chunks,),
            in_specs=[whole(item) for item in att_parts]
            + [
                whole(tok),
                whole(cot),
                whole(w_out),
                whole(vectors),
                pl.BlockSpec((width, width), lambda s, words: (0, chunk_at(s, words))),
                pl.BlockSpec((width, width), lambda s, words: (chunk_at(s, words), 0)),
            ],
            out_specs=specs,
            scratch_shapes=[
                pltpu.VMEM((16, width), F32),
                pltpu.VMEM((count * span, rows), BF16),
                pltpu.VMEM((count * span, rows), BF16),
                pltpu.VMEM((rows, width), F32),
                pltpu.VMEM((rows, 128), F32),
                pltpu.VMEM((rows, width), F32),
                pltpu.VMEM((rows, width), BF16),
                pltpu.VMEM((width, rows), BF16),
                pltpu.VMEM((chunks, rows, width), BF16),
                pltpu.VMEM((chunks, rows, width), F32),
                pltpu.VMEM((rows, width), F32),
                pltpu.VMEM((rows, width), F32),
                pltpu.VMEM((rows, width), BF16),
            ],
        ),
        out_shape=shapes,
        compiler_params=pltpu.CompilerParams(vmem_limit_bytes=VMEM_LIMIT),
        cost_estimate=pl.CostEstimate(
            flops=2 * rows * width * (6 * hidden + 3 * width),
            bytes_accessed=8 * width * hidden + 16 * rows * width,
            transcendentals=2 * rows * hidden,
        ),
        name="middle",
    )(words, *att_parts, tok, cot, w_out, vectors, w_expand, w_reduce)


def input_kernel(pages, count, span, base, *refs):
    words_ref = refs[0]
    own_refs = refs[1 : 1 + pages]
    message_refs = refs[1 + pages : pages + count]
    weight_refs = refs[pages + count : 3 + pages + count]
    first_in_ref, out_ref, held = refs[3 + pages + count :]
    rank = words_ref[0]
    width = out_ref.shape[1]
    block = out_ref.shape[0] // pages
    for page in range(pages):
        for at in range(count):
            part = message_refs[at - 1] if at else own_refs[page]
            top = base + page * span if at else 0
            place = pl.multiple_of((rank ^ at) * span, span)
            for kind in range(3):
                held[kind, pl.ds(place, span), page * block : (page + 1) * block] = part[
                    top : top + span, kind * block : (kind + 1) * block
                ]
    total = dot(weight_refs[0][...], held[0, :width])
    for kind in range(1, 3):
        total = total + dot(weight_refs[kind][...], held[kind, :width])
    out_ref[...] = (first_in_ref[...] + total.T).astype(BF16)


def input_gradient(words, own, messages, base, span, weights, first_in):
    pages = len(own)
    count = 1 + len(messages)
    rows, width = first_in.shape
    vmem = pl.BlockSpec(memory_space=pltpu.VMEM)
    return pl.pallas_call(
        functools.partial(input_kernel, pages, count, span, base),
        in_specs=[pl.BlockSpec(memory_space=pltpu.SMEM)] + [vmem] * (pages + count + 3),
        out_specs=vmem,
        out_shape=jax.ShapeDtypeStruct((rows, width), BF16),
        scratch_shapes=[pltpu.VMEM((3, count * span, rows), BF16)],
        compiler_params=pltpu.CompilerParams(vmem_limit_bytes=VMEM_LIMIT),
        cost_estimate=pl.CostEstimate(
            flops=6 * rows * width * count * span,
            bytes_accessed=2 * width * (5 * rows + 3 * count * span),
            transcendentals=0,
        ),
        name="input_gradient",
    )(words, *own, *messages, *weights, first_in)


def local(body, name, words, arrays, shapes, costly=False):
    def kernel(words_ref, *refs):
        body(words_ref, refs[: len(arrays)], refs[len(arrays) :])

    vmem = pl.BlockSpec(memory_space=pltpu.VMEM)
    shapes = [jax.ShapeDtypeStruct(shape, kind) for shape, kind in shapes]
    moved = sum(item.size * item.dtype.itemsize for item in list(arrays) + shapes)
    cost = pl.CostEstimate(flops=0, bytes_accessed=moved, transcendentals=0)
    return pl.pallas_call(
        kernel,
        in_specs=[pl.BlockSpec(memory_space=pltpu.SMEM)] + [vmem] * len(arrays),
        out_specs=[vmem] * len(shapes),
        out_shape=shapes,
        compiler_params=pltpu.CompilerParams(vmem_limit_bytes=VMEM_LIMIT),
        cost_estimate=cost if costly else NO_COST,
        name=name,
    )(words, *arrays)


def shard(index, rows, base=0):
    return pl.ds(pl.multiple_of(base + index * rows, 16), rows)


def total_of(refs, rows=slice(None)):
    if len(refs) == 2 and all(ref.dtype == BF16 for ref in refs):
        return refs[0][rows] + refs[1][rows]
    total = refs[0][rows].astype(F32)
    for ref in refs[1:]:
        total = total + ref[rows].astype(F32)
    return total


def tree_sum(terms):
    while len(terms) > 1:
        terms = [terms[i] + terms[i + 1] for i in range(0, len(terms), 2)]
    return terms[0]


def bit_of(words, level):
    return lax.shift_right_logical(words[1], level) & 1


def pair_sum(words, mine, other):
    def body(words, ins, outs):
        outs[0][...] = total_of(ins).astype(BF16)

    return local(body, "pair_sum", words, [mine, other], [(mine.shape, BF16)])[0]


def halve(words, level, mine, other):
    rows, width = mine.shape
    half = rows // 2

    def body(words, ins, outs):
        bit = bit_of(words, level)
        outs[0][...] = total_of(ins, shard(bit, half)).astype(BF16)
        outs[1][...] = total_of(ins, shard(1 - bit, half)).astype(BF16)

    return local(body, "halve", words, [mine, other], [((half, width), BF16)] * 2)


def join_halves(words, level, mine, other):
    rows, width = mine.shape

    def body(words, ins, outs):
        bit = bit_of(words, level)
        outs[0][shard(bit, rows)] = ins[0][...]
        outs[0][shard(1 - bit, rows)] = ins[1][...]

    return local(body, "join_halves", words, [mine, other], [((2 * rows, width), BF16)])[0]


def across(block, level):
    return swapped(block, 1 << level, "depth")


class Plan:
    def __init__(self, rows, rows_a, more, span, width):
        self.count = lax.axis_size("blk")
        self.levels = lax.axis_size("depth").bit_length() - 1
        self.rows = rows
        self.rows_a = rows_a
        self.more = more
        self.span = span
        self.width = width
        self.a_ff = rows_a // self.count
        self.a_more = more // self.count
        self.a = self.a_ff + self.a_more
        self.b = (rows - rows_a) >> self.levels

    def shapes(self, *sizes):
        return [((rows, self.width), BF16) for rows in sizes]

    def scatter_one(self, words, halves):
        count, width = self.count, self.width
        a_ff, a_more = self.a_ff, self.a_more
        b_rows = (self.rows - self.rows_a) // count
        steps = count // 2

        def kernel(words_ref, *refs):
            parts = refs[6 : 6 + count]
            keep_ref, send_ref = refs[6 + count :]
            for i in range(count):

                @pl.when(pl.program_id(0) == i)
                def _(i=i):
                    parts[i][:a_ff] = total_of(refs[:2]).astype(BF16)
                    parts[i][a_ff:] = total_of(refs[2:4]).astype(BF16)
                    side = send_ref if i < steps else keep_ref
                    side[...] = total_of(refs[4:6]).astype(BF16)

        def there(rows):
            return pl.BlockSpec((rows, width), lambda i, words: (words[0] ^ i, 0))

        def b_at(i, words):
            bit = bit_of(words, 0)
            side = jnp.where(i < steps, 1 - bit, bit)
            return self.rows_a // b_rows + side * steps + i % steps, 0

        own_b = pl.BlockSpec((b_rows, width), b_at)
        shapes = [jax.ShapeDtypeStruct((self.a, width), BF16)] * count
        shapes += [jax.ShapeDtypeStruct((b_rows * steps, width), BF16)] * 2
        *parts_a, keep, send = pl.pallas_call(
            kernel,
            grid_spec=pltpu.PrefetchScalarGridSpec(
                num_scalar_prefetch=1,
                grid=(count,),
                in_specs=[there(a_ff)] * 2 + [there(a_more)] * 2 + [own_b] * 2,
                out_specs=[fixed(item) for item in shapes[:count]]
                + [
                    pl.BlockSpec((b_rows, width), lambda i, words: (jnp.maximum(i - steps, 0), 0)),
                    pl.BlockSpec((b_rows, width), lambda i, words: (jnp.minimum(i, steps - 1), 0)),
                ],
            ),
            out_shape=shapes,
            compiler_params=pltpu.CompilerParams(vmem_limit_bytes=VMEM_LIMIT),
            cost_estimate=NO_COST,
            name="scatter_one",
        )(words, *halves, *halves[:2])
        return [from_blk(part, i) for i, part in enumerate(parts_a)], keep, across(send, 0)

    def scatter_two(self, words, parts_a, keep_b, other_b, pages):
        count = self.count
        half = self.a // 2

        def body(words, ins, outs):
            bit = bit_of(words, 0)
            outs[0][...] = total_of(ins[:count], shard(bit, half)).astype(BF16)
            outs[1][...] = total_of(ins[:count], shard(1 - bit, half)).astype(BF16)
            part_b = total_of(ins[count : count + 2]).astype(BF16)
            outs[2][...] = part_b
            for i, out in enumerate(outs[3:]):
                out[: self.b] = part_b
                for page in range(len(pages)):
                    piece = ins[count + 2 + page * (count - 1) + i]
                    base = self.b + page * self.span
                    out[base : base + self.span, : piece.shape[1]] = piece[...]

        message = self.b + len(pages) * self.span
        shapes = self.shapes(half, half, self.b, *[message] * (count - 1))
        pieces = [piece for page in pages for piece in page[1:]]
        keep, send, part_b, *messages = local(
            body, "scatter_two", words, [*parts_a, keep_b, other_b, *pieces], shapes
        )
        return (
            keep,
            across(send, 0),
            part_b,
            [from_blk(item, i + 1) for i, item in enumerate(messages)],
        )

    def sum_b(self, words, part_b, messages):
        def body(words, ins, outs):
            terms = [ref[: self.b].astype(F32) for ref in ins]
            outs[0][...] = tree_sum(terms).astype(BF16)

        return local(body, "sum_b", words, [part_b, *messages], self.shapes(self.b))[0]

    def gather_b(self, words, part_b):
        for level in range(self.levels - 1, 0, -1):
            part_b = join_halves(words, level, part_b, across(part_b, level))
        return part_b, across(part_b, 0)


def gather_blk(part, cut, late=None):
    count = lax.axis_size("blk")
    if count != 4:
        return [(i, 0, from_blk(part, i)) for i in range(count)]
    one, two = swapped(part, 1), swapped(part, 2)
    if late is not None:
        one, two = after(late, (one, two))
    first, second = swapped(one[:cut], 2), swapped(two[cut:], 1)
    return [(0, 0, part), (1, 0, one), (2, 0, two), (3, 0, first), (3, cut, second)]


def with_core(pieces):
    return [(distance, base, from_core(item)) for distance, base, item in pieces]


SEGMENT = 256
SLOTS = 4


def widen_own(words, plan, pieces, halves_b, hidden):
    width = plan.width
    chunks = hidden // width
    pairs = chunks // 2
    per_matrix = width // SEGMENT
    arrays = [item for _, _, item in pieces] + list(halves_b)
    segments = []
    extras = []
    for at, (distance, base, item) in enumerate(pieces):
        stop = min(item.shape[0], plan.a_ff - base)
        for top in range(0, stop, SEGMENT):
            segments.append((at, top, min(SEGMENT, stop - top), distance, base + top))
        if base + item.shape[0] == plan.a:
            extras.append((at, distance))
    for at, item in enumerate(halves_b):
        for top in range(0, item.shape[0], SEGMENT):
            segments.append((len(pieces) + at, top, SEGMENT, None, top))

    def kernel(words_ref, *refs):
        ins = refs[: len(arrays)]
        joined_ref, expand_ref, reduce_ref, held, sems = refs[len(arrays) :]
        copies = []
        for index, (at, top, rows, distance, base) in enumerate(segments):
            slot = index % SLOTS
            if index >= SLOTS:
                copies[index - SLOTS].wait()
            part = ins[at][top : top + rows]
            held[slot, :rows] = part.astype(F32)
            if distance is None:
                half = ins[len(pieces)].shape[0]
                bit = bit_of(words_ref, 0)
                place = plan.rows_a + half * (bit if at == len(pieces) else 1 - bit) + base
            else:
                place = (words_ref[0] ^ distance) * plan.a_ff + base
            joined_ref[pl.ds(pl.multiple_of(place, SEGMENT), rows)] = part
            block = lax.div(place, SEGMENT)
            matrix = lax.div(block, per_matrix)
            row = (block - matrix * per_matrix) * SEGMENT
            chunk = (lax.div(matrix, 2) + words_ref[2] * pairs) % chunks
            column = pl.multiple_of(chunk * width, width)
            source = held.at[slot, :rows]
            to_expand = pltpu.make_async_copy(
                source,
                expand_ref.at[pl.ds(pl.multiple_of(row, SEGMENT), rows), pl.ds(column, width)],
                sems.at[slot],
            )
            to_reduce = pltpu.make_async_copy(
                source,
                reduce_ref.at[pl.ds(pl.multiple_of(column + row, SEGMENT), rows)],
                sems.at[slot],
            )
            is_expand = lax.rem(matrix, 2) == 0
            pl.when(is_expand)(to_expand.start)
            pl.when(jnp.logical_not(is_expand))(to_reduce.start)
            copies.append(to_reduce)
        for at, distance in extras:
            rows = shard(words_ref[0] ^ distance, plan.a_more, plan.rows)
            joined_ref[rows] = ins[at][ins[at].shape[0] - plan.a_more :]
        for copy in copies[-SLOTS:]:
            copy.wait()

    assert all(base % SEGMENT == 0 for *_, base in segments)
    vmem = pl.BlockSpec(memory_space=pltpu.VMEM)
    anywhere = pl.BlockSpec(memory_space=pl.ANY)
    return pl.pallas_call(
        kernel,
        in_specs=[pl.BlockSpec(memory_space=pltpu.SMEM)] + [vmem] * len(arrays),
        out_specs=[vmem, anywhere, anywhere],
        out_shape=[
            jax.ShapeDtypeStruct((plan.rows + plan.more, width), BF16),
            jax.ShapeDtypeStruct((width, hidden), F32),
            jax.ShapeDtypeStruct((hidden, width), F32),
        ],
        scratch_shapes=[
            pltpu.VMEM((SLOTS, SEGMENT, width), F32),
            pltpu.SemaphoreType.DMA((SLOTS,)),
        ],
        compiler_params=pltpu.CompilerParams(vmem_limit_bytes=VMEM_LIMIT),
        cost_estimate=pl.CostEstimate(
            flops=0, bytes_accessed=6 * hidden * width, transcendentals=0
        ),
        name="widen_own",
    )(words, *arrays)


def widen_other(words, joined, expand, reduce):
    width, hidden = expand.shape
    chunks = hidden // width
    pairs = chunks // 2

    def kernel(words_ref, half_ref, before_ref, before_too_ref, expand_ref, reduce_ref):
        expand_ref[...] = half_ref[:width].astype(F32)
        reduce_ref[...] = half_ref[width:].astype(F32)

    def place(s, words):
        return (s + (words[2] + 1) * pairs) % chunks

    anywhere = pl.BlockSpec(memory_space=pl.ANY)
    return pl.pallas_call(
        kernel,
        grid_spec=pltpu.PrefetchScalarGridSpec(
            num_scalar_prefetch=1,
            grid=(pairs,),
            in_specs=[
                pl.BlockSpec((2 * width, width), lambda s, words: (s, 0)),
                anywhere,
                anywhere,
            ],
            out_specs=[
                pl.BlockSpec((width, width), lambda s, words: (0, place(s, words))),
                pl.BlockSpec((width, width), lambda s, words: (place(s, words), 0)),
            ],
        ),
        out_shape=[
            jax.ShapeDtypeStruct((width, hidden), F32),
            jax.ShapeDtypeStruct((hidden, width), F32),
        ],
        input_output_aliases={2: 0, 3: 1},
        compiler_params=pltpu.CompilerParams(vmem_limit_bytes=VMEM_LIMIT),
        cost_estimate=pl.CostEstimate(
            flops=0, bytes_accessed=6 * hidden * width, transcendentals=0
        ),
        name="widen_other",
    )(words, joined, expand, reduce)


def finished(words, plan, heads, joined, side, before=()):
    count = plan.count
    span = plan.span
    width = plan.width
    half_rows = width // 2
    arrays = [item for _, _, item in heads]

    def kernel(words_ref, *refs):
        heads_refs, refs = refs[: len(heads)], refs[len(heads) :]
        extra_ref, refs = refs[0], refs[1 + len(before) :]
        outs, refs = refs[:5], refs[5:]
        gathered, wide, project, sems = refs
        rank = words_ref[0]
        half = words_ref[2] ^ side
        for ref, (distance, base, _) in zip(heads_refs, heads):
            rows = ref.shape[0]
            place = pl.multiple_of((rank ^ distance) * span, HEAD_DIM)
            for part in range(2):
                low, high = max(base, part * span), min(base + rows, (part + 1) * span)
                if low < high:
                    gathered[part, pl.ds(place + (low - part * span), high - low)] = ref[
                        low - base : high - base
                    ]
        for part in range(2):
            wide[part] = gathered[part, :width].astype(F32).T
        project[...] = extra_ref[:half_rows].astype(F32)

        @pl.when(half == 1)
        def _():
            wide[1] = entry_order(wide[1])

        def copy(source, target, at):
            return pltpu.make_async_copy(source, target, sems.at[at])

        for part in range(2):
            pl.when(half == 0)(copy(wide.at[part], outs[part], part).start)
            pl.when(half == 1)(copy(wide.at[part], outs[2 + part], part).start)
        rows = pl.ds(pl.multiple_of(half * half_rows, half_rows), half_rows)
        last = copy(project, outs[4].at[rows], 2)
        last.start()
        for part in range(2):
            copy(wide.at[part], outs[part], part).wait()
        last.wait()

    def whole(item):
        return pl.BlockSpec(item.shape, lambda s: (0, 0))

    more = pl.BlockSpec((plan.more, width), lambda s: (plan.rows // plan.more, 0))
    anywhere = pl.BlockSpec(memory_space=pl.ANY)
    first = 2 + len(heads)
    shapes = [jax.ShapeDtypeStruct((width, width), F32)] * 5
    return pl.pallas_call(
        kernel,
        grid=(1,),
        in_specs=[pl.BlockSpec(memory_space=pltpu.SMEM)]
        + [whole(item) for item in arrays]
        + [more]
        + [anywhere] * len(before),
        out_specs=[anywhere] * 5,
        out_shape=shapes,
        scratch_shapes=[
            pltpu.VMEM((2, count * span, width), BF16),
            pltpu.VMEM((2, width, width), F32),
            pltpu.VMEM((half_rows, width), F32),
            pltpu.SemaphoreType.DMA((3,)),
        ],
        input_output_aliases={first + at: at for at in range(len(before))},
        compiler_params=pltpu.CompilerParams(vmem_limit_bytes=VMEM_LIMIT),
        cost_estimate=pl.CostEstimate(
            flops=0, bytes_accessed=16 * width * width, transcendentals=0
        ),
        name="finish",
    )(words, *arrays, joined, *before)


def per_device(
    tokens,
    boxes,
    w_query,
    w_key,
    w_value,
    w_output,
    box_weight,
    first_gain,
    first_shift,
    w_expand,
    w_reduce,
    second_gain,
    second_shift,
    cotangent,
):
    pages, block, width = tokens.shape
    count = lax.axis_size("blk")
    depth = lax.axis_size("depth")
    words = jnp.stack(
        [lax.axis_index("blk"), lax.axis_index("depth"), lax.axis_index("core")]
    ).astype(jnp.int32)
    hidden = w_expand.shape[1]
    span = -(-HEADS // count) * HEAD_DIM
    unit = 16 * count * depth
    more = -(-(width // 2 + 16) // unit) * unit

    own_places = jnp.stack([boxes[0] + boxes[2], boxes[1] + boxes[3]], axis=1)
    own_places = jnp.stack([lax.shift_right_logical(own_places, 6), own_places & 63], axis=2)
    own_places = own_places.reshape(4 * pages, block).astype(BF16)
    own_places = jnp.pad(own_places, ((0, 16 - 4 * pages), (0, width - block)))
    message = jnp.concatenate([tokens[0], own_places])
    messages = [from_blk(message, i) for i in range(count)]
    w_own, box_own, rot_cos, rot_sin = prepare(
        words, w_query, w_key, w_value, box_weight, span, count * block
    )
    messages, rot_cos = lax.optimization_barrier((messages, rot_cos))
    own = after(messages, tokens[1])
    pieces = [messages, [from_blk(own, i) for i in range(count)]]

    saved = []
    att_parts = []
    for page in range(pages):
        results = attention_forward(
            words, page, messages, pieces[page], w_own, box_own, rot_cos, rot_sin
        )
        saved.append(results[:6])
        att_parts += [from_blk(results[6 + i], i) for i in range(count)]

    vectors = jnp.stack([first_gain, first_shift, second_gain, second_shift])
    results = middle(
        words,
        att_parts,
        tokens.reshape(pages * block, width),
        cotangent.reshape(pages * block, width),
        w_output,
        vectors,
        w_expand,
        w_reduce,
        pages,
        more,
    )
    layer_out, first_in, theirs, mine, more_theirs, more_mine = results[:6]
    grads = [from_blk(results[6 + i], i) for i in range(count)]
    plan = Plan(hidden, 2 * hidden // 3, more, span, width)
    parts_a, keep_b, other_b = plan.scatter_one(
        after(grads[:2], words), [mine, from_core(theirs), more_mine, from_core(more_theirs)]
    )

    def backward(page, words, before=None):
        return attention_backward(
            words,
            page,
            grads,
            pieces[page],
            saved[page],
            box_own,
            rot_cos,
            rot_sin,
            before,
        )

    *pre_one, before = backward(0, after(parts_a[0], words))
    done = before
    for level in range(1, plan.levels):
        keep_b, send_b = halve(after(done, words), level, keep_b, other_b)
        other_b = across(send_b, level)
        done = keep_b
    *pre_two, heads_mine, heads_theirs = backward(1, after(done, words), before)
    own = [pre_one[0], pre_two[0]]
    part_a, other_a, part_b, messages_b = plan.scatter_two(
        after(heads_mine, words), parts_a, keep_b, other_b, [pre_one, pre_two]
    )
    heads, other = halve(
        after(part_a, words), 0, heads_mine, from_core(after(part_a, heads_theirs))
    )
    part_a = pair_sum(after(heads, words), part_a, other_a)
    other = across(after(part_a, other), 0)
    heads = pair_sum(after(part_a, words), heads, other)
    done = heads
    for level in range(1, plan.levels):
        part_a = pair_sum(after(done, words), part_a, across(part_a, level))
        done = part_a
    other_a = across(part_a, 0)
    other = across(after(part_a, heads), 1)
    part_b = plan.sum_b(after(part_a, words), part_b, messages_b)
    heads = pair_sum(after(part_b, words), heads, other)
    part_a = join_halves(after(heads, words), 0, part_a, other_a)
    part_b = after(part_a, part_b)
    for level in range(2, plan.levels):
        heads = pair_sum(words, heads, across(heads, level))
    heads = join_halves(words, 0, heads, across(heads, 0))
    parts_b = plan.gather_b(after(heads, words), part_b)
    input_grad = input_gradient(
        after(parts_b[0], words),
        own,
        messages_b,
        plan.b,
        span,
        (w_query, w_key, w_value),
        first_in,
    )
    pieces_a = gather_blk(part_a, plan.a_ff // 2, input_grad)
    heads = after(([item for _, _, item in pieces_a], parts_b), heads)
    joined, *wide = widen_own(after(heads, words), plan, pieces_a, parts_b, hidden)
    pieces_heads = gather_blk(heads, span, joined)
    joined_other = from_core(after(pieces_heads[1][2], joined))
    grads = finished(words, plan, pieces_heads, joined, 0)
    at = plan.rows + width // 2
    sums = jnp.where(words[2] == 0, joined[at : at + 4], joined_other[at : at + 4])
    sums = [sums[i].astype(F32) for i in range(4)]
    grad_expand, grad_reduce = widen_other(after((sums, grads), words), joined_other, *wide)
    grad_query, grad_key, grad_value, grad_box, grad_project = finished(
        after(grad_expand, words), plan, with_core(pieces_heads), joined_other, 1, grads
    )
    return (
        layer_out.reshape(tokens.shape),
        input_grad.reshape(tokens.shape),
        grad_query,
        grad_key,
        grad_value,
        grad_project,
        grad_box,
        sums[0],
        sums[1],
        grad_expand,
        grad_reduce,
        sums[2],
        sums[3],
    )


def solution(mesh):
    blocks, rest = mesh.devices.shape
    parts = jax.sharding.Mesh(
        mesh.devices.reshape(blocks, rest // 2, 2), ("blk", "depth", "core")
    )
    split = P(("depth", "core"), "blk", None)
    return jax.shard_map(
        per_device,
        mesh=parts,
        in_specs=(split, P(None, ("depth", "core"), "blk")) + (P(),) * 11 + (split,),
        out_specs=(split, split) + (P(),) * 11,
        check_vma=False,
    )
```

```python
import functools

import jax
import jax.numpy as jnp
import numpy as np
from jax import lax
from jax.experimental import pallas as pl
from jax.experimental.pallas import tpu as pltpu
from jax.sharding import PartitionSpec as P

HEADS = 12
HEAD_DIM = 64
HALF = 32
FREQS = 192
CODES = 4 * FREQS
VMEM_LIMIT = 60 * 1024 * 1024
NO_COST = pl.CostEstimate(flops=0, bytes_accessed=0, transcendentals=0)
F32 = jnp.float32
BF16 = jnp.bfloat16


def dot(left, right):
    return lax.dot_general(left, right, (((1,), (0,)), ((), ())), preferred_element_type=F32)


def dot_nt(left, right):
    return lax.dot_general(left, right, (((1,), (1,)), ((), ())), preferred_element_type=F32)


def dot_tn(left, right):
    return lax.dot_general(left, right, (((0,), (0,)), ((), ())), preferred_element_type=F32)


def swapped(block, distance, axis="blk"):
    count = lax.axis_size(axis)
    return lax.ppermute(block, axis, [(i, i ^ distance) for i in range(count)])


def from_blk(block, distance):
    return swapped(block, distance) if distance else block


def from_core(block):
    return swapped(block, 1, "core")


def after(done, value):
    return lax.optimization_barrier((value, done))[0]


def turned(upper, lower, cosines, sines):
    return upper * cosines - lower * sines, lower * cosines + upper * sines


def entry_order(rows):
    return jnp.concatenate(
        [
            rows[:FREQS],
            rows[2 * FREQS : 3 * FREQS],
            rows[FREQS : 2 * FREQS],
            rows[3 * FREQS :],
        ],
        axis=0,
    )


def angle_tables():
    rates = np.float32(10000.0) ** (-np.arange(FREQS, dtype=np.float32) / np.float32(FREQS))
    tables = []
    for places in (32.0 * np.arange(32), 0.5 * np.arange(64)):
        angles = rates.astype(np.float64)[:, None] * places[None, :]
        left = np.concatenate([np.sin(angles), np.cos(angles)])
        parts = []
        for _ in range(3):
            parts.append(left.astype(jnp.bfloat16))
            left = left - parts[-1].astype(np.float64)
        tables.append(np.concatenate(parts, axis=1))
    return tables


def rotary_tables(length):
    rates = np.float32(10000.0) ** (-np.arange(HALF, dtype=np.float32) / np.float32(HALF))
    angles = np.arange(length, dtype=np.float32)[None, :] * rates[:, None]
    angles = angles.astype(np.float64)
    return np.cos(angles).astype(np.float32), np.sin(angles).astype(np.float32)


def prepare_kernel(
    words_ref,
    query_ref,
    key_ref,
    value_ref,
    box_ref,
    cos_ref,
    sin_ref,
    own_ref,
    own_box_ref,
    own_cos_ref,
    own_sin_ref,
):
    rank = words_ref[0]
    span = own_box_ref.shape[0]
    width = query_ref.shape[1]
    count = lax.axis_size("blk")
    block = cos_ref.shape[1] // count
    row = lax.broadcasted_iota(jnp.int32, (span, width), 0) + rank * span
    column = lax.broadcasted_iota(jnp.int32, (span, width), 1)
    pick = jnp.where(row == column, 1.0, 0.0).astype(BF16)
    for kind, ref in enumerate((query_ref, key_ref, value_ref)):
        own_ref[kind * span : (kind + 1) * span] = dot_nt(pick, ref[...]).astype(BF16)
    own_box_ref[...] = dot_nt(pick, entry_order(box_ref[...])).astype(BF16)
    for i in range(count):
        from_cols = pl.ds(pl.multiple_of((rank ^ i) * block, block), block)
        own_cos_ref[:, i * block : (i + 1) * block] = cos_ref[:, from_cols]
        own_sin_ref[:, i * block : (i + 1) * block] = sin_ref[:, from_cols]


def prepare(words, w_query, w_key, w_value, box_weight, span, length):
    width = w_query.shape[0]
    vmem = pl.BlockSpec(memory_space=pltpu.VMEM)
    return pl.pallas_call(
        prepare_kernel,
        in_specs=[pl.BlockSpec(memory_space=pltpu.SMEM)] + [vmem] * 6,
        out_specs=[vmem] * 4,
        out_shape=[
            jax.ShapeDtypeStruct((3 * span, width), BF16),
            jax.ShapeDtypeStruct((span, CODES), BF16),
            jax.ShapeDtypeStruct((HALF, length), F32),
            jax.ShapeDtypeStruct((HALF, length), F32),
        ],
        compiler_params=pltpu.CompilerParams(vmem_limit_bytes=VMEM_LIMIT),
        cost_estimate=pl.CostEstimate(
            flops=8 * span * width * width, bytes_accessed=10 * width * width, transcendentals=0
        ),
        name="prepare",
    )(words, w_query, w_key, w_value, box_weight, *map(jnp.asarray, rotary_tables(length)))


def fold(value, combine):
    while value.shape[0] > 8:
        half = value.shape[0] // 2
        value = combine(value[:half], value[half:])
    return value


def write_codes(page, place_refs, high_ref, low_ref, sin_ref, cos_ref, codes_ref):
    block = sin_ref.shape[1] // len(place_refs)

    def looked_up(table_ref, index):
        spots = table_ref.shape[1] // 3
        rows = lax.broadcasted_iota(jnp.int32, (spots, block), 0).astype(F32)
        once = jnp.where(rows == index, 1.0, 0.0)
        found = dot(table_ref[...], jnp.concatenate([once] * 3, axis=0).astype(BF16))
        return found[:FREQS], found[FREQS:]

    for i, place_ref in enumerate(place_refs):
        columns = slice(i * block, (i + 1) * block)
        places = place_ref[:, :block].astype(F32)
        for axis in range(2):
            at = 4 * page + 2 * axis
            high_sin, high_cos = looked_up(high_ref, places[at : at + 1])
            low_sin, low_cos = looked_up(low_ref, places[at + 1 : at + 2])
            sines = high_sin * low_cos + high_cos * low_sin
            cosines = high_cos * low_cos - high_sin * low_sin
            rows = slice(axis * FREQS, (axis + 1) * FREQS)
            later = slice((2 + axis) * FREQS, (3 + axis) * FREQS)
            sin_ref[rows, columns] = sines
            cos_ref[rows, columns] = cosines
            codes_ref[rows, columns] = sines.astype(BF16)
            codes_ref[later, columns] = cosines.astype(BF16)


def forward_kernel(page, count, words_ref, *refs):
    place_refs, refs = refs[:count], refs[count:]
    piece_refs, refs = refs[:count], refs[count:]
    high_ref, low_ref, w_ref, box_ref, rot_cos_ref, rot_sin_ref = refs[:6]
    probs_ref, att_ref, heads_ref, sin_ref, cos_ref, codes_ref = refs[6:12]
    low_refs = refs[12 : 12 + count]
    tok_ref, pre_ref, kc_ref, qr_ref = refs[12 + count :]
    rows = tok_ref.shape[0]
    block = rows // count
    head = pl.program_id(0)
    span = pl.num_programs(0) * HEAD_DIM

    @pl.when(head == 0)
    def _():
        for i in range(count):
            tok_ref[i * block : (i + 1) * block] = piece_refs[i][...]
        pre_ref[...] = dot_nt(w_ref[...], tok_ref[...])
        write_codes(page, place_refs, high_ref, low_ref, sin_ref, cos_ref, codes_ref)
        kc_ref[:, :CODES] = codes_ref[...].astype(F32).T.astype(BF16)

    def pre(kind):
        at = kind * span + head * HEAD_DIM
        return pre_ref[pl.ds(pl.multiple_of(at, HEAD_DIM), HEAD_DIM)]

    rot_cos = rot_cos_ref[...]
    rot_sin = rot_sin_ref[...]
    query_pre = pre(0).astype(BF16)
    wide = query_pre.astype(F32)
    query = jnp.concatenate(turned(wide[:HALF], wide[HALF:], rot_cos, rot_sin), axis=0)
    key_pre = pre(1)
    key = jnp.concatenate(turned(key_pre[:HALF], key_pre[HALF:], rot_cos, rot_sin), axis=0)
    value = pre(2).astype(BF16)
    heads_ref[0, :HEAD_DIM] = query_pre
    heads_ref[0, HEAD_DIM : 2 * HEAD_DIM] = query.astype(BF16)
    heads_ref[0, 2 * HEAD_DIM : 3 * HEAD_DIM] = key.astype(BF16)
    heads_ref[0, 3 * HEAD_DIM :] = value
    kc_ref[:, CODES:] = key.T.astype(BF16)
    qr_ref[CODES:] = (query * 0.125).astype(BF16)
    step = min(256, block)

    def logits_at(at):
        part = slice(at, at + step)
        projected = dot_tn(box_ref[...], query_pre[:, part])
        sines = sin_ref[:, part]
        cosines = cos_ref[:, part]
        upper = projected[: 2 * FREQS]
        lower = projected[2 * FREQS :]
        qr_ref[: 2 * FREQS, part] = ((upper * cosines + lower * sines) * 0.125).astype(BF16)
        qr_ref[2 * FREQS : CODES, part] = ((lower * cosines - upper * sines) * 0.125).astype(BF16)
        return dot(kc_ref[...], qr_ref[:, part])

    following = logits_at(0)
    for at in range(0, rows, step):
        logits = following
        if at + step < rows:
            following = logits_at(at + step)
        peak = jnp.max(fold(logits, jnp.maximum), axis=0, keepdims=True)
        weight = jnp.exp(logits - peak)
        total = jnp.sum(fold(weight, jnp.add), axis=0, keepdims=True)
        probs = (weight * (1.0 / total)).astype(BF16)
        probs_ref[0, :, at : at + step] = probs
        attended = dot(value, probs)
        att_ref[0, :, at : at + step] = attended
        inner = at % block
        low_refs[at // block][:, inner : inner + step] = attended.astype(BF16)


def fixed(array):
    return pl.BlockSpec(array.shape, lambda *at: (0,) * len(array.shape))


def attention_forward(words, page, messages, pieces, w_own, box_own, rot_cos, rot_sin):
    count = len(messages)
    block, width = messages[0].shape[0] - 16, messages[0].shape[1]
    rows = count * block
    span = box_own.shape[0]
    heads = span // HEAD_DIM
    tables = [jnp.asarray(item) for item in angle_tables()]
    specs = [pl.BlockSpec((block, width), lambda h, words: (0, 0))] * count
    places = pl.BlockSpec((16, width), lambda h, words: (block // 16, 0))
    out_shape = [
        jax.ShapeDtypeStruct((heads, rows, rows), BF16),
        jax.ShapeDtypeStruct((heads, HEAD_DIM, rows), F32),
        jax.ShapeDtypeStruct((heads, 4 * HEAD_DIM, rows), BF16),
        jax.ShapeDtypeStruct((2 * FREQS, rows), F32),
        jax.ShapeDtypeStruct((2 * FREQS, rows), F32),
        jax.ShapeDtypeStruct((CODES, rows), BF16),
    ] + [jax.ShapeDtypeStruct((span, block), BF16)] * count
    return pl.pallas_call(
        functools.partial(forward_kernel, page, count),
        grid_spec=pltpu.PrefetchScalarGridSpec(
            num_scalar_prefetch=1,
            grid=(heads,),
            in_specs=[places] * count
            + specs
            + [fixed(item) for item in (*tables, w_own)]
            + [
                pl.BlockSpec((HEAD_DIM, CODES), lambda h, words: (h, 0)),
                fixed(rot_cos),
                fixed(rot_sin),
            ],
            out_specs=[
                pl.BlockSpec((1, rows, rows), lambda h, words: (h, 0, 0)),
                pl.BlockSpec((1, HEAD_DIM, rows), lambda h, words: (h, 0, 0)),
                pl.BlockSpec((1, 4 * HEAD_DIM, rows), lambda h, words: (h, 0, 0)),
            ]
            + [fixed(item) for item in out_shape[3:6]]
            + [pl.BlockSpec((HEAD_DIM, block), lambda h, words: (h, 0))] * count,
            scratch_shapes=[
                pltpu.VMEM((rows, width), BF16),
                pltpu.VMEM((3 * span, rows), F32),
                pltpu.VMEM((rows, CODES + HEAD_DIM), BF16),
                pltpu.VMEM((CODES + HEAD_DIM, rows), BF16),
            ],
        ),
        out_shape=out_shape,
        compiler_params=pltpu.CompilerParams(vmem_limit_bytes=VMEM_LIMIT),
        cost_estimate=pl.CostEstimate(
            flops=2 * heads * rows * (rows * 1100 + 200 * width + 64 * CODES),
            bytes_accessed=2 * heads * rows * rows + 12 * rows * width,
            transcendentals=heads * rows * rows,
        ),
        name="attention_forward",
    )(words, *messages, *pieces, *tables, w_own, box_own, rot_cos, rot_sin)


def backward_kernel(count, last, words_ref, *refs):
    grad_refs, refs = refs[:count], refs[count:]
    piece_refs, refs = refs[:count], refs[count:]
    probs_ref, att_ref, heads_ref, box_ref, codes_ref, sin_ref, cos_ref = refs[:7]
    rot_cos_ref, rot_sin_ref = refs[7:9]
    refs = refs[9:]
    if last:
        before_ref, refs = refs[0], refs[1:]
    pre_refs, refs = refs[:count], refs[count:]
    if last:
        mine_ref, theirs_ref, *refs = refs
    weight_grad_ref, kc_ref, logit_grad_ref, entry_grad_ref, turned_ref = refs
    block, width = piece_refs[0].shape
    rows = count * block
    head = pl.program_id(0)
    span = pl.num_programs(0) * HEAD_DIM

    @pl.when(head == 0)
    def _():
        kc_ref[:CODES] = codes_ref[...]

    kc_ref[CODES:] = heads_ref[0, 2 * HEAD_DIM : 3 * HEAD_DIM]
    packed = heads_ref[0].astype(F32).T.astype(BF16)
    query_pre = packed[:, :HEAD_DIM]
    query = packed[:, HEAD_DIM : 2 * HEAD_DIM]
    value = packed[:, 3 * HEAD_DIM :] * jnp.asarray(0.125, BF16)
    rot_cos = rot_cos_ref[...]
    rot_sin = rot_sin_ref[...]
    grad = jnp.concatenate([ref[...] for ref in grad_refs], axis=1)
    grad_tall = grad.astype(F32).T.astype(BF16)
    offsets = jnp.sum(grad.astype(F32) * att_ref[0], axis=0, keepdims=True) * 0.125
    step = min(256, block)
    place = pl.multiple_of(head * HEAD_DIM, HEAD_DIM)
    here = pl.ds(place, HEAD_DIM)

    def logits_back(at):
        part = slice(at, at + step)
        grad_probs = dot(value, grad[:, part])
        logit_grad_ref[:, part] = (
            probs_ref[0, :, part].astype(F32) * (grad_probs - offsets[:, part])
        ).astype(BF16)

    logits_back(0)
    for at in range(0, rows, step):
        if at + step < rows:
            logits_back(at + step)
        part = slice(at, at + step)
        back = dot(kc_ref[...], logit_grad_ref[:, part])
        sines = sin_ref[:, part]
        cosines = cos_ref[:, part]
        upper = back[: 2 * FREQS]
        lower = back[2 * FREQS : CODES]
        entry_grad_ref[: 2 * FREQS, part] = (upper * cosines - lower * sines).astype(BF16)
        entry_grad_ref[2 * FREQS :, part] = (lower * cosines + upper * sines).astype(BF16)
        first = back[CODES : CODES + HALF]
        second = back[CODES + HALF :]
        turned_ref[:HALF, part], turned_ref[HALF:, part] = turned(
            first, second, rot_cos[:, part], -rot_sin[:, part]
        )
    key_flat = dot(logit_grad_ref[...], query).T
    value_low = dot(probs_ref[0], grad_tall).T.astype(BF16)
    query_low = (turned_ref[...] + dot(box_ref[...], entry_grad_ref[...])).astype(BF16)
    key_low = jnp.concatenate(
        turned(key_flat[:HALF], key_flat[HALF:], rot_cos, -rot_sin), axis=0
    ).astype(BF16)
    for i in range(count):
        columns = slice(i * block, (i + 1) * block)
        pre_refs[i][here, :block] = query_low[:, columns]
        pre_refs[i][here, block : 2 * block] = key_low[:, columns]
        pre_refs[i][here, 2 * block :] = value_low[:, columns]
    weight_grad_ref[pl.ds(3 * span + place, HEAD_DIM)] = dot(entry_grad_ref[...], query_pre).T

    @pl.when(head == pl.num_programs(0) - 1)
    def _():
        for kind in range(3):
            columns = slice(kind * block, (kind + 1) * block)
            total = dot(pre_refs[0][:, columns], piece_refs[0][...])
            for i in range(1, count):
                total = total + dot(pre_refs[i][:, columns], piece_refs[i][...])
            weight_grad_ref[kind * span : (kind + 1) * span] = total
        if last:
            half = 2 * span
            core = words_ref[2]
            ours = pl.ds(pl.multiple_of(core * half, half), half)
            there = pl.ds(pl.multiple_of((1 - core) * half, half), half)
            mine_ref[...] = weight_grad_ref[ours] + before_ref[ours]
            theirs_ref[...] = (weight_grad_ref[there] + before_ref[there]).astype(BF16)


def attention_backward(
    words, page, grads, pieces, saved, box_own, rot_cos, rot_sin, before=None
):
    probs, att, heads_saved, sines, cosines, codes = saved
    count = len(pieces)
    rows, width = probs.shape[1], pieces[0].shape[1]
    block = rows // count
    span = box_own.shape[0]
    heads = span // HEAD_DIM
    last = before is not None
    extra = (before,) if last else ()
    full_shape = (4 * span, width)
    specs = [pl.BlockSpec((block, width), lambda h, words: (0, 0))] * count
    out_shape = [jax.ShapeDtypeStruct((span, 3 * block), BF16)] * count
    if last:
        out_shape += [
            jax.ShapeDtypeStruct((2 * span, width), F32),
            jax.ShapeDtypeStruct((2 * span, width), BF16),
        ]
    else:
        out_shape.append(jax.ShapeDtypeStruct(full_shape, F32))
    return pl.pallas_call(
        functools.partial(backward_kernel, count, last),
        grid_spec=pltpu.PrefetchScalarGridSpec(
            num_scalar_prefetch=1,
            grid=(heads,),
            in_specs=[pl.BlockSpec((HEAD_DIM, block), lambda h, words: (h, page))] * count
            + specs
            + [
                pl.BlockSpec((1, rows, rows), lambda h, words: (h, 0, 0)),
                pl.BlockSpec((1, HEAD_DIM, rows), lambda h, words: (h, 0, 0)),
                pl.BlockSpec((1, 4 * HEAD_DIM, rows), lambda h, words: (h, 0, 0)),
                pl.BlockSpec((HEAD_DIM, CODES), lambda h, words: (h, 0)),
            ]
            + [fixed(item) for item in (codes, sines, cosines, rot_cos, rot_sin, *extra)],
            out_specs=[fixed(item) for item in out_shape],
            scratch_shapes=([pltpu.VMEM(full_shape, F32)] if last else [])
            + [
                pltpu.VMEM((CODES + HEAD_DIM, rows), BF16),
                pltpu.VMEM((rows, rows), BF16),
                pltpu.VMEM((CODES, rows), BF16),
                pltpu.VMEM((HEAD_DIM, rows), F32),
            ],
        ),
        out_shape=out_shape,
        compiler_params=pltpu.CompilerParams(vmem_limit_bytes=VMEM_LIMIT),
        cost_estimate=pl.CostEstimate(
            flops=2 * heads * rows * (rows * 1400 + 200 * width + 128 * CODES),
            bytes_accessed=2 * heads * rows * rows + 12 * rows * width,
            transcendentals=0,
        ),
        name="attention_backward",
    )(
        words,
        *grads,
        *pieces,
        probs,
        att,
        heads_saved,
        box_own,
        codes,
        sines,
        cosines,
        rot_cos,
        rot_sin,
        *extra,
    )


def normed(value):
    centered = value - jnp.mean(value, axis=-1, keepdims=True)
    scale = lax.rsqrt(jnp.mean(centered * centered, axis=-1, keepdims=True) + 1e-05)
    return centered * scale, scale


def norm_back(grad, gain, unit, scale):
    scaled = grad * gain
    return scale * (
        scaled
        - jnp.mean(scaled, axis=-1, keepdims=True)
        - unit * jnp.mean(scaled * unit, axis=-1, keepdims=True)
    )


def column_sum(value):
    return jnp.sum(value, axis=0, keepdims=True)


def middle_kernel(pages, count, span, chunks, *refs):
    total = pages * count
    words_ref = refs[0]
    att_refs = refs[1 : 1 + total]
    (
        tok_ref,
        cot_ref,
        w_out_ref,
        vectors_ref,
        w_expand_ref,
        w_reduce_ref,
    ) = refs[1 + total : 7 + total]
    outs = refs[7 + total :]
    layer_ref, first_in_ref, theirs_ref, mine_ref, more_theirs_ref, more_mine_ref = outs[:6]
    grad_refs = outs[6 : 6 + count]
    (
        sums_ref,
        att_all,
        grad_all,
        unit_one,
        scale_one,
        first_wide,
        first_low,
        first_tall,
        active,
        slope,
        gathered,
        second_in,
        second_low,
    ) = outs[6 + count :]
    rank = words_ref[0]
    width = tok_ref.shape[1]
    block = tok_ref.shape[0] // pages
    step = pl.program_id(0)

    def rows_of(at):
        return pl.ds(pl.multiple_of((rank ^ at) * span, span), span)

    @pl.when(step == 0)
    def _():
        for page in range(pages):
            for at in range(count):
                att_all[rows_of(at), page * block : (page + 1) * block] = att_refs[
                    page * count + at
                ][...]
        branch = dot_tn(att_all[: w_out_ref.shape[0]], w_out_ref[...])
        unit, scale = normed(tok_ref[...].astype(F32) + branch)
        unit_one[...] = unit
        scale_one[...] = jnp.broadcast_to(scale, scale_one.shape)
        first_out = unit * vectors_ref[0:1] + vectors_ref[1:2]
        first_wide[...] = first_out
        first_low[...] = first_out.astype(BF16)
        first_tall[...] = first_out.T.astype(BF16)
        gathered[...] = jnp.zeros_like(gathered)
        sums_ref[...] = jnp.zeros_like(sums_ref)

    for chunk in range(chunks):

        @pl.when(step == chunk)
        def _(chunk=chunk):
            expanded = dot(first_low[...], w_expand_ref[...])
            gate = 0.5 + 0.5 * lax.erf(expanded * np.float32(np.sqrt(0.5)))
            bell = jnp.exp(expanded * expanded * -0.5) * np.float32(1.0 / np.sqrt(2.0 * np.pi))
            low = (expanded * gate).astype(BF16)
            active[chunk] = low
            slope[chunk] = gate + expanded * bell
            gathered[...] += dot(low, w_reduce_ref[...])

    @pl.when(step == chunks - 1)
    def _():
        unit, scale = normed(first_wide[...] + gathered[...])
        layer_ref[...] = (unit * vectors_ref[2:3] + vectors_ref[3:4]).astype(BF16)
        cot = cot_ref[...].astype(F32)
        sums_ref[2:3] = column_sum(cot * unit)
        sums_ref[3:4] = column_sum(cot)
        grad = norm_back(cot, vectors_ref[2:3], unit, scale)
        second_in[...] = grad
        second_low[...] = grad.astype(BF16)
        gathered[...] = grad

    for chunk in range(chunks):

        @pl.when(step == 2 * chunks - 1 - chunk)
        def _(chunk=chunk):
            grad_active = dot_nt(second_low[...], w_reduce_ref[...])
            grad_expanded = (grad_active * slope[chunk]).astype(BF16)
            grads_ref = mine_ref if chunk < chunks // 2 else theirs_ref
            grads_ref[:width] = dot(first_tall[...], grad_expanded).astype(BF16)
            grads_ref[width:] = dot_tn(active[chunk], second_low[...]).astype(BF16)
            gathered[...] += dot_nt(grad_expanded, w_expand_ref[...])

    @pl.when(step == 2 * chunks - 1)
    def _():
        unit = unit_one[...]
        grad_out = gathered[...]
        sums_ref[0:1] = column_sum(grad_out * unit)
        sums_ref[1:2] = column_sum(grad_out)
        grad = norm_back(grad_out, vectors_ref[0:1], unit, scale_one[:, :1])
        first_in_ref[...] = grad
        low = grad.astype(BF16)
        real = w_out_ref.shape[0]
        half = real // 2
        core = words_ref[2]
        for ref, side in ((more_mine_ref, core), (more_theirs_ref, 1 - core)):
            rows = pl.ds(pl.multiple_of(side * half, half), half)
            ref[:half] = dot(att_all[rows], low).astype(BF16)
            ref[half:] = jnp.zeros((ref.shape[0] - half, width), BF16)
            ref[half : half + 16] = sums_ref[...].astype(BF16)
        if grad_all.shape[0] > real:
            grad_all[real:] = jnp.zeros((grad_all.shape[0] - real, low.shape[0]), BF16)
        grad_all[:real] = dot_nt(w_out_ref[...], low).astype(BF16)
        for at in range(count):
            grad_refs[at][...] = grad_all[rows_of(at)]


def middle(words, att_parts, tok, cot, w_out, vectors, w_expand, w_reduce, pages, more):
    rows, width = tok.shape
    count = len(att_parts) // pages
    span, block = att_parts[0].shape
    hidden = w_expand.shape[1]
    chunks = hidden // width
    pairs = chunks // 2

    def whole(array):
        return pl.BlockSpec(array.shape, lambda s, words: (0,) * len(array.shape))

    def chunk_at(s, words):
        at = jnp.minimum(s, 2 * chunks - 1 - s)
        return (at + words[2] * pairs) % chunks

    def theirs_at(s, words):
        return jnp.clip(2 * chunks - 1 - s - pairs, 0, pairs - 1), 0

    def mine_at(s, words):
        return jnp.clip(2 * chunks - 1 - s, 0, pairs - 1), 0

    shapes = [
        jax.ShapeDtypeStruct((rows, width), BF16),
        jax.ShapeDtypeStruct((rows, width), F32),
        jax.ShapeDtypeStruct((hidden, width), BF16),
        jax.ShapeDtypeStruct((hidden, width), BF16),
        jax.ShapeDtypeStruct((more, width), BF16),
        jax.ShapeDtypeStruct((more, width), BF16),
    ] + [jax.ShapeDtypeStruct((span, pages * block), BF16)] * count
    specs = [whole(item) for item in shapes]
    specs[2] = pl.BlockSpec((2 * width, width), theirs_at)
    specs[3] = pl.BlockSpec((2 * width, width), mine_at)
    return pl.pallas_call(
        functools.partial(middle_kernel, pages, count, span, chunks),
        grid_spec=pltpu.PrefetchScalarGridSpec(
            num_scalar_prefetch=1,
            grid=(2 * chunks,),
            in_specs=[whole(item) for item in att_parts]
            + [
                whole(tok),
                whole(cot),
                whole(w_out),
                whole(vectors),
                pl.BlockSpec((width, width), lambda s, words: (0, chunk_at(s, words))),
                pl.BlockSpec((width, width), lambda s, words: (chunk_at(s, words), 0)),
            ],
            out_specs=specs,
            scratch_shapes=[
                pltpu.VMEM((16, width), F32),
                pltpu.VMEM((count * span, rows), BF16),
                pltpu.VMEM((count * span, rows), BF16),
                pltpu.VMEM((rows, width), F32),
                pltpu.VMEM((rows, 128), F32),
                pltpu.VMEM((rows, width), F32),
                pltpu.VMEM((rows, width), BF16),
                pltpu.VMEM((width, rows), BF16),
                pltpu.VMEM((chunks, rows, width), BF16),
                pltpu.VMEM((chunks, rows, width), F32),
                pltpu.VMEM((rows, width), F32),
                pltpu.VMEM((rows, width), F32),
                pltpu.VMEM((rows, width), BF16),
            ],
        ),
        out_shape=shapes,
        compiler_params=pltpu.CompilerParams(vmem_limit_bytes=VMEM_LIMIT),
        cost_estimate=pl.CostEstimate(
            flops=2 * rows * width * (6 * hidden + 3 * width),
            bytes_accessed=8 * width * hidden + 16 * rows * width,
            transcendentals=2 * rows * hidden,
        ),
        name="middle",
    )(words, *att_parts, tok, cot, w_out, vectors, w_expand, w_reduce)


def input_kernel(pages, count, span, base, *refs):
    words_ref = refs[0]
    own_refs = refs[1 : 1 + pages]
    message_refs = refs[1 + pages : pages + count]
    weight_refs = refs[pages + count : 3 + pages + count]
    first_in_ref, out_ref, held = refs[3 + pages + count :]
    rank = words_ref[0]
    width = out_ref.shape[1]
    block = out_ref.shape[0] // pages
    for page in range(pages):
        for at in range(count):
            part = message_refs[at - 1] if at else own_refs[page]
            top = base + page * span if at else 0
            place = pl.multiple_of((rank ^ at) * span, span)
            for kind in range(3):
                held[kind, pl.ds(place, span), page * block : (page + 1) * block] = part[
                    top : top + span, kind * block : (kind + 1) * block
                ]
    total = dot(weight_refs[0][...], held[0, :width])
    for kind in range(1, 3):
        total = total + dot(weight_refs[kind][...], held[kind, :width])
    out_ref[...] = (first_in_ref[...] + total.T).astype(BF16)


def input_gradient(words, own, messages, base, span, weights, first_in):
    pages = len(own)
    count = 1 + len(messages)
    rows, width = first_in.shape
    vmem = pl.BlockSpec(memory_space=pltpu.VMEM)
    return pl.pallas_call(
        functools.partial(input_kernel, pages, count, span, base),
        in_specs=[pl.BlockSpec(memory_space=pltpu.SMEM)] + [vmem] * (pages + count + 3),
        out_specs=vmem,
        out_shape=jax.ShapeDtypeStruct((rows, width), BF16),
        scratch_shapes=[pltpu.VMEM((3, count * span, rows), BF16)],
        compiler_params=pltpu.CompilerParams(vmem_limit_bytes=VMEM_LIMIT),
        cost_estimate=pl.CostEstimate(
            flops=6 * rows * width * count * span,
            bytes_accessed=2 * width * (5 * rows + 3 * count * span),
            transcendentals=0,
        ),
        name="input_gradient",
    )(words, *own, *messages, *weights, first_in)


def local(body, name, words, arrays, shapes, costly=False):
    def kernel(words_ref, *refs):
        body(words_ref, refs[: len(arrays)], refs[len(arrays) :])

    vmem = pl.BlockSpec(memory_space=pltpu.VMEM)
    shapes = [jax.ShapeDtypeStruct(shape, kind) for shape, kind in shapes]
    moved = sum(item.size * item.dtype.itemsize for item in list(arrays) + shapes)
    cost = pl.CostEstimate(flops=0, bytes_accessed=moved, transcendentals=0)
    return pl.pallas_call(
        kernel,
        in_specs=[pl.BlockSpec(memory_space=pltpu.SMEM)] + [vmem] * len(arrays),
        out_specs=[vmem] * len(shapes),
        out_shape=shapes,
        compiler_params=pltpu.CompilerParams(vmem_limit_bytes=VMEM_LIMIT),
        cost_estimate=cost if costly else NO_COST,
        name=name,
    )(words, *arrays)


def shard(index, rows, base=0):
    return pl.ds(pl.multiple_of(base + index * rows, 16), rows)


def total_of(refs, rows=slice(None)):
    if len(refs) == 2 and all(ref.dtype == BF16 for ref in refs):
        return refs[0][rows] + refs[1][rows]
    total = refs[0][rows].astype(F32)
    for ref in refs[1:]:
        total = total + ref[rows].astype(F32)
    return total


def tree_sum(terms):
    while len(terms) > 1:
        terms = [terms[i] + terms[i + 1] for i in range(0, len(terms), 2)]
    return terms[0]


def bit_of(words, level):
    return lax.shift_right_logical(words[1], level) & 1


def pair_sum(words, mine, other):
    def body(words, ins, outs):
        outs[0][...] = total_of(ins).astype(BF16)

    return local(body, "pair_sum", words, [mine, other], [(mine.shape, BF16)])[0]


def halve(words, level, mine, other):
    rows, width = mine.shape
    half = rows // 2

    def body(words, ins, outs):
        bit = bit_of(words, level)
        outs[0][...] = total_of(ins, shard(bit, half)).astype(BF16)
        outs[1][...] = total_of(ins, shard(1 - bit, half)).astype(BF16)

    return local(body, "halve", words, [mine, other], [((half, width), BF16)] * 2)


def join_halves(words, level, mine, other):
    rows, width = mine.shape

    def body(words, ins, outs):
        bit = bit_of(words, level)
        outs[0][shard(bit, rows)] = ins[0][...]
        outs[0][shard(1 - bit, rows)] = ins[1][...]

    return local(body, "join_halves", words, [mine, other], [((2 * rows, width), BF16)])[0]


def across(block, level):
    return swapped(block, 1 << level, "depth")


class Plan:
    def __init__(self, rows, rows_a, more, span, width):
        self.count = lax.axis_size("blk")
        self.levels = lax.axis_size("depth").bit_length() - 1
        self.rows = rows
        self.rows_a = rows_a
        self.more = more
        self.span = span
        self.width = width
        self.a_ff = rows_a // self.count
        self.a_more = more // self.count
        self.a = self.a_ff + self.a_more
        self.b = (rows - rows_a) >> self.levels

    def shapes(self, *sizes):
        return [((rows, self.width), BF16) for rows in sizes]

    def scatter_one(self, words, halves):
        count, width = self.count, self.width
        a_ff, a_more = self.a_ff, self.a_more
        b_rows = (self.rows - self.rows_a) // count
        steps = count // 2

        def kernel(words_ref, *refs):
            parts = refs[6 : 6 + count]
            keep_ref, send_ref = refs[6 + count :]
            for i in range(count):

                @pl.when(pl.program_id(0) == i)
                def _(i=i):
                    parts[i][:a_ff] = total_of(refs[:2]).astype(BF16)
                    parts[i][a_ff:] = total_of(refs[2:4]).astype(BF16)
                    side = send_ref if i < steps else keep_ref
                    side[...] = total_of(refs[4:6]).astype(BF16)

        def there(rows):
            return pl.BlockSpec((rows, width), lambda i, words: (words[0] ^ i, 0))

        def b_at(i, words):
            bit = bit_of(words, 0)
            side = jnp.where(i < steps, 1 - bit, bit)
            return self.rows_a // b_rows + side * steps + i % steps, 0

        own_b = pl.BlockSpec((b_rows, width), b_at)
        shapes = [jax.ShapeDtypeStruct((self.a, width), BF16)] * count
        shapes += [jax.ShapeDtypeStruct((b_rows * steps, width), BF16)] * 2
        *parts_a, keep, send = pl.pallas_call(
            kernel,
            grid_spec=pltpu.PrefetchScalarGridSpec(
                num_scalar_prefetch=1,
                grid=(count,),
                in_specs=[there(a_ff)] * 2 + [there(a_more)] * 2 + [own_b] * 2,
                out_specs=[fixed(item) for item in shapes[:count]]
                + [
                    pl.BlockSpec((b_rows, width), lambda i, words: (jnp.maximum(i - steps, 0), 0)),
                    pl.BlockSpec((b_rows, width), lambda i, words: (jnp.minimum(i, steps - 1), 0)),
                ],
            ),
            out_shape=shapes,
            compiler_params=pltpu.CompilerParams(vmem_limit_bytes=VMEM_LIMIT),
            cost_estimate=NO_COST,
            name="scatter_one",
        )(words, *halves, *halves[:2])
        return [from_blk(part, i) for i, part in enumerate(parts_a)], keep, across(send, 0)

    def scatter_two(self, words, parts_a, keep_b, other_b, pages):
        count = self.count
        half = self.a // 2

        def body(words, ins, outs):
            bit = bit_of(words, 0)
            outs[0][...] = total_of(ins[:count], shard(bit, half)).astype(BF16)
            outs[1][...] = total_of(ins[:count], shard(1 - bit, half)).astype(BF16)
            part_b = total_of(ins[count : count + 2]).astype(BF16)
            outs[2][...] = part_b
            for i, out in enumerate(outs[3:]):
                out[: self.b] = part_b
                for page in range(len(pages)):
                    piece = ins[count + 2 + page * (count - 1) + i]
                    base = self.b + page * self.span
                    out[base : base + self.span, : piece.shape[1]] = piece[...]

        message = self.b + len(pages) * self.span
        shapes = self.shapes(half, half, self.b, *[message] * (count - 1))
        pieces = [piece for page in pages for piece in page[1:]]
        keep, send, part_b, *messages = local(
            body, "scatter_two", words, [*parts_a, keep_b, other_b, *pieces], shapes
        )
        return (
            keep,
            across(send, 0),
            part_b,
            [from_blk(item, i + 1) for i, item in enumerate(messages)],
        )

    def sum_b(self, words, part_b, messages):
        def body(words, ins, outs):
            terms = [ref[: self.b].astype(F32) for ref in ins]
            outs[0][...] = tree_sum(terms).astype(BF16)

        return local(body, "sum_b", words, [part_b, *messages], self.shapes(self.b))[0]

    def gather_b(self, words, part_b):
        for level in range(self.levels - 1, 0, -1):
            part_b = join_halves(words, level, part_b, across(part_b, level))
        return part_b, across(part_b, 0)


def gather_blk(part, cut, late=None):
    count = lax.axis_size("blk")
    if count != 4:
        return [(i, 0, from_blk(part, i)) for i in range(count)]
    one, two = swapped(part, 1), swapped(part, 2)
    if late is not None:
        one, two = after(late, (one, two))
    first, second = swapped(one[:cut], 2), swapped(two[cut:], 1)
    return [(0, 0, part), (1, 0, one), (2, 0, two), (3, 0, first), (3, cut, second)]


def with_core(pieces):
    return [(distance, base, from_core(item)) for distance, base, item in pieces]


SEGMENT = 256
SLOTS = 4


def widen_own(words, plan, pieces, halves_b, hidden):
    width = plan.width
    chunks = hidden // width
    pairs = chunks // 2
    per_matrix = width // SEGMENT
    arrays = [item for _, _, item in pieces] + list(halves_b)
    segments = []
    extras = []
    for at, (distance, base, item) in enumerate(pieces):
        stop = min(item.shape[0], plan.a_ff - base)
        for top in range(0, stop, SEGMENT):
            segments.append((at, top, min(SEGMENT, stop - top), distance, base + top))
        if base + item.shape[0] == plan.a:
            extras.append((at, distance))
    for at, item in enumerate(halves_b):
        for top in range(0, item.shape[0], SEGMENT):
            segments.append((len(pieces) + at, top, SEGMENT, None, top))

    def kernel(words_ref, *refs):
        ins = refs[: len(arrays)]
        joined_ref, expand_ref, reduce_ref, held, sems = refs[len(arrays) :]
        copies = []
        for index, (at, top, rows, distance, base) in enumerate(segments):
            slot = index % SLOTS
            if index >= SLOTS:
                copies[index - SLOTS].wait()
            part = ins[at][top : top + rows]
            held[slot, :rows] = part.astype(F32)
            if distance is None:
                half = ins[len(pieces)].shape[0]
                bit = bit_of(words_ref, 0)
                place = plan.rows_a + half * (bit if at == len(pieces) else 1 - bit) + base
            else:
                place = (words_ref[0] ^ distance) * plan.a_ff + base
            joined_ref[pl.ds(pl.multiple_of(place, SEGMENT), rows)] = part
            block = lax.div(place, SEGMENT)
            matrix = lax.div(block, per_matrix)
            row = (block - matrix * per_matrix) * SEGMENT
            chunk = (lax.div(matrix, 2) + words_ref[2] * pairs) % chunks
            column = pl.multiple_of(chunk * width, width)
            source = held.at[slot, :rows]
            to_expand = pltpu.make_async_copy(
                source,
                expand_ref.at[pl.ds(pl.multiple_of(row, SEGMENT), rows), pl.ds(column, width)],
                sems.at[slot],
            )
            to_reduce = pltpu.make_async_copy(
                source,
                reduce_ref.at[pl.ds(pl.multiple_of(column + row, SEGMENT), rows)],
                sems.at[slot],
            )
            is_expand = lax.rem(matrix, 2) == 0
            pl.when(is_expand)(to_expand.start)
            pl.when(jnp.logical_not(is_expand))(to_reduce.start)
            copies.append(to_reduce)
        for at, distance in extras:
            rows = shard(words_ref[0] ^ distance, plan.a_more, plan.rows)
            joined_ref[rows] = ins[at][ins[at].shape[0] - plan.a_more :]
        for copy in copies[-SLOTS:]:
            copy.wait()

    assert all(base % SEGMENT == 0 for *_, base in segments)
    vmem = pl.BlockSpec(memory_space=pltpu.VMEM)
    anywhere = pl.BlockSpec(memory_space=pl.ANY)
    return pl.pallas_call(
        kernel,
        in_specs=[pl.BlockSpec(memory_space=pltpu.SMEM)] + [vmem] * len(arrays),
        out_specs=[vmem, anywhere, anywhere],
        out_shape=[
            jax.ShapeDtypeStruct((plan.rows + plan.more, width), BF16),
            jax.ShapeDtypeStruct((width, hidden), F32),
            jax.ShapeDtypeStruct((hidden, width), F32),
        ],
        scratch_shapes=[
            pltpu.VMEM((SLOTS, SEGMENT, width), F32),
            pltpu.SemaphoreType.DMA((SLOTS,)),
        ],
        compiler_params=pltpu.CompilerParams(vmem_limit_bytes=VMEM_LIMIT),
        cost_estimate=pl.CostEstimate(
            flops=0, bytes_accessed=6 * hidden * width, transcendentals=0
        ),
        name="widen_own",
    )(words, *arrays)


def widen_other(words, joined, expand, reduce):
    width, hidden = expand.shape
    chunks = hidden // width
    pairs = chunks // 2

    def kernel(words_ref, half_ref, before_ref, before_too_ref, expand_ref, reduce_ref):
        expand_ref[...] = half_ref[:width].astype(F32)
        reduce_ref[...] = half_ref[width:].astype(F32)

    def place(s, words):
        return (s + (words[2] + 1) * pairs) % chunks

    anywhere = pl.BlockSpec(memory_space=pl.ANY)
    return pl.pallas_call(
        kernel,
        grid_spec=pltpu.PrefetchScalarGridSpec(
            num_scalar_prefetch=1,
            grid=(pairs,),
            in_specs=[
                pl.BlockSpec((2 * width, width), lambda s, words: (s, 0)),
                anywhere,
                anywhere,
            ],
            out_specs=[
                pl.BlockSpec((width, width), lambda s, words: (0, place(s, words))),
                pl.BlockSpec((width, width), lambda s, words: (place(s, words), 0)),
            ],
        ),
        out_shape=[
            jax.ShapeDtypeStruct((width, hidden), F32),
            jax.ShapeDtypeStruct((hidden, width), F32),
        ],
        input_output_aliases={2: 0, 3: 1},
        compiler_params=pltpu.CompilerParams(vmem_limit_bytes=VMEM_LIMIT),
        cost_estimate=pl.CostEstimate(
            flops=0, bytes_accessed=6 * hidden * width, transcendentals=0
        ),
        name="widen_other",
    )(words, joined, expand, reduce)


def finished(words, plan, heads, joined, side, before=()):
    count = plan.count
    span = plan.span
    width = plan.width
    half_rows = width // 2
    arrays = [item for _, _, item in heads]

    def kernel(words_ref, *refs):
        heads_refs, refs = refs[: len(heads)], refs[len(heads) :]
        extra_ref, refs = refs[0], refs[1 + len(before) :]
        outs, refs = refs[:5], refs[5:]
        gathered, wide, project, sems = refs
        rank = words_ref[0]
        half = words_ref[2] ^ side
        for ref, (distance, base, _) in zip(heads_refs, heads):
            rows = ref.shape[0]
            place = pl.multiple_of((rank ^ distance) * span, HEAD_DIM)
            for part in range(2):
                low, high = max(base, part * span), min(base + rows, (part + 1) * span)
                if low < high:
                    gathered[part, pl.ds(place + (low - part * span), high - low)] = ref[
                        low - base : high - base
                    ]
        for part in range(2):
            wide[part] = gathered[part, :width].astype(F32).T
        project[...] = extra_ref[:half_rows].astype(F32)

        @pl.when(half == 1)
        def _():
            wide[1] = entry_order(wide[1])

        def copy(source, target, at):
            return pltpu.make_async_copy(source, target, sems.at[at])

        for part in range(2):
            pl.when(half == 0)(copy(wide.at[part], outs[part], part).start)
            pl.when(half == 1)(copy(wide.at[part], outs[2 + part], part).start)
        rows = pl.ds(pl.multiple_of(half * half_rows, half_rows), half_rows)
        last = copy(project, outs[4].at[rows], 2)
        last.start()
        for part in range(2):
            copy(wide.at[part], outs[part], part).wait()
        last.wait()

    def whole(item):
        return pl.BlockSpec(item.shape, lambda s: (0, 0))

    more = pl.BlockSpec((plan.more, width), lambda s: (plan.rows // plan.more, 0))
    anywhere = pl.BlockSpec(memory_space=pl.ANY)
    first = 2 + len(heads)
    shapes = [jax.ShapeDtypeStruct((width, width), F32)] * 5
    return pl.pallas_call(
        kernel,
        grid=(1,),
        in_specs=[pl.BlockSpec(memory_space=pltpu.SMEM)]
        + [whole(item) for item in arrays]
        + [more]
        + [anywhere] * len(before),
        out_specs=[anywhere] * 5,
        out_shape=shapes,
        scratch_shapes=[
            pltpu.VMEM((2, count * span, width), BF16),
            pltpu.VMEM((2, width, width), F32),
            pltpu.VMEM((half_rows, width), F32),
            pltpu.SemaphoreType.DMA((3,)),
        ],
        input_output_aliases={first + at: at for at in range(len(before))},
        compiler_params=pltpu.CompilerParams(vmem_limit_bytes=VMEM_LIMIT),
        cost_estimate=pl.CostEstimate(
            flops=0, bytes_accessed=16 * width * width, transcendentals=0
        ),
        name="finish",
    )(words, *arrays, joined, *before)


def per_device(
    tokens,
    boxes,
    w_query,
    w_key,
    w_value,
    w_output,
    box_weight,
    first_gain,
    first_shift,
    w_expand,
    w_reduce,
    second_gain,
    second_shift,
    cotangent,
):
    pages, block, width = tokens.shape
    count = lax.axis_size("blk")
    depth = lax.axis_size("depth")
    words = jnp.stack(
        [lax.axis_index("blk"), lax.axis_index("depth"), lax.axis_index("core")]
    ).astype(jnp.int32)
    hidden = w_expand.shape[1]
    span = -(-HEADS // count) * HEAD_DIM
    unit = 16 * count * depth
    more = -(-(width // 2 + 16) // unit) * unit

    own_places = jnp.stack([boxes[0] + boxes[2], boxes[1] + boxes[3]], axis=1)
    own_places = jnp.stack([lax.shift_right_logical(own_places, 6), own_places & 63], axis=2)
    own_places = own_places.reshape(4 * pages, block).astype(BF16)
    own_places = jnp.pad(own_places, ((0, 16 - 4 * pages), (0, width - block)))
    message = jnp.concatenate([tokens[0], own_places])
    messages = [from_blk(message, i) for i in range(count)]
    w_own, box_own, rot_cos, rot_sin = prepare(
        words, w_query, w_key, w_value, box_weight, span, count * block
    )
    messages, rot_cos = lax.optimization_barrier((messages, rot_cos))
    own = after(messages, tokens[1])
    pieces = [messages, [from_blk(own, i) for i in range(count)]]

    saved = []
    att_parts = []
    for page in range(pages):
        results = attention_forward(
            words, page, messages, pieces[page], w_own, box_own, rot_cos, rot_sin
        )
        saved.append(results[:6])
        att_parts += [from_blk(results[6 + i], i) for i in range(count)]

    vectors = jnp.stack([first_gain, first_shift, second_gain, second_shift])
    results = middle(
        words,
        att_parts,
        tokens.reshape(pages * block, width),
        cotangent.reshape(pages * block, width),
        w_output,
        vectors,
        w_expand,
        w_reduce,
        pages,
        more,
    )
    layer_out, first_in, theirs, mine, more_theirs, more_mine = results[:6]
    grads = [from_blk(results[6 + i], i) for i in range(count)]
    plan = Plan(hidden, 2 * hidden // 3, more, span, width)
    parts_a, keep_b, other_b = plan.scatter_one(
        after(grads[:2], words), [mine, from_core(theirs), more_mine, from_core(more_theirs)]
    )

    def backward(page, words, before=None):
        return attention_backward(
            words,
            page,
            grads,
            pieces[page],
            saved[page],
            box_own,
            rot_cos,
            rot_sin,
            before,
        )

    *pre_one, before = backward(0, after(parts_a[0], words))
    done = before
    for level in range(1, plan.levels):
        keep_b, send_b = halve(after(done, words), level, keep_b, other_b)
        other_b = across(send_b, level)
        done = keep_b
    *pre_two, heads_mine, heads_theirs = backward(1, after(done, words), before)
    own = [pre_one[0], pre_two[0]]
    part_a, other_a, part_b, messages_b = plan.scatter_two(
        after(heads_mine, words), parts_a, keep_b, other_b, [pre_one, pre_two]
    )
    heads, other = halve(
        after(part_a, words), 0, heads_mine, from_core(after(part_a, heads_theirs))
    )
    part_a = pair_sum(after(heads, words), part_a, other_a)
    other = across(after(part_a, other), 0)
    heads = pair_sum(after(part_a, words), heads, other)
    done = heads
    for level in range(1, plan.levels):
        part_a = pair_sum(after(done, words), part_a, across(part_a, level))
        done = part_a
    other_a = across(part_a, 0)
    other = across(heads, 1)
    part_b = plan.sum_b(after(part_a, words), part_b, messages_b)
    heads = pair_sum(after(part_b, words), heads, other)
    part_a = join_halves(after(heads, words), 0, part_a, other_a)
    part_b = after(part_a, part_b)
    for level in range(2, plan.levels):
        heads = pair_sum(words, heads, across(heads, level))
    input_grad = input_gradient(
        after(part_a, words),
        own,
        messages_b,
        plan.b,
        span,
        (w_query, w_key, w_value),
        first_in,
    )
    heads = join_halves(after(input_grad, words), 0, heads, across(heads, 0))
    parts_b = plan.gather_b(after(heads, words), part_b)
    pieces_a = gather_blk(part_a, plan.a_ff // 2, parts_b[0])
    heads = after(([item for _, _, item in pieces_a], parts_b), heads)
    joined, *wide = widen_own(after(heads, words), plan, pieces_a, parts_b, hidden)
    at = plan.rows + width // 2
    sums = [joined[at + i].astype(F32) for i in range(4)]
    pieces_heads = gather_blk(heads, span, (joined, sums))
    joined_other = from_core(after(pieces_heads[1][2], joined))
    grads = finished(words, plan, pieces_heads, joined, 0)
    grad_expand, grad_reduce = widen_other(after(grads, words), joined_other, *wide)
    grad_query, grad_key, grad_value, grad_box, grad_project = finished(
        after(grad_expand, words), plan, with_core(pieces_heads), joined_other, 1, grads
    )
    return (
        layer_out.reshape(tokens.shape),
        input_grad.reshape(tokens.shape),
        grad_query,
        grad_key,
        grad_value,
        grad_project,
        grad_box,
        sums[0],
        sums[1],
        grad_expand,
        grad_reduce,
        sums[2],
        sums[3],
    )


def solution(mesh):
    blocks, rest = mesh.devices.shape
    parts = jax.sharding.Mesh(
        mesh.devices.reshape(blocks, rest // 2, 2), ("blk", "depth", "core")
    )
    split = P(("depth", "core"), "blk", None)
    return jax.shard_map(
        per_device,
        mesh=parts,
        in_specs=(split, P(None, ("depth", "core"), "blk")) + (P(),) * 11 + (split,),
        out_specs=(split, split) + (P(),) * 11,
        check_vma=False,
    )
```

```python
import functools

import jax
import jax.numpy as jnp
import numpy as np
from jax import lax
from jax.experimental import pallas as pl
from jax.experimental.pallas import tpu as pltpu
from jax.sharding import PartitionSpec as P

HEADS = 12
HEAD_DIM = 64
HALF = 32
FREQS = 192
CODES = 4 * FREQS
VMEM_LIMIT = 60 * 1024 * 1024
NO_COST = pl.CostEstimate(flops=0, bytes_accessed=0, transcendentals=0)
F32 = jnp.float32
BF16 = jnp.bfloat16


def dot(left, right):
    return lax.dot_general(left, right, (((1,), (0,)), ((), ())), preferred_element_type=F32)


def dot_nt(left, right):
    return lax.dot_general(left, right, (((1,), (1,)), ((), ())), preferred_element_type=F32)


def dot_tn(left, right):
    return lax.dot_general(left, right, (((0,), (0,)), ((), ())), preferred_element_type=F32)


def swapped(block, distance, axis="blk"):
    count = lax.axis_size(axis)
    return lax.ppermute(block, axis, [(i, i ^ distance) for i in range(count)])


def from_blk(block, distance):
    return swapped(block, distance) if distance else block


def from_core(block):
    return swapped(block, 1, "core")


def after(done, value):
    return lax.optimization_barrier((value, done))[0]


def turned(upper, lower, cosines, sines):
    return upper * cosines - lower * sines, lower * cosines + upper * sines


def entry_order(rows):
    return jnp.concatenate(
        [
            rows[:FREQS],
            rows[2 * FREQS : 3 * FREQS],
            rows[FREQS : 2 * FREQS],
            rows[3 * FREQS :],
        ],
        axis=0,
    )


def angle_tables():
    rates = np.float32(10000.0) ** (-np.arange(FREQS, dtype=np.float32) / np.float32(FREQS))
    tables = []
    for places in (32.0 * np.arange(32), 0.5 * np.arange(64)):
        angles = rates.astype(np.float64)[:, None] * places[None, :]
        left = np.concatenate([np.sin(angles), np.cos(angles)])
        parts = []
        for _ in range(3):
            parts.append(left.astype(jnp.bfloat16))
            left = left - parts[-1].astype(np.float64)
        tables.append(np.concatenate(parts, axis=1))
    return tables


def rotary_tables(length):
    rates = np.float32(10000.0) ** (-np.arange(HALF, dtype=np.float32) / np.float32(HALF))
    angles = np.arange(length, dtype=np.float32)[None, :] * rates[:, None]
    angles = angles.astype(np.float64)
    return np.cos(angles).astype(np.float32), np.sin(angles).astype(np.float32)


def prepare_kernel(
    words_ref,
    query_ref,
    key_ref,
    value_ref,
    box_ref,
    cos_ref,
    sin_ref,
    own_ref,
    own_box_ref,
    own_cos_ref,
    own_sin_ref,
):
    rank = words_ref[0]
    span = own_box_ref.shape[0]
    width = query_ref.shape[1]
    count = lax.axis_size("blk")
    block = cos_ref.shape[1] // count
    row = lax.broadcasted_iota(jnp.int32, (span, width), 0) + rank * span
    column = lax.broadcasted_iota(jnp.int32, (span, width), 1)
    pick = jnp.where(row == column, 1.0, 0.0).astype(BF16)
    for kind, ref in enumerate((query_ref, key_ref, value_ref)):
        own_ref[kind * span : (kind + 1) * span] = dot_nt(pick, ref[...]).astype(BF16)
    own_box_ref[...] = dot_nt(pick, entry_order(box_ref[...])).astype(BF16)
    for i in range(count):
        from_cols = pl.ds(pl.multiple_of((rank ^ i) * block, block), block)
        own_cos_ref[:, i * block : (i + 1) * block] = cos_ref[:, from_cols]
        own_sin_ref[:, i * block : (i + 1) * block] = sin_ref[:, from_cols]


def prepare(words, w_query, w_key, w_value, box_weight, span, length):
    width = w_query.shape[0]
    vmem = pl.BlockSpec(memory_space=pltpu.VMEM)
    return pl.pallas_call(
        prepare_kernel,
        in_specs=[pl.BlockSpec(memory_space=pltpu.SMEM)] + [vmem] * 6,
        out_specs=[vmem] * 4,
        out_shape=[
            jax.ShapeDtypeStruct((3 * span, width), BF16),
            jax.ShapeDtypeStruct((span, CODES), BF16),
            jax.ShapeDtypeStruct((HALF, length), F32),
            jax.ShapeDtypeStruct((HALF, length), F32),
        ],
        compiler_params=pltpu.CompilerParams(vmem_limit_bytes=VMEM_LIMIT),
        cost_estimate=pl.CostEstimate(
            flops=8 * span * width * width, bytes_accessed=10 * width * width, transcendentals=0
        ),
        name="prepare",
    )(words, w_query, w_key, w_value, box_weight, *map(jnp.asarray, rotary_tables(length)))


def fold(value, combine):
    while value.shape[0] > 8:
        half = value.shape[0] // 2
        value = combine(value[:half], value[half:])
    return value


def write_codes(page, place_refs, high_ref, low_ref, sin_ref, cos_ref, codes_ref):
    block = sin_ref.shape[1] // len(place_refs)

    def looked_up(table_ref, index):
        spots = table_ref.shape[1] // 3
        rows = lax.broadcasted_iota(jnp.int32, (spots, block), 0).astype(F32)
        once = jnp.where(rows == index, 1.0, 0.0)
        found = dot(table_ref[...], jnp.concatenate([once] * 3, axis=0).astype(BF16))
        return found[:FREQS], found[FREQS:]

    for i, place_ref in enumerate(place_refs):
        columns = slice(i * block, (i + 1) * block)
        places = place_ref[:, :block].astype(F32)
        for axis in range(2):
            at = 4 * page + 2 * axis
            high_sin, high_cos = looked_up(high_ref, places[at : at + 1])
            low_sin, low_cos = looked_up(low_ref, places[at + 1 : at + 2])
            sines = high_sin * low_cos + high_cos * low_sin
            cosines = high_cos * low_cos - high_sin * low_sin
            rows = slice(axis * FREQS, (axis + 1) * FREQS)
            later = slice((2 + axis) * FREQS, (3 + axis) * FREQS)
            sin_ref[rows, columns] = sines
            cos_ref[rows, columns] = cosines
            codes_ref[rows, columns] = sines.astype(BF16)
            codes_ref[later, columns] = cosines.astype(BF16)


def forward_kernel(page, count, words_ref, *refs):
    place_refs, refs = refs[:count], refs[count:]
    piece_refs, refs = refs[:count], refs[count:]
    high_ref, low_ref, w_ref, box_ref, rot_cos_ref, rot_sin_ref = refs[:6]
    probs_ref, att_ref, heads_ref, sin_ref, cos_ref, codes_ref = refs[6:12]
    low_refs = refs[12 : 12 + count]
    tok_ref, pre_ref, kc_ref, qr_ref = refs[12 + count :]
    rows = tok_ref.shape[0]
    block = rows // count
    head = pl.program_id(0)
    span = pl.num_programs(0) * HEAD_DIM

    @pl.when(head == 0)
    def _():
        for i in range(count):
            tok_ref[i * block : (i + 1) * block] = piece_refs[i][...]
        pre_ref[...] = dot_nt(w_ref[...], tok_ref[...])
        write_codes(page, place_refs, high_ref, low_ref, sin_ref, cos_ref, codes_ref)
        kc_ref[:, :CODES] = codes_ref[...].astype(F32).T.astype(BF16)

    def pre(kind):
        at = kind * span + head * HEAD_DIM
        return pre_ref[pl.ds(pl.multiple_of(at, HEAD_DIM), HEAD_DIM)]

    rot_cos = rot_cos_ref[...]
    rot_sin = rot_sin_ref[...]
    query_pre = pre(0).astype(BF16)
    wide = query_pre.astype(F32)
    query = jnp.concatenate(turned(wide[:HALF], wide[HALF:], rot_cos, rot_sin), axis=0)
    key_pre = pre(1)
    key = jnp.concatenate(turned(key_pre[:HALF], key_pre[HALF:], rot_cos, rot_sin), axis=0)
    value = pre(2).astype(BF16)
    heads_ref[0, :HEAD_DIM] = query_pre
    heads_ref[0, HEAD_DIM : 2 * HEAD_DIM] = query.astype(BF16)
    heads_ref[0, 2 * HEAD_DIM : 3 * HEAD_DIM] = key.astype(BF16)
    heads_ref[0, 3 * HEAD_DIM :] = value
    kc_ref[:, CODES:] = key.T.astype(BF16)
    qr_ref[CODES:] = (query * 0.125).astype(BF16)
    step = min(256, block)

    def logits_at(at):
        part = slice(at, at + step)
        projected = dot_tn(box_ref[...], query_pre[:, part])
        sines = sin_ref[:, part]
        cosines = cos_ref[:, part]
        upper = projected[: 2 * FREQS]
        lower = projected[2 * FREQS :]
        qr_ref[: 2 * FREQS, part] = ((upper * cosines + lower * sines) * 0.125).astype(BF16)
        qr_ref[2 * FREQS : CODES, part] = ((lower * cosines - upper * sines) * 0.125).astype(BF16)
        return dot(kc_ref[...], qr_ref[:, part])

    following = logits_at(0)
    for at in range(0, rows, step):
        logits = following
        if at + step < rows:
            following = logits_at(at + step)
        peak = jnp.max(fold(logits, jnp.maximum), axis=0, keepdims=True)
        weight = jnp.exp(logits - peak)
        total = jnp.sum(fold(weight, jnp.add), axis=0, keepdims=True)
        probs = (weight * (1.0 / total)).astype(BF16)
        probs_ref[0, :, at : at + step] = probs
        attended = dot(value, probs)
        att_ref[0, :, at : at + step] = attended
        inner = at % block
        low_refs[at // block][:, inner : inner + step] = attended.astype(BF16)


def fixed(array):
    return pl.BlockSpec(array.shape, lambda *at: (0,) * len(array.shape))


def attention_forward(words, page, messages, pieces, w_own, box_own, rot_cos, rot_sin):
    count = len(messages)
    block, width = messages[0].shape[0] - 16, messages[0].shape[1]
    rows = count * block
    span = box_own.shape[0]
    heads = span // HEAD_DIM
    tables = [jnp.asarray(item) for item in angle_tables()]
    specs = [pl.BlockSpec((block, width), lambda h, words: (0, 0))] * count
    places = pl.BlockSpec((16, width), lambda h, words: (block // 16, 0))
    out_shape = [
        jax.ShapeDtypeStruct((heads, rows, rows), BF16),
        jax.ShapeDtypeStruct((heads, HEAD_DIM, rows), F32),
        jax.ShapeDtypeStruct((heads, 4 * HEAD_DIM, rows), BF16),
        jax.ShapeDtypeStruct((2 * FREQS, rows), F32),
        jax.ShapeDtypeStruct((2 * FREQS, rows), F32),
        jax.ShapeDtypeStruct((CODES, rows), BF16),
    ] + [jax.ShapeDtypeStruct((span, block), BF16)] * count
    return pl.pallas_call(
        functools.partial(forward_kernel, page, count),
        grid_spec=pltpu.PrefetchScalarGridSpec(
            num_scalar_prefetch=1,
            grid=(heads,),
            in_specs=[places] * count
            + specs
            + [fixed(item) for item in (*tables, w_own)]
            + [
                pl.BlockSpec((HEAD_DIM, CODES), lambda h, words: (h, 0)),
                fixed(rot_cos),
                fixed(rot_sin),
            ],
            out_specs=[
                pl.BlockSpec((1, rows, rows), lambda h, words: (h, 0, 0)),
                pl.BlockSpec((1, HEAD_DIM, rows), lambda h, words: (h, 0, 0)),
                pl.BlockSpec((1, 4 * HEAD_DIM, rows), lambda h, words: (h, 0, 0)),
            ]
            + [fixed(item) for item in out_shape[3:6]]
            + [pl.BlockSpec((HEAD_DIM, block), lambda h, words: (h, 0))] * count,
            scratch_shapes=[
                pltpu.VMEM((rows, width), BF16),
                pltpu.VMEM((3 * span, rows), F32),
                pltpu.VMEM((rows, CODES + HEAD_DIM), BF16),
                pltpu.VMEM((CODES + HEAD_DIM, rows), BF16),
            ],
        ),
        out_shape=out_shape,
        compiler_params=pltpu.CompilerParams(vmem_limit_bytes=VMEM_LIMIT),
        cost_estimate=pl.CostEstimate(
            flops=2 * heads * rows * (rows * 1100 + 200 * width + 64 * CODES),
            bytes_accessed=2 * heads * rows * rows + 12 * rows * width,
            transcendentals=heads * rows * rows,
        ),
        name="attention_forward",
    )(words, *messages, *pieces, *tables, w_own, box_own, rot_cos, rot_sin)


def backward_kernel(count, last, words_ref, *refs):
    grad_refs, refs = refs[:count], refs[count:]
    piece_refs, refs = refs[:count], refs[count:]
    probs_ref, att_ref, heads_ref, box_ref, codes_ref, sin_ref, cos_ref = refs[:7]
    rot_cos_ref, rot_sin_ref = refs[7:9]
    refs = refs[9:]
    if last:
        before_ref, refs = refs[0], refs[1:]
    pre_refs, refs = refs[:count], refs[count:]
    if last:
        mine_ref, theirs_ref, *refs = refs
    weight_grad_ref, kc_ref, logit_grad_ref, entry_grad_ref, turned_ref = refs
    block, width = piece_refs[0].shape
    rows = count * block
    head = pl.program_id(0)
    span = pl.num_programs(0) * HEAD_DIM

    @pl.when(head == 0)
    def _():
        kc_ref[:CODES] = codes_ref[...]

    kc_ref[CODES:] = heads_ref[0, 2 * HEAD_DIM : 3 * HEAD_DIM]
    packed = heads_ref[0].astype(F32).T.astype(BF16)
    query_pre = packed[:, :HEAD_DIM]
    query = packed[:, HEAD_DIM : 2 * HEAD_DIM]
    value = packed[:, 3 * HEAD_DIM :] * jnp.asarray(0.125, BF16)
    rot_cos = rot_cos_ref[...]
    rot_sin = rot_sin_ref[...]
    grad = jnp.concatenate([ref[...] for ref in grad_refs], axis=1)
    grad_tall = grad.astype(F32).T.astype(BF16)
    offsets = jnp.sum(grad.astype(F32) * att_ref[0], axis=0, keepdims=True) * 0.125
    step = min(256, block)
    place = pl.multiple_of(head * HEAD_DIM, HEAD_DIM)
    here = pl.ds(place, HEAD_DIM)

    def logits_back(at):
        part = slice(at, at + step)
        grad_probs = dot(value, grad[:, part])
        logit_grad_ref[:, part] = (
            probs_ref[0, :, part].astype(F32) * (grad_probs - offsets[:, part])
        ).astype(BF16)

    logits_back(0)
    for at in range(0, rows, step):
        if at + step < rows:
            logits_back(at + step)
        part = slice(at, at + step)
        back = dot(kc_ref[...], logit_grad_ref[:, part])
        sines = sin_ref[:, part]
        cosines = cos_ref[:, part]
        upper = back[: 2 * FREQS]
        lower = back[2 * FREQS : CODES]
        entry_grad_ref[: 2 * FREQS, part] = (upper * cosines - lower * sines).astype(BF16)
        entry_grad_ref[2 * FREQS :, part] = (lower * cosines + upper * sines).astype(BF16)
        first = back[CODES : CODES + HALF]
        second = back[CODES + HALF :]
        turned_ref[:HALF, part], turned_ref[HALF:, part] = turned(
            first, second, rot_cos[:, part], -rot_sin[:, part]
        )
    key_flat = dot(logit_grad_ref[...], query).T
    value_low = dot(probs_ref[0], grad_tall).T.astype(BF16)
    query_low = (turned_ref[...] + dot(box_ref[...], entry_grad_ref[...])).astype(BF16)
    key_low = jnp.concatenate(
        turned(key_flat[:HALF], key_flat[HALF:], rot_cos, -rot_sin), axis=0
    ).astype(BF16)
    for i in range(count):
        columns = slice(i * block, (i + 1) * block)
        pre_refs[i][here, :block] = query_low[:, columns]
        pre_refs[i][here, block : 2 * block] = key_low[:, columns]
        pre_refs[i][here, 2 * block :] = value_low[:, columns]
    weight_grad_ref[pl.ds(3 * span + place, HEAD_DIM)] = dot(entry_grad_ref[...], query_pre).T

    @pl.when(head == pl.num_programs(0) - 1)
    def _():
        for kind in range(3):
            columns = slice(kind * block, (kind + 1) * block)
            total = dot(pre_refs[0][:, columns], piece_refs[0][...])
            for i in range(1, count):
                total = total + dot(pre_refs[i][:, columns], piece_refs[i][...])
            weight_grad_ref[kind * span : (kind + 1) * span] = total
        if last:
            half = 2 * span
            core = words_ref[2]
            ours = pl.ds(pl.multiple_of(core * half, half), half)
            there = pl.ds(pl.multiple_of((1 - core) * half, half), half)
            mine_ref[...] = weight_grad_ref[ours] + before_ref[ours]
            theirs_ref[...] = (weight_grad_ref[there] + before_ref[there]).astype(BF16)


def attention_backward(
    words, page, grads, pieces, saved, box_own, rot_cos, rot_sin, before=None
):
    probs, att, heads_saved, sines, cosines, codes = saved
    count = len(pieces)
    rows, width = probs.shape[1], pieces[0].shape[1]
    block = rows // count
    span = box_own.shape[0]
    heads = span // HEAD_DIM
    last = before is not None
    extra = (before,) if last else ()
    full_shape = (4 * span, width)
    specs = [pl.BlockSpec((block, width), lambda h, words: (0, 0))] * count
    out_shape = [jax.ShapeDtypeStruct((span, 3 * block), BF16)] * count
    if last:
        out_shape += [
            jax.ShapeDtypeStruct((2 * span, width), F32),
            jax.ShapeDtypeStruct((2 * span, width), BF16),
        ]
    else:
        out_shape.append(jax.ShapeDtypeStruct(full_shape, F32))
    return pl.pallas_call(
        functools.partial(backward_kernel, count, last),
        grid_spec=pltpu.PrefetchScalarGridSpec(
            num_scalar_prefetch=1,
            grid=(heads,),
            in_specs=[pl.BlockSpec((HEAD_DIM, block), lambda h, words: (h, page))] * count
            + specs
            + [
                pl.BlockSpec((1, rows, rows), lambda h, words: (h, 0, 0)),
                pl.BlockSpec((1, HEAD_DIM, rows), lambda h, words: (h, 0, 0)),
                pl.BlockSpec((1, 4 * HEAD_DIM, rows), lambda h, words: (h, 0, 0)),
                pl.BlockSpec((HEAD_DIM, CODES), lambda h, words: (h, 0)),
            ]
            + [fixed(item) for item in (codes, sines, cosines, rot_cos, rot_sin, *extra)],
            out_specs=[fixed(item) for item in out_shape],
            scratch_shapes=([pltpu.VMEM(full_shape, F32)] if last else [])
            + [
                pltpu.VMEM((CODES + HEAD_DIM, rows), BF16),
                pltpu.VMEM((rows, rows), BF16),
                pltpu.VMEM((CODES, rows), BF16),
                pltpu.VMEM((HEAD_DIM, rows), F32),
            ],
        ),
        out_shape=out_shape,
        compiler_params=pltpu.CompilerParams(vmem_limit_bytes=VMEM_LIMIT),
        cost_estimate=pl.CostEstimate(
            flops=2 * heads * rows * (rows * 1400 + 200 * width + 128 * CODES),
            bytes_accessed=2 * heads * rows * rows + 12 * rows * width,
            transcendentals=0,
        ),
        name="attention_backward",
    )(
        words,
        *grads,
        *pieces,
        probs,
        att,
        heads_saved,
        box_own,
        codes,
        sines,
        cosines,
        rot_cos,
        rot_sin,
        *extra,
    )


def normed(value):
    centered = value - jnp.mean(value, axis=-1, keepdims=True)
    scale = lax.rsqrt(jnp.mean(centered * centered, axis=-1, keepdims=True) + 1e-05)
    return centered * scale, scale


def norm_back(grad, gain, unit, scale):
    scaled = grad * gain
    return scale * (
        scaled
        - jnp.mean(scaled, axis=-1, keepdims=True)
        - unit * jnp.mean(scaled * unit, axis=-1, keepdims=True)
    )


def column_sum(value):
    return jnp.sum(value, axis=0, keepdims=True)


def middle_kernel(pages, count, span, chunks, *refs):
    total = pages * count
    words_ref = refs[0]
    att_refs = refs[1 : 1 + total]
    (
        tok_ref,
        cot_ref,
        w_out_ref,
        vectors_ref,
        w_expand_ref,
        w_reduce_ref,
    ) = refs[1 + total : 7 + total]
    outs = refs[7 + total :]
    layer_ref, first_in_ref, theirs_ref, mine_ref, more_theirs_ref, more_mine_ref = outs[:6]
    grad_refs = outs[6 : 6 + count]
    (
        sums_ref,
        att_all,
        grad_all,
        unit_one,
        scale_one,
        first_wide,
        first_low,
        first_tall,
        active,
        slope,
        gathered,
        second_in,
        second_low,
    ) = outs[6 + count :]
    rank = words_ref[0]
    width = tok_ref.shape[1]
    block = tok_ref.shape[0] // pages
    step = pl.program_id(0)

    def rows_of(at):
        return pl.ds(pl.multiple_of((rank ^ at) * span, span), span)

    @pl.when(step == 0)
    def _():
        for page in range(pages):
            for at in range(count):
                att_all[rows_of(at), page * block : (page + 1) * block] = att_refs[
                    page * count + at
                ][...]
        branch = dot_tn(att_all[: w_out_ref.shape[0]], w_out_ref[...])
        unit, scale = normed(tok_ref[...].astype(F32) + branch)
        unit_one[...] = unit
        scale_one[...] = jnp.broadcast_to(scale, scale_one.shape)
        first_out = unit * vectors_ref[0:1] + vectors_ref[1:2]
        first_wide[...] = first_out
        first_low[...] = first_out.astype(BF16)
        first_tall[...] = first_out.T.astype(BF16)
        gathered[...] = jnp.zeros_like(gathered)
        sums_ref[...] = jnp.zeros_like(sums_ref)

    for chunk in range(chunks):

        @pl.when(step == chunk)
        def _(chunk=chunk):
            expanded = dot(first_low[...], w_expand_ref[...])
            gate = 0.5 + 0.5 * lax.erf(expanded * np.float32(np.sqrt(0.5)))
            bell = jnp.exp(expanded * expanded * -0.5) * np.float32(1.0 / np.sqrt(2.0 * np.pi))
            low = (expanded * gate).astype(BF16)
            active[chunk] = low
            slope[chunk] = gate + expanded * bell
            gathered[...] += dot(low, w_reduce_ref[...])

    @pl.when(step == chunks - 1)
    def _():
        unit, scale = normed(first_wide[...] + gathered[...])
        layer_ref[...] = (unit * vectors_ref[2:3] + vectors_ref[3:4]).astype(BF16)
        cot = cot_ref[...].astype(F32)
        sums_ref[2:3] = column_sum(cot * unit)
        sums_ref[3:4] = column_sum(cot)
        grad = norm_back(cot, vectors_ref[2:3], unit, scale)
        second_in[...] = grad
        second_low[...] = grad.astype(BF16)
        gathered[...] = grad

    for chunk in range(chunks):

        @pl.when(step == 2 * chunks - 1 - chunk)
        def _(chunk=chunk):
            grad_active = dot_nt(second_low[...], w_reduce_ref[...])
            grad_expanded = (grad_active * slope[chunk]).astype(BF16)
            grads_ref = mine_ref if chunk < chunks // 2 else theirs_ref
            grads_ref[:width] = dot(first_tall[...], grad_expanded).astype(BF16)
            grads_ref[width:] = dot_tn(active[chunk], second_low[...]).astype(BF16)
            gathered[...] += dot_nt(grad_expanded, w_expand_ref[...])

    @pl.when(step == 2 * chunks - 1)
    def _():
        unit = unit_one[...]
        grad_out = gathered[...]
        sums_ref[0:1] = column_sum(grad_out * unit)
        sums_ref[1:2] = column_sum(grad_out)
        grad = norm_back(grad_out, vectors_ref[0:1], unit, scale_one[:, :1])
        first_in_ref[...] = grad
        low = grad.astype(BF16)
        real = w_out_ref.shape[0]
        half = real // 2
        core = words_ref[2]
        for ref, side in ((more_mine_ref, core), (more_theirs_ref, 1 - core)):
            rows = pl.ds(pl.multiple_of(side * half, half), half)
            ref[:half] = dot(att_all[rows], low).astype(BF16)
            ref[half:] = jnp.zeros((ref.shape[0] - half, width), BF16)
            ref[half : half + 16] = sums_ref[...].astype(BF16)
        if grad_all.shape[0] > real:
            grad_all[real:] = jnp.zeros((grad_all.shape[0] - real, low.shape[0]), BF16)
        grad_all[:real] = dot_nt(w_out_ref[...], low).astype(BF16)
        for at in range(count):
            grad_refs[at][...] = grad_all[rows_of(at)]


def middle(words, att_parts, tok, cot, w_out, vectors, w_expand, w_reduce, pages, more):
    rows, width = tok.shape
    count = len(att_parts) // pages
    span, block = att_parts[0].shape
    hidden = w_expand.shape[1]
    chunks = hidden // width
    pairs = chunks // 2

    def whole(array):
        return pl.BlockSpec(array.shape, lambda s, words: (0,) * len(array.shape))

    def chunk_at(s, words):
        at = jnp.minimum(s, 2 * chunks - 1 - s)
        return (at + words[2] * pairs) % chunks

    def theirs_at(s, words):
        return jnp.clip(2 * chunks - 1 - s - pairs, 0, pairs - 1), 0

    def mine_at(s, words):
        return jnp.clip(2 * chunks - 1 - s, 0, pairs - 1), 0

    shapes = [
        jax.ShapeDtypeStruct((rows, width), BF16),
        jax.ShapeDtypeStruct((rows, width), F32),
        jax.ShapeDtypeStruct((hidden, width), BF16),
        jax.ShapeDtypeStruct((hidden, width), BF16),
        jax.ShapeDtypeStruct((more, width), BF16),
        jax.ShapeDtypeStruct((more, width), BF16),
    ] + [jax.ShapeDtypeStruct((span, pages * block), BF16)] * count
    specs = [whole(item) for item in shapes]
    specs[2] = pl.BlockSpec((2 * width, width), theirs_at)
    specs[3] = pl.BlockSpec((2 * width, width), mine_at)
    return pl.pallas_call(
        functools.partial(middle_kernel, pages, count, span, chunks),
        grid_spec=pltpu.PrefetchScalarGridSpec(
            num_scalar_prefetch=1,
            grid=(2 * chunks,),
            in_specs=[whole(item) for item in att_parts]
            + [
                whole(tok),
                whole(cot),
                whole(w_out),
                whole(vectors),
                pl.BlockSpec((width, width), lambda s, words: (0, chunk_at(s, words))),
                pl.BlockSpec((width, width), lambda s, words: (chunk_at(s, words), 0)),
            ],
            out_specs=specs,
            scratch_shapes=[
                pltpu.VMEM((16, width), F32),
                pltpu.VMEM((count * span, rows), BF16),
                pltpu.VMEM((count * span, rows), BF16),
                pltpu.VMEM((rows, width), F32),
                pltpu.VMEM((rows, 128), F32),
                pltpu.VMEM((rows, width), F32),
                pltpu.VMEM((rows, width), BF16),
                pltpu.VMEM((width, rows), BF16),
                pltpu.VMEM((chunks, rows, width), BF16),
                pltpu.VMEM((chunks, rows, width), F32),
                pltpu.VMEM((rows, width), F32),
                pltpu.VMEM((rows, width), F32),
                pltpu.VMEM((rows, width), BF16),
            ],
        ),
        out_shape=shapes,
        compiler_params=pltpu.CompilerParams(vmem_limit_bytes=VMEM_LIMIT),
        cost_estimate=pl.CostEstimate(
            flops=2 * rows * width * (6 * hidden + 3 * width),
            bytes_accessed=8 * width * hidden + 16 * rows * width,
            transcendentals=2 * rows * hidden,
        ),
        name="middle",
    )(words, *att_parts, tok, cot, w_out, vectors, w_expand, w_reduce)


def input_kernel(pages, count, span, base, *refs):
    words_ref = refs[0]
    own_refs = refs[1 : 1 + pages]
    message_refs = refs[1 + pages : pages + count]
    weight_refs = refs[pages + count : 3 + pages + count]
    first_in_ref, out_ref, held = refs[3 + pages + count :]
    rank = words_ref[0]
    width = out_ref.shape[1]
    block = out_ref.shape[0] // pages
    for page in range(pages):
        for at in range(count):
            part = message_refs[at - 1] if at else own_refs[page]
            top = base + page * span if at else 0
            place = pl.multiple_of((rank ^ at) * span, span)
            for kind in range(3):
                held[kind, pl.ds(place, span), page * block : (page + 1) * block] = part[
                    top : top + span, kind * block : (kind + 1) * block
                ]
    total = dot(weight_refs[0][...], held[0, :width])
    for kind in range(1, 3):
        total = total + dot(weight_refs[kind][...], held[kind, :width])
    out_ref[...] = (first_in_ref[...] + total.T).astype(BF16)


def input_gradient(words, own, messages, base, span, weights, first_in):
    pages = len(own)
    count = 1 + len(messages)
    rows, width = first_in.shape
    vmem = pl.BlockSpec(memory_space=pltpu.VMEM)
    return pl.pallas_call(
        functools.partial(input_kernel, pages, count, span, base),
        in_specs=[pl.BlockSpec(memory_space=pltpu.SMEM)] + [vmem] * (pages + count + 3),
        out_specs=vmem,
        out_shape=jax.ShapeDtypeStruct((rows, width), BF16),
        scratch_shapes=[pltpu.VMEM((3, count * span, rows), BF16)],
        compiler_params=pltpu.CompilerParams(vmem_limit_bytes=VMEM_LIMIT),
        cost_estimate=pl.CostEstimate(
            flops=6 * rows * width * count * span,
            bytes_accessed=2 * width * (5 * rows + 3 * count * span),
            transcendentals=0,
        ),
        name="input_gradient",
    )(words, *own, *messages, *weights, first_in)


def local(body, name, words, arrays, shapes, costly=False):
    def kernel(words_ref, *refs):
        body(words_ref, refs[: len(arrays)], refs[len(arrays) :])

    vmem = pl.BlockSpec(memory_space=pltpu.VMEM)
    shapes = [jax.ShapeDtypeStruct(shape, kind) for shape, kind in shapes]
    moved = sum(item.size * item.dtype.itemsize for item in list(arrays) + shapes)
    cost = pl.CostEstimate(flops=0, bytes_accessed=moved, transcendentals=0)
    return pl.pallas_call(
        kernel,
        in_specs=[pl.BlockSpec(memory_space=pltpu.SMEM)] + [vmem] * len(arrays),
        out_specs=[vmem] * len(shapes),
        out_shape=shapes,
        compiler_params=pltpu.CompilerParams(vmem_limit_bytes=VMEM_LIMIT),
        cost_estimate=cost if costly else NO_COST,
        name=name,
    )(words, *arrays)


def shard(index, rows, base=0):
    return pl.ds(pl.multiple_of(base + index * rows, 16), rows)


def total_of(refs, rows=slice(None)):
    if len(refs) == 2 and all(ref.dtype == BF16 for ref in refs):
        return refs[0][rows] + refs[1][rows]
    total = refs[0][rows].astype(F32)
    for ref in refs[1:]:
        total = total + ref[rows].astype(F32)
    return total


def tree_sum(terms):
    while len(terms) > 1:
        terms = [terms[i] + terms[i + 1] for i in range(0, len(terms), 2)]
    return terms[0]


def bit_of(words, level):
    return lax.shift_right_logical(words[1], level) & 1


def pair_sum(words, mine, other):
    def body(words, ins, outs):
        outs[0][...] = total_of(ins).astype(BF16)

    return local(body, "pair_sum", words, [mine, other], [(mine.shape, BF16)])[0]


def halve(words, level, mine, other):
    rows, width = mine.shape
    half = rows // 2

    def body(words, ins, outs):
        bit = bit_of(words, level)
        outs[0][...] = total_of(ins, shard(bit, half)).astype(BF16)
        outs[1][...] = total_of(ins, shard(1 - bit, half)).astype(BF16)

    return local(body, "halve", words, [mine, other], [((half, width), BF16)] * 2)


def join_halves(words, level, mine, other):
    rows, width = mine.shape

    def body(words, ins, outs):
        bit = bit_of(words, level)
        outs[0][shard(bit, rows)] = ins[0][...]
        outs[0][shard(1 - bit, rows)] = ins[1][...]

    return local(body, "join_halves", words, [mine, other], [((2 * rows, width), BF16)])[0]


def across(block, level):
    return swapped(block, 1 << level, "depth")


class Plan:
    def __init__(self, rows, rows_a, more, span, width):
        self.count = lax.axis_size("blk")
        self.levels = lax.axis_size("depth").bit_length() - 1
        self.rows = rows
        self.rows_a = rows_a
        self.more = more
        self.span = span
        self.width = width
        self.a_ff = rows_a // self.count
        self.a_more = more // self.count
        self.a = self.a_ff + self.a_more
        self.b = (rows - rows_a) >> self.levels

    def shapes(self, *sizes):
        return [((rows, self.width), BF16) for rows in sizes]

    def scatter_one(self, words, halves):
        count, width = self.count, self.width
        a_ff, a_more = self.a_ff, self.a_more
        b_rows = (self.rows - self.rows_a) // count
        steps = count // 2

        def kernel(words_ref, *refs):
            parts = refs[6 : 6 + count]
            keep_ref, send_ref = refs[6 + count :]
            for i in range(count):

                @pl.when(pl.program_id(0) == i)
                def _(i=i):
                    parts[i][:a_ff] = total_of(refs[:2]).astype(BF16)
                    parts[i][a_ff:] = total_of(refs[2:4]).astype(BF16)
                    side = send_ref if i < steps else keep_ref
                    side[...] = total_of(refs[4:6]).astype(BF16)

        def there(rows):
            return pl.BlockSpec((rows, width), lambda i, words: (words[0] ^ i, 0))

        def b_at(i, words):
            bit = bit_of(words, 0)
            side = jnp.where(i < steps, 1 - bit, bit)
            return self.rows_a // b_rows + side * steps + i % steps, 0

        own_b = pl.BlockSpec((b_rows, width), b_at)
        shapes = [jax.ShapeDtypeStruct((self.a, width), BF16)] * count
        shapes += [jax.ShapeDtypeStruct((b_rows * steps, width), BF16)] * 2
        *parts_a, keep, send = pl.pallas_call(
            kernel,
            grid_spec=pltpu.PrefetchScalarGridSpec(
                num_scalar_prefetch=1,
                grid=(count,),
                in_specs=[there(a_ff)] * 2 + [there(a_more)] * 2 + [own_b] * 2,
                out_specs=[fixed(item) for item in shapes[:count]]
                + [
                    pl.BlockSpec((b_rows, width), lambda i, words: (jnp.maximum(i - steps, 0), 0)),
                    pl.BlockSpec((b_rows, width), lambda i, words: (jnp.minimum(i, steps - 1), 0)),
                ],
            ),
            out_shape=shapes,
            compiler_params=pltpu.CompilerParams(vmem_limit_bytes=VMEM_LIMIT),
            cost_estimate=NO_COST,
            name="scatter_one",
        )(words, *halves, *halves[:2])
        return [from_blk(part, i) for i, part in enumerate(parts_a)], keep, across(send, 0)

    def scatter_two(self, words, parts_a, keep_b, other_b, pages):
        count = self.count
        half = self.a // 2

        def body(words, ins, outs):
            bit = bit_of(words, 0)
            outs[0][...] = total_of(ins[:count], shard(bit, half)).astype(BF16)
            outs[1][...] = total_of(ins[:count], shard(1 - bit, half)).astype(BF16)
            part_b = total_of(ins[count : count + 2]).astype(BF16)
            outs[2][...] = part_b
            for i, out in enumerate(outs[3:]):
                out[: self.b] = part_b
                for page in range(len(pages)):
                    piece = ins[count + 2 + page * (count - 1) + i]
                    base = self.b + page * self.span
                    out[base : base + self.span, : piece.shape[1]] = piece[...]

        message = self.b + len(pages) * self.span
        shapes = self.shapes(half, half, self.b, *[message] * (count - 1))
        pieces = [piece for page in pages for piece in page[1:]]
        keep, send, part_b, *messages = local(
            body, "scatter_two", words, [*parts_a, keep_b, other_b, *pieces], shapes
        )
        return (
            keep,
            across(send, 0),
            part_b,
            [from_blk(item, i + 1) for i, item in enumerate(messages)],
        )

    def sum_b(self, words, part_b, messages):
        def body(words, ins, outs):
            terms = [ref[: self.b].astype(F32) for ref in ins]
            outs[0][...] = tree_sum(terms).astype(BF16)

        return local(body, "sum_b", words, [part_b, *messages], self.shapes(self.b))[0]

    def gather_b(self, words, part_b):
        for level in range(self.levels - 1, 0, -1):
            part_b = join_halves(words, level, part_b, across(part_b, level))
        return part_b, across(part_b, 0)


def gather_blk(part, cut, late=None):
    count = lax.axis_size("blk")
    if count != 4:
        return [(i, 0, from_blk(part, i)) for i in range(count)]
    one, two = swapped(part, 1), swapped(part, 2)
    if late is not None:
        one, two = after(late, (one, two))
    first, second = swapped(one[:cut], 2), swapped(two[cut:], 1)
    return [(0, 0, part), (1, 0, one), (2, 0, two), (3, 0, first), (3, cut, second)]


def with_core(pieces):
    return [(distance, base, from_core(item)) for distance, base, item in pieces]


SEGMENT = 256
SLOTS = 4


def widen_own(words, plan, pieces, halves_b, hidden):
    width = plan.width
    chunks = hidden // width
    pairs = chunks // 2
    per_matrix = width // SEGMENT
    arrays = [item for _, _, item in pieces] + list(halves_b)
    segments = []
    extras = []
    for at, (distance, base, item) in enumerate(pieces):
        stop = min(item.shape[0], plan.a_ff - base)
        for top in range(0, stop, SEGMENT):
            segments.append((at, top, min(SEGMENT, stop - top), distance, base + top))
        if base + item.shape[0] == plan.a:
            extras.append((at, distance))
    for at, item in enumerate(halves_b):
        for top in range(0, item.shape[0], SEGMENT):
            segments.append((len(pieces) + at, top, SEGMENT, None, top))

    def kernel(words_ref, *refs):
        ins = refs[: len(arrays)]
        joined_ref, expand_ref, reduce_ref, held, sems = refs[len(arrays) :]
        copies = []
        for index, (at, top, rows, distance, base) in enumerate(segments):
            slot = index % SLOTS
            if index >= SLOTS:
                copies[index - SLOTS].wait()
            part = ins[at][top : top + rows]
            held[slot, :rows] = part.astype(F32)
            if distance is None:
                half = ins[len(pieces)].shape[0]
                bit = bit_of(words_ref, 0)
                place = plan.rows_a + half * (bit if at == len(pieces) else 1 - bit) + base
            else:
                place = (words_ref[0] ^ distance) * plan.a_ff + base
            joined_ref[pl.ds(pl.multiple_of(place, SEGMENT), rows)] = part
            block = lax.div(place, SEGMENT)
            matrix = lax.div(block, per_matrix)
            row = (block - matrix * per_matrix) * SEGMENT
            chunk = (lax.div(matrix, 2) + words_ref[2] * pairs) % chunks
            column = pl.multiple_of(chunk * width, width)
            source = held.at[slot, :rows]
            to_expand = pltpu.make_async_copy(
                source,
                expand_ref.at[pl.ds(pl.multiple_of(row, SEGMENT), rows), pl.ds(column, width)],
                sems.at[slot],
            )
            to_reduce = pltpu.make_async_copy(
                source,
                reduce_ref.at[pl.ds(pl.multiple_of(column + row, SEGMENT), rows)],
                sems.at[slot],
            )
            is_expand = lax.rem(matrix, 2) == 0
            pl.when(is_expand)(to_expand.start)
            pl.when(jnp.logical_not(is_expand))(to_reduce.start)
            copies.append(to_reduce)
        for at, distance in extras:
            rows = shard(words_ref[0] ^ distance, plan.a_more, plan.rows)
            joined_ref[rows] = ins[at][ins[at].shape[0] - plan.a_more :]
        for copy in copies[-SLOTS:]:
            copy.wait()

    assert all(base % SEGMENT == 0 for *_, base in segments)
    vmem = pl.BlockSpec(memory_space=pltpu.VMEM)
    anywhere = pl.BlockSpec(memory_space=pl.ANY)
    return pl.pallas_call(
        kernel,
        in_specs=[pl.BlockSpec(memory_space=pltpu.SMEM)] + [vmem] * len(arrays),
        out_specs=[vmem, anywhere, anywhere],
        out_shape=[
            jax.ShapeDtypeStruct((plan.rows + plan.more, width), BF16),
            jax.ShapeDtypeStruct((width, hidden), F32),
            jax.ShapeDtypeStruct((hidden, width), F32),
        ],
        scratch_shapes=[
            pltpu.VMEM((SLOTS, SEGMENT, width), F32),
            pltpu.SemaphoreType.DMA((SLOTS,)),
        ],
        compiler_params=pltpu.CompilerParams(vmem_limit_bytes=VMEM_LIMIT),
        cost_estimate=pl.CostEstimate(
            flops=0, bytes_accessed=6 * hidden * width, transcendentals=0
        ),
        name="widen_own",
    )(words, *arrays)


def widen_other(words, joined, expand, reduce):
    width, hidden = expand.shape
    chunks = hidden // width
    pairs = chunks // 2

    def kernel(words_ref, half_ref, before_ref, before_too_ref, expand_ref, reduce_ref):
        expand_ref[...] = half_ref[:width].astype(F32)
        reduce_ref[...] = half_ref[width:].astype(F32)

    def place(s, words):
        return (s + (words[2] + 1) * pairs) % chunks

    anywhere = pl.BlockSpec(memory_space=pl.ANY)
    return pl.pallas_call(
        kernel,
        grid_spec=pltpu.PrefetchScalarGridSpec(
            num_scalar_prefetch=1,
            grid=(pairs,),
            in_specs=[
                pl.BlockSpec((2 * width, width), lambda s, words: (s, 0)),
                anywhere,
                anywhere,
            ],
            out_specs=[
                pl.BlockSpec((width, width), lambda s, words: (0, place(s, words))),
                pl.BlockSpec((width, width), lambda s, words: (place(s, words), 0)),
            ],
        ),
        out_shape=[
            jax.ShapeDtypeStruct((width, hidden), F32),
            jax.ShapeDtypeStruct((hidden, width), F32),
        ],
        input_output_aliases={2: 0, 3: 1},
        compiler_params=pltpu.CompilerParams(vmem_limit_bytes=VMEM_LIMIT),
        cost_estimate=pl.CostEstimate(
            flops=0, bytes_accessed=6 * hidden * width, transcendentals=0
        ),
        name="widen_other",
    )(words, joined, expand, reduce)


def finished(words, plan, heads, joined, side, before=()):
    count = plan.count
    span = plan.span
    width = plan.width
    half_rows = width // 2
    arrays = [item for _, _, item in heads]

    def kernel(words_ref, *refs):
        heads_refs, refs = refs[: len(heads)], refs[len(heads) :]
        extra_ref, refs = refs[0], refs[1 + len(before) :]
        outs, refs = refs[:5], refs[5:]
        gathered, wide, project, sems = refs
        rank = words_ref[0]
        half = words_ref[2] ^ side
        for ref, (distance, base, _) in zip(heads_refs, heads):
            rows = ref.shape[0]
            place = pl.multiple_of((rank ^ distance) * span, HEAD_DIM)
            for part in range(2):
                low, high = max(base, part * span), min(base + rows, (part + 1) * span)
                if low < high:
                    gathered[part, pl.ds(place + (low - part * span), high - low)] = ref[
                        low - base : high - base
                    ]
        for part in range(2):
            wide[part] = gathered[part, :width].astype(F32).T
        project[...] = extra_ref[:half_rows].astype(F32)

        @pl.when(half == 1)
        def _():
            wide[1] = entry_order(wide[1])

        def copy(source, target, at):
            return pltpu.make_async_copy(source, target, sems.at[at])

        for part in range(2):
            pl.when(half == 0)(copy(wide.at[part], outs[part], part).start)
            pl.when(half == 1)(copy(wide.at[part], outs[2 + part], part).start)
        rows = pl.ds(pl.multiple_of(half * half_rows, half_rows), half_rows)
        last = copy(project, outs[4].at[rows], 2)
        last.start()
        for part in range(2):
            copy(wide.at[part], outs[part], part).wait()
        last.wait()

    def whole(item):
        return pl.BlockSpec(item.shape, lambda s: (0, 0))

    more = pl.BlockSpec((plan.more, width), lambda s: (plan.rows // plan.more, 0))
    anywhere = pl.BlockSpec(memory_space=pl.ANY)
    first = 2 + len(heads)
    shapes = [jax.ShapeDtypeStruct((width, width), F32)] * 5
    return pl.pallas_call(
        kernel,
        grid=(1,),
        in_specs=[pl.BlockSpec(memory_space=pltpu.SMEM)]
        + [whole(item) for item in arrays]
        + [more]
        + [anywhere] * len(before),
        out_specs=[anywhere] * 5,
        out_shape=shapes,
        scratch_shapes=[
            pltpu.VMEM((2, count * span, width), BF16),
            pltpu.VMEM((2, width, width), F32),
            pltpu.VMEM((half_rows, width), F32),
            pltpu.SemaphoreType.DMA((3,)),
        ],
        input_output_aliases={first + at: at for at in range(len(before))},
        compiler_params=pltpu.CompilerParams(vmem_limit_bytes=VMEM_LIMIT),
        cost_estimate=pl.CostEstimate(
            flops=0, bytes_accessed=16 * width * width, transcendentals=0
        ),
        name="finish",
    )(words, *arrays, joined, *before)


def per_device(
    tokens,
    boxes,
    w_query,
    w_key,
    w_value,
    w_output,
    box_weight,
    first_gain,
    first_shift,
    w_expand,
    w_reduce,
    second_gain,
    second_shift,
    cotangent,
):
    pages, block, width = tokens.shape
    count = lax.axis_size("blk")
    depth = lax.axis_size("depth")
    words = jnp.stack(
        [lax.axis_index("blk"), lax.axis_index("depth"), lax.axis_index("core")]
    ).astype(jnp.int32)
    hidden = w_expand.shape[1]
    span = -(-HEADS // count) * HEAD_DIM
    unit = 16 * count * depth
    more = -(-(width // 2 + 16) // unit) * unit

    own_places = jnp.stack([boxes[0] + boxes[2], boxes[1] + boxes[3]], axis=1)
    own_places = jnp.stack([lax.shift_right_logical(own_places, 6), own_places & 63], axis=2)
    own_places = own_places.reshape(4 * pages, block).astype(BF16)
    own_places = jnp.pad(own_places, ((0, 16 - 4 * pages), (0, width - block)))
    message = jnp.concatenate([tokens[0], own_places])
    messages = [from_blk(message, i) for i in range(count)]
    w_own, box_own, rot_cos, rot_sin = prepare(
        words, w_query, w_key, w_value, box_weight, span, count * block
    )
    messages, rot_cos = lax.optimization_barrier((messages, rot_cos))
    own = after(messages, tokens[1])
    pieces = [messages, [from_blk(own, i) for i in range(count)]]

    saved = []
    att_parts = []
    for page in range(pages):
        results = attention_forward(
            words, page, messages, pieces[page], w_own, box_own, rot_cos, rot_sin
        )
        saved.append(results[:6])
        att_parts += [from_blk(results[6 + i], i) for i in range(count)]

    vectors = jnp.stack([first_gain, first_shift, second_gain, second_shift])
    results = middle(
        words,
        att_parts,
        tokens.reshape(pages * block, width),
        cotangent.reshape(pages * block, width),
        w_output,
        vectors,
        w_expand,
        w_reduce,
        pages,
        more,
    )
    layer_out, first_in, theirs, mine, more_theirs, more_mine = results[:6]
    grads = [from_blk(results[6 + i], i) for i in range(count)]
    plan = Plan(hidden, 2 * hidden // 3, more, span, width)
    parts_a, keep_b, other_b = plan.scatter_one(
        after(grads[:2], words), [mine, from_core(theirs), more_mine, from_core(more_theirs)]
    )

    def backward(page, words, before=None):
        return attention_backward(
            words,
            page,
            grads,
            pieces[page],
            saved[page],
            box_own,
            rot_cos,
            rot_sin,
            before,
        )

    *pre_one, before = backward(0, after(parts_a[0], words))
    done = before
    for level in range(1, plan.levels):
        keep_b, send_b = halve(after(done, words), level, keep_b, other_b)
        other_b = across(send_b, level)
        done = keep_b
    *pre_two, heads_mine, heads_theirs = backward(1, after(done, words), before)
    own = [pre_one[0], pre_two[0]]
    part_a, other_a, part_b, messages_b = plan.scatter_two(
        after(heads_mine, words), parts_a, keep_b, other_b, [pre_one, pre_two]
    )
    heads, other = halve(
        after(part_a, words), 0, heads_mine, from_core(after(part_a, heads_theirs))
    )
    part_a = pair_sum(after(heads, words), part_a, other_a)
    other = across(after(part_a, other), 0)
    heads = pair_sum(after(part_a, words), heads, other)
    done = heads
    for level in range(1, plan.levels):
        part_a = pair_sum(after(done, words), part_a, across(part_a, level))
        done = part_a
    other_a = across(part_a, 0)
    part_b = plan.sum_b(after(part_a, words), part_b, messages_b)
    part_a = join_halves(after(part_b, words), 0, part_a, other_a)
    part_b = after(part_a, part_b)
    input_grad = input_gradient(
        after(part_a, words),
        own,
        messages_b,
        plan.b,
        span,
        (w_query, w_key, w_value),
        first_in,
    )
    parts_b = plan.gather_b(after(input_grad, words), part_b)
    heads = after(parts_b[0], heads)
    pieces_a = gather_blk(part_a, plan.a_ff // 2, parts_b[0])
    for level in range(1, plan.levels):
        heads = pair_sum(after(pieces_a[1][2], words), heads, across(heads, level))
    heads = join_halves(words, 0, heads, across(heads, 0))
    heads = after(([item for _, _, item in pieces_a], parts_b), heads)
    joined, *wide = widen_own(after(heads, words), plan, pieces_a, parts_b, hidden)
    at = plan.rows + width // 2
    sums = [joined[at + i].astype(F32) for i in range(4)]
    pieces_heads = gather_blk(heads, span, (joined, sums))
    joined_other = from_core(after(pieces_heads[1][2], joined))
    grads = finished(words, plan, pieces_heads, joined, 0)
    grad_expand, grad_reduce = widen_other(after(grads, words), joined_other, *wide)
    grad_query, grad_key, grad_value, grad_box, grad_project = finished(
        after(grad_expand, words), plan, with_core(pieces_heads), joined_other, 1, grads
    )
    return (
        layer_out.reshape(tokens.shape),
        input_grad.reshape(tokens.shape),
        grad_query,
        grad_key,
        grad_value,
        grad_project,
        grad_box,
        sums[0],
        sums[1],
        grad_expand,
        grad_reduce,
        sums[2],
        sums[3],
    )


def solution(mesh):
    blocks, rest = mesh.devices.shape
    parts = jax.sharding.Mesh(
        mesh.devices.reshape(blocks, rest // 2, 2), ("blk", "depth", "core")
    )
    split = P(("depth", "core"), "blk", None)
    return jax.shard_map(
        per_device,
        mesh=parts,
        in_specs=(split, P(None, ("depth", "core"), "blk")) + (P(),) * 11 + (split,),
        out_specs=(split, split) + (P(),) * 11,
        check_vma=False,
    )
```

```python
import functools

import jax
import jax.numpy as jnp
import numpy as np
from jax import lax
from jax.experimental import pallas as pl
from jax.experimental.pallas import tpu as pltpu
from jax.sharding import PartitionSpec as P

HEADS = 12
HEAD_DIM = 64
HALF = 32
FREQS = 192
CODES = 4 * FREQS
VMEM_LIMIT = 60 * 1024 * 1024
NO_COST = pl.CostEstimate(flops=0, bytes_accessed=0, transcendentals=0)
F32 = jnp.float32
BF16 = jnp.bfloat16


def dot(left, right):
    return lax.dot_general(left, right, (((1,), (0,)), ((), ())), preferred_element_type=F32)


def dot_nt(left, right):
    return lax.dot_general(left, right, (((1,), (1,)), ((), ())), preferred_element_type=F32)


def dot_tn(left, right):
    return lax.dot_general(left, right, (((0,), (0,)), ((), ())), preferred_element_type=F32)


def swapped(block, distance, axis="blk"):
    count = lax.axis_size(axis)
    return lax.ppermute(block, axis, [(i, i ^ distance) for i in range(count)])


def from_blk(block, distance):
    return swapped(block, distance) if distance else block


def from_core(block):
    return swapped(block, 1, "core")


def after(done, value):
    return lax.optimization_barrier((value, done))[0]


def turned(upper, lower, cosines, sines):
    return upper * cosines - lower * sines, lower * cosines + upper * sines


def entry_order(rows):
    return jnp.concatenate(
        [
            rows[:FREQS],
            rows[2 * FREQS : 3 * FREQS],
            rows[FREQS : 2 * FREQS],
            rows[3 * FREQS :],
        ],
        axis=0,
    )


def angle_tables():
    rates = np.float32(10000.0) ** (-np.arange(FREQS, dtype=np.float32) / np.float32(FREQS))
    tables = []
    for places in (32.0 * np.arange(32), 0.5 * np.arange(64)):
        angles = rates.astype(np.float64)[:, None] * places[None, :]
        left = np.concatenate([np.sin(angles), np.cos(angles)])
        parts = []
        for _ in range(3):
            parts.append(left.astype(jnp.bfloat16))
            left = left - parts[-1].astype(np.float64)
        tables.append(np.concatenate(parts, axis=1))
    return tables


def rotary_tables(length):
    rates = np.float32(10000.0) ** (-np.arange(HALF, dtype=np.float32) / np.float32(HALF))
    angles = np.arange(length, dtype=np.float32)[None, :] * rates[:, None]
    angles = angles.astype(np.float64)
    return np.cos(angles).astype(np.float32), np.sin(angles).astype(np.float32)


def prepare_kernel(
    words_ref,
    query_ref,
    key_ref,
    value_ref,
    box_ref,
    cos_ref,
    sin_ref,
    own_ref,
    own_box_ref,
    own_cos_ref,
    own_sin_ref,
):
    rank = words_ref[0]
    span = own_box_ref.shape[0]
    width = query_ref.shape[1]
    count = lax.axis_size("blk")
    block = cos_ref.shape[1] // count
    row = lax.broadcasted_iota(jnp.int32, (span, width), 0) + rank * span
    column = lax.broadcasted_iota(jnp.int32, (span, width), 1)
    pick = jnp.where(row == column, 1.0, 0.0).astype(BF16)
    for kind, ref in enumerate((query_ref, key_ref, value_ref)):
        own_ref[kind * span : (kind + 1) * span] = dot_nt(pick, ref[...]).astype(BF16)
    own_box_ref[...] = dot_nt(pick, entry_order(box_ref[...])).astype(BF16)
    for i in range(count):
        from_cols = pl.ds(pl.multiple_of((rank ^ i) * block, block), block)
        own_cos_ref[:, i * block : (i + 1) * block] = cos_ref[:, from_cols]
        own_sin_ref[:, i * block : (i + 1) * block] = sin_ref[:, from_cols]


def prepare(words, w_query, w_key, w_value, box_weight, span, length):
    width = w_query.shape[0]
    vmem = pl.BlockSpec(memory_space=pltpu.VMEM)
    return pl.pallas_call(
        prepare_kernel,
        in_specs=[pl.BlockSpec(memory_space=pltpu.SMEM)] + [vmem] * 6,
        out_specs=[vmem] * 4,
        out_shape=[
            jax.ShapeDtypeStruct((3 * span, width), BF16),
            jax.ShapeDtypeStruct((span, CODES), BF16),
            jax.ShapeDtypeStruct((HALF, length), F32),
            jax.ShapeDtypeStruct((HALF, length), F32),
        ],
        compiler_params=pltpu.CompilerParams(vmem_limit_bytes=VMEM_LIMIT),
        cost_estimate=pl.CostEstimate(
            flops=8 * span * width * width, bytes_accessed=10 * width * width, transcendentals=0
        ),
        name="prepare",
    )(words, w_query, w_key, w_value, box_weight, *map(jnp.asarray, rotary_tables(length)))


def fold(value, combine):
    while value.shape[0] > 8:
        half = value.shape[0] // 2
        value = combine(value[:half], value[half:])
    return value


def write_codes(page, place_refs, high_ref, low_ref, sin_ref, cos_ref, codes_ref):
    block = sin_ref.shape[1] // len(place_refs)

    def looked_up(table_ref, index):
        spots = table_ref.shape[1] // 3
        rows = lax.broadcasted_iota(jnp.int32, (spots, block), 0).astype(F32)
        once = jnp.where(rows == index, 1.0, 0.0)
        found = dot(table_ref[...], jnp.concatenate([once] * 3, axis=0).astype(BF16))
        return found[:FREQS], found[FREQS:]

    for i, place_ref in enumerate(place_refs):
        columns = slice(i * block, (i + 1) * block)
        places = place_ref[:, :block].astype(F32)
        for axis in range(2):
            at = 4 * page + 2 * axis
            high_sin, high_cos = looked_up(high_ref, places[at : at + 1])
            low_sin, low_cos = looked_up(low_ref, places[at + 1 : at + 2])
            sines = high_sin * low_cos + high_cos * low_sin
            cosines = high_cos * low_cos - high_sin * low_sin
            rows = slice(axis * FREQS, (axis + 1) * FREQS)
            later = slice((2 + axis) * FREQS, (3 + axis) * FREQS)
            sin_ref[rows, columns] = sines
            cos_ref[rows, columns] = cosines
            codes_ref[rows, columns] = sines.astype(BF16)
            codes_ref[later, columns] = cosines.astype(BF16)


def forward_kernel(page, count, words_ref, *refs):
    place_refs, refs = refs[:count], refs[count:]
    piece_refs, refs = refs[:count], refs[count:]
    high_ref, low_ref, w_ref, box_ref, rot_cos_ref, rot_sin_ref = refs[:6]
    probs_ref, att_ref, heads_ref, sin_ref, cos_ref, codes_ref = refs[6:12]
    low_refs = refs[12 : 12 + count]
    tok_ref, pre_ref, kc_ref, qr_ref = refs[12 + count :]
    rows = tok_ref.shape[0]
    block = rows // count
    head = pl.program_id(0)
    span = pl.num_programs(0) * HEAD_DIM

    @pl.when(head == 0)
    def _():
        for i in range(count):
            tok_ref[i * block : (i + 1) * block] = piece_refs[i][...]
        pre_ref[...] = dot_nt(w_ref[...], tok_ref[...])
        write_codes(page, place_refs, high_ref, low_ref, sin_ref, cos_ref, codes_ref)
        kc_ref[:, :CODES] = codes_ref[...].astype(F32).T.astype(BF16)

    def pre(kind):
        at = kind * span + head * HEAD_DIM
        return pre_ref[pl.ds(pl.multiple_of(at, HEAD_DIM), HEAD_DIM)]

    rot_cos = rot_cos_ref[...]
    rot_sin = rot_sin_ref[...]
    query_pre = pre(0).astype(BF16)
    wide = query_pre.astype(F32)
    query = jnp.concatenate(turned(wide[:HALF], wide[HALF:], rot_cos, rot_sin), axis=0)
    key_pre = pre(1)
    key = jnp.concatenate(turned(key_pre[:HALF], key_pre[HALF:], rot_cos, rot_sin), axis=0)
    value = pre(2).astype(BF16)
    heads_ref[0, :HEAD_DIM] = query_pre
    heads_ref[0, HEAD_DIM : 2 * HEAD_DIM] = query.astype(BF16)
    heads_ref[0, 2 * HEAD_DIM : 3 * HEAD_DIM] = key.astype(BF16)
    heads_ref[0, 3 * HEAD_DIM :] = value
    kc_ref[:, CODES:] = key.T.astype(BF16)
    qr_ref[CODES:] = (query * 0.125).astype(BF16)
    step = min(256, block)

    def logits_at(at):
        part = slice(at, at + step)
        projected = dot_tn(box_ref[...], query_pre[:, part])
        sines = sin_ref[:, part]
        cosines = cos_ref[:, part]
        upper = projected[: 2 * FREQS]
        lower = projected[2 * FREQS :]
        qr_ref[: 2 * FREQS, part] = ((upper * cosines + lower * sines) * 0.125).astype(BF16)
        qr_ref[2 * FREQS : CODES, part] = ((lower * cosines - upper * sines) * 0.125).astype(BF16)
        return dot(kc_ref[...], qr_ref[:, part])

    following = logits_at(0)
    for at in range(0, rows, step):
        logits = following
        if at + step < rows:
            following = logits_at(at + step)
        peak = jnp.max(fold(logits, jnp.maximum), axis=0, keepdims=True)
        weight = jnp.exp(logits - peak)
        total = jnp.sum(fold(weight, jnp.add), axis=0, keepdims=True)
        probs = (weight * (1.0 / total)).astype(BF16)
        probs_ref[0, :, at : at + step] = probs
        attended = dot(value, probs)
        att_ref[0, :, at : at + step] = attended
        inner = at % block
        low_refs[at // block][:, inner : inner + step] = attended.astype(BF16)


def fixed(array):
    return pl.BlockSpec(array.shape, lambda *at: (0,) * len(array.shape))


def attention_forward(words, page, messages, pieces, w_own, box_own, rot_cos, rot_sin):
    count = len(messages)
    block, width = messages[0].shape[0] - 16, messages[0].shape[1]
    rows = count * block
    span = box_own.shape[0]
    heads = span // HEAD_DIM
    tables = [jnp.asarray(item) for item in angle_tables()]
    specs = [pl.BlockSpec((block, width), lambda h, words: (0, 0))] * count
    places = pl.BlockSpec((16, width), lambda h, words: (block // 16, 0))
    out_shape = [
        jax.ShapeDtypeStruct((heads, rows, rows), BF16),
        jax.ShapeDtypeStruct((heads, HEAD_DIM, rows), F32),
        jax.ShapeDtypeStruct((heads, 4 * HEAD_DIM, rows), BF16),
        jax.ShapeDtypeStruct((2 * FREQS, rows), F32),
        jax.ShapeDtypeStruct((2 * FREQS, rows), F32),
        jax.ShapeDtypeStruct((CODES, rows), BF16),
    ] + [jax.ShapeDtypeStruct((span, block), BF16)] * count
    return pl.pallas_call(
        functools.partial(forward_kernel, page, count),
        grid_spec=pltpu.PrefetchScalarGridSpec(
            num_scalar_prefetch=1,
            grid=(heads,),
            in_specs=[places] * count
            + specs
            + [fixed(item) for item in (*tables, w_own)]
            + [
                pl.BlockSpec((HEAD_DIM, CODES), lambda h, words: (h, 0)),
                fixed(rot_cos),
                fixed(rot_sin),
            ],
            out_specs=[
                pl.BlockSpec((1, rows, rows), lambda h, words: (h, 0, 0)),
                pl.BlockSpec((1, HEAD_DIM, rows), lambda h, words: (h, 0, 0)),
                pl.BlockSpec((1, 4 * HEAD_DIM, rows), lambda h, words: (h, 0, 0)),
            ]
            + [fixed(item) for item in out_shape[3:6]]
            + [pl.BlockSpec((HEAD_DIM, block), lambda h, words: (h, 0))] * count,
            scratch_shapes=[
                pltpu.VMEM((rows, width), BF16),
                pltpu.VMEM((3 * span, rows), F32),
                pltpu.VMEM((rows, CODES + HEAD_DIM), BF16),
                pltpu.VMEM((CODES + HEAD_DIM, rows), BF16),
            ],
        ),
        out_shape=out_shape,
        compiler_params=pltpu.CompilerParams(vmem_limit_bytes=VMEM_LIMIT),
        cost_estimate=pl.CostEstimate(
            flops=2 * heads * rows * (rows * 1100 + 200 * width + 64 * CODES),
            bytes_accessed=2 * heads * rows * rows + 12 * rows * width,
            transcendentals=heads * rows * rows,
        ),
        name="attention_forward",
    )(words, *messages, *pieces, *tables, w_own, box_own, rot_cos, rot_sin)


def backward_kernel(count, last, words_ref, *refs):
    grad_refs, refs = refs[:count], refs[count:]
    piece_refs, refs = refs[:count], refs[count:]
    probs_ref, att_ref, heads_ref, box_ref, codes_ref, sin_ref, cos_ref = refs[:7]
    rot_cos_ref, rot_sin_ref = refs[7:9]
    refs = refs[9:]
    if last:
        before_ref, refs = refs[0], refs[1:]
    pre_refs, refs = refs[:count], refs[count:]
    if last:
        mine_ref, theirs_ref, *refs = refs
    weight_grad_ref, kc_ref, logit_grad_ref, entry_grad_ref, turned_ref = refs
    block, width = piece_refs[0].shape
    rows = count * block
    head = pl.program_id(0)
    span = pl.num_programs(0) * HEAD_DIM

    @pl.when(head == 0)
    def _():
        kc_ref[:CODES] = codes_ref[...]

    kc_ref[CODES:] = heads_ref[0, 2 * HEAD_DIM : 3 * HEAD_DIM]
    packed = heads_ref[0].astype(F32).T.astype(BF16)
    query_pre = packed[:, :HEAD_DIM]
    query = packed[:, HEAD_DIM : 2 * HEAD_DIM]
    value = packed[:, 3 * HEAD_DIM :] * jnp.asarray(0.125, BF16)
    rot_cos = rot_cos_ref[...]
    rot_sin = rot_sin_ref[...]
    grad = jnp.concatenate([ref[...] for ref in grad_refs], axis=1)
    grad_tall = grad.astype(F32).T.astype(BF16)
    offsets = jnp.sum(grad.astype(F32) * att_ref[0], axis=0, keepdims=True) * 0.125
    step = min(256, block)
    place = pl.multiple_of(head * HEAD_DIM, HEAD_DIM)
    here = pl.ds(place, HEAD_DIM)

    def logits_back(at):
        part = slice(at, at + step)
        grad_probs = dot(value, grad[:, part])
        logit_grad_ref[:, part] = (
            probs_ref[0, :, part].astype(F32) * (grad_probs - offsets[:, part])
        ).astype(BF16)

    logits_back(0)
    for at in range(0, rows, step):
        if at + step < rows:
            logits_back(at + step)
        part = slice(at, at + step)
        back = dot(kc_ref[...], logit_grad_ref[:, part])
        sines = sin_ref[:, part]
        cosines = cos_ref[:, part]
        upper = back[: 2 * FREQS]
        lower = back[2 * FREQS : CODES]
        entry_grad_ref[: 2 * FREQS, part] = (upper * cosines - lower * sines).astype(BF16)
        entry_grad_ref[2 * FREQS :, part] = (lower * cosines + upper * sines).astype(BF16)
        first = back[CODES : CODES + HALF]
        second = back[CODES + HALF :]
        turned_ref[:HALF, part], turned_ref[HALF:, part] = turned(
            first, second, rot_cos[:, part], -rot_sin[:, part]
        )
    key_flat = dot(logit_grad_ref[...], query).T
    value_low = dot(probs_ref[0], grad_tall).T.astype(BF16)
    query_low = (turned_ref[...] + dot(box_ref[...], entry_grad_ref[...])).astype(BF16)
    key_low = jnp.concatenate(
        turned(key_flat[:HALF], key_flat[HALF:], rot_cos, -rot_sin), axis=0
    ).astype(BF16)
    for i in range(count):
        columns = slice(i * block, (i + 1) * block)
        pre_refs[i][here, :block] = query_low[:, columns]
        pre_refs[i][here, block : 2 * block] = key_low[:, columns]
        pre_refs[i][here, 2 * block :] = value_low[:, columns]
    weight_grad_ref[pl.ds(3 * span + place, HEAD_DIM)] = dot(entry_grad_ref[...], query_pre).T

    @pl.when(head == pl.num_programs(0) - 1)
    def _():
        for kind in range(3):
            columns = slice(kind * block, (kind + 1) * block)
            total = dot(pre_refs[0][:, columns], piece_refs[0][...])
            for i in range(1, count):
                total = total + dot(pre_refs[i][:, columns], piece_refs[i][...])
            weight_grad_ref[kind * span : (kind + 1) * span] = total
        if last:
            half = 2 * span
            core = words_ref[2]
            ours = pl.ds(pl.multiple_of(core * half, half), half)
            there = pl.ds(pl.multiple_of((1 - core) * half, half), half)
            mine_ref[...] = weight_grad_ref[ours] + before_ref[ours]
            theirs_ref[...] = (weight_grad_ref[there] + before_ref[there]).astype(BF16)


def attention_backward(
    words, page, grads, pieces, saved, box_own, rot_cos, rot_sin, before=None
):
    probs, att, heads_saved, sines, cosines, codes = saved
    count = len(pieces)
    rows, width = probs.shape[1], pieces[0].shape[1]
    block = rows // count
    span = box_own.shape[0]
    heads = span // HEAD_DIM
    last = before is not None
    extra = (before,) if last else ()
    full_shape = (4 * span, width)
    specs = [pl.BlockSpec((block, width), lambda h, words: (0, 0))] * count
    out_shape = [jax.ShapeDtypeStruct((span, 3 * block), BF16)] * count
    if last:
        out_shape += [
            jax.ShapeDtypeStruct((2 * span, width), F32),
            jax.ShapeDtypeStruct((2 * span, width), BF16),
        ]
    else:
        out_shape.append(jax.ShapeDtypeStruct(full_shape, F32))
    return pl.pallas_call(
        functools.partial(backward_kernel, count, last),
        grid_spec=pltpu.PrefetchScalarGridSpec(
            num_scalar_prefetch=1,
            grid=(heads,),
            in_specs=[pl.BlockSpec((HEAD_DIM, block), lambda h, words: (h, page))] * count
            + specs
            + [
                pl.BlockSpec((1, rows, rows), lambda h, words: (h, 0, 0)),
                pl.BlockSpec((1, HEAD_DIM, rows), lambda h, words: (h, 0, 0)),
                pl.BlockSpec((1, 4 * HEAD_DIM, rows), lambda h, words: (h, 0, 0)),
                pl.BlockSpec((HEAD_DIM, CODES), lambda h, words: (h, 0)),
            ]
            + [fixed(item) for item in (codes, sines, cosines, rot_cos, rot_sin, *extra)],
            out_specs=[fixed(item) for item in out_shape],
            scratch_shapes=([pltpu.VMEM(full_shape, F32)] if last else [])
            + [
                pltpu.VMEM((CODES + HEAD_DIM, rows), BF16),
                pltpu.VMEM((rows, rows), BF16),
                pltpu.VMEM((CODES, rows), BF16),
                pltpu.VMEM((HEAD_DIM, rows), F32),
            ],
        ),
        out_shape=out_shape,
        compiler_params=pltpu.CompilerParams(vmem_limit_bytes=VMEM_LIMIT),
        cost_estimate=pl.CostEstimate(
            flops=2 * heads * rows * (rows * 1400 + 200 * width + 128 * CODES),
            bytes_accessed=2 * heads * rows * rows + 12 * rows * width,
            transcendentals=0,
        ),
        name="attention_backward",
    )(
        words,
        *grads,
        *pieces,
        probs,
        att,
        heads_saved,
        box_own,
        codes,
        sines,
        cosines,
        rot_cos,
        rot_sin,
        *extra,
    )


def normed(value):
    centered = value - jnp.mean(value, axis=-1, keepdims=True)
    scale = lax.rsqrt(jnp.mean(centered * centered, axis=-1, keepdims=True) + 1e-05)
    return centered * scale, scale


def norm_back(grad, gain, unit, scale):
    scaled = grad * gain
    return scale * (
        scaled
        - jnp.mean(scaled, axis=-1, keepdims=True)
        - unit * jnp.mean(scaled * unit, axis=-1, keepdims=True)
    )


def column_sum(value):
    return jnp.sum(value, axis=0, keepdims=True)


def middle_kernel(pages, count, span, chunks, *refs):
    total = pages * count
    words_ref = refs[0]
    att_refs = refs[1 : 1 + total]
    (
        tok_ref,
        cot_ref,
        w_out_ref,
        vectors_ref,
        w_expand_ref,
        w_reduce_ref,
    ) = refs[1 + total : 7 + total]
    outs = refs[7 + total :]
    layer_ref, first_in_ref, theirs_ref, mine_ref, more_theirs_ref, more_mine_ref = outs[:6]
    grad_refs = outs[6 : 6 + count]
    (
        sums_ref,
        att_all,
        grad_all,
        unit_one,
        scale_one,
        first_wide,
        first_low,
        first_tall,
        active,
        slope,
        gathered,
        second_in,
        second_low,
    ) = outs[6 + count :]
    rank = words_ref[0]
    width = tok_ref.shape[1]
    block = tok_ref.shape[0] // pages
    step = pl.program_id(0)

    def rows_of(at):
        return pl.ds(pl.multiple_of((rank ^ at) * span, span), span)

    @pl.when(step == 0)
    def _():
        for page in range(pages):
            for at in range(count):
                att_all[rows_of(at), page * block : (page + 1) * block] = att_refs[
                    page * count + at
                ][...]
        branch = dot_tn(att_all[: w_out_ref.shape[0]], w_out_ref[...])
        unit, scale = normed(tok_ref[...].astype(F32) + branch)
        unit_one[...] = unit
        scale_one[...] = jnp.broadcast_to(scale, scale_one.shape)
        first_out = unit * vectors_ref[0:1] + vectors_ref[1:2]
        first_wide[...] = first_out
        first_low[...] = first_out.astype(BF16)
        first_tall[...] = first_out.T.astype(BF16)
        gathered[...] = jnp.zeros_like(gathered)
        sums_ref[...] = jnp.zeros_like(sums_ref)

    for chunk in range(chunks):

        @pl.when(step == chunk)
        def _(chunk=chunk):
            expanded = dot(first_low[...], w_expand_ref[...])
            gate = 0.5 + 0.5 * lax.erf(expanded * np.float32(np.sqrt(0.5)))
            bell = jnp.exp(expanded * expanded * -0.5) * np.float32(1.0 / np.sqrt(2.0 * np.pi))
            low = (expanded * gate).astype(BF16)
            active[chunk] = low
            slope[chunk] = gate + expanded * bell
            gathered[...] += dot(low, w_reduce_ref[...])

    @pl.when(step == chunks - 1)
    def _():
        unit, scale = normed(first_wide[...] + gathered[...])
        layer_ref[...] = (unit * vectors_ref[2:3] + vectors_ref[3:4]).astype(BF16)
        cot = cot_ref[...].astype(F32)
        sums_ref[2:3] = column_sum(cot * unit)
        sums_ref[3:4] = column_sum(cot)
        grad = norm_back(cot, vectors_ref[2:3], unit, scale)
        second_in[...] = grad
        second_low[...] = grad.astype(BF16)
        gathered[...] = grad

    for chunk in range(chunks):

        @pl.when(step == 2 * chunks - 1 - chunk)
        def _(chunk=chunk):
            grad_active = dot_nt(second_low[...], w_reduce_ref[...])
            grad_expanded = (grad_active * slope[chunk]).astype(BF16)
            grads_ref = mine_ref if chunk < chunks // 2 else theirs_ref
            grads_ref[:width] = dot(first_tall[...], grad_expanded).astype(BF16)
            grads_ref[width:] = dot_tn(active[chunk], second_low[...]).astype(BF16)
            gathered[...] += dot_nt(grad_expanded, w_expand_ref[...])

    @pl.when(step == 2 * chunks - 1)
    def _():
        unit = unit_one[...]
        grad_out = gathered[...]
        sums_ref[0:1] = column_sum(grad_out * unit)
        sums_ref[1:2] = column_sum(grad_out)
        grad = norm_back(grad_out, vectors_ref[0:1], unit, scale_one[:, :1])
        first_in_ref[...] = grad
        low = grad.astype(BF16)
        real = w_out_ref.shape[0]
        half = real // 2
        core = words_ref[2]
        for ref, side in ((more_mine_ref, core), (more_theirs_ref, 1 - core)):
            rows = pl.ds(pl.multiple_of(side * half, half), half)
            ref[:half] = dot(att_all[rows], low).astype(BF16)
            ref[half:] = jnp.zeros((ref.shape[0] - half, width), BF16)
            ref[half : half + 16] = sums_ref[...].astype(BF16)
        if grad_all.shape[0] > real:
            grad_all[real:] = jnp.zeros((grad_all.shape[0] - real, low.shape[0]), BF16)
        grad_all[:real] = dot_nt(w_out_ref[...], low).astype(BF16)
        for at in range(count):
            grad_refs[at][...] = grad_all[rows_of(at)]


def middle(words, att_parts, tok, cot, w_out, vectors, w_expand, w_reduce, pages, more):
    rows, width = tok.shape
    count = len(att_parts) // pages
    span, block = att_parts[0].shape
    hidden = w_expand.shape[1]
    chunks = hidden // width
    pairs = chunks // 2

    def whole(array):
        return pl.BlockSpec(array.shape, lambda s, words: (0,) * len(array.shape))

    def chunk_at(s, words):
        at = jnp.minimum(s, 2 * chunks - 1 - s)
        return (at + words[2] * pairs) % chunks

    def theirs_at(s, words):
        return jnp.clip(2 * chunks - 1 - s - pairs, 0, pairs - 1), 0

    def mine_at(s, words):
        return jnp.clip(2 * chunks - 1 - s, 0, pairs - 1), 0

    shapes = [
        jax.ShapeDtypeStruct((rows, width), BF16),
        jax.ShapeDtypeStruct((rows, width), F32),
        jax.ShapeDtypeStruct((hidden, width), BF16),
        jax.ShapeDtypeStruct((hidden, width), BF16),
        jax.ShapeDtypeStruct((more, width), BF16),
        jax.ShapeDtypeStruct((more, width), BF16),
    ] + [jax.ShapeDtypeStruct((span, pages * block), BF16)] * count
    specs = [whole(item) for item in shapes]
    specs[2] = pl.BlockSpec((2 * width, width), theirs_at)
    specs[3] = pl.BlockSpec((2 * width, width), mine_at)
    return pl.pallas_call(
        functools.partial(middle_kernel, pages, count, span, chunks),
        grid_spec=pltpu.PrefetchScalarGridSpec(
            num_scalar_prefetch=1,
            grid=(2 * chunks,),
            in_specs=[whole(item) for item in att_parts]
            + [
                whole(tok),
                whole(cot),
                whole(w_out),
                whole(vectors),
                pl.BlockSpec((width, width), lambda s, words: (0, chunk_at(s, words))),
                pl.BlockSpec((width, width), lambda s, words: (chunk_at(s, words), 0)),
            ],
            out_specs=specs,
            scratch_shapes=[
                pltpu.VMEM((16, width), F32),
                pltpu.VMEM((count * span, rows), BF16),
                pltpu.VMEM((count * span, rows), BF16),
                pltpu.VMEM((rows, width), F32),
                pltpu.VMEM((rows, 128), F32),
                pltpu.VMEM((rows, width), F32),
                pltpu.VMEM((rows, width), BF16),
                pltpu.VMEM((width, rows), BF16),
                pltpu.VMEM((chunks, rows, width), BF16),
                pltpu.VMEM((chunks, rows, width), F32),
                pltpu.VMEM((rows, width), F32),
                pltpu.VMEM((rows, width), F32),
                pltpu.VMEM((rows, width), BF16),
            ],
        ),
        out_shape=shapes,
        compiler_params=pltpu.CompilerParams(vmem_limit_bytes=VMEM_LIMIT),
        cost_estimate=pl.CostEstimate(
            flops=2 * rows * width * (6 * hidden + 3 * width),
            bytes_accessed=8 * width * hidden + 16 * rows * width,
            transcendentals=2 * rows * hidden,
        ),
        name="middle",
    )(words, *att_parts, tok, cot, w_out, vectors, w_expand, w_reduce)


def input_kernel(pages, count, span, base, *refs):
    words_ref = refs[0]
    own_refs = refs[1 : 1 + pages]
    message_refs = refs[1 + pages : pages + count]
    weight_refs = refs[pages + count : 3 + pages + count]
    first_in_ref, out_ref, held = refs[3 + pages + count :]
    rank = words_ref[0]
    width = out_ref.shape[1]
    block = out_ref.shape[0] // pages
    for page in range(pages):
        for at in range(count):
            part = message_refs[at - 1] if at else own_refs[page]
            top = base + page * span if at else 0
            place = pl.multiple_of((rank ^ at) * span, span)
            for kind in range(3):
                held[kind, pl.ds(place, span), page * block : (page + 1) * block] = part[
                    top : top + span, kind * block : (kind + 1) * block
                ]
    total = dot(weight_refs[0][...], held[0, :width])
    for kind in range(1, 3):
        total = total + dot(weight_refs[kind][...], held[kind, :width])
    out_ref[...] = (first_in_ref[...] + total.T).astype(BF16)


def input_gradient(words, own, messages, base, span, weights, first_in):
    pages = len(own)
    count = 1 + len(messages)
    rows, width = first_in.shape
    vmem = pl.BlockSpec(memory_space=pltpu.VMEM)
    return pl.pallas_call(
        functools.partial(input_kernel, pages, count, span, base),
        in_specs=[pl.BlockSpec(memory_space=pltpu.SMEM)] + [vmem] * (pages + count + 3),
        out_specs=vmem,
        out_shape=jax.ShapeDtypeStruct((rows, width), BF16),
        scratch_shapes=[pltpu.VMEM((3, count * span, rows), BF16)],
        compiler_params=pltpu.CompilerParams(vmem_limit_bytes=VMEM_LIMIT),
        cost_estimate=pl.CostEstimate(
            flops=6 * rows * width * count * span,
            bytes_accessed=2 * width * (5 * rows + 3 * count * span),
            transcendentals=0,
        ),
        name="input_gradient",
    )(words, *own, *messages, *weights, first_in)


def local(body, name, words, arrays, shapes, costly=False):
    def kernel(words_ref, *refs):
        body(words_ref, refs[: len(arrays)], refs[len(arrays) :])

    vmem = pl.BlockSpec(memory_space=pltpu.VMEM)
    shapes = [jax.ShapeDtypeStruct(shape, kind) for shape, kind in shapes]
    moved = sum(item.size * item.dtype.itemsize for item in list(arrays) + shapes)
    cost = pl.CostEstimate(flops=0, bytes_accessed=moved, transcendentals=0)
    return pl.pallas_call(
        kernel,
        in_specs=[pl.BlockSpec(memory_space=pltpu.SMEM)] + [vmem] * len(arrays),
        out_specs=[vmem] * len(shapes),
        out_shape=shapes,
        compiler_params=pltpu.CompilerParams(vmem_limit_bytes=VMEM_LIMIT),
        cost_estimate=cost if costly else NO_COST,
        name=name,
    )(words, *arrays)


def shard(index, rows, base=0):
    return pl.ds(pl.multiple_of(base + index * rows, 16), rows)


def total_of(refs, rows=slice(None)):
    if len(refs) == 2 and all(ref.dtype == BF16 for ref in refs):
        return refs[0][rows] + refs[1][rows]
    total = refs[0][rows].astype(F32)
    for ref in refs[1:]:
        total = total + ref[rows].astype(F32)
    return total


def tree_sum(terms):
    while len(terms) > 1:
        terms = [terms[i] + terms[i + 1] for i in range(0, len(terms), 2)]
    return terms[0]


def bit_of(words, level):
    return lax.shift_right_logical(words[1], level) & 1


def pair_sum(words, mine, other):
    return after(words, mine) + other


def halve(words, level, mine, other):
    rows, width = mine.shape
    half = rows // 2

    def body(words, ins, outs):
        bit = bit_of(words, level)
        outs[0][...] = total_of(ins, shard(bit, half)).astype(BF16)
        outs[1][...] = total_of(ins, shard(1 - bit, half)).astype(BF16)

    return local(body, "halve", words, [mine, other], [((half, width), BF16)] * 2)


def join_halves(words, level, mine, other):
    words, mine = lax.optimization_barrier((words, mine))
    low = bit_of(words, level) == 0
    return jnp.concatenate([jnp.where(low, mine, other), jnp.where(low, other, mine)])


def across(block, level):
    return swapped(block, 1 << level, "depth")


class Plan:
    def __init__(self, rows, rows_a, more, span, width):
        self.count = lax.axis_size("blk")
        self.levels = lax.axis_size("depth").bit_length() - 1
        self.rows = rows
        self.rows_a = rows_a
        self.more = more
        self.span = span
        self.width = width
        self.a_ff = rows_a // self.count
        self.a_more = more // self.count
        self.a = self.a_ff + self.a_more
        self.b = (rows - rows_a) >> self.levels

    def shapes(self, *sizes):
        return [((rows, self.width), BF16) for rows in sizes]

    def scatter_one(self, words, halves):
        count, width = self.count, self.width
        a_ff, a_more = self.a_ff, self.a_more
        b_rows = (self.rows - self.rows_a) // count
        steps = count // 2

        def kernel(words_ref, *refs):
            parts = refs[6 : 6 + count]
            keep_ref, send_ref = refs[6 + count :]
            for i in range(count):

                @pl.when(pl.program_id(0) == i)
                def _(i=i):
                    parts[i][:a_ff] = total_of(refs[:2]).astype(BF16)
                    parts[i][a_ff:] = total_of(refs[2:4]).astype(BF16)
                    side = send_ref if i < steps else keep_ref
                    side[...] = total_of(refs[4:6]).astype(BF16)

        def there(rows):
            return pl.BlockSpec((rows, width), lambda i, words: (words[0] ^ i, 0))

        def b_at(i, words):
            bit = bit_of(words, 0)
            side = jnp.where(i < steps, 1 - bit, bit)
            return self.rows_a // b_rows + side * steps + i % steps, 0

        own_b = pl.BlockSpec((b_rows, width), b_at)
        shapes = [jax.ShapeDtypeStruct((self.a, width), BF16)] * count
        shapes += [jax.ShapeDtypeStruct((b_rows * steps, width), BF16)] * 2
        *parts_a, keep, send = pl.pallas_call(
            kernel,
            grid_spec=pltpu.PrefetchScalarGridSpec(
                num_scalar_prefetch=1,
                grid=(count,),
                in_specs=[there(a_ff)] * 2 + [there(a_more)] * 2 + [own_b] * 2,
                out_specs=[fixed(item) for item in shapes[:count]]
                + [
                    pl.BlockSpec((b_rows, width), lambda i, words: (jnp.maximum(i - steps, 0), 0)),
                    pl.BlockSpec((b_rows, width), lambda i, words: (jnp.minimum(i, steps - 1), 0)),
                ],
            ),
            out_shape=shapes,
            compiler_params=pltpu.CompilerParams(vmem_limit_bytes=VMEM_LIMIT),
            cost_estimate=NO_COST,
            name="scatter_one",
        )(words, *halves, *halves[:2])
        return [from_blk(part, i) for i, part in enumerate(parts_a)], keep, across(send, 0)

    def scatter_two(self, words, parts_a, keep_b, other_b, pages):
        count = self.count
        half = self.a // 2

        def body(words, ins, outs):
            bit = bit_of(words, 0)
            outs[0][...] = total_of(ins[:count], shard(bit, half)).astype(BF16)
            outs[1][...] = total_of(ins[:count], shard(1 - bit, half)).astype(BF16)
            part_b = total_of(ins[count : count + 2]).astype(BF16)
            outs[2][...] = part_b
            for i, out in enumerate(outs[3:]):
                out[: self.b] = part_b
                for page in range(len(pages)):
                    piece = ins[count + 2 + page * (count - 1) + i]
                    base = self.b + page * self.span
                    out[base : base + self.span, : piece.shape[1]] = piece[...]

        message = self.b + len(pages) * self.span
        shapes = self.shapes(half, half, self.b, *[message] * (count - 1))
        pieces = [piece for page in pages for piece in page[1:]]
        keep, send, part_b, *messages = local(
            body, "scatter_two", words, [*parts_a, keep_b, other_b, *pieces], shapes
        )
        return (
            keep,
            across(send, 0),
            part_b,
            [from_blk(item, i + 1) for i, item in enumerate(messages)],
        )

    def sum_b(self, words, part_b, messages):
        def body(words, ins, outs):
            terms = [ref[: self.b].astype(F32) for ref in ins]
            outs[0][...] = tree_sum(terms).astype(BF16)

        return local(body, "sum_b", words, [part_b, *messages], self.shapes(self.b))[0]

    def gather_b(self, words, part_b):
        for level in range(self.levels - 1, 0, -1):
            part_b = join_halves(words, level, part_b, across(part_b, level))
        return part_b, across(part_b, 0)


def gather_blk(part, cut, late=None):
    count = lax.axis_size("blk")
    if count != 4:
        return [(i, 0, from_blk(part, i)) for i in range(count)]
    one, two = swapped(part, 1), swapped(part, 2)
    if late is not None:
        one, two = after(late, (one, two))
    first, second = swapped(one[:cut], 2), swapped(two[cut:], 1)
    return [(0, 0, part), (1, 0, one), (2, 0, two), (3, 0, first), (3, cut, second)]


def with_core(pieces):
    return [(distance, base, from_core(item)) for distance, base, item in pieces]


SEGMENT = 256
SLOTS = 4


def widen_own(words, plan, pieces, halves_b, hidden):
    width = plan.width
    chunks = hidden // width
    pairs = chunks // 2
    per_matrix = width // SEGMENT
    arrays = [item for _, _, item in pieces] + list(halves_b)
    segments = []
    extras = []
    for at, (distance, base, item) in enumerate(pieces):
        stop = min(item.shape[0], plan.a_ff - base)
        for top in range(0, stop, SEGMENT):
            segments.append((at, top, min(SEGMENT, stop - top), distance, base + top))
        if base + item.shape[0] == plan.a:
            extras.append((at, distance))
    for at, item in enumerate(halves_b):
        for top in range(0, item.shape[0], SEGMENT):
            segments.append((len(pieces) + at, top, SEGMENT, None, top))

    def kernel(words_ref, *refs):
        ins = refs[: len(arrays)]
        joined_ref, expand_ref, reduce_ref, held, sems = refs[len(arrays) :]
        copies = []
        for index, (at, top, rows, distance, base) in enumerate(segments):
            slot = index % SLOTS
            if index >= SLOTS:
                copies[index - SLOTS].wait()
            part = ins[at][top : top + rows]
            held[slot, :rows] = part.astype(F32)
            if distance is None:
                half = ins[len(pieces)].shape[0]
                bit = bit_of(words_ref, 0)
                place = plan.rows_a + half * (bit if at == len(pieces) else 1 - bit) + base
            else:
                place = (words_ref[0] ^ distance) * plan.a_ff + base
            joined_ref[pl.ds(pl.multiple_of(place, SEGMENT), rows)] = part
            block = lax.div(place, SEGMENT)
            matrix = lax.div(block, per_matrix)
            row = (block - matrix * per_matrix) * SEGMENT
            chunk = (lax.div(matrix, 2) + words_ref[2] * pairs) % chunks
            column = pl.multiple_of(chunk * width, width)
            source = held.at[slot, :rows]
            to_expand = pltpu.make_async_copy(
                source,
                expand_ref.at[pl.ds(pl.multiple_of(row, SEGMENT), rows), pl.ds(column, width)],
                sems.at[slot],
            )
            to_reduce = pltpu.make_async_copy(
                source,
                reduce_ref.at[pl.ds(pl.multiple_of(column + row, SEGMENT), rows)],
                sems.at[slot],
            )
            is_expand = lax.rem(matrix, 2) == 0
            pl.when(is_expand)(to_expand.start)
            pl.when(jnp.logical_not(is_expand))(to_reduce.start)
            copies.append(to_reduce)
        for at, distance in extras:
            rows = shard(words_ref[0] ^ distance, plan.a_more, plan.rows)
            joined_ref[rows] = ins[at][ins[at].shape[0] - plan.a_more :]
        for copy in copies[-SLOTS:]:
            copy.wait()

    assert all(base % SEGMENT == 0 for *_, base in segments)
    vmem = pl.BlockSpec(memory_space=pltpu.VMEM)
    anywhere = pl.BlockSpec(memory_space=pl.ANY)
    return pl.pallas_call(
        kernel,
        in_specs=[pl.BlockSpec(memory_space=pltpu.SMEM)] + [vmem] * len(arrays),
        out_specs=[vmem, anywhere, anywhere],
        out_shape=[
            jax.ShapeDtypeStruct((plan.rows + plan.more, width), BF16),
            jax.ShapeDtypeStruct((width, hidden), F32),
            jax.ShapeDtypeStruct((hidden, width), F32),
        ],
        scratch_shapes=[
            pltpu.VMEM((SLOTS, SEGMENT, width), F32),
            pltpu.SemaphoreType.DMA((SLOTS,)),
        ],
        compiler_params=pltpu.CompilerParams(vmem_limit_bytes=VMEM_LIMIT),
        cost_estimate=pl.CostEstimate(
            flops=0, bytes_accessed=6 * hidden * width, transcendentals=0
        ),
        name="widen_own",
    )(words, *arrays)


def widen_other(words, joined, expand, reduce):
    width, hidden = expand.shape
    chunks = hidden // width
    pairs = chunks // 2

    def kernel(words_ref, half_ref, before_ref, before_too_ref, expand_ref, reduce_ref):
        expand_ref[...] = half_ref[:width].astype(F32)
        reduce_ref[...] = half_ref[width:].astype(F32)

    def place(s, words):
        return (s + (words[2] + 1) * pairs) % chunks

    anywhere = pl.BlockSpec(memory_space=pl.ANY)
    return pl.pallas_call(
        kernel,
        grid_spec=pltpu.PrefetchScalarGridSpec(
            num_scalar_prefetch=1,
            grid=(pairs,),
            in_specs=[
                pl.BlockSpec((2 * width, width), lambda s, words: (s, 0)),
                anywhere,
                anywhere,
            ],
            out_specs=[
                pl.BlockSpec((width, width), lambda s, words: (0, place(s, words))),
                pl.BlockSpec((width, width), lambda s, words: (place(s, words), 0)),
            ],
        ),
        out_shape=[
            jax.ShapeDtypeStruct((width, hidden), F32),
            jax.ShapeDtypeStruct((hidden, width), F32),
        ],
        input_output_aliases={2: 0, 3: 1},
        compiler_params=pltpu.CompilerParams(vmem_limit_bytes=VMEM_LIMIT),
        cost_estimate=pl.CostEstimate(
            flops=0, bytes_accessed=6 * hidden * width, transcendentals=0
        ),
        name="widen_other",
    )(words, joined, expand, reduce)


def finished(words, plan, heads, joined, side, before=()):
    count = plan.count
    span = plan.span
    width = plan.width
    half_rows = width // 2
    arrays = [item for _, _, item in heads]

    def kernel(words_ref, *refs):
        heads_refs, refs = refs[: len(heads)], refs[len(heads) :]
        extra_ref, refs = refs[0], refs[1 + len(before) :]
        outs, refs = refs[:5], refs[5:]
        gathered, wide, project, sems = refs
        rank = words_ref[0]
        half = words_ref[2] ^ side
        for ref, (distance, base, _) in zip(heads_refs, heads):
            rows = ref.shape[0]
            place = pl.multiple_of((rank ^ distance) * span, HEAD_DIM)
            for part in range(2):
                low, high = max(base, part * span), min(base + rows, (part + 1) * span)
                if low < high:
                    gathered[part, pl.ds(place + (low - part * span), high - low)] = ref[
                        low - base : high - base
                    ]
        for part in range(2):
            wide[part] = gathered[part, :width].astype(F32).T
        project[...] = extra_ref[:half_rows].astype(F32)

        @pl.when(half == 1)
        def _():
            wide[1] = entry_order(wide[1])

        def copy(source, target, at):
            return pltpu.make_async_copy(source, target, sems.at[at])

        for part in range(2):
            pl.when(half == 0)(copy(wide.at[part], outs[part], part).start)
            pl.when(half == 1)(copy(wide.at[part], outs[2 + part], part).start)
        rows = pl.ds(pl.multiple_of(half * half_rows, half_rows), half_rows)
        last = copy(project, outs[4].at[rows], 2)
        last.start()
        for part in range(2):
            copy(wide.at[part], outs[part], part).wait()
        last.wait()

    def whole(item):
        return pl.BlockSpec(item.shape, lambda s: (0, 0))

    more = pl.BlockSpec((plan.more, width), lambda s: (plan.rows // plan.more, 0))
    anywhere = pl.BlockSpec(memory_space=pl.ANY)
    first = 2 + len(heads)
    shapes = [jax.ShapeDtypeStruct((width, width), F32)] * 5
    return pl.pallas_call(
        kernel,
        grid=(1,),
        in_specs=[pl.BlockSpec(memory_space=pltpu.SMEM)]
        + [whole(item) for item in arrays]
        + [more]
        + [anywhere] * len(before),
        out_specs=[anywhere] * 5,
        out_shape=shapes,
        scratch_shapes=[
            pltpu.VMEM((2, count * span, width), BF16),
            pltpu.VMEM((2, width, width), F32),
            pltpu.VMEM((half_rows, width), F32),
            pltpu.SemaphoreType.DMA((3,)),
        ],
        input_output_aliases={first + at: at for at in range(len(before))},
        compiler_params=pltpu.CompilerParams(vmem_limit_bytes=VMEM_LIMIT),
        cost_estimate=pl.CostEstimate(
            flops=0, bytes_accessed=16 * width * width, transcendentals=0
        ),
        name="finish",
    )(words, *arrays, joined, *before)


def per_device(
    tokens,
    boxes,
    w_query,
    w_key,
    w_value,
    w_output,
    box_weight,
    first_gain,
    first_shift,
    w_expand,
    w_reduce,
    second_gain,
    second_shift,
    cotangent,
):
    pages, block, width = tokens.shape
    count = lax.axis_size("blk")
    depth = lax.axis_size("depth")
    words = jnp.stack(
        [lax.axis_index("blk"), lax.axis_index("depth"), lax.axis_index("core")]
    ).astype(jnp.int32)
    hidden = w_expand.shape[1]
    span = -(-HEADS // count) * HEAD_DIM
    unit = 16 * count * depth
    more = -(-(width // 2 + 16) // unit) * unit

    own_places = jnp.stack([boxes[0] + boxes[2], boxes[1] + boxes[3]], axis=1)
    own_places = jnp.stack([lax.shift_right_logical(own_places, 6), own_places & 63], axis=2)
    own_places = own_places.reshape(4 * pages, block).astype(BF16)
    own_places = jnp.pad(own_places, ((0, 16 - 4 * pages), (0, width - block)))
    message = jnp.concatenate([tokens[0], own_places])
    messages = [from_blk(message, i) for i in range(count)]
    w_own, box_own, rot_cos, rot_sin = prepare(
        words, w_query, w_key, w_value, box_weight, span, count * block
    )
    messages, rot_cos = lax.optimization_barrier((messages, rot_cos))
    own = after(messages, tokens[1])
    pieces = [messages, [from_blk(own, i) for i in range(count)]]

    saved = []
    att_parts = []
    for page in range(pages):
        results = attention_forward(
            words, page, messages, pieces[page], w_own, box_own, rot_cos, rot_sin
        )
        saved.append(results[:6])
        att_parts += [from_blk(results[6 + i], i) for i in range(count)]

    vectors = jnp.stack([first_gain, first_shift, second_gain, second_shift])
    results = middle(
        words,
        att_parts,
        tokens.reshape(pages * block, width),
        cotangent.reshape(pages * block, width),
        w_output,
        vectors,
        w_expand,
        w_reduce,
        pages,
        more,
    )
    layer_out, first_in, theirs, mine, more_theirs, more_mine = results[:6]
    grads = [from_blk(results[6 + i], i) for i in range(count)]
    plan = Plan(hidden, 2 * hidden // 3, more, span, width)
    parts_a, keep_b, other_b = plan.scatter_one(
        after(grads[:2], words), [mine, from_core(theirs), more_mine, from_core(more_theirs)]
    )

    def backward(page, words, before=None):
        return attention_backward(
            words,
            page,
            grads,
            pieces[page],
            saved[page],
            box_own,
            rot_cos,
            rot_sin,
            before,
        )

    *pre_one, before = backward(0, after(parts_a[0], words))
    done = before
    for level in range(1, plan.levels):
        keep_b, send_b = halve(after(done, words), level, keep_b, other_b)
        other_b = across(send_b, level)
        done = keep_b
    *pre_two, heads_mine, heads_theirs = backward(1, after(done, words), before)
    own = [pre_one[0], pre_two[0]]
    part_a, other_a, part_b, messages_b = plan.scatter_two(
        after(heads_mine, words), parts_a, keep_b, other_b, [pre_one, pre_two]
    )
    heads, other = halve(
        after(part_a, words), 0, heads_mine, from_core(after(part_a, heads_theirs))
    )
    part_a = pair_sum(after(heads, words), part_a, other_a)
    other = across(after(part_a, other), 0)
    heads = pair_sum(after(part_a, words), heads, other)
    done = heads
    for level in range(1, plan.levels):
        part_a = pair_sum(after(done, words), part_a, across(part_a, level))
        done = part_a
    other_a = across(part_a, 0)
    other = across(heads, 1)
    part_b = plan.sum_b(after(part_a, words), part_b, messages_b)
    heads = pair_sum(after(part_b, words), heads, other)
    part_a = join_halves(after(heads, words), 0, part_a, other_a)
    part_b = after(part_a, part_b)
    for level in range(2, plan.levels):
        heads = pair_sum(words, heads, across(heads, level))
    input_grad = input_gradient(
        after(part_a, words),
        own,
        messages_b,
        plan.b,
        span,
        (w_query, w_key, w_value),
        first_in,
    )
    heads = join_halves(after(input_grad, words), 0, heads, across(heads, 0))
    parts_b = plan.gather_b(after(heads, words), part_b)
    pieces_a = gather_blk(part_a, plan.a_ff // 2, parts_b[0])
    heads = after(([item for _, _, item in pieces_a], parts_b), heads)
    joined, *wide = widen_own(after(heads, words), plan, pieces_a, parts_b, hidden)
    at = plan.rows + width // 2
    sums = [joined[at + i].astype(F32) for i in range(4)]
    pieces_heads = gather_blk(heads, span, (joined, sums))
    joined_other = from_core(after(pieces_heads[1][2], joined))
    grads = finished(words, plan, pieces_heads, joined, 0)
    grad_expand, grad_reduce = widen_other(after(grads, words), joined_other, *wide)
    grad_query, grad_key, grad_value, grad_box, grad_project = finished(
        after(grad_expand, words), plan, with_core(pieces_heads), joined_other, 1, grads
    )
    return (
        layer_out.reshape(tokens.shape),
        input_grad.reshape(tokens.shape),
        grad_query,
        grad_key,
        grad_value,
        grad_project,
        grad_box,
        sums[0],
        sums[1],
        grad_expand,
        grad_reduce,
        sums[2],
        sums[3],
    )


def solution(mesh):
    blocks, rest = mesh.devices.shape
    parts = jax.sharding.Mesh(
        mesh.devices.reshape(blocks, rest // 2, 2), ("blk", "depth", "core")
    )
    split = P(("depth", "core"), "blk", None)
    return jax.shard_map(
        per_device,
        mesh=parts,
        in_specs=(split, P(None, ("depth", "core"), "blk")) + (P(),) * 11 + (split,),
        out_specs=(split, split) + (P(),) * 11,
        check_vma=False,
    )
```

```python
import functools

import jax
import jax.numpy as jnp
import numpy as np
from jax import lax
from jax.experimental import pallas as pl
from jax.experimental.pallas import tpu as pltpu
from jax.sharding import PartitionSpec as P

HEADS = 12
HEAD_DIM = 64
HALF = 32
FREQS = 192
CODES = 4 * FREQS
VMEM_LIMIT = 60 * 1024 * 1024
NO_COST = pl.CostEstimate(flops=0, bytes_accessed=0, transcendentals=0)
F32 = jnp.float32
BF16 = jnp.bfloat16


def dot(left, right):
    return lax.dot_general(left, right, (((1,), (0,)), ((), ())), preferred_element_type=F32)


def dot_nt(left, right):
    return lax.dot_general(left, right, (((1,), (1,)), ((), ())), preferred_element_type=F32)


def dot_tn(left, right):
    return lax.dot_general(left, right, (((0,), (0,)), ((), ())), preferred_element_type=F32)


def swapped(block, distance, axis="blk"):
    count = lax.axis_size(axis)
    return lax.ppermute(block, axis, [(i, i ^ distance) for i in range(count)])


def from_blk(block, distance):
    return swapped(block, distance) if distance else block


def from_core(block):
    return swapped(block, 1, "core")


def after(done, value):
    return lax.optimization_barrier((value, done))[0]


def turned(upper, lower, cosines, sines):
    return upper * cosines - lower * sines, lower * cosines + upper * sines


def entry_order(rows):
    return jnp.concatenate(
        [
            rows[:FREQS],
            rows[2 * FREQS : 3 * FREQS],
            rows[FREQS : 2 * FREQS],
            rows[3 * FREQS :],
        ],
        axis=0,
    )


def angle_tables():
    rates = np.float32(10000.0) ** (-np.arange(FREQS, dtype=np.float32) / np.float32(FREQS))
    tables = []
    for places in (32.0 * np.arange(32), 0.5 * np.arange(64)):
        angles = rates.astype(np.float64)[:, None] * places[None, :]
        left = np.concatenate([np.sin(angles), np.cos(angles)])
        parts = []
        for _ in range(3):
            parts.append(left.astype(jnp.bfloat16))
            left = left - parts[-1].astype(np.float64)
        tables.append(np.concatenate(parts, axis=1))
    return tables


def rotary_tables(length):
    rates = np.float32(10000.0) ** (-np.arange(HALF, dtype=np.float32) / np.float32(HALF))
    angles = np.arange(length, dtype=np.float32)[None, :] * rates[:, None]
    angles = angles.astype(np.float64)
    return np.cos(angles).astype(np.float32), np.sin(angles).astype(np.float32)


def prepare_kernel(
    words_ref,
    query_ref,
    key_ref,
    value_ref,
    box_ref,
    cos_ref,
    sin_ref,
    own_ref,
    own_box_ref,
    own_cos_ref,
    own_sin_ref,
):
    rank = words_ref[0]
    span = own_box_ref.shape[0]
    width = query_ref.shape[1]
    count = lax.axis_size("blk")
    block = cos_ref.shape[1] // count
    row = lax.broadcasted_iota(jnp.int32, (span, width), 0) + rank * span
    column = lax.broadcasted_iota(jnp.int32, (span, width), 1)
    pick = jnp.where(row == column, 1.0, 0.0).astype(BF16)
    for kind, ref in enumerate((query_ref, key_ref, value_ref)):
        own_ref[kind * span : (kind + 1) * span] = dot_nt(pick, ref[...]).astype(BF16)
    own_box_ref[...] = dot_nt(pick, entry_order(box_ref[...])).astype(BF16)
    for i in range(count):
        from_cols = pl.ds(pl.multiple_of((rank ^ i) * block, block), block)
        own_cos_ref[:, i * block : (i + 1) * block] = cos_ref[:, from_cols]
        own_sin_ref[:, i * block : (i + 1) * block] = sin_ref[:, from_cols]


def prepare(words, w_query, w_key, w_value, box_weight, span, length):
    width = w_query.shape[0]
    vmem = pl.BlockSpec(memory_space=pltpu.VMEM)
    return pl.pallas_call(
        prepare_kernel,
        in_specs=[pl.BlockSpec(memory_space=pltpu.SMEM)] + [vmem] * 6,
        out_specs=[vmem] * 4,
        out_shape=[
            jax.ShapeDtypeStruct((3 * span, width), BF16),
            jax.ShapeDtypeStruct((span, CODES), BF16),
            jax.ShapeDtypeStruct((HALF, length), F32),
            jax.ShapeDtypeStruct((HALF, length), F32),
        ],
        compiler_params=pltpu.CompilerParams(vmem_limit_bytes=VMEM_LIMIT),
        cost_estimate=pl.CostEstimate(
            flops=8 * span * width * width, bytes_accessed=10 * width * width, transcendentals=0
        ),
        name="prepare",
    )(words, w_query, w_key, w_value, box_weight, *map(jnp.asarray, rotary_tables(length)))


def fold(value, combine):
    while value.shape[0] > 8:
        half = value.shape[0] // 2
        value = combine(value[:half], value[half:])
    return value


def write_codes(page, place_refs, high_ref, low_ref, sin_ref, cos_ref, codes_ref):
    block = sin_ref.shape[1] // len(place_refs)

    def looked_up(table_ref, index):
        spots = table_ref.shape[1] // 3
        rows = lax.broadcasted_iota(jnp.int32, (spots, block), 0).astype(F32)
        once = jnp.where(rows == index, 1.0, 0.0)
        found = dot(table_ref[...], jnp.concatenate([once] * 3, axis=0).astype(BF16))
        return found[:FREQS], found[FREQS:]

    for i, place_ref in enumerate(place_refs):
        columns = slice(i * block, (i + 1) * block)
        places = place_ref[:, :block].astype(F32)
        for axis in range(2):
            at = 4 * page + 2 * axis
            high_sin, high_cos = looked_up(high_ref, places[at : at + 1])
            low_sin, low_cos = looked_up(low_ref, places[at + 1 : at + 2])
            sines = high_sin * low_cos + high_cos * low_sin
            cosines = high_cos * low_cos - high_sin * low_sin
            rows = slice(axis * FREQS, (axis + 1) * FREQS)
            later = slice((2 + axis) * FREQS, (3 + axis) * FREQS)
            sin_ref[rows, columns] = sines
            cos_ref[rows, columns] = cosines
            codes_ref[rows, columns] = sines.astype(BF16)
            codes_ref[later, columns] = cosines.astype(BF16)


def forward_kernel(page, count, words_ref, *refs):
    place_refs, refs = refs[:count], refs[count:]
    piece_refs, refs = refs[:count], refs[count:]
    high_ref, low_ref, w_ref, box_ref, rot_cos_ref, rot_sin_ref = refs[:6]
    probs_ref, att_ref, heads_ref, sin_ref, cos_ref, codes_ref = refs[6:12]
    low_refs = refs[12 : 12 + count]
    tok_ref, pre_ref, kc_ref, qr_ref = refs[12 + count :]
    rows = tok_ref.shape[0]
    block = rows // count
    head = pl.program_id(0)
    span = pl.num_programs(0) * HEAD_DIM

    @pl.when(head == 0)
    def _():
        for i in range(count):
            tok_ref[i * block : (i + 1) * block] = piece_refs[i][...]
        pre_ref[...] = dot_nt(w_ref[...], tok_ref[...])
        write_codes(page, place_refs, high_ref, low_ref, sin_ref, cos_ref, codes_ref)
        kc_ref[:, :CODES] = codes_ref[...].astype(F32).T.astype(BF16)

    def pre(kind):
        at = kind * span + head * HEAD_DIM
        return pre_ref[pl.ds(pl.multiple_of(at, HEAD_DIM), HEAD_DIM)]

    rot_cos = rot_cos_ref[...]
    rot_sin = rot_sin_ref[...]
    query_pre = pre(0).astype(BF16)
    wide = query_pre.astype(F32)
    query = jnp.concatenate(turned(wide[:HALF], wide[HALF:], rot_cos, rot_sin), axis=0)
    key_pre = pre(1)
    key = jnp.concatenate(turned(key_pre[:HALF], key_pre[HALF:], rot_cos, rot_sin), axis=0)
    value = pre(2).astype(BF16)
    heads_ref[0, :HEAD_DIM] = query_pre
    heads_ref[0, HEAD_DIM : 2 * HEAD_DIM] = query.astype(BF16)
    heads_ref[0, 2 * HEAD_DIM : 3 * HEAD_DIM] = key.astype(BF16)
    heads_ref[0, 3 * HEAD_DIM :] = value
    kc_ref[:, CODES:] = key.T.astype(BF16)
    qr_ref[CODES:] = (query * 0.125).astype(BF16)
    step = min(256, block)

    def logits_at(at):
        part = slice(at, at + step)
        projected = dot_tn(box_ref[...], query_pre[:, part])
        sines = sin_ref[:, part]
        cosines = cos_ref[:, part]
        upper = projected[: 2 * FREQS]
        lower = projected[2 * FREQS :]
        qr_ref[: 2 * FREQS, part] = ((upper * cosines + lower * sines) * 0.125).astype(BF16)
        qr_ref[2 * FREQS : CODES, part] = ((lower * cosines - upper * sines) * 0.125).astype(BF16)
        return dot(kc_ref[...], qr_ref[:, part])

    following = logits_at(0)
    for at in range(0, rows, step):
        logits = following
        if at + step < rows:
            following = logits_at(at + step)
        peak = jnp.max(fold(logits, jnp.maximum), axis=0, keepdims=True)
        weight = jnp.exp(logits - peak)
        total = jnp.sum(fold(weight, jnp.add), axis=0, keepdims=True)
        probs = (weight * (1.0 / total)).astype(BF16)
        probs_ref[0, :, at : at + step] = probs
        attended = dot(value, probs)
        att_ref[0, :, at : at + step] = attended
        inner = at % block
        low_refs[at // block][:, inner : inner + step] = attended.astype(BF16)


def fixed(array):
    return pl.BlockSpec(array.shape, lambda *at: (0,) * len(array.shape))


def attention_forward(words, page, messages, pieces, w_own, box_own, rot_cos, rot_sin):
    count = len(messages)
    block, width = messages[0].shape[0] - 16, messages[0].shape[1]
    rows = count * block
    span = box_own.shape[0]
    heads = span // HEAD_DIM
    tables = [jnp.asarray(item) for item in angle_tables()]
    specs = [pl.BlockSpec((block, width), lambda h, words: (0, 0))] * count
    places = pl.BlockSpec((16, width), lambda h, words: (block // 16, 0))
    out_shape = [
        jax.ShapeDtypeStruct((heads, rows, rows), BF16),
        jax.ShapeDtypeStruct((heads, HEAD_DIM, rows), F32),
        jax.ShapeDtypeStruct((heads, 4 * HEAD_DIM, rows), BF16),
        jax.ShapeDtypeStruct((2 * FREQS, rows), F32),
        jax.ShapeDtypeStruct((2 * FREQS, rows), F32),
        jax.ShapeDtypeStruct((CODES, rows), BF16),
    ] + [jax.ShapeDtypeStruct((span, block), BF16)] * count
    return pl.pallas_call(
        functools.partial(forward_kernel, page, count),
        grid_spec=pltpu.PrefetchScalarGridSpec(
            num_scalar_prefetch=1,
            grid=(heads,),
            in_specs=[places] * count
            + specs
            + [fixed(item) for item in (*tables, w_own)]
            + [
                pl.BlockSpec((HEAD_DIM, CODES), lambda h, words: (h, 0)),
                fixed(rot_cos),
                fixed(rot_sin),
            ],
            out_specs=[
                pl.BlockSpec((1, rows, rows), lambda h, words: (h, 0, 0)),
                pl.BlockSpec((1, HEAD_DIM, rows), lambda h, words: (h, 0, 0)),
                pl.BlockSpec((1, 4 * HEAD_DIM, rows), lambda h, words: (h, 0, 0)),
            ]
            + [fixed(item) for item in out_shape[3:6]]
            + [pl.BlockSpec((HEAD_DIM, block), lambda h, words: (h, 0))] * count,
            scratch_shapes=[
                pltpu.VMEM((rows, width), BF16),
                pltpu.VMEM((3 * span, rows), F32),
                pltpu.VMEM((rows, CODES + HEAD_DIM), BF16),
                pltpu.VMEM((CODES + HEAD_DIM, rows), BF16),
            ],
        ),
        out_shape=out_shape,
        compiler_params=pltpu.CompilerParams(vmem_limit_bytes=VMEM_LIMIT),
        cost_estimate=pl.CostEstimate(
            flops=2 * heads * rows * (rows * 1100 + 200 * width + 64 * CODES),
            bytes_accessed=2 * heads * rows * rows + 12 * rows * width,
            transcendentals=heads * rows * rows,
        ),
        name="attention_forward",
    )(words, *messages, *pieces, *tables, w_own, box_own, rot_cos, rot_sin)


def backward_kernel(count, last, words_ref, *refs):
    grad_refs, refs = refs[:count], refs[count:]
    piece_refs, refs = refs[:count], refs[count:]
    probs_ref, att_ref, heads_ref, box_ref, codes_ref, sin_ref, cos_ref = refs[:7]
    rot_cos_ref, rot_sin_ref = refs[7:9]
    refs = refs[9:]
    if last:
        before_ref, refs = refs[0], refs[1:]
    pre_refs, refs = refs[:count], refs[count:]
    if last:
        mine_ref, theirs_ref, *refs = refs
    weight_grad_ref, kc_ref, logit_grad_ref, entry_grad_ref, turned_ref = refs
    block, width = piece_refs[0].shape
    rows = count * block
    head = pl.program_id(0)
    span = pl.num_programs(0) * HEAD_DIM

    @pl.when(head == 0)
    def _():
        kc_ref[:CODES] = codes_ref[...]

    kc_ref[CODES:] = heads_ref[0, 2 * HEAD_DIM : 3 * HEAD_DIM]
    packed = heads_ref[0].astype(F32).T.astype(BF16)
    query_pre = packed[:, :HEAD_DIM]
    query = packed[:, HEAD_DIM : 2 * HEAD_DIM]
    value = packed[:, 3 * HEAD_DIM :] * jnp.asarray(0.125, BF16)
    rot_cos = rot_cos_ref[...]
    rot_sin = rot_sin_ref[...]
    grad = jnp.concatenate([ref[...] for ref in grad_refs], axis=1)
    grad_tall = grad.astype(F32).T.astype(BF16)
    offsets = jnp.sum(grad.astype(F32) * att_ref[0], axis=0, keepdims=True) * 0.125
    step = min(256, block)
    place = pl.multiple_of(head * HEAD_DIM, HEAD_DIM)
    here = pl.ds(place, HEAD_DIM)

    def logits_back(at):
        part = slice(at, at + step)
        grad_probs = dot(value, grad[:, part])
        logit_grad_ref[:, part] = (
            probs_ref[0, :, part].astype(F32) * (grad_probs - offsets[:, part])
        ).astype(BF16)

    logits_back(0)
    for at in range(0, rows, step):
        if at + step < rows:
            logits_back(at + step)
        part = slice(at, at + step)
        back = dot(kc_ref[...], logit_grad_ref[:, part])
        sines = sin_ref[:, part]
        cosines = cos_ref[:, part]
        upper = back[: 2 * FREQS]
        lower = back[2 * FREQS : CODES]
        entry_grad_ref[: 2 * FREQS, part] = (upper * cosines - lower * sines).astype(BF16)
        entry_grad_ref[2 * FREQS :, part] = (lower * cosines + upper * sines).astype(BF16)
        first = back[CODES : CODES + HALF]
        second = back[CODES + HALF :]
        turned_ref[:HALF, part], turned_ref[HALF:, part] = turned(
            first, second, rot_cos[:, part], -rot_sin[:, part]
        )
    key_flat = dot(logit_grad_ref[...], query).T
    value_low = dot(probs_ref[0], grad_tall).T.astype(BF16)
    query_low = (turned_ref[...] + dot(box_ref[...], entry_grad_ref[...])).astype(BF16)
    key_low = jnp.concatenate(
        turned(key_flat[:HALF], key_flat[HALF:], rot_cos, -rot_sin), axis=0
    ).astype(BF16)
    for i in range(count):
        columns = slice(i * block, (i + 1) * block)
        pre_refs[i][here, :block] = query_low[:, columns]
        pre_refs[i][here, block : 2 * block] = key_low[:, columns]
        pre_refs[i][here, 2 * block :] = value_low[:, columns]
    weight_grad_ref[pl.ds(3 * span + place, HEAD_DIM)] = dot(entry_grad_ref[...], query_pre).T

    @pl.when(head == pl.num_programs(0) - 1)
    def _():
        for kind in range(3):
            columns = slice(kind * block, (kind + 1) * block)
            total = dot(pre_refs[0][:, columns], piece_refs[0][...])
            for i in range(1, count):
                total = total + dot(pre_refs[i][:, columns], piece_refs[i][...])
            weight_grad_ref[kind * span : (kind + 1) * span] = total
        if last:
            half = 2 * span
            core = words_ref[2]
            ours = pl.ds(pl.multiple_of(core * half, half), half)
            there = pl.ds(pl.multiple_of((1 - core) * half, half), half)
            mine_ref[...] = weight_grad_ref[ours] + before_ref[ours]
            theirs_ref[...] = (weight_grad_ref[there] + before_ref[there]).astype(BF16)


def attention_backward(
    words, page, grads, pieces, saved, box_own, rot_cos, rot_sin, before=None
):
    probs, att, heads_saved, sines, cosines, codes = saved
    count = len(pieces)
    rows, width = probs.shape[1], pieces[0].shape[1]
    block = rows // count
    span = box_own.shape[0]
    heads = span // HEAD_DIM
    last = before is not None
    extra = (before,) if last else ()
    full_shape = (4 * span, width)
    specs = [pl.BlockSpec((block, width), lambda h, words: (0, 0))] * count
    out_shape = [jax.ShapeDtypeStruct((span, 3 * block), BF16)] * count
    if last:
        out_shape += [
            jax.ShapeDtypeStruct((2 * span, width), F32),
            jax.ShapeDtypeStruct((2 * span, width), BF16),
        ]
    else:
        out_shape.append(jax.ShapeDtypeStruct(full_shape, F32))
    return pl.pallas_call(
        functools.partial(backward_kernel, count, last),
        grid_spec=pltpu.PrefetchScalarGridSpec(
            num_scalar_prefetch=1,
            grid=(heads,),
            in_specs=[pl.BlockSpec((HEAD_DIM, block), lambda h, words: (h, page))] * count
            + specs
            + [
                pl.BlockSpec((1, rows, rows), lambda h, words: (h, 0, 0)),
                pl.BlockSpec((1, HEAD_DIM, rows), lambda h, words: (h, 0, 0)),
                pl.BlockSpec((1, 4 * HEAD_DIM, rows), lambda h, words: (h, 0, 0)),
                pl.BlockSpec((HEAD_DIM, CODES), lambda h, words: (h, 0)),
            ]
            + [fixed(item) for item in (codes, sines, cosines, rot_cos, rot_sin, *extra)],
            out_specs=[fixed(item) for item in out_shape],
            scratch_shapes=([pltpu.VMEM(full_shape, F32)] if last else [])
            + [
                pltpu.VMEM((CODES + HEAD_DIM, rows), BF16),
                pltpu.VMEM((rows, rows), BF16),
                pltpu.VMEM((CODES, rows), BF16),
                pltpu.VMEM((HEAD_DIM, rows), F32),
            ],
        ),
        out_shape=out_shape,
        compiler_params=pltpu.CompilerParams(vmem_limit_bytes=VMEM_LIMIT),
        cost_estimate=pl.CostEstimate(
            flops=2 * heads * rows * (rows * 1400 + 200 * width + 128 * CODES),
            bytes_accessed=2 * heads * rows * rows + 12 * rows * width,
            transcendentals=0,
        ),
        name="attention_backward",
    )(
        words,
        *grads,
        *pieces,
        probs,
        att,
        heads_saved,
        box_own,
        codes,
        sines,
        cosines,
        rot_cos,
        rot_sin,
        *extra,
    )


def normed(value):
    centered = value - jnp.mean(value, axis=-1, keepdims=True)
    scale = lax.rsqrt(jnp.mean(centered * centered, axis=-1, keepdims=True) + 1e-05)
    return centered * scale, scale


def norm_back(grad, gain, unit, scale):
    scaled = grad * gain
    return scale * (
        scaled
        - jnp.mean(scaled, axis=-1, keepdims=True)
        - unit * jnp.mean(scaled * unit, axis=-1, keepdims=True)
    )


def column_sum(value):
    return jnp.sum(value, axis=0, keepdims=True)


def middle_kernel(pages, count, span, chunks, *refs):
    total = pages * count
    words_ref = refs[0]
    att_refs = refs[1 : 1 + total]
    (
        tok_ref,
        cot_ref,
        w_out_ref,
        vectors_ref,
        w_expand_ref,
        w_reduce_ref,
    ) = refs[1 + total : 7 + total]
    outs = refs[7 + total :]
    layer_ref, first_in_ref, theirs_ref, mine_ref, more_theirs_ref, more_mine_ref = outs[:6]
    grad_refs = outs[6 : 6 + count]
    (
        sums_ref,
        att_all,
        grad_all,
        unit_one,
        scale_one,
        first_wide,
        first_low,
        first_tall,
        active,
        slope,
        gathered,
        second_in,
        second_low,
    ) = outs[6 + count :]
    rank = words_ref[0]
    width = tok_ref.shape[1]
    block = tok_ref.shape[0] // pages
    step = pl.program_id(0)

    def rows_of(at):
        return pl.ds(pl.multiple_of((rank ^ at) * span, span), span)

    @pl.when(step == 0)
    def _():
        for page in range(pages):
            for at in range(count):
                att_all[rows_of(at), page * block : (page + 1) * block] = att_refs[
                    page * count + at
                ][...]
        branch = dot_tn(att_all[: w_out_ref.shape[0]], w_out_ref[...])
        unit, scale = normed(tok_ref[...].astype(F32) + branch)
        unit_one[...] = unit
        scale_one[...] = jnp.broadcast_to(scale, scale_one.shape)
        first_out = unit * vectors_ref[0:1] + vectors_ref[1:2]
        first_wide[...] = first_out
        first_low[...] = first_out.astype(BF16)
        first_tall[...] = first_out.T.astype(BF16)
        gathered[...] = jnp.zeros_like(gathered)
        sums_ref[...] = jnp.zeros_like(sums_ref)

    for chunk in range(chunks):

        @pl.when(step == chunk)
        def _(chunk=chunk):
            expanded = dot(first_low[...], w_expand_ref[...])
            gate = 0.5 + 0.5 * lax.erf(expanded * np.float32(np.sqrt(0.5)))
            bell = jnp.exp(expanded * expanded * -0.5) * np.float32(1.0 / np.sqrt(2.0 * np.pi))
            low = (expanded * gate).astype(BF16)
            active[chunk] = low
            slope[chunk] = gate + expanded * bell
            gathered[...] += dot(low, w_reduce_ref[...])

    @pl.when(step == chunks - 1)
    def _():
        unit, scale = normed(first_wide[...] + gathered[...])
        layer_ref[...] = (unit * vectors_ref[2:3] + vectors_ref[3:4]).astype(BF16)
        cot = cot_ref[...].astype(F32)
        sums_ref[2:3] = column_sum(cot * unit)
        sums_ref[3:4] = column_sum(cot)
        grad = norm_back(cot, vectors_ref[2:3], unit, scale)
        second_in[...] = grad
        second_low[...] = grad.astype(BF16)
        gathered[...] = grad

    for chunk in range(chunks):

        @pl.when(step == 2 * chunks - 1 - chunk)
        def _(chunk=chunk):
            grad_active = dot_nt(second_low[...], w_reduce_ref[...])
            grad_expanded = (grad_active * slope[chunk]).astype(BF16)
            grads_ref = mine_ref if chunk < chunks // 2 else theirs_ref
            grads_ref[:width] = dot(first_tall[...], grad_expanded).astype(BF16)
            grads_ref[width:] = dot_tn(active[chunk], second_low[...]).astype(BF16)
            gathered[...] += dot_nt(grad_expanded, w_expand_ref[...])

    @pl.when(step == 2 * chunks - 1)
    def _():
        unit = unit_one[...]
        grad_out = gathered[...]
        sums_ref[0:1] = column_sum(grad_out * unit)
        sums_ref[1:2] = column_sum(grad_out)
        grad = norm_back(grad_out, vectors_ref[0:1], unit, scale_one[:, :1])
        first_in_ref[...] = grad
        low = grad.astype(BF16)
        real = w_out_ref.shape[0]
        half = real // 2
        core = words_ref[2]
        for ref, side in ((more_mine_ref, core), (more_theirs_ref, 1 - core)):
            rows = pl.ds(pl.multiple_of(side * half, half), half)
            ref[:half] = dot(att_all[rows], low).astype(BF16)
            ref[half:] = jnp.zeros((ref.shape[0] - half, width), BF16)
            ref[half : half + 16] = sums_ref[...].astype(BF16)
        if grad_all.shape[0] > real:
            grad_all[real:] = jnp.zeros((grad_all.shape[0] - real, low.shape[0]), BF16)
        grad_all[:real] = dot_nt(w_out_ref[...], low).astype(BF16)
        for at in range(count):
            grad_refs[at][...] = grad_all[rows_of(at)]


def middle(words, att_parts, tok, cot, w_out, vectors, w_expand, w_reduce, pages, more):
    rows, width = tok.shape
    count = len(att_parts) // pages
    span, block = att_parts[0].shape
    hidden = w_expand.shape[1]
    chunks = hidden // width
    pairs = chunks // 2

    def whole(array):
        return pl.BlockSpec(array.shape, lambda s, words: (0,) * len(array.shape))

    def chunk_at(s, words):
        at = jnp.minimum(s, 2 * chunks - 1 - s)
        return (at + words[2] * pairs) % chunks

    def theirs_at(s, words):
        return jnp.clip(2 * chunks - 1 - s - pairs, 0, pairs - 1), 0

    def mine_at(s, words):
        return jnp.clip(2 * chunks - 1 - s, 0, pairs - 1), 0

    shapes = [
        jax.ShapeDtypeStruct((rows, width), BF16),
        jax.ShapeDtypeStruct((rows, width), F32),
        jax.ShapeDtypeStruct((hidden, width), BF16),
        jax.ShapeDtypeStruct((hidden, width), BF16),
        jax.ShapeDtypeStruct((more, width), BF16),
        jax.ShapeDtypeStruct((more, width), BF16),
    ] + [jax.ShapeDtypeStruct((span, pages * block), BF16)] * count
    specs = [whole(item) for item in shapes]
    specs[2] = pl.BlockSpec((2 * width, width), theirs_at)
    specs[3] = pl.BlockSpec((2 * width, width), mine_at)
    return pl.pallas_call(
        functools.partial(middle_kernel, pages, count, span, chunks),
        grid_spec=pltpu.PrefetchScalarGridSpec(
            num_scalar_prefetch=1,
            grid=(2 * chunks,),
            in_specs=[whole(item) for item in att_parts]
            + [
                whole(tok),
                whole(cot),
                whole(w_out),
                whole(vectors),
                pl.BlockSpec((width, width), lambda s, words: (0, chunk_at(s, words))),
                pl.BlockSpec((width, width), lambda s, words: (chunk_at(s, words), 0)),
            ],
            out_specs=specs,
            scratch_shapes=[
                pltpu.VMEM((16, width), F32),
                pltpu.VMEM((count * span, rows), BF16),
                pltpu.VMEM((count * span, rows), BF16),
                pltpu.VMEM((rows, width), F32),
                pltpu.VMEM((rows, 128), F32),
                pltpu.VMEM((rows, width), F32),
                pltpu.VMEM((rows, width), BF16),
                pltpu.VMEM((width, rows), BF16),
                pltpu.VMEM((chunks, rows, width), BF16),
                pltpu.VMEM((chunks, rows, width), F32),
                pltpu.VMEM((rows, width), F32),
                pltpu.VMEM((rows, width), F32),
                pltpu.VMEM((rows, width), BF16),
            ],
        ),
        out_shape=shapes,
        compiler_params=pltpu.CompilerParams(vmem_limit_bytes=VMEM_LIMIT),
        cost_estimate=pl.CostEstimate(
            flops=2 * rows * width * (6 * hidden + 3 * width),
            bytes_accessed=8 * width * hidden + 16 * rows * width,
            transcendentals=2 * rows * hidden,
        ),
        name="middle",
    )(words, *att_parts, tok, cot, w_out, vectors, w_expand, w_reduce)


def input_kernel(pages, count, span, base, *refs):
    words_ref = refs[0]
    own_refs = refs[1 : 1 + pages]
    message_refs = refs[1 + pages : pages + count]
    weight_refs = refs[pages + count : 3 + pages + count]
    first_in_ref, out_ref, held = refs[3 + pages + count :]
    rank = words_ref[0]
    width = out_ref.shape[1]
    block = out_ref.shape[0] // pages
    for page in range(pages):
        for at in range(count):
            part = message_refs[at - 1] if at else own_refs[page]
            top = base + page * span if at else 0
            place = pl.multiple_of((rank ^ at) * span, span)
            for kind in range(3):
                held[kind, pl.ds(place, span), page * block : (page + 1) * block] = part[
                    top : top + span, kind * block : (kind + 1) * block
                ]
    total = dot(weight_refs[0][...], held[0, :width])
    for kind in range(1, 3):
        total = total + dot(weight_refs[kind][...], held[kind, :width])
    out_ref[...] = (first_in_ref[...] + total.T).astype(BF16)


def input_gradient(words, own, messages, base, span, weights, first_in):
    pages = len(own)
    count = 1 + len(messages)
    rows, width = first_in.shape
    vmem = pl.BlockSpec(memory_space=pltpu.VMEM)
    return pl.pallas_call(
        functools.partial(input_kernel, pages, count, span, base),
        in_specs=[pl.BlockSpec(memory_space=pltpu.SMEM)] + [vmem] * (pages + count + 3),
        out_specs=vmem,
        out_shape=jax.ShapeDtypeStruct((rows, width), BF16),
        scratch_shapes=[pltpu.VMEM((3, count * span, rows), BF16)],
        compiler_params=pltpu.CompilerParams(vmem_limit_bytes=VMEM_LIMIT),
        cost_estimate=pl.CostEstimate(
            flops=6 * rows * width * count * span,
            bytes_accessed=2 * width * (5 * rows + 3 * count * span),
            transcendentals=0,
        ),
        name="input_gradient",
    )(words, *own, *messages, *weights, first_in)


def local(body, name, words, arrays, shapes, costly=False):
    def kernel(words_ref, *refs):
        body(words_ref, refs[: len(arrays)], refs[len(arrays) :])

    vmem = pl.BlockSpec(memory_space=pltpu.VMEM)
    shapes = [jax.ShapeDtypeStruct(shape, kind) for shape, kind in shapes]
    moved = sum(item.size * item.dtype.itemsize for item in list(arrays) + shapes)
    cost = pl.CostEstimate(flops=0, bytes_accessed=moved, transcendentals=0)
    return pl.pallas_call(
        kernel,
        in_specs=[pl.BlockSpec(memory_space=pltpu.SMEM)] + [vmem] * len(arrays),
        out_specs=[vmem] * len(shapes),
        out_shape=shapes,
        compiler_params=pltpu.CompilerParams(vmem_limit_bytes=VMEM_LIMIT),
        cost_estimate=cost if costly else NO_COST,
        name=name,
    )(words, *arrays)


def shard(index, rows, base=0):
    return pl.ds(pl.multiple_of(base + index * rows, 16), rows)


def total_of(refs, rows=slice(None)):
    if len(refs) == 2 and all(ref.dtype == BF16 for ref in refs):
        return refs[0][rows] + refs[1][rows]
    total = refs[0][rows].astype(F32)
    for ref in refs[1:]:
        total = total + ref[rows].astype(F32)
    return total


def tree_sum(terms):
    while len(terms) > 1:
        terms = [terms[i] + terms[i + 1] for i in range(0, len(terms), 2)]
    return terms[0]


def bit_of(words, level):
    return lax.shift_right_logical(words[1], level) & 1


def pair_sum(words, mine, other):
    return after(words, mine) + other


def halve(words, level, mine, other):
    rows, width = mine.shape
    half = rows // 2

    def body(words, ins, outs):
        bit = bit_of(words, level)
        outs[0][...] = total_of(ins, shard(bit, half)).astype(BF16)
        outs[1][...] = total_of(ins, shard(1 - bit, half)).astype(BF16)

    return local(body, "halve", words, [mine, other], [((half, width), BF16)] * 2)


def join_halves(words, level, mine, other):
    words, mine = lax.optimization_barrier((words, mine))
    low = bit_of(words, level) == 0
    return jnp.concatenate([jnp.where(low, mine, other), jnp.where(low, other, mine)])


def across(block, level):
    return swapped(block, 1 << level, "depth")


class Plan:
    def __init__(self, rows, rows_a, more, span, width):
        self.count = lax.axis_size("blk")
        self.levels = lax.axis_size("depth").bit_length() - 1
        self.rows = rows
        self.rows_a = rows_a
        self.more = more
        self.span = span
        self.width = width
        self.a_ff = rows_a // self.count
        self.a_more = more // self.count
        self.a = self.a_ff + self.a_more
        self.b = (rows - rows_a) >> self.levels

    def shapes(self, *sizes):
        return [((rows, self.width), BF16) for rows in sizes]

    def scatter_one(self, words, halves):
        count, width = self.count, self.width
        a_ff, a_more = self.a_ff, self.a_more
        b_rows = (self.rows - self.rows_a) // count
        steps = count // 2

        def kernel(words_ref, *refs):
            parts = refs[6 : 6 + count]
            keep_ref, send_ref = refs[6 + count :]
            for i in range(count):

                @pl.when(pl.program_id(0) == i)
                def _(i=i):
                    parts[i][:a_ff] = total_of(refs[:2]).astype(BF16)
                    parts[i][a_ff:] = total_of(refs[2:4]).astype(BF16)
                    side = send_ref if i < steps else keep_ref
                    side[...] = total_of(refs[4:6]).astype(BF16)

        def there(rows):
            return pl.BlockSpec((rows, width), lambda i, words: (words[0] ^ i, 0))

        def b_at(i, words):
            bit = bit_of(words, 0)
            side = jnp.where(i < steps, 1 - bit, bit)
            return self.rows_a // b_rows + side * steps + i % steps, 0

        own_b = pl.BlockSpec((b_rows, width), b_at)
        shapes = [jax.ShapeDtypeStruct((self.a, width), BF16)] * count
        shapes += [jax.ShapeDtypeStruct((b_rows * steps, width), BF16)] * 2
        *parts_a, keep, send = pl.pallas_call(
            kernel,
            grid_spec=pltpu.PrefetchScalarGridSpec(
                num_scalar_prefetch=1,
                grid=(count,),
                in_specs=[there(a_ff)] * 2 + [there(a_more)] * 2 + [own_b] * 2,
                out_specs=[fixed(item) for item in shapes[:count]]
                + [
                    pl.BlockSpec((b_rows, width), lambda i, words: (jnp.maximum(i - steps, 0), 0)),
                    pl.BlockSpec((b_rows, width), lambda i, words: (jnp.minimum(i, steps - 1), 0)),
                ],
            ),
            out_shape=shapes,
            compiler_params=pltpu.CompilerParams(vmem_limit_bytes=VMEM_LIMIT),
            cost_estimate=NO_COST,
            name="scatter_one",
        )(words, *halves, *halves[:2])
        return [from_blk(part, i) for i, part in enumerate(parts_a)], keep, across(send, 0)

    def scatter_two(self, words, parts_a, keep_b, other_b, pages):
        count = self.count
        half = self.a // 2

        def body(words, ins, outs):
            bit = bit_of(words, 0)
            outs[0][...] = total_of(ins[:count], shard(bit, half)).astype(BF16)
            outs[1][...] = total_of(ins[:count], shard(1 - bit, half)).astype(BF16)
            part_b = total_of(ins[count : count + 2]).astype(BF16)
            outs[2][...] = part_b
            for i, out in enumerate(outs[3:]):
                out[: self.b] = part_b
                for page in range(len(pages)):
                    piece = ins[count + 2 + page * (count - 1) + i]
                    base = self.b + page * self.span
                    out[base : base + self.span, : piece.shape[1]] = piece[...]

        message = self.b + len(pages) * self.span
        shapes = self.shapes(half, half, self.b, *[message] * (count - 1))
        pieces = [piece for page in pages for piece in page[1:]]
        keep, send, part_b, *messages = local(
            body, "scatter_two", words, [*parts_a, keep_b, other_b, *pieces], shapes
        )
        return (
            keep,
            across(send, 0),
            part_b,
            [from_blk(item, i + 1) for i, item in enumerate(messages)],
        )

    def sum_b(self, words, part_b, messages):
        terms = [after(words, part_b)] + [item[: self.b] for item in messages]
        return tree_sum([item.astype(F32) for item in terms]).astype(BF16)

    def gather_b(self, words, part_b):
        for level in range(self.levels - 1, 0, -1):
            part_b = join_halves(words, level, part_b, across(part_b, level))
        return part_b, across(part_b, 0)


def gather_blk(part, cut, late=None):
    count = lax.axis_size("blk")
    if count != 4:
        return [(i, 0, from_blk(part, i)) for i in range(count)]
    one, two = swapped(part, 1), swapped(part, 2)
    if late is not None:
        one, two = after(late, (one, two))
    first, second = swapped(one[:cut], 2), swapped(two[cut:], 1)
    return [(0, 0, part), (1, 0, one), (2, 0, two), (3, 0, first), (3, cut, second)]


def with_core(pieces):
    return [(distance, base, from_core(item)) for distance, base, item in pieces]


SEGMENT = 256
SLOTS = 4


def widen_own(words, plan, pieces, halves_b, hidden):
    width = plan.width
    chunks = hidden // width
    pairs = chunks // 2
    per_matrix = width // SEGMENT
    arrays = [item for _, _, item in pieces] + list(halves_b)
    segments = []
    extras = []
    for at, (distance, base, item) in enumerate(pieces):
        stop = min(item.shape[0], plan.a_ff - base)
        for top in range(0, stop, SEGMENT):
            segments.append((at, top, min(SEGMENT, stop - top), distance, base + top))
        if base + item.shape[0] == plan.a:
            extras.append((at, distance))
    for at, item in enumerate(halves_b):
        for top in range(0, item.shape[0], SEGMENT):
            segments.append((len(pieces) + at, top, SEGMENT, None, top))

    def kernel(words_ref, *refs):
        ins = refs[: len(arrays)]
        joined_ref, expand_ref, reduce_ref, held, sems = refs[len(arrays) :]
        copies = []
        for index, (at, top, rows, distance, base) in enumerate(segments):
            slot = index % SLOTS
            if index >= SLOTS:
                copies[index - SLOTS].wait()
            part = ins[at][top : top + rows]
            held[slot, :rows] = part.astype(F32)
            if distance is None:
                half = ins[len(pieces)].shape[0]
                bit = bit_of(words_ref, 0)
                place = plan.rows_a + half * (bit if at == len(pieces) else 1 - bit) + base
            else:
                place = (words_ref[0] ^ distance) * plan.a_ff + base
            joined_ref[pl.ds(pl.multiple_of(place, SEGMENT), rows)] = part
            block = lax.div(place, SEGMENT)
            matrix = lax.div(block, per_matrix)
            row = (block - matrix * per_matrix) * SEGMENT
            chunk = (lax.div(matrix, 2) + words_ref[2] * pairs) % chunks
            column = pl.multiple_of(chunk * width, width)
            source = held.at[slot, :rows]
            to_expand = pltpu.make_async_copy(
                source,
                expand_ref.at[pl.ds(pl.multiple_of(row, SEGMENT), rows), pl.ds(column, width)],
                sems.at[slot],
            )
            to_reduce = pltpu.make_async_copy(
                source,
                reduce_ref.at[pl.ds(pl.multiple_of(column + row, SEGMENT), rows)],
                sems.at[slot],
            )
            is_expand = lax.rem(matrix, 2) == 0
            pl.when(is_expand)(to_expand.start)
            pl.when(jnp.logical_not(is_expand))(to_reduce.start)
            copies.append(to_reduce)
        for at, distance in extras:
            rows = shard(words_ref[0] ^ distance, plan.a_more, plan.rows)
            joined_ref[rows] = ins[at][ins[at].shape[0] - plan.a_more :]
        for copy in copies[-SLOTS:]:
            copy.wait()

    assert all(base % SEGMENT == 0 for *_, base in segments)
    vmem = pl.BlockSpec(memory_space=pltpu.VMEM)
    anywhere = pl.BlockSpec(memory_space=pl.ANY)
    return pl.pallas_call(
        kernel,
        in_specs=[pl.BlockSpec(memory_space=pltpu.SMEM)] + [vmem] * len(arrays),
        out_specs=[vmem, anywhere, anywhere],
        out_shape=[
            jax.ShapeDtypeStruct((plan.rows + plan.more, width), BF16),
            jax.ShapeDtypeStruct((width, hidden), F32),
            jax.ShapeDtypeStruct((hidden, width), F32),
        ],
        scratch_shapes=[
            pltpu.VMEM((SLOTS, SEGMENT, width), F32),
            pltpu.SemaphoreType.DMA((SLOTS,)),
        ],
        compiler_params=pltpu.CompilerParams(vmem_limit_bytes=VMEM_LIMIT),
        cost_estimate=pl.CostEstimate(
            flops=0, bytes_accessed=6 * hidden * width, transcendentals=0
        ),
        name="widen_own",
    )(words, *arrays)


def widen_other(words, joined, expand, reduce):
    width, hidden = expand.shape
    chunks = hidden // width
    pairs = chunks // 2

    def kernel(words_ref, half_ref, before_ref, before_too_ref, expand_ref, reduce_ref):
        expand_ref[...] = half_ref[:width].astype(F32)
        reduce_ref[...] = half_ref[width:].astype(F32)

    def place(s, words):
        return (s + (words[2] + 1) * pairs) % chunks

    anywhere = pl.BlockSpec(memory_space=pl.ANY)
    return pl.pallas_call(
        kernel,
        grid_spec=pltpu.PrefetchScalarGridSpec(
            num_scalar_prefetch=1,
            grid=(pairs,),
            in_specs=[
                pl.BlockSpec((2 * width, width), lambda s, words: (s, 0)),
                anywhere,
                anywhere,
            ],
            out_specs=[
                pl.BlockSpec((width, width), lambda s, words: (0, place(s, words))),
                pl.BlockSpec((width, width), lambda s, words: (place(s, words), 0)),
            ],
        ),
        out_shape=[
            jax.ShapeDtypeStruct((width, hidden), F32),
            jax.ShapeDtypeStruct((hidden, width), F32),
        ],
        input_output_aliases={2: 0, 3: 1},
        compiler_params=pltpu.CompilerParams(vmem_limit_bytes=VMEM_LIMIT),
        cost_estimate=pl.CostEstimate(
            flops=0, bytes_accessed=6 * hidden * width, transcendentals=0
        ),
        name="widen_other",
    )(words, joined, expand, reduce)


def finished(words, plan, heads, joined, side, before=()):
    count = plan.count
    span = plan.span
    width = plan.width
    half_rows = width // 2
    arrays = [item for _, _, item in heads]

    def kernel(words_ref, *refs):
        heads_refs, refs = refs[: len(heads)], refs[len(heads) :]
        extra_ref, refs = refs[0], refs[1 + len(before) :]
        outs, refs = refs[:5], refs[5:]
        gathered, wide, project, sems = refs
        rank = words_ref[0]
        half = words_ref[2] ^ side
        for ref, (distance, base, _) in zip(heads_refs, heads):
            rows = ref.shape[0]
            place = pl.multiple_of((rank ^ distance) * span, HEAD_DIM)
            for part in range(2):
                low, high = max(base, part * span), min(base + rows, (part + 1) * span)
                if low < high:
                    gathered[part, pl.ds(place + (low - part * span), high - low)] = ref[
                        low - base : high - base
                    ]
        for part in range(2):
            wide[part] = gathered[part, :width].astype(F32).T
        project[...] = extra_ref[:half_rows].astype(F32)

        @pl.when(half == 1)
        def _():
            wide[1] = entry_order(wide[1])

        def copy(source, target, at):
            return pltpu.make_async_copy(source, target, sems.at[at])

        for part in range(2):
            pl.when(half == 0)(copy(wide.at[part], outs[part], part).start)
            pl.when(half == 1)(copy(wide.at[part], outs[2 + part], part).start)
        rows = pl.ds(pl.multiple_of(half * half_rows, half_rows), half_rows)
        last = copy(project, outs[4].at[rows], 2)
        last.start()
        for part in range(2):
            copy(wide.at[part], outs[part], part).wait()
        last.wait()

    def whole(item):
        return pl.BlockSpec(item.shape, lambda s: (0, 0))

    more = pl.BlockSpec((plan.more, width), lambda s: (plan.rows // plan.more, 0))
    anywhere = pl.BlockSpec(memory_space=pl.ANY)
    first = 2 + len(heads)
    shapes = [jax.ShapeDtypeStruct((width, width), F32)] * 5
    return pl.pallas_call(
        kernel,
        grid=(1,),
        in_specs=[pl.BlockSpec(memory_space=pltpu.SMEM)]
        + [whole(item) for item in arrays]
        + [more]
        + [anywhere] * len(before),
        out_specs=[anywhere] * 5,
        out_shape=shapes,
        scratch_shapes=[
            pltpu.VMEM((2, count * span, width), BF16),
            pltpu.VMEM((2, width, width), F32),
            pltpu.VMEM((half_rows, width), F32),
            pltpu.SemaphoreType.DMA((3,)),
        ],
        input_output_aliases={first + at: at for at in range(len(before))},
        compiler_params=pltpu.CompilerParams(vmem_limit_bytes=VMEM_LIMIT),
        cost_estimate=pl.CostEstimate(
            flops=0, bytes_accessed=16 * width * width, transcendentals=0
        ),
        name="finish",
    )(words, *arrays, joined, *before)


def per_device(
    tokens,
    boxes,
    w_query,
    w_key,
    w_value,
    w_output,
    box_weight,
    first_gain,
    first_shift,
    w_expand,
    w_reduce,
    second_gain,
    second_shift,
    cotangent,
):
    pages, block, width = tokens.shape
    count = lax.axis_size("blk")
    depth = lax.axis_size("depth")
    words = jnp.stack(
        [lax.axis_index("blk"), lax.axis_index("depth"), lax.axis_index("core")]
    ).astype(jnp.int32)
    hidden = w_expand.shape[1]
    span = -(-HEADS // count) * HEAD_DIM
    unit = 16 * count * depth
    more = -(-(width // 2 + 16) // unit) * unit

    own_places = jnp.stack([boxes[0] + boxes[2], boxes[1] + boxes[3]], axis=1)
    own_places = jnp.stack([lax.shift_right_logical(own_places, 6), own_places & 63], axis=2)
    own_places = own_places.reshape(4 * pages, block).astype(BF16)
    own_places = jnp.pad(own_places, ((0, 16 - 4 * pages), (0, width - block)))
    message = jnp.concatenate([tokens[0], own_places])
    messages = [from_blk(message, i) for i in range(count)]
    w_own, box_own, rot_cos, rot_sin = prepare(
        words, w_query, w_key, w_value, box_weight, span, count * block
    )
    messages, rot_cos = lax.optimization_barrier((messages, rot_cos))
    own = after(messages, tokens[1])
    pieces = [messages, [from_blk(own, i) for i in range(count)]]

    saved = []
    att_parts = []
    for page in range(pages):
        results = attention_forward(
            words, page, messages, pieces[page], w_own, box_own, rot_cos, rot_sin
        )
        saved.append(results[:6])
        att_parts += [from_blk(results[6 + i], i) for i in range(count)]

    vectors = jnp.stack([first_gain, first_shift, second_gain, second_shift])
    results = middle(
        words,
        att_parts,
        tokens.reshape(pages * block, width),
        cotangent.reshape(pages * block, width),
        w_output,
        vectors,
        w_expand,
        w_reduce,
        pages,
        more,
    )
    layer_out, first_in, theirs, mine, more_theirs, more_mine = results[:6]
    grads = [from_blk(results[6 + i], i) for i in range(count)]
    plan = Plan(hidden, 2 * hidden // 3, more, span, width)
    parts_a, keep_b, other_b = plan.scatter_one(
        after(grads[:2], words), [mine, from_core(theirs), more_mine, from_core(more_theirs)]
    )

    def backward(page, words, before=None):
        return attention_backward(
            words,
            page,
            grads,
            pieces[page],
            saved[page],
            box_own,
            rot_cos,
            rot_sin,
            before,
        )

    *pre_one, before = backward(0, after(parts_a[0], words))
    done = before
    for level in range(1, plan.levels):
        keep_b, send_b = halve(after(done, words), level, keep_b, other_b)
        other_b = across(send_b, level)
        done = keep_b
    *pre_two, heads_mine, heads_theirs = backward(1, after(done, words), before)
    own = [pre_one[0], pre_two[0]]
    part_a, other_a, part_b, messages_b = plan.scatter_two(
        after(heads_mine, words), parts_a, keep_b, other_b, [pre_one, pre_two]
    )
    heads, other = halve(
        after(part_a, words), 0, heads_mine, from_core(after(part_a, heads_theirs))
    )
    part_a = pair_sum(after(heads, words), part_a, other_a)
    other = across(after(part_a, other), 0)
    heads = pair_sum(after(part_a, words), heads, other)
    done = heads
    for level in range(1, plan.levels):
        part_a = pair_sum(after(done, words), part_a, across(part_a, level))
        done = part_a
    other_a = across(part_a, 0)
    other = across(heads, 1)
    part_b = plan.sum_b(after(part_a, words), part_b, messages_b)
    heads = pair_sum(after(part_b, words), heads, other)
    part_a = join_halves(after(heads, words), 0, part_a, other_a)
    part_b = after(part_a, part_b)
    for level in range(2, plan.levels):
        heads = pair_sum(words, heads, across(heads, level))
    input_grad = input_gradient(
        after(part_a, words),
        own,
        messages_b,
        plan.b,
        span,
        (w_query, w_key, w_value),
        first_in,
    )
    heads = join_halves(after(input_grad, words), 0, heads, across(heads, 0))
    parts_b = plan.gather_b(after(heads, words), part_b)
    pieces_a = gather_blk(part_a, plan.a_ff // 2, parts_b[0])
    heads = after(([item for _, _, item in pieces_a], parts_b), heads)
    joined, *wide = widen_own(after(heads, words), plan, pieces_a, parts_b, hidden)
    at = plan.rows + width // 2
    sums = [joined[at + i].astype(F32) for i in range(4)]
    pieces_heads = gather_blk(heads, span, (joined, sums))
    joined_other = from_core(after(pieces_heads[1][2], joined))
    grads = finished(words, plan, pieces_heads, joined, 0)
    grad_expand, grad_reduce = widen_other(after(grads, words), joined_other, *wide)
    grad_query, grad_key, grad_value, grad_box, grad_project = finished(
        after(grad_expand, words), plan, with_core(pieces_heads), joined_other, 1, grads
    )
    return (
        layer_out.reshape(tokens.shape),
        input_grad.reshape(tokens.shape),
        grad_query,
        grad_key,
        grad_value,
        grad_project,
        grad_box,
        sums[0],
        sums[1],
        grad_expand,
        grad_reduce,
        sums[2],
        sums[3],
    )


def solution(mesh):
    blocks, rest = mesh.devices.shape
    parts = jax.sharding.Mesh(
        mesh.devices.reshape(blocks, rest // 2, 2), ("blk", "depth", "core")
    )
    split = P(("depth", "core"), "blk", None)
    return jax.shard_map(
        per_device,
        mesh=parts,
        in_specs=(split, P(None, ("depth", "core"), "blk")) + (P(),) * 11 + (split,),
        out_specs=(split, split) + (P(),) * 11,
        check_vma=False,
    )
```
